32 devices in a mesh: groups: 2 (over y), wide: 4 (over z), narrow: 2 (over x), pair: 2 (over core).
Axes of the slice: x: 2, y: 2, z: 4, core: 2. Of those that a mesh axis runs over, the one named last changes fastest.
Arguments:
- density: float32 [16384], P(('groups', 'wide', 'narrow', 'pair')), parts along dimension 0, may hold values from -4 to 4
- surface_flag: int32 [16384], P(('groups', 'wide', 'narrow', 'pair')), parts along dimension 0, may hold values 0 or 1
- stencil_base: int32 [3, 16384], P(None, ('groups', 'wide', 'narrow', 'pair')), parts along dimension 1, may hold values from 0 to 124, as said below
- sample_weights: float32 [64, 16384], P(None, ('groups', 'wide', 'narrow', 'pair')), parts along dimension 1, may hold values from 0 to 0.125
- dipole_weights: float32 [64, 16384], P(None, ('groups', 'wide', 'narrow', 'pair')), parts along dimension 1, may hold values from -0.5 to 0.5
- near_target: int32 [768], P(('groups', 'wide', 'narrow', 'pair')), parts along dimension 0, may hold values from -1 to 3, as said below
- near_source: int32 [768], P(('groups', 'wide', 'narrow', 'pair')), parts along dimension 0, may hold values from 0 to 35, as said below
- near_tiles: bfloat16 [768, 128, 128], P(('groups', 'wide', 'narrow', 'pair')), parts along dimension 0, may hold values from -0.039794922 to 0.039794922
Outputs:
- krylov: float32 [2, 16384], P(None, ('groups', 'wide', 'narrow', 'pair')), parts along dimension 1
The draws below stay inside these ranges and needn't reach their ends.
There are 2 independent parts, one for each index of `groups`. The reference program is written for one: setup_inputs(seed, part) draws one part's arguments, and reference() takes and returns one part's arrays. A program takes and returns all parts, laid end to end along the dimension named above; each array names one. Nothing has to cross between parts.
Inputs may be any that keep to these rules, and one draw needn't show every extreme that they name: `stencil_base`: for the panels of the device at position w along wide and y along narrow+pair, row 0 lies from w * 32 - 2 to w * 32 + 30 and row 1 from y * 32 - 2 to y * 32 + 30, each clipped to 0 to 124; on every device both ends of both ranges are taken. `near_target`: -1 marks an empty slot; on each device the live slots come first and a live value names one of its 4 blocks; some device has all 24 slots live. The device that near_source names lies within one position of the slot's device along wide and along narrow+pair, and exists.
All inputs are finite; a program needn't handle non-finite values. No bound on the sum of `surface_flag` on one device may be relied on, other than what follows from the above.
Results may differ from the reference program's by a relative error of at most 0.00041.
Values may be sent and summed in bfloat16 or wider, within the bound.
No kernel may reach another device: no remote copies, remote signals or barrier semaphores. Data moves between devices by JAX's collectives and lax.ppermute only.
A program may use at most 128 MiB of HBM per device.

```python
import jax
import jax.numpy as jnp
from jax import lax

GRID = 256
REGION = 128
POINTS = 64
BLOCK = 128
PAN_DEV = 512
BRICKS_X = 4
BRICKS_Y = 4
SPAN_X = 32
SPAN_Y = 32
BLK_DEV = 4
TILE_CAP = 24
PANELS = 8192
TILE_SLOTS = 384
N_WIDE = 4
N_NARROW = 2
N_PAIR = 2


def draw_density(key, part):
    key = jax.random.fold_in(key, 5)
    panel_total = BRICKS_X * BRICKS_Y * PAN_DEV
    return jnp.clip(jax.random.normal(key, (panel_total,), jnp.float32), -4.0, 4.0)


def draw_sample_weights(key, part):
    key = jax.random.fold_in(key, 23)
    panel_total = BRICKS_X * BRICKS_Y * PAN_DEV
    subkeys = jax.random.split(key, 3)
    depth = jax.random.randint(subkeys[0], (panel_total,), 0, 4)
    major = jax.random.uniform(subkeys[1], (16, panel_total), jnp.float32, 0.03125, 0.125)
    minor = jax.random.uniform(subkeys[2], (POINTS, panel_total), jnp.float32, 0.0, 0.015625)
    point_ids = jnp.arange(POINTS, dtype=jnp.int32)
    on_depth = (point_ids % 4)[:, None] == depth[None, :]
    return jnp.where(on_depth, major[point_ids // 4], minor)


def draw_dipole_weights(key, part):
    key = jax.random.fold_in(key, 29)
    panel_total = BRICKS_X * BRICKS_Y * PAN_DEV
    subkeys = jax.random.split(key, 3)
    pattern_kind = jax.random.randint(subkeys[0], (panel_total,), 0, 2)
    panel_sign = (2 * jax.random.randint(subkeys[1], (panel_total,), 0, 2) - 1).astype(jnp.float32)
    point_ids = jnp.arange(POINTS, dtype=jnp.int32)
    depth = point_ids % 4
    paired = jnp.where(depth < 2, 1.0, -1.0).astype(jnp.float32)
    alternate = jnp.where(depth % 2 == 0, 1.0, -1.0).astype(jnp.float32)
    pattern = jnp.where(pattern_kind[None, :] == 0, paired[:, None], alternate[:, None])
    size = jax.random.uniform(subkeys[2], (POINTS, panel_total), jnp.float32, 0.5, 1.0)
    return 0.5 * panel_sign[None, :] * pattern * size


def draw_stencil_base(key, part):
    key = jax.random.fold_in(key, 11)
    panel_total = BRICKS_X * BRICKS_Y * PAN_DEV
    subkeys = jax.random.split(key, 3)
    panel_ids = jnp.arange(panel_total, dtype=jnp.int32)
    owner_dev = panel_ids // PAN_DEV
    position = panel_ids % PAN_DEV
    lowest_x = owner_dev // BRICKS_Y * SPAN_X - 2
    lowest_y = owner_dev % BRICKS_Y * SPAN_Y - 2
    offset_x = jax.random.randint(subkeys[0], (panel_total,), 0, SPAN_X + 1)
    offset_y = jax.random.randint(subkeys[1], (panel_total,), 0, SPAN_Y + 1)
    offset_x = jnp.where(position == 0, 0, jnp.where(position == 1, SPAN_X, offset_x))
    offset_y = jnp.where(position == 0, 0, jnp.where(position == 1, SPAN_Y, offset_y))
    base_x = jnp.clip(lowest_x + offset_x, 0, REGION - 4)
    base_y = jnp.clip(lowest_y + offset_y, 0, REGION - 4)
    base_z = jax.random.randint(subkeys[2], (panel_total,), 0, REGION - 3)
    return jnp.stack([base_x, base_y, base_z]).astype(jnp.int32)


def near_lists(key):
    devices = BRICKS_X * BRICKS_Y
    slot_total = devices * TILE_CAP
    subkeys = jax.random.split(key, 5)
    live_count = jax.random.randint(subkeys[0], (devices,), TILE_CAP // 4, TILE_CAP + 1)
    live_count = live_count.at[0].set(TILE_CAP)
    slot_ids = jnp.arange(slot_total, dtype=jnp.int32)
    owner_dev = slot_ids // TILE_CAP
    is_live = slot_ids % TILE_CAP < live_count[owner_dev]
    target = jnp.where(is_live, jax.random.randint(subkeys[1], (slot_total,), 0, BLK_DEV), -1)
    x_position = owner_dev // BRICKS_Y
    y_position = owner_dev % BRICKS_Y
    shift_x = jnp.clip(x_position + jax.random.randint(subkeys[2], (slot_total,), -1, 2), 0, BRICKS_X - 1) - x_position
    shift_y = jnp.clip(y_position + jax.random.randint(subkeys[3], (slot_total,), -1, 2), 0, BRICKS_Y - 1) - y_position
    source_block = jax.random.randint(subkeys[4], (slot_total,), 0, BLK_DEV)
    source = ((shift_x + 1) * 3 + shift_y + 1) * BLK_DEV + source_block
    return (target.astype(jnp.int32), source.astype(jnp.int32))


def draw_near_target(key, part):
    return near_lists(jax.random.fold_in(key, 17))[0]


def draw_near_source(key, part):
    return near_lists(jax.random.fold_in(key, 17))[1]


def with_ends(array, stream_key, low, largest):
    dims = array.shape
    place = [jax.random.randint(jax.random.fold_in(stream_key, axis), (), 0, dims[axis]) for axis in range(len(dims))]
    array = array.at[tuple(place)].set(low)
    longest = dims.index(max(dims))
    place[longest] = (place[longest] + 1) % dims[longest]
    return array.at[tuple(place)].set(largest)


def block_levels(stream_key, shape, cuts, smallest, top_value):
    loudness = 1.0
    for axis_at, parts in cuts:
        steps = jax.random.uniform(jax.random.fold_in(jax.random.fold_in(stream_key, 6), axis_at), (parts,), jnp.float32, smallest / len(cuts), top_value / len(cuts))
        loudness = loudness * jnp.repeat(jnp.exp(steps), shape[axis_at] // parts).reshape((-1,) + (1,) * (len(shape) - 1 - axis_at))
    return loudness


def bell_draw(own_key, shape, width, most, shards=(), kind=jnp.bfloat16):
    loudness = block_levels(own_key, shape, shards, -0.22, 0.18) if shards else 1.0
    values = jax.random.normal(own_key, shape, jnp.float32) * width * loudness
    return jnp.minimum(jnp.maximum(values, -most), most).astype(kind)


def setup_inputs(seed: int = 0, part: int = 0) -> dict:
    key_list = jax.random.split(jax.random.key(seed), 9)
    part_splits = jax.random.split(jax.random.fold_in(key_list[8], part), 9)
    density = draw_density(jax.random.fold_in(jax.random.fold_in(key_list[8], part), 71), part)
    surface_flag = with_ends((jax.random.randint(part_splits[1], (PANELS,), 0, 3) < 1).astype(jnp.int32), jax.random.fold_in(part_splits[1], 1), 0, 1)
    stencil_base = draw_stencil_base(jax.random.fold_in(jax.random.fold_in(key_list[8], part), 71), part)
    sample_weights = draw_sample_weights(jax.random.fold_in(jax.random.fold_in(key_list[8], part), 71), part)
    dipole_weights = draw_dipole_weights(jax.random.fold_in(jax.random.fold_in(key_list[8], part), 71), part)
    near_target = draw_near_target(jax.random.fold_in(jax.random.fold_in(key_list[8], part), 71), part)
    near_source = draw_near_source(jax.random.fold_in(jax.random.fold_in(key_list[8], part), 71), part)
    near_tiles = bell_draw(part_splits[7], (TILE_SLOTS, BLOCK, BLOCK), 0.01, 0.039794922, ((0, 16),))
    return {"density": density, "surface_flag": surface_flag, "stencil_base": stencil_base, "sample_weights": sample_weights, "dipole_weights": dipole_weights, "near_target": near_target, "near_source": near_source, "near_tiles": near_tiles}


KERNEL_GAIN = 4.0
SCREEN = 1.0 / 1024.0


def symbol(wave_ids):
    sine_wave = jnp.sin(jnp.pi * wave_ids.astype(jnp.float32) / GRID)
    return 4.0 * sine_wave * sine_wave


def apply_operator(vector, charged, cell_ids, sample_weights, dipole_weights, near_target, near_source, near_tiles):
    sources = jnp.where(charged[None, :], -sample_weights * vector[None, :], dipole_weights * vector[None, :])
    charge_grid = jnp.zeros((REGION * REGION * REGION,), jnp.float32).at[cell_ids.reshape(-1)].add(sources.reshape(-1))
    spectrum = jnp.fft.rfftn(charge_grid.reshape(REGION, REGION, REGION), s=(GRID, GRID, GRID))
    full_waves = symbol(jnp.arange(GRID, dtype=jnp.int32))
    half_waves = symbol(jnp.arange(GRID // 2 + 1, dtype=jnp.int32))
    kernel = KERNEL_GAIN / (SCREEN + full_waves[:, None, None] + full_waves[None, :, None] + half_waves[None, None, :])
    potential = jnp.fft.irfftn(spectrum * kernel, s=(GRID, GRID, GRID))[:REGION, :REGION, :REGION]
    sampled = jnp.sum(sample_weights * potential.reshape(-1)[cell_ids], axis=0)
    devices = N_WIDE * N_NARROW * N_PAIR
    across = N_NARROW * N_PAIR
    rounded = vector.astype(jnp.bfloat16).reshape(devices * BLK_DEV, BLOCK)
    slot_ids = jnp.arange(TILE_SLOTS, dtype=jnp.int32)
    owner_dev = slot_ids // TILE_CAP
    neighbor = near_source // BLK_DEV
    source_dev = owner_dev + (neighbor // 3 - 1) * across + (neighbor % 3 - 1)
    picked = rounded[(source_dev * BLK_DEV + near_source % BLK_DEV).astype(jnp.int32)]

    def one_device(pieces):
        return jnp.einsum('tij,tj->ti', pieces[0].astype(jnp.float32), pieces[1].astype(jnp.float32))

    products = lax.map(one_device, (near_tiles.reshape(devices, TILE_CAP, BLOCK, BLOCK), picked.reshape(devices, TILE_CAP, BLOCK)))
    target = jnp.where(near_target >= 0, owner_dev * BLK_DEV + near_target, devices * BLK_DEV).astype(jnp.int32)
    near_part = jax.ops.segment_sum(products.reshape(TILE_SLOTS, BLOCK), target, num_segments=devices * BLK_DEV + 1)
    near_part = near_part[:devices * BLK_DEV].reshape(-1)
    return 0.5 * jnp.where(charged, 0.0, vector) + sampled + near_part


def reference(density, surface_flag, stencil_base, sample_weights, dipole_weights, near_target, near_source, near_tiles):
    point_ids = jnp.arange(64, dtype=jnp.int32)
    cell_ids = ((stencil_base[0][None, :] + (point_ids // 16)[:, None]) * REGION + stencil_base[1][None, :] + ((point_ids // 4) % 4)[:, None]) * REGION + stencil_base[2][None, :] + (point_ids % 4)[:, None]
    charged = surface_flag == 1
    first_image = apply_operator(density, charged, cell_ids, sample_weights, dipole_weights, near_target, near_source, near_tiles)
    second = apply_operator(first_image, charged, cell_ids, sample_weights, dipole_weights, near_target, near_source, near_tiles)
    return jnp.stack([first_image, second])
```

```python
import functools

import jax
import jax.numpy as jnp
import numpy as np
from jax import lax
from jax.experimental import pallas as pl
from jax.experimental.pallas import tpu as pltpu
from jax.sharding import PartitionSpec as P

GRID = 256
REGION = 128
BLOCK = 128
HALF = 64
KERNEL_GAIN = 4.0
SCREEN = 1.0 / 1024.0
HIGHEST = lax.Precision.HIGHEST
Y_AXES = ("narrow", "pair")
ALL_AXES = ("wide", "narrow", "pair")
F32 = jnp.float32
VMEM_LIMIT = 24 * 1024 * 1024


def cas(angles):
    return np.cos(angles) + np.sin(angles)


def low_lanes(rows):
    return lax.broadcasted_iota(jnp.int32, (rows, 2 * HALF), 1) < HALF


def swap(values):
    return pltpu.roll(values, HALF, 1)


def dot(left, right):
    return jnp.dot(left, right, precision=HIGHEST, preferred_element_type=F32)


def params():
    return pltpu.CompilerParams(vmem_limit_bytes=VMEM_LIMIT)


def whole_vmem():
    return pl.BlockSpec(memory_space=pltpu.VMEM)


def in_smem():
    return pl.BlockSpec(memory_space=pltpu.SMEM)


def cost(flops, moved):
    return pl.CostEstimate(flops=flops, bytes_accessed=moved, transcendentals=0)


def tables(y_count, span_y):
    depth = GRID // y_count
    reach = span_y + 4
    waves = np.arange(GRID)
    step = 2.0 * np.pi / GRID
    z_table = cas(step * np.outer(np.arange(REGION), waves))
    z_forward = np.zeros((y_count, 2 * REGION, 2 * HALF))
    z_inverse = np.zeros((y_count, 2 * HALF, 2 * REGION))
    symbols = 4.0 * np.sin(np.pi * waves / GRID) ** 2
    shift = np.full((y_count, GRID, 2 * HALF), 1.0)
    y_forward = np.zeros((y_count, GRID, reach))
    for block in range(y_count):
        mine = z_table[:, block * depth : (block + 1) * depth]
        for half in range(2):
            rows = slice(half * REGION, (half + 1) * REGION)
            lanes = slice(half * HALF, half * HALF + depth)
            z_forward[block, rows, lanes] = mine
            z_inverse[block, lanes, rows] = mine.T / GRID
            shift[block, :, lanes] = (
                SCREEN + symbols[:, None] + symbols[None, block * depth : (block + 1) * depth]
            )
        cells = block * span_y - 2 + np.arange(reach)
        y_forward[block] = cas(step * np.outer(waves, cells))
    root = np.sqrt(shift * (shift + 4.0))
    decay = 2.0 / (2.0 + shift + root)
    log_decay = np.log(decay)
    ring = 1.0 / (1.0 - np.exp(GRID * log_decay))
    gain = KERNEL_GAIN / root
    modes = np.stack([decay, log_decay, ring, gain], axis=1)
    single = lambda values: values.astype(np.float32)
    return single(z_forward), single(z_inverse), single(y_forward), single(modes)


def lines_kernel(depth_ref, flag_ref, sample_ref, dipole_ref, source_out, sample_out):
    first = pl.program_id(0) * BLOCK
    sample = sample_ref[...]
    source = jnp.where(flag_ref[...] == 1, -sample, dipole_ref[...])
    lanes = lax.broadcasted_iota(jnp.int32, (16, REGION), 1)
    for panel in range(BLOCK):
        offset = lanes - depth_ref[first + panel]
        rows = slice(panel * 16, panel * 16 + 16)
        for coeff, out in ((source, source_out), (sample, sample_out)):
            line = jnp.zeros((16, REGION), F32)
            for depth in range(4):
                column = coeff[depth * 16 : depth * 16 + 16, panel : panel + 1]
                line = jnp.where(offset == depth, column, line)
            out[rows, :] = line


def panel_lines(base_z, flag, sample, dipole):
    count = base_z.shape[0]
    by_depth = lambda w: w.reshape(16, 4, count).transpose(1, 0, 2).reshape(64, count)
    wide_block = pl.BlockSpec((64, BLOCK), lambda i: (0, i))
    out_block = pl.BlockSpec((16 * BLOCK, REGION), lambda i: (i, 0))
    shape = jax.ShapeDtypeStruct((16 * count, REGION), F32)
    return pl.pallas_call(
        lines_kernel,
        grid=(count // BLOCK,),
        in_specs=[in_smem(), pl.BlockSpec((1, BLOCK), lambda i: (0, i)), wide_block, wide_block],
        out_specs=[out_block, out_block],
        out_shape=[shape, shape],
        compiler_params=params(),
        name="panel_lines",
    )(base_z, flag.reshape(1, -1), by_depth(sample), by_depth(dipole))


def spread_kernel(reach, pieces, vector_ref, row_ref, line_ref, table_ref, *refs):
    outs, grids = refs[:pieces], refs[pieces:]
    step = pl.program_id(0)

    @pl.when(step == 0)
    def _():
        for grid in grids:
            grid[...] = jnp.zeros_like(grid)

    chains = len(grids)

    def body(group, carry):
        for chain in range(chains):
            local = group * chains + chain
            panel = step * BLOCK + local
            value = vector_ref[panel]
            row = row_ref[panel]
            places = [pl.ds(row + a * reach, 4) for a in range(4)]
            held = [grids[chain][place, :] for place in places]
            added = [line_ref[pl.ds(local * 16 + 4 * a, 4), :] * value for a in range(4)]
            for a in range(4):
                grids[chain][places[a], :] = held[a] + added[a]
        return carry

    lax.fori_loop(0, BLOCK // chains, body, 0, unroll=4)

    @pl.when(step == pl.num_programs(0) - 1)
    def _():
        total = grids[0][...]
        for grid in grids[1:]:
            total = total + grid[...]
        half = total.shape[0] // 2
        both = jnp.concatenate([total[:half], total[half:]], axis=1)
        for piece in range(pieces):
            outs[piece][...] = dot(both, table_ref[piece])


def spread(vector, rows, lines, table, reach_x, reach_y):
    count = vector.shape[0]
    pieces = table.shape[0]
    line_count = reach_x * reach_y
    half = line_count // 2
    return pl.pallas_call(
        functools.partial(spread_kernel, reach_y, pieces),
        grid=(count // BLOCK,),
        in_specs=[
            in_smem(),
            in_smem(),
            pl.BlockSpec((16 * BLOCK, REGION), lambda i: (i, 0)),
            pl.BlockSpec(table.shape, lambda i: (0, 0, 0)),
        ],
        out_specs=[pl.BlockSpec((half, 2 * HALF), lambda i: (0, 0))] * pieces,
        out_shape=[jax.ShapeDtypeStruct((half, 2 * HALF), F32)] * pieces,
        scratch_shapes=[pltpu.VMEM((line_count, REGION), F32)] * 4,
        compiler_params=params(),
        cost_estimate=cost(2 * half * 256 * 512, 4 * 16 * count * REGION),
        name="spread",
    )(vector, rows, lines, table)


def forward_kernel(reach_x, reach_y, pieces, *refs):
    parts = refs[:pieces]
    table_ref, modes_ref, spectrum, right_out, left_out, own_out, stacked = refs[pieces:]
    half = reach_x // 2
    tall = pieces * reach_y
    for i in range(half):
        for piece in range(pieces):
            stacked[i * tall + piece * reach_y : i * tall + (piece + 1) * reach_y, :] = parts[
                piece
            ][i * reach_y : (i + 1) * reach_y, :]
    table = table_ref[...]
    for i in range(0, half, 2):
        if i + 1 < half:
            pair = jnp.concatenate(
                [stacked[i * tall : (i + 1) * tall, :], stacked[(i + 1) * tall : (i + 2) * tall, :]],
                axis=1,
            )
            both = dot(table, pair)
            spectrum[i] = both[:, : 2 * HALF]
            spectrum[i + 1] = both[:, 2 * HALF :]
        else:
            spectrum[i] = dot(table, stacked[i * tall : (i + 1) * tall, :])

    chunk = 32

    def body(index, carry):
        rows = pl.ds(pl.multiple_of(index * chunk, chunk), chunk)
        low = low_lanes(chunk)
        decay = modes_ref[0, rows, :]
        log_decay = modes_ref[1, rows, :]
        across_half = jnp.exp(half * log_decay)
        across_cut = jnp.exp((half - 4) * log_decay)
        layers = [spectrum[i, rows, :] for i in range(half)]
        run = layers[0]
        cut_right = run
        for i in range(1, half):
            run = decay * run + layers[i]
            if i == half - 5:
                cut_right = run
        right = run
        run = layers[half - 1]
        cut_left = run
        for i in range(half - 2, -1, -1):
            run = decay * run + layers[i]
            if i == 4:
                cut_left = run
        left = run
        swapped_right, swapped_left = swap(right), swap(left)
        own = jnp.where(low, left + across_half * swapped_left, right + across_half * swapped_right)
        own_out[rows, :] = own
        right_out[0, rows, :] = jnp.where(low, swap(layers[half - 4]), layers[half - 3])
        right_out[1, rows, :] = jnp.where(low, swap(layers[half - 2]), layers[half - 1])
        right_out[2, rows, :] = jnp.where(low, own, cut_right + across_cut * swapped_right)
        left_out[0, rows, :] = jnp.where(low, layers[0], swap(layers[1]))
        left_out[1, rows, :] = jnp.where(low, layers[2], swap(layers[3]))
        left_out[2, rows, :] = jnp.where(low, cut_left + across_cut * swapped_left, own)
        return carry

    lax.fori_loop(0, GRID // chunk, body, 0)


def forward(parts, table, modes, reach_x, reach_y):
    pieces = len(parts)
    half = reach_x // 2
    lanes = 2 * HALF
    struct = lambda *shape: jax.ShapeDtypeStruct(shape, F32)
    return pl.pallas_call(
        functools.partial(forward_kernel, reach_x, reach_y, pieces),
        in_specs=[whole_vmem()] * (pieces + 2),
        out_specs=[whole_vmem()] * 4,
        out_shape=[
            struct(half, GRID, lanes),
            struct(3, GRID, lanes),
            struct(3, GRID, lanes),
            struct(GRID, lanes),
        ],
        scratch_shapes=[pltpu.VMEM((half * pieces * reach_y, lanes), F32)],
        compiler_params=params(),
        cost_estimate=cost(2 * half * 256 * 256 * 128, 4 * half * GRID * lanes * 2),
        name="forward",
    )(*parts, table, modes)


def inverse_kernel(reach_x, reach_y, pieces, fars, *refs):
    power_ref, spectrum, from_left, from_right, own_ref = refs[:5]
    far_refs = refs[5 : 5 + fars]
    table_ref, modes_ref = refs[5 + fars : 7 + fars]
    outs = refs[7 + fars : 7 + fars + pieces]
    field = refs[7 + fars + pieces]
    half = reach_x // 2
    span = reach_x - 4
    chunk = 16

    def body(index, carry):
        rows = pl.ds(pl.multiple_of(index * chunk, chunk), chunk)
        low = low_lanes(chunk)
        decay = modes_ref[0, rows, :]
        log_decay = modes_ref[1, rows, :]
        ring = modes_ref[2, rows, :]
        gain = modes_ref[3, rows, :]
        across_half = jnp.exp(half * log_decay)
        around = jnp.exp((GRID - 4) * log_decay)
        beside = jnp.exp((GRID - reach_x - span) * log_decay)
        layers = [spectrum[i, rows, :] for i in range(half)]
        head = from_left[0, rows, :], from_left[1, rows, :]
        tail = from_right[0, rows, :], from_right[1, rows, :]
        zero = jnp.zeros_like(decay)
        from_head = [head[0], swap(head[0]), head[1], swap(head[1])]
        from_tail = [swap(tail[0]), tail[0], swap(tail[1]), tail[1]]
        head_sum = from_head[0]
        for i in range(1, 4):
            head_sum = decay * head_sum + from_head[i]
        tail_sum = from_tail[3]
        for i in range(2, -1, -1):
            tail_sum = decay * tail_sum + from_tail[i]
        for i in range(4):
            layers[i] = layers[i] + jnp.where(low, from_head[i], zero)
        for i in range(4):
            place = half - 4 + i
            layers[place] = layers[place] + jnp.where(low, zero, from_tail[i])
        total = own_ref[rows, :] * jnp.exp((GRID - reach_x) * log_decay)
        one = jnp.ones_like(decay)
        total = total + from_left[2, rows, :] * jnp.where(low, beside, one)
        total = total + from_right[2, rows, :] * jnp.where(low, one, beside)
        for far in range(fars):
            power = jnp.where(low, power_ref[2 * far], power_ref[2 * far + 1])
            total = total + far_refs[far][rows, :] * jnp.exp(power * log_decay)
        entering = (swap(total) + around * jnp.where(low, head_sum, tail_sum)) * ring
        run = layers[0]
        for i in range(1, half):
            run = decay * run + layers[i]
        right_start = jnp.where(low, entering, swap(across_half * entering + run))
        run = layers[half - 1]
        for i in range(half - 2, -1, -1):
            run = decay * run + layers[i]
        left_start = jnp.where(low, swap(across_half * entering + run), entering)
        run = right_start
        forward_runs = []
        for i in range(half):
            run = decay * run + layers[i]
            forward_runs.append(run)
        run = left_start
        for i in range(half - 1, -1, -1):
            ahead = decay * run
            field[i, rows, :] = gain * (forward_runs[i] + ahead)
            run = ahead + layers[i]
        return carry

    lax.fori_loop(0, GRID // chunk, body, 0)
    table = table_ref[...]
    for i in range(0, half, 2):
        if i + 1 < half:
            pair = dot(table, jnp.concatenate([field[i], field[i + 1]], axis=1))
            results = [pair[:, : 2 * HALF], pair[:, 2 * HALF :]]
        else:
            results = [dot(table, field[i])]
        for j, result in enumerate(results):
            place = slice((i + j) * reach_y, (i + j + 1) * reach_y)
            for piece in range(pieces):
                outs[piece][place, :] = result[piece * reach_y : (piece + 1) * reach_y]


def inverse(powers, spectrum, from_left, from_right, own, fars, table, modes, reach_x, reach_y):
    pieces = table.shape[0] // reach_y
    half = reach_x // 2
    shape = jax.ShapeDtypeStruct((half * reach_y, 2 * HALF), F32)
    return pl.pallas_call(
        functools.partial(inverse_kernel, reach_x, reach_y, pieces, len(fars)),
        in_specs=[in_smem()] + [whole_vmem()] * (6 + len(fars)),
        out_specs=[whole_vmem()] * pieces,
        out_shape=[shape] * pieces,
        scratch_shapes=[pltpu.VMEM((half, GRID, 2 * HALF), F32)],
        compiler_params=params(),
        cost_estimate=cost(2 * half * 256 * 256 * 128, 4 * half * GRID * 2 * HALF * 2),
        name="inverse",
    )(powers, spectrum, from_left, from_right, own, *fars, table, modes)


def sample_kernel(reach, pieces, row_ref, *refs):
    parts = refs[:pieces]
    table_ref, line_ref, base_ref, near_ref, out_ref, field, sums = refs[pieces:]
    step = pl.program_id(0)

    @pl.when(step == 0)
    def _():
        both = dot(jnp.concatenate([part[...] for part in parts], axis=1), table_ref[...])
        half = both.shape[0]
        field[:half, :] = both[:, :REGION]
        field[half:, :] = both[:, REGION:]

    def body(local, carry):
        row = row_ref[step * BLOCK + local]
        total = field[pl.ds(row, 4), :] * line_ref[pl.ds(local * 16, 4), :]
        for a in range(1, 4):
            total = total + field[pl.ds(row + a * reach, 4), :] * line_ref[
                pl.ds(local * 16 + 4 * a, 4), :
            ]
        sums[pl.ds(local, 1), :] = jnp.sum(total, axis=0, keepdims=True)
        return carry

    lax.fori_loop(0, BLOCK, body, 0, unroll=8)
    sampled = lax.dot_general(
        jnp.ones((8, REGION), F32),
        sums[...],
        (((1,), (1,)), ((), ())),
        precision=HIGHEST,
        preferred_element_type=F32,
    )
    out_ref[...] = base_ref[...] + sampled[:1] + near_ref[pl.ds(step, 1), :]


def sample(rows, parts, table, lines, base, near, reach):
    count = rows.shape[0]
    pieces = len(parts)
    half = parts[0].shape[0]
    constant = lambda shape: pl.BlockSpec(shape, lambda i: (0,) * len(shape))
    panel_row = pl.BlockSpec((1, BLOCK), lambda i: (0, i))
    return pl.pallas_call(
        functools.partial(sample_kernel, reach, pieces),
        grid=(count // BLOCK,),
        in_specs=[in_smem()]
        + [constant(part.shape) for part in parts]
        + [
            constant(table.shape),
            pl.BlockSpec((16 * BLOCK, REGION), lambda i: (i, 0)),
            panel_row,
            constant(near.shape),
        ],
        out_specs=panel_row,
        out_shape=jax.ShapeDtypeStruct((1, count), F32),
        scratch_shapes=[
            pltpu.VMEM((2 * half, REGION), F32),
            pltpu.VMEM((BLOCK, REGION), F32),
        ],
        compiler_params=params(),
        cost_estimate=cost(2 * half * 256 * 512, 4 * 16 * count * REGION),
        name="sample",
    )(rows, *parts, table, lines, base, near)


def near_kernel(slots, place_ref, target_ref, vector_ref, tile_ref, out_ref):
    out_ref[...] = jnp.zeros_like(out_ref)
    for slot in range(slots):
        picked = vector_ref[pl.ds(place_ref[slot], 1), :]
        picked = jnp.broadcast_to(picked, (16, BLOCK)).astype(jnp.bfloat16)
        product = lax.dot_general(
            picked,
            tile_ref[slot],
            (((1,), (1,)), ((), ())),
            preferred_element_type=F32,
        )
        target = pl.ds(target_ref[slot], 1)
        out_ref[target, :] = out_ref[target, :] + product[:1]


def near_field(places, targets, blocks, tiles, out_rows):
    slots = tiles.shape[0]
    return pl.pallas_call(
        functools.partial(near_kernel, slots),
        in_specs=[in_smem(), in_smem(), whole_vmem(), whole_vmem()],
        out_specs=whole_vmem(),
        out_shape=jax.ShapeDtypeStruct((out_rows, BLOCK), F32),
        compiler_params=params(),
        cost_estimate=cost(2 * slots * 16 * BLOCK * BLOCK, 2 * slots * BLOCK * BLOCK),
        name="near_field",
    )(places, targets, blocks, tiles)


def shards(
    density,
    surface_flag,
    stencil_base,
    sample_weights,
    dipole_weights,
    near_target,
    near_source,
    near_tiles,
):
    x_count = lax.axis_size("wide")
    y_count = lax.axis_size(Y_AXES)
    x_index = lax.axis_index("wide")
    y_index = lax.axis_index(Y_AXES)
    span_x = REGION // x_count
    span_y = REGION // y_count
    reach_x = span_x + 4
    reach_y = span_y + 4
    count = density.shape[0]
    blocks_dev = count // BLOCK

    z_forward, z_inverse, y_forward, modes = (jnp.asarray(t) for t in tables(y_count, span_y))
    order = y_index ^ jnp.arange(y_count, dtype=jnp.int32)
    z_forward = jnp.take(z_forward, order, axis=0)
    z_inverse = jnp.take(z_inverse, order, axis=0).reshape(y_count * 2 * HALF, 2 * REGION)
    y_picked = jnp.take(y_forward, order, axis=0)
    y_inverse = y_picked.transpose(0, 2, 1).reshape(y_count * reach_y, GRID)
    y_forward = y_inverse.T
    y_inverse = y_inverse / GRID
    modes = lax.dynamic_index_in_dim(modes, y_index, 0, keepdims=False)

    local_x = stencil_base[0] - (x_index * span_x - 2)
    local_y = stencil_base[1] - (y_index * span_y - 2)
    rows = local_x * reach_y + local_y
    source_lines, sample_lines = panel_lines(
        stencil_base[2], surface_flag, sample_weights, dipole_weights
    )
    own_share = jnp.where(surface_flag == 1, 0.0, 0.5).astype(F32)

    neighbour = near_source // blocks_dev
    source_x = x_index + neighbour // 3 - 1
    source_y = y_index + neighbour % 3 - 1
    places = (source_x * y_count + source_y) * blocks_dev + near_source % blocks_dev
    out_rows = 8 * ((blocks_dev + 8) // 8)
    live = near_target >= 0
    places = jnp.where(live, places, 0)
    targets = jnp.where(live, near_target, out_rows - 1)

    far_moves = []
    powers = []

    def add_far(pairs, behind):
        far_moves.append(pairs)
        for distance in (-behind, behind):
            ahead = span_x * distance - reach_x
            powers.append(jnp.where(distance >= 2, ahead, ahead + GRID))

    for shift in range(2, x_count - 1):
        pairs = [(i, (i + shift) % x_count) for i in range(x_count)]
        add_far(pairs, jnp.where(x_index >= shift, shift, shift - x_count))
    if x_count > 2:
        last = x_count - 1
        behind = jnp.where(x_index == 0, -last, jnp.where(x_index == last, last, 0))
        add_far([(0, last), (last, 0)], behind)
    powers = jnp.stack(powers).astype(F32) if powers else jnp.zeros((2,), F32)
    to_right = [(i, i + 1) for i in range(x_count - 1)]
    to_left = [(i + 1, i) for i in range(x_count - 1)]

    def turn(parts):
        return [
            part
            if flip == 0
            else lax.ppermute(part, Y_AXES, [(i, i ^ flip) for i in range(y_count)])
            for flip, part in enumerate(parts)
        ]

    def apply_operator(vector):
        beside = lax.all_gather(
            vector.astype(jnp.bfloat16).reshape(blocks_dev, BLOCK), ALL_AXES, axis=0, tiled=True
        ).astype(F32)
        near_part = near_field(places, targets, beside, near_tiles, out_rows)
        parts = turn(spread(vector, rows, source_lines, z_forward, reach_x, reach_y))
        spectrum, right_going, left_going, own = forward(parts, y_forward, modes, reach_x, reach_y)
        from_left = lax.ppermute(right_going, "wide", to_right)
        from_right = lax.ppermute(left_going, "wide", to_left)
        fars = [lax.ppermute(own, "wide", pairs) for pairs in far_moves]
        parts = turn(
            inverse(
                powers,
                spectrum,
                from_left,
                from_right,
                own,
                fars,
                y_inverse,
                modes,
                reach_x,
                reach_y,
            )
        )
        base = (own_share * vector).reshape(1, -1)
        return sample(rows, parts, z_inverse, sample_lines, base, near_part, reach_y)[0]

    first_image = apply_operator(density)
    second = apply_operator(first_image)
    return jnp.stack([first_image, second])


def solution(mesh):
    panels = P(("groups",) + ALL_AXES)
    columns = P(None, ("groups",) + ALL_AXES)
    in_specs = (
        panels,
        panels,
        columns,
        columns,
        columns,
        panels,
        panels,
        P(("groups",) + ALL_AXES, None, None),
    )
    return jax.shard_map(
        shards, mesh=mesh, in_specs=in_specs, out_specs=columns, check_vma=False
    )
```

```python
import functools
import math

import jax
import jax.numpy as jnp
import numpy as np
from jax import lax
from jax.experimental import pallas as pl
from jax.experimental.pallas import tpu as pltpu
from jax.sharding import PartitionSpec as P

GRID = 256
REGION = 128
BLOCK = 128
HALF = 64
KERNEL_GAIN = 4.0
SCREEN = 1.0 / 1024.0
LN2 = math.log(2.0)
Y_AXES = ("narrow", "pair")
ALL_AXES = ("wide", "narrow", "pair")
F32 = jnp.float32
BF16 = jnp.bfloat16
VMEM_LIMIT = 24 * 1024 * 1024
GROUP = 32
CHAINS = 4


def cas(angles):
    return np.cos(angles) + np.sin(angles)


def up_to(count, multiple):
    return -(-count // multiple) * multiple


def low_lanes(rows):
    return lax.broadcasted_iota(jnp.int32, (rows, 2 * HALF), 1) < HALF


def swap(values):
    return pltpu.roll(values, HALF, 1)


def split(values):
    high = values.astype(BF16)
    return high, (values - high.astype(F32)).astype(BF16)


def dot(left, right):
    return jnp.dot(left, right, preferred_element_type=F32)


def dot_three(left, right):
    return dot(left[0], right[0]) + (dot(left[0], right[1]) + dot(left[1], right[0]))


def params():
    return pltpu.CompilerParams(vmem_limit_bytes=VMEM_LIMIT)


def whole_vmem():
    return pl.BlockSpec(memory_space=pltpu.VMEM)


def in_smem():
    return pl.BlockSpec(memory_space=pltpu.SMEM)


def cost(flops, moved):
    return pl.CostEstimate(flops=flops, bytes_accessed=moved, transcendentals=0)


def full_scale(exponent, fraction):
    return fraction * jnp.exp(exponent * LN2) * (1.0 / 1024.0)


def fit_scale(largest):
    largest = jnp.maximum(largest, 1e-30)
    exponent = jnp.floor(jnp.log(largest) * (1.0 / LN2))
    fraction = jnp.ceil(largest * jnp.exp(-exponent * LN2) * 1024.0) + 1.0
    return exponent, fraction


def to_short(values):
    return values.astype(jnp.int32).astype(jnp.int16)


def from_short(values):
    return values.astype(jnp.int32).astype(F32)


def quantize(values, exponent, fraction):
    return to_short(jnp.round(values * (32767.0 / full_scale(exponent, fraction))))


def unit(exponent, fraction):
    return full_scale(exponent, fraction) * (1.0 / 32767.0)


def encode_rounded(values):
    rounded = values.astype(BF16).astype(F32)
    size = jnp.maximum(jnp.abs(rounded), 1e-30)
    exponent = jnp.floor(jnp.log(size) * (1.0 / LN2))
    return jnp.round(rounded * jnp.exp((10.0 - exponent) * LN2)), exponent


def decode_rounded(mantissa, exponent):
    return (mantissa * jnp.exp((exponent - 10.0) * LN2)).astype(BF16).astype(F32)


def send_piece(out, head, values):
    exponent, fraction = fit_scale(jnp.max(jnp.abs(values), axis=0, keepdims=True))
    head[0:1, :] = exponent
    head[1:2, :] = fraction
    top = head.shape[0]
    out[:top, :] = to_short(head[...])
    out[top:, :] = quantize(values, exponent, fraction)


def y_position():
    return lax.axis_index("narrow") * lax.axis_size("pair") + lax.axis_index("pair")


def halves(table):
    high = table.astype(jnp.bfloat16)
    return high, (table - high.astype(np.float64)).astype(jnp.bfloat16)


def tables(y_count, span_y):
    depth = GRID // y_count
    reach = span_y + 4
    waves = np.arange(GRID)
    step = 2.0 * np.pi / GRID
    z_table = cas(step * np.outer(np.arange(REGION), waves))
    z_forward = np.zeros((y_count, 2 * REGION, 2 * HALF))
    z_inverse = np.zeros((y_count, 2 * HALF, 2 * REGION))
    symbols = 4.0 * np.sin(np.pi * waves / GRID) ** 2
    shift = np.full((y_count, GRID, 2 * HALF), 1.0)
    y_forward = np.zeros((GRID, y_count, up_to(reach, 8)))
    y_inverse = np.zeros((y_count, up_to(reach, 16), GRID))
    for block in range(y_count):
        mine = z_table[:, block * depth : (block + 1) * depth]
        for half in range(2):
            rows = slice(half * REGION, (half + 1) * REGION)
            lanes = slice(half * HALF, half * HALF + depth)
            z_forward[block, rows, lanes] = mine
            z_inverse[block, lanes, rows] = mine.T / GRID
            shift[block, :, lanes] = (
                SCREEN + symbols[:, None] + symbols[None, block * depth : (block + 1) * depth]
            )
        cells = block * span_y - 2 + np.arange(reach)
        y_table = cas(step * np.outer(waves, cells))
        y_forward[:, block, :reach] = y_table
        y_inverse[block, :reach] = y_table.T / GRID
    y_forward = halves(y_forward.reshape(GRID, -1))
    y_forward = np.concatenate([y_forward[0], y_forward[0], y_forward[1]], axis=1)
    root = np.sqrt(shift * (shift + 4.0))
    decay = 2.0 / (2.0 + shift + root)
    log_decay = np.log(decay)
    ring = 1.0 / (1.0 - np.exp(GRID * log_decay))
    gain = KERNEL_GAIN / root
    modes = np.stack([decay, log_decay, ring, gain], axis=1).astype(np.float32)
    return (
        halves(z_forward),
        halves(z_inverse),
        y_forward,
        halves(y_inverse.reshape(-1, GRID)),
        modes,
    )


def weave_kernel(flag_ref, sample_ref, dipole_ref, source_out, sample_out):
    charged = flag_ref[...] == 1
    rows = []
    for depth in range(4):
        sample = sample_ref[pl.ds(depth, 16, stride=4), :]
        dipole = dipole_ref[pl.ds(depth, 16, stride=4), :]
        rows.append(jnp.concatenate([jnp.where(charged, -sample, dipole), sample], axis=0))
    weights = jnp.concatenate(rows, axis=1)
    first, rest = split(weights)
    second, third = split(weights - first.astype(F32))
    place = lax.broadcasted_iota(jnp.int32, (4 * BLOCK, 4 * BLOCK), 0)
    lane = lax.broadcasted_iota(jnp.int32, (4 * BLOCK, 4 * BLOCK), 1)
    wanted = 4 * (place % BLOCK) + place // BLOCK
    weave = jnp.where(lane == wanted, 1.0, 0.0).astype(BF16)
    woven = dot(first, weave) + (dot(second, weave) + dot(third, weave))
    for part in range(4):
        source_out[part] = woven[:16, part * BLOCK : (part + 1) * BLOCK]
        sample_out[part] = woven[16:, part * BLOCK : (part + 1) * BLOCK]


def weave(flag, sample, dipole):
    count = sample.shape[1]
    shape = jax.ShapeDtypeStruct((count // GROUP, 16, BLOCK), F32)
    columns = lambda rows: pl.BlockSpec((rows, BLOCK), lambda i: (0, i))
    out_block = pl.BlockSpec((BLOCK // GROUP, 16, BLOCK), lambda i: (i, 0, 0))
    return pl.pallas_call(
        weave_kernel,
        grid=(count // BLOCK,),
        in_specs=[columns(1), columns(64), columns(64)],
        out_specs=[out_block] * 2,
        out_shape=[shape, shape],
        compiler_params=params(),
        name="weave",
    )(flag.reshape(1, -1), sample, dipole)


def placed_weights(coeff_ref, panel, depth):
    held = coeff_ref[panel // GROUP]
    return pltpu.roll(held, (depth - (panel % GROUP) * 4) & (REGION - 1), 1)


def spread_kernel(reach, pieces, *refs):
    vector_ref, row_ref, depth_ref, rounded_ref, coeff_ref, high_ref, low_ref = refs[:7]
    outs = refs[7 : 7 + pieces]
    head = refs[7 + pieces]
    grids = refs[8 + pieces :]
    for grid in grids:
        grid[...] = jnp.zeros_like(grid)
    lanes = lax.broadcasted_iota(jnp.int32, (4, REGION), 1)
    chains = len(grids)

    def body(group, carry):
        for chain in range(chains):
            panel = group * chains + chain
            row = row_ref[panel]
            depth = depth_ref[panel]
            line = placed_weights(coeff_ref, panel, depth)
            offset = lanes - depth
            value = jnp.where((offset >= 0) & (offset < 4), vector_ref[panel], 0.0)
            places = [pl.ds(row + a * reach, 4) for a in range(4)]
            held = [grids[chain][place, :] for place in places]
            added = [line[4 * a : 4 * a + 4] * value for a in range(4)]
            for a in range(4):
                grids[chain][places[a], :] = held[a] + added[a]
        return carry

    lax.fori_loop(0, vector_ref.shape[0] // chains, body, 0, unroll=2)

    total = grids[0][...]
    for grid in grids[1:]:
        total = total + grid[...]
    half = total.shape[0] // 2
    both = jnp.concatenate([total[:half], total[half:]], axis=1)
    extra = outs[0].shape[0] - head.shape[0] - half
    if extra:
        both = jnp.concatenate([both, jnp.zeros((extra, 2 * REGION), F32)], axis=0)
    both = split(both)
    blocks = rounded_ref.shape[0]
    mantissa, exponent = encode_rounded(rounded_ref[...])
    head[...] = jnp.zeros_like(head)
    head[2 : 2 + blocks, :] = mantissa
    head[2 + blocks : 2 + 2 * blocks, :] = exponent
    mine = y_position()
    for piece in range(0, pieces, 2):
        pick = lambda ref: jnp.concatenate([ref[mine ^ piece], ref[mine ^ (piece + 1)]], axis=1)
        result = dot_three(both, (pick(high_ref), pick(low_ref)))
        send_piece(outs[piece], head, result[:, : 2 * HALF])
        send_piece(outs[piece + 1], head, result[:, 2 * HALF :])


def spread(vector, rows, depths, coeff, table, reach_x, reach_y):
    pieces = table[0].shape[0]
    line_count = reach_x * reach_y
    half = line_count // 2
    blocks = vector.shape[0] // BLOCK
    top = up_to(2 + 2 * blocks, 16)
    lanes = 2 * HALF
    return pl.pallas_call(
        functools.partial(spread_kernel, reach_y, pieces),
        in_specs=[in_smem()] * 3 + [whole_vmem()] * 4,
        out_specs=[whole_vmem()] * pieces,
        out_shape=[jax.ShapeDtypeStruct((top + up_to(half, 16), lanes), jnp.int16)] * pieces,
        scratch_shapes=[pltpu.VMEM((top, lanes), F32)]
        + [pltpu.VMEM((line_count, REGION), F32)] * CHAINS,
        compiler_params=params(),
        cost_estimate=cost(2 * half * 256 * 512, 4 * 16 * vector.shape[0] * REGION),
        name="spread",
    )(vector, rows, depths, vector.reshape(blocks, BLOCK), coeff, *table)


def forward_kernel(reach_x, reach_y, blocks, pieces, *refs):
    parts = refs[:pieces]
    table_ref, modes_ref = refs[pieces : pieces + 2]
    spectrum, right_out, left_out, own_out, peers_out = refs[pieces + 2 : pieces + 7]
    opened, stacked, slabs, head = refs[pieces + 7 :]
    half = reach_x // 2
    pitch = up_to(reach_y, 8)
    tall = pieces * pitch
    top = parts[0].shape[0] - opened.shape[0]
    mine = y_position()
    if pitch > reach_y:
        stacked[...] = jnp.zeros_like(stacked)
    head[...] = jnp.zeros_like(head)
    for piece in range(pieces):
        first = from_short(parts[piece][:top, :])
        mantissa, exponent = first[2 : 2 + blocks], first[2 + blocks : 2 + 2 * blocks]
        peers_out[piece * blocks : (piece + 1) * blocks, :] = decode_rounded(mantissa, exponent)
        at = 6 + 2 * piece * blocks
        head[at : at + blocks, :] = mantissa
        head[at + blocks : at + 2 * blocks, :] = exponent
        opened[...] = from_short(parts[piece][top:, :]) * unit(first[0:1], first[1:2])
        place = (mine ^ piece) * pitch
        for i in range(half):
            stacked[pl.ds(pl.multiple_of(i * tall + place, 8), reach_y), :] = opened[
                i * reach_y : (i + 1) * reach_y, :
            ]
    table = table_ref[...]

    def tripled(values):
        high, low = split(values)
        return jnp.concatenate([high, low, high], axis=0)

    for i in range(0, half, 2):
        if i + 1 < half:
            pair = jnp.concatenate(
                [stacked[i * tall : (i + 1) * tall, :], stacked[(i + 1) * tall : (i + 2) * tall, :]],
                axis=1,
            )
            both = dot(table, tripled(pair))
            spectrum[i] = both[:, : 2 * HALF]
            spectrum[i + 1] = both[:, 2 * HALF :]
        else:
            spectrum[i] = dot(table, tripled(stacked[i * tall : (i + 1) * tall, :]))

    chunk = 32

    def body(index, largest):
        rows = pl.ds(pl.multiple_of(index * chunk, chunk), chunk)
        low = low_lanes(chunk)
        decay = modes_ref[0, rows, :]
        log_decay = modes_ref[1, rows, :]
        across_half = jnp.exp(half * log_decay)
        across_cut = jnp.exp((half - 4) * log_decay)
        layers = [spectrum[i, rows, :] for i in range(half)]
        run = layers[0]
        cut_right = run
        for i in range(1, half):
            run = decay * run + layers[i]
            if i == half - 5:
                cut_right = run
        right = run
        run = layers[half - 1]
        cut_left = run
        for i in range(half - 2, -1, -1):
            run = decay * run + layers[i]
            if i == 4:
                cut_left = run
        left = run
        swapped_right, swapped_left = swap(right), swap(left)
        own = jnp.where(low, left + across_half * swapped_left, right + across_half * swapped_right)
        made = [
            jnp.where(low, swap(layers[half - 4]), layers[half - 3]),
            jnp.where(low, swap(layers[half - 2]), layers[half - 1]),
            jnp.where(low, own, cut_right + across_cut * swapped_right),
            jnp.where(low, layers[0], swap(layers[1])),
            jnp.where(low, layers[2], swap(layers[3])),
            jnp.where(low, cut_left + across_cut * swapped_left, own),
            own,
        ]
        for slab, values in enumerate(made):
            slabs[slab, rows, :] = values
        return tuple(
            jnp.maximum(old, jnp.max(jnp.abs(values).reshape(chunk // 8, 8, 2 * HALF), axis=0))
            for old, values in zip(largest, made)
        )

    zero = jnp.zeros((8, 2 * HALF), F32)
    largest = lax.fori_loop(0, GRID // chunk, body, (zero,) * 7)
    scales = [fit_scale(jnp.max(value, axis=0, keepdims=True)) for value in largest]
    head_rows = head.shape[0]
    for out, first in ((right_out, 0), (left_out, 3)):
        for slab in range(3):
            exponent, fraction = scales[first + slab]
            head[2 * slab : 2 * slab + 1, :] = exponent
            head[2 * slab + 1 : 2 * slab + 2, :] = fraction
            at = head_rows + slab * GRID
            out[at : at + GRID, :] = quantize(slabs[first + slab], exponent, fraction)
        out[:head_rows, :] = to_short(head[...])
    exponent, fraction = scales[6]
    head[0:1, :] = exponent
    head[1:2, :] = fraction
    own_out[:16, :] = to_short(head[:16, :])
    own_out[16:, :] = quantize(slabs[6], exponent, fraction)


def forward(parts, table, modes, reach_x, reach_y, blocks):
    pieces = len(parts)
    half = reach_x // 2
    lanes = 2 * HALF
    head = up_to(6 + 2 * pieces * blocks, 16)
    body = up_to(half * reach_y, 16)
    short = lambda rows: jax.ShapeDtypeStruct((rows, lanes), jnp.int16)
    return pl.pallas_call(
        functools.partial(forward_kernel, reach_x, reach_y, blocks, pieces),
        in_specs=[whole_vmem()] * (pieces + 2),
        out_specs=[whole_vmem()] * 5,
        out_shape=[
            jax.ShapeDtypeStruct((half, GRID, lanes), F32),
            short(head + 3 * GRID),
            short(head + 3 * GRID),
            short(16 + GRID),
            jax.ShapeDtypeStruct((pieces * blocks, BLOCK), F32),
        ],
        scratch_shapes=[
            pltpu.VMEM((body, lanes), F32),
            pltpu.VMEM((half * pieces * up_to(reach_y, 8), lanes), F32),
            pltpu.VMEM((7, GRID, lanes), F32),
            pltpu.VMEM((head, lanes), F32),
        ],
        compiler_params=params(),
        cost_estimate=cost(2 * half * 256 * 256 * 128, 4 * half * GRID * lanes * 2),
        name="forward",
    )(*parts, table, modes)


def inverse_kernel(reach_x, reach_y, pieces, fars, *refs):
    spectrum, from_left, from_right, own_ref = refs[:4]
    far_refs = refs[4 : 4 + fars]
    high_ref, low_ref, modes_ref = refs[4 + fars : 7 + fars]
    outs = refs[7 + fars : 7 + fars + pieces]
    field, blocks_out, ready, head = refs[7 + fars + pieces :]
    half = reach_x // 2
    span = reach_x - 4
    chunk = 16
    head_rows = from_left.shape[0] - 3 * GRID
    x_count = lax.axis_size("wide")
    x_index = lax.axis_index("wide")

    left_head = from_short(from_left[:16, :])
    right_head = from_short(from_right[:16, :])
    left_units = [unit(left_head[2 * s : 2 * s + 1], left_head[2 * s + 1 : 2 * s + 2]) for s in range(3)]
    right_units = [
        unit(right_head[2 * s : 2 * s + 1], right_head[2 * s + 1 : 2 * s + 2]) for s in range(3)
    ]
    far_units = []
    own_head = from_short(own_ref[:16, :])
    own_unit = unit(own_head[0:1], own_head[1:2])
    for far in far_refs:
        first = from_short(far[:16, :])
        far_units.append(unit(first[0:1], first[1:2]))
    powers = []
    for far, shift in enumerate(list(range(2, x_count - 1)) + [x_count - 1][: int(x_count > 2)]):
        if shift < x_count - 1:
            behind = jnp.where(x_index >= shift, shift, shift - x_count)
        else:
            behind = jnp.where(x_index == 0, -shift, jnp.where(x_index == shift, shift, 0))
        both = []
        for distance in (-behind, behind):
            ahead = span * distance - reach_x
            both.append(jnp.where(distance >= 2, ahead, ahead + GRID).astype(F32))
        powers.append(both)

    def body(index, carry):
        first = pl.multiple_of(index * chunk, chunk)
        rows = pl.ds(first, chunk)
        low = low_lanes(chunk)
        decay = modes_ref[0, rows, :]
        log_decay = modes_ref[1, rows, :]
        ring = modes_ref[2, rows, :]
        gain = modes_ref[3, rows, :]
        across_half = jnp.exp(half * log_decay)
        around = jnp.exp((GRID - 4) * log_decay)
        beside = jnp.exp((GRID - reach_x - span) * log_decay)
        layers = [spectrum[i, rows, :] for i in range(half)]

        def slab(ref, which, units):
            at = pl.ds(pl.multiple_of(head_rows + which * GRID + index * chunk, chunk), chunk)
            return from_short(ref[at, :]) * units[which]

        def moment(ref, scale):
            at = pl.ds(pl.multiple_of(16 + index * chunk, chunk), chunk)
            return from_short(ref[at, :]) * scale

        head_layers = [slab(from_left, 0, left_units), slab(from_left, 1, left_units)]
        tail_layers = [slab(from_right, 0, right_units), slab(from_right, 1, right_units)]
        zero = jnp.zeros_like(decay)
        from_head = [head_layers[0], swap(head_layers[0]), head_layers[1], swap(head_layers[1])]
        from_tail = [swap(tail_layers[0]), tail_layers[0], swap(tail_layers[1]), tail_layers[1]]
        head_sum = from_head[0]
        for i in range(1, 4):
            head_sum = decay * head_sum + from_head[i]
        tail_sum = from_tail[3]
        for i in range(2, -1, -1):
            tail_sum = decay * tail_sum + from_tail[i]
        for i in range(4):
            layers[i] = layers[i] + jnp.where(low, from_head[i], zero)
        for i in range(4):
            place = half - 4 + i
            layers[place] = layers[place] + jnp.where(low, zero, from_tail[i])
        total = moment(own_ref, own_unit) * jnp.exp((GRID - reach_x) * log_decay)
        one = jnp.ones_like(decay)
        total = total + slab(from_left, 2, left_units) * jnp.where(low, beside, one)
        total = total + slab(from_right, 2, right_units) * jnp.where(low, one, beside)
        for far in range(fars):
            power = jnp.where(low, powers[far][0], powers[far][1])
            total = total + moment(far_refs[far], far_units[far]) * jnp.exp(power * log_decay)
        entering = (swap(total) + around * jnp.where(low, head_sum, tail_sum)) * ring
        run = layers[0]
        for i in range(1, half):
            run = decay * run + layers[i]
        right_start = jnp.where(low, entering, swap(across_half * entering + run))
        run = layers[half - 1]
        for i in range(half - 2, -1, -1):
            run = decay * run + layers[i]
        left_start = jnp.where(low, swap(across_half * entering + run), entering)
        run = right_start
        forward_runs = []
        for i in range(half):
            run = decay * run + layers[i]
            forward_runs.append(run)
        run = left_start
        for i in range(half - 1, -1, -1):
            ahead = decay * run
            field[i, rows, :] = gain * (forward_runs[i] + ahead)
            run = ahead + layers[i]
        return carry

    lax.fori_loop(0, GRID // chunk, body, 0)
    table = (high_ref[...], low_ref[...])
    pitch = up_to(reach_y, 16)
    for i in range(0, half, 2):
        if i + 1 < half:
            pair = dot_three(table, split(jnp.concatenate([field[i], field[i + 1]], axis=1)))
            blocks_out[i] = pair[:, : 2 * HALF]
            blocks_out[i + 1] = pair[:, 2 * HALF :]
        else:
            blocks_out[i] = dot_three(table, split(field[i]))
    mine = y_position()
    if ready.shape[0] > half * reach_y:
        ready[half * reach_y :, :] = jnp.zeros_like(ready[half * reach_y :, :])
    head[...] = jnp.zeros_like(head)
    for piece in range(pieces):
        place = pl.ds(pl.multiple_of((mine ^ piece) * pitch, 16), reach_y)
        for i in range(half):
            ready[i * reach_y : (i + 1) * reach_y, :] = blocks_out[i, place, :]
        send_piece(outs[piece], head, ready[...])


def inverse(spectrum, from_left, from_right, own, fars, table, modes, reach_x, reach_y, pieces):
    half = reach_x // 2
    lanes = 2 * HALF
    body = up_to(half * reach_y, 16)
    return pl.pallas_call(
        functools.partial(inverse_kernel, reach_x, reach_y, pieces, len(fars)),
        in_specs=[whole_vmem()] * (7 + len(fars)),
        out_specs=[whole_vmem()] * pieces,
        out_shape=[jax.ShapeDtypeStruct((16 + body, lanes), jnp.int16)] * pieces,
        scratch_shapes=[
            pltpu.VMEM((half, GRID, lanes), F32),
            pltpu.VMEM((half, pieces * up_to(reach_y, 16), lanes), F32),
            pltpu.VMEM((body, lanes), F32),
            pltpu.VMEM((16, lanes), F32),
        ],
        compiler_params=params(),
        cost_estimate=cost(2 * half * 256 * 256 * 128, 4 * half * GRID * lanes * 2),
        name="inverse",
    )(spectrum, from_left, from_right, own, *fars, *table, modes)


def sample_kernel(reach, half_rows, pieces, row_ref, depth_ref, *refs):
    parts = refs[:pieces]
    high_ref, low_ref, coeff_ref, base_ref, near_ref, out_ref, field, sums = refs[pieces:]
    mine = y_position()
    opened = []
    for part in parts:
        first = from_short(part[:16, :])
        opened.append(from_short(part[16:, :]) * unit(first[0:1], first[1:2]))
    values = split(jnp.concatenate(opened, axis=1))
    pick = lambda ref: jnp.concatenate([ref[mine ^ piece] for piece in range(pieces)], axis=0)
    both = dot_three(values, (pick(high_ref), pick(low_ref)))
    field[:half_rows, :] = both[:half_rows, :REGION]
    field[half_rows:, :] = both[:half_rows, REGION:]
    lanes = lax.broadcasted_iota(jnp.int32, (1, REGION), 1)

    def body(panel, carry):
        row = row_ref[panel]
        depth = depth_ref[panel]
        line = placed_weights(coeff_ref, panel, depth)
        total = field[pl.ds(row, 4), :] * line[:4]
        for a in range(1, 4):
            total = total + field[pl.ds(row + a * reach, 4), :] * line[4 * a : 4 * a + 4]
        offset = lanes - depth
        total = jnp.sum(total, axis=0, keepdims=True)
        sums[pl.ds(panel, 1), :] = jnp.where((offset >= 0) & (offset < 4), total, 0.0)
        return carry

    count = row_ref.shape[0]
    lax.fori_loop(0, count, body, 0, unroll=8)
    sampled = lax.dot_general(
        jnp.ones((8, REGION), F32),
        sums[...],
        (((1,), (1,)), ((), ())),
        precision=lax.Precision.HIGHEST,
        preferred_element_type=F32,
    )
    for block in range(count // BLOCK):
        lane = slice(block * BLOCK, (block + 1) * BLOCK)
        out_ref[block : block + 1, :] = (
            base_ref[block : block + 1, :] + sampled[:1, lane] + near_ref[block : block + 1, :]
        )


def sample(rows, depths, parts, table, coeff, base, near, reach_x, reach_y):
    count = rows.shape[0]
    pieces = len(parts)
    half_rows = reach_x * reach_y // 2
    return pl.pallas_call(
        functools.partial(sample_kernel, reach_y, half_rows, pieces),
        in_specs=[in_smem()] * 2 + [whole_vmem()] * (pieces + 5),
        out_specs=whole_vmem(),
        out_shape=jax.ShapeDtypeStruct((count // BLOCK, BLOCK), F32),
        scratch_shapes=[
            pltpu.VMEM((2 * half_rows, REGION), F32),
            pltpu.VMEM((count, REGION), F32),
        ],
        compiler_params=params(),
        cost_estimate=cost(2 * half_rows * 256 * 512, 4 * 16 * count * REGION),
        name="sample",
    )(rows, depths, *parts, *table, coeff, base, near)


def near_kernel(slots, blocks, place_ref, target_ref, *refs):
    left_ref, right_ref, peers_ref, tile_ref, out_ref, held = refs
    count = peers_ref.shape[0]
    held[count : 2 * count, :] = peers_ref[...]
    for first, ref in ((0, left_ref), (2 * count, right_ref)):
        top = from_short(ref[...])
        for piece in range(count // blocks):
            at = 6 + 2 * piece * blocks
            held[first + piece * blocks : first + (piece + 1) * blocks, :] = decode_rounded(
                top[at : at + blocks], top[at + blocks : at + 2 * blocks]
            )
    out_ref[...] = jnp.zeros_like(out_ref)
    for slot in range(slots):
        picked = held[pl.ds(place_ref[slot], 1), :]
        picked = jnp.broadcast_to(picked, (16, BLOCK)).astype(BF16)
        product = lax.dot_general(
            picked,
            tile_ref[slot],
            (((1,), (1,)), ((), ())),
            preferred_element_type=F32,
        )
        target = pl.ds(target_ref[slot], 1)
        out_ref[target, :] = out_ref[target, :] + product[:1]


def near_field(places, targets, from_left, from_right, peers, tiles, blocks, out_rows):
    slots = tiles.shape[0]
    head = from_left.shape[0] - 3 * GRID
    constant = lambda shape: pl.BlockSpec(shape, lambda i: (0,) * len(shape))
    return pl.pallas_call(
        functools.partial(near_kernel, slots, blocks),
        grid=(1,),
        in_specs=[
            in_smem(),
            in_smem(),
            constant((head, BLOCK)),
            constant((head, BLOCK)),
            constant(peers.shape),
            constant(tiles.shape),
        ],
        out_specs=constant((out_rows, BLOCK)),
        out_shape=jax.ShapeDtypeStruct((out_rows, BLOCK), F32),
        scratch_shapes=[pltpu.VMEM((3 * peers.shape[0], BLOCK), F32)],
        compiler_params=params(),
        cost_estimate=cost(2 * slots * 16 * BLOCK * BLOCK, 2 * slots * BLOCK * BLOCK),
        name="near_field",
    )(places, targets, from_left, from_right, peers, tiles)


def shards(
    density,
    surface_flag,
    stencil_base,
    sample_weights,
    dipole_weights,
    near_target,
    near_source,
    near_tiles,
):
    x_count = lax.axis_size("wide")
    y_count = lax.axis_size(Y_AXES)
    x_index = lax.axis_index("wide")
    y_index = lax.axis_index(Y_AXES)
    span_x = REGION // x_count
    span_y = REGION // y_count
    reach_x = span_x + 4
    reach_y = span_y + 4
    count = density.shape[0]
    blocks = count // BLOCK

    z_forward, z_inverse, y_forward, y_inverse, modes = tables(y_count, span_y)
    modes = lax.dynamic_index_in_dim(jnp.asarray(modes), y_index, 0, keepdims=False)

    rows = (stencil_base[0] - (x_index * span_x - 2)) * reach_y + (
        stencil_base[1] - (y_index * span_y - 2)
    )
    depths = stencil_base[2]
    source_coeff, sample_coeff = weave(surface_flag, sample_weights, dipole_weights)
    own_share = jnp.where(surface_flag == 1, 0.0, 0.5).astype(F32)

    neighbour = near_source // blocks
    flip = (y_index + neighbour % 3 - 1) ^ y_index
    places = ((neighbour // 3) * y_count + flip) * blocks + near_source % blocks
    out_rows = up_to(blocks + 1, 8)
    live = near_target >= 0
    places = jnp.where(live, places, 0)
    targets = jnp.where(live, near_target, out_rows - 1)

    far_moves = [
        [(i, (i + shift) % x_count) for i in range(x_count)] for shift in range(2, x_count - 1)
    ]
    if x_count > 2:
        far_moves.append([(0, x_count - 1), (x_count - 1, 0)])
    to_right = [(i, i + 1) for i in range(x_count - 1)]
    to_left = [(i + 1, i) for i in range(x_count - 1)]

    def turn(parts):
        return [
            part
            if flip == 0
            else lax.ppermute(part, Y_AXES, [(i, i ^ flip) for i in range(y_count)])
            for flip, part in enumerate(parts)
        ]

    def apply_operator(vector):
        parts = turn(spread(vector, rows, depths, source_coeff, z_forward, reach_x, reach_y))
        spectrum, right_going, left_going, own, peers = forward(
            parts, y_forward, modes, reach_x, reach_y, blocks
        )
        from_left = lax.ppermute(right_going, "wide", to_right)
        from_right = lax.ppermute(left_going, "wide", to_left)
        fars = [lax.ppermute(own, "wide", pairs) for pairs in far_moves]
        near_part = near_field(
            places, targets, from_left, from_right, peers, near_tiles, blocks, out_rows
        )
        parts = turn(
            inverse(
                spectrum,
                from_left,
                from_right,
                own,
                fars,
                y_inverse,
                modes,
                reach_x,
                reach_y,
                y_count,
            )
        )
        base = (own_share * vector).reshape(blocks, BLOCK)
        return sample(
            rows, depths, parts, z_inverse, sample_coeff, base, near_part, reach_x, reach_y
        ).reshape(-1)

    first_image = apply_operator(density)
    second = apply_operator(first_image)
    return jnp.stack([first_image, second])


def solution(mesh):
    panels = P(("groups",) + ALL_AXES)
    columns = P(None, ("groups",) + ALL_AXES)
    in_specs = (
        panels,
        panels,
        columns,
        columns,
        columns,
        panels,
        panels,
        P(("groups",) + ALL_AXES, None, None),
    )
    return jax.shard_map(
        shards, mesh=mesh, in_specs=in_specs, out_specs=columns, check_vma=False
    )
```

```python
import functools
import math

import jax
import jax.numpy as jnp
import numpy as np
from jax import lax
from jax.experimental import pallas as pl
from jax.experimental.pallas import tpu as pltpu
from jax.sharding import PartitionSpec as P

GRID = 256
REGION = 128
BLOCK = 128
HALF = 64
KERNEL_GAIN = 4.0
SCREEN = 1.0 / 1024.0
LN2 = math.log(2.0)
Y_AXES = ("narrow", "pair")
ALL_AXES = ("wide", "narrow", "pair")
F32 = jnp.float32
BF16 = jnp.bfloat16
VMEM_LIMIT = 24 * 1024 * 1024
START_LIMIT = 56 * 1024 * 1024
GROUP = 32
CHAINS = 2


def cas(angles):
    return np.cos(angles) + np.sin(angles)


def up_to(count, multiple):
    return -(-count // multiple) * multiple


def low_lanes(rows):
    return lax.broadcasted_iota(jnp.int32, (rows, 2 * HALF), 1) < HALF


def swap(values):
    return pltpu.roll(values, HALF, 1)


def split(values):
    high = values.astype(BF16)
    return high, (values - high.astype(F32)).astype(BF16)


def dot(left, right):
    return jnp.dot(left, right, preferred_element_type=F32)


def dot_three(left, right):
    return dot(left[0], right[0]) + (dot(left[0], right[1]) + dot(left[1], right[0]))


def params():
    return pltpu.CompilerParams(vmem_limit_bytes=VMEM_LIMIT)


def whole_vmem():
    return pl.BlockSpec(memory_space=pltpu.VMEM)


def in_smem():
    return pl.BlockSpec(memory_space=pltpu.SMEM)


def cost(flops, moved):
    return pl.CostEstimate(flops=flops, bytes_accessed=moved, transcendentals=0)


def full_scale(exponent, fraction):
    return fraction * jnp.exp(exponent * LN2) * (1.0 / 1024.0)


def fit_scale(largest):
    largest = jnp.maximum(largest, 1e-30)
    exponent = jnp.floor(jnp.log(largest) * (1.0 / LN2))
    fraction = jnp.ceil(largest * jnp.exp(-exponent * LN2) * 1024.0) + 1.0
    return exponent, fraction


def to_short(values):
    return values.astype(jnp.int32).astype(jnp.int16)


def from_short(values):
    return values.astype(jnp.int32).astype(F32)


def quantize(values, exponent, fraction):
    return to_short(jnp.round(values * (32767.0 / full_scale(exponent, fraction))))


def unit(exponent, fraction):
    return full_scale(exponent, fraction) * (1.0 / 32767.0)


def encode_rounded(values):
    rounded = values.astype(BF16).astype(F32)
    size = jnp.maximum(jnp.abs(rounded), 1e-30)
    exponent = jnp.floor(jnp.log(size) * (1.0 / LN2))
    return jnp.round(rounded * jnp.exp((10.0 - exponent) * LN2)), exponent


def decode_rounded(mantissa, exponent):
    return (mantissa * jnp.exp((exponent - 10.0) * LN2)).astype(BF16).astype(F32)


def send_piece(out, head, values):
    exponent, fraction = fit_scale(jnp.max(jnp.abs(values), axis=0, keepdims=True))
    head[0:1, :] = exponent
    head[1:2, :] = fraction
    top = head.shape[0]
    out[:top, :] = to_short(head[...])
    out[top:, :] = quantize(values, exponent, fraction)


def y_position():
    return lax.axis_index("narrow") * lax.axis_size("pair") + lax.axis_index("pair")


def halves(table):
    high = table.astype(jnp.bfloat16)
    return high, (table - high.astype(np.float64)).astype(jnp.bfloat16)


def tables(y_count, span_y):
    depth = GRID // y_count
    reach = span_y + 4
    waves = np.arange(GRID)
    step = 2.0 * np.pi / GRID
    z_table = cas(step * np.outer(np.arange(REGION), waves))
    z_forward = np.zeros((y_count, 2 * REGION, 2 * HALF))
    z_inverse = np.zeros((y_count, 2 * HALF, 2 * REGION))
    symbols = 4.0 * np.sin(np.pi * waves / GRID) ** 2
    shift = np.full((y_count, GRID, 2 * HALF), 1.0)
    y_forward = np.zeros((GRID, y_count, up_to(reach, 8)))
    y_inverse = np.zeros((y_count, up_to(reach, 16), GRID))
    for block in range(y_count):
        mine = z_table[:, block * depth : (block + 1) * depth]
        for half in range(2):
            rows = slice(half * REGION, (half + 1) * REGION)
            lanes = slice(half * HALF, half * HALF + depth)
            z_forward[block, rows, lanes] = mine
            z_inverse[block, lanes, rows] = mine.T / GRID
            shift[block, :, lanes] = (
                SCREEN + symbols[:, None] + symbols[None, block * depth : (block + 1) * depth]
            )
        cells = block * span_y - 2 + np.arange(reach)
        y_table = cas(step * np.outer(waves, cells))
        y_forward[:, block, :reach] = y_table
        y_inverse[block, :reach] = y_table.T / GRID
    y_forward = halves(y_forward.reshape(GRID, -1))
    y_forward = np.concatenate([y_forward[0], y_forward[0], y_forward[1]], axis=1)
    root = np.sqrt(shift * (shift + 4.0))
    decay = 2.0 / (2.0 + shift + root)
    log_decay = np.log(decay)
    ring = 1.0 / (1.0 - np.exp(GRID * log_decay))
    gain = KERNEL_GAIN / root
    modes = np.stack([decay, log_decay, ring, gain], axis=1).astype(np.float32)
    return (
        halves(z_forward),
        halves(z_inverse),
        y_forward,
        halves(y_inverse.reshape(-1, GRID)),
        modes,
    )


def weave(flag, sample_refs, dipole_refs, source_out, sample_out):
    place = lax.broadcasted_iota(jnp.int32, (4 * BLOCK, 4 * BLOCK), 0)
    lane = lax.broadcasted_iota(jnp.int32, (4 * BLOCK, 4 * BLOCK), 1)
    wanted = 4 * (place % BLOCK) + place // BLOCK
    mixing = jnp.where(lane == wanted, 1.0, 0.0).astype(BF16)
    stacked = []
    for tile, (sample_ref, dipole_ref) in enumerate(zip(sample_refs, dipole_refs)):
        charged = flag[:, tile * BLOCK : (tile + 1) * BLOCK] == 1
        rows = []
        for depth in range(4):
            sample = sample_ref[pl.ds(depth, 16, stride=4), :]
            dipole = dipole_ref[pl.ds(depth, 16, stride=4), :]
            rows.append(jnp.concatenate([jnp.where(charged, -sample, dipole), sample], axis=0))
        stacked.append(jnp.concatenate(rows, axis=1))
    weights = jnp.concatenate(stacked, axis=0)
    first, rest = split(weights)
    second, third = split(weights - first.astype(F32))
    woven = dot(first, mixing) + (dot(second, mixing) + dot(third, mixing))
    for tile in range(len(sample_refs)):
        for which, out in enumerate((source_out, sample_out)):
            for part in range(BLOCK // GROUP):
                at = (tile * (BLOCK // GROUP) + part) * 16
                lanes = slice(part * BLOCK, (part + 1) * BLOCK)
                for a in range(4):
                    row = tile * 32 + which * 16 + 4 * a
                    out[pl.ds(at + 8 * (a // 2) + a % 2, 4, stride=2), :] = woven[
                        row : row + 4, lanes
                    ]


def pair_rows(x, reach_x, reach_y):
    even = (x // 2) * 2 * reach_y + x % 2
    if x == 0 or x == reach_x - 1:
        return [even]
    return [even, reach_x * reach_y + ((x - 1) // 2) * 2 * reach_y + (x - 1) % 2]


def pair_count(reach_x, reach_y):
    return (2 * reach_x - 2) * reach_y


def add_panels(reach, vector_ref, row_ref, depth_ref, coeff_ref, grids):
    lanes = lax.broadcasted_iota(jnp.int32, (8, REGION), 1)

    def body(group, carry):
        at = pl.multiple_of(group * 16, 16)
        coeff = [coeff_ref[pl.ds(at, 8), :], coeff_ref[pl.ds(at + 8, 8), :]]
        for local in range(GROUP):
            panel = group * GROUP + local
            grid = grids[local % len(grids)]
            row = row_ref[panel]
            depth = depth_ref[panel]
            shift = (depth - 4 * local) & (REGION - 1)
            value = jnp.where(((lanes - depth) & -4) == 0, vector_ref[panel], 0.0)
            places = [pl.ds(row, 8), pl.ds(row + 2 * reach, 8)]
            held = [grid[place, :] for place in places]
            for q in range(2):
                grid[places[q], :] = held[q] + pltpu.roll(coeff[q], shift, 1) * value
        return carry

    lax.fori_loop(0, vector_ref.shape[0] // GROUP, body, 0)


def spread_kernel(first, reach_x, reach_y, pieces, tiles, *refs):
    vector_ref, row_ref, depth_ref, rounded_ref, high_ref, low_ref = refs[:6]
    refs = refs[6:]
    if first:
        flag_ref, sample_refs, dipole_refs = refs[0], refs[1 : 1 + tiles], refs[1 + tiles : 1 + 2 * tiles]
        refs = refs[1 + 2 * tiles :]
    else:
        coeff_ref = refs[0]
        refs = refs[1:]
    outs, refs = refs[:pieces], refs[pieces:]
    if first:
        coeff_ref, sample_coeff_ref = refs[:2]
        refs = refs[2:]
        weave(flag_ref[...], sample_refs, dipole_refs, coeff_ref, sample_coeff_ref)
    head, total = refs[:2]
    grids = refs[2:]
    for grid in grids:
        grid[...] = jnp.zeros_like(grid)
    add_panels(reach_y, vector_ref, row_ref, depth_ref, coeff_ref, grids)
    for x in range(reach_x):
        parts = [
            grid[pl.ds(row, reach_y, stride=2), :]
            for row in pair_rows(x, reach_x, reach_y)
            for grid in grids
        ]
        total[x * reach_y : (x + 1) * reach_y, :] = sum(parts[1:], parts[0])
    half = reach_x * reach_y // 2
    both = jnp.concatenate([total[:half, :], total[half:, :]], axis=1)
    extra = outs[0].shape[0] - head.shape[0] - half
    if extra:
        both = jnp.concatenate([both, jnp.zeros((extra, 2 * REGION), F32)], axis=0)
    both = split(both)
    blocks = rounded_ref.shape[0]
    mantissa, exponent = encode_rounded(rounded_ref[...])
    head[...] = jnp.zeros_like(head)
    head[2 : 2 + blocks, :] = mantissa
    head[2 + blocks : 2 + 2 * blocks, :] = exponent
    mine = y_position()
    for piece in range(0, pieces, 2):
        pick = lambda ref: jnp.concatenate([ref[mine ^ piece], ref[mine ^ (piece + 1)]], axis=1)
        result = dot_three(both, (pick(high_ref), pick(low_ref)))
        send_piece(outs[piece], head, result[:, : 2 * HALF])
        send_piece(outs[piece + 1], head, result[:, 2 * HALF :])


def spread(vector, rows, depths, table, coeff, raw, reach_x, reach_y):
    pieces = table[0].shape[0]
    count = vector.shape[0]
    half = reach_x * reach_y // 2
    blocks = count // BLOCK
    top = up_to(2 + 2 * blocks, 16)
    lanes = 2 * HALF
    constant = lambda shape: pl.BlockSpec(shape, lambda i: (0,) * len(shape))
    piece = (top + up_to(half, 16), lanes)
    woven = (count // GROUP * 16, BLOCK)
    out_shapes = [jax.ShapeDtypeStruct(piece, jnp.int16)] * pieces
    operands = [vector, rows, depths, vector.reshape(blocks, BLOCK), *table]
    in_specs = [in_smem()] * 3 + [constant(value.shape) for value in operands[3:]]
    first = coeff is None
    if first:
        flag, sample, dipole = raw
        tile = lambda t: pl.BlockSpec((64, BLOCK), lambda i: (0, t))
        operands += [flag.reshape(1, -1)] + [sample] * blocks + [dipole] * blocks
        in_specs += [constant((1, count))] + [tile(t) for t in range(blocks)] * 2
        out_shapes += [jax.ShapeDtypeStruct(woven, F32)] * 2
    else:
        operands.append(coeff)
        in_specs.append(constant(woven))
    return pl.pallas_call(
        functools.partial(spread_kernel, first, reach_x, reach_y, pieces, blocks),
        grid=(1,),
        in_specs=in_specs,
        out_specs=[constant(out.shape) for out in out_shapes],
        out_shape=out_shapes,
        scratch_shapes=[
            pltpu.VMEM((top, lanes), F32),
            pltpu.VMEM((reach_x * reach_y, REGION), F32),
        ]
        + [pltpu.VMEM((pair_count(reach_x, reach_y), REGION), F32)] * CHAINS,
        compiler_params=pltpu.CompilerParams(
            vmem_limit_bytes=START_LIMIT if first else VMEM_LIMIT
        ),
        cost_estimate=cost(2 * half * 256 * 512, 4 * 16 * count * REGION),
        name="start" if first else "spread",
    )(*operands)


def forward_kernel(reach_x, reach_y, blocks, pieces, *refs):
    parts = refs[:pieces]
    table_ref, modes_ref = refs[pieces : pieces + 2]
    spectrum, right_out, left_out, own_out, peers_out = refs[pieces + 2 : pieces + 7]
    opened, stacked, slabs, head = refs[pieces + 7 :]
    half = reach_x // 2
    pitch = up_to(reach_y, 8)
    tall = pieces * pitch
    top = parts[0].shape[0] - opened.shape[0]
    mine = y_position()
    if pitch > reach_y:
        stacked[...] = jnp.zeros_like(stacked)
    head[...] = jnp.zeros_like(head)
    for piece in range(pieces):
        first = from_short(parts[piece][:top, :])
        mantissa, exponent = first[2 : 2 + blocks], first[2 + blocks : 2 + 2 * blocks]
        peers_out[piece * blocks : (piece + 1) * blocks, :] = decode_rounded(mantissa, exponent)
        at = 6 + 2 * piece * blocks
        head[at : at + blocks, :] = mantissa
        head[at + blocks : at + 2 * blocks, :] = exponent
        opened[...] = from_short(parts[piece][top:, :]) * unit(first[0:1], first[1:2])
        place = (mine ^ piece) * pitch
        for i in range(half):
            stacked[pl.ds(pl.multiple_of(i * tall + place, 8), reach_y), :] = opened[
                i * reach_y : (i + 1) * reach_y, :
            ]
    table = table_ref[...]

    def tripled(values):
        high, low = split(values)
        return jnp.concatenate([high, low, high], axis=0)

    for i in range(0, half, 2):
        if i + 1 < half:
            pair = jnp.concatenate(
                [stacked[i * tall : (i + 1) * tall, :], stacked[(i + 1) * tall : (i + 2) * tall, :]],
                axis=1,
            )
            both = dot(table, tripled(pair))
            spectrum[i] = both[:, : 2 * HALF]
            spectrum[i + 1] = both[:, 2 * HALF :]
        else:
            spectrum[i] = dot(table, tripled(stacked[i * tall : (i + 1) * tall, :]))

    chunk = 32

    def body(index, largest):
        rows = pl.ds(pl.multiple_of(index * chunk, chunk), chunk)
        low = low_lanes(chunk)
        decay = modes_ref[0, rows, :]
        log_decay = modes_ref[1, rows, :]
        across_half = jnp.exp(half * log_decay)
        across_cut = jnp.exp((half - 4) * log_decay)
        layers = [spectrum[i, rows, :] for i in range(half)]
        run = layers[0]
        cut_right = run
        for i in range(1, half):
            run = decay * run + layers[i]
            if i == half - 5:
                cut_right = run
        right = run
        run = layers[half - 1]
        cut_left = run
        for i in range(half - 2, -1, -1):
            run = decay * run + layers[i]
            if i == 4:
                cut_left = run
        left = run
        swapped_right, swapped_left = swap(right), swap(left)
        own = jnp.where(low, left + across_half * swapped_left, right + across_half * swapped_right)
        made = [
            jnp.where(low, swap(layers[half - 4]), layers[half - 3]),
            jnp.where(low, swap(layers[half - 2]), layers[half - 1]),
            jnp.where(low, own, cut_right + across_cut * swapped_right),
            jnp.where(low, layers[0], swap(layers[1])),
            jnp.where(low, layers[2], swap(layers[3])),
            jnp.where(low, cut_left + across_cut * swapped_left, own),
            own,
        ]
        for slab, values in enumerate(made):
            slabs[slab, rows, :] = values
        return tuple(
            jnp.maximum(old, jnp.max(jnp.abs(values).reshape(chunk // 8, 8, 2 * HALF), axis=0))
            for old, values in zip(largest, made)
        )

    zero = jnp.zeros((8, 2 * HALF), F32)
    largest = lax.fori_loop(0, GRID // chunk, body, (zero,) * 7)
    scales = [fit_scale(jnp.max(value, axis=0, keepdims=True)) for value in largest]
    head_rows = head.shape[0]
    for out, first in ((right_out, 0), (left_out, 3)):
        for slab in range(3):
            exponent, fraction = scales[first + slab]
            head[2 * slab : 2 * slab + 1, :] = exponent
            head[2 * slab + 1 : 2 * slab + 2, :] = fraction
            at = head_rows + slab * GRID
            out[at : at + GRID, :] = quantize(slabs[first + slab], exponent, fraction)
        out[:head_rows, :] = to_short(head[...])
    exponent, fraction = scales[6]
    head[0:1, :] = exponent
    head[1:2, :] = fraction
    own_out[:16, :] = to_short(head[:16, :])
    own_out[16:, :] = quantize(slabs[6], exponent, fraction)


def forward(parts, table, modes, reach_x, reach_y, blocks):
    pieces = len(parts)
    half = reach_x // 2
    lanes = 2 * HALF
    head = up_to(6 + 2 * pieces * blocks, 16)
    body = up_to(half * reach_y, 16)
    short = lambda rows: jax.ShapeDtypeStruct((rows, lanes), jnp.int16)
    return pl.pallas_call(
        functools.partial(forward_kernel, reach_x, reach_y, blocks, pieces),
        in_specs=[whole_vmem()] * (pieces + 2),
        out_specs=[whole_vmem()] * 5,
        out_shape=[
            jax.ShapeDtypeStruct((half, GRID, lanes), F32),
            short(head + 3 * GRID),
            short(head + 3 * GRID),
            short(16 + GRID),
            jax.ShapeDtypeStruct((pieces * blocks, BLOCK), F32),
        ],
        scratch_shapes=[
            pltpu.VMEM((body, lanes), F32),
            pltpu.VMEM((half * pieces * up_to(reach_y, 8), lanes), F32),
            pltpu.VMEM((7, GRID, lanes), F32),
            pltpu.VMEM((head, lanes), F32),
        ],
        compiler_params=params(),
        cost_estimate=cost(2 * half * 256 * 256 * 128, 4 * half * GRID * lanes * 2),
        name="forward",
    )(*parts, table, modes)


def inverse_kernel(reach_x, reach_y, pieces, fars, *refs):
    spectrum, from_left, from_right, own_ref = refs[:4]
    far_refs = refs[4 : 4 + fars]
    high_ref, low_ref, modes_ref = refs[4 + fars : 7 + fars]
    outs = refs[7 + fars : 7 + fars + pieces]
    field, blocks_out, ready, head = refs[7 + fars + pieces :]
    half = reach_x // 2
    span = reach_x - 4
    chunk = 16
    head_rows = from_left.shape[0] - 3 * GRID
    x_count = lax.axis_size("wide")
    x_index = lax.axis_index("wide")

    left_head = from_short(from_left[:16, :])
    right_head = from_short(from_right[:16, :])
    left_units = [unit(left_head[2 * s : 2 * s + 1], left_head[2 * s + 1 : 2 * s + 2]) for s in range(3)]
    right_units = [
        unit(right_head[2 * s : 2 * s + 1], right_head[2 * s + 1 : 2 * s + 2]) for s in range(3)
    ]
    far_units = []
    own_head = from_short(own_ref[:16, :])
    own_unit = unit(own_head[0:1], own_head[1:2])
    for far in far_refs:
        first = from_short(far[:16, :])
        far_units.append(unit(first[0:1], first[1:2]))
    powers = []
    for far, shift in enumerate(list(range(2, x_count - 1)) + [x_count - 1][: int(x_count > 2)]):
        if shift < x_count - 1:
            behind = jnp.where(x_index >= shift, shift, shift - x_count)
        else:
            behind = jnp.where(x_index == 0, -shift, jnp.where(x_index == shift, shift, 0))
        both = []
        for distance in (-behind, behind):
            ahead = span * distance - reach_x
            both.append(jnp.where(distance >= 2, ahead, ahead + GRID).astype(F32))
        powers.append(both)

    def body(index, carry):
        first = pl.multiple_of(index * chunk, chunk)
        rows = pl.ds(first, chunk)
        low = low_lanes(chunk)
        decay = modes_ref[0, rows, :]
        log_decay = modes_ref[1, rows, :]
        ring = modes_ref[2, rows, :]
        gain = modes_ref[3, rows, :]
        across_half = jnp.exp(half * log_decay)
        around = jnp.exp((GRID - 4) * log_decay)
        beside = jnp.exp((GRID - reach_x - span) * log_decay)
        layers = [spectrum[i, rows, :] for i in range(half)]

        def slab(ref, which, units):
            at = pl.ds(pl.multiple_of(head_rows + which * GRID + index * chunk, chunk), chunk)
            return from_short(ref[at, :]) * units[which]

        def moment(ref, scale):
            at = pl.ds(pl.multiple_of(16 + index * chunk, chunk), chunk)
            return from_short(ref[at, :]) * scale

        head_layers = [slab(from_left, 0, left_units), slab(from_left, 1, left_units)]
        tail_layers = [slab(from_right, 0, right_units), slab(from_right, 1, right_units)]
        zero = jnp.zeros_like(decay)
        from_head = [head_layers[0], swap(head_layers[0]), head_layers[1], swap(head_layers[1])]
        from_tail = [swap(tail_layers[0]), tail_layers[0], swap(tail_layers[1]), tail_layers[1]]
        head_sum = from_head[0]
        for i in range(1, 4):
            head_sum = decay * head_sum + from_head[i]
        tail_sum = from_tail[3]
        for i in range(2, -1, -1):
            tail_sum = decay * tail_sum + from_tail[i]
        for i in range(4):
            layers[i] = layers[i] + jnp.where(low, from_head[i], zero)
        for i in range(4):
            place = half - 4 + i
            layers[place] = layers[place] + jnp.where(low, zero, from_tail[i])
        total = moment(own_ref, own_unit) * jnp.exp((GRID - reach_x) * log_decay)
        one = jnp.ones_like(decay)
        total = total + slab(from_left, 2, left_units) * jnp.where(low, beside, one)
        total = total + slab(from_right, 2, right_units) * jnp.where(low, one, beside)
        for far in range(fars):
            power = jnp.where(low, powers[far][0], powers[far][1])
            total = total + moment(far_refs[far], far_units[far]) * jnp.exp(power * log_decay)
        entering = (swap(total) + around * jnp.where(low, head_sum, tail_sum)) * ring
        run = layers[0]
        for i in range(1, half):
            run = decay * run + layers[i]
        right_start = jnp.where(low, entering, swap(across_half * entering + run))
        run = layers[half - 1]
        for i in range(half - 2, -1, -1):
            run = decay * run + layers[i]
        left_start = jnp.where(low, swap(across_half * entering + run), entering)
        run = right_start
        forward_runs = []
        for i in range(half):
            run = decay * run + layers[i]
            forward_runs.append(run)
        run = left_start
        for i in range(half - 1, -1, -1):
            ahead = decay * run
            field[i, rows, :] = gain * (forward_runs[i] + ahead)
            run = ahead + layers[i]
        return carry

    lax.fori_loop(0, GRID // chunk, body, 0)
    table = (high_ref[...], low_ref[...])
    pitch = up_to(reach_y, 16)
    for i in range(0, half, 2):
        if i + 1 < half:
            pair = dot_three(table, split(jnp.concatenate([field[i], field[i + 1]], axis=1)))
            blocks_out[i] = pair[:, : 2 * HALF]
            blocks_out[i + 1] = pair[:, 2 * HALF :]
        else:
            blocks_out[i] = dot_three(table, split(field[i]))
    mine = y_position()
    if ready.shape[0] > half * reach_y:
        ready[half * reach_y :, :] = jnp.zeros_like(ready[half * reach_y :, :])
    head[...] = jnp.zeros_like(head)
    for piece in range(pieces):
        place = pl.ds(pl.multiple_of((mine ^ piece) * pitch, 16), reach_y)
        for i in range(half):
            ready[i * reach_y : (i + 1) * reach_y, :] = blocks_out[i, place, :]
        send_piece(outs[piece], head, ready[...])


def inverse(spectrum, from_left, from_right, own, fars, table, modes, reach_x, reach_y, pieces):
    half = reach_x // 2
    lanes = 2 * HALF
    body = up_to(half * reach_y, 16)
    return pl.pallas_call(
        functools.partial(inverse_kernel, reach_x, reach_y, pieces, len(fars)),
        in_specs=[whole_vmem()] * (7 + len(fars)),
        out_specs=[whole_vmem()] * pieces,
        out_shape=[jax.ShapeDtypeStruct((16 + body, lanes), jnp.int16)] * pieces,
        scratch_shapes=[
            pltpu.VMEM((half, GRID, lanes), F32),
            pltpu.VMEM((half, pieces * up_to(reach_y, 16), lanes), F32),
            pltpu.VMEM((body, lanes), F32),
            pltpu.VMEM((16, lanes), F32),
        ],
        compiler_params=params(),
        cost_estimate=cost(2 * half * 256 * 256 * 128, 4 * half * GRID * lanes * 2),
        name="inverse",
    )(spectrum, from_left, from_right, own, *fars, *table, modes)


def sum_rows(values):
    row = lax.broadcasted_iota(jnp.int32, values[0].shape, 0)
    for step in (4, 2, 1):
        low = (row & step) == 0
        paired = []
        for one, other in zip(values[: len(values) // 2], values[len(values) // 2 :]):
            kept = jnp.where(low, one, other)
            moved = jnp.where(low, other, one)
            if step == 4:
                moved = pltpu.roll(moved, 4, 0)
            else:
                moved = jnp.where(low, pltpu.roll(moved, 8 - step, 0), pltpu.roll(moved, step, 0))
            paired.append(kept + moved)
        values = paired
    return values[0]


def sample_kernel(last, reach_x, reach_y, pieces, row_ref, depth_ref, *refs):
    parts = refs[:pieces]
    high_ref, low_ref, coeff_ref, own_ref, vector_ref, near_ref, out_ref, flat, field, sums = refs[
        pieces:
    ]
    mine = y_position()
    half_rows = reach_x * reach_y // 2
    opened = []
    for part in parts:
        first = from_short(part[:16, :])
        opened.append(from_short(part[16:, :]) * unit(first[0:1], first[1:2]))
    values = split(jnp.concatenate(opened, axis=1))
    pick = lambda ref: jnp.concatenate([ref[mine ^ piece] for piece in range(pieces)], axis=0)
    both = dot_three(values, (pick(high_ref), pick(low_ref)))
    flat[:half_rows, :] = both[:half_rows, :REGION]
    flat[half_rows:, :] = both[:half_rows, REGION:]
    for x in range(reach_x):
        layer = flat[x * reach_y : (x + 1) * reach_y, :]
        for row in pair_rows(x, reach_x, reach_y):
            field[pl.ds(row, reach_y, stride=2), :] = layer
    lanes = lax.broadcasted_iota(jnp.int32, (8, REGION), 1)

    def body(group, carry):
        at = pl.multiple_of(group * 16, 16)
        coeff = [coeff_ref[pl.ds(at, 8), :], coeff_ref[pl.ds(at + 8, 8), :]]
        for eight in range(0, GROUP, 8):
            totals = []
            for local in range(eight, eight + 8):
                panel = group * GROUP + local
                row = row_ref[panel]
                depth = depth_ref[panel]
                shift = (depth - 4 * local) & (REGION - 1)
                total = field[pl.ds(row, 8), :] * pltpu.roll(coeff[0], shift, 1)
                total = total + field[pl.ds(row + 2 * reach_y, 8), :] * pltpu.roll(
                    coeff[1], shift, 1
                )
                totals.append(jnp.where(((lanes - depth) & -4) == 0, total, 0.0))
            sums[pl.ds(pl.multiple_of(group * GROUP + eight, 8), 8), :] = sum_rows(totals)
        return carry

    count = row_ref.shape[0]
    lax.fori_loop(0, count // GROUP, body, 0)
    sampled = lax.dot_general(
        jnp.ones((8, REGION), F32),
        sums[...],
        (((1,), (1,)), ((), ())),
        precision=lax.Precision.HIGHEST,
        preferred_element_type=F32,
    )
    for block in range(count // BLOCK):
        lane = slice(block * BLOCK, (block + 1) * BLOCK)
        row = slice(block, block + 1)
        vector = vector_ref[row, :]
        image = jnp.where(own_ref[row, :] == 1, 0.0, 0.5 * vector) + sampled[:1, lane]
        image = image + near_ref[row, :]
        if last:
            out_ref[0:1, lane] = vector
            out_ref[1:2, lane] = image
        else:
            out_ref[row, :] = image


def sample(last, rows, depths, parts, table, coeff, flag, vector, near, reach_x, reach_y):
    count = rows.shape[0]
    blocks = count // BLOCK
    pieces = len(parts)
    shape = (2, count) if last else (blocks, BLOCK)
    return pl.pallas_call(
        functools.partial(sample_kernel, last, reach_x, reach_y, pieces),
        in_specs=[in_smem()] * 2 + [whole_vmem()] * (pieces + 6),
        out_specs=whole_vmem(),
        out_shape=jax.ShapeDtypeStruct(shape, F32),
        scratch_shapes=[
            pltpu.VMEM((reach_x * reach_y, REGION), F32),
            pltpu.VMEM((pair_count(reach_x, reach_y), REGION), F32),
            pltpu.VMEM((count, REGION), F32),
        ],
        compiler_params=params(),
        cost_estimate=cost(reach_x * reach_y * 256 * 512, 4 * 16 * count * REGION),
        name="sample",
    )(
        rows,
        depths,
        *parts,
        *table,
        coeff,
        flag.reshape(blocks, BLOCK),
        vector.reshape(blocks, BLOCK),
        near,
    )


def near_kernel(slots, blocks, place_ref, target_ref, *refs):
    left_ref, right_ref, peers_ref, tile_ref, out_ref, held = refs
    count = peers_ref.shape[0]
    held[count : 2 * count, :] = peers_ref[...]
    for first, ref in ((0, left_ref), (2 * count, right_ref)):
        top = from_short(ref[...])
        for piece in range(count // blocks):
            at = 6 + 2 * piece * blocks
            held[first + piece * blocks : first + (piece + 1) * blocks, :] = decode_rounded(
                top[at : at + blocks], top[at + blocks : at + 2 * blocks]
            )
    out_ref[...] = jnp.zeros_like(out_ref)
    for slot in range(slots):
        picked = held[pl.ds(place_ref[slot], 1), :]
        picked = jnp.broadcast_to(picked, (16, BLOCK)).astype(BF16)
        product = lax.dot_general(
            picked,
            tile_ref[slot],
            (((1,), (1,)), ((), ())),
            preferred_element_type=F32,
        )
        target = pl.ds(target_ref[slot], 1)
        out_ref[target, :] = out_ref[target, :] + product[:1]


def near_field(places, targets, from_left, from_right, peers, tiles, blocks, out_rows):
    slots = tiles.shape[0]
    head = from_left.shape[0] - 3 * GRID
    constant = lambda shape: pl.BlockSpec(shape, lambda i: (0,) * len(shape))
    return pl.pallas_call(
        functools.partial(near_kernel, slots, blocks),
        grid=(1,),
        in_specs=[
            in_smem(),
            in_smem(),
            constant((head, BLOCK)),
            constant((head, BLOCK)),
            constant(peers.shape),
            constant(tiles.shape),
        ],
        out_specs=constant((out_rows, BLOCK)),
        out_shape=jax.ShapeDtypeStruct((out_rows, BLOCK), F32),
        scratch_shapes=[pltpu.VMEM((3 * peers.shape[0], BLOCK), F32)],
        compiler_params=params(),
        cost_estimate=cost(2 * slots * 16 * BLOCK * BLOCK, 2 * slots * BLOCK * BLOCK),
        name="near_field",
    )(places, targets, from_left, from_right, peers, tiles)


def shards(
    density,
    surface_flag,
    stencil_base,
    sample_weights,
    dipole_weights,
    near_target,
    near_source,
    near_tiles,
):
    x_count = lax.axis_size("wide")
    y_count = lax.axis_size(Y_AXES)
    x_index = lax.axis_index("wide")
    y_index = lax.axis_index(Y_AXES)
    span_x = REGION // x_count
    span_y = REGION // y_count
    reach_x = span_x + 4
    reach_y = span_y + 4
    count = density.shape[0]
    blocks = count // BLOCK

    z_forward, z_inverse, y_forward, y_inverse, modes = tables(y_count, span_y)
    modes = lax.dynamic_index_in_dim(jnp.asarray(modes), y_index, 0, keepdims=False)

    local_x = stencil_base[0] - (x_index * span_x - 2)
    local_y = stencil_base[1] - (y_index * span_y - 2)
    rows = (
        (local_x % 2) * (reach_x * reach_y) + (local_x // 2) * (2 * reach_y) + 2 * local_y
    )
    depths = stencil_base[2]

    neighbour = near_source // blocks
    flip = (y_index + neighbour % 3 - 1) ^ y_index
    places = ((neighbour // 3) * y_count + flip) * blocks + near_source % blocks
    out_rows = up_to(blocks + 1, 8)
    live = near_target >= 0
    places = jnp.where(live, places, 0)
    targets = jnp.where(live, near_target, out_rows - 1)

    far_moves = [
        [(i, (i + shift) % x_count) for i in range(x_count)] for shift in range(2, x_count - 1)
    ]
    if x_count > 2:
        far_moves.append([(0, x_count - 1), (x_count - 1, 0)])
    to_right = [(i, i + 1) for i in range(x_count - 1)]
    to_left = [(i + 1, i) for i in range(x_count - 1)]

    def turn(parts):
        return [
            part
            if flip == 0
            else lax.ppermute(part, Y_AXES, [(i, i ^ flip) for i in range(y_count)])
            for flip, part in enumerate(parts)
        ]

    def convolve_and_sample(last, vector, sent, sample_coeff):
        spectrum, right_going, left_going, own, peers = forward(
            turn(sent), y_forward, modes, reach_x, reach_y, blocks
        )
        from_left = lax.ppermute(right_going, "wide", to_right)
        from_right = lax.ppermute(left_going, "wide", to_left)
        fars = [lax.ppermute(own, "wide", pairs) for pairs in far_moves]
        near_part = near_field(
            places, targets, from_left, from_right, peers, near_tiles, blocks, out_rows
        )
        parts = inverse(
            spectrum,
            from_left,
            from_right,
            own,
            fars,
            y_inverse,
            modes,
            reach_x,
            reach_y,
            y_count,
        )
        return sample(
            last,
            rows,
            depths,
            turn(parts),
            z_inverse,
            sample_coeff,
            surface_flag,
            vector,
            near_part,
            reach_x,
            reach_y,
        )

    raw = (surface_flag, sample_weights, dipole_weights)
    *sent, source_coeff, sample_coeff = spread(
        density, rows, depths, z_forward, None, raw, reach_x, reach_y
    )
    first_image = convolve_and_sample(False, density, sent, sample_coeff).reshape(-1)
    sent = spread(first_image, rows, depths, z_forward, source_coeff, None, reach_x, reach_y)
    return convolve_and_sample(True, first_image, sent, sample_coeff)


def solution(mesh):
    panels = P(("groups",) + ALL_AXES)
    columns = P(None, ("groups",) + ALL_AXES)
    in_specs = (
        panels,
        panels,
        columns,
        columns,
        columns,
        panels,
        panels,
        P(("groups",) + ALL_AXES, None, None),
    )
    return jax.shard_map(
        shards, mesh=mesh, in_specs=in_specs, out_specs=columns, check_vma=False
    )
```

```python
import functools
import math

import jax
import jax.numpy as jnp
import numpy as np
from jax import lax
from jax.experimental import pallas as pl
from jax.experimental.pallas import tpu as pltpu
from jax.sharding import PartitionSpec as P

GRID = 256
REGION = 128
BLOCK = 128
HALF = 64
KERNEL_GAIN = 4.0
SCREEN = 1.0 / 1024.0
LN2 = math.log(2.0)
Y_AXES = ("narrow", "pair")
ALL_AXES = ("wide", "narrow", "pair")
F32 = jnp.float32
BF16 = jnp.bfloat16
VMEM_LIMIT = 24 * 1024 * 1024
START_LIMIT = 56 * 1024 * 1024
GROUP = 32
CHAINS = 2


def cas(angles):
    return np.cos(angles) + np.sin(angles)


def up_to(count, multiple):
    return -(-count // multiple) * multiple


def low_lanes(rows):
    return lax.broadcasted_iota(jnp.int32, (rows, 2 * HALF), 1) < HALF


def swap(values):
    return pltpu.roll(values, HALF, 1)


def split(values):
    high = values.astype(BF16)
    return high, (values - high.astype(F32)).astype(BF16)


def dot(left, right):
    return jnp.dot(left, right, preferred_element_type=F32)


def dot_three(left, right):
    return dot(left[0], right[0]) + (dot(left[0], right[1]) + dot(left[1], right[0]))


def params():
    return pltpu.CompilerParams(vmem_limit_bytes=VMEM_LIMIT)


def whole_vmem():
    return pl.BlockSpec(memory_space=pltpu.VMEM)


def in_smem():
    return pl.BlockSpec(memory_space=pltpu.SMEM)


def cost(flops, moved):
    return pl.CostEstimate(flops=flops, bytes_accessed=moved, transcendentals=0)


def full_scale(exponent, fraction):
    return fraction * jnp.exp(exponent * LN2) * (1.0 / 1024.0)


def fit_scale(largest):
    largest = jnp.maximum(largest, 1e-30)
    exponent = jnp.floor(jnp.log(largest) * (1.0 / LN2))
    fraction = jnp.ceil(largest * jnp.exp(-exponent * LN2) * 1024.0) + 1.0
    return exponent, fraction


def to_short(values):
    return values.astype(jnp.int32).astype(jnp.int16)


def from_short(values):
    return values.astype(jnp.int32).astype(F32)


def quantize(values, exponent, fraction):
    return to_short(jnp.round(values * (32767.0 / full_scale(exponent, fraction))))


def unit(exponent, fraction):
    return full_scale(exponent, fraction) * (1.0 / 32767.0)


def encode_rounded(values):
    rounded = values.astype(BF16).astype(F32)
    size = jnp.maximum(jnp.abs(rounded), 1e-30)
    exponent = jnp.floor(jnp.log(size) * (1.0 / LN2))
    return jnp.round(rounded * jnp.exp((10.0 - exponent) * LN2)), exponent


def decode_rounded(mantissa, exponent):
    return (mantissa * jnp.exp((exponent - 10.0) * LN2)).astype(BF16).astype(F32)


def send_piece(out, head, values):
    exponent, fraction = fit_scale(jnp.max(jnp.abs(values), axis=0, keepdims=True))
    head[0:1, :] = exponent
    head[1:2, :] = fraction
    top = head.shape[0]
    out[:top, :] = to_short(head[...])
    out[top:, :] = quantize(values, exponent, fraction)


def y_position():
    return lax.axis_index("narrow") * lax.axis_size("pair") + lax.axis_index("pair")


def halves(table):
    high = table.astype(jnp.bfloat16)
    return high, (table - high.astype(np.float64)).astype(jnp.bfloat16)


def tables(y_count, span_y):
    depth = GRID // y_count
    reach = span_y + 4
    waves = np.arange(GRID)
    step = 2.0 * np.pi / GRID
    z_table = cas(step * np.outer(np.arange(REGION), waves))
    z_forward = np.zeros((y_count, 2 * REGION, 2 * HALF))
    z_inverse = np.zeros((y_count, 2 * HALF, 2 * REGION))
    symbols = 4.0 * np.sin(np.pi * waves / GRID) ** 2
    shift = np.full((y_count, GRID, 2 * HALF), 1.0)
    y_forward = np.zeros((GRID, y_count, up_to(reach, 8)))
    y_inverse = np.zeros((y_count, up_to(reach, 16), GRID))
    for block in range(y_count):
        mine = z_table[:, block * depth : (block + 1) * depth]
        for half in range(2):
            rows = slice(half * REGION, (half + 1) * REGION)
            lanes = slice(half * HALF, half * HALF + depth)
            z_forward[block, rows, lanes] = mine
            z_inverse[block, lanes, rows] = mine.T / GRID
            shift[block, :, lanes] = (
                SCREEN + symbols[:, None] + symbols[None, block * depth : (block + 1) * depth]
            )
        cells = block * span_y - 2 + np.arange(reach)
        y_table = cas(step * np.outer(waves, cells))
        y_forward[:, block, :reach] = y_table
        y_inverse[block, :reach] = y_table.T / GRID
    y_forward = halves(y_forward.reshape(GRID, -1))
    y_forward = np.concatenate([y_forward[0], y_forward[0], y_forward[1]], axis=1)
    root = np.sqrt(shift * (shift + 4.0))
    decay = 2.0 / (2.0 + shift + root)
    log_decay = np.log(decay)
    ring = 1.0 / (1.0 - np.exp(GRID * log_decay))
    gain = KERNEL_GAIN / root
    modes = np.stack([decay, log_decay, ring, gain], axis=1).astype(np.float32)
    return (
        halves(z_forward),
        halves(z_inverse),
        y_forward,
        halves(y_inverse),
        modes,
    )


def weave(flag, sample_refs, dipole_refs, source_out, sample_out):
    place = lax.broadcasted_iota(jnp.int32, (4 * BLOCK, 4 * BLOCK), 0)
    lane = lax.broadcasted_iota(jnp.int32, (4 * BLOCK, 4 * BLOCK), 1)
    wanted = 4 * (place % BLOCK) + place // BLOCK
    mixing = jnp.where(lane == wanted, 1.0, 0.0).astype(BF16)
    stacked = []
    for tile, (sample_ref, dipole_ref) in enumerate(zip(sample_refs, dipole_refs)):
        charged = flag[:, tile * BLOCK : (tile + 1) * BLOCK] == 1
        rows = []
        for depth in range(4):
            sample = sample_ref[pl.ds(depth, 16, stride=4), :]
            dipole = dipole_ref[pl.ds(depth, 16, stride=4), :]
            rows.append(jnp.concatenate([jnp.where(charged, -sample, dipole), sample], axis=0))
        stacked.append(jnp.concatenate(rows, axis=1))
    weights = jnp.concatenate(stacked, axis=0)
    first, rest = split(weights)
    second, third = split(weights - first.astype(F32))
    woven = dot(first, mixing) + (dot(second, mixing) + dot(third, mixing))
    for tile in range(len(sample_refs)):
        for which, out in enumerate((source_out, sample_out)):
            for part in range(BLOCK // GROUP):
                at = (tile * (BLOCK // GROUP) + part) * 16
                lanes = slice(part * BLOCK, (part + 1) * BLOCK)
                for a in range(4):
                    row = tile * 32 + which * 16 + 4 * a
                    out[pl.ds(at + 8 * (a // 2) + a % 2, 4, stride=2), :] = woven[
                        row : row + 4, lanes
                    ]


def pair_rows(x, reach_x, reach_y):
    even = (x // 2) * 2 * reach_y + x % 2
    if x == 0 or x == reach_x - 1:
        return [even]
    return [even, reach_x * reach_y + ((x - 1) // 2) * 2 * reach_y + (x - 1) % 2]


def pair_count(reach_x, reach_y):
    return (2 * reach_x - 2) * reach_y


def in_window(lanes, depth):
    return ((lanes - depth) & -4) == 0


def add_panels(reach, woven, vector_ref, place_ref, weight_ref, grids):
    lanes = lax.broadcasted_iota(jnp.int32, (8, REGION), 1)

    def body(group, carry):
        at = pl.multiple_of(group * 16, 16)
        coeff = [weight_ref[pl.ds(at + 8 * q, 8), :] for q in range(2)] if woven else None
        for local in range(GROUP):
            panel = group * GROUP + local
            grid = grids[local % len(grids)]
            row = place_ref[0, panel]
            value = vector_ref[panel]
            if woven:
                depth = place_ref[1, panel]
                shift = (depth - 4 * local) & (REGION - 1)
                value = jnp.where(in_window(lanes, depth), value, 0.0)
                lines = [pltpu.roll(coeff[q], shift, 1) for q in range(2)]
            else:
                first = pl.multiple_of(panel * 16, 16)
                lines = [weight_ref[pl.ds(first + 8 * q, 8), :] for q in range(2)]
            places = [pl.ds(row, 8), pl.ds(row + 2 * reach, 8)]
            held = [grid[place, :] for place in places]
            for q in range(2):
                grid[places[q], :] = held[q] + lines[q] * value
        return carry

    lax.fori_loop(0, vector_ref.shape[0] // GROUP, body, 0)


def send_pieces(outs, flips, head, rounded, both, high_ref, low_ref):
    blocks = rounded.shape[0]
    mantissa, exponent = encode_rounded(rounded)
    head[...] = jnp.zeros_like(head)
    head[2 : 2 + blocks, :] = mantissa
    head[2 + blocks : 2 + 2 * blocks, :] = exponent
    mine = y_position()
    for at in range(0, len(flips), 2):
        pick = lambda ref: jnp.concatenate([ref[mine ^ flip] for flip in flips[at : at + 2]], axis=1)
        result = dot_three(both, (pick(high_ref), pick(low_ref)))
        for i, out in enumerate(outs[at : at + 2]):
            send_piece(out, head, result[:, i * 2 * HALF : (i + 1) * 2 * HALF])


def spread_kernel(first, reach_x, reach_y, flips, tiles, *refs):
    vector_ref, rounded_ref, high_ref, low_ref = refs[:4]
    refs = refs[4:]
    if first:
        stencil_ref, flag_ref = refs[:2]
        sample_refs, dipole_refs = refs[2 : 2 + tiles], refs[2 + tiles : 2 + 2 * tiles]
        refs = refs[2 + 2 * tiles :]
    else:
        place_ref, weight_ref = refs[:2]
        refs = refs[2:]
    outs, (wide_high, wide_low), refs = refs[: len(flips)], refs[len(flips) :][:2], refs[len(flips) + 2 :]
    if first:
        weight_ref, sample_coeff_ref, places_out = refs[:3]
        place_ref, sem = refs[-2:]
        refs = refs[3:-2]
        span_x, span_y = reach_x - 4, reach_y - 4
        local_x = stencil_ref[0:1, :] - (lax.axis_index("wide") * span_x - 2)
        local_y = stencil_ref[1:2, :] - (y_position() * span_y - 2)
        odd = local_x & 1
        places_out[0:1, :] = (
            odd * (reach_x * reach_y) + (local_x >> 1) * (2 * reach_y) + 2 * local_y
        )
        places_out[1:2, :] = stencil_ref[2:3, :]
        copy = pltpu.make_async_copy(places_out, place_ref, sem)
        copy.start()
    head, total = refs[:2]
    grids = refs[2:]
    for grid in grids:
        grid[...] = jnp.zeros_like(grid)
    if first:
        weave(flag_ref[...], sample_refs, dipole_refs, weight_ref, sample_coeff_ref)
        copy.wait()
    add_panels(reach_y, first, vector_ref, place_ref, weight_ref, grids)
    for x in range(reach_x):
        parts = [
            grid[pl.ds(row, reach_y, stride=2), :]
            for row in pair_rows(x, reach_x, reach_y)
            for grid in grids
        ]
        total[x * reach_y : (x + 1) * reach_y, :] = sum(parts[1:], parts[0])
    half = reach_x * reach_y // 2
    both = jnp.concatenate([total[:half, :], total[half:, :]], axis=1)
    extra = wide_high.shape[0] - half
    if extra:
        both = jnp.concatenate([both, jnp.zeros((extra, 2 * REGION), F32)], axis=0)
    high, low = split(both)
    wide_high[...] = high
    wide_low[...] = low
    send_pieces(outs, flips, head, rounded_ref[...], (high, low), high_ref, low_ref)


def spread(vector, places, table, lines, raw, reach_x, reach_y, flips):
    count = vector.shape[0]
    half = reach_x * reach_y // 2
    blocks = count // BLOCK
    top = up_to(2 + 2 * blocks, 16)
    lanes = 2 * HALF
    constant = lambda shape: pl.BlockSpec(shape, lambda i: (0,) * len(shape))
    body = up_to(half, 16)
    woven = (count // GROUP * 16, BLOCK)
    out_shapes = [jax.ShapeDtypeStruct((top + body, lanes), jnp.int16)] * len(flips)
    out_shapes += [jax.ShapeDtypeStruct((body, 2 * REGION), BF16)] * 2
    operands = [vector, vector.reshape(blocks, BLOCK), *table]
    in_specs = [in_smem()] + [constant(value.shape) for value in operands[1:]]
    scratch = [
        pltpu.VMEM((top, lanes), F32),
        pltpu.VMEM((reach_x * reach_y, REGION), F32),
    ] + [pltpu.VMEM((pair_count(reach_x, reach_y), REGION), F32)] * CHAINS
    first = lines is None
    if first:
        stencil, flag, sample, dipole = raw
        tile = lambda t: pl.BlockSpec((64, BLOCK), lambda i: (0, t))
        operands += [stencil, flag.reshape(1, -1)] + [sample] * blocks + [dipole] * blocks
        in_specs += [constant(stencil.shape), constant((1, count))]
        in_specs += [tile(t) for t in range(blocks)] * 2
        out_shapes += [jax.ShapeDtypeStruct(woven, F32)] * 2
        out_shapes += [jax.ShapeDtypeStruct((2, count), jnp.int32)]
        scratch += [pltpu.SMEM((2, count), jnp.int32), pltpu.SemaphoreType.DMA]
    else:
        operands += [places, lines]
        in_specs += [in_smem(), whole_vmem()]
    return pl.pallas_call(
        functools.partial(spread_kernel, first, reach_x, reach_y, flips, blocks),
        grid=(1,),
        in_specs=in_specs,
        out_specs=[constant(out.shape) for out in out_shapes],
        out_shape=out_shapes,
        scratch_shapes=scratch,
        compiler_params=pltpu.CompilerParams(
            vmem_limit_bytes=START_LIMIT if first else VMEM_LIMIT
        ),
        cost_estimate=cost(2 * half * 256 * 512, 4 * 16 * count * REGION),
        name="start" if first else "spread",
    )(*operands)


def spread_rest_kernel(flips, rounded_ref, wide_high, wide_low, high_ref, low_ref, *refs):
    outs, head = refs[:-1], refs[-1]
    both = (wide_high[...], wide_low[...])
    send_pieces(outs, flips, head, rounded_ref[...], both, high_ref, low_ref)


def spread_rest(vector, both, table, flips):
    blocks = vector.shape[0] // BLOCK
    top = up_to(2 + 2 * blocks, 16)
    shape = (top + both[0].shape[0], 2 * HALF)
    return pl.pallas_call(
        functools.partial(spread_rest_kernel, flips),
        in_specs=[whole_vmem()] * 5,
        out_specs=[whole_vmem()] * len(flips),
        out_shape=[jax.ShapeDtypeStruct(shape, jnp.int16)] * len(flips),
        scratch_shapes=[pltpu.VMEM((top, 2 * HALF), F32)],
        compiler_params=params(),
        cost_estimate=cost(2 * shape[0] * 256 * 256 * 3, 4 * shape[0] * 512),
        name="spread_rest",
    )(vector.reshape(blocks, BLOCK), *both, *table)


def lines_kernel(place_ref, coeff_ref, out_ref):
    lanes = lax.broadcasted_iota(jnp.int32, (8, REGION), 1)

    def body(group, carry):
        at = pl.multiple_of(group * 16, 16)
        coeff = [coeff_ref[pl.ds(at + 8 * q, 8), :] for q in range(2)]
        for local in range(GROUP):
            panel = group * GROUP + local
            depth = place_ref[1, panel]
            shift = (depth - 4 * local) & (REGION - 1)
            inside = in_window(lanes, depth)
            for q in range(2):
                first = pl.multiple_of(panel * 16 + 8 * q, 8)
                out_ref[pl.ds(first, 8), :] = jnp.where(inside, pltpu.roll(coeff[q], shift, 1), 0.0)
        return carry

    lax.fori_loop(0, place_ref.shape[1] // GROUP, body, 0)


def place_lines(places, coeff):
    count = places.shape[1]
    shape = (count * 16, REGION)
    return pl.pallas_call(
        lines_kernel,
        in_specs=[in_smem(), whole_vmem()],
        out_specs=whole_vmem(),
        out_shape=jax.ShapeDtypeStruct(shape, F32),
        compiler_params=params(),
        cost_estimate=cost(16 * count * REGION, 4 * 16 * count * REGION),
        name="place_lines",
    )(places, coeff)


def forward_kernel(reach_x, reach_y, blocks, pieces, *refs):
    parts = refs[:pieces]
    table_ref, modes_ref = refs[pieces : pieces + 2]
    spectrum, right_out, left_out, own_out, peers_out, inner_out = refs[pieces + 2 : pieces + 8]
    opened, stacked, slabs, head = refs[pieces + 8 :]
    half = reach_x // 2
    pitch = up_to(reach_y, 8)
    tall = pieces * pitch
    top = parts[0].shape[0] - opened.shape[0]
    mine = y_position()
    if pitch > reach_y:
        stacked[...] = jnp.zeros_like(stacked)
    head[...] = jnp.zeros_like(head)
    for piece in range(pieces):
        first = from_short(parts[piece][:top, :])
        mantissa, exponent = first[2 : 2 + blocks], first[2 + blocks : 2 + 2 * blocks]
        peers_out[piece * blocks : (piece + 1) * blocks, :] = decode_rounded(mantissa, exponent)
        at = 6 + 2 * piece * blocks
        head[at : at + blocks, :] = mantissa
        head[at + blocks : at + 2 * blocks, :] = exponent
        opened[...] = from_short(parts[piece][top:, :]) * unit(first[0:1], first[1:2])
        place = (mine ^ piece) * pitch
        for i in range(half):
            stacked[pl.ds(pl.multiple_of(i * tall + place, 8), reach_y), :] = opened[
                i * reach_y : (i + 1) * reach_y, :
            ]
    table = table_ref[...]

    def tripled(values):
        high, low = split(values)
        return jnp.concatenate([high, low, high], axis=0)

    for i in range(0, half, 2):
        if i + 1 < half:
            pair = jnp.concatenate(
                [stacked[i * tall : (i + 1) * tall, :], stacked[(i + 1) * tall : (i + 2) * tall, :]],
                axis=1,
            )
            both = dot(table, tripled(pair))
            spectrum[i] = both[:, : 2 * HALF]
            spectrum[i + 1] = both[:, 2 * HALF :]
        else:
            spectrum[i] = dot(table, tripled(stacked[i * tall : (i + 1) * tall, :]))

    chunk = 32

    def body(index, largest):
        rows = pl.ds(pl.multiple_of(index * chunk, chunk), chunk)
        low = low_lanes(chunk)
        decay = modes_ref[0, rows, :]
        log_decay = modes_ref[1, rows, :]
        across_half = jnp.exp(half * log_decay)
        across_cut = jnp.exp((half - 4) * log_decay)
        layers = [spectrum[i, rows, :] for i in range(half)]
        run = layers[0]
        cut_right = run
        for i in range(1, half):
            run = decay * run + layers[i]
            if i == half - 5:
                cut_right = run
        right = run
        run = layers[half - 1]
        cut_left = run
        for i in range(half - 2, -1, -1):
            run = decay * run + layers[i]
            if i == 4:
                cut_left = run
        left = run
        inner_out[rows, :] = jnp.where(low, right, left)
        swapped_right, swapped_left = swap(right), swap(left)
        own = jnp.where(low, left + across_half * swapped_left, right + across_half * swapped_right)
        made = [
            jnp.where(low, swap(layers[half - 4]), layers[half - 3]),
            jnp.where(low, swap(layers[half - 2]), layers[half - 1]),
            jnp.where(low, own, cut_right + across_cut * swapped_right),
            jnp.where(low, layers[0], swap(layers[1])),
            jnp.where(low, layers[2], swap(layers[3])),
            jnp.where(low, cut_left + across_cut * swapped_left, own),
            own,
        ]
        for slab, values in enumerate(made):
            slabs[slab, rows, :] = values
        return tuple(
            jnp.maximum(old, jnp.max(jnp.abs(values).reshape(chunk // 8, 8, 2 * HALF), axis=0))
            for old, values in zip(largest, made)
        )

    zero = jnp.zeros((8, 2 * HALF), F32)
    largest = lax.fori_loop(0, GRID // chunk, body, (zero,) * 7)
    scales = [fit_scale(jnp.max(value, axis=0, keepdims=True)) for value in largest]
    head_rows = head.shape[0]
    for out, first in ((right_out, 0), (left_out, 3)):
        for slab in range(3):
            exponent, fraction = scales[first + slab]
            head[2 * slab : 2 * slab + 1, :] = exponent
            head[2 * slab + 1 : 2 * slab + 2, :] = fraction
            at = head_rows + slab * GRID
            out[at : at + GRID, :] = quantize(slabs[first + slab], exponent, fraction)
        out[:head_rows, :] = to_short(head[...])
    exponent, fraction = scales[6]
    head[0:1, :] = exponent
    head[1:2, :] = fraction
    own_out[:16, :] = to_short(head[:16, :])
    own_out[16:, :] = quantize(slabs[6], exponent, fraction)


def forward(parts, table, modes, reach_x, reach_y, blocks):
    pieces = len(parts)
    half = reach_x // 2
    lanes = 2 * HALF
    head = up_to(6 + 2 * pieces * blocks, 16)
    body = up_to(half * reach_y, 16)
    short = lambda rows: jax.ShapeDtypeStruct((rows, lanes), jnp.int16)
    return pl.pallas_call(
        functools.partial(forward_kernel, reach_x, reach_y, blocks, pieces),
        in_specs=[whole_vmem()] * (pieces + 2),
        out_specs=[whole_vmem()] * 6,
        out_shape=[
            jax.ShapeDtypeStruct((half, GRID, lanes), F32),
            short(head + 3 * GRID),
            short(head + 3 * GRID),
            short(16 + GRID),
            jax.ShapeDtypeStruct((pieces * blocks, BLOCK), F32),
            jax.ShapeDtypeStruct((GRID, lanes), F32),
        ],
        scratch_shapes=[
            pltpu.VMEM((body, lanes), F32),
            pltpu.VMEM((half * pieces * up_to(reach_y, 8), lanes), F32),
            pltpu.VMEM((7, GRID, lanes), F32),
            pltpu.VMEM((head, lanes), F32),
        ],
        compiler_params=params(),
        cost_estimate=cost(2 * half * 256 * 256 * 128, 4 * half * GRID * lanes * 2),
        name="forward",
    )(*parts, table, modes)


def send_fields(outs, flips, reach_y, field_high, field_low, high_ref, low_ref, ready, head):
    half = field_high.shape[0]
    mine = y_position()
    pitch = up_to(reach_y, 16)
    pick = lambda ref: jnp.concatenate([ref[mine ^ flip] for flip in flips], axis=0)
    table = (pick(high_ref), pick(low_ref))
    for i in range(0, half, 2):
        many = min(2, half - i)
        join = lambda ref: jnp.concatenate([ref[i + j] for j in range(many)], axis=1)
        result = dot_three(table, (join(field_high), join(field_low)))
        for j in range(many):
            for piece in range(len(flips)):
                ready[piece, (i + j) * reach_y : (i + j + 1) * reach_y, :] = result[
                    piece * pitch : piece * pitch + reach_y, j * 2 * HALF : (j + 1) * 2 * HALF
                ]
    head[...] = jnp.zeros_like(head)
    for piece, out in enumerate(outs):
        if ready.shape[1] > half * reach_y:
            ready[piece, half * reach_y :, :] = jnp.zeros_like(ready[piece, half * reach_y :, :])
        send_piece(out, head, ready[piece])


def inverse_kernel(reach_x, reach_y, flips, fars, *refs):
    spectrum, from_left, from_right, own_ref, inner_ref = refs[:5]
    far_refs = refs[5 : 5 + fars]
    high_ref, low_ref, modes_ref = refs[5 + fars : 8 + fars]
    outs = refs[8 + fars : 8 + fars + len(flips)]
    field_high, field_low, ready, head = refs[8 + fars + len(flips) :]
    half = reach_x // 2
    span = reach_x - 4
    chunk = 32
    head_rows = from_left.shape[0] - 3 * GRID
    x_count = lax.axis_size("wide")
    x_index = lax.axis_index("wide")

    left_head = from_short(from_left[:16, :])
    right_head = from_short(from_right[:16, :])
    left_units = [unit(left_head[2 * s : 2 * s + 1], left_head[2 * s + 1 : 2 * s + 2]) for s in range(3)]
    right_units = [
        unit(right_head[2 * s : 2 * s + 1], right_head[2 * s + 1 : 2 * s + 2]) for s in range(3)
    ]
    far_units = []
    own_head = from_short(own_ref[:16, :])
    own_unit = unit(own_head[0:1], own_head[1:2])
    for far in far_refs:
        first = from_short(far[:16, :])
        far_units.append(unit(first[0:1], first[1:2]))
    powers = []
    for far, shift in enumerate(list(range(2, x_count - 1)) + [x_count - 1][: int(x_count > 2)]):
        if shift < x_count - 1:
            behind = jnp.where(x_index >= shift, shift, shift - x_count)
        else:
            behind = jnp.where(x_index == 0, -shift, jnp.where(x_index == shift, shift, 0))
        both = []
        for distance in (-behind, behind):
            ahead = span * distance - reach_x
            both.append(jnp.where(distance >= 2, ahead, ahead + GRID).astype(F32))
        powers.append(both)

    def body(index, carry):
        first = pl.multiple_of(index * chunk, chunk)
        rows = pl.ds(first, chunk)
        low = low_lanes(chunk)
        decay = modes_ref[0, rows, :]
        log_decay = modes_ref[1, rows, :]
        ring = modes_ref[2, rows, :]
        gain = modes_ref[3, rows, :]
        across_half = jnp.exp(half * log_decay)
        across_cut = jnp.exp((half - 4) * log_decay)
        around = jnp.exp((GRID - 4) * log_decay)
        beside = jnp.exp((GRID - reach_x - span) * log_decay)
        layers = [spectrum[i, rows, :] for i in range(half)]

        def slab(ref, which, units):
            at = pl.ds(pl.multiple_of(head_rows + which * GRID + index * chunk, chunk), chunk)
            return from_short(ref[at, :]) * units[which]

        def moment(ref, scale):
            at = pl.ds(pl.multiple_of(16 + index * chunk, chunk), chunk)
            return from_short(ref[at, :]) * scale

        head_layers = [slab(from_left, 0, left_units), slab(from_left, 1, left_units)]
        tail_layers = [slab(from_right, 0, right_units), slab(from_right, 1, right_units)]
        zero = jnp.zeros_like(decay)
        from_head = [head_layers[0], swap(head_layers[0]), head_layers[1], swap(head_layers[1])]
        from_tail = [swap(tail_layers[0]), tail_layers[0], swap(tail_layers[1]), tail_layers[1]]
        head_sum = from_head[0]
        for i in range(1, 4):
            head_sum = decay * head_sum + from_head[i]
        tail_sum = from_tail[3]
        for i in range(2, -1, -1):
            tail_sum = decay * tail_sum + from_tail[i]
        for i in range(4):
            layers[i] = layers[i] + jnp.where(low, from_head[i], zero)
        for i in range(4):
            place = half - 4 + i
            layers[place] = layers[place] + jnp.where(low, zero, from_tail[i])
        total = moment(own_ref, own_unit) * jnp.exp((GRID - reach_x) * log_decay)
        one = jnp.ones_like(decay)
        total = total + slab(from_left, 2, left_units) * jnp.where(low, beside, one)
        total = total + slab(from_right, 2, right_units) * jnp.where(low, one, beside)
        for far in range(fars):
            power = jnp.where(low, powers[far][0], powers[far][1])
            total = total + moment(far_refs[far], far_units[far]) * jnp.exp(power * log_decay)
        shared = jnp.where(low, head_sum, tail_sum)
        entering = (swap(total) + around * shared) * ring
        leaving = swap(across_half * entering + across_cut * shared + inner_ref[rows, :])
        run = jnp.where(low, entering, leaving)
        forward_runs = []
        for i in range(half):
            run = decay * run + layers[i]
            forward_runs.append(run)
        run = jnp.where(low, leaving, entering)
        for i in range(half - 1, -1, -1):
            ahead = decay * run
            high, rest = split(gain * (forward_runs[i] + ahead))
            field_high[i, rows, :] = high
            field_low[i, rows, :] = rest
            run = ahead + layers[i]
        return carry

    lax.fori_loop(0, GRID // chunk, body, 0)
    send_fields(outs, flips, reach_y, field_high, field_low, high_ref, low_ref, ready, head)


def inverse(
    spectrum, from_left, from_right, own, inner, fars, table, modes, reach_x, reach_y, flips
):
    half = reach_x // 2
    lanes = 2 * HALF
    body = up_to(half * reach_y, 16)
    shapes = [jax.ShapeDtypeStruct((16 + body, lanes), jnp.int16)] * len(flips)
    shapes += [jax.ShapeDtypeStruct((half, GRID, lanes), BF16)] * 2
    return pl.pallas_call(
        functools.partial(inverse_kernel, reach_x, reach_y, flips, len(fars)),
        in_specs=[whole_vmem()] * (8 + len(fars)),
        out_specs=[whole_vmem()] * len(shapes),
        out_shape=shapes,
        scratch_shapes=[
            pltpu.VMEM((len(flips), body, lanes), F32),
            pltpu.VMEM((16, lanes), F32),
        ],
        compiler_params=params(),
        cost_estimate=cost(2 * half * 256 * 256 * 128, 4 * half * GRID * lanes * 2),
        name="inverse",
    )(spectrum, from_left, from_right, own, inner, *fars, *table, modes)


def inverse_rest_kernel(reach_y, flips, field_high, field_low, high_ref, low_ref, *refs):
    outs, (ready, head) = refs[: len(flips)], refs[len(flips) :]
    send_fields(outs, flips, reach_y, field_high, field_low, high_ref, low_ref, ready, head)


def inverse_rest(field, table, reach_y, flips):
    half = field[0].shape[0]
    lanes = 2 * HALF
    body = up_to(half * reach_y, 16)
    return pl.pallas_call(
        functools.partial(inverse_rest_kernel, reach_y, flips),
        in_specs=[whole_vmem()] * 4,
        out_specs=[whole_vmem()] * len(flips),
        out_shape=[jax.ShapeDtypeStruct((16 + body, lanes), jnp.int16)] * len(flips),
        scratch_shapes=[
            pltpu.VMEM((len(flips), body, lanes), F32),
            pltpu.VMEM((16, lanes), F32),
        ],
        compiler_params=params(),
        cost_estimate=cost(2 * half * 256 * 256 * 128, 4 * half * GRID * lanes * 2),
        name="inverse_rest",
    )(*field, *table)


def sum_rows(values):
    row = lax.broadcasted_iota(jnp.int32, values[0].shape, 0)
    for step in (4, 2, 1):
        low = (row & step) == 0
        paired = []
        for one, other in zip(values[: len(values) // 2], values[len(values) // 2 :]):
            kept = jnp.where(low, one, other)
            moved = jnp.where(low, other, one)
            if step == 4:
                moved = pltpu.roll(moved, 4, 0)
            else:
                moved = jnp.where(low, pltpu.roll(moved, 8 - step, 0), pltpu.roll(moved, step, 0))
            paired.append(kept + moved)
        values = paired
    return values[0]


def sample_kernel(last, reach_x, reach_y, pieces, place_ref, *refs):
    parts = refs[:pieces]
    high_ref, low_ref, line_ref, own_ref, vector_ref, near_ref, out_ref, flat, field, sums = refs[
        pieces:
    ]
    mine = y_position()
    half_rows = reach_x * reach_y // 2
    opened = []
    for part in parts:
        first = from_short(part[:16, :])
        opened.append(from_short(part[16:, :]) * unit(first[0:1], first[1:2]))
    values = split(jnp.concatenate(opened, axis=1))
    pick = lambda ref: jnp.concatenate([ref[mine ^ piece] for piece in range(pieces)], axis=0)
    both = dot_three(values, (pick(high_ref), pick(low_ref)))
    flat[:half_rows, :] = both[:half_rows, :REGION]
    flat[half_rows:, :] = both[:half_rows, REGION:]
    for x in range(reach_x):
        layer = flat[x * reach_y : (x + 1) * reach_y, :]
        for row in pair_rows(x, reach_x, reach_y):
            field[pl.ds(row, reach_y, stride=2), :] = layer
    count = place_ref.shape[1]

    def body(group, carry):
        for eight in range(0, GROUP, 8):
            totals = []
            for local in range(eight, eight + 8):
                panel = group * GROUP + local
                row = place_ref[0, panel]
                first = pl.multiple_of(panel * 16, 16)
                totals.append(
                    field[pl.ds(row, 8), :] * line_ref[pl.ds(first, 8), :]
                    + field[pl.ds(row + 2 * reach_y, 8), :] * line_ref[pl.ds(first + 8, 8), :]
                )
            sums[pl.ds(pl.multiple_of(group * GROUP + eight, 8), 8), :] = sum_rows(totals)
        return carry

    lax.fori_loop(0, count // GROUP, body, 0)
    sampled = lax.dot_general(
        jnp.ones((8, REGION), F32),
        sums[...],
        (((1,), (1,)), ((), ())),
        precision=lax.Precision.HIGHEST,
        preferred_element_type=F32,
    )
    for block in range(count // BLOCK):
        lane = slice(block * BLOCK, (block + 1) * BLOCK)
        row = slice(block, block + 1)
        vector = vector_ref[row, :]
        image = jnp.where(own_ref[row, :] == 1, 0.0, 0.5 * vector) + sampled[:1, lane]
        image = image + near_ref[row, :]
        if last:
            out_ref[0:1, lane] = vector
            out_ref[1:2, lane] = image
        else:
            out_ref[row, :] = image


def sample(last, places, parts, table, lines, flag, vector, near, reach_x, reach_y):
    count = places.shape[1]
    blocks = count // BLOCK
    pieces = len(parts)
    shape = (2, count) if last else (blocks, BLOCK)
    return pl.pallas_call(
        functools.partial(sample_kernel, last, reach_x, reach_y, pieces),
        in_specs=[in_smem()] + [whole_vmem()] * (pieces + 6),
        out_specs=whole_vmem(),
        out_shape=jax.ShapeDtypeStruct(shape, F32),
        scratch_shapes=[
            pltpu.VMEM((reach_x * reach_y, REGION), F32),
            pltpu.VMEM((pair_count(reach_x, reach_y), REGION), F32),
            pltpu.VMEM((count, REGION), F32),
        ],
        compiler_params=params(),
        cost_estimate=cost(reach_x * reach_y * 256 * 512, 4 * 16 * count * REGION),
        name="sample",
    )(
        places,
        *parts,
        *table,
        lines,
        flag.reshape(blocks, BLOCK),
        vector.reshape(blocks, BLOCK),
        near,
    )


def near_kernel(slots, blocks, place_ref, target_ref, *refs):
    left_ref, right_ref, peers_ref, tile_ref, out_ref, held = refs
    count = peers_ref.shape[0]
    held[count : 2 * count, :] = peers_ref[...]
    for first, ref in ((0, left_ref), (2 * count, right_ref)):
        top = from_short(ref[...])
        for piece in range(count // blocks):
            at = 6 + 2 * piece * blocks
            held[first + piece * blocks : first + (piece + 1) * blocks, :] = decode_rounded(
                top[at : at + blocks], top[at + blocks : at + 2 * blocks]
            )
    out_ref[...] = jnp.zeros_like(out_ref)
    for slot in range(slots):
        picked = held[pl.ds(place_ref[slot], 1), :]
        picked = jnp.broadcast_to(picked, (16, BLOCK)).astype(BF16)
        product = lax.dot_general(
            picked,
            tile_ref[slot],
            (((1,), (1,)), ((), ())),
            preferred_element_type=F32,
        )
        target = pl.ds(target_ref[slot], 1)
        out_ref[target, :] = out_ref[target, :] + product[:1]


def near_field(places, targets, from_left, from_right, peers, tiles, blocks, out_rows):
    slots = tiles.shape[0]
    head = from_left.shape[0] - 3 * GRID
    constant = lambda shape: pl.BlockSpec(shape, lambda i: (0,) * len(shape))
    return pl.pallas_call(
        functools.partial(near_kernel, slots, blocks),
        grid=(1,),
        in_specs=[
            in_smem(),
            in_smem(),
            constant((head, BLOCK)),
            constant((head, BLOCK)),
            constant(peers.shape),
            constant(tiles.shape),
        ],
        out_specs=constant((out_rows, BLOCK)),
        out_shape=jax.ShapeDtypeStruct((out_rows, BLOCK), F32),
        scratch_shapes=[pltpu.VMEM((3 * peers.shape[0], BLOCK), F32)],
        compiler_params=params(),
        cost_estimate=cost(2 * slots * 16 * BLOCK * BLOCK, 2 * slots * BLOCK * BLOCK),
        name="near_field",
    )(places, targets, from_left, from_right, peers, tiles)


def shards(
    density,
    surface_flag,
    stencil_base,
    sample_weights,
    dipole_weights,
    near_target,
    near_source,
    near_tiles,
):
    x_count = lax.axis_size("wide")
    y_count = lax.axis_size(Y_AXES)
    y_index = lax.axis_index(Y_AXES)
    span_x = REGION // x_count
    span_y = REGION // y_count
    reach_x = span_x + 4
    reach_y = span_y + 4
    count = density.shape[0]
    blocks = count // BLOCK

    z_forward, z_inverse, y_forward, y_inverse, modes = tables(y_count, span_y)
    modes = lax.dynamic_index_in_dim(jnp.asarray(modes), y_index, 0, keepdims=False)

    neighbour = near_source // blocks
    flip = (y_index + neighbour % 3 - 1) ^ y_index
    sources = ((neighbour // 3) * y_count + flip) * blocks + near_source % blocks
    out_rows = up_to(blocks + 1, 8)
    live = near_target >= 0
    sources = jnp.where(live, sources, 0)
    targets = jnp.where(live, near_target, out_rows - 1)

    far_moves = [
        [(i, (i + shift) % x_count) for i in range(x_count)] for shift in range(2, x_count - 1)
    ]
    if x_count > 2:
        far_moves.append([(0, x_count - 1), (x_count - 1, 0)])
    to_right = [(i, i + 1) for i in range(x_count - 1)]
    to_left = [(i + 1, i) for i in range(x_count - 1)]

    pair = lax.axis_size("pair")
    inside, outside = list(range(pair)), list(range(pair, y_count))

    def flipped(parts, flips):
        return [
            part
            if flip == 0
            else lax.ppermute(part, Y_AXES, [(i, i ^ flip) for i in range(y_count)])
            for flip, part in zip(flips, parts)
        ]

    def convolve_and_sample(last, vector, sent, both, places, sample_lines):
        arrived = flipped(sent, outside)
        arrived = flipped(spread_rest(vector, both, z_forward, inside), inside) + arrived
        spectrum, right_going, left_going, own, peers, inner = forward(
            arrived, y_forward, modes, reach_x, reach_y, blocks
        )
        from_left = lax.ppermute(right_going, "wide", to_right)
        from_right = lax.ppermute(left_going, "wide", to_left)
        fars = [lax.ppermute(own, "wide", pairs) for pairs in far_moves]
        near_part = near_field(
            sources, targets, from_left, from_right, peers, near_tiles, blocks, out_rows
        )
        *sent, high, low = inverse(
            spectrum,
            from_left,
            from_right,
            own,
            inner,
            fars,
            y_inverse,
            modes,
            reach_x,
            reach_y,
            outside,
        )
        arrived = flipped(sent, outside)
        arrived = flipped(inverse_rest((high, low), y_inverse, reach_y, inside), inside) + arrived
        return sample(
            last,
            places,
            arrived,
            z_inverse,
            sample_lines,
            surface_flag,
            vector,
            near_part,
            reach_x,
            reach_y,
        )

    raw = (stencil_base, surface_flag, sample_weights, dipole_weights)
    *sent, high, low, source_coeff, sample_coeff, places = spread(
        density, None, z_forward, None, raw, reach_x, reach_y, outside
    )
    sample_lines = place_lines(places, sample_coeff)
    source_lines = place_lines(places, source_coeff)
    first_image = convolve_and_sample(
        False, density, sent, (high, low), places, sample_lines
    ).reshape(-1)
    *sent, high, low = spread(
        first_image, places, z_forward, source_lines, None, reach_x, reach_y, outside
    )
    return convolve_and_sample(True, first_image, sent, (high, low), places, sample_lines)


def solution(mesh):
    panels = P(("groups",) + ALL_AXES)
    columns = P(None, ("groups",) + ALL_AXES)
    in_specs = (
        panels,
        panels,
        columns,
        columns,
        columns,
        panels,
        panels,
        P(("groups",) + ALL_AXES, None, None),
    )
    return jax.shard_map(
        shards, mesh=mesh, in_specs=in_specs, out_specs=columns, check_vma=False
    )
```

```python
import functools
import math

import jax
import jax.numpy as jnp
import numpy as np
from jax import lax
from jax.experimental import pallas as pl
from jax.experimental.pallas import tpu as pltpu
from jax.sharding import PartitionSpec as P

GRID = 256
REGION = 128
BLOCK = 128
HALF = 64
KERNEL_GAIN = 4.0
SCREEN = 1.0 / 1024.0
LN2 = math.log(2.0)
Y_AXES = ("narrow", "pair")
ALL_AXES = ("wide", "narrow", "pair")
F32 = jnp.float32
BF16 = jnp.bfloat16
VMEM_LIMIT = 24 * 1024 * 1024
GROUP = 32
CHAINS = 2


def cas(angles):
    return np.cos(angles) + np.sin(angles)


def up_to(count, multiple):
    return -(-count // multiple) * multiple


def low_lanes(rows):
    return lax.broadcasted_iota(jnp.int32, (rows, 2 * HALF), 1) < HALF


def swap(values):
    return pltpu.roll(values, HALF, 1)


def split(values):
    high = values.astype(BF16)
    return high, (values - high.astype(F32)).astype(BF16)


def dot(left, right):
    return jnp.dot(left, right, preferred_element_type=F32)


def dot_three(left, right):
    return dot(left[0], right[0]) + (dot(left[0], right[1]) + dot(left[1], right[0]))


def params():
    return pltpu.CompilerParams(vmem_limit_bytes=VMEM_LIMIT)


def whole_vmem():
    return pl.BlockSpec(memory_space=pltpu.VMEM)


def in_smem():
    return pl.BlockSpec(memory_space=pltpu.SMEM)


def cost(flops, moved):
    return pl.CostEstimate(flops=flops, bytes_accessed=moved, transcendentals=0)


def full_scale(exponent, fraction):
    return fraction * jnp.exp(exponent * LN2) * (1.0 / 1024.0)


def fit_scale(largest):
    largest = jnp.maximum(largest, 1e-30)
    exponent = jnp.floor(jnp.log(largest) * (1.0 / LN2))
    fraction = jnp.ceil(largest * jnp.exp(-exponent * LN2) * 1024.0) + 1.0
    return exponent, fraction


def to_short(values):
    return values.astype(jnp.int32).astype(jnp.int16)


def from_short(values):
    return values.astype(jnp.int32).astype(F32)


def quantize(values, exponent, fraction):
    return to_short(jnp.round(values * (32767.0 / full_scale(exponent, fraction))))


def unit(exponent, fraction):
    return full_scale(exponent, fraction) * (1.0 / 32767.0)


def encode_rounded(values):
    rounded = values.astype(BF16).astype(F32)
    size = jnp.maximum(jnp.abs(rounded), 1e-30)
    exponent = jnp.floor(jnp.log(size) * (1.0 / LN2))
    return jnp.round(rounded * jnp.exp((10.0 - exponent) * LN2)), exponent


def decode_rounded(mantissa, exponent):
    return (mantissa * jnp.exp((exponent - 10.0) * LN2)).astype(BF16).astype(F32)


def send_piece(out, head, values):
    exponent, fraction = fit_scale(jnp.max(jnp.abs(values), axis=0, keepdims=True))
    head[0:1, :] = exponent
    head[1:2, :] = fraction
    top = head.shape[0]
    out[:top, :] = to_short(head[...])
    out[top:, :] = quantize(values, exponent, fraction)


def y_position():
    return lax.axis_index("narrow") * lax.axis_size("pair") + lax.axis_index("pair")


def halves(table):
    high = table.astype(jnp.bfloat16)
    return high, (table - high.astype(np.float64)).astype(jnp.bfloat16)


def tables(y_count, span_y):
    depth = GRID // y_count
    reach = span_y + 4
    waves = np.arange(GRID)
    step = 2.0 * np.pi / GRID
    z_table = cas(step * np.outer(np.arange(REGION), waves))
    z_forward = np.zeros((y_count, 2 * REGION, 2 * HALF))
    z_inverse = np.zeros((y_count, 2 * HALF, 2 * REGION))
    symbols = 4.0 * np.sin(np.pi * waves / GRID) ** 2
    shift = np.full((y_count, GRID, 2 * HALF), 1.0)
    y_forward = np.zeros((GRID, y_count, up_to(reach, 8)))
    y_inverse = np.zeros((y_count, up_to(reach, 16), GRID))
    for block in range(y_count):
        mine = z_table[:, block * depth : (block + 1) * depth]
        for half in range(2):
            rows = slice(half * REGION, (half + 1) * REGION)
            lanes = slice(half * HALF, half * HALF + depth)
            z_forward[block, rows, lanes] = mine
            z_inverse[block, lanes, rows] = mine.T / GRID
            shift[block, :, lanes] = (
                SCREEN + symbols[:, None] + symbols[None, block * depth : (block + 1) * depth]
            )
        cells = block * span_y - 2 + np.arange(reach)
        y_table = cas(step * np.outer(waves, cells))
        y_forward[:, block, :reach] = y_table
        y_inverse[block, :reach] = y_table.T / GRID
    y_forward = halves(y_forward.reshape(GRID, -1))
    y_forward = np.concatenate([y_forward[0], y_forward[0], y_forward[1]], axis=1)
    root = np.sqrt(shift * (shift + 4.0))
    decay = 2.0 / (2.0 + shift + root)
    log_decay = np.log(decay)
    ring = 1.0 / (1.0 - np.exp(GRID * log_decay))
    gain = KERNEL_GAIN / root
    modes = np.stack([decay, log_decay, ring, gain], axis=1).astype(np.float32)
    return (
        halves(z_forward),
        halves(z_inverse),
        y_forward,
        halves(y_inverse),
        modes,
    )


def weave(flag, sample_refs, dipole_refs, source_out, sample_out):
    place = lax.broadcasted_iota(jnp.int32, (4 * BLOCK, 4 * BLOCK), 0)
    lane = lax.broadcasted_iota(jnp.int32, (4 * BLOCK, 4 * BLOCK), 1)
    wanted = 4 * (place % BLOCK) + place // BLOCK
    mixing = jnp.where(lane == wanted, 1.0, 0.0).astype(BF16)
    stacked = []
    for tile, (sample_ref, dipole_ref) in enumerate(zip(sample_refs, dipole_refs)):
        charged = flag[:, tile * BLOCK : (tile + 1) * BLOCK] == 1
        rows = []
        for depth in range(4):
            sample = sample_ref[pl.ds(depth, 16, stride=4), :]
            dipole = dipole_ref[pl.ds(depth, 16, stride=4), :]
            rows.append(jnp.concatenate([jnp.where(charged, -sample, dipole), sample], axis=0))
        stacked.append(jnp.concatenate(rows, axis=1))
    weights = jnp.concatenate(stacked, axis=0)
    first, rest = split(weights)
    second, third = split(weights - first.astype(F32))
    woven = dot(first, mixing) + (dot(second, mixing) + dot(third, mixing))
    for tile in range(len(sample_refs)):
        for which, out in enumerate((source_out, sample_out)):
            for part in range(BLOCK // GROUP):
                at = (tile * (BLOCK // GROUP) + part) * 16
                lanes = slice(part * BLOCK, (part + 1) * BLOCK)
                for a in range(4):
                    row = tile * 32 + which * 16 + 4 * a
                    out[pl.ds(at + 8 * (a // 2) + a % 2, 4, stride=2), :] = woven[
                        row : row + 4, lanes
                    ]


def pair_rows(x, reach_x, reach_y):
    even = (x // 2) * 2 * reach_y + x % 2
    if x == 0 or x == reach_x - 1:
        return [even]
    return [even, reach_x * reach_y + ((x - 1) // 2) * 2 * reach_y + (x - 1) % 2]


def pair_count(reach_x, reach_y):
    return (2 * reach_x - 2) * reach_y


def in_window(lanes, depth):
    return ((lanes - depth) & -4) == 0


def add_panels(reach, woven, vector_ref, place_ref, weight_ref, grids):
    lanes = lax.broadcasted_iota(jnp.int32, (8, REGION), 1)

    def body(group, carry):
        at = pl.multiple_of(group * 16, 16)
        coeff = [weight_ref[pl.ds(at + 8 * q, 8), :] for q in range(2)] if woven else None
        for local in range(GROUP):
            panel = group * GROUP + local
            grid = grids[local % len(grids)]
            row = place_ref[0, panel]
            value = vector_ref[panel]
            if woven:
                depth = place_ref[1, panel]
                shift = (depth - 4 * local) & (REGION - 1)
                value = jnp.where(in_window(lanes, depth), value, 0.0)
                lines = [pltpu.roll(coeff[q], shift, 1) for q in range(2)]
            else:
                first = pl.multiple_of(panel * 16, 16)
                lines = [weight_ref[pl.ds(first + 8 * q, 8), :] for q in range(2)]
            places = [pl.ds(row, 8), pl.ds(row + 2 * reach, 8)]
            held = [grid[place, :] for place in places]
            for q in range(2):
                grid[places[q], :] = held[q] + lines[q] * value
        return carry

    lax.fori_loop(0, vector_ref.shape[0] // GROUP, body, 0)


def send_pieces(outs, flips, head, rounded, both, high_ref, low_ref):
    blocks = rounded.shape[0]
    mantissa, exponent = encode_rounded(rounded)
    head[...] = jnp.zeros_like(head)
    head[2 : 2 + blocks, :] = mantissa
    head[2 + blocks : 2 + 2 * blocks, :] = exponent
    mine = y_position()
    for at in range(0, len(flips), 2):
        pick = lambda ref: jnp.concatenate([ref[mine ^ flip] for flip in flips[at : at + 2]], axis=1)
        result = dot_three(both, (pick(high_ref), pick(low_ref)))
        for i, out in enumerate(outs[at : at + 2]):
            send_piece(out, head, result[:, i * 2 * HALF : (i + 1) * 2 * HALF])


def spread_grid(reach_x, reach_y, rounded, tables, outs, flips, wides, head, total, grids):
    for x in range(reach_x):
        parts = [
            grid[pl.ds(row, reach_y, stride=2), :]
            for row in pair_rows(x, reach_x, reach_y)
            for grid in grids
        ]
        total[x * reach_y : (x + 1) * reach_y, :] = sum(parts[1:], parts[0])
    half = reach_x * reach_y // 2
    both = jnp.concatenate([total[:half, :], total[half:, :]], axis=1)
    extra = wides[0].shape[0] - half
    if extra:
        both = jnp.concatenate([both, jnp.zeros((extra, 2 * REGION), F32)], axis=0)
    both = split(both)
    for wide, values in zip(wides, both):
        wide[...] = values
    send_pieces(outs, flips, head, rounded, both, *tables)


def start_kernel(reach_x, reach_y, flips, *refs):
    vector_ref, *remote = refs[:8]
    refs = refs[8:]
    outs, refs = refs[: len(flips)], refs[len(flips) :]
    wides, (weight_ref, sample_coeff_ref, places_out), refs = refs[:2], refs[2:5], refs[5:]
    rounded, high, low, stencil, flag, samples, dipoles = refs[:7]
    place_ref, sems, head, total = refs[7:11]
    grids = refs[11:]
    tiles = samples.shape[0]
    copies = []
    fetch = lambda source, target: copies.append(
        pltpu.make_async_copy(source, target, sems.at[len(copies)])
    )
    rounded_in, high_in, low_in, stencil_in, flag_in, sample_in, dipole_in = remote
    fetch(stencil_in, stencil)
    fetch(flag_in, flag)
    for tile in range(tiles):
        lanes = pl.ds(tile * BLOCK, BLOCK)
        fetch(sample_in.at[:, lanes], samples.at[tile])
        fetch(dipole_in.at[:, lanes], dipoles.at[tile])
    needed_first = len(copies)
    fetch(rounded_in, rounded)
    fetch(high_in, high)
    fetch(low_in, low)
    for copy in copies:
        copy.start()
    for grid in grids:
        grid[...] = jnp.zeros_like(grid)
    copies[0].wait()
    span_x, span_y = reach_x - 4, reach_y - 4
    local_x = stencil[0:1, :] - (lax.axis_index("wide") * span_x - 2)
    local_y = stencil[1:2, :] - (y_position() * span_y - 2)
    odd = local_x & 1
    places_out[0:1, :] = odd * (reach_x * reach_y) + (local_x >> 1) * (2 * reach_y) + 2 * local_y
    places_out[1:2, :] = stencil[2:3, :]
    to_scalar = pltpu.make_async_copy(places_out, place_ref, sems.at[len(copies)])
    to_scalar.start()
    for copy in copies[1:needed_first]:
        copy.wait()
    each = lambda values: [values.at[tile] for tile in range(tiles)]
    weave(flag[...], each(samples), each(dipoles), weight_ref, sample_coeff_ref)
    to_scalar.wait()
    add_panels(reach_y, True, vector_ref, place_ref, weight_ref, grids)
    for copy in copies[needed_first:]:
        copy.wait()
    spread_grid(
        reach_x, reach_y, rounded[...], (high, low), outs, flips, wides, head, total, grids
    )


def spread_kernel(reach_x, reach_y, flips, *refs):
    vector_ref, place_ref, rounded_ref, high_ref, low_ref, line_ref = refs[:6]
    refs = refs[6:]
    outs, wides, (head, total), grids = (
        refs[: len(flips)],
        refs[len(flips) : len(flips) + 2],
        refs[len(flips) + 2 : len(flips) + 4],
        refs[len(flips) + 4 :],
    )
    for grid in grids:
        grid[...] = jnp.zeros_like(grid)
    add_panels(reach_y, False, vector_ref, place_ref, line_ref, grids)
    spread_grid(
        reach_x,
        reach_y,
        rounded_ref[...],
        (high_ref, low_ref),
        outs,
        flips,
        wides,
        head,
        total,
        grids,
    )


def spread(vector, table, placed, raw, reach_x, reach_y, flips):
    count = vector.shape[0]
    half = reach_x * reach_y // 2
    blocks = count // BLOCK
    top = up_to(2 + 2 * blocks, 16)
    lanes = 2 * HALF
    body = up_to(half, 16)
    woven = (count // GROUP * 16, BLOCK)
    out_shapes = [jax.ShapeDtypeStruct((top + body, lanes), jnp.int16)] * len(flips)
    out_shapes += [jax.ShapeDtypeStruct((body, 2 * REGION), BF16)] * 2
    rounded = vector.reshape(blocks, BLOCK)
    work = [
        pltpu.VMEM((top, lanes), F32),
        pltpu.VMEM((reach_x * reach_y, REGION), F32),
    ] + [pltpu.VMEM((pair_count(reach_x, reach_y), REGION), F32)] * CHAINS
    if placed is None:
        stencil, flag, sample, dipole = raw
        operands = [vector, rounded, *table, stencil, flag.reshape(1, -1), sample, dipole]
        in_specs = [in_smem()] + [pl.BlockSpec(memory_space=pltpu.HBM)] * 7
        out_shapes += [jax.ShapeDtypeStruct(woven, F32)] * 2
        out_shapes += [jax.ShapeDtypeStruct((2, count), jnp.int32)]
        tiled = pltpu.VMEM((blocks, 64, BLOCK), F32)
        work = [
            pltpu.VMEM(rounded.shape, F32),
            pltpu.VMEM(table[0].shape, BF16),
            pltpu.VMEM(table[1].shape, BF16),
            pltpu.VMEM(stencil.shape, jnp.int32),
            pltpu.VMEM((1, count), jnp.int32),
            tiled,
            tiled,
            pltpu.SMEM((2, count), jnp.int32),
            pltpu.SemaphoreType.DMA((6 + 2 * blocks,)),
        ] + work
    else:
        operands = [vector, placed[0], rounded, *table, placed[1]]
        in_specs = [in_smem()] * 2 + [whole_vmem()] * 4
    return pl.pallas_call(
        functools.partial(
            start_kernel if placed is None else spread_kernel, reach_x, reach_y, flips
        ),
        in_specs=in_specs,
        out_specs=[whole_vmem()] * len(out_shapes),
        out_shape=out_shapes,
        scratch_shapes=work,
        compiler_params=params(),
        cost_estimate=cost(2 * half * 256 * 512, 4 * 16 * count * REGION),
        name="start" if placed is None else "spread",
    )(*operands)


def spread_rest_kernel(flips, rounded_ref, wide_high, wide_low, high_ref, low_ref, *refs):
    outs, head = refs[:-1], refs[-1]
    both = (wide_high[...], wide_low[...])
    send_pieces(outs, flips, head, rounded_ref[...], both, high_ref, low_ref)


def spread_rest(vector, both, table, flips):
    blocks = vector.shape[0] // BLOCK
    top = up_to(2 + 2 * blocks, 16)
    shape = (top + both[0].shape[0], 2 * HALF)
    return pl.pallas_call(
        functools.partial(spread_rest_kernel, flips),
        in_specs=[whole_vmem()] * 5,
        out_specs=[whole_vmem()] * len(flips),
        out_shape=[jax.ShapeDtypeStruct(shape, jnp.int16)] * len(flips),
        scratch_shapes=[pltpu.VMEM((top, 2 * HALF), F32)],
        compiler_params=params(),
        cost_estimate=cost(2 * shape[0] * 256 * 256 * 3, 4 * shape[0] * 512),
        name="spread_rest",
    )(vector.reshape(blocks, BLOCK), *both, *table)


def lines_kernel(place_ref, coeff_ref, out_ref):
    lanes = lax.broadcasted_iota(jnp.int32, (8, REGION), 1)

    def body(group, carry):
        at = pl.multiple_of(group * 16, 16)
        coeff = [coeff_ref[pl.ds(at + 8 * q, 8), :] for q in range(2)]
        for local in range(GROUP):
            panel = group * GROUP + local
            depth = place_ref[1, panel]
            shift = (depth - 4 * local) & (REGION - 1)
            inside = in_window(lanes, depth)
            for q in range(2):
                first = pl.multiple_of(panel * 16 + 8 * q, 8)
                out_ref[pl.ds(first, 8), :] = jnp.where(inside, pltpu.roll(coeff[q], shift, 1), 0.0)
        return carry

    lax.fori_loop(0, place_ref.shape[1] // GROUP, body, 0)


def place_lines(places, coeff):
    count = places.shape[1]
    shape = (count * 16, REGION)
    return pl.pallas_call(
        lines_kernel,
        in_specs=[in_smem(), whole_vmem()],
        out_specs=whole_vmem(),
        out_shape=jax.ShapeDtypeStruct(shape, F32),
        compiler_params=params(),
        cost_estimate=cost(16 * count * REGION, 4 * 16 * count * REGION),
        name="place_lines",
    )(places, coeff)


def forward_kernel(reach_x, reach_y, blocks, pieces, *refs):
    parts = refs[:pieces]
    table_ref, modes_ref = refs[pieces : pieces + 2]
    spectrum, even_out, odd_out, own_out, peers_out, inner_out = refs[pieces + 2 : pieces + 8]
    opened, stacked, slabs, head = refs[pieces + 8 :]
    half = reach_x // 2
    pitch = up_to(reach_y, 8)
    tall = pieces * pitch
    top = parts[0].shape[0] - opened.shape[0]
    mine = y_position()
    if pitch > reach_y:
        stacked[...] = jnp.zeros_like(stacked)
    head[...] = jnp.zeros_like(head)
    for piece in range(pieces):
        first = from_short(parts[piece][:top, :])
        mantissa, exponent = first[2 : 2 + blocks], first[2 + blocks : 2 + 2 * blocks]
        peers_out[piece * blocks : (piece + 1) * blocks, :] = decode_rounded(mantissa, exponent)
        at = 6 + 2 * piece * blocks
        head[at : at + blocks, :] = mantissa
        head[at + blocks : at + 2 * blocks, :] = exponent
        opened[...] = from_short(parts[piece][top:, :]) * unit(first[0:1], first[1:2])
        place = (mine ^ piece) * pitch
        for i in range(half):
            stacked[pl.ds(pl.multiple_of(i * tall + place, 8), reach_y), :] = opened[
                i * reach_y : (i + 1) * reach_y, :
            ]
    table = table_ref[...]

    def tripled(values):
        high, low = split(values)
        return jnp.concatenate([high, low, high], axis=0)

    for i in range(0, half, 2):
        if i + 1 < half:
            pair = jnp.concatenate(
                [stacked[i * tall : (i + 1) * tall, :], stacked[(i + 1) * tall : (i + 2) * tall, :]],
                axis=1,
            )
            both = dot(table, tripled(pair))
            spectrum[i] = both[:, : 2 * HALF]
            spectrum[i + 1] = both[:, 2 * HALF :]
        else:
            spectrum[i] = dot(table, tripled(stacked[i * tall : (i + 1) * tall, :]))

    chunk = 32

    def body(index, largest):
        rows = pl.ds(pl.multiple_of(index * chunk, chunk), chunk)
        low = low_lanes(chunk)
        decay = modes_ref[0, rows, :]
        log_decay = modes_ref[1, rows, :]
        across_half = jnp.exp(half * log_decay)
        across_cut = jnp.exp((half - 4) * log_decay)
        layers = [spectrum[i, rows, :] for i in range(half)]
        run = layers[0]
        cut_right = run
        for i in range(1, half):
            run = decay * run + layers[i]
            if i == half - 5:
                cut_right = run
        right = run
        run = layers[half - 1]
        cut_left = run
        for i in range(half - 2, -1, -1):
            run = decay * run + layers[i]
            if i == 4:
                cut_left = run
        left = run
        inner_out[rows, :] = jnp.where(low, right, left)
        swapped_right, swapped_left = swap(right), swap(left)
        own = jnp.where(low, left + across_half * swapped_left, right + across_half * swapped_right)
        made = [
            jnp.where(low, swap(layers[half - 4]), layers[half - 3]),
            jnp.where(low, swap(layers[half - 2]), layers[half - 1]),
            jnp.where(low, own, cut_right + across_cut * swapped_right),
            jnp.where(low, layers[0], swap(layers[1])),
            jnp.where(low, layers[2], swap(layers[3])),
            jnp.where(low, cut_left + across_cut * swapped_left, own),
            own,
        ]
        for slab, values in enumerate(made):
            slabs[slab, rows, :] = values
        return tuple(
            jnp.maximum(old, jnp.max(jnp.abs(values).reshape(chunk // 8, 8, 2 * HALF), axis=0))
            for old, values in zip(largest, made)
        )

    zero = jnp.zeros((8, 2 * HALF), F32)
    largest = lax.fori_loop(0, GRID // chunk, body, (zero,) * 7)
    scales = [fit_scale(jnp.max(value, axis=0, keepdims=True)) for value in largest]
    head_rows = head.shape[0]

    def send(out, first):
        for slab in range(3):
            exponent, fraction = scales[first + slab]
            head[2 * slab : 2 * slab + 1, :] = exponent
            head[2 * slab + 1 : 2 * slab + 2, :] = fraction
            at = head_rows + slab * GRID
            out[at : at + GRID, :] = quantize(slabs[first + slab], exponent, fraction)
        out[:head_rows, :] = to_short(head[...])

    on_left = lax.axis_index("wide") & 1

    @pl.when(on_left == 0)
    def _():
        send(even_out, 0)
        send(odd_out, 3)

    @pl.when(on_left == 1)
    def _():
        send(even_out, 3)
        send(odd_out, 0)

    exponent, fraction = scales[6]
    head[0:1, :] = exponent
    head[1:2, :] = fraction
    own_out[:16, :] = to_short(head[:16, :])
    own_out[16:, :] = quantize(slabs[6], exponent, fraction)


def forward(parts, table, modes, reach_x, reach_y, blocks):
    pieces = len(parts)
    half = reach_x // 2
    lanes = 2 * HALF
    head = up_to(6 + 2 * pieces * blocks, 16)
    body = up_to(half * reach_y, 16)
    short = lambda rows: jax.ShapeDtypeStruct((rows, lanes), jnp.int16)
    return pl.pallas_call(
        functools.partial(forward_kernel, reach_x, reach_y, blocks, pieces),
        in_specs=[whole_vmem()] * (pieces + 2),
        out_specs=[whole_vmem()] * 6,
        out_shape=[
            jax.ShapeDtypeStruct((half, GRID, lanes), F32),
            short(head + 3 * GRID),
            short(head + 3 * GRID),
            short(16 + GRID),
            jax.ShapeDtypeStruct((pieces * blocks, BLOCK), F32),
            jax.ShapeDtypeStruct((GRID, lanes), F32),
        ],
        scratch_shapes=[
            pltpu.VMEM((body, lanes), F32),
            pltpu.VMEM((half * pieces * up_to(reach_y, 8), lanes), F32),
            pltpu.VMEM((7, GRID, lanes), F32),
            pltpu.VMEM((head, lanes), F32),
        ],
        compiler_params=params(),
        cost_estimate=cost(2 * half * 256 * 256 * 128, 4 * half * GRID * lanes * 2),
        name="forward",
    )(*parts, table, modes)


def send_fields(outs, flips, reach_y, field_high, field_low, high_ref, low_ref, ready, head):
    half = field_high.shape[0]
    mine = y_position()
    pitch = up_to(reach_y, 16)
    pick = lambda ref: jnp.concatenate([ref[mine ^ flip] for flip in flips], axis=0)
    table = (pick(high_ref), pick(low_ref))
    for i in range(0, half, 2):
        many = min(2, half - i)
        join = lambda ref: jnp.concatenate([ref[i + j] for j in range(many)], axis=1)
        result = dot_three(table, (join(field_high), join(field_low)))
        for j in range(many):
            for piece in range(len(flips)):
                ready[piece, (i + j) * reach_y : (i + j + 1) * reach_y, :] = result[
                    piece * pitch : piece * pitch + reach_y, j * 2 * HALF : (j + 1) * 2 * HALF
                ]
    head[...] = jnp.zeros_like(head)
    for piece, out in enumerate(outs):
        if ready.shape[1] > half * reach_y:
            ready[piece, half * reach_y :, :] = jnp.zeros_like(ready[piece, half * reach_y :, :])
        send_piece(out, head, ready[piece])


def inverse_kernel(reach_x, reach_y, flips, fars, *refs):
    spectrum, from_even, from_odd, own_ref, inner_ref = refs[:5]
    far_refs = refs[5 : 5 + fars]
    high_ref, low_ref, modes_ref = refs[5 + fars : 8 + fars]
    outs = refs[8 + fars : 8 + fars + len(flips)]
    field_high, field_low, ready, head = refs[8 + fars + len(flips) :]
    half = reach_x // 2
    span = reach_x - 4
    chunk = 32
    head_rows = from_even.shape[0] - 3 * GRID
    x_count = lax.axis_size("wide")
    x_index = lax.axis_index("wide")

    on_left = (x_index & 1) == 1
    both_heads = from_short(from_even[:16, :]), from_short(from_odd[:16, :])
    both_units = [
        [unit(first[2 * slab : 2 * slab + 1], first[2 * slab + 1 : 2 * slab + 2]) for slab in range(3)]
        for first in both_heads
    ]

    def sided(even, odd):
        return jnp.where(on_left, even, odd), jnp.where(on_left, odd, even)

    far_units = []
    own_head = from_short(own_ref[:16, :])
    own_unit = unit(own_head[0:1], own_head[1:2])
    for far in far_refs:
        first = from_short(far[:16, :])
        far_units.append(unit(first[0:1], first[1:2]))
    powers = []
    for flip in range(2, x_count):
        behind = x_index - (x_index ^ flip)
        both = []
        for distance in (-behind, behind):
            ahead = span * distance - reach_x
            both.append(jnp.where(distance >= 2, ahead, ahead + GRID).astype(F32))
        powers.append(both)

    def body(index, carry):
        first = pl.multiple_of(index * chunk, chunk)
        rows = pl.ds(first, chunk)
        low = low_lanes(chunk)
        decay = modes_ref[0, rows, :]
        log_decay = modes_ref[1, rows, :]
        ring = modes_ref[2, rows, :]
        gain = modes_ref[3, rows, :]
        across_half = jnp.exp(half * log_decay)
        across_cut = jnp.exp((half - 4) * log_decay)
        around = jnp.exp((GRID - 4) * log_decay)
        beside = jnp.exp((GRID - reach_x - span) * log_decay)
        layers = [spectrum[i, rows, :] for i in range(half)]

        def slab(which):
            at = pl.ds(pl.multiple_of(head_rows + which * GRID + index * chunk, chunk), chunk)
            even = from_short(from_even[at, :]) * both_units[0][which]
            return sided(even, from_short(from_odd[at, :]) * both_units[1][which])

        def moment(ref, scale):
            at = pl.ds(pl.multiple_of(16 + index * chunk, chunk), chunk)
            return from_short(ref[at, :]) * scale

        head_layers, tail_layers = zip(slab(0), slab(1))
        left_moments, right_moments = slab(2)
        zero = jnp.zeros_like(decay)
        from_head = [head_layers[0], swap(head_layers[0]), head_layers[1], swap(head_layers[1])]
        from_tail = [swap(tail_layers[0]), tail_layers[0], swap(tail_layers[1]), tail_layers[1]]
        head_sum = from_head[0]
        for i in range(1, 4):
            head_sum = decay * head_sum + from_head[i]
        tail_sum = from_tail[3]
        for i in range(2, -1, -1):
            tail_sum = decay * tail_sum + from_tail[i]
        for i in range(4):
            layers[i] = layers[i] + jnp.where(low, from_head[i], zero)
        for i in range(4):
            place = half - 4 + i
            layers[place] = layers[place] + jnp.where(low, zero, from_tail[i])
        total = moment(own_ref, own_unit) * jnp.exp((GRID - reach_x) * log_decay)
        one = jnp.ones_like(decay)
        total = total + left_moments * jnp.where(low, beside, one)
        total = total + right_moments * jnp.where(low, one, beside)
        for far in range(fars):
            power = jnp.where(low, powers[far][0], powers[far][1])
            total = total + moment(far_refs[far], far_units[far]) * jnp.exp(power * log_decay)
        shared = jnp.where(low, head_sum, tail_sum)
        entering = (swap(total) + around * shared) * ring
        leaving = swap(across_half * entering + across_cut * shared + inner_ref[rows, :])
        run = jnp.where(low, entering, leaving)
        forward_runs = []
        for i in range(half):
            run = decay * run + layers[i]
            forward_runs.append(run)
        run = jnp.where(low, leaving, entering)
        for i in range(half - 1, -1, -1):
            ahead = decay * run
            high, rest = split(gain * (forward_runs[i] + ahead))
            field_high[i, rows, :] = high
            field_low[i, rows, :] = rest
            run = ahead + layers[i]
        return carry

    lax.fori_loop(0, GRID // chunk, body, 0)
    send_fields(outs, flips, reach_y, field_high, field_low, high_ref, low_ref, ready, head)


def inverse(
    spectrum, from_even, from_odd, own, inner, fars, table, modes, reach_x, reach_y, flips
):
    half = reach_x // 2
    lanes = 2 * HALF
    body = up_to(half * reach_y, 16)
    shapes = [jax.ShapeDtypeStruct((16 + body, lanes), jnp.int16)] * len(flips)
    shapes += [jax.ShapeDtypeStruct((half, GRID, lanes), BF16)] * 2
    return pl.pallas_call(
        functools.partial(inverse_kernel, reach_x, reach_y, flips, len(fars)),
        in_specs=[whole_vmem()] * (8 + len(fars)),
        out_specs=[whole_vmem()] * len(shapes),
        out_shape=shapes,
        scratch_shapes=[
            pltpu.VMEM((len(flips), body, lanes), F32),
            pltpu.VMEM((16, lanes), F32),
        ],
        compiler_params=params(),
        cost_estimate=cost(2 * half * 256 * 256 * 128, 4 * half * GRID * lanes * 2),
        name="inverse",
    )(spectrum, from_even, from_odd, own, inner, *fars, *table, modes)


def inverse_rest_kernel(reach_y, flips, field_high, field_low, high_ref, low_ref, *refs):
    outs, (ready, head) = refs[: len(flips)], refs[len(flips) :]
    send_fields(outs, flips, reach_y, field_high, field_low, high_ref, low_ref, ready, head)


def inverse_rest(field, table, reach_y, flips):
    half = field[0].shape[0]
    lanes = 2 * HALF
    body = up_to(half * reach_y, 16)
    return pl.pallas_call(
        functools.partial(inverse_rest_kernel, reach_y, flips),
        in_specs=[whole_vmem()] * 4,
        out_specs=[whole_vmem()] * len(flips),
        out_shape=[jax.ShapeDtypeStruct((16 + body, lanes), jnp.int16)] * len(flips),
        scratch_shapes=[
            pltpu.VMEM((len(flips), body, lanes), F32),
            pltpu.VMEM((16, lanes), F32),
        ],
        compiler_params=params(),
        cost_estimate=cost(2 * half * 256 * 256 * 128, 4 * half * GRID * lanes * 2),
        name="inverse_rest",
    )(*field, *table)


def sum_rows(values):
    row = lax.broadcasted_iota(jnp.int32, values[0].shape, 0)
    for step in (4, 2, 1):
        low = (row & step) == 0
        paired = []
        for one, other in zip(values[: len(values) // 2], values[len(values) // 2 :]):
            kept = jnp.where(low, one, other)
            moved = jnp.where(low, other, one)
            if step == 4:
                moved = pltpu.roll(moved, 4, 0)
            else:
                moved = jnp.where(low, pltpu.roll(moved, 8 - step, 0), pltpu.roll(moved, step, 0))
            paired.append(kept + moved)
        values = paired
    return values[0]


def sample_kernel(last, reach_x, reach_y, pieces, place_ref, *refs):
    parts = refs[:pieces]
    high_ref, low_ref, line_ref, own_ref, vector_ref, near_ref, out_ref, flat, field, sums = refs[
        pieces:
    ]
    mine = y_position()
    half_rows = reach_x * reach_y // 2
    opened = []
    for part in parts:
        first = from_short(part[:16, :])
        opened.append(from_short(part[16:, :]) * unit(first[0:1], first[1:2]))
    values = split(jnp.concatenate(opened, axis=1))
    pick = lambda ref: jnp.concatenate([ref[mine ^ piece] for piece in range(pieces)], axis=0)
    both = dot_three(values, (pick(high_ref), pick(low_ref)))
    flat[:half_rows, :] = both[:half_rows, :REGION]
    flat[half_rows:, :] = both[:half_rows, REGION:]
    for x in range(reach_x):
        layer = flat[x * reach_y : (x + 1) * reach_y, :]
        for row in pair_rows(x, reach_x, reach_y):
            field[pl.ds(row, reach_y, stride=2), :] = layer
    count = place_ref.shape[1]

    def body(group, carry):
        for eight in range(0, GROUP, 8):
            totals = []
            for local in range(eight, eight + 8):
                panel = group * GROUP + local
                row = place_ref[0, panel]
                first = pl.multiple_of(panel * 16, 16)
                totals.append(
                    field[pl.ds(row, 8), :] * line_ref[pl.ds(first, 8), :]
                    + field[pl.ds(row + 2 * reach_y, 8), :] * line_ref[pl.ds(first + 8, 8), :]
                )
            sums[pl.ds(pl.multiple_of(group * GROUP + eight, 8), 8), :] = sum_rows(totals)
        return carry

    lax.fori_loop(0, count // GROUP, body, 0)
    sampled = lax.dot_general(
        jnp.ones((8, REGION), F32),
        sums[...],
        (((1,), (1,)), ((), ())),
        precision=lax.Precision.HIGHEST,
        preferred_element_type=F32,
    )
    for block in range(count // BLOCK):
        lane = slice(block * BLOCK, (block + 1) * BLOCK)
        row = slice(block, block + 1)
        vector = vector_ref[row, :]
        image = jnp.where(own_ref[row, :] == 1, 0.0, 0.5 * vector) + sampled[:1, lane]
        image = image + near_ref[row, :]
        if last:
            out_ref[0:1, lane] = vector
            out_ref[1:2, lane] = image
        else:
            out_ref[row, :] = image


def sample(last, places, parts, table, lines, flag, vector, near, reach_x, reach_y):
    count = places.shape[1]
    blocks = count // BLOCK
    pieces = len(parts)
    shape = (2, count) if last else (blocks, BLOCK)
    return pl.pallas_call(
        functools.partial(sample_kernel, last, reach_x, reach_y, pieces),
        in_specs=[in_smem()] + [whole_vmem()] * (pieces + 6),
        out_specs=whole_vmem(),
        out_shape=jax.ShapeDtypeStruct(shape, F32),
        scratch_shapes=[
            pltpu.VMEM((reach_x * reach_y, REGION), F32),
            pltpu.VMEM((pair_count(reach_x, reach_y), REGION), F32),
            pltpu.VMEM((count, REGION), F32),
        ],
        compiler_params=params(),
        cost_estimate=cost(reach_x * reach_y * 256 * 512, 4 * 16 * count * REGION),
        name="sample",
    )(
        places,
        *parts,
        *table,
        lines,
        flag.reshape(blocks, BLOCK),
        vector.reshape(blocks, BLOCK),
        near,
    )


def near_kernel(slots, blocks, place_ref, target_ref, *refs):
    even_ref, odd_ref, peers_ref, tile_ref, out_ref, held = refs
    count = peers_ref.shape[0]
    held[count : 2 * count, :] = peers_ref[...]
    on_left = lax.axis_index("wide") & 1
    for side, ref in ((1 - on_left, even_ref), (on_left, odd_ref)):
        top = from_short(ref[...])
        for piece in range(count // blocks):
            at = 6 + 2 * piece * blocks
            held[pl.ds(side * (2 * count) + piece * blocks, blocks), :] = decode_rounded(
                top[at : at + blocks], top[at + blocks : at + 2 * blocks]
            )
    out_ref[...] = jnp.zeros_like(out_ref)
    for slot in range(slots):
        picked = held[pl.ds(place_ref[slot], 1), :]
        picked = jnp.broadcast_to(picked, (16, BLOCK)).astype(BF16)
        product = lax.dot_general(
            picked,
            tile_ref[slot],
            (((1,), (1,)), ((), ())),
            preferred_element_type=F32,
        )
        target = pl.ds(target_ref[slot], 1)
        out_ref[target, :] = out_ref[target, :] + product[:1]


def near_field(places, targets, from_even, from_odd, peers, tiles, blocks, out_rows):
    slots = tiles.shape[0]
    head = from_even.shape[0] - 3 * GRID
    constant = lambda shape: pl.BlockSpec(shape, lambda i: (0,) * len(shape))
    return pl.pallas_call(
        functools.partial(near_kernel, slots, blocks),
        grid=(1,),
        in_specs=[
            in_smem(),
            in_smem(),
            constant((head, BLOCK)),
            constant((head, BLOCK)),
            constant(peers.shape),
            constant(tiles.shape),
        ],
        out_specs=constant((out_rows, BLOCK)),
        out_shape=jax.ShapeDtypeStruct((out_rows, BLOCK), F32),
        scratch_shapes=[pltpu.VMEM((3 * peers.shape[0], BLOCK), F32)],
        compiler_params=params(),
        cost_estimate=cost(2 * slots * 16 * BLOCK * BLOCK, 2 * slots * BLOCK * BLOCK),
        name="near_field",
    )(places, targets, from_even, from_odd, peers, tiles)


def shards(
    density,
    surface_flag,
    stencil_base,
    sample_weights,
    dipole_weights,
    near_target,
    near_source,
    near_tiles,
):
    x_count = lax.axis_size("wide")
    y_count = lax.axis_size(Y_AXES)
    y_index = lax.axis_index(Y_AXES)
    span_x = REGION // x_count
    span_y = REGION // y_count
    reach_x = span_x + 4
    reach_y = span_y + 4
    count = density.shape[0]
    blocks = count // BLOCK

    z_forward, z_inverse, y_forward, y_inverse, modes = tables(y_count, span_y)
    modes = lax.dynamic_index_in_dim(jnp.asarray(modes), y_index, 0, keepdims=False)

    neighbour = near_source // blocks
    flip = (y_index + neighbour % 3 - 1) ^ y_index
    sources = ((neighbour // 3) * y_count + flip) * blocks + near_source % blocks
    out_rows = up_to(blocks + 1, 8)
    live = near_target >= 0
    sources = jnp.where(live, sources, 0)
    targets = jnp.where(live, near_target, out_rows - 1)

    swaps = lambda pairs: [(i, j) for i, j in pairs] + [(j, i) for i, j in pairs]
    even_swap = swaps([(i, i + 1) for i in range(0, x_count - 1, 2)])
    odd_swap = swaps([(i, i + 1) for i in range(1, x_count - 1, 2)])
    far_swaps = [
        swaps([(i, i ^ flip) for i in range(x_count) if (i ^ flip) > i + 1])
        for flip in range(2, x_count)
    ]

    local, moving = [0], list(range(1, y_count))

    def flipped(parts, flips):
        return [
            lax.ppermute(part, Y_AXES, [(i, i ^ flip) for i in range(y_count)])
            for flip, part in zip(flips, parts)
        ]

    def convolve_and_sample(last, vector, sent, both, places, sample_lines):
        arrived = flipped(sent, moving)
        arrived = list(spread_rest(vector, both, z_forward, local)) + arrived
        spectrum, even_message, odd_message, own, peers, inner = forward(
            arrived, y_forward, modes, reach_x, reach_y, blocks
        )
        from_even = lax.ppermute(even_message, "wide", even_swap)
        from_odd = lax.ppermute(odd_message, "wide", odd_swap)
        fars = [lax.ppermute(own, "wide", pairs) for pairs in far_swaps]
        near_part = near_field(
            sources, targets, from_even, from_odd, peers, near_tiles, blocks, out_rows
        )
        *sent, high, low = inverse(
            spectrum,
            from_even,
            from_odd,
            own,
            inner,
            fars,
            y_inverse,
            modes,
            reach_x,
            reach_y,
            moving,
        )
        arrived = flipped(sent, moving)
        arrived = list(inverse_rest((high, low), y_inverse, reach_y, local)) + arrived
        return sample(
            last,
            places,
            arrived,
            z_inverse,
            sample_lines,
            surface_flag,
            vector,
            near_part,
            reach_x,
            reach_y,
        )

    raw = (stencil_base, surface_flag, sample_weights, dipole_weights)
    *sent, high, low, source_coeff, sample_coeff, places = spread(
        density, z_forward, None, raw, reach_x, reach_y, moving
    )
    sample_lines = place_lines(places, sample_coeff)
    source_lines = place_lines(places, source_coeff)
    first_image = convolve_and_sample(
        False, density, sent, (high, low), places, sample_lines
    ).reshape(-1)
    *sent, high, low = spread(
        first_image, z_forward, (places, source_lines), None, reach_x, reach_y, moving
    )
    return convolve_and_sample(True, first_image, sent, (high, low), places, sample_lines)


def solution(mesh):
    panels = P(("groups",) + ALL_AXES)
    columns = P(None, ("groups",) + ALL_AXES)
    in_specs = (
        panels,
        panels,
        columns,
        columns,
        columns,
        panels,
        panels,
        P(("groups",) + ALL_AXES, None, None),
    )
    return jax.shard_map(
        shards, mesh=mesh, in_specs=in_specs, out_specs=columns, check_vma=False
    )
```

```python
import functools
import math

import jax
import jax.numpy as jnp
import numpy as np
from jax import lax
from jax.experimental import pallas as pl
from jax.experimental.pallas import tpu as pltpu
from jax.sharding import PartitionSpec as P

GRID = 256
REGION = 128
BLOCK = 128
HALF = 64
KERNEL_GAIN = 4.0
SCREEN = 1.0 / 1024.0
LN2 = math.log(2.0)
Y_AXES = ("narrow", "pair")
ALL_AXES = ("wide", "narrow", "pair")
F32 = jnp.float32
BF16 = jnp.bfloat16
VMEM_LIMIT = 24 * 1024 * 1024
START_LIMIT = 60 * 1024 * 1024
FAR_FLOPS = 8 * 10**9
GROUP = 32
CHAINS = 2


def cas(angles):
    return np.cos(angles) + np.sin(angles)


def up_to(count, multiple):
    return -(-count // multiple) * multiple


def low_lanes(rows):
    return lax.broadcasted_iota(jnp.int32, (rows, 2 * HALF), 1) < HALF


def swap(values):
    return pltpu.roll(values, HALF, 1)


def split(values):
    high = values.astype(BF16)
    return high, (values - high.astype(F32)).astype(BF16)


def dot(left, right):
    return jnp.dot(left, right, preferred_element_type=F32)


def dot_three(left, right):
    return dot(left[0], right[0]) + (dot(left[0], right[1]) + dot(left[1], right[0]))


def params():
    return pltpu.CompilerParams(vmem_limit_bytes=VMEM_LIMIT)


def whole_vmem():
    return pl.BlockSpec(memory_space=pltpu.VMEM)


def anywhere():
    return pl.BlockSpec(memory_space=pl.ANY)


def in_smem():
    return pl.BlockSpec(memory_space=pltpu.SMEM)


def cost(flops, moved):
    return pl.CostEstimate(flops=flops, bytes_accessed=moved, transcendentals=0)


def full_scale(exponent, fraction):
    return fraction * jnp.exp(exponent * LN2) * (1.0 / 1024.0)


def fit_scale(largest):
    largest = jnp.maximum(largest, 1e-30)
    exponent = jnp.floor(jnp.log(largest) * (1.0 / LN2))
    fraction = jnp.ceil(largest * jnp.exp(-exponent * LN2) * 1024.0) + 1.0
    return exponent, fraction


def to_short(values):
    return values.astype(jnp.int32).astype(jnp.int16)


def from_short(values):
    return values.astype(jnp.int32).astype(F32)


def quantize(values, exponent, fraction):
    return to_short(jnp.round(values * (32767.0 / full_scale(exponent, fraction))))


def unit(exponent, fraction):
    return full_scale(exponent, fraction) * (1.0 / 32767.0)


def encode_rounded(values):
    rounded = values.astype(BF16).astype(F32)
    size = jnp.maximum(jnp.abs(rounded), 1e-30)
    exponent = jnp.floor(jnp.log(size) * (1.0 / LN2))
    return jnp.round(rounded * jnp.exp((10.0 - exponent) * LN2)), exponent


def decode_rounded(mantissa, exponent):
    return (mantissa * jnp.exp((exponent - 10.0) * LN2)).astype(BF16).astype(F32)


def send_piece(out, head, values):
    exponent, fraction = fit_scale(jnp.max(jnp.abs(values), axis=0, keepdims=True))
    head[0:1, :] = exponent
    head[1:2, :] = fraction
    top = head.shape[0]
    out[:top, :] = to_short(head[...])
    out[top:, :] = quantize(values, exponent, fraction)


def y_position():
    return lax.axis_index("narrow") * lax.axis_size("pair") + lax.axis_index("pair")


def halves(table):
    high = table.astype(jnp.bfloat16)
    return high, (table - high.astype(np.float64)).astype(jnp.bfloat16)


def tables(y_count, pair, span_y):
    depth = GRID // y_count
    reach = span_y + 4
    waves = np.arange(GRID)
    step = 2.0 * np.pi / GRID
    z_table = cas(step * np.outer(np.arange(REGION), waves))
    z_forward = np.zeros((y_count, 2 * REGION, 2 * HALF))
    z_inverse = np.zeros((y_count, 2 * HALF, 2 * REGION))
    symbols = 4.0 * np.sin(np.pi * waves / GRID) ** 2
    shift = np.full((y_count, GRID, 2 * HALF), 1.0)
    y_forward = np.zeros((GRID, y_count, up_to(reach, 8)))
    y_inverse = np.zeros((y_count, up_to(reach, 16), GRID))
    for block in range(y_count):
        mine = z_table[:, block * depth : (block + 1) * depth]
        for half in range(2):
            rows = slice(half * REGION, (half + 1) * REGION)
            lanes = slice(half * HALF, half * HALF + depth)
            z_forward[block, rows, lanes] = mine
            z_inverse[block, lanes, rows] = mine.T / GRID
            shift[block, :, lanes] = (
                SCREEN + symbols[:, None] + symbols[None, block * depth : (block + 1) * depth]
            )
        cells = block * span_y - 2 + np.arange(reach)
        y_table = cas(step * np.outer(waves, cells))
        y_forward[:, block, :reach] = y_table
        y_inverse[block, :reach] = y_table.T / GRID
    y_forward = y_forward.reshape(GRID, y_count // pair, -1).transpose(1, 0, 2)
    y_forward = halves(y_forward)
    y_forward = np.concatenate([y_forward[0], y_forward[0], y_forward[1]], axis=2)
    root = np.sqrt(shift * (shift + 4.0))
    decay = 2.0 / (2.0 + shift + root)
    log_decay = np.log(decay)
    ring = 1.0 / (1.0 - np.exp(GRID * log_decay))
    gain = KERNEL_GAIN / root
    modes = np.stack([decay, log_decay, ring, gain], axis=1).astype(np.float32)
    return (
        halves(z_forward),
        halves(z_inverse),
        y_forward,
        halves(y_inverse),
        modes,
    )


def weave(flag, sample_refs, dipole_refs, source_out, sample_out):
    place = lax.broadcasted_iota(jnp.int32, (4 * BLOCK, 4 * BLOCK), 0)
    lane = lax.broadcasted_iota(jnp.int32, (4 * BLOCK, 4 * BLOCK), 1)
    wanted = 4 * (place % BLOCK) + place // BLOCK
    mixing = jnp.where(lane == wanted, 1.0, 0.0).astype(BF16)
    stacked = []
    for tile, (sample_ref, dipole_ref) in enumerate(zip(sample_refs, dipole_refs)):
        charged = flag[:, tile * BLOCK : (tile + 1) * BLOCK] == 1
        rows = []
        for depth in range(4):
            sample = sample_ref[pl.ds(depth, 16, stride=4), :]
            dipole = dipole_ref[pl.ds(depth, 16, stride=4), :]
            rows.append(jnp.concatenate([jnp.where(charged, -sample, dipole), sample], axis=0))
        stacked.append(jnp.concatenate(rows, axis=1))
    weights = jnp.concatenate(stacked, axis=0)
    first, rest = split(weights)
    second, third = split(weights - first.astype(F32))
    woven = dot(first, mixing) + (dot(second, mixing) + dot(third, mixing))
    for tile in range(len(sample_refs)):
        for which, out in enumerate((source_out, sample_out)):
            for part in range(BLOCK // GROUP):
                at = (tile * (BLOCK // GROUP) + part) * 16
                lanes = slice(part * BLOCK, (part + 1) * BLOCK)
                for a in range(4):
                    row = tile * 32 + which * 16 + 4 * a
                    out[pl.ds(at + 8 * (a // 2) + a % 2, 4, stride=2), :] = woven[
                        row : row + 4, lanes
                    ]


def pair_rows(x, reach_x, reach_y):
    even = (x // 2) * 2 * reach_y + x % 2
    if x == 0 or x == reach_x - 1:
        return [even]
    return [even, reach_x * reach_y + ((x - 1) // 2) * 2 * reach_y + (x - 1) % 2]


def pair_count(reach_x, reach_y):
    return (2 * reach_x - 2) * reach_y


def in_window(lanes, depth):
    return ((lanes - depth) & -4) == 0


def add_panels(reach, woven, vector_ref, place_ref, weight_ref, grids):
    lanes = lax.broadcasted_iota(jnp.int32, (8, REGION), 1)

    def body(group, carry):
        at = pl.multiple_of(group * 16, 16)
        coeff = [weight_ref[pl.ds(at + 8 * q, 8), :] for q in range(2)] if woven else None
        for local in range(GROUP):
            panel = group * GROUP + local
            grid = grids[local % len(grids)]
            row = place_ref[0, panel]
            value = vector_ref[panel]
            if woven:
                depth = place_ref[1, panel]
                shift = (depth - 4 * local) & (REGION - 1)
                value = jnp.where(in_window(lanes, depth), value, 0.0)
                lines = [pltpu.roll(coeff[q], shift, 1) for q in range(2)]
            else:
                first = pl.multiple_of(panel * 16, 16)
                lines = [weight_ref[pl.ds(first + 8 * q, 8), :] for q in range(2)]
            places = [pl.ds(row, 8), pl.ds(row + 2 * reach, 8)]
            held = [grid[place, :] for place in places]
            for q in range(2):
                grid[places[q], :] = held[q] + lines[q] * value
        return carry

    lax.fori_loop(0, vector_ref.shape[0] // GROUP, body, 0)


def send_pieces(outs, flips, head, rounded, both, high_ref, low_ref):
    blocks = rounded.shape[0]
    mantissa, exponent = encode_rounded(rounded)
    head[...] = jnp.zeros_like(head)
    head[2 : 2 + blocks, :] = mantissa
    head[2 + blocks : 2 + 2 * blocks, :] = exponent
    mine = y_position()
    for at in range(0, len(flips), 2):
        pick = lambda ref: jnp.concatenate([ref[mine ^ flip] for flip in flips[at : at + 2]], axis=1)
        result = dot_three(both, (pick(high_ref), pick(low_ref)))
        for i, out in enumerate(outs[at : at + 2]):
            send_piece(out, head, result[:, i * 2 * HALF : (i + 1) * 2 * HALF])


def spread_grid(reach_x, reach_y, rounded, tables, outs, flips, wides, head, total, grids):
    for x in range(reach_x):
        parts = [
            grid[pl.ds(row, reach_y, stride=2), :]
            for row in pair_rows(x, reach_x, reach_y)
            for grid in grids
        ]
        total[x * reach_y : (x + 1) * reach_y, :] = sum(parts[1:], parts[0])
    half = reach_x * reach_y // 2
    both = jnp.concatenate([total[:half, :], total[half:, :]], axis=1)
    extra = wides[0].shape[0] - half
    if extra:
        both = jnp.concatenate([both, jnp.zeros((extra, 2 * REGION), F32)], axis=0)
    both = split(both)
    for wide, values in zip(wides, both):
        wide[...] = values
    send_pieces(outs, flips, head, rounded, both, *tables)


def start_kernel(reach_x, reach_y, flips, *refs):
    vector_ref, *remote = refs[:8]
    refs = refs[8:]
    outs, refs = refs[: len(flips)], refs[len(flips) :]
    wides, (weight_ref, sample_coeff_ref, places_out), refs = refs[:2], refs[2:5], refs[5:]
    rounded, high, low, stencil, flag, samples, dipoles = refs[:7]
    place_ref, sems, head, total = refs[7:11]
    grids = refs[11:]
    tiles = samples.shape[0]
    copies = []
    fetch = lambda source, target: copies.append(
        pltpu.make_async_copy(source, target, sems.at[len(copies)])
    )
    rounded_in, high_in, low_in, stencil_in, flag_in, sample_in, dipole_in = remote
    fetch(stencil_in, stencil)
    fetch(flag_in, flag)
    for tile in range(tiles):
        lanes = pl.ds(tile * BLOCK, BLOCK)
        fetch(sample_in.at[:, lanes], samples.at[tile])
        fetch(dipole_in.at[:, lanes], dipoles.at[tile])
    needed_first = len(copies)
    fetch(rounded_in, rounded)
    fetch(high_in, high)
    fetch(low_in, low)
    for copy in copies:
        copy.start()
    for grid in grids:
        grid[...] = jnp.zeros_like(grid)
    copies[0].wait()
    span_x, span_y = reach_x - 4, reach_y - 4
    local_x = stencil[0:1, :] - (lax.axis_index("wide") * span_x - 2)
    local_y = stencil[1:2, :] - (y_position() * span_y - 2)
    odd = local_x & 1
    places_out[0:1, :] = odd * (reach_x * reach_y) + (local_x >> 1) * (2 * reach_y) + 2 * local_y
    places_out[1:2, :] = stencil[2:3, :]
    to_scalar = pltpu.make_async_copy(places_out, place_ref, sems.at[len(copies)])
    to_scalar.start()
    for copy in copies[1:needed_first]:
        copy.wait()
    each = lambda values: [values.at[tile] for tile in range(tiles)]
    weave(flag[...], each(samples), each(dipoles), weight_ref, sample_coeff_ref)
    to_scalar.wait()
    add_panels(reach_y, True, vector_ref, place_ref, weight_ref, grids)
    for copy in copies[needed_first:]:
        copy.wait()
    spread_grid(
        reach_x, reach_y, rounded[...], (high, low), outs, flips, wides, head, total, grids
    )


def spread_kernel(reach_x, reach_y, flips, *refs):
    vector_ref, place_ref, rounded_ref, high_ref, low_ref, line_ref = refs[:6]
    refs = refs[6:]
    outs, wides, (head, total), grids = (
        refs[: len(flips)],
        refs[len(flips) : len(flips) + 2],
        refs[len(flips) + 2 : len(flips) + 4],
        refs[len(flips) + 4 :],
    )
    for grid in grids:
        grid[...] = jnp.zeros_like(grid)
    add_panels(reach_y, False, vector_ref, place_ref, line_ref, grids)
    spread_grid(
        reach_x,
        reach_y,
        rounded_ref[...],
        (high_ref, low_ref),
        outs,
        flips,
        wides,
        head,
        total,
        grids,
    )


def spread(vector, table, placed, raw, reach_x, reach_y, flips):
    count = vector.shape[0]
    half = reach_x * reach_y // 2
    blocks = count // BLOCK
    top = up_to(2 + 2 * blocks, 16)
    lanes = 2 * HALF
    body = up_to(half, 16)
    woven = (count // GROUP * 16, BLOCK)
    out_shapes = [jax.ShapeDtypeStruct((top + body, lanes), jnp.int16)] * len(flips)
    out_shapes += [jax.ShapeDtypeStruct((body, 2 * REGION), BF16)] * 2
    rounded = vector.reshape(blocks, BLOCK)
    work = [
        pltpu.VMEM((top, lanes), F32),
        pltpu.VMEM((reach_x * reach_y, REGION), F32),
    ] + [pltpu.VMEM((pair_count(reach_x, reach_y), REGION), F32)] * CHAINS
    if placed is None:
        stencil, flag, sample, dipole = raw
        operands = [vector, rounded, *table, stencil, flag.reshape(1, -1), sample, dipole]
        in_specs = [in_smem()] + [pl.BlockSpec(memory_space=pltpu.HBM)] * 7
        out_shapes += [jax.ShapeDtypeStruct(woven, F32)] * 2
        out_shapes += [jax.ShapeDtypeStruct((2, count), jnp.int32)]
        tiled = pltpu.VMEM((blocks, 64, BLOCK), F32)
        work = [
            pltpu.VMEM(rounded.shape, F32),
            pltpu.VMEM(table[0].shape, BF16),
            pltpu.VMEM(table[1].shape, BF16),
            pltpu.VMEM(stencil.shape, jnp.int32),
            pltpu.VMEM((1, count), jnp.int32),
            tiled,
            tiled,
            pltpu.SMEM((2, count), jnp.int32),
            pltpu.SemaphoreType.DMA((6 + 2 * blocks,)),
        ] + work
    else:
        operands = [vector, placed[0], rounded, *table, placed[1]]
        in_specs = [in_smem()] * 2 + [whole_vmem()] * 4
    return pl.pallas_call(
        functools.partial(
            start_kernel if placed is None else spread_kernel, reach_x, reach_y, flips
        ),
        in_specs=in_specs,
        out_specs=[whole_vmem()] * len(out_shapes),
        out_shape=out_shapes,
        scratch_shapes=work,
        compiler_params=pltpu.CompilerParams(
            vmem_limit_bytes=START_LIMIT if placed is None else VMEM_LIMIT
        ),
        cost_estimate=cost(2 * half * 256 * 512, 4 * 16 * count * REGION),
        name="start" if placed is None else "spread",
    )(*operands)


def spread_rest_kernel(flips, rounded_ref, wide_high, wide_low, high_ref, low_ref, *refs):
    outs, head = refs[:-1], refs[-1]
    both = (wide_high[...], wide_low[...])
    send_pieces(outs, flips, head, rounded_ref[...], both, high_ref, low_ref)


def spread_rest(vector, both, table, flips):
    blocks = vector.shape[0] // BLOCK
    top = up_to(2 + 2 * blocks, 16)
    shape = (top + both[0].shape[0], 2 * HALF)
    return pl.pallas_call(
        functools.partial(spread_rest_kernel, flips),
        in_specs=[whole_vmem()] * 5,
        out_specs=[whole_vmem()] * len(flips),
        out_shape=[jax.ShapeDtypeStruct(shape, jnp.int16)] * len(flips),
        scratch_shapes=[pltpu.VMEM((top, 2 * HALF), F32)],
        compiler_params=params(),
        cost_estimate=cost(2 * shape[0] * 256 * 256 * 3, 4 * shape[0] * 512),
        name="spread_rest",
    )(vector.reshape(blocks, BLOCK), *both, *table)


def lines_kernel(place_ref, coeff_ref, *refs):
    out_ref = refs[-1]
    lanes = lax.broadcasted_iota(jnp.int32, (8, REGION), 1)

    def body(group, carry):
        at = pl.multiple_of(group * 16, 16)
        coeff = [coeff_ref[pl.ds(at + 8 * q, 8), :] for q in range(2)]
        for local in range(GROUP):
            panel = group * GROUP + local
            depth = place_ref[1, panel]
            shift = (depth - 4 * local) & (REGION - 1)
            inside = in_window(lanes, depth)
            for q in range(2):
                first = pl.multiple_of(panel * 16 + 8 * q, 8)
                out_ref[pl.ds(first, 8), :] = jnp.where(inside, pltpu.roll(coeff[q], shift, 1), 0.0)
        return carry

    lax.fori_loop(0, place_ref.shape[1] // GROUP, body, 0)


def place_lines(places, coeff, awaited):
    count = places.shape[1]
    shape = (count * 16, REGION)
    return pl.pallas_call(
        lines_kernel,
        in_specs=[in_smem(), whole_vmem()] + [anywhere()] * len(awaited),
        out_specs=whole_vmem(),
        out_shape=jax.ShapeDtypeStruct(shape, F32),
        compiler_params=params(),
        cost_estimate=cost(16 * count * REGION, 4 * 16 * count * REGION),
        name="place_lines",
    )(places, coeff, *awaited)


def stack_pieces(parts, reach_x, reach_y, top, opened, stacked):
    half = reach_x // 2
    pitch = up_to(reach_y, 8)
    tall = len(parts) * pitch
    core = lax.axis_index("pair")
    for bit, part in enumerate(parts):
        first = from_short(part[:top, :])
        opened[...] = from_short(part[top:, :]) * unit(first[0:1], first[1:2])
        place = (core ^ bit) * pitch
        for i in range(half):
            stacked[pl.ds(pl.multiple_of(i * tall + place, 8), reach_y), :] = opened[
                i * reach_y : (i + 1) * reach_y, :
            ]


def transform_pieces(table, stacked, before, spectrum):
    half = spectrum.shape[0]
    tall = stacked.shape[0] // half

    def tripled(values):
        high, low = split(values)
        return jnp.concatenate([high, low, high], axis=0)

    for i in range(0, half, 2):
        places = range(i, min(i + 2, half))
        held = jnp.concatenate([stacked[j * tall : (j + 1) * tall, :] for j in places], axis=1)
        result = dot(table, tripled(held))
        for j in places:
            made = result[:, (j - i) * 2 * HALF : (j - i + 1) * 2 * HALF]
            spectrum[j] = made if before is None else before[j] + made


def forward_early_kernel(reach_x, reach_y, pair, *refs):
    parts = refs[:pair]
    table_ref, spectrum, opened, stacked = refs[pair:]
    top = parts[0].shape[0] - opened.shape[0]
    stacked[...] = jnp.zeros_like(stacked)
    stack_pieces(parts, reach_x, reach_y, top, opened, stacked)
    transform_pieces(table_ref[lax.axis_index("narrow")], stacked, None, spectrum)


def stacking_scratch(pair, reach_x, reach_y):
    half = reach_x // 2
    return [
        pltpu.VMEM((up_to(half * reach_y, 16), 2 * HALF), F32),
        pltpu.VMEM((half * pair * up_to(reach_y, 8), 2 * HALF), F32),
    ]


def forward_early(parts, table, reach_x, reach_y):
    half = reach_x // 2
    pair = len(parts)
    return pl.pallas_call(
        functools.partial(forward_early_kernel, reach_x, reach_y, pair),
        in_specs=[whole_vmem()] * (pair + 1),
        out_specs=whole_vmem(),
        out_shape=jax.ShapeDtypeStruct((half, GRID, 2 * HALF), F32),
        scratch_shapes=stacking_scratch(pair, reach_x, reach_y),
        compiler_params=params(),
        cost_estimate=cost(2 * half * 256 * 256 * 128, 4 * half * GRID * 2 * HALF * 2),
        name="forward_early",
    )(*parts, table)


def forward_kernel(reach_x, reach_y, blocks, pieces, awaited, *refs):
    parts = refs[:pieces]
    early_ref, table_ref, modes_ref = refs[pieces : pieces + 3]
    refs = refs[: pieces + 3] + refs[pieces + 3 + awaited :]
    spectrum, even_out, odd_out, own_out, peers_out, inner_out = refs[pieces + 3 : pieces + 9]
    opened, stacked, slabs, head = refs[pieces + 9 :]
    half = reach_x // 2
    pair = lax.axis_size("pair")
    top = parts[0].shape[0] - opened.shape[0]
    stacked[...] = jnp.zeros_like(stacked)
    head[...] = jnp.zeros_like(head)
    for piece in range(pieces):
        first = from_short(parts[piece][:top, :])
        mantissa, exponent = first[2 : 2 + blocks], first[2 + blocks : 2 + 2 * blocks]
        peers_out[piece * blocks : (piece + 1) * blocks, :] = decode_rounded(mantissa, exponent)
        at = 6 + 2 * piece * blocks
        head[at : at + blocks, :] = mantissa
        head[at + blocks : at + 2 * blocks, :] = exponent
    before = early_ref
    for chip in range(1, pieces // pair):
        stack_pieces(parts[chip * pair : (chip + 1) * pair], reach_x, reach_y, top, opened, stacked)
        transform_pieces(table_ref[lax.axis_index("narrow") ^ chip], stacked, before, spectrum)
        before = spectrum

    chunk = 32

    def body(index, largest):
        rows = pl.ds(pl.multiple_of(index * chunk, chunk), chunk)
        low = low_lanes(chunk)
        decay = modes_ref[0, rows, :]
        log_decay = modes_ref[1, rows, :]
        across_half = jnp.exp(half * log_decay)
        across_cut = jnp.exp((half - 4) * log_decay)
        layers = [spectrum[i, rows, :] for i in range(half)]
        run = layers[0]
        cut_right = run
        for i in range(1, half):
            run = decay * run + layers[i]
            if i == half - 5:
                cut_right = run
        right = run
        run = layers[half - 1]
        cut_left = run
        for i in range(half - 2, -1, -1):
            run = decay * run + layers[i]
            if i == 4:
                cut_left = run
        left = run
        inner_out[rows, :] = jnp.where(low, right, left)
        swapped_right, swapped_left = swap(right), swap(left)
        own = jnp.where(low, left + across_half * swapped_left, right + across_half * swapped_right)
        made = [
            jnp.where(low, swap(layers[half - 4]), layers[half - 3]),
            jnp.where(low, swap(layers[half - 2]), layers[half - 1]),
            jnp.where(low, own, cut_right + across_cut * swapped_right),
            jnp.where(low, layers[0], swap(layers[1])),
            jnp.where(low, layers[2], swap(layers[3])),
            jnp.where(low, cut_left + across_cut * swapped_left, own),
            own,
        ]
        for slab, values in enumerate(made):
            slabs[slab, rows, :] = values
        return tuple(
            jnp.maximum(old, jnp.max(jnp.abs(values).reshape(chunk // 8, 8, 2 * HALF), axis=0))
            for old, values in zip(largest, made)
        )

    zero = jnp.zeros((8, 2 * HALF), F32)
    largest = lax.fori_loop(0, GRID // chunk, body, (zero,) * 7)
    scales = [fit_scale(jnp.max(value, axis=0, keepdims=True)) for value in largest]
    head_rows = head.shape[0]

    def send(out, first):
        for slab in range(3):
            exponent, fraction = scales[first + slab]
            head[2 * slab : 2 * slab + 1, :] = exponent
            head[2 * slab + 1 : 2 * slab + 2, :] = fraction
            at = head_rows + slab * GRID
            out[at : at + GRID, :] = quantize(slabs[first + slab], exponent, fraction)
        out[:head_rows, :] = to_short(head[...])

    on_left = lax.axis_index("wide") & 1

    @pl.when(on_left == 0)
    def _():
        send(even_out, 0)
        send(odd_out, 3)

    @pl.when(on_left == 1)
    def _():
        send(even_out, 3)
        send(odd_out, 0)

    exponent, fraction = scales[6]
    head[0:1, :] = exponent
    head[1:2, :] = fraction
    own_out[:16, :] = to_short(head[:16, :])
    own_out[16:, :] = quantize(slabs[6], exponent, fraction)


def forward(parts, early, table, modes, reach_x, reach_y, blocks, awaited):
    pieces = len(parts)
    half = reach_x // 2
    lanes = 2 * HALF
    head = up_to(6 + 2 * pieces * blocks, 16)
    short = lambda rows: jax.ShapeDtypeStruct((rows, lanes), jnp.int16)
    return pl.pallas_call(
        functools.partial(
            forward_kernel, reach_x, reach_y, blocks, pieces, len(awaited)
        ),
        in_specs=[whole_vmem()] * (pieces + 3) + [anywhere()] * len(awaited),
        out_specs=[whole_vmem()] * 6,
        out_shape=[
            jax.ShapeDtypeStruct((half, GRID, lanes), F32),
            short(head + 3 * GRID),
            short(head + 3 * GRID),
            short(16 + GRID),
            jax.ShapeDtypeStruct((pieces * blocks, BLOCK), F32),
            jax.ShapeDtypeStruct((GRID, lanes), F32),
        ],
        scratch_shapes=stacking_scratch(pieces // table.shape[0], reach_x, reach_y)
        + [
            pltpu.VMEM((7, GRID, lanes), F32),
            pltpu.VMEM((head, lanes), F32),
        ],
        compiler_params=params(),
        cost_estimate=cost(2 * half * 256 * 256 * 128, 4 * half * GRID * lanes * 2),
        name="forward",
    )(*parts, early, table, modes, *awaited)


def far_kernel(reach_x, *refs):
    own_ref, *far_refs = refs[:-2]
    modes_ref, out_ref = refs[-2:]
    span = reach_x - 4
    x_index = lax.axis_index("wide")
    low = low_lanes(GRID)
    log_decay = modes_ref[1]

    def moment(ref):
        first = from_short(ref[:16, :])
        return from_short(ref[16:, :]) * unit(first[0:1], first[1:2])

    total = moment(own_ref) * jnp.exp((GRID - reach_x) * log_decay)
    for flip, ref in enumerate(far_refs, 2):
        behind = x_index - (x_index ^ flip)
        powers = []
        for distance in (-behind, behind):
            ahead = span * distance - reach_x
            powers.append(jnp.where(distance >= 2, ahead, ahead + GRID).astype(F32))
        total = total + moment(ref) * jnp.exp(jnp.where(low, *powers) * log_decay)
    out_ref[...] = total


def far_moments(own, fars, modes, reach_x):
    return pl.pallas_call(
        functools.partial(far_kernel, reach_x),
        in_specs=[whole_vmem()] * (2 + len(fars)),
        out_specs=whole_vmem(),
        out_shape=jax.ShapeDtypeStruct((GRID, 2 * HALF), F32),
        compiler_params=params(),
        cost_estimate=cost(FAR_FLOPS, 4 * GRID * 2 * HALF * (3 + len(fars))),
        name="far_moments",
    )(own, *fars, modes)


def send_fields(outs, flips, reach_y, field_high, field_low, high_ref, low_ref, ready, head):
    half = field_high.shape[0]
    mine = y_position()
    pitch = up_to(reach_y, 16)
    pick = lambda ref: jnp.concatenate([ref[mine ^ flip] for flip in flips], axis=0)
    table = (pick(high_ref), pick(low_ref))
    for i in range(0, half, 2):
        many = min(2, half - i)
        join = lambda ref: jnp.concatenate([ref[i + j] for j in range(many)], axis=1)
        result = dot_three(table, (join(field_high), join(field_low)))
        for j in range(many):
            for piece in range(len(flips)):
                ready[piece, (i + j) * reach_y : (i + j + 1) * reach_y, :] = result[
                    piece * pitch : piece * pitch + reach_y, j * 2 * HALF : (j + 1) * 2 * HALF
                ]
    head[...] = jnp.zeros_like(head)
    for piece, out in enumerate(outs):
        if ready.shape[1] > half * reach_y:
            ready[piece, half * reach_y :, :] = jnp.zeros_like(ready[piece, half * reach_y :, :])
        send_piece(out, head, ready[piece])


def inverse_kernel(reach_x, reach_y, flips, *refs):
    spectrum, from_even, from_odd, far_ref, inner_ref = refs[:5]
    high_ref, low_ref, modes_ref = refs[5:8]
    outs = refs[8 : 8 + len(flips)]
    field_high, field_low, ready, head = refs[8 + len(flips) :]
    half = reach_x // 2
    span = reach_x - 4
    chunk = 32
    head_rows = from_even.shape[0] - 3 * GRID
    on_left = (lax.axis_index("wide") & 1) == 1
    both_heads = from_short(from_even[:16, :]), from_short(from_odd[:16, :])
    both_units = [
        [unit(first[2 * slab : 2 * slab + 1], first[2 * slab + 1 : 2 * slab + 2]) for slab in range(3)]
        for first in both_heads
    ]

    def sided(even, odd):
        return jnp.where(on_left, even, odd), jnp.where(on_left, odd, even)

    def body(index, carry):
        first = pl.multiple_of(index * chunk, chunk)
        rows = pl.ds(first, chunk)
        low = low_lanes(chunk)
        decay = modes_ref[0, rows, :]
        log_decay = modes_ref[1, rows, :]
        ring = modes_ref[2, rows, :]
        gain = modes_ref[3, rows, :]
        across_half = jnp.exp(half * log_decay)
        across_cut = jnp.exp((half - 4) * log_decay)
        around = jnp.exp((GRID - 4) * log_decay)
        beside = jnp.exp((GRID - reach_x - span) * log_decay)
        layers = [spectrum[i, rows, :] for i in range(half)]

        def slab(which):
            at = pl.ds(pl.multiple_of(head_rows + which * GRID + index * chunk, chunk), chunk)
            even = from_short(from_even[at, :]) * both_units[0][which]
            return sided(even, from_short(from_odd[at, :]) * both_units[1][which])

        head_layers, tail_layers = zip(slab(0), slab(1))
        left_moments, right_moments = slab(2)
        zero = jnp.zeros_like(decay)
        from_head = [head_layers[0], swap(head_layers[0]), head_layers[1], swap(head_layers[1])]
        from_tail = [swap(tail_layers[0]), tail_layers[0], swap(tail_layers[1]), tail_layers[1]]
        head_sum = from_head[0]
        for i in range(1, 4):
            head_sum = decay * head_sum + from_head[i]
        tail_sum = from_tail[3]
        for i in range(2, -1, -1):
            tail_sum = decay * tail_sum + from_tail[i]
        for i in range(4):
            layers[i] = layers[i] + jnp.where(low, from_head[i], zero)
        for i in range(4):
            place = half - 4 + i
            layers[place] = layers[place] + jnp.where(low, zero, from_tail[i])
        total = far_ref[rows, :]
        one = jnp.ones_like(decay)
        total = total + left_moments * jnp.where(low, beside, one)
        total = total + right_moments * jnp.where(low, one, beside)
        shared = jnp.where(low, head_sum, tail_sum)
        entering = (swap(total) + around * shared) * ring
        leaving = swap(across_half * entering + across_cut * shared + inner_ref[rows, :])
        run = jnp.where(low, entering, leaving)
        forward_runs = []
        for i in range(half):
            run = decay * run + layers[i]
            forward_runs.append(run)
        run = jnp.where(low, leaving, entering)
        for i in range(half - 1, -1, -1):
            ahead = decay * run
            high, rest = split(gain * (forward_runs[i] + ahead))
            field_high[i, rows, :] = high
            field_low[i, rows, :] = rest
            run = ahead + layers[i]
        return carry

    lax.fori_loop(0, GRID // chunk, body, 0)
    send_fields(outs, flips, reach_y, field_high, field_low, high_ref, low_ref, ready, head)


def inverse(spectrum, from_even, from_odd, far, inner, table, modes, reach_x, reach_y, flips):
    half = reach_x // 2
    lanes = 2 * HALF
    body = up_to(half * reach_y, 16)
    shapes = [jax.ShapeDtypeStruct((16 + body, lanes), jnp.int16)] * len(flips)
    shapes += [jax.ShapeDtypeStruct((half, GRID, lanes), BF16)] * 2
    return pl.pallas_call(
        functools.partial(inverse_kernel, reach_x, reach_y, flips),
        in_specs=[whole_vmem()] * 8,
        out_specs=[whole_vmem()] * len(shapes),
        out_shape=shapes,
        scratch_shapes=[
            pltpu.VMEM((len(flips), body, lanes), F32),
            pltpu.VMEM((16, lanes), F32),
        ],
        compiler_params=params(),
        cost_estimate=cost(2 * half * 256 * 256 * 128, 4 * half * GRID * lanes * 2),
        name="inverse",
    )(spectrum, from_even, from_odd, far, inner, *table, modes)


def inverse_rest_kernel(reach_y, flips, field_high, field_low, high_ref, low_ref, *refs):
    outs, (ready, head) = refs[: len(flips)], refs[len(flips) :]
    send_fields(outs, flips, reach_y, field_high, field_low, high_ref, low_ref, ready, head)


def inverse_rest(field, table, reach_y, flips):
    half = field[0].shape[0]
    lanes = 2 * HALF
    body = up_to(half * reach_y, 16)
    return pl.pallas_call(
        functools.partial(inverse_rest_kernel, reach_y, flips),
        in_specs=[whole_vmem()] * 4,
        out_specs=[whole_vmem()] * len(flips),
        out_shape=[jax.ShapeDtypeStruct((16 + body, lanes), jnp.int16)] * len(flips),
        scratch_shapes=[
            pltpu.VMEM((len(flips), body, lanes), F32),
            pltpu.VMEM((16, lanes), F32),
        ],
        compiler_params=params(),
        cost_estimate=cost(2 * half * 256 * 256 * 128, 4 * half * GRID * lanes * 2),
        name="inverse_rest",
    )(*field, *table)


def sum_rows(values):
    row = lax.broadcasted_iota(jnp.int32, values[0].shape, 0)
    for step in (4, 2, 1):
        low = (row & step) == 0
        paired = []
        for one, other in zip(values[: len(values) // 2], values[len(values) // 2 :]):
            kept = jnp.where(low, one, other)
            moved = jnp.where(low, other, one)
            if step == 4:
                moved = pltpu.roll(moved, 4, 0)
            else:
                moved = jnp.where(low, pltpu.roll(moved, 8 - step, 0), pltpu.roll(moved, step, 0))
            paired.append(kept + moved)
        values = paired
    return values[0]


def z_lines(parts, flips, high_ref, low_ref):
    mine = y_position()
    opened = []
    for part in parts:
        first = from_short(part[:16, :])
        opened.append(from_short(part[16:, :]) * unit(first[0:1], first[1:2]))
    values = split(jnp.concatenate(opened, axis=1))
    pick = lambda ref: jnp.concatenate([ref[mine ^ flip] for flip in flips], axis=0)
    return dot_three(values, (pick(high_ref), pick(low_ref)))


def sample_early_kernel(*refs):
    *parts, high_ref, low_ref, out_ref = refs
    out_ref[...] = z_lines(parts, range(len(parts)), high_ref, low_ref)


def sample_early(parts, table):
    rows = parts[0].shape[0] - 16
    return pl.pallas_call(
        sample_early_kernel,
        in_specs=[whole_vmem()] * (len(parts) + 2),
        out_specs=whole_vmem(),
        out_shape=jax.ShapeDtypeStruct((rows, 2 * REGION), F32),
        compiler_params=params(),
        cost_estimate=cost(2 * rows * 256 * 256 * 3, 4 * rows * 512),
        name="sample_early",
    )(*parts, *table)


def sample_kernel(last, reach_x, reach_y, flips, place_ref, *refs):
    parts = refs[: len(flips)]
    early_ref, high_ref, low_ref, line_ref, own_ref, vector_ref, near_ref, out_ref = refs[
        len(flips) : len(flips) + 8
    ]
    flat, field, sums = refs[len(flips) + 8 :]
    half_rows = reach_x * reach_y // 2
    both = early_ref[...] + z_lines(parts, flips, high_ref, low_ref)
    flat[:half_rows, :] = both[:half_rows, :REGION]
    flat[half_rows:, :] = both[:half_rows, REGION:]
    for x in range(reach_x):
        layer = flat[x * reach_y : (x + 1) * reach_y, :]
        for row in pair_rows(x, reach_x, reach_y):
            field[pl.ds(row, reach_y, stride=2), :] = layer
    count = place_ref.shape[1]

    def body(group, carry):
        for eight in range(0, GROUP, 8):
            totals = []
            for local in range(eight, eight + 8):
                panel = group * GROUP + local
                row = place_ref[0, panel]
                first = pl.multiple_of(panel * 16, 16)
                totals.append(
                    field[pl.ds(row, 8), :] * line_ref[pl.ds(first, 8), :]
                    + field[pl.ds(row + 2 * reach_y, 8), :] * line_ref[pl.ds(first + 8, 8), :]
                )
            sums[pl.ds(pl.multiple_of(group * GROUP + eight, 8), 8), :] = sum_rows(totals)
        return carry

    lax.fori_loop(0, count // GROUP, body, 0)
    sampled = lax.dot_general(
        jnp.ones((8, REGION), F32),
        sums[...],
        (((1,), (1,)), ((), ())),
        precision=lax.Precision.HIGHEST,
        preferred_element_type=F32,
    )
    for block in range(count // BLOCK):
        lane = slice(block * BLOCK, (block + 1) * BLOCK)
        row = slice(block, block + 1)
        vector = vector_ref[row, :]
        image = jnp.where(own_ref[row, :] == 1, 0.0, 0.5 * vector) + sampled[:1, lane]
        image = image + near_ref[row, :]
        if last:
            out_ref[0:1, lane] = vector
            out_ref[1:2, lane] = image
        else:
            out_ref[row, :] = image


def sample(last, places, parts, flips, early, table, lines, flag, vector, near, reach_x, reach_y):
    count = places.shape[1]
    blocks = count // BLOCK
    shape = (2, count) if last else (blocks, BLOCK)
    return pl.pallas_call(
        functools.partial(sample_kernel, last, reach_x, reach_y, flips),
        in_specs=[in_smem()] + [whole_vmem()] * (len(parts) + 7),
        out_specs=whole_vmem(),
        out_shape=jax.ShapeDtypeStruct(shape, F32),
        scratch_shapes=[
            pltpu.VMEM((reach_x * reach_y, REGION), F32),
            pltpu.VMEM((pair_count(reach_x, reach_y), REGION), F32),
            pltpu.VMEM((count, REGION), F32),
        ],
        compiler_params=params(),
        cost_estimate=cost(reach_x * reach_y * 256 * 512, 4 * 16 * count * REGION),
        name="sample",
    )(
        places,
        *parts,
        early,
        *table,
        lines,
        flag.reshape(blocks, BLOCK),
        vector.reshape(blocks, BLOCK),
        near,
    )


def near_kernel(slots, blocks, place_ref, target_ref, *refs):
    even_ref, odd_ref, peers_ref, tile_ref, out_ref, held = refs
    count = peers_ref.shape[0]
    held[count : 2 * count, :] = peers_ref[...]
    on_left = lax.axis_index("wide") & 1
    for side, ref in ((1 - on_left, even_ref), (on_left, odd_ref)):
        top = from_short(ref[...])
        for piece in range(count // blocks):
            at = 6 + 2 * piece * blocks
            held[pl.ds(side * (2 * count) + piece * blocks, blocks), :] = decode_rounded(
                top[at : at + blocks], top[at + blocks : at + 2 * blocks]
            )
    out_ref[...] = jnp.zeros_like(out_ref)
    for slot in range(slots):
        picked = held[pl.ds(place_ref[slot], 1), :]
        picked = jnp.broadcast_to(picked, (16, BLOCK)).astype(BF16)
        product = lax.dot_general(
            picked,
            tile_ref[slot],
            (((1,), (1,)), ((), ())),
            preferred_element_type=F32,
        )
        target = pl.ds(target_ref[slot], 1)
        out_ref[target, :] = out_ref[target, :] + product[:1]


def near_field(places, targets, from_even, from_odd, peers, tiles, blocks, out_rows):
    slots = tiles.shape[0]
    head = from_even.shape[0] - 3 * GRID
    constant = lambda shape: pl.BlockSpec(shape, lambda i: (0,) * len(shape))
    return pl.pallas_call(
        functools.partial(near_kernel, slots, blocks),
        grid=(1,),
        in_specs=[
            in_smem(),
            in_smem(),
            constant((head, BLOCK)),
            constant((head, BLOCK)),
            constant(peers.shape),
            constant(tiles.shape),
        ],
        out_specs=constant((out_rows, BLOCK)),
        out_shape=jax.ShapeDtypeStruct((out_rows, BLOCK), F32),
        scratch_shapes=[pltpu.VMEM((3 * peers.shape[0], BLOCK), F32)],
        compiler_params=params(),
        cost_estimate=cost(2 * slots * 16 * BLOCK * BLOCK, 2 * slots * BLOCK * BLOCK),
        name="near_field",
    )(places, targets, from_even, from_odd, peers, tiles)


def shards(
    density,
    surface_flag,
    stencil_base,
    sample_weights,
    dipole_weights,
    near_target,
    near_source,
    near_tiles,
):
    x_count = lax.axis_size("wide")
    y_count = lax.axis_size(Y_AXES)
    y_index = lax.axis_index(Y_AXES)
    pair = lax.axis_size("pair")
    span_x = REGION // x_count
    span_y = REGION // y_count
    reach_x = span_x + 4
    reach_y = span_y + 4
    count = density.shape[0]
    blocks = count // BLOCK

    z_forward, z_inverse, y_forward, y_inverse, modes = tables(y_count, pair, span_y)
    modes = lax.dynamic_index_in_dim(jnp.asarray(modes), y_index, 0, keepdims=False)

    neighbour = near_source // blocks
    flip = (y_index + neighbour % 3 - 1) ^ y_index
    sources = ((neighbour // 3) * y_count + flip) * blocks + near_source % blocks
    out_rows = up_to(blocks + 1, 8)
    live = near_target >= 0
    sources = jnp.where(live, sources, 0)
    targets = jnp.where(live, near_target, out_rows - 1)

    swaps = lambda pairs: [(i, j) for i, j in pairs] + [(j, i) for i, j in pairs]
    even_swap = swaps([(i, i + 1) for i in range(0, x_count - 1, 2)])
    odd_swap = swaps([(i, i + 1) for i in range(1, x_count - 1, 2)])
    far_swaps = [
        swaps([(i, i ^ flip) for i in range(x_count) if (i ^ flip) > i + 1])
        for flip in range(2, x_count)
    ]

    local, moving = [0], list(range(1, y_count))

    def flipped(parts, flips):
        return [
            lax.ppermute(part, Y_AXES, [(i, i ^ flip) for i in range(y_count)])
            for flip, part in zip(flips, parts)
        ]

    def convolve_and_sample(last, vector, sent, both, places, sample_lines, awaited):
        arrived = flipped(sent, moving)
        arrived = list(spread_rest(vector, both, z_forward, local)) + arrived
        early = forward_early(arrived[:pair], y_forward, reach_x, reach_y)
        spectrum, even_message, odd_message, own, peers, inner = forward(
            arrived, early, y_forward, modes, reach_x, reach_y, blocks, awaited
        )
        fars = [lax.ppermute(own, "wide", pairs) for pairs in far_swaps]
        from_even = lax.ppermute(even_message, "wide", even_swap)
        from_odd = lax.ppermute(odd_message, "wide", odd_swap)
        near_part = near_field(
            sources, targets, from_even, from_odd, peers, near_tiles, blocks, out_rows
        )
        *sent, high, low = inverse(
            spectrum,
            from_even,
            from_odd,
            far_moments(own, fars, modes, reach_x),
            inner,
            y_inverse,
            modes,
            reach_x,
            reach_y,
            moving,
        )
        arrived = flipped(sent, moving)
        arrived = list(inverse_rest((high, low), y_inverse, reach_y, local)) + arrived
        image = sample(
            last,
            places,
            arrived[pair:],
            list(range(pair, y_count)),
            sample_early(arrived[:pair], z_inverse),
            z_inverse,
            sample_lines,
            surface_flag,
            vector,
            near_part,
            reach_x,
            reach_y,
        )
        return image, near_part

    raw = (stencil_base, surface_flag, sample_weights, dipole_weights)
    *sent, high, low, source_coeff, sample_coeff, places = spread(
        density, z_forward, None, raw, reach_x, reach_y, moving
    )
    sample_lines = place_lines(places, sample_coeff, [])
    first_image, near_part = convolve_and_sample(
        False, density, sent, (high, low), places, sample_lines, [sample_lines]
    )
    first_image = first_image.reshape(-1)
    source_lines = place_lines(places, source_coeff, [near_part])
    *sent, high, low = spread(
        first_image, z_forward, (places, source_lines), None, reach_x, reach_y, moving
    )
    both_images, _ = convolve_and_sample(
        True, first_image, sent, (high, low), places, sample_lines, []
    )
    return both_images


def solution(mesh):
    panels = P(("groups",) + ALL_AXES)
    columns = P(None, ("groups",) + ALL_AXES)
    in_specs = (
        panels,
        panels,
        columns,
        columns,
        columns,
        panels,
        panels,
        P(("groups",) + ALL_AXES, None, None),
    )
    return jax.shard_map(
        shards, mesh=mesh, in_specs=in_specs, out_specs=columns, check_vma=False
    )
```

```python
import functools
import math

import jax
import jax.numpy as jnp
import numpy as np
from jax import lax
from jax.experimental import pallas as pl
from jax.experimental.pallas import tpu as pltpu
from jax.sharding import PartitionSpec as P

GRID = 256
REGION = 128
BLOCK = 128
HALF = 64
KERNEL_GAIN = 4.0
SCREEN = 1.0 / 1024.0
LN2 = math.log(2.0)
Y_AXES = ("narrow", "pair")
ALL_AXES = ("wide", "narrow", "pair")
F32 = jnp.float32
BF16 = jnp.bfloat16
VMEM_LIMIT = 24 * 1024 * 1024
START_LIMIT = 60 * 1024 * 1024
GROUP = 32
CHAINS = 2


def cas(angles):
    return np.cos(angles) + np.sin(angles)


def up_to(count, multiple):
    return -(-count // multiple) * multiple


def low_lanes(rows):
    return lax.broadcasted_iota(jnp.int32, (rows, 2 * HALF), 1) < HALF


def swap(values):
    return pltpu.roll(values, HALF, 1)


def split(values):
    high = values.astype(BF16)
    return high, (values - high.astype(F32)).astype(BF16)


def dot(left, right):
    return jnp.dot(left, right, preferred_element_type=F32)


def dot_three(left, right):
    return dot(left[0], right[0]) + (dot(left[0], right[1]) + dot(left[1], right[0]))


def params():
    return pltpu.CompilerParams(vmem_limit_bytes=VMEM_LIMIT)


def whole_vmem():
    return pl.BlockSpec(memory_space=pltpu.VMEM)


def anywhere():
    return pl.BlockSpec(memory_space=pl.ANY)


def in_smem():
    return pl.BlockSpec(memory_space=pltpu.SMEM)


def cost(flops, moved):
    return pl.CostEstimate(flops=flops, bytes_accessed=moved, transcendentals=0)


def full_scale(exponent, fraction):
    return fraction * jnp.exp(exponent * LN2) * (1.0 / 1024.0)


def fit_scale(largest):
    largest = jnp.maximum(largest, 1e-30)
    exponent = jnp.floor(jnp.log(largest) * (1.0 / LN2))
    fraction = jnp.ceil(largest * jnp.exp(-exponent * LN2) * 1024.0) + 1.0
    return exponent, fraction


def to_short(values):
    return values.astype(jnp.int32).astype(jnp.int16)


def from_short(values):
    return values.astype(jnp.int32).astype(F32)


def quantize(values, exponent, fraction):
    return to_short(jnp.round(values * (32767.0 / full_scale(exponent, fraction))))


def unit(exponent, fraction):
    return full_scale(exponent, fraction) * (1.0 / 32767.0)


def encode_rounded(values):
    rounded = values.astype(BF16).astype(F32)
    size = jnp.maximum(jnp.abs(rounded), 1e-30)
    exponent = jnp.floor(jnp.log(size) * (1.0 / LN2))
    return jnp.round(rounded * jnp.exp((10.0 - exponent) * LN2)), exponent


def decode_rounded(mantissa, exponent):
    return (mantissa * jnp.exp((exponent - 10.0) * LN2)).astype(BF16).astype(F32)


def send_piece(out, head, values):
    exponent, fraction = fit_scale(jnp.max(jnp.abs(values), axis=0, keepdims=True))
    head[0:1, :] = exponent
    head[1:2, :] = fraction
    top = head.shape[0]
    out[:top, :] = to_short(head[...])
    out[top:, :] = quantize(values, exponent, fraction)


def y_position():
    return lax.axis_index("narrow") * lax.axis_size("pair") + lax.axis_index("pair")


def halves(table):
    high = table.astype(jnp.bfloat16)
    return high, (table - high.astype(np.float64)).astype(jnp.bfloat16)


def tables(y_count, pair, span_y):
    depth = GRID // y_count
    reach = span_y + 4
    waves = np.arange(GRID)
    step = 2.0 * np.pi / GRID
    z_table = cas(step * np.outer(np.arange(REGION), waves))
    z_forward = np.zeros((y_count, 2 * REGION, 2 * HALF))
    z_inverse = np.zeros((y_count, 2 * HALF, 2 * REGION))
    symbols = 4.0 * np.sin(np.pi * waves / GRID) ** 2
    shift = np.full((y_count, GRID, 2 * HALF), 1.0)
    y_forward = np.zeros((GRID, y_count, up_to(reach, 8)))
    y_inverse = np.zeros((y_count, up_to(reach, 16), GRID))
    for block in range(y_count):
        mine = z_table[:, block * depth : (block + 1) * depth]
        for half in range(2):
            rows = slice(half * REGION, (half + 1) * REGION)
            lanes = slice(half * HALF, half * HALF + depth)
            z_forward[block, rows, lanes] = mine
            z_inverse[block, lanes, rows] = mine.T / GRID
            shift[block, :, lanes] = (
                SCREEN + symbols[:, None] + symbols[None, block * depth : (block + 1) * depth]
            )
        cells = block * span_y - 2 + np.arange(reach)
        y_table = cas(step * np.outer(waves, cells))
        y_forward[:, block, :reach] = y_table
        y_inverse[block, :reach] = y_table.T / GRID
    y_forward = y_forward.reshape(GRID, y_count // pair, -1).transpose(1, 0, 2)
    y_forward = halves(y_forward)
    y_forward = np.concatenate([y_forward[0], y_forward[0], y_forward[1]], axis=2)
    root = np.sqrt(shift * (shift + 4.0))
    decay = 2.0 / (2.0 + shift + root)
    log_decay = np.log(decay)
    ring = 1.0 / (1.0 - np.exp(GRID * log_decay))
    gain = KERNEL_GAIN / root
    modes = np.stack([decay, log_decay, ring, gain], axis=1).astype(np.float32)
    return (
        halves(z_forward),
        halves(z_inverse),
        y_forward,
        halves(y_inverse),
        modes,
    )


def weave(flag, sample_refs, dipole_refs, source_out, sample_out):
    place = lax.broadcasted_iota(jnp.int32, (4 * BLOCK, 4 * BLOCK), 0)
    lane = lax.broadcasted_iota(jnp.int32, (4 * BLOCK, 4 * BLOCK), 1)
    wanted = 4 * (place % BLOCK) + place // BLOCK
    mixing = jnp.where(lane == wanted, 1.0, 0.0).astype(BF16)
    stacked = []
    for tile, (sample_ref, dipole_ref) in enumerate(zip(sample_refs, dipole_refs)):
        charged = flag[:, tile * BLOCK : (tile + 1) * BLOCK] == 1
        rows = []
        for depth in range(4):
            sample = sample_ref[pl.ds(depth, 16, stride=4), :]
            dipole = dipole_ref[pl.ds(depth, 16, stride=4), :]
            rows.append(jnp.concatenate([jnp.where(charged, -sample, dipole), sample], axis=0))
        stacked.append(jnp.concatenate(rows, axis=1))
    weights = jnp.concatenate(stacked, axis=0)
    first, rest = split(weights)
    second, third = split(weights - first.astype(F32))
    woven = dot(first, mixing) + (dot(second, mixing) + dot(third, mixing))
    for tile in range(len(sample_refs)):
        for which, out in enumerate((source_out, sample_out)):
            for part in range(BLOCK // GROUP):
                at = (tile * (BLOCK // GROUP) + part) * 16
                lanes = slice(part * BLOCK, (part + 1) * BLOCK)
                for a in range(4):
                    row = tile * 32 + which * 16 + 4 * a
                    out[pl.ds(at + 8 * (a // 2) + a % 2, 4, stride=2), :] = woven[
                        row : row + 4, lanes
                    ]


def pair_rows(x, reach_x, reach_y):
    even = (x // 2) * 2 * reach_y + x % 2
    if x == 0 or x == reach_x - 1:
        return [even]
    return [even, reach_x * reach_y + ((x - 1) // 2) * 2 * reach_y + (x - 1) % 2]


def pair_count(reach_x, reach_y):
    return (2 * reach_x - 2) * reach_y


def in_window(lanes, depth):
    return ((lanes - depth) & -4) == 0


def add_panels(reach, woven, vector_ref, place_ref, weight_ref, grids):
    lanes = lax.broadcasted_iota(jnp.int32, (8, REGION), 1)

    def body(group, carry):
        at = pl.multiple_of(group * 16, 16)
        coeff = [weight_ref[pl.ds(at + 8 * q, 8), :] for q in range(2)] if woven else None
        for local in range(GROUP):
            panel = group * GROUP + local
            grid = grids[local % len(grids)]
            row = place_ref[0, panel]
            value = vector_ref[panel]
            if woven:
                depth = place_ref[1, panel]
                shift = (depth - 4 * local) & (REGION - 1)
                value = jnp.where(in_window(lanes, depth), value, 0.0)
                lines = [pltpu.roll(coeff[q], shift, 1) for q in range(2)]
            else:
                first = pl.multiple_of(panel * 16, 16)
                lines = [weight_ref[pl.ds(first + 8 * q, 8), :] for q in range(2)]
            places = [pl.ds(row, 8), pl.ds(row + 2 * reach, 8)]
            held = [grid[place, :] for place in places]
            for q in range(2):
                grid[places[q], :] = held[q] + lines[q] * value
        return carry

    lax.fori_loop(0, vector_ref.shape[0] // GROUP, body, 0)


def send_pieces(outs, flips, head, rounded, both, high_ref, low_ref):
    blocks = rounded.shape[0]
    mantissa, exponent = encode_rounded(rounded)
    head[...] = jnp.zeros_like(head)
    head[2 : 2 + blocks, :] = mantissa
    head[2 + blocks : 2 + 2 * blocks, :] = exponent
    mine = y_position()
    for at in range(0, len(flips), 2):
        pick = lambda ref: jnp.concatenate([ref[mine ^ flip] for flip in flips[at : at + 2]], axis=1)
        result = dot_three(both, (pick(high_ref), pick(low_ref)))
        for i, out in enumerate(outs[at : at + 2]):
            send_piece(out, head, result[:, i * 2 * HALF : (i + 1) * 2 * HALF])


def spread_grid(reach_x, reach_y, rounded, tables, outs, flips, wides, head, total, grids):
    for x in range(reach_x):
        parts = [
            grid[pl.ds(row, reach_y, stride=2), :]
            for row in pair_rows(x, reach_x, reach_y)
            for grid in grids
        ]
        total[x * reach_y : (x + 1) * reach_y, :] = sum(parts[1:], parts[0])
    half = reach_x * reach_y // 2
    both = jnp.concatenate([total[:half, :], total[half:, :]], axis=1)
    extra = wides[0].shape[0] - half
    if extra:
        both = jnp.concatenate([both, jnp.zeros((extra, 2 * REGION), F32)], axis=0)
    both = split(both)
    for wide, values in zip(wides, both):
        wide[...] = values
    send_pieces(outs, flips, head, rounded, both, *tables)


def start_kernel(reach_x, reach_y, flips, *refs):
    vector_ref, *remote = refs[:8]
    refs = refs[8:]
    outs, refs = refs[: len(flips)], refs[len(flips) :]
    wides, (weight_ref, sample_coeff_ref, places_out), refs = refs[:2], refs[2:5], refs[5:]
    rounded, high, low, stencil, flag, samples, dipoles = refs[:7]
    place_ref, sems, head, total = refs[7:11]
    grids = refs[11:]
    tiles = samples.shape[0]
    copies = []
    fetch = lambda source, target: copies.append(
        pltpu.make_async_copy(source, target, sems.at[len(copies)])
    )
    rounded_in, high_in, low_in, stencil_in, flag_in, sample_in, dipole_in = remote
    fetch(stencil_in, stencil)
    fetch(flag_in, flag)
    for tile in range(tiles):
        lanes = pl.ds(tile * BLOCK, BLOCK)
        fetch(sample_in.at[:, lanes], samples.at[tile])
        fetch(dipole_in.at[:, lanes], dipoles.at[tile])
    needed_first = len(copies)
    fetch(rounded_in, rounded)
    fetch(high_in, high)
    fetch(low_in, low)
    for copy in copies:
        copy.start()
    for grid in grids:
        grid[...] = jnp.zeros_like(grid)
    copies[0].wait()
    span_x, span_y = reach_x - 4, reach_y - 4
    local_x = stencil[0:1, :] - (lax.axis_index("wide") * span_x - 2)
    local_y = stencil[1:2, :] - (y_position() * span_y - 2)
    odd = local_x & 1
    places_out[0:1, :] = odd * (reach_x * reach_y) + (local_x >> 1) * (2 * reach_y) + 2 * local_y
    places_out[1:2, :] = stencil[2:3, :]
    to_scalar = pltpu.make_async_copy(places_out, place_ref, sems.at[len(copies)])
    to_scalar.start()
    for copy in copies[1:needed_first]:
        copy.wait()
    each = lambda values: [values.at[tile] for tile in range(tiles)]
    weave(flag[...], each(samples), each(dipoles), weight_ref, sample_coeff_ref)
    to_scalar.wait()
    add_panels(reach_y, True, vector_ref, place_ref, weight_ref, grids)
    for copy in copies[needed_first:]:
        copy.wait()
    spread_grid(
        reach_x, reach_y, rounded[...], (high, low), outs, flips, wides, head, total, grids
    )


def spread_kernel(reach_x, reach_y, flips, *refs):
    vector_ref, place_ref, rounded_ref, high_ref, low_ref, line_ref = refs[:6]
    refs = refs[6:]
    outs, wides, (head, total), grids = (
        refs[: len(flips)],
        refs[len(flips) : len(flips) + 2],
        refs[len(flips) + 2 : len(flips) + 4],
        refs[len(flips) + 4 :],
    )
    for grid in grids:
        grid[...] = jnp.zeros_like(grid)
    add_panels(reach_y, False, vector_ref, place_ref, line_ref, grids)
    spread_grid(
        reach_x,
        reach_y,
        rounded_ref[...],
        (high_ref, low_ref),
        outs,
        flips,
        wides,
        head,
        total,
        grids,
    )


def spread(vector, table, placed, raw, reach_x, reach_y, flips):
    count = vector.shape[0]
    half = reach_x * reach_y // 2
    blocks = count // BLOCK
    top = up_to(2 + 2 * blocks, 16)
    lanes = 2 * HALF
    body = up_to(half, 16)
    woven = (count // GROUP * 16, BLOCK)
    out_shapes = [jax.ShapeDtypeStruct((top + body, lanes), jnp.int16)] * len(flips)
    out_shapes += [jax.ShapeDtypeStruct((body, 2 * REGION), BF16)] * 2
    rounded = vector.reshape(blocks, BLOCK)
    work = [
        pltpu.VMEM((top, lanes), F32),
        pltpu.VMEM((reach_x * reach_y, REGION), F32),
    ] + [pltpu.VMEM((pair_count(reach_x, reach_y), REGION), F32)] * CHAINS
    if placed is None:
        stencil, flag, sample, dipole = raw
        operands = [vector, rounded, *table, stencil, flag.reshape(1, -1), sample, dipole]
        in_specs = [in_smem()] + [pl.BlockSpec(memory_space=pltpu.HBM)] * 7
        out_shapes += [jax.ShapeDtypeStruct(woven, F32)] * 2
        out_shapes += [jax.ShapeDtypeStruct((2, count), jnp.int32)]
        tiled = pltpu.VMEM((blocks, 64, BLOCK), F32)
        work = [
            pltpu.VMEM(rounded.shape, F32),
            pltpu.VMEM(table[0].shape, BF16),
            pltpu.VMEM(table[1].shape, BF16),
            pltpu.VMEM(stencil.shape, jnp.int32),
            pltpu.VMEM((1, count), jnp.int32),
            tiled,
            tiled,
            pltpu.SMEM((2, count), jnp.int32),
            pltpu.SemaphoreType.DMA((6 + 2 * blocks,)),
        ] + work
    else:
        operands = [vector, placed[0], rounded, *table, placed[1]]
        in_specs = [in_smem()] * 2 + [whole_vmem()] * 4
    return pl.pallas_call(
        functools.partial(
            start_kernel if placed is None else spread_kernel, reach_x, reach_y, flips
        ),
        in_specs=in_specs,
        out_specs=[whole_vmem()] * len(out_shapes),
        out_shape=out_shapes,
        scratch_shapes=work,
        compiler_params=pltpu.CompilerParams(
            vmem_limit_bytes=START_LIMIT if placed is None else VMEM_LIMIT
        ),
        cost_estimate=cost(2 * half * 256 * 512, 4 * 16 * count * REGION),
        name="start" if placed is None else "spread",
    )(*operands)


def spread_rest_kernel(flips, rounded_ref, wide_high, wide_low, high_ref, low_ref, *refs):
    outs, head = refs[:-1], refs[-1]
    both = (wide_high[...], wide_low[...])
    send_pieces(outs, flips, head, rounded_ref[...], both, high_ref, low_ref)


def spread_rest(vector, both, table, flips):
    blocks = vector.shape[0] // BLOCK
    top = up_to(2 + 2 * blocks, 16)
    shape = (top + both[0].shape[0], 2 * HALF)
    return pl.pallas_call(
        functools.partial(spread_rest_kernel, flips),
        in_specs=[whole_vmem()] * 5,
        out_specs=[whole_vmem()] * len(flips),
        out_shape=[jax.ShapeDtypeStruct(shape, jnp.int16)] * len(flips),
        scratch_shapes=[pltpu.VMEM((top, 2 * HALF), F32)],
        compiler_params=params(),
        cost_estimate=cost(2 * shape[0] * 256 * 256 * 3, 4 * shape[0] * 512),
        name="spread_rest",
    )(vector.reshape(blocks, BLOCK), *both, *table)


def lines_kernel(place_ref, coeff_ref, *refs):
    out_ref = refs[-1]
    lanes = lax.broadcasted_iota(jnp.int32, (8, REGION), 1)

    def body(group, carry):
        at = pl.multiple_of(group * 16, 16)
        coeff = [coeff_ref[pl.ds(at + 8 * q, 8), :] for q in range(2)]
        for local in range(GROUP):
            panel = group * GROUP + local
            depth = place_ref[1, panel]
            shift = (depth - 4 * local) & (REGION - 1)
            inside = in_window(lanes, depth)
            for q in range(2):
                first = pl.multiple_of(panel * 16 + 8 * q, 8)
                out_ref[pl.ds(first, 8), :] = jnp.where(inside, pltpu.roll(coeff[q], shift, 1), 0.0)
        return carry

    lax.fori_loop(0, place_ref.shape[1] // GROUP, body, 0)


def place_lines(places, coeff, awaited):
    count = places.shape[1]
    shape = (count * 16, REGION)
    return pl.pallas_call(
        lines_kernel,
        in_specs=[in_smem(), whole_vmem()] + [anywhere()] * len(awaited),
        out_specs=whole_vmem(),
        out_shape=jax.ShapeDtypeStruct(shape, F32),
        compiler_params=params(),
        cost_estimate=cost(16 * count * REGION, 4 * 16 * count * REGION),
        name="place_lines",
    )(places, coeff, *awaited)


def stack_pieces(parts, reach_x, reach_y, top, opened, stacked):
    half = reach_x // 2
    pitch = up_to(reach_y, 8)
    tall = len(parts) * pitch
    core = lax.axis_index("pair")
    for bit, part in enumerate(parts):
        first = from_short(part[:top, :])
        opened[...] = from_short(part[top:, :]) * unit(first[0:1], first[1:2])
        place = (core ^ bit) * pitch
        for i in range(half):
            stacked[pl.ds(pl.multiple_of(i * tall + place, 8), reach_y), :] = opened[
                i * reach_y : (i + 1) * reach_y, :
            ]


def transform_pieces(table, stacked, before, spectrum):
    half = spectrum.shape[0]
    tall = stacked.shape[0] // half

    def tripled(values):
        high, low = split(values)
        return jnp.concatenate([high, low, high], axis=0)

    for i in range(0, half, 2):
        places = range(i, min(i + 2, half))
        held = jnp.concatenate([stacked[j * tall : (j + 1) * tall, :] for j in places], axis=1)
        result = dot(table, tripled(held))
        for j in places:
            made = result[:, (j - i) * 2 * HALF : (j - i + 1) * 2 * HALF]
            spectrum[j] = made if before is None else before[j] + made


def forward_early_kernel(reach_x, reach_y, pair, *refs):
    parts = refs[:pair]
    table_ref, spectrum, opened, stacked = refs[pair:]
    top = parts[0].shape[0] - opened.shape[0]
    stacked[...] = jnp.zeros_like(stacked)
    stack_pieces(parts, reach_x, reach_y, top, opened, stacked)
    transform_pieces(table_ref[lax.axis_index("narrow")], stacked, None, spectrum)


def stacking_scratch(pair, reach_x, reach_y):
    half = reach_x // 2
    return [
        pltpu.VMEM((up_to(half * reach_y, 16), 2 * HALF), F32),
        pltpu.VMEM((half * pair * up_to(reach_y, 8), 2 * HALF), F32),
    ]


def forward_early(parts, table, reach_x, reach_y):
    half = reach_x // 2
    pair = len(parts)
    return pl.pallas_call(
        functools.partial(forward_early_kernel, reach_x, reach_y, pair),
        in_specs=[whole_vmem()] * (pair + 1),
        out_specs=whole_vmem(),
        out_shape=jax.ShapeDtypeStruct((half, GRID, 2 * HALF), F32),
        scratch_shapes=stacking_scratch(pair, reach_x, reach_y),
        compiler_params=params(),
        cost_estimate=cost(2 * half * 256 * 256 * 128, 4 * half * GRID * 2 * HALF * 2),
        name="forward_early",
    )(*parts, table)


def forward_kernel(reach_x, reach_y, blocks, pieces, awaited, *refs):
    parts = refs[:pieces]
    early_ref, table_ref, modes_ref = refs[pieces : pieces + 3]
    refs = refs[: pieces + 3] + refs[pieces + 3 + awaited :]
    spectrum, even_out, odd_out, own_out, peers_out, inner_out = refs[pieces + 3 : pieces + 9]
    opened, stacked, slabs, head = refs[pieces + 9 :]
    half = reach_x // 2
    pair = lax.axis_size("pair")
    top = parts[0].shape[0] - opened.shape[0]
    stacked[...] = jnp.zeros_like(stacked)
    head[...] = jnp.zeros_like(head)
    for piece in range(pieces):
        first = from_short(parts[piece][:top, :])
        mantissa, exponent = first[2 : 2 + blocks], first[2 + blocks : 2 + 2 * blocks]
        peers_out[piece * blocks : (piece + 1) * blocks, :] = decode_rounded(mantissa, exponent)
        at = 6 + 2 * piece * blocks
        head[at : at + blocks, :] = mantissa
        head[at + blocks : at + 2 * blocks, :] = exponent
    before = early_ref
    for chip in range(1, pieces // pair):
        stack_pieces(parts[chip * pair : (chip + 1) * pair], reach_x, reach_y, top, opened, stacked)
        transform_pieces(table_ref[lax.axis_index("narrow") ^ chip], stacked, before, spectrum)
        before = spectrum

    chunk = 32

    def body(index, largest):
        rows = pl.ds(pl.multiple_of(index * chunk, chunk), chunk)
        low = low_lanes(chunk)
        decay = modes_ref[0, rows, :]
        log_decay = modes_ref[1, rows, :]
        across_half = jnp.exp(half * log_decay)
        across_cut = jnp.exp((half - 4) * log_decay)
        layers = [spectrum[i, rows, :] for i in range(half)]
        run = layers[0]
        cut_right = run
        for i in range(1, half):
            run = decay * run + layers[i]
            if i == half - 5:
                cut_right = run
        right = run
        run = layers[half - 1]
        cut_left = run
        for i in range(half - 2, -1, -1):
            run = decay * run + layers[i]
            if i == 4:
                cut_left = run
        left = run
        inner_out[rows, :] = jnp.where(low, right, left)
        swapped_right, swapped_left = swap(right), swap(left)
        own = jnp.where(low, left + across_half * swapped_left, right + across_half * swapped_right)
        made = [
            jnp.where(low, swap(layers[half - 4]), layers[half - 3]),
            jnp.where(low, swap(layers[half - 2]), layers[half - 1]),
            jnp.where(low, own, cut_right + across_cut * swapped_right),
            jnp.where(low, layers[0], swap(layers[1])),
            jnp.where(low, layers[2], swap(layers[3])),
            jnp.where(low, cut_left + across_cut * swapped_left, own),
        ]
        own_out[rows, :] = own
        for slab, values in enumerate(made):
            slabs[slab, rows, :] = values
        return tuple(
            jnp.maximum(old, jnp.max(jnp.abs(values).reshape(chunk // 8, 8, 2 * HALF), axis=0))
            for old, values in zip(largest, made)
        )

    zero = jnp.zeros((8, 2 * HALF), F32)
    largest = lax.fori_loop(0, GRID // chunk, body, (zero,) * 6)
    scales = [fit_scale(jnp.max(value, axis=0, keepdims=True)) for value in largest]
    head_rows = head.shape[0]

    def send(out, first):
        for slab in range(3):
            exponent, fraction = scales[first + slab]
            head[2 * slab : 2 * slab + 1, :] = exponent
            head[2 * slab + 1 : 2 * slab + 2, :] = fraction
            at = head_rows + slab * GRID
            out[at : at + GRID, :] = quantize(slabs[first + slab], exponent, fraction)
        out[:head_rows, :] = to_short(head[...])

    on_left = lax.axis_index("wide") & 1

    @pl.when(on_left == 0)
    def _():
        send(even_out, 0)
        send(odd_out, 3)

    @pl.when(on_left == 1)
    def _():
        send(even_out, 3)
        send(odd_out, 0)


def forward(parts, early, table, modes, reach_x, reach_y, blocks, awaited):
    pieces = len(parts)
    half = reach_x // 2
    lanes = 2 * HALF
    head = up_to(6 + 2 * pieces * blocks, 16)
    short = lambda rows: jax.ShapeDtypeStruct((rows, lanes), jnp.int16)
    return pl.pallas_call(
        functools.partial(
            forward_kernel, reach_x, reach_y, blocks, pieces, len(awaited)
        ),
        in_specs=[whole_vmem()] * (pieces + 3) + [anywhere()] * len(awaited),
        out_specs=[whole_vmem()] * 6,
        out_shape=[
            jax.ShapeDtypeStruct((half, GRID, lanes), F32),
            short(head + 3 * GRID),
            short(head + 3 * GRID),
            jax.ShapeDtypeStruct((GRID, lanes), F32),
            jax.ShapeDtypeStruct((pieces * blocks, BLOCK), F32),
            jax.ShapeDtypeStruct((GRID, lanes), F32),
        ],
        scratch_shapes=stacking_scratch(pieces // table.shape[0], reach_x, reach_y)
        + [
            pltpu.VMEM((6, GRID, lanes), F32),
            pltpu.VMEM((head, lanes), F32),
        ],
        compiler_params=params(),
        cost_estimate=cost(2 * half * 256 * 256 * 128, 4 * half * GRID * lanes * 2),
        name="forward",
    )(*parts, early, table, modes, *awaited)


def opened_slabs(ref, count, head_rows):
    first = from_short(ref[:16, :])
    for slab in range(count):
        scale = unit(first[2 * slab : 2 * slab + 1], first[2 * slab + 1 : 2 * slab + 2])
        at = head_rows + slab * GRID
        yield from_short(ref[at : at + GRID, :]) * scale


def pair_kernel(reach_x, flips, own_ref, even_ref, modes_ref, *refs):
    outs, head = refs[:-1], refs[-1]
    span = reach_x - 4
    here = lax.axis_index("wide")
    low = low_lanes(GRID)
    decay, log_decay = modes_ref[0], modes_ref[1]
    own = own_ref[...]
    one, two, cut = opened_slabs(even_ref, 3, even_ref.shape[0] - 3 * GRID)
    left = ((decay * cut + swap(one)) * decay + one) * decay + swap(two)
    left = jnp.where(low, cut, left * decay + two)
    right = ((decay * cut + swap(two)) * decay + two) * decay + swap(one)
    right = jnp.where(low, right * decay + one, cut)
    partner = jnp.where((here & 1) == 1, left, right)

    def weight(distances):
        powers = []
        for distance in distances:
            ahead = span * distance - reach_x
            powers.append(jnp.where(distance >= 2, ahead, ahead + GRID).astype(F32))
        return jnp.exp(jnp.where(low, *powers) * log_decay)

    head[...] = jnp.zeros_like(head)
    for flip, out in zip(flips, outs):
        behind = (here ^ flip) - here
        message = own * weight((-behind, behind))
        behind = (here ^ flip) - (here ^ 1)
        beside = jnp.where(jnp.abs(behind) == 1, 0.0, 1.0)
        send_piece(out, head, message + partner * (weight((-behind, behind)) * beside))


def pair_messages(own, from_even, modes, reach_x, flips):
    return pl.pallas_call(
        functools.partial(pair_kernel, reach_x, flips),
        in_specs=[whole_vmem()] * 3,
        out_specs=[whole_vmem()] * len(flips),
        out_shape=[jax.ShapeDtypeStruct((16 + GRID, 2 * HALF), jnp.int16)] * len(flips),
        scratch_shapes=[pltpu.VMEM((16, 2 * HALF), F32)],
        compiler_params=params(),
        cost_estimate=cost(16 * GRID * 2 * HALF, 4 * GRID * 2 * HALF * (6 + len(flips))),
        name="pair_messages",
    )(own, from_even, modes)


def send_fields(outs, flips, reach_y, field_high, field_low, high_ref, low_ref, ready, head):
    half = field_high.shape[0]
    mine = y_position()
    pitch = up_to(reach_y, 16)
    pick = lambda ref: jnp.concatenate([ref[mine ^ flip] for flip in flips], axis=0)
    table = (pick(high_ref), pick(low_ref))
    for i in range(0, half, 2):
        many = min(2, half - i)
        join = lambda ref: jnp.concatenate([ref[i + j] for j in range(many)], axis=1)
        result = dot_three(table, (join(field_high), join(field_low)))
        for j in range(many):
            for piece in range(len(flips)):
                ready[piece, (i + j) * reach_y : (i + j + 1) * reach_y, :] = result[
                    piece * pitch : piece * pitch + reach_y, j * 2 * HALF : (j + 1) * 2 * HALF
                ]
    head[...] = jnp.zeros_like(head)
    for piece, out in enumerate(outs):
        if ready.shape[1] > half * reach_y:
            ready[piece, half * reach_y :, :] = jnp.zeros_like(ready[piece, half * reach_y :, :])
        send_piece(out, head, ready[piece])


def inverse_kernel(reach_x, reach_y, flips, fars, *refs):
    spectrum, from_even, from_odd, own_ref, inner_ref, *far_refs = refs[: 5 + fars]
    refs = refs[5 + fars :]
    high_ref, low_ref, modes_ref = refs[:3]
    outs = refs[3 : 3 + len(flips)]
    field_high, field_low, ready, head = refs[3 + len(flips) :]
    half = reach_x // 2
    span = reach_x - 4
    chunk = 32
    head_rows = from_even.shape[0] - 3 * GRID
    on_left = (lax.axis_index("wide") & 1) == 1
    both_heads = from_short(from_even[:16, :]), from_short(from_odd[:16, :])
    both_units = [
        [unit(first[2 * slab : 2 * slab + 1], first[2 * slab + 1 : 2 * slab + 2]) for slab in range(3)]
        for first in both_heads
    ]

    def sided(even, odd):
        return jnp.where(on_left, even, odd), jnp.where(on_left, odd, even)

    far_units = []
    for ref in far_refs:
        first = from_short(ref[:16, :])
        far_units.append(unit(first[0:1], first[1:2]))

    def body(index, carry):
        first = pl.multiple_of(index * chunk, chunk)
        rows = pl.ds(first, chunk)
        low = low_lanes(chunk)
        decay = modes_ref[0, rows, :]
        log_decay = modes_ref[1, rows, :]
        ring = modes_ref[2, rows, :]
        gain = modes_ref[3, rows, :]
        across_half = jnp.exp(half * log_decay)
        across_cut = jnp.exp((half - 4) * log_decay)
        around = jnp.exp((GRID - 4) * log_decay)
        beside = jnp.exp((GRID - reach_x - span) * log_decay)
        layers = [spectrum[i, rows, :] for i in range(half)]

        def slab(which):
            at = pl.ds(pl.multiple_of(head_rows + which * GRID + index * chunk, chunk), chunk)
            even = from_short(from_even[at, :]) * both_units[0][which]
            return sided(even, from_short(from_odd[at, :]) * both_units[1][which])

        head_layers, tail_layers = zip(slab(0), slab(1))
        left_moments, right_moments = slab(2)
        zero = jnp.zeros_like(decay)
        from_head = [head_layers[0], swap(head_layers[0]), head_layers[1], swap(head_layers[1])]
        from_tail = [swap(tail_layers[0]), tail_layers[0], swap(tail_layers[1]), tail_layers[1]]
        head_sum = from_head[0]
        for i in range(1, 4):
            head_sum = decay * head_sum + from_head[i]
        tail_sum = from_tail[3]
        for i in range(2, -1, -1):
            tail_sum = decay * tail_sum + from_tail[i]
        for i in range(4):
            layers[i] = layers[i] + jnp.where(low, from_head[i], zero)
        for i in range(4):
            place = half - 4 + i
            layers[place] = layers[place] + jnp.where(low, zero, from_tail[i])
        total = own_ref[rows, :] * jnp.exp((GRID - reach_x) * log_decay)
        at = pl.ds(pl.multiple_of(16 + index * chunk, 16), chunk)
        for ref, scale in zip(far_refs, far_units):
            total = total + from_short(ref[at, :]) * scale
        one = jnp.ones_like(decay)
        total = total + left_moments * jnp.where(low, beside, one)
        total = total + right_moments * jnp.where(low, one, beside)
        shared = jnp.where(low, head_sum, tail_sum)
        entering = (swap(total) + around * shared) * ring
        leaving = swap(across_half * entering + across_cut * shared + inner_ref[rows, :])
        run = jnp.where(low, entering, leaving)
        forward_runs = []
        for i in range(half):
            run = decay * run + layers[i]
            forward_runs.append(run)
        run = jnp.where(low, leaving, entering)
        for i in range(half - 1, -1, -1):
            ahead = decay * run
            high, rest = split(gain * (forward_runs[i] + ahead))
            field_high[i, rows, :] = high
            field_low[i, rows, :] = rest
            run = ahead + layers[i]
        return carry

    lax.fori_loop(0, GRID // chunk, body, 0)
    send_fields(outs, flips, reach_y, field_high, field_low, high_ref, low_ref, ready, head)


def inverse(
    spectrum, from_even, from_odd, own, inner, fars, table, modes, reach_x, reach_y, flips
):
    half = reach_x // 2
    lanes = 2 * HALF
    body = up_to(half * reach_y, 16)
    shapes = [jax.ShapeDtypeStruct((16 + body, lanes), jnp.int16)] * len(flips)
    shapes += [jax.ShapeDtypeStruct((half, GRID, lanes), BF16)] * 2
    return pl.pallas_call(
        functools.partial(inverse_kernel, reach_x, reach_y, flips, len(fars)),
        in_specs=[whole_vmem()] * (8 + len(fars)),
        out_specs=[whole_vmem()] * len(shapes),
        out_shape=shapes,
        scratch_shapes=[
            pltpu.VMEM((len(flips), body, lanes), F32),
            pltpu.VMEM((16, lanes), F32),
        ],
        compiler_params=params(),
        cost_estimate=cost(2 * half * 256 * 256 * 128, 4 * half * GRID * lanes * 2),
        name="inverse",
    )(spectrum, from_even, from_odd, own, inner, *fars, *table, modes)


def inverse_rest_kernel(reach_y, flips, field_high, field_low, high_ref, low_ref, *refs):
    outs, (ready, head) = refs[: len(flips)], refs[len(flips) :]
    send_fields(outs, flips, reach_y, field_high, field_low, high_ref, low_ref, ready, head)


def inverse_rest(field, table, reach_y, flips):
    half = field[0].shape[0]
    lanes = 2 * HALF
    body = up_to(half * reach_y, 16)
    return pl.pallas_call(
        functools.partial(inverse_rest_kernel, reach_y, flips),
        in_specs=[whole_vmem()] * 4,
        out_specs=[whole_vmem()] * len(flips),
        out_shape=[jax.ShapeDtypeStruct((16 + body, lanes), jnp.int16)] * len(flips),
        scratch_shapes=[
            pltpu.VMEM((len(flips), body, lanes), F32),
            pltpu.VMEM((16, lanes), F32),
        ],
        compiler_params=params(),
        cost_estimate=cost(2 * half * 256 * 256 * 128, 4 * half * GRID * lanes * 2),
        name="inverse_rest",
    )(*field, *table)


def sum_rows(values):
    row = lax.broadcasted_iota(jnp.int32, values[0].shape, 0)
    for step in (4, 2, 1):
        low = (row & step) == 0
        paired = []
        for one, other in zip(values[: len(values) // 2], values[len(values) // 2 :]):
            kept = jnp.where(low, one, other)
            moved = jnp.where(low, other, one)
            if step == 4:
                moved = pltpu.roll(moved, 4, 0)
            else:
                moved = jnp.where(low, pltpu.roll(moved, 8 - step, 0), pltpu.roll(moved, step, 0))
            paired.append(kept + moved)
        values = paired
    return values[0]


def z_lines(parts, flips, high_ref, low_ref):
    mine = y_position()
    opened = []
    for part in parts:
        first = from_short(part[:16, :])
        opened.append(from_short(part[16:, :]) * unit(first[0:1], first[1:2]))
    values = split(jnp.concatenate(opened, axis=1))
    pick = lambda ref: jnp.concatenate([ref[mine ^ flip] for flip in flips], axis=0)
    return dot_three(values, (pick(high_ref), pick(low_ref)))


def sample_early_kernel(*refs):
    *parts, high_ref, low_ref, out_ref = refs
    out_ref[...] = z_lines(parts, range(len(parts)), high_ref, low_ref)


def sample_early(parts, table):
    rows = parts[0].shape[0] - 16
    return pl.pallas_call(
        sample_early_kernel,
        in_specs=[whole_vmem()] * (len(parts) + 2),
        out_specs=whole_vmem(),
        out_shape=jax.ShapeDtypeStruct((rows, 2 * REGION), F32),
        compiler_params=params(),
        cost_estimate=cost(2 * rows * 256 * 256 * 3, 4 * rows * 512),
        name="sample_early",
    )(*parts, *table)


def sample_kernel(last, reach_x, reach_y, flips, place_ref, *refs):
    parts = refs[: len(flips)]
    early_ref, high_ref, low_ref, line_ref, own_ref, vector_ref, near_ref, out_ref = refs[
        len(flips) : len(flips) + 8
    ]
    flat, field, sums = refs[len(flips) + 8 :]
    half_rows = reach_x * reach_y // 2
    both = early_ref[...] + z_lines(parts, flips, high_ref, low_ref)
    flat[:half_rows, :] = both[:half_rows, :REGION]
    flat[half_rows:, :] = both[:half_rows, REGION:]
    for x in range(reach_x):
        layer = flat[x * reach_y : (x + 1) * reach_y, :]
        for row in pair_rows(x, reach_x, reach_y):
            field[pl.ds(row, reach_y, stride=2), :] = layer
    count = place_ref.shape[1]

    def body(group, carry):
        for eight in range(0, GROUP, 8):
            totals = []
            for local in range(eight, eight + 8):
                panel = group * GROUP + local
                row = place_ref[0, panel]
                first = pl.multiple_of(panel * 16, 16)
                totals.append(
                    field[pl.ds(row, 8), :] * line_ref[pl.ds(first, 8), :]
                    + field[pl.ds(row + 2 * reach_y, 8), :] * line_ref[pl.ds(first + 8, 8), :]
                )
            sums[pl.ds(pl.multiple_of(group * GROUP + eight, 8), 8), :] = sum_rows(totals)
        return carry

    lax.fori_loop(0, count // GROUP, body, 0)
    sampled = lax.dot_general(
        jnp.ones((8, REGION), F32),
        sums[...],
        (((1,), (1,)), ((), ())),
        precision=lax.Precision.HIGHEST,
        preferred_element_type=F32,
    )
    for block in range(count // BLOCK):
        lane = slice(block * BLOCK, (block + 1) * BLOCK)
        row = slice(block, block + 1)
        vector = vector_ref[row, :]
        image = jnp.where(own_ref[row, :] == 1, 0.0, 0.5 * vector) + sampled[:1, lane]
        image = image + near_ref[row, :]
        if last:
            out_ref[0:1, lane] = vector
            out_ref[1:2, lane] = image
        else:
            out_ref[row, :] = image


def sample(last, places, parts, flips, early, table, lines, flag, vector, near, reach_x, reach_y):
    count = places.shape[1]
    blocks = count // BLOCK
    shape = (2, count) if last else (blocks, BLOCK)
    return pl.pallas_call(
        functools.partial(sample_kernel, last, reach_x, reach_y, flips),
        in_specs=[in_smem()] + [whole_vmem()] * (len(parts) + 7),
        out_specs=whole_vmem(),
        out_shape=jax.ShapeDtypeStruct(shape, F32),
        scratch_shapes=[
            pltpu.VMEM((reach_x * reach_y, REGION), F32),
            pltpu.VMEM((pair_count(reach_x, reach_y), REGION), F32),
            pltpu.VMEM((count, REGION), F32),
        ],
        compiler_params=params(),
        cost_estimate=cost(reach_x * reach_y * 256 * 512, 4 * 16 * count * REGION),
        name="sample",
    )(
        places,
        *parts,
        early,
        *table,
        lines,
        flag.reshape(blocks, BLOCK),
        vector.reshape(blocks, BLOCK),
        near,
    )


def near_kernel(slots, blocks, place_ref, target_ref, *refs):
    even_ref, odd_ref, peers_ref, tile_ref, out_ref, held = refs
    count = peers_ref.shape[0]
    held[count : 2 * count, :] = peers_ref[...]
    on_left = lax.axis_index("wide") & 1
    for side, ref in ((1 - on_left, even_ref), (on_left, odd_ref)):
        top = from_short(ref[...])
        for piece in range(count // blocks):
            at = 6 + 2 * piece * blocks
            held[pl.ds(side * (2 * count) + piece * blocks, blocks), :] = decode_rounded(
                top[at : at + blocks], top[at + blocks : at + 2 * blocks]
            )
    out_ref[...] = jnp.zeros_like(out_ref)
    for slot in range(slots):
        picked = held[pl.ds(place_ref[slot], 1), :]
        picked = jnp.broadcast_to(picked, (16, BLOCK)).astype(BF16)
        product = lax.dot_general(
            picked,
            tile_ref[slot],
            (((1,), (1,)), ((), ())),
            preferred_element_type=F32,
        )
        target = pl.ds(target_ref[slot], 1)
        out_ref[target, :] = out_ref[target, :] + product[:1]


def near_field(places, targets, from_even, from_odd, peers, tiles, blocks, out_rows):
    slots = tiles.shape[0]
    head = from_even.shape[0] - 3 * GRID
    constant = lambda shape: pl.BlockSpec(shape, lambda i: (0,) * len(shape))
    return pl.pallas_call(
        functools.partial(near_kernel, slots, blocks),
        grid=(1,),
        in_specs=[
            in_smem(),
            in_smem(),
            constant((head, BLOCK)),
            constant((head, BLOCK)),
            constant(peers.shape),
            constant(tiles.shape),
        ],
        out_specs=constant((out_rows, BLOCK)),
        out_shape=jax.ShapeDtypeStruct((out_rows, BLOCK), F32),
        scratch_shapes=[pltpu.VMEM((3 * peers.shape[0], BLOCK), F32)],
        compiler_params=params(),
        cost_estimate=cost(2 * slots * 16 * BLOCK * BLOCK, 2 * slots * BLOCK * BLOCK),
        name="near_field",
    )(places, targets, from_even, from_odd, peers, tiles)


def shards(
    density,
    surface_flag,
    stencil_base,
    sample_weights,
    dipole_weights,
    near_target,
    near_source,
    near_tiles,
):
    x_count = lax.axis_size("wide")
    y_count = lax.axis_size(Y_AXES)
    y_index = lax.axis_index(Y_AXES)
    pair = lax.axis_size("pair")
    span_x = REGION // x_count
    span_y = REGION // y_count
    reach_x = span_x + 4
    reach_y = span_y + 4
    count = density.shape[0]
    blocks = count // BLOCK

    z_forward, z_inverse, y_forward, y_inverse, modes = tables(y_count, pair, span_y)
    modes = lax.dynamic_index_in_dim(jnp.asarray(modes), y_index, 0, keepdims=False)

    neighbour = near_source // blocks
    flip = (y_index + neighbour % 3 - 1) ^ y_index
    sources = ((neighbour // 3) * y_count + flip) * blocks + near_source % blocks
    out_rows = up_to(blocks + 1, 8)
    live = near_target >= 0
    sources = jnp.where(live, sources, 0)
    targets = jnp.where(live, near_target, out_rows - 1)

    swaps = lambda pairs: [(i, j) for i, j in pairs] + [(j, i) for i, j in pairs]
    even_swap = swaps([(i, i + 1) for i in range(0, x_count - 1, 2)])
    odd_swap = swaps([(i, i + 1) for i in range(1, x_count - 1, 2)])
    far_flips = list(range(2, x_count, 2))

    local, moving = [0], list(range(1, y_count))

    def flipped(parts, flips):
        return [
            lax.ppermute(part, Y_AXES, [(i, i ^ flip) for i in range(y_count)])
            for flip, part in zip(flips, parts)
        ]

    def convolve_and_sample(last, vector, sent, both, places, sample_lines, awaited):
        arrived = flipped(sent, moving)
        arrived = list(spread_rest(vector, both, z_forward, local)) + arrived
        early = forward_early(arrived[:pair], y_forward, reach_x, reach_y)
        spectrum, even_message, odd_message, own, peers, inner = forward(
            arrived, early, y_forward, modes, reach_x, reach_y, blocks, awaited
        )
        from_even = lax.ppermute(even_message, "wide", even_swap)
        from_odd = lax.ppermute(odd_message, "wide", odd_swap)
        fars = [
            lax.ppermute(message, "wide", [(i, i ^ flip) for i in range(x_count)])
            for flip, message in zip(
                far_flips, pair_messages(own, from_even, modes, reach_x, far_flips)
            )
        ]
        near_part = near_field(
            sources, targets, from_even, from_odd, peers, near_tiles, blocks, out_rows
        )
        *sent, high, low = inverse(
            spectrum,
            from_even,
            from_odd,
            own,
            inner,
            fars,
            y_inverse,
            modes,
            reach_x,
            reach_y,
            moving,
        )
        arrived = flipped(sent, moving)
        arrived = list(inverse_rest((high, low), y_inverse, reach_y, local)) + arrived
        image = sample(
            last,
            places,
            arrived[pair:],
            list(range(pair, y_count)),
            sample_early(arrived[:pair], z_inverse),
            z_inverse,
            sample_lines,
            surface_flag,
            vector,
            near_part,
            reach_x,
            reach_y,
        )
        return image, near_part

    raw = (stencil_base, surface_flag, sample_weights, dipole_weights)
    *sent, high, low, source_coeff, sample_coeff, places = spread(
        density, z_forward, None, raw, reach_x, reach_y, moving
    )
    sample_lines = place_lines(places, sample_coeff, [])
    first_image, near_part = convolve_and_sample(
        False, density, sent, (high, low), places, sample_lines, [sample_lines]
    )
    first_image = first_image.reshape(-1)
    source_lines = place_lines(places, source_coeff, [near_part])
    *sent, high, low = spread(
        first_image, z_forward, (places, source_lines), None, reach_x, reach_y, moving
    )
    both_images, _ = convolve_and_sample(
        True, first_image, sent, (high, low), places, sample_lines, []
    )
    return both_images


def solution(mesh):
    panels = P(("groups",) + ALL_AXES)
    columns = P(None, ("groups",) + ALL_AXES)
    in_specs = (
        panels,
        panels,
        columns,
        columns,
        columns,
        panels,
        panels,
        P(("groups",) + ALL_AXES, None, None),
    )
    return jax.shard_map(
        shards, mesh=mesh, in_specs=in_specs, out_specs=columns, check_vma=False
    )
```

```python
import functools
import math

import jax
import jax.numpy as jnp
import numpy as np
from jax import lax
from jax.experimental import pallas as pl
from jax.experimental.pallas import tpu as pltpu
from jax.sharding import PartitionSpec as P

GRID = 256
REGION = 128
BLOCK = 128
HALF = 64
KERNEL_GAIN = 4.0
SCREEN = 1.0 / 1024.0
LN2 = math.log(2.0)
Y_AXES = ("narrow", "pair")
ALL_AXES = ("wide", "narrow", "pair")
F32 = jnp.float32
BF16 = jnp.bfloat16
VMEM_LIMIT = 24 * 1024 * 1024
START_LIMIT = VMEM_LIMIT
GROUP = 32
CHAINS = 4


def cas(angles):
    return np.cos(angles) + np.sin(angles)


def up_to(count, multiple):
    return -(-count // multiple) * multiple


def low_lanes(rows):
    return lax.broadcasted_iota(jnp.int32, (rows, 2 * HALF), 1) < HALF


def swap(values):
    return pltpu.roll(values, HALF, 1)


def split(values):
    high = values.astype(BF16)
    return high, (values - high.astype(F32)).astype(BF16)


def dot(left, right):
    return jnp.dot(left, right, preferred_element_type=F32)


def dot_three(left, right):
    return dot(left[0], right[0]) + (dot(left[0], right[1]) + dot(left[1], right[0]))


def params():
    return pltpu.CompilerParams(vmem_limit_bytes=VMEM_LIMIT)


def whole_vmem():
    return pl.BlockSpec(memory_space=pltpu.VMEM)


def anywhere():
    return pl.BlockSpec(memory_space=pl.ANY)


def in_smem():
    return pl.BlockSpec(memory_space=pltpu.SMEM)


def cost(flops, moved):
    return pl.CostEstimate(flops=flops, bytes_accessed=moved, transcendentals=0)


def full_scale(exponent, fraction):
    return fraction * jnp.exp(exponent * LN2) * (1.0 / 1024.0)


def fit_scale(largest):
    largest = jnp.maximum(largest, 1e-30)
    exponent = jnp.floor(jnp.log(largest) * (1.0 / LN2))
    fraction = jnp.ceil(largest * jnp.exp(-exponent * LN2) * 1024.0) + 1.0
    return exponent, fraction


def to_short(values):
    return values.astype(jnp.int32).astype(jnp.int16)


def from_short(values):
    return values.astype(jnp.int32).astype(F32)


def quantize(values, exponent, fraction):
    return to_short(jnp.round(values * (32767.0 / full_scale(exponent, fraction))))


def unit(exponent, fraction):
    return full_scale(exponent, fraction) * (1.0 / 32767.0)


def encode_rounded(values):
    rounded = values.astype(BF16).astype(F32)
    size = jnp.maximum(jnp.abs(rounded), 1e-30)
    exponent = jnp.floor(jnp.log(size) * (1.0 / LN2))
    return jnp.round(rounded * jnp.exp((10.0 - exponent) * LN2)), exponent


def decode_rounded(mantissa, exponent):
    return (mantissa * jnp.exp((exponent - 10.0) * LN2)).astype(BF16).astype(F32)


def send_piece(out, head, values):
    exponent, fraction = fit_scale(jnp.max(jnp.abs(values), axis=0, keepdims=True))
    head[0:1, :] = exponent
    head[1:2, :] = fraction
    top = head.shape[0]
    out[:top, :] = to_short(head[...])
    out[top:, :] = quantize(values, exponent, fraction)


def y_position():
    return lax.axis_index("narrow") * lax.axis_size("pair") + lax.axis_index("pair")


def halves(table):
    high = table.astype(jnp.bfloat16)
    return high, (table - high.astype(np.float64)).astype(jnp.bfloat16)


def tables(y_count, pair, span_y):
    depth = GRID // y_count
    reach = span_y + 4
    waves = np.arange(GRID)
    step = 2.0 * np.pi / GRID
    z_table = cas(step * np.outer(np.arange(REGION), waves))
    z_forward = np.zeros((y_count, 2 * REGION, 2 * HALF))
    z_inverse = np.zeros((y_count, 2 * HALF, 2 * REGION))
    symbols = 4.0 * np.sin(np.pi * waves / GRID) ** 2
    shift = np.full((y_count, GRID, 2 * HALF), 1.0)
    y_forward = np.zeros((GRID, y_count, up_to(reach, 8)))
    y_inverse = np.zeros((y_count, up_to(reach, 16), GRID))
    for block in range(y_count):
        mine = z_table[:, block * depth : (block + 1) * depth]
        for half in range(2):
            rows = slice(half * REGION, (half + 1) * REGION)
            lanes = slice(half * HALF, half * HALF + depth)
            z_forward[block, rows, lanes] = mine
            z_inverse[block, lanes, rows] = mine.T / GRID
            shift[block, :, lanes] = (
                SCREEN + symbols[:, None] + symbols[None, block * depth : (block + 1) * depth]
            )
        cells = block * span_y - 2 + np.arange(reach)
        y_table = cas(step * np.outer(waves, cells))
        y_forward[:, block, :reach] = y_table
        y_inverse[block, :reach] = y_table.T / GRID
    y_forward = y_forward.reshape(GRID, y_count // pair, -1).transpose(1, 0, 2)
    y_forward = halves(y_forward)
    y_forward = np.concatenate([y_forward[0], y_forward[0], y_forward[1]], axis=2)
    root = np.sqrt(shift * (shift + 4.0))
    decay = 2.0 / (2.0 + shift + root)
    log_decay = np.log(decay)
    ring = 1.0 / (1.0 - np.exp(GRID * log_decay))
    gain = KERNEL_GAIN / root
    modes = np.stack([decay, log_decay, ring, gain], axis=1).astype(np.float32)
    return (
        halves(z_forward),
        halves(z_inverse),
        y_forward,
        halves(y_inverse),
        modes,
    )


def weave(flag, sample_refs, dipole_refs, source_out, sample_out):
    place = lax.broadcasted_iota(jnp.int32, (4 * BLOCK, 4 * BLOCK), 0)
    lane = lax.broadcasted_iota(jnp.int32, (4 * BLOCK, 4 * BLOCK), 1)
    wanted = 4 * (place % BLOCK) + place // BLOCK
    mixing = jnp.where(lane == wanted, 1.0, 0.0).astype(BF16)
    stacked = []
    for tile, (sample_ref, dipole_ref) in enumerate(zip(sample_refs, dipole_refs)):
        charged = flag[:, tile * BLOCK : (tile + 1) * BLOCK] == 1
        rows = []
        for depth in range(4):
            sample = sample_ref[pl.ds(depth, 16, stride=4), :]
            dipole = dipole_ref[pl.ds(depth, 16, stride=4), :]
            rows.append(jnp.concatenate([jnp.where(charged, -sample, dipole), sample], axis=0))
        stacked.append(jnp.concatenate(rows, axis=1))
    weights = jnp.concatenate(stacked, axis=0)
    first, rest = split(weights)
    second, third = split(weights - first.astype(F32))
    woven = dot(first, mixing) + (dot(second, mixing) + dot(third, mixing))
    for tile in range(len(sample_refs)):
        for which, out in enumerate((source_out, sample_out)):
            for part in range(BLOCK // GROUP):
                at = (tile * (BLOCK // GROUP) + part) * 16
                lanes = slice(part * BLOCK, (part + 1) * BLOCK)
                for a in range(4):
                    row = tile * 32 + which * 16 + 4 * a
                    out[pl.ds(at + 8 * (a // 2) + a % 2, 4, stride=2), :] = woven[
                        row : row + 4, lanes
                    ]


def pair_rows(x, reach_x, reach_y):
    even = (x // 2) * 2 * reach_y + x % 2
    if x == 0 or x == reach_x - 1:
        return [even]
    return [even, reach_x * reach_y + ((x - 1) // 2) * 2 * reach_y + (x - 1) % 2]


def pair_count(reach_x, reach_y):
    return (2 * reach_x - 2) * reach_y


def in_window(lanes, depth):
    return ((lanes - depth) & -4) == 0


def add_panels(reach, woven, vector_ref, place_ref, weight_ref, grids):
    lanes = lax.broadcasted_iota(jnp.int32, (8, REGION), 1)

    def body(group, carry):
        at = pl.multiple_of(group * 16, 16)
        coeff = [weight_ref[pl.ds(at + 8 * q, 8), :] for q in range(2)] if woven else None
        for local in range(GROUP):
            panel = group * GROUP + local
            grid = grids[local % len(grids)]
            row = place_ref[0, panel]
            value = vector_ref[panel]
            if woven:
                depth = place_ref[1, panel]
                shift = (depth - 4 * local) & (REGION - 1)
                value = jnp.where(in_window(lanes, depth), value, 0.0)
                lines = [pltpu.roll(coeff[q], shift, 1) for q in range(2)]
            else:
                first = pl.multiple_of(panel * 16, 16)
                lines = [weight_ref[pl.ds(first + 8 * q, 8), :] for q in range(2)]
            places = [pl.ds(row, 8), pl.ds(row + 2 * reach, 8)]
            held = [grid[place, :] for place in places]
            for q in range(2):
                grid[places[q], :] = held[q] + lines[q] * value
        return carry

    lax.fori_loop(0, vector_ref.shape[0] // GROUP, body, 0)


def send_pieces(outs, flips, head, rounded, both, high_ref, low_ref):
    blocks = rounded.shape[0]
    mantissa, exponent = encode_rounded(rounded)
    head[...] = jnp.zeros_like(head)
    head[2 : 2 + blocks, :] = mantissa
    head[2 + blocks : 2 + 2 * blocks, :] = exponent
    mine = y_position()
    for at in range(0, len(flips), 2):
        pick = lambda ref: jnp.concatenate([ref[mine ^ flip] for flip in flips[at : at + 2]], axis=1)
        result = dot_three(both, (pick(high_ref), pick(low_ref)))
        for i, out in enumerate(outs[at : at + 2]):
            send_piece(out, head, result[:, i * 2 * HALF : (i + 1) * 2 * HALF])


def spread_grid(reach_x, reach_y, rounded, tables, outs, flips, wides, head, total, grids):
    for x in range(reach_x):
        parts = [
            grid[pl.ds(row, reach_y, stride=2), :]
            for row in pair_rows(x, reach_x, reach_y)
            for grid in grids
        ]
        total[x * reach_y : (x + 1) * reach_y, :] = sum(parts[1:], parts[0])
    half = reach_x * reach_y // 2
    both = jnp.concatenate([total[:half, :], total[half:, :]], axis=1)
    extra = wides[0].shape[0] - half
    if extra:
        both = jnp.concatenate([both, jnp.zeros((extra, 2 * REGION), F32)], axis=0)
    both = split(both)
    for wide, values in zip(wides, both):
        wide[...] = values
    send_pieces(outs, flips, head, rounded, both, *tables)


def start_kernel(reach_x, reach_y, flips, *refs):
    vector_ref, *remote = refs[:8]
    refs = refs[8:]
    outs, refs = refs[: len(flips)], refs[len(flips) :]
    wides, (weight_ref, sample_coeff_ref, places_out), refs = refs[:2], refs[2:5], refs[5:]
    rounded, high, low, stencil, flag, samples, dipoles = refs[:7]
    place_ref, sems, head, total = refs[7:11]
    grids = refs[11:]
    tiles = samples.shape[0]
    copies = []
    fetch = lambda source, target: copies.append(
        pltpu.make_async_copy(source, target, sems.at[len(copies)])
    )
    rounded_in, high_in, low_in, stencil_in, flag_in, sample_in, dipole_in = remote
    fetch(stencil_in, stencil)
    fetch(flag_in, flag)
    for tile in range(tiles):
        lanes = pl.ds(tile * BLOCK, BLOCK)
        fetch(sample_in.at[:, lanes], samples.at[tile])
        fetch(dipole_in.at[:, lanes], dipoles.at[tile])
    needed_first = len(copies)
    fetch(rounded_in, rounded)
    fetch(high_in, high)
    fetch(low_in, low)
    for copy in copies:
        copy.start()
    for grid in grids:
        grid[...] = jnp.zeros_like(grid)
    copies[0].wait()
    span_x, span_y = reach_x - 4, reach_y - 4
    local_x = stencil[0:1, :] - (lax.axis_index("wide") * span_x - 2)
    local_y = stencil[1:2, :] - (y_position() * span_y - 2)
    odd = local_x & 1
    places_out[0:1, :] = odd * (reach_x * reach_y) + (local_x >> 1) * (2 * reach_y) + 2 * local_y
    places_out[1:2, :] = stencil[2:3, :]
    to_scalar = pltpu.make_async_copy(places_out, place_ref, sems.at[len(copies)])
    to_scalar.start()
    for copy in copies[1:needed_first]:
        copy.wait()
    each = lambda values: [values.at[tile] for tile in range(tiles)]
    weave(flag[...], each(samples), each(dipoles), weight_ref, sample_coeff_ref)
    to_scalar.wait()
    add_panels(reach_y, True, vector_ref, place_ref, weight_ref, grids)
    for copy in copies[needed_first:]:
        copy.wait()
    spread_grid(
        reach_x, reach_y, rounded[...], (high, low), outs, flips, wides, head, total, grids
    )


def spread_kernel(reach_x, reach_y, flips, *refs):
    vector_ref, place_ref, rounded_ref, high_ref, low_ref, line_ref = refs[:6]
    refs = refs[6:]
    outs, wides, (head, total), grids = (
        refs[: len(flips)],
        refs[len(flips) : len(flips) + 2],
        refs[len(flips) + 2 : len(flips) + 4],
        refs[len(flips) + 4 :],
    )
    for grid in grids:
        grid[...] = jnp.zeros_like(grid)
    add_panels(reach_y, False, vector_ref, place_ref, line_ref, grids)
    spread_grid(
        reach_x,
        reach_y,
        rounded_ref[...],
        (high_ref, low_ref),
        outs,
        flips,
        wides,
        head,
        total,
        grids,
    )


def spread(vector, table, placed, raw, reach_x, reach_y, flips):
    count = vector.shape[0]
    half = reach_x * reach_y // 2
    blocks = count // BLOCK
    top = up_to(2 + 2 * blocks, 16)
    lanes = 2 * HALF
    body = up_to(half, 16)
    woven = (count // GROUP * 16, BLOCK)
    out_shapes = [jax.ShapeDtypeStruct((top + body, lanes), jnp.int16)] * len(flips)
    out_shapes += [jax.ShapeDtypeStruct((body, 2 * REGION), BF16)] * 2
    rounded = vector.reshape(blocks, BLOCK)
    work = [
        pltpu.VMEM((top, lanes), F32),
        pltpu.VMEM((reach_x * reach_y, REGION), F32),
    ] + [pltpu.VMEM((pair_count(reach_x, reach_y), REGION), F32)] * CHAINS
    if placed is None:
        stencil, flag, sample, dipole = raw
        operands = [vector, rounded, *table, stencil, flag.reshape(1, -1), sample, dipole]
        pinned = [pltpu.with_memory_space_constraint(value, pltpu.HBM) for value in operands[1:]]
        operands = [vector] + pinned
        in_specs = [in_smem()] + [pl.BlockSpec(memory_space=pltpu.HBM)] * 7
        out_shapes += [jax.ShapeDtypeStruct(woven, F32)] * 2
        out_shapes += [jax.ShapeDtypeStruct((2, count), jnp.int32)]
        tiled = pltpu.VMEM((blocks, 64, BLOCK), F32)
        work = [
            pltpu.VMEM(rounded.shape, F32),
            pltpu.VMEM(table[0].shape, BF16),
            pltpu.VMEM(table[1].shape, BF16),
            pltpu.VMEM(stencil.shape, jnp.int32),
            pltpu.VMEM((1, count), jnp.int32),
            tiled,
            tiled,
            pltpu.SMEM((2, count), jnp.int32),
            pltpu.SemaphoreType.DMA((6 + 2 * blocks,)),
        ] + work
    else:
        operands = [vector, placed[0], rounded, *table, placed[1]]
        in_specs = [in_smem()] * 2 + [whole_vmem()] * 4
    return pl.pallas_call(
        functools.partial(
            start_kernel if placed is None else spread_kernel, reach_x, reach_y, flips
        ),
        in_specs=in_specs,
        out_specs=[whole_vmem()] * len(out_shapes),
        out_shape=out_shapes,
        scratch_shapes=work,
        compiler_params=pltpu.CompilerParams(
            vmem_limit_bytes=START_LIMIT if placed is None else VMEM_LIMIT
        ),
        cost_estimate=cost(2 * half * 256 * 512, 4 * 16 * count * REGION),
        name="start" if placed is None else "spread",
    )(*operands)


def spread_rest_kernel(flips, rounded_ref, wide_high, wide_low, high_ref, low_ref, *refs):
    outs, head = refs[:-1], refs[-1]
    both = (wide_high[...], wide_low[...])
    send_pieces(outs, flips, head, rounded_ref[...], both, high_ref, low_ref)


def spread_rest(vector, both, table, flips):
    blocks = vector.shape[0] // BLOCK
    top = up_to(2 + 2 * blocks, 16)
    shape = (top + both[0].shape[0], 2 * HALF)
    return pl.pallas_call(
        functools.partial(spread_rest_kernel, flips),
        in_specs=[whole_vmem()] * 5,
        out_specs=[whole_vmem()] * len(flips),
        out_shape=[jax.ShapeDtypeStruct(shape, jnp.int16)] * len(flips),
        scratch_shapes=[pltpu.VMEM((top, 2 * HALF), F32)],
        compiler_params=params(),
        cost_estimate=cost(2 * shape[0] * 256 * 256 * 3, 4 * shape[0] * 512),
        name="spread_rest",
    )(vector.reshape(blocks, BLOCK), *both, *table)


def lines_kernel(place_ref, coeff_ref, *refs):
    out_ref = refs[-1]
    lanes = lax.broadcasted_iota(jnp.int32, (8, REGION), 1)

    def body(group, carry):
        at = pl.multiple_of(group * 16, 16)
        coeff = [coeff_ref[pl.ds(at + 8 * q, 8), :] for q in range(2)]
        for local in range(GROUP):
            panel = group * GROUP + local
            depth = place_ref[1, panel]
            shift = (depth - 4 * local) & (REGION - 1)
            inside = in_window(lanes, depth)
            for q in range(2):
                first = pl.multiple_of(panel * 16 + 8 * q, 8)
                out_ref[pl.ds(first, 8), :] = jnp.where(inside, pltpu.roll(coeff[q], shift, 1), 0.0)
        return carry

    lax.fori_loop(0, place_ref.shape[1] // GROUP, body, 0)


def place_lines(places, coeff, awaited):
    count = places.shape[1]
    shape = (count * 16, REGION)
    return pl.pallas_call(
        lines_kernel,
        in_specs=[in_smem(), whole_vmem()] + [anywhere()] * len(awaited),
        out_specs=whole_vmem(),
        out_shape=jax.ShapeDtypeStruct(shape, F32),
        compiler_params=params(),
        cost_estimate=cost(16 * count * REGION, 4 * 16 * count * REGION),
        name="place_lines",
    )(places, coeff, *awaited)


def stack_pieces(parts, reach_x, reach_y, top, opened, stacked):
    half = reach_x // 2
    pitch = up_to(reach_y, 8)
    tall = len(parts) * pitch
    core = lax.axis_index("pair")
    for bit, part in enumerate(parts):
        first = from_short(part[:top, :])
        opened[...] = from_short(part[top:, :]) * unit(first[0:1], first[1:2])
        place = (core ^ bit) * pitch
        for i in range(half):
            stacked[pl.ds(pl.multiple_of(i * tall + place, 8), reach_y), :] = opened[
                i * reach_y : (i + 1) * reach_y, :
            ]


def transform_pieces(table, stacked, before, spectrum):
    half = spectrum.shape[0]
    tall = stacked.shape[0] // half

    def tripled(values):
        high, low = split(values)
        return jnp.concatenate([high, low, high], axis=0)

    for i in range(0, half, 2):
        places = range(i, min(i + 2, half))
        held = jnp.concatenate([stacked[j * tall : (j + 1) * tall, :] for j in places], axis=1)
        result = dot(table, tripled(held))
        for j in places:
            made = result[:, (j - i) * 2 * HALF : (j - i + 1) * 2 * HALF]
            spectrum[j] = made if before is None else before[j] + made


def forward_early_kernel(reach_x, reach_y, pair, *refs):
    parts = refs[:pair]
    table_ref, spectrum, opened, stacked = refs[pair:]
    top = parts[0].shape[0] - opened.shape[0]
    stacked[...] = jnp.zeros_like(stacked)
    stack_pieces(parts, reach_x, reach_y, top, opened, stacked)
    transform_pieces(table_ref[lax.axis_index("narrow")], stacked, None, spectrum)


def stacking_scratch(pair, reach_x, reach_y):
    half = reach_x // 2
    return [
        pltpu.VMEM((up_to(half * reach_y, 16), 2 * HALF), F32),
        pltpu.VMEM((half * pair * up_to(reach_y, 8), 2 * HALF), F32),
    ]


def forward_early(parts, table, reach_x, reach_y):
    half = reach_x // 2
    pair = len(parts)
    return pl.pallas_call(
        functools.partial(forward_early_kernel, reach_x, reach_y, pair),
        in_specs=[whole_vmem()] * (pair + 1),
        out_specs=whole_vmem(),
        out_shape=jax.ShapeDtypeStruct((half, GRID, 2 * HALF), F32),
        scratch_shapes=stacking_scratch(pair, reach_x, reach_y),
        compiler_params=params(),
        cost_estimate=cost(2 * half * 256 * 256 * 128, 4 * half * GRID * 2 * HALF * 2),
        name="forward_early",
    )(*parts, table)


def forward_kernel(reach_x, reach_y, blocks, pieces, awaited, *refs):
    parts = refs[:pieces]
    early_ref, table_ref, modes_ref = refs[pieces : pieces + 3]
    refs = refs[: pieces + 3] + refs[pieces + 3 + awaited :]
    spectrum, even_out, odd_out, own_out, peers_out, inner_out = refs[pieces + 3 : pieces + 9]
    opened, stacked, slabs, head = refs[pieces + 9 :]
    half = reach_x // 2
    pair = lax.axis_size("pair")
    top = parts[0].shape[0] - opened.shape[0]
    stacked[...] = jnp.zeros_like(stacked)
    head[...] = jnp.zeros_like(head)
    for piece in range(pieces):
        first = from_short(parts[piece][:top, :])
        mantissa, exponent = first[2 : 2 + blocks], first[2 + blocks : 2 + 2 * blocks]
        peers_out[piece * blocks : (piece + 1) * blocks, :] = decode_rounded(mantissa, exponent)
        at = 6 + 2 * piece * blocks
        head[at : at + blocks, :] = mantissa
        head[at + blocks : at + 2 * blocks, :] = exponent
    before = early_ref
    for chip in range(1, pieces // pair):
        stack_pieces(parts[chip * pair : (chip + 1) * pair], reach_x, reach_y, top, opened, stacked)
        transform_pieces(table_ref[lax.axis_index("narrow") ^ chip], stacked, before, spectrum)
        before = spectrum

    chunk = 32

    def body(index, largest):
        rows = pl.ds(pl.multiple_of(index * chunk, chunk), chunk)
        low = low_lanes(chunk)
        decay = modes_ref[0, rows, :]
        log_decay = modes_ref[1, rows, :]
        across_half = jnp.exp(half * log_decay)
        across_cut = jnp.exp((half - 4) * log_decay)
        layers = [spectrum[i, rows, :] for i in range(half)]
        run = layers[0]
        cut_right = run
        for i in range(1, half):
            run = decay * run + layers[i]
            if i == half - 5:
                cut_right = run
        right = run
        run = layers[half - 1]
        cut_left = run
        for i in range(half - 2, -1, -1):
            run = decay * run + layers[i]
            if i == 4:
                cut_left = run
        left = run
        inner_out[rows, :] = jnp.where(low, right, left)
        swapped_right, swapped_left = swap(right), swap(left)
        own = jnp.where(low, left + across_half * swapped_left, right + across_half * swapped_right)
        made = [
            jnp.where(low, swap(layers[half - 4]), layers[half - 3]),
            jnp.where(low, swap(layers[half - 2]), layers[half - 1]),
            jnp.where(low, own, cut_right + across_cut * swapped_right),
            jnp.where(low, layers[0], swap(layers[1])),
            jnp.where(low, layers[2], swap(layers[3])),
            jnp.where(low, cut_left + across_cut * swapped_left, own),
        ]
        own_out[rows, :] = own
        for slab, values in enumerate(made):
            slabs[slab, rows, :] = values
        return tuple(
            jnp.maximum(old, jnp.max(jnp.abs(values).reshape(chunk // 8, 8, 2 * HALF), axis=0))
            for old, values in zip(largest, made)
        )

    zero = jnp.zeros((8, 2 * HALF), F32)
    largest = lax.fori_loop(0, GRID // chunk, body, (zero,) * 6)
    scales = [fit_scale(jnp.max(value, axis=0, keepdims=True)) for value in largest]
    head_rows = head.shape[0]

    def send(out, first):
        for slab in range(3):
            exponent, fraction = scales[first + slab]
            head[2 * slab : 2 * slab + 1, :] = exponent
            head[2 * slab + 1 : 2 * slab + 2, :] = fraction
            at = head_rows + slab * GRID
            out[at : at + GRID, :] = quantize(slabs[first + slab], exponent, fraction)
        out[:head_rows, :] = to_short(head[...])

    on_left = lax.axis_index("wide") & 1

    @pl.when(on_left == 0)
    def _():
        send(even_out, 0)
        send(odd_out, 3)

    @pl.when(on_left == 1)
    def _():
        send(even_out, 3)
        send(odd_out, 0)


def forward(parts, early, table, modes, reach_x, reach_y, blocks, awaited):
    pieces = len(parts)
    half = reach_x // 2
    lanes = 2 * HALF
    head = up_to(6 + 2 * pieces * blocks, 16)
    short = lambda rows: jax.ShapeDtypeStruct((rows, lanes), jnp.int16)
    return pl.pallas_call(
        functools.partial(
            forward_kernel, reach_x, reach_y, blocks, pieces, len(awaited)
        ),
        in_specs=[whole_vmem()] * (pieces + 3) + [anywhere()] * len(awaited),
        out_specs=[whole_vmem()] * 6,
        out_shape=[
            jax.ShapeDtypeStruct((half, GRID, lanes), F32),
            short(head + 3 * GRID),
            short(head + 3 * GRID),
            jax.ShapeDtypeStruct((GRID, lanes), F32),
            jax.ShapeDtypeStruct((pieces * blocks, BLOCK), F32),
            jax.ShapeDtypeStruct((GRID, lanes), F32),
        ],
        scratch_shapes=stacking_scratch(pieces // table.shape[0], reach_x, reach_y)
        + [
            pltpu.VMEM((6, GRID, lanes), F32),
            pltpu.VMEM((head, lanes), F32),
        ],
        compiler_params=params(),
        cost_estimate=cost(2 * half * 256 * 256 * 128, 4 * half * GRID * lanes * 2),
        name="forward",
    )(*parts, early, table, modes, *awaited)


def opened_slabs(ref, count, head_rows):
    first = from_short(ref[:16, :])
    for slab in range(count):
        scale = unit(first[2 * slab : 2 * slab + 1], first[2 * slab + 1 : 2 * slab + 2])
        at = head_rows + slab * GRID
        yield from_short(ref[at : at + GRID, :]) * scale


def pair_kernel(reach_x, flips, own_ref, even_ref, modes_ref, *refs):
    outs, head = refs[:-1], refs[-1]
    span = reach_x - 4
    here = lax.axis_index("wide")
    low = low_lanes(GRID)
    decay, log_decay = modes_ref[0], modes_ref[1]
    own = own_ref[...]
    one, two, cut = opened_slabs(even_ref, 3, even_ref.shape[0] - 3 * GRID)
    left = ((decay * cut + swap(one)) * decay + one) * decay + swap(two)
    left = jnp.where(low, cut, left * decay + two)
    right = ((decay * cut + swap(two)) * decay + two) * decay + swap(one)
    right = jnp.where(low, right * decay + one, cut)
    partner = jnp.where((here & 1) == 1, left, right)

    def weight(distances):
        powers = []
        for distance in distances:
            ahead = span * distance - reach_x
            powers.append(jnp.where(distance >= 2, ahead, ahead + GRID).astype(F32))
        return jnp.exp(jnp.where(low, *powers) * log_decay)

    head[...] = jnp.zeros_like(head)
    for flip, out in zip(flips, outs):
        behind = (here ^ flip) - here
        message = own * weight((-behind, behind))
        behind = (here ^ flip) - (here ^ 1)
        beside = jnp.where(jnp.abs(behind) == 1, 0.0, 1.0)
        send_piece(out, head, message + partner * (weight((-behind, behind)) * beside))


def pair_messages(own, from_even, modes, reach_x, flips):
    return pl.pallas_call(
        functools.partial(pair_kernel, reach_x, flips),
        in_specs=[whole_vmem()] * 3,
        out_specs=[whole_vmem()] * len(flips),
        out_shape=[jax.ShapeDtypeStruct((16 + GRID, 2 * HALF), jnp.int16)] * len(flips),
        scratch_shapes=[pltpu.VMEM((16, 2 * HALF), F32)],
        compiler_params=params(),
        cost_estimate=cost(16 * GRID * 2 * HALF, 4 * GRID * 2 * HALF * (6 + len(flips))),
        name="pair_messages",
    )(own, from_even, modes)


def send_fields(outs, flips, reach_y, field_high, field_low, high_ref, low_ref, ready, head):
    half = field_high.shape[0]
    mine = y_position()
    pitch = up_to(reach_y, 16)
    pick = lambda ref: jnp.concatenate([ref[mine ^ flip] for flip in flips], axis=0)
    table = (pick(high_ref), pick(low_ref))
    for i in range(0, half, 2):
        many = min(2, half - i)
        join = lambda ref: jnp.concatenate([ref[i + j] for j in range(many)], axis=1)
        result = dot_three(table, (join(field_high), join(field_low)))
        for j in range(many):
            for piece in range(len(flips)):
                ready[piece, (i + j) * reach_y : (i + j + 1) * reach_y, :] = result[
                    piece * pitch : piece * pitch + reach_y, j * 2 * HALF : (j + 1) * 2 * HALF
                ]
    head[...] = jnp.zeros_like(head)
    for piece, out in enumerate(outs):
        if ready.shape[1] > half * reach_y:
            ready[piece, half * reach_y :, :] = jnp.zeros_like(ready[piece, half * reach_y :, :])
        send_piece(out, head, ready[piece])


def inverse_kernel(reach_x, reach_y, flips, fars, *refs):
    spectrum, from_even, from_odd, own_ref, inner_ref, *far_refs = refs[: 5 + fars]
    refs = refs[5 + fars :]
    high_ref, low_ref, modes_ref = refs[:3]
    outs = refs[3 : 3 + len(flips)]
    field_high, field_low, ready, head = refs[3 + len(flips) :]
    half = reach_x // 2
    span = reach_x - 4
    chunk = 32
    head_rows = from_even.shape[0] - 3 * GRID
    on_left = (lax.axis_index("wide") & 1) == 1
    both_heads = from_short(from_even[:16, :]), from_short(from_odd[:16, :])
    both_units = [
        [unit(first[2 * slab : 2 * slab + 1], first[2 * slab + 1 : 2 * slab + 2]) for slab in range(3)]
        for first in both_heads
    ]

    def sided(even, odd):
        return jnp.where(on_left, even, odd), jnp.where(on_left, odd, even)

    far_units = []
    for ref in far_refs:
        first = from_short(ref[:16, :])
        far_units.append(unit(first[0:1], first[1:2]))

    def body(index, carry):
        first = pl.multiple_of(index * chunk, chunk)
        rows = pl.ds(first, chunk)
        low = low_lanes(chunk)
        decay = modes_ref[0, rows, :]
        log_decay = modes_ref[1, rows, :]
        ring = modes_ref[2, rows, :]
        gain = modes_ref[3, rows, :]
        across_half = jnp.exp(half * log_decay)
        across_cut = jnp.exp((half - 4) * log_decay)
        around = jnp.exp((GRID - 4) * log_decay)
        beside = jnp.exp((GRID - reach_x - span) * log_decay)
        layers = [spectrum[i, rows, :] for i in range(half)]

        def slab(which):
            at = pl.ds(pl.multiple_of(head_rows + which * GRID + index * chunk, chunk), chunk)
            even = from_short(from_even[at, :]) * both_units[0][which]
            return sided(even, from_short(from_odd[at, :]) * both_units[1][which])

        head_layers, tail_layers = zip(slab(0), slab(1))
        left_moments, right_moments = slab(2)
        zero = jnp.zeros_like(decay)
        from_head = [head_layers[0], swap(head_layers[0]), head_layers[1], swap(head_layers[1])]
        from_tail = [swap(tail_layers[0]), tail_layers[0], swap(tail_layers[1]), tail_layers[1]]
        head_sum = from_head[0]
        for i in range(1, 4):
            head_sum = decay * head_sum + from_head[i]
        tail_sum = from_tail[3]
        for i in range(2, -1, -1):
            tail_sum = decay * tail_sum + from_tail[i]
        for i in range(4):
            layers[i] = layers[i] + jnp.where(low, from_head[i], zero)
        for i in range(4):
            place = half - 4 + i
            layers[place] = layers[place] + jnp.where(low, zero, from_tail[i])
        total = own_ref[rows, :] * jnp.exp((GRID - reach_x) * log_decay)
        at = pl.ds(pl.multiple_of(16 + index * chunk, 16), chunk)
        for ref, scale in zip(far_refs, far_units):
            total = total + from_short(ref[at, :]) * scale
        one = jnp.ones_like(decay)
        total = total + left_moments * jnp.where(low, beside, one)
        total = total + right_moments * jnp.where(low, one, beside)
        shared = jnp.where(low, head_sum, tail_sum)
        entering = (swap(total) + around * shared) * ring
        leaving = swap(across_half * entering + across_cut * shared + inner_ref[rows, :])
        run = jnp.where(low, entering, leaving)
        forward_runs = []
        for i in range(half):
            run = decay * run + layers[i]
            forward_runs.append(run)
        run = jnp.where(low, leaving, entering)
        for i in range(half - 1, -1, -1):
            ahead = decay * run
            high, rest = split(gain * (forward_runs[i] + ahead))
            field_high[i, rows, :] = high
            field_low[i, rows, :] = rest
            run = ahead + layers[i]
        return carry

    lax.fori_loop(0, GRID // chunk, body, 0)
    send_fields(outs, flips, reach_y, field_high, field_low, high_ref, low_ref, ready, head)


def inverse(
    spectrum, from_even, from_odd, own, inner, fars, table, modes, reach_x, reach_y, flips
):
    half = reach_x // 2
    lanes = 2 * HALF
    body = up_to(half * reach_y, 16)
    shapes = [jax.ShapeDtypeStruct((16 + body, lanes), jnp.int16)] * len(flips)
    shapes += [jax.ShapeDtypeStruct((half, GRID, lanes), BF16)] * 2
    return pl.pallas_call(
        functools.partial(inverse_kernel, reach_x, reach_y, flips, len(fars)),
        in_specs=[whole_vmem()] * (8 + len(fars)),
        out_specs=[whole_vmem()] * len(shapes),
        out_shape=shapes,
        scratch_shapes=[
            pltpu.VMEM((len(flips), body, lanes), F32),
            pltpu.VMEM((16, lanes), F32),
        ],
        compiler_params=params(),
        cost_estimate=cost(2 * half * 256 * 256 * 128, 4 * half * GRID * lanes * 2),
        name="inverse",
    )(spectrum, from_even, from_odd, own, inner, *fars, *table, modes)


def inverse_rest_kernel(reach_y, flips, field_high, field_low, high_ref, low_ref, *refs):
    outs, (ready, head) = refs[: len(flips)], refs[len(flips) :]
    send_fields(outs, flips, reach_y, field_high, field_low, high_ref, low_ref, ready, head)


def inverse_rest(field, table, reach_y, flips):
    half = field[0].shape[0]
    lanes = 2 * HALF
    body = up_to(half * reach_y, 16)
    return pl.pallas_call(
        functools.partial(inverse_rest_kernel, reach_y, flips),
        in_specs=[whole_vmem()] * 4,
        out_specs=[whole_vmem()] * len(flips),
        out_shape=[jax.ShapeDtypeStruct((16 + body, lanes), jnp.int16)] * len(flips),
        scratch_shapes=[
            pltpu.VMEM((len(flips), body, lanes), F32),
            pltpu.VMEM((16, lanes), F32),
        ],
        compiler_params=params(),
        cost_estimate=cost(2 * half * 256 * 256 * 128, 4 * half * GRID * lanes * 2),
        name="inverse_rest",
    )(*field, *table)


def sum_rows(values):
    row = lax.broadcasted_iota(jnp.int32, values[0].shape, 0)
    for step in (4, 2, 1):
        low = (row & step) == 0
        paired = []
        for one, other in zip(values[: len(values) // 2], values[len(values) // 2 :]):
            kept = jnp.where(low, one, other)
            moved = jnp.where(low, other, one)
            if step == 4:
                moved = pltpu.roll(moved, 4, 0)
            else:
                moved = jnp.where(low, pltpu.roll(moved, 8 - step, 0), pltpu.roll(moved, step, 0))
            paired.append(kept + moved)
        values = paired
    return values[0]


def z_lines(parts, flips, high_ref, low_ref):
    mine = y_position()
    opened = []
    for part in parts:
        first = from_short(part[:16, :])
        opened.append(from_short(part[16:, :]) * unit(first[0:1], first[1:2]))
    values = split(jnp.concatenate(opened, axis=1))
    pick = lambda ref: jnp.concatenate([ref[mine ^ flip] for flip in flips], axis=0)
    return dot_three(values, (pick(high_ref), pick(low_ref)))


def sample_early_kernel(*refs):
    *parts, high_ref, low_ref, out_ref = refs
    out_ref[...] = z_lines(parts, range(len(parts)), high_ref, low_ref)


def sample_early(parts, table):
    rows = parts[0].shape[0] - 16
    return pl.pallas_call(
        sample_early_kernel,
        in_specs=[whole_vmem()] * (len(parts) + 2),
        out_specs=whole_vmem(),
        out_shape=jax.ShapeDtypeStruct((rows, 2 * REGION), F32),
        compiler_params=params(),
        cost_estimate=cost(2 * rows * 256 * 256 * 3, 4 * rows * 512),
        name="sample_early",
    )(*parts, *table)


def sample_kernel(last, reach_x, reach_y, flips, place_ref, *refs):
    parts = refs[: len(flips)]
    early_ref, high_ref, low_ref, line_ref, own_ref, vector_ref, near_ref, out_ref = refs[
        len(flips) : len(flips) + 8
    ]
    flat, field, sums = refs[len(flips) + 8 :]
    half_rows = reach_x * reach_y // 2
    both = early_ref[...] + z_lines(parts, flips, high_ref, low_ref)
    flat[:half_rows, :] = both[:half_rows, :REGION]
    flat[half_rows:, :] = both[:half_rows, REGION:]
    for x in range(reach_x):
        layer = flat[x * reach_y : (x + 1) * reach_y, :]
        for row in pair_rows(x, reach_x, reach_y):
            field[pl.ds(row, reach_y, stride=2), :] = layer
    count = place_ref.shape[1]

    def body(group, carry):
        for eight in range(0, GROUP, 8):
            totals = []
            for local in range(eight, eight + 8):
                panel = group * GROUP + local
                row = place_ref[0, panel]
                first = pl.multiple_of(panel * 16, 16)
                totals.append(
                    field[pl.ds(row, 8), :] * line_ref[pl.ds(first, 8), :]
                    + field[pl.ds(row + 2 * reach_y, 8), :] * line_ref[pl.ds(first + 8, 8), :]
                )
            sums[pl.ds(pl.multiple_of(group * GROUP + eight, 8), 8), :] = sum_rows(totals)
        return carry

    lax.fori_loop(0, count // GROUP, body, 0)
    sampled = lax.dot_general(
        jnp.ones((8, REGION), F32),
        sums[...],
        (((1,), (1,)), ((), ())),
        precision=lax.Precision.HIGHEST,
        preferred_element_type=F32,
    )
    for block in range(count // BLOCK):
        lane = slice(block * BLOCK, (block + 1) * BLOCK)
        row = slice(block, block + 1)
        vector = vector_ref[row, :]
        image = jnp.where(own_ref[row, :] == 1, 0.0, 0.5 * vector) + sampled[:1, lane]
        image = image + near_ref[row, :]
        if last:
            out_ref[0:1, lane] = vector
            out_ref[1:2, lane] = image
        else:
            out_ref[row, :] = image


def sample(last, places, parts, flips, early, table, lines, flag, vector, near, reach_x, reach_y):
    count = places.shape[1]
    blocks = count // BLOCK
    shape = (2, count) if last else (blocks, BLOCK)
    return pl.pallas_call(
        functools.partial(sample_kernel, last, reach_x, reach_y, flips),
        in_specs=[in_smem()] + [whole_vmem()] * (len(parts) + 7),
        out_specs=whole_vmem(),
        out_shape=jax.ShapeDtypeStruct(shape, F32),
        scratch_shapes=[
            pltpu.VMEM((reach_x * reach_y, REGION), F32),
            pltpu.VMEM((pair_count(reach_x, reach_y), REGION), F32),
            pltpu.VMEM((count, REGION), F32),
        ],
        compiler_params=params(),
        cost_estimate=cost(reach_x * reach_y * 256 * 512, 4 * 16 * count * REGION),
        name="sample",
    )(
        places,
        *parts,
        early,
        *table,
        lines,
        flag.reshape(blocks, BLOCK),
        vector.reshape(blocks, BLOCK),
        near,
    )


def near_kernel(slots, blocks, place_ref, target_ref, *refs):
    even_ref, odd_ref, peers_ref, tile_ref, out_ref, held = refs
    count = peers_ref.shape[0]
    held[count : 2 * count, :] = peers_ref[...]
    on_left = lax.axis_index("wide") & 1
    for side, ref in ((1 - on_left, even_ref), (on_left, odd_ref)):
        top = from_short(ref[...])
        for piece in range(count // blocks):
            at = 6 + 2 * piece * blocks
            held[pl.ds(side * (2 * count) + piece * blocks, blocks), :] = decode_rounded(
                top[at : at + blocks], top[at + blocks : at + 2 * blocks]
            )
    out_ref[...] = jnp.zeros_like(out_ref)
    for slot in range(slots):
        picked = held[pl.ds(place_ref[slot], 1), :]
        picked = jnp.broadcast_to(picked, (16, BLOCK)).astype(BF16)
        product = lax.dot_general(
            picked,
            tile_ref[slot],
            (((1,), (1,)), ((), ())),
            preferred_element_type=F32,
        )
        target = pl.ds(target_ref[slot], 1)
        out_ref[target, :] = out_ref[target, :] + product[:1]


def near_field(places, targets, from_even, from_odd, peers, tiles, blocks, out_rows):
    slots = tiles.shape[0]
    head = from_even.shape[0] - 3 * GRID
    constant = lambda shape: pl.BlockSpec(shape, lambda i: (0,) * len(shape))
    return pl.pallas_call(
        functools.partial(near_kernel, slots, blocks),
        grid=(1,),
        in_specs=[
            in_smem(),
            in_smem(),
            constant((head, BLOCK)),
            constant((head, BLOCK)),
            constant(peers.shape),
            constant(tiles.shape),
        ],
        out_specs=constant((out_rows, BLOCK)),
        out_shape=jax.ShapeDtypeStruct((out_rows, BLOCK), F32),
        scratch_shapes=[pltpu.VMEM((3 * peers.shape[0], BLOCK), F32)],
        compiler_params=params(),
        cost_estimate=cost(2 * slots * 16 * BLOCK * BLOCK, 2 * slots * BLOCK * BLOCK),
        name="near_field",
    )(places, targets, from_even, from_odd, peers, tiles)


def shards(
    density,
    surface_flag,
    stencil_base,
    sample_weights,
    dipole_weights,
    near_target,
    near_source,
    near_tiles,
):
    x_count = lax.axis_size("wide")
    y_count = lax.axis_size(Y_AXES)
    y_index = lax.axis_index(Y_AXES)
    pair = lax.axis_size("pair")
    span_x = REGION // x_count
    span_y = REGION // y_count
    reach_x = span_x + 4
    reach_y = span_y + 4
    count = density.shape[0]
    blocks = count // BLOCK

    z_forward, z_inverse, y_forward, y_inverse, modes = tables(y_count, pair, span_y)
    modes = lax.dynamic_index_in_dim(jnp.asarray(modes), y_index, 0, keepdims=False)

    neighbour = near_source // blocks
    flip = (y_index + neighbour % 3 - 1) ^ y_index
    sources = ((neighbour // 3) * y_count + flip) * blocks + near_source % blocks
    out_rows = up_to(blocks + 1, 8)
    live = near_target >= 0
    sources = jnp.where(live, sources, 0)
    targets = jnp.where(live, near_target, out_rows - 1)

    swaps = lambda pairs: [(i, j) for i, j in pairs] + [(j, i) for i, j in pairs]
    even_swap = swaps([(i, i + 1) for i in range(0, x_count - 1, 2)])
    odd_swap = swaps([(i, i + 1) for i in range(1, x_count - 1, 2)])
    far_flips = list(range(2, x_count, 2))

    local, moving = [0], list(range(1, y_count))

    def flipped(parts, flips):
        return [
            lax.ppermute(part, Y_AXES, [(i, i ^ flip) for i in range(y_count)])
            for flip, part in zip(flips, parts)
        ]

    def convolve_and_sample(last, vector, sent, both, places, sample_lines, awaited):
        arrived = flipped(sent, moving)
        arrived = list(spread_rest(vector, both, z_forward, local)) + arrived
        early = forward_early(arrived[:pair], y_forward, reach_x, reach_y)
        spectrum, even_message, odd_message, own, peers, inner = forward(
            arrived, early, y_forward, modes, reach_x, reach_y, blocks, awaited
        )
        from_even = lax.ppermute(even_message, "wide", even_swap)
        from_odd = lax.ppermute(odd_message, "wide", odd_swap)
        fars = [
            lax.ppermute(message, "wide", [(i, i ^ flip) for i in range(x_count)])
            for flip, message in zip(
                far_flips, pair_messages(own, from_even, modes, reach_x, far_flips)
            )
        ]
        near_part = near_field(
            sources, targets, from_even, from_odd, peers, near_tiles, blocks, out_rows
        )
        *sent, high, low = inverse(
            spectrum,
            from_even,
            from_odd,
            own,
            inner,
            fars,
            y_inverse,
            modes,
            reach_x,
            reach_y,
            moving,
        )
        arrived = flipped(sent, moving)
        arrived = list(inverse_rest((high, low), y_inverse, reach_y, local)) + arrived
        image = sample(
            last,
            places,
            arrived[pair:],
            list(range(pair, y_count)),
            sample_early(arrived[:pair], z_inverse),
            z_inverse,
            sample_lines,
            surface_flag,
            vector,
            near_part,
            reach_x,
            reach_y,
        )
        return image, near_part

    raw = (stencil_base, surface_flag, sample_weights, dipole_weights)
    *sent, high, low, source_coeff, sample_coeff, places = spread(
        density, z_forward, None, raw, reach_x, reach_y, moving
    )
    sample_lines = place_lines(places, sample_coeff, [])
    first_image, near_part = convolve_and_sample(
        False, density, sent, (high, low), places, sample_lines, [sample_lines]
    )
    first_image = first_image.reshape(-1)
    source_lines = place_lines(places, source_coeff, [near_part])
    *sent, high, low = spread(
        first_image, z_forward, (places, source_lines), None, reach_x, reach_y, moving
    )
    both_images, _ = convolve_and_sample(
        True, first_image, sent, (high, low), places, sample_lines, []
    )
    return both_images


def solution(mesh):
    panels = P(("groups",) + ALL_AXES)
    columns = P(None, ("groups",) + ALL_AXES)
    in_specs = (
        panels,
        panels,
        columns,
        columns,
        columns,
        panels,
        panels,
        P(("groups",) + ALL_AXES, None, None),
    )
    return jax.shard_map(
        shards, mesh=mesh, in_specs=in_specs, out_specs=columns, check_vma=False
    )
```

```python
import functools
import math

import jax
import jax.numpy as jnp
import numpy as np
from jax import lax
from jax.experimental import pallas as pl
from jax.experimental.pallas import tpu as pltpu
from jax.sharding import PartitionSpec as P

GRID = 256
REGION = 128
BLOCK = 128
HALF = 64
KERNEL_GAIN = 4.0
SCREEN = 1.0 / 1024.0
LN2 = math.log(2.0)
Y_AXES = ("narrow", "pair")
ALL_AXES = ("wide", "narrow", "pair")
F32 = jnp.float32
BF16 = jnp.bfloat16
VMEM_LIMIT = 24 * 1024 * 1024
START_LIMIT = VMEM_LIMIT
GROUP = 32
CHAINS = 2


def cas(angles):
    return np.cos(angles) + np.sin(angles)


def up_to(count, multiple):
    return -(-count // multiple) * multiple


def low_lanes(rows):
    return lax.broadcasted_iota(jnp.int32, (rows, 2 * HALF), 1) < HALF


def swap(values):
    return pltpu.roll(values, HALF, 1)


def split(values):
    high = values.astype(BF16)
    return high, (values - high.astype(F32)).astype(BF16)


def dot(left, right):
    return jnp.dot(left, right, preferred_element_type=F32)


def dot_three(left, right):
    return dot(left[0], right[0]) + (dot(left[0], right[1]) + dot(left[1], right[0]))


def params():
    return pltpu.CompilerParams(vmem_limit_bytes=VMEM_LIMIT)


def whole_vmem():
    return pl.BlockSpec(memory_space=pltpu.VMEM)


def anywhere():
    return pl.BlockSpec(memory_space=pl.ANY)


def in_smem():
    return pl.BlockSpec(memory_space=pltpu.SMEM)


def cost(flops, moved):
    return pl.CostEstimate(flops=flops, bytes_accessed=moved, transcendentals=0)


def full_scale(exponent, fraction):
    return fraction * jnp.exp(exponent * LN2) * (1.0 / 1024.0)


def fit_scale(largest):
    largest = jnp.maximum(largest, 1e-30)
    exponent = jnp.floor(jnp.log(largest) * (1.0 / LN2))
    fraction = jnp.ceil(largest * jnp.exp(-exponent * LN2) * 1024.0) + 1.0
    return exponent, fraction


def to_short(values):
    return values.astype(jnp.int32).astype(jnp.int16)


def from_short(values):
    return values.astype(jnp.int32).astype(F32)


def quantize(values, exponent, fraction):
    return to_short(jnp.round(values * (32767.0 / full_scale(exponent, fraction))))


def unit(exponent, fraction):
    return full_scale(exponent, fraction) * (1.0 / 32767.0)


def encode_rounded(values):
    rounded = values.astype(BF16).astype(F32)
    size = jnp.maximum(jnp.abs(rounded), 1e-30)
    exponent = jnp.floor(jnp.log(size) * (1.0 / LN2))
    return jnp.round(rounded * jnp.exp((10.0 - exponent) * LN2)), exponent


def decode_rounded(mantissa, exponent):
    return (mantissa * jnp.exp((exponent - 10.0) * LN2)).astype(BF16).astype(F32)


def send_piece(out, head, values):
    exponent, fraction = fit_scale(jnp.max(jnp.abs(values), axis=0, keepdims=True))
    head[0:1, :] = exponent
    head[1:2, :] = fraction
    top = head.shape[0]
    out[:top, :] = to_short(head[...])
    out[top:, :] = quantize(values, exponent, fraction)


def y_position():
    return lax.axis_index("narrow") * lax.axis_size("pair") + lax.axis_index("pair")


def halves(table):
    high = table.astype(jnp.bfloat16)
    return high, (table - high.astype(np.float64)).astype(jnp.bfloat16)


def tables(y_count, pair, span_y):
    depth = GRID // y_count
    reach = span_y + 4
    waves = np.arange(GRID)
    step = 2.0 * np.pi / GRID
    z_table = cas(step * np.outer(np.arange(REGION), waves))
    z_forward = np.zeros((y_count, 2 * REGION, 2 * HALF))
    z_inverse = np.zeros((y_count, 2 * HALF, 2 * REGION))
    symbols = 4.0 * np.sin(np.pi * waves / GRID) ** 2
    shift = np.full((y_count, GRID, 2 * HALF), 1.0)
    y_forward = np.zeros((GRID, y_count, up_to(reach, 8)))
    y_inverse = np.zeros((y_count, up_to(reach, 16), GRID))
    for block in range(y_count):
        mine = z_table[:, block * depth : (block + 1) * depth]
        for half in range(2):
            rows = slice(half * REGION, (half + 1) * REGION)
            lanes = slice(half * HALF, half * HALF + depth)
            z_forward[block, rows, lanes] = mine
            z_inverse[block, lanes, rows] = mine.T / GRID
            shift[block, :, lanes] = (
                SCREEN + symbols[:, None] + symbols[None, block * depth : (block + 1) * depth]
            )
        cells = block * span_y - 2 + np.arange(reach)
        y_table = cas(step * np.outer(waves, cells))
        y_forward[:, block, :reach] = y_table
        y_inverse[block, :reach] = y_table.T / GRID
    y_forward = y_forward.reshape(GRID, y_count // pair, -1).transpose(1, 0, 2)
    y_forward = halves(y_forward)
    y_forward = np.concatenate([y_forward[0], y_forward[0], y_forward[1]], axis=2)
    root = np.sqrt(shift * (shift + 4.0))
    decay = 2.0 / (2.0 + shift + root)
    log_decay = np.log(decay)
    ring = 1.0 / (1.0 - np.exp(GRID * log_decay))
    gain = KERNEL_GAIN / root
    modes = np.stack([decay, log_decay, ring, gain], axis=1).astype(np.float32)
    return (
        halves(z_forward),
        halves(z_inverse),
        y_forward,
        halves(y_inverse),
        modes,
    )


def weave(flag, sample_refs, dipole_refs, source_out, sample_out):
    place = lax.broadcasted_iota(jnp.int32, (4 * BLOCK, 4 * BLOCK), 0)
    lane = lax.broadcasted_iota(jnp.int32, (4 * BLOCK, 4 * BLOCK), 1)
    wanted = 4 * (place % BLOCK) + place // BLOCK
    mixing = jnp.where(lane == wanted, 1.0, 0.0).astype(BF16)
    stacked = []
    for tile, (sample_ref, dipole_ref) in enumerate(zip(sample_refs, dipole_refs)):
        charged = flag[:, tile * BLOCK : (tile + 1) * BLOCK] == 1
        rows = []
        for depth in range(4):
            sample = sample_ref[pl.ds(depth, 16, stride=4), :]
            dipole = dipole_ref[pl.ds(depth, 16, stride=4), :]
            rows.append(jnp.concatenate([jnp.where(charged, -sample, dipole), sample], axis=0))
        stacked.append(jnp.concatenate(rows, axis=1))
    weights = jnp.concatenate(stacked, axis=0)
    first, rest = split(weights)
    second, third = split(weights - first.astype(F32))
    woven = dot(first, mixing) + (dot(second, mixing) + dot(third, mixing))
    for tile in range(len(sample_refs)):
        for which, out in enumerate((source_out, sample_out)):
            for part in range(BLOCK // GROUP):
                at = (tile * (BLOCK // GROUP) + part) * 16
                lanes = slice(part * BLOCK, (part + 1) * BLOCK)
                for a in range(4):
                    row = tile * 32 + which * 16 + 4 * a
                    out[pl.ds(at + 8 * (a // 2) + a % 2, 4, stride=2), :] = woven[
                        row : row + 4, lanes
                    ]


def pair_rows(x, reach_x, reach_y):
    even = (x // 2) * 2 * reach_y + x % 2
    if x == 0 or x == reach_x - 1:
        return [even]
    return [even, reach_x * reach_y + ((x - 1) // 2) * 2 * reach_y + (x - 1) % 2]


def pair_count(reach_x, reach_y):
    return (2 * reach_x - 2) * reach_y


def in_window(lanes, depth):
    return ((lanes - depth) & -4) == 0


def add_panels(reach, woven, vector_ref, place_ref, weight_ref, grids):
    lanes = lax.broadcasted_iota(jnp.int32, (8, REGION), 1)

    def body(group, carry):
        at = pl.multiple_of(group * 16, 16)
        coeff = [weight_ref[pl.ds(at + 8 * q, 8), :] for q in range(2)] if woven else None
        for local in range(GROUP):
            panel = group * GROUP + local
            grid = grids[local % len(grids)]
            row = place_ref[0, panel]
            value = vector_ref[panel]
            if woven:
                depth = place_ref[1, panel]
                shift = (depth - 4 * local) & (REGION - 1)
                value = jnp.where(in_window(lanes, depth), value, 0.0)
                lines = [pltpu.roll(coeff[q], shift, 1) for q in range(2)]
            else:
                first = pl.multiple_of(panel * 16, 16)
                lines = [weight_ref[pl.ds(first + 8 * q, 8), :] for q in range(2)]
            places = [pl.ds(row, 8), pl.ds(row + 2 * reach, 8)]
            held = [grid[place, :] for place in places]
            for q in range(2):
                grid[places[q], :] = held[q] + lines[q] * value
        return carry

    lax.fori_loop(0, vector_ref.shape[0] // GROUP, body, 0)


def send_pieces(outs, flips, head, rounded, both, high_ref, low_ref):
    blocks = rounded.shape[0]
    mantissa, exponent = encode_rounded(rounded)
    head[...] = jnp.zeros_like(head)
    head[2 : 2 + blocks, :] = mantissa
    head[2 + blocks : 2 + 2 * blocks, :] = exponent
    mine = y_position()
    for at in range(0, len(flips), 2):
        pick = lambda ref: jnp.concatenate([ref[mine ^ flip] for flip in flips[at : at + 2]], axis=1)
        result = dot_three(both, (pick(high_ref), pick(low_ref)))
        for i, out in enumerate(outs[at : at + 2]):
            send_piece(out, head, result[:, i * 2 * HALF : (i + 1) * 2 * HALF])


def spread_grid(reach_x, reach_y, rounded, tables, outs, flips, wides, head, total, grids):
    for x in range(reach_x):
        parts = [
            grid[pl.ds(row, reach_y, stride=2), :]
            for row in pair_rows(x, reach_x, reach_y)
            for grid in grids
        ]
        total[x * reach_y : (x + 1) * reach_y, :] = sum(parts[1:], parts[0])
    half = reach_x * reach_y // 2
    both = jnp.concatenate([total[:half, :], total[half:, :]], axis=1)
    extra = wides[0].shape[0] - half
    if extra:
        both = jnp.concatenate([both, jnp.zeros((extra, 2 * REGION), F32)], axis=0)
    both = split(both)
    for wide, values in zip(wides, both):
        wide[...] = values
    send_pieces(outs, flips, head, rounded, both, *tables)


def start_kernel(reach_x, reach_y, flips, *refs):
    vector_ref, *remote = refs[:8]
    refs = refs[8:]
    outs, refs = refs[: len(flips)], refs[len(flips) :]
    wides, (weight_ref, sample_coeff_ref, places_out), refs = refs[:2], refs[2:5], refs[5:]
    rounded, high, low, stencil, flag, samples, dipoles = refs[:7]
    place_ref, sems, head, total = refs[7:11]
    grids = refs[11:]
    tiles = samples.shape[0]
    copies = []
    fetch = lambda source, target: copies.append(
        pltpu.make_async_copy(source, target, sems.at[len(copies)])
    )
    rounded_in, high_in, low_in, stencil_in, flag_in, sample_in, dipole_in = remote
    fetch(stencil_in, stencil)
    fetch(flag_in, flag)
    for tile in range(tiles):
        lanes = pl.ds(tile * BLOCK, BLOCK)
        fetch(sample_in.at[:, lanes], samples.at[tile])
        fetch(dipole_in.at[:, lanes], dipoles.at[tile])
    needed_first = len(copies)
    fetch(rounded_in, rounded)
    fetch(high_in, high)
    fetch(low_in, low)
    for copy in copies:
        copy.start()
    for grid in grids:
        grid[...] = jnp.zeros_like(grid)
    copies[0].wait()
    span_x, span_y = reach_x - 4, reach_y - 4
    local_x = stencil[0:1, :] - (lax.axis_index("wide") * span_x - 2)
    local_y = stencil[1:2, :] - (y_position() * span_y - 2)
    odd = local_x & 1
    places_out[0:1, :] = odd * (reach_x * reach_y) + (local_x >> 1) * (2 * reach_y) + 2 * local_y
    places_out[1:2, :] = stencil[2:3, :]
    to_scalar = pltpu.make_async_copy(places_out, place_ref, sems.at[len(copies)])
    to_scalar.start()
    for copy in copies[1:needed_first]:
        copy.wait()
    each = lambda values: [values.at[tile] for tile in range(tiles)]
    weave(flag[...], each(samples), each(dipoles), weight_ref, sample_coeff_ref)
    to_scalar.wait()
    add_panels(reach_y, True, vector_ref, place_ref, weight_ref, grids)
    for copy in copies[needed_first:]:
        copy.wait()
    spread_grid(
        reach_x, reach_y, rounded[...], (high, low), outs, flips, wides, head, total, grids
    )


def spread_kernel(reach_x, reach_y, flips, *refs):
    vector_ref, place_ref, rounded_ref, high_ref, low_ref, line_ref = refs[:6]
    refs = refs[6:]
    outs, wides, (head, total), grids = (
        refs[: len(flips)],
        refs[len(flips) : len(flips) + 2],
        refs[len(flips) + 2 : len(flips) + 4],
        refs[len(flips) + 4 :],
    )
    for grid in grids:
        grid[...] = jnp.zeros_like(grid)
    add_panels(reach_y, False, vector_ref, place_ref, line_ref, grids)
    spread_grid(
        reach_x,
        reach_y,
        rounded_ref[...],
        (high_ref, low_ref),
        outs,
        flips,
        wides,
        head,
        total,
        grids,
    )


def spread(vector, table, placed, raw, reach_x, reach_y, flips):
    count = vector.shape[0]
    half = reach_x * reach_y // 2
    blocks = count // BLOCK
    top = up_to(2 + 2 * blocks, 16)
    lanes = 2 * HALF
    body = up_to(half, 16)
    woven = (count // GROUP * 16, BLOCK)
    out_shapes = [jax.ShapeDtypeStruct((top + body, lanes), jnp.int16)] * len(flips)
    out_shapes += [jax.ShapeDtypeStruct((body, 2 * REGION), BF16)] * 2
    rounded = vector.reshape(blocks, BLOCK)
    work = [
        pltpu.VMEM((top, lanes), F32),
        pltpu.VMEM((reach_x * reach_y, REGION), F32),
    ] + [pltpu.VMEM((pair_count(reach_x, reach_y), REGION), F32)] * CHAINS
    if placed is None:
        stencil, flag, sample, dipole = raw
        operands = [vector, rounded, *table, stencil, flag.reshape(1, -1), sample, dipole]
        pinned = [pltpu.with_memory_space_constraint(value, pltpu.HBM) for value in operands[1:]]
        operands = [vector] + pinned
        in_specs = [in_smem()] + [pl.BlockSpec(memory_space=pltpu.HBM)] * 7
        out_shapes += [jax.ShapeDtypeStruct(woven, F32)] * 2
        out_shapes += [jax.ShapeDtypeStruct((2, count), jnp.int32)]
        tiled = pltpu.VMEM((blocks, 64, BLOCK), F32)
        work = [
            pltpu.VMEM(rounded.shape, F32),
            pltpu.VMEM(table[0].shape, BF16),
            pltpu.VMEM(table[1].shape, BF16),
            pltpu.VMEM(stencil.shape, jnp.int32),
            pltpu.VMEM((1, count), jnp.int32),
            tiled,
            tiled,
            pltpu.SMEM((2, count), jnp.int32),
            pltpu.SemaphoreType.DMA((6 + 2 * blocks,)),
        ] + work
    else:
        operands = [vector, placed[0], rounded, *table, placed[1]]
        in_specs = [in_smem()] * 2 + [whole_vmem()] * 4
    return pl.pallas_call(
        functools.partial(
            start_kernel if placed is None else spread_kernel, reach_x, reach_y, flips
        ),
        in_specs=in_specs,
        out_specs=[whole_vmem()] * len(out_shapes),
        out_shape=out_shapes,
        scratch_shapes=work,
        compiler_params=pltpu.CompilerParams(
            vmem_limit_bytes=START_LIMIT if placed is None else VMEM_LIMIT
        ),
        cost_estimate=cost(2 * half * 256 * 512, 4 * 16 * count * REGION),
        name="start" if placed is None else "spread",
    )(*operands)


def spread_rest_kernel(flips, rounded_ref, wide_high, wide_low, high_ref, low_ref, *refs):
    outs, head = refs[:-1], refs[-1]
    both = (wide_high[...], wide_low[...])
    send_pieces(outs, flips, head, rounded_ref[...], both, high_ref, low_ref)


def spread_rest(vector, both, table, flips):
    blocks = vector.shape[0] // BLOCK
    top = up_to(2 + 2 * blocks, 16)
    shape = (top + both[0].shape[0], 2 * HALF)
    return pl.pallas_call(
        functools.partial(spread_rest_kernel, flips),
        in_specs=[whole_vmem()] * 5,
        out_specs=[whole_vmem()] * len(flips),
        out_shape=[jax.ShapeDtypeStruct(shape, jnp.int16)] * len(flips),
        scratch_shapes=[pltpu.VMEM((top, 2 * HALF), F32)],
        compiler_params=params(),
        cost_estimate=cost(2 * shape[0] * 256 * 256 * 3, 4 * shape[0] * 512),
        name="spread_rest",
    )(vector.reshape(blocks, BLOCK), *both, *table)


def lines_kernel(place_ref, coeff_ref, *refs):
    out_ref = refs[-1]
    lanes = lax.broadcasted_iota(jnp.int32, (8, REGION), 1)

    def body(group, carry):
        at = pl.multiple_of(group * 16, 16)
        coeff = [coeff_ref[pl.ds(at + 8 * q, 8), :] for q in range(2)]
        for local in range(GROUP):
            panel = group * GROUP + local
            depth = place_ref[1, panel]
            shift = (depth - 4 * local) & (REGION - 1)
            inside = in_window(lanes, depth)
            for q in range(2):
                first = pl.multiple_of(panel * 16 + 8 * q, 8)
                out_ref[pl.ds(first, 8), :] = jnp.where(inside, pltpu.roll(coeff[q], shift, 1), 0.0)
        return carry

    lax.fori_loop(0, place_ref.shape[1] // GROUP, body, 0)


def place_lines(places, coeff, awaited):
    count = places.shape[1]
    shape = (count * 16, REGION)
    return pl.pallas_call(
        lines_kernel,
        in_specs=[in_smem(), whole_vmem()] + [anywhere()] * len(awaited),
        out_specs=whole_vmem(),
        out_shape=jax.ShapeDtypeStruct(shape, F32),
        compiler_params=params(),
        cost_estimate=cost(16 * count * REGION, 4 * 16 * count * REGION),
        name="place_lines",
    )(places, coeff, *awaited)


def stack_pieces(parts, reach_x, reach_y, top, opened, stacked):
    half = reach_x // 2
    pitch = up_to(reach_y, 8)
    tall = len(parts) * pitch
    core = lax.axis_index("pair")
    for bit, part in enumerate(parts):
        first = from_short(part[:top, :])
        opened[...] = from_short(part[top:, :]) * unit(first[0:1], first[1:2])
        place = (core ^ bit) * pitch
        for i in range(half):
            stacked[pl.ds(pl.multiple_of(i * tall + place, 8), reach_y), :] = opened[
                i * reach_y : (i + 1) * reach_y, :
            ]


def transform_pieces(table, stacked, before, spectrum):
    half = spectrum.shape[0]
    tall = stacked.shape[0] // half

    def tripled(values):
        high, low = split(values)
        return jnp.concatenate([high, low, high], axis=0)

    for i in range(0, half, 2):
        places = range(i, min(i + 2, half))
        held = jnp.concatenate([stacked[j * tall : (j + 1) * tall, :] for j in places], axis=1)
        result = dot(table, tripled(held))
        for j in places:
            made = result[:, (j - i) * 2 * HALF : (j - i + 1) * 2 * HALF]
            spectrum[j] = made if before is None else before[j] + made


def forward_early_kernel(reach_x, reach_y, pair, *refs):
    parts = refs[:pair]
    table_ref, spectrum, opened, stacked = refs[pair:]
    top = parts[0].shape[0] - opened.shape[0]
    stacked[...] = jnp.zeros_like(stacked)
    stack_pieces(parts, reach_x, reach_y, top, opened, stacked)
    transform_pieces(table_ref[lax.axis_index("narrow")], stacked, None, spectrum)


def stacking_scratch(pair, reach_x, reach_y):
    half = reach_x // 2
    return [
        pltpu.VMEM((up_to(half * reach_y, 16), 2 * HALF), F32),
        pltpu.VMEM((half * pair * up_to(reach_y, 8), 2 * HALF), F32),
    ]


def forward_early(parts, table, reach_x, reach_y):
    half = reach_x // 2
    pair = len(parts)
    return pl.pallas_call(
        functools.partial(forward_early_kernel, reach_x, reach_y, pair),
        in_specs=[whole_vmem()] * (pair + 1),
        out_specs=whole_vmem(),
        out_shape=jax.ShapeDtypeStruct((half, GRID, 2 * HALF), F32),
        scratch_shapes=stacking_scratch(pair, reach_x, reach_y),
        compiler_params=params(),
        cost_estimate=cost(2 * half * 256 * 256 * 128, 4 * half * GRID * 2 * HALF * 2),
        name="forward_early",
    )(*parts, table)


def forward_kernel(reach_x, reach_y, blocks, pieces, awaited, *refs):
    parts = refs[:pieces]
    early_ref, table_ref, modes_ref = refs[pieces : pieces + 3]
    refs = refs[: pieces + 3] + refs[pieces + 3 + awaited :]
    spectrum, even_out, layers_out, odd_out, own_out, peers_out, inner_out, *refs = refs[pieces + 3 :]
    opened, stacked, slabs, head = refs
    half = reach_x // 2
    pair = lax.axis_size("pair")
    top = parts[0].shape[0] - opened.shape[0]
    stacked[...] = jnp.zeros_like(stacked)
    head[...] = jnp.zeros_like(head)
    for piece in range(pieces):
        first = from_short(parts[piece][:top, :])
        mantissa, exponent = first[2 : 2 + blocks], first[2 + blocks : 2 + 2 * blocks]
        peers_out[piece * blocks : (piece + 1) * blocks, :] = decode_rounded(mantissa, exponent)
        at = 6 + 2 * piece * blocks
        head[at : at + blocks, :] = mantissa
        head[at + blocks : at + 2 * blocks, :] = exponent
    before = early_ref
    for chip in range(1, pieces // pair):
        stack_pieces(parts[chip * pair : (chip + 1) * pair], reach_x, reach_y, top, opened, stacked)
        transform_pieces(table_ref[lax.axis_index("narrow") ^ chip], stacked, before, spectrum)
        before = spectrum

    chunk = 32

    def body(index, largest):
        rows = pl.ds(pl.multiple_of(index * chunk, chunk), chunk)
        low = low_lanes(chunk)
        decay = modes_ref[0, rows, :]
        log_decay = modes_ref[1, rows, :]
        across_half = jnp.exp(half * log_decay)
        across_cut = jnp.exp((half - 4) * log_decay)
        layers = [spectrum[i, rows, :] for i in range(half)]
        run = layers[0]
        cut_right = run
        for i in range(1, half):
            run = decay * run + layers[i]
            if i == half - 5:
                cut_right = run
        right = run
        run = layers[half - 1]
        cut_left = run
        for i in range(half - 2, -1, -1):
            run = decay * run + layers[i]
            if i == 4:
                cut_left = run
        left = run
        inner_out[rows, :] = jnp.where(low, right, left)
        swapped_right, swapped_left = swap(right), swap(left)
        own = jnp.where(low, left + across_half * swapped_left, right + across_half * swapped_right)
        made = [
            jnp.where(low, swap(layers[half - 4]), layers[half - 3]),
            jnp.where(low, swap(layers[half - 2]), layers[half - 1]),
            jnp.where(low, own, cut_right + across_cut * swapped_right),
            jnp.where(low, layers[0], swap(layers[1])),
            jnp.where(low, layers[2], swap(layers[3])),
            jnp.where(low, cut_left + across_cut * swapped_left, own),
            own,
        ]
        own_out[rows, :] = own
        for slab, values in enumerate(made):
            slabs[slab, rows, :] = values
        return tuple(
            jnp.maximum(old, jnp.max(jnp.abs(values).reshape(chunk // 8, 8, 2 * HALF), axis=0))
            for old, values in zip(largest, made)
        )

    zero = jnp.zeros((8, 2 * HALF), F32)
    largest = lax.fori_loop(0, GRID // chunk, body, (zero,) * 7)
    scales = [fit_scale(jnp.max(value, axis=0, keepdims=True)) for value in largest]
    head_rows = head.shape[0]

    def send(out, top, which):
        for place, slab in enumerate(which):
            exponent, fraction = scales[slab]
            head[2 * place : 2 * place + 1, :] = exponent
            head[2 * place + 1 : 2 * place + 2, :] = fraction
            at = top + place * GRID
            out[at : at + GRID, :] = quantize(slabs[slab], exponent, fraction)
        out[:top, :] = to_short(head[:top, :])

    on_left = lax.axis_index("wide") & 1
    for side, (even, odd) in enumerate(((0, 3), (3, 0))):

        @pl.when(on_left == side)
        def _():
            send(even_out, head_rows, (even + 2, 6))
            send(layers_out, 16, (even, even + 1))
            send(odd_out, head_rows, (odd + 2, odd, odd + 1))


def forward(parts, early, table, modes, reach_x, reach_y, blocks, awaited):
    pieces = len(parts)
    half = reach_x // 2
    lanes = 2 * HALF
    head = up_to(6 + 2 * pieces * blocks, 16)
    short = lambda rows: jax.ShapeDtypeStruct((rows, lanes), jnp.int16)
    return pl.pallas_call(
        functools.partial(
            forward_kernel, reach_x, reach_y, blocks, pieces, len(awaited)
        ),
        in_specs=[whole_vmem()] * (pieces + 3) + [anywhere()] * len(awaited),
        out_specs=[whole_vmem()] * 7,
        out_shape=[
            jax.ShapeDtypeStruct((half, GRID, lanes), F32),
            short(head + 2 * GRID),
            short(16 + 2 * GRID),
            short(head + 3 * GRID),
            jax.ShapeDtypeStruct((GRID, lanes), F32),
            jax.ShapeDtypeStruct((pieces * blocks, BLOCK), F32),
            jax.ShapeDtypeStruct((GRID, lanes), F32),
        ],
        scratch_shapes=stacking_scratch(pieces // table.shape[0], reach_x, reach_y)
        + [
            pltpu.VMEM((7, GRID, lanes), F32),
            pltpu.VMEM((head, lanes), F32),
        ],
        compiler_params=params(),
        cost_estimate=cost(2 * half * 256 * 256 * 128, 4 * half * GRID * lanes * 2),
        name="forward",
    )(*parts, early, table, modes, *awaited)


def opened_slabs(ref, count, head_rows):
    first = from_short(ref[:16, :])
    for slab in range(count):
        scale = unit(first[2 * slab : 2 * slab + 1], first[2 * slab + 1 : 2 * slab + 2])
        at = head_rows + slab * GRID
        yield from_short(ref[at : at + GRID, :]) * scale


def pair_kernel(reach_x, flips, own_ref, even_ref, modes_ref, *refs):
    outs, head = refs[:-1], refs[-1]
    span = reach_x - 4
    here = lax.axis_index("wide")
    low = low_lanes(GRID)
    log_decay = modes_ref[1]
    own = own_ref[...]
    _, partner = opened_slabs(even_ref, 2, even_ref.shape[0] - 2 * GRID)

    def weight(distances):
        powers = []
        for distance in distances:
            ahead = span * distance - reach_x
            powers.append(jnp.where(distance >= 2, ahead, ahead + GRID).astype(F32))
        return jnp.exp(jnp.where(low, *powers) * log_decay)

    head[...] = jnp.zeros_like(head)
    for flip, out in zip(flips, outs):
        behind = (here ^ flip) - here
        message = own * weight((-behind, behind))
        behind = (here ^ flip) - (here ^ 1)
        beside = jnp.where(jnp.abs(behind) == 1, 0.0, 1.0)
        send_piece(out, head, message + partner * (weight((-behind, behind)) * beside))


def pair_messages(own, from_even, modes, reach_x, flips):
    return pl.pallas_call(
        functools.partial(pair_kernel, reach_x, flips),
        in_specs=[whole_vmem()] * 3,
        out_specs=[whole_vmem()] * len(flips),
        out_shape=[jax.ShapeDtypeStruct((16 + GRID, 2 * HALF), jnp.int16)] * len(flips),
        scratch_shapes=[pltpu.VMEM((16, 2 * HALF), F32)],
        compiler_params=params(),
        cost_estimate=cost(16 * GRID * 2 * HALF, 4 * GRID * 2 * HALF * (6 + len(flips))),
        name="pair_messages",
    )(own, from_even, modes)


def send_fields(outs, flips, reach_y, field_high, field_low, high_ref, low_ref, ready, head):
    half = field_high.shape[0]
    mine = y_position()
    pitch = up_to(reach_y, 16)
    pick = lambda ref: jnp.concatenate([ref[mine ^ flip] for flip in flips], axis=0)
    table = (pick(high_ref), pick(low_ref))
    for i in range(0, half, 2):
        many = min(2, half - i)
        join = lambda ref: jnp.concatenate([ref[i + j] for j in range(many)], axis=1)
        result = dot_three(table, (join(field_high), join(field_low)))
        for j in range(many):
            for piece in range(len(flips)):
                ready[piece, (i + j) * reach_y : (i + j + 1) * reach_y, :] = result[
                    piece * pitch : piece * pitch + reach_y, j * 2 * HALF : (j + 1) * 2 * HALF
                ]
    head[...] = jnp.zeros_like(head)
    for piece, out in enumerate(outs):
        if ready.shape[1] > half * reach_y:
            ready[piece, half * reach_y :, :] = jnp.zeros_like(ready[piece, half * reach_y :, :])
        send_piece(out, head, ready[piece])


def inverse_kernel(reach_x, reach_y, flips, fars, *refs):
    spectrum, from_even, even_layers, from_odd, own_ref, inner_ref, *far_refs = refs[: 6 + fars]
    refs = refs[6 + fars :]
    high_ref, low_ref, modes_ref = refs[:3]
    outs = refs[3 : 3 + len(flips)]
    field_high, field_low, ready, head = refs[3 + len(flips) :]
    half = reach_x // 2
    span = reach_x - 4
    chunk = 32
    head_rows = from_even.shape[0] - 2 * GRID
    on_left = (lax.axis_index("wide") & 1) == 1
    even_places = (from_even, head_rows, 0), (even_layers, 16, 0), (even_layers, 16, 1)
    odd_places = tuple((from_odd, head_rows, place) for place in range(3))

    def slab_unit(place):
        ref, _, at = place
        first = from_short(ref[:16, :])
        return unit(first[2 * at : 2 * at + 1], first[2 * at + 1 : 2 * at + 2])

    both_units = [[slab_unit(place) for place in places] for places in (even_places, odd_places)]

    def sided(even, odd):
        return jnp.where(on_left, even, odd), jnp.where(on_left, odd, even)

    far_units = []
    for ref in far_refs:
        first = from_short(ref[:16, :])
        far_units.append(unit(first[0:1], first[1:2]))

    def body(index, carry):
        first = pl.multiple_of(index * chunk, chunk)
        rows = pl.ds(first, chunk)
        low = low_lanes(chunk)
        decay = modes_ref[0, rows, :]
        log_decay = modes_ref[1, rows, :]
        ring = modes_ref[2, rows, :]
        gain = modes_ref[3, rows, :]
        across_half = jnp.exp(half * log_decay)
        across_cut = jnp.exp((half - 4) * log_decay)
        around = jnp.exp((GRID - 4) * log_decay)
        beside = jnp.exp((GRID - reach_x - span) * log_decay)
        layers = [spectrum[i, rows, :] for i in range(half)]

        def slab(which):
            found = []
            for places, units in zip((even_places, odd_places), both_units):
                ref, top, place = places[which]
                at = pl.multiple_of(top + place * GRID + index * chunk, 16)
                found.append(from_short(ref[pl.ds(at, chunk), :]) * units[which])
            return sided(*found)

        left_moments, right_moments = slab(0)
        head_layers, tail_layers = zip(slab(1), slab(2))
        zero = jnp.zeros_like(decay)
        from_head = [head_layers[0], swap(head_layers[0]), head_layers[1], swap(head_layers[1])]
        from_tail = [swap(tail_layers[0]), tail_layers[0], swap(tail_layers[1]), tail_layers[1]]
        head_sum = from_head[0]
        for i in range(1, 4):
            head_sum = decay * head_sum + from_head[i]
        tail_sum = from_tail[3]
        for i in range(2, -1, -1):
            tail_sum = decay * tail_sum + from_tail[i]
        for i in range(4):
            layers[i] = layers[i] + jnp.where(low, from_head[i], zero)
        for i in range(4):
            place = half - 4 + i
            layers[place] = layers[place] + jnp.where(low, zero, from_tail[i])
        total = own_ref[rows, :] * jnp.exp((GRID - reach_x) * log_decay)
        at = pl.ds(pl.multiple_of(16 + index * chunk, 16), chunk)
        for ref, scale in zip(far_refs, far_units):
            total = total + from_short(ref[at, :]) * scale
        one = jnp.ones_like(decay)
        total = total + left_moments * jnp.where(low, beside, one)
        total = total + right_moments * jnp.where(low, one, beside)
        shared = jnp.where(low, head_sum, tail_sum)
        entering = (swap(total) + around * shared) * ring
        leaving = swap(across_half * entering + across_cut * shared + inner_ref[rows, :])
        run = jnp.where(low, entering, leaving)
        forward_runs = []
        for i in range(half):
            run = decay * run + layers[i]
            forward_runs.append(run)
        run = jnp.where(low, leaving, entering)
        for i in range(half - 1, -1, -1):
            ahead = decay * run
            high, rest = split(gain * (forward_runs[i] + ahead))
            field_high[i, rows, :] = high
            field_low[i, rows, :] = rest
            run = ahead + layers[i]
        return carry

    lax.fori_loop(0, GRID // chunk, body, 0)
    send_fields(outs, flips, reach_y, field_high, field_low, high_ref, low_ref, ready, head)


def inverse(
    spectrum,
    from_even,
    even_layers,
    from_odd,
    own,
    inner,
    fars,
    table,
    modes,
    reach_x,
    reach_y,
    flips,
):
    half = reach_x // 2
    lanes = 2 * HALF
    body = up_to(half * reach_y, 16)
    shapes = [jax.ShapeDtypeStruct((16 + body, lanes), jnp.int16)] * len(flips)
    shapes += [jax.ShapeDtypeStruct((half, GRID, lanes), BF16)] * 2
    return pl.pallas_call(
        functools.partial(inverse_kernel, reach_x, reach_y, flips, len(fars)),
        in_specs=[whole_vmem()] * (9 + len(fars)),
        out_specs=[whole_vmem()] * len(shapes),
        out_shape=shapes,
        scratch_shapes=[
            pltpu.VMEM((len(flips), body, lanes), F32),
            pltpu.VMEM((16, lanes), F32),
        ],
        compiler_params=params(),
        cost_estimate=cost(2 * half * 256 * 256 * 128, 4 * half * GRID * lanes * 2),
        name="inverse",
    )(spectrum, from_even, even_layers, from_odd, own, inner, *fars, *table, modes)


def inverse_rest_kernel(reach_y, flips, field_high, field_low, high_ref, low_ref, *refs):
    outs, (ready, head) = refs[: len(flips)], refs[len(flips) :]
    send_fields(outs, flips, reach_y, field_high, field_low, high_ref, low_ref, ready, head)


def inverse_rest(field, table, reach_y, flips):
    half = field[0].shape[0]
    lanes = 2 * HALF
    body = up_to(half * reach_y, 16)
    return pl.pallas_call(
        functools.partial(inverse_rest_kernel, reach_y, flips),
        in_specs=[whole_vmem()] * 4,
        out_specs=[whole_vmem()] * len(flips),
        out_shape=[jax.ShapeDtypeStruct((16 + body, lanes), jnp.int16)] * len(flips),
        scratch_shapes=[
            pltpu.VMEM((len(flips), body, lanes), F32),
            pltpu.VMEM((16, lanes), F32),
        ],
        compiler_params=params(),
        cost_estimate=cost(2 * half * 256 * 256 * 128, 4 * half * GRID * lanes * 2),
        name="inverse_rest",
    )(*field, *table)


def sum_rows(values):
    row = lax.broadcasted_iota(jnp.int32, values[0].shape, 0)
    for step in (4, 2, 1):
        low = (row & step) == 0
        paired = []
        for one, other in zip(values[: len(values) // 2], values[len(values) // 2 :]):
            kept = jnp.where(low, one, other)
            moved = jnp.where(low, other, one)
            if step == 4:
                moved = pltpu.roll(moved, 4, 0)
            else:
                moved = jnp.where(low, pltpu.roll(moved, 8 - step, 0), pltpu.roll(moved, step, 0))
            paired.append(kept + moved)
        values = paired
    return values[0]


def z_lines(parts, flips, high_ref, low_ref):
    mine = y_position()
    opened = []
    for part in parts:
        first = from_short(part[:16, :])
        opened.append(from_short(part[16:, :]) * unit(first[0:1], first[1:2]))
    values = split(jnp.concatenate(opened, axis=1))
    pick = lambda ref: jnp.concatenate([ref[mine ^ flip] for flip in flips], axis=0)
    return dot_three(values, (pick(high_ref), pick(low_ref)))


def sample_early_kernel(*refs):
    *parts, high_ref, low_ref, out_ref = refs
    out_ref[...] = z_lines(parts, range(len(parts)), high_ref, low_ref)


def sample_early(parts, table):
    rows = parts[0].shape[0] - 16
    return pl.pallas_call(
        sample_early_kernel,
        in_specs=[whole_vmem()] * (len(parts) + 2),
        out_specs=whole_vmem(),
        out_shape=jax.ShapeDtypeStruct((rows, 2 * REGION), F32),
        compiler_params=params(),
        cost_estimate=cost(2 * rows * 256 * 256 * 3, 4 * rows * 512),
        name="sample_early",
    )(*parts, *table)


def sample_kernel(last, reach_x, reach_y, flips, place_ref, *refs):
    parts = refs[: len(flips)]
    early_ref, high_ref, low_ref, line_ref, own_ref, vector_ref, near_ref, out_ref = refs[
        len(flips) : len(flips) + 8
    ]
    flat, field, sums = refs[len(flips) + 8 :]
    half_rows = reach_x * reach_y // 2
    both = early_ref[...] + z_lines(parts, flips, high_ref, low_ref)
    flat[:half_rows, :] = both[:half_rows, :REGION]
    flat[half_rows:, :] = both[:half_rows, REGION:]
    for x in range(reach_x):
        layer = flat[x * reach_y : (x + 1) * reach_y, :]
        for row in pair_rows(x, reach_x, reach_y):
            field[pl.ds(row, reach_y, stride=2), :] = layer
    count = place_ref.shape[1]

    def body(group, carry):
        for eight in range(0, GROUP, 8):
            totals = []
            for local in range(eight, eight + 8):
                panel = group * GROUP + local
                row = place_ref[0, panel]
                first = pl.multiple_of(panel * 16, 16)
                totals.append(
                    field[pl.ds(row, 8), :] * line_ref[pl.ds(first, 8), :]
                    + field[pl.ds(row + 2 * reach_y, 8), :] * line_ref[pl.ds(first + 8, 8), :]
                )
            sums[pl.ds(pl.multiple_of(group * GROUP + eight, 8), 8), :] = sum_rows(totals)
        return carry

    lax.fori_loop(0, count // GROUP, body, 0)
    sampled = lax.dot_general(
        jnp.ones((8, REGION), F32),
        sums[...],
        (((1,), (1,)), ((), ())),
        precision=lax.Precision.HIGHEST,
        preferred_element_type=F32,
    )
    for block in range(count // BLOCK):
        lane = slice(block * BLOCK, (block + 1) * BLOCK)
        row = slice(block, block + 1)
        vector = vector_ref[row, :]
        image = jnp.where(own_ref[row, :] == 1, 0.0, 0.5 * vector) + sampled[:1, lane]
        image = image + near_ref[row, :]
        if last:
            out_ref[0:1, lane] = vector
            out_ref[1:2, lane] = image
        else:
            out_ref[row, :] = image


def sample(last, places, parts, flips, early, table, lines, flag, vector, near, reach_x, reach_y):
    count = places.shape[1]
    blocks = count // BLOCK
    shape = (2, count) if last else (blocks, BLOCK)
    return pl.pallas_call(
        functools.partial(sample_kernel, last, reach_x, reach_y, flips),
        in_specs=[in_smem()] + [whole_vmem()] * (len(parts) + 7),
        out_specs=whole_vmem(),
        out_shape=jax.ShapeDtypeStruct(shape, F32),
        scratch_shapes=[
            pltpu.VMEM((reach_x * reach_y, REGION), F32),
            pltpu.VMEM((pair_count(reach_x, reach_y), REGION), F32),
            pltpu.VMEM((count, REGION), F32),
        ],
        compiler_params=params(),
        cost_estimate=cost(reach_x * reach_y * 256 * 512, 4 * 16 * count * REGION),
        name="sample",
    )(
        places,
        *parts,
        early,
        *table,
        lines,
        flag.reshape(blocks, BLOCK),
        vector.reshape(blocks, BLOCK),
        near,
    )


def near_kernel(slots, blocks, place_ref, target_ref, *refs):
    even_ref, odd_ref, peers_ref, tile_ref, out_ref, held = refs
    count = peers_ref.shape[0]
    held[count : 2 * count, :] = peers_ref[...]
    on_left = lax.axis_index("wide") & 1
    for side, ref in ((1 - on_left, even_ref), (on_left, odd_ref)):
        top = from_short(ref[...])
        for piece in range(count // blocks):
            at = 6 + 2 * piece * blocks
            held[pl.ds(side * (2 * count) + piece * blocks, blocks), :] = decode_rounded(
                top[at : at + blocks], top[at + blocks : at + 2 * blocks]
            )
    out_ref[...] = jnp.zeros_like(out_ref)
    for slot in range(slots):
        picked = held[pl.ds(place_ref[slot], 1), :]
        picked = jnp.broadcast_to(picked, (16, BLOCK)).astype(BF16)
        product = lax.dot_general(
            picked,
            tile_ref[slot],
            (((1,), (1,)), ((), ())),
            preferred_element_type=F32,
        )
        target = pl.ds(target_ref[slot], 1)
        out_ref[target, :] = out_ref[target, :] + product[:1]


def near_field(places, targets, from_even, from_odd, peers, tiles, blocks, out_rows):
    slots = tiles.shape[0]
    head = from_even.shape[0] - 2 * GRID
    constant = lambda shape: pl.BlockSpec(shape, lambda i: (0,) * len(shape))
    return pl.pallas_call(
        functools.partial(near_kernel, slots, blocks),
        grid=(1,),
        in_specs=[
            in_smem(),
            in_smem(),
            constant((head, BLOCK)),
            constant((head, BLOCK)),
            constant(peers.shape),
            constant(tiles.shape),
        ],
        out_specs=constant((out_rows, BLOCK)),
        out_shape=jax.ShapeDtypeStruct((out_rows, BLOCK), F32),
        scratch_shapes=[pltpu.VMEM((3 * peers.shape[0], BLOCK), F32)],
        compiler_params=params(),
        cost_estimate=cost(2 * slots * 16 * BLOCK * BLOCK, 2 * slots * BLOCK * BLOCK),
        name="near_field",
    )(places, targets, from_even, from_odd, peers, tiles)


def shards(
    density,
    surface_flag,
    stencil_base,
    sample_weights,
    dipole_weights,
    near_target,
    near_source,
    near_tiles,
):
    x_count = lax.axis_size("wide")
    y_count = lax.axis_size(Y_AXES)
    y_index = lax.axis_index(Y_AXES)
    pair = lax.axis_size("pair")
    span_x = REGION // x_count
    span_y = REGION // y_count
    reach_x = span_x + 4
    reach_y = span_y + 4
    count = density.shape[0]
    blocks = count // BLOCK

    z_forward, z_inverse, y_forward, y_inverse, modes = tables(y_count, pair, span_y)
    modes = lax.dynamic_index_in_dim(jnp.asarray(modes), y_index, 0, keepdims=False)

    neighbour = near_source // blocks
    flip = (y_index + neighbour % 3 - 1) ^ y_index
    sources = ((neighbour // 3) * y_count + flip) * blocks + near_source % blocks
    out_rows = up_to(blocks + 1, 8)
    live = near_target >= 0
    sources = jnp.where(live, sources, 0)
    targets = jnp.where(live, near_target, out_rows - 1)

    swaps = lambda pairs: [(i, j) for i, j in pairs] + [(j, i) for i, j in pairs]
    even_swap = swaps([(i, i + 1) for i in range(0, x_count - 1, 2)])
    odd_swap = swaps([(i, i + 1) for i in range(1, x_count - 1, 2)])
    far_flips = list(range(2, x_count, 2))

    local, moving = [0], list(range(1, y_count))

    def flipped(parts, flips):
        return [
            lax.ppermute(part, Y_AXES, [(i, i ^ flip) for i in range(y_count)])
            for flip, part in zip(flips, parts)
        ]

    def convolve_and_sample(last, vector, sent, both, places, sample_lines, awaited):
        arrived = flipped(sent, moving)
        arrived = list(spread_rest(vector, both, z_forward, local)) + arrived
        early = forward_early(arrived[:pair], y_forward, reach_x, reach_y)
        spectrum, even_message, layers, odd_message, own, peers, inner = forward(
            arrived, early, y_forward, modes, reach_x, reach_y, blocks, awaited
        )
        from_even = lax.ppermute(even_message, "wide", even_swap)
        from_odd = lax.ppermute(odd_message, "wide", odd_swap)
        even_layers = lax.ppermute(layers, "wide", even_swap)
        fars = [
            lax.ppermute(message, "wide", [(i, i ^ flip) for i in range(x_count)])
            for flip, message in zip(
                far_flips, pair_messages(own, from_even, modes, reach_x, far_flips)
            )
        ]
        near_part = near_field(
            sources, targets, from_even, from_odd, peers, near_tiles, blocks, out_rows
        )
        *sent, high, low = inverse(
            spectrum,
            from_even,
            even_layers,
            from_odd,
            own,
            inner,
            fars,
            y_inverse,
            modes,
            reach_x,
            reach_y,
            moving,
        )
        arrived = flipped(sent, moving)
        arrived = list(inverse_rest((high, low), y_inverse, reach_y, local)) + arrived
        image = sample(
            last,
            places,
            arrived[pair:],
            list(range(pair, y_count)),
            sample_early(arrived[:pair], z_inverse),
            z_inverse,
            sample_lines,
            surface_flag,
            vector,
            near_part,
            reach_x,
            reach_y,
        )
        return image, near_part

    raw = (stencil_base, surface_flag, sample_weights, dipole_weights)
    *sent, high, low, source_coeff, sample_coeff, places = spread(
        density, z_forward, None, raw, reach_x, reach_y, moving
    )
    sample_lines = place_lines(places, sample_coeff, [])
    first_image, near_part = convolve_and_sample(
        False, density, sent, (high, low), places, sample_lines, [sample_lines]
    )
    first_image = first_image.reshape(-1)
    source_lines = place_lines(places, source_coeff, [near_part])
    *sent, high, low = spread(
        first_image, z_forward, (places, source_lines), None, reach_x, reach_y, moving
    )
    both_images, _ = convolve_and_sample(
        True, first_image, sent, (high, low), places, sample_lines, []
    )
    return both_images


def solution(mesh):
    panels = P(("groups",) + ALL_AXES)
    columns = P(None, ("groups",) + ALL_AXES)
    in_specs = (
        panels,
        panels,
        columns,
        columns,
        columns,
        panels,
        panels,
        P(("groups",) + ALL_AXES, None, None),
    )
    return jax.shard_map(
        shards, mesh=mesh, in_specs=in_specs, out_specs=columns, check_vma=False
    )
```

```python
import functools
import math

import jax
import jax.numpy as jnp
import numpy as np
from jax import lax
from jax.experimental import pallas as pl
from jax.experimental.pallas import tpu as pltpu
from jax.sharding import PartitionSpec as P

GRID = 256
REGION = 128
BLOCK = 128
HALF = 64
KERNEL_GAIN = 4.0
SCREEN = 1.0 / 1024.0
LN2 = math.log(2.0)
Y_AXES = ("narrow", "pair")
ALL_AXES = ("wide", "narrow", "pair")
F32 = jnp.float32
BF16 = jnp.bfloat16
VMEM_LIMIT = 24 * 1024 * 1024
START_LIMIT = VMEM_LIMIT
EARLY_FLOPS = 5 * 10**9
GROUP = 32
CHAINS = 2


def cas(angles):
    return np.cos(angles) + np.sin(angles)


def up_to(count, multiple):
    return -(-count // multiple) * multiple


def low_lanes(rows):
    return lax.broadcasted_iota(jnp.int32, (rows, 2 * HALF), 1) < HALF


def swap(values):
    return pltpu.roll(values, HALF, 1)


def split(values):
    high = values.astype(BF16)
    return high, (values - high.astype(F32)).astype(BF16)


def dot(left, right):
    return jnp.dot(left, right, preferred_element_type=F32)


def dot_three(left, right):
    return dot(left[0], right[0]) + (dot(left[0], right[1]) + dot(left[1], right[0]))


def params():
    return pltpu.CompilerParams(vmem_limit_bytes=VMEM_LIMIT)


def whole_vmem():
    return pl.BlockSpec(memory_space=pltpu.VMEM)


def anywhere():
    return pl.BlockSpec(memory_space=pl.ANY)


def in_smem():
    return pl.BlockSpec(memory_space=pltpu.SMEM)


def cost(flops, moved):
    return pl.CostEstimate(flops=flops, bytes_accessed=moved, transcendentals=0)


def full_scale(exponent, fraction):
    return fraction * jnp.exp(exponent * LN2) * (1.0 / 1024.0)


def fit_scale(largest):
    largest = jnp.maximum(largest, 1e-30)
    exponent = jnp.floor(jnp.log(largest) * (1.0 / LN2))
    fraction = jnp.ceil(largest * jnp.exp(-exponent * LN2) * 1024.0) + 1.0
    return exponent, fraction


def to_short(values):
    return values.astype(jnp.int32).astype(jnp.int16)


def from_short(values):
    return values.astype(jnp.int32).astype(F32)


def quantize(values, exponent, fraction):
    return to_short(jnp.round(values * (32767.0 / full_scale(exponent, fraction))))


def unit(exponent, fraction):
    return full_scale(exponent, fraction) * (1.0 / 32767.0)


def encode_rounded(values):
    rounded = values.astype(BF16).astype(F32)
    size = jnp.maximum(jnp.abs(rounded), 1e-30)
    exponent = jnp.floor(jnp.log(size) * (1.0 / LN2))
    return jnp.round(rounded * jnp.exp((10.0 - exponent) * LN2)), exponent


def decode_rounded(mantissa, exponent):
    return (mantissa * jnp.exp((exponent - 10.0) * LN2)).astype(BF16).astype(F32)


def send_piece(out, head, values):
    exponent, fraction = fit_scale(jnp.max(jnp.abs(values), axis=0, keepdims=True))
    head[0:1, :] = exponent
    head[1:2, :] = fraction
    top = head.shape[0]
    out[:top, :] = to_short(head[...])
    out[top:, :] = quantize(values, exponent, fraction)


def y_position():
    return lax.axis_index("narrow") * lax.axis_size("pair") + lax.axis_index("pair")


def halves(table):
    high = table.astype(jnp.bfloat16)
    return high, (table - high.astype(np.float64)).astype(jnp.bfloat16)


def tables(y_count, pair, span_y):
    depth = GRID // y_count
    reach = span_y + 4
    waves = np.arange(GRID)
    step = 2.0 * np.pi / GRID
    z_table = cas(step * np.outer(np.arange(REGION), waves))
    z_forward = np.zeros((y_count, 2 * REGION, 2 * HALF))
    z_inverse = np.zeros((y_count, 2 * HALF, 2 * REGION))
    symbols = 4.0 * np.sin(np.pi * waves / GRID) ** 2
    shift = np.full((y_count, GRID, 2 * HALF), 1.0)
    y_forward = np.zeros((GRID, y_count, up_to(reach, 8)))
    y_inverse = np.zeros((y_count, up_to(reach, 16), GRID))
    for block in range(y_count):
        mine = z_table[:, block * depth : (block + 1) * depth]
        for half in range(2):
            rows = slice(half * REGION, (half + 1) * REGION)
            lanes = slice(half * HALF, half * HALF + depth)
            z_forward[block, rows, lanes] = mine
            z_inverse[block, lanes, rows] = mine.T / GRID
            shift[block, :, lanes] = (
                SCREEN + symbols[:, None] + symbols[None, block * depth : (block + 1) * depth]
            )
        cells = block * span_y - 2 + np.arange(reach)
        y_table = cas(step * np.outer(waves, cells))
        y_forward[:, block, :reach] = y_table
        y_inverse[block, :reach] = y_table.T / GRID
    y_forward = y_forward.reshape(GRID, y_count // pair, pair, -1).transpose(2, 0, 1, 3)
    y_forward = halves(y_forward.reshape(pair, GRID, -1))
    y_forward = np.concatenate([y_forward[0], y_forward[0], y_forward[1]], axis=2)
    root = np.sqrt(shift * (shift + 4.0))
    decay = 2.0 / (2.0 + shift + root)
    log_decay = np.log(decay)
    ring = 1.0 / (1.0 - np.exp(GRID * log_decay))
    gain = KERNEL_GAIN / root
    modes = np.stack([decay, log_decay, ring, gain], axis=1).astype(np.float32)
    return (
        halves(z_forward),
        halves(z_inverse),
        y_forward,
        halves(y_inverse),
        modes,
    )


def weave(flag, sample_refs, dipole_refs, source_out, sample_out):
    place = lax.broadcasted_iota(jnp.int32, (4 * BLOCK, 4 * BLOCK), 0)
    lane = lax.broadcasted_iota(jnp.int32, (4 * BLOCK, 4 * BLOCK), 1)
    wanted = 4 * (place % BLOCK) + place // BLOCK
    mixing = jnp.where(lane == wanted, 1.0, 0.0).astype(BF16)
    stacked = []
    for tile, (sample_ref, dipole_ref) in enumerate(zip(sample_refs, dipole_refs)):
        charged = flag[:, tile * BLOCK : (tile + 1) * BLOCK] == 1
        rows = []
        for depth in range(4):
            sample = sample_ref[pl.ds(depth, 16, stride=4), :]
            dipole = dipole_ref[pl.ds(depth, 16, stride=4), :]
            rows.append(jnp.concatenate([jnp.where(charged, -sample, dipole), sample], axis=0))
        stacked.append(jnp.concatenate(rows, axis=1))
    weights = jnp.concatenate(stacked, axis=0)
    first, rest = split(weights)
    second, third = split(weights - first.astype(F32))
    woven = dot(first, mixing) + (dot(second, mixing) + dot(third, mixing))
    for tile in range(len(sample_refs)):
        for which, out in enumerate((source_out, sample_out)):
            for part in range(BLOCK // GROUP):
                at = (tile * (BLOCK // GROUP) + part) * 16
                lanes = slice(part * BLOCK, (part + 1) * BLOCK)
                for a in range(4):
                    row = tile * 32 + which * 16 + 4 * a
                    out[pl.ds(at + 8 * (a // 2) + a % 2, 4, stride=2), :] = woven[
                        row : row + 4, lanes
                    ]


def pair_rows(x, reach_x, reach_y):
    even = (x // 2) * 2 * reach_y + x % 2
    if x == 0 or x == reach_x - 1:
        return [even]
    return [even, reach_x * reach_y + ((x - 1) // 2) * 2 * reach_y + (x - 1) % 2]


def pair_count(reach_x, reach_y):
    return (2 * reach_x - 2) * reach_y


def in_window(lanes, depth):
    return ((lanes - depth) & -4) == 0


def add_panels(reach, woven, vector_ref, place_ref, weight_ref, grids):
    lanes = lax.broadcasted_iota(jnp.int32, (8, REGION), 1)

    def body(group, carry):
        at = pl.multiple_of(group * 16, 16)
        coeff = [weight_ref[pl.ds(at + 8 * q, 8), :] for q in range(2)] if woven else None
        for local in range(GROUP):
            panel = group * GROUP + local
            grid = grids[local % len(grids)]
            row = place_ref[0, panel]
            value = vector_ref[panel]
            if woven:
                depth = place_ref[1, panel]
                shift = (depth - 4 * local) & (REGION - 1)
                value = jnp.where(in_window(lanes, depth), value, 0.0)
                lines = [pltpu.roll(coeff[q], shift, 1) for q in range(2)]
            else:
                first = pl.multiple_of(panel * 16, 16)
                lines = [weight_ref[pl.ds(first + 8 * q, 8), :] for q in range(2)]
            places = [pl.ds(row, 8), pl.ds(row + 2 * reach, 8)]
            held = [grid[place, :] for place in places]
            for q in range(2):
                grid[places[q], :] = held[q] + lines[q] * value
        return carry

    lax.fori_loop(0, vector_ref.shape[0] // GROUP, body, 0)


def send_pieces(outs, flips, head, rounded, both, high_ref, low_ref):
    blocks = rounded.shape[0]
    mantissa, exponent = encode_rounded(rounded)
    head[...] = jnp.zeros_like(head)
    head[2 : 2 + blocks, :] = mantissa
    head[2 + blocks : 2 + 2 * blocks, :] = exponent
    mine = y_position()
    for at in range(0, len(flips), 2):
        pick = lambda ref: jnp.concatenate([ref[mine ^ flip] for flip in flips[at : at + 2]], axis=1)
        result = dot_three(both, (pick(high_ref), pick(low_ref)))
        for i, out in enumerate(outs[at : at + 2]):
            send_piece(out, head, result[:, i * 2 * HALF : (i + 1) * 2 * HALF])


def spread_grid(reach_x, reach_y, rounded, tables, outs, flips, wides, head, total, grids):
    for x in range(reach_x):
        parts = [
            grid[pl.ds(row, reach_y, stride=2), :]
            for row in pair_rows(x, reach_x, reach_y)
            for grid in grids
        ]
        total[x * reach_y : (x + 1) * reach_y, :] = sum(parts[1:], parts[0])
    half = reach_x * reach_y // 2
    both = jnp.concatenate([total[:half, :], total[half:, :]], axis=1)
    extra = wides[0].shape[0] - half
    if extra:
        both = jnp.concatenate([both, jnp.zeros((extra, 2 * REGION), F32)], axis=0)
    both = split(both)
    for wide, values in zip(wides, both):
        wide[...] = values
    send_pieces(outs, flips, head, rounded, both, *tables)


def start_kernel(reach_x, reach_y, flips, *refs):
    vector_ref, *remote = refs[:8]
    refs = refs[8:]
    outs, refs = refs[: len(flips)], refs[len(flips) :]
    wides, (weight_ref, sample_coeff_ref, places_out), refs = refs[:2], refs[2:5], refs[5:]
    rounded, high, low, stencil, flag, samples, dipoles = refs[:7]
    place_ref, sems, head, total = refs[7:11]
    grids = refs[11:]
    tiles = samples.shape[0]
    copies = []
    fetch = lambda source, target: copies.append(
        pltpu.make_async_copy(source, target, sems.at[len(copies)])
    )
    rounded_in, high_in, low_in, stencil_in, flag_in, sample_in, dipole_in = remote
    fetch(stencil_in, stencil)
    fetch(flag_in, flag)
    for tile in range(tiles):
        lanes = pl.ds(tile * BLOCK, BLOCK)
        fetch(sample_in.at[:, lanes], samples.at[tile])
        fetch(dipole_in.at[:, lanes], dipoles.at[tile])
    needed_first = len(copies)
    fetch(rounded_in, rounded)
    fetch(high_in, high)
    fetch(low_in, low)
    for copy in copies:
        copy.start()
    for grid in grids:
        grid[...] = jnp.zeros_like(grid)
    copies[0].wait()
    span_x, span_y = reach_x - 4, reach_y - 4
    local_x = stencil[0:1, :] - (lax.axis_index("wide") * span_x - 2)
    local_y = stencil[1:2, :] - (y_position() * span_y - 2)
    odd = local_x & 1
    places_out[0:1, :] = odd * (reach_x * reach_y) + (local_x >> 1) * (2 * reach_y) + 2 * local_y
    places_out[1:2, :] = stencil[2:3, :]
    to_scalar = pltpu.make_async_copy(places_out, place_ref, sems.at[len(copies)])
    to_scalar.start()
    for copy in copies[1:needed_first]:
        copy.wait()
    each = lambda values: [values.at[tile] for tile in range(tiles)]
    weave(flag[...], each(samples), each(dipoles), weight_ref, sample_coeff_ref)
    to_scalar.wait()
    add_panels(reach_y, True, vector_ref, place_ref, weight_ref, grids)
    for copy in copies[needed_first:]:
        copy.wait()
    spread_grid(
        reach_x, reach_y, rounded[...], (high, low), outs, flips, wides, head, total, grids
    )


def spread_kernel(reach_x, reach_y, flips, *refs):
    vector_ref, place_ref, rounded_ref, high_ref, low_ref, line_ref = refs[:6]
    refs = refs[6:]
    outs, wides, (head, total), grids = (
        refs[: len(flips)],
        refs[len(flips) : len(flips) + 2],
        refs[len(flips) + 2 : len(flips) + 4],
        refs[len(flips) + 4 :],
    )
    for grid in grids:
        grid[...] = jnp.zeros_like(grid)
    add_panels(reach_y, False, vector_ref, place_ref, line_ref, grids)
    spread_grid(
        reach_x,
        reach_y,
        rounded_ref[...],
        (high_ref, low_ref),
        outs,
        flips,
        wides,
        head,
        total,
        grids,
    )


def spread(vector, table, placed, raw, reach_x, reach_y, flips):
    count = vector.shape[0]
    half = reach_x * reach_y // 2
    blocks = count // BLOCK
    top = up_to(2 + 2 * blocks, 16)
    lanes = 2 * HALF
    body = up_to(half, 16)
    woven = (count // GROUP * 16, BLOCK)
    out_shapes = [jax.ShapeDtypeStruct((top + body, lanes), jnp.int16)] * len(flips)
    out_shapes += [jax.ShapeDtypeStruct((body, 2 * REGION), BF16)] * 2
    rounded = vector.reshape(blocks, BLOCK)
    work = [
        pltpu.VMEM((top, lanes), F32),
        pltpu.VMEM((reach_x * reach_y, REGION), F32),
    ] + [pltpu.VMEM((pair_count(reach_x, reach_y), REGION), F32)] * CHAINS
    if placed is None:
        stencil, flag, sample, dipole = raw
        operands = [vector, rounded, *table, stencil, flag.reshape(1, -1), sample, dipole]
        pinned = [pltpu.with_memory_space_constraint(value, pltpu.HBM) for value in operands[1:]]
        operands = [vector] + pinned
        in_specs = [in_smem()] + [pl.BlockSpec(memory_space=pltpu.HBM)] * 7
        out_shapes += [jax.ShapeDtypeStruct(woven, F32)] * 2
        out_shapes += [jax.ShapeDtypeStruct((2, count), jnp.int32)]
        tiled = pltpu.VMEM((blocks, 64, BLOCK), F32)
        work = [
            pltpu.VMEM(rounded.shape, F32),
            pltpu.VMEM(table[0].shape, BF16),
            pltpu.VMEM(table[1].shape, BF16),
            pltpu.VMEM(stencil.shape, jnp.int32),
            pltpu.VMEM((1, count), jnp.int32),
            tiled,
            tiled,
            pltpu.SMEM((2, count), jnp.int32),
            pltpu.SemaphoreType.DMA((6 + 2 * blocks,)),
        ] + work
    else:
        operands = [vector, placed[0], rounded, *table, placed[1]]
        in_specs = [in_smem()] * 2 + [whole_vmem()] * 4
    return pl.pallas_call(
        functools.partial(
            start_kernel if placed is None else spread_kernel, reach_x, reach_y, flips
        ),
        in_specs=in_specs,
        out_specs=[whole_vmem()] * len(out_shapes),
        out_shape=out_shapes,
        scratch_shapes=work,
        compiler_params=pltpu.CompilerParams(
            vmem_limit_bytes=START_LIMIT if placed is None else VMEM_LIMIT
        ),
        cost_estimate=cost(2 * half * 256 * 512, 4 * 16 * count * REGION),
        name="start" if placed is None else "spread",
    )(*operands)


def spread_rest_kernel(flips, rounded_ref, wide_high, wide_low, high_ref, low_ref, *refs):
    outs, head = refs[:-1], refs[-1]
    both = (wide_high[...], wide_low[...])
    send_pieces(outs, flips, head, rounded_ref[...], both, high_ref, low_ref)


def spread_rest(vector, both, table, flips):
    blocks = vector.shape[0] // BLOCK
    top = up_to(2 + 2 * blocks, 16)
    shape = (top + both[0].shape[0], 2 * HALF)
    return pl.pallas_call(
        functools.partial(spread_rest_kernel, flips),
        in_specs=[whole_vmem()] * 5,
        out_specs=[whole_vmem()] * len(flips),
        out_shape=[jax.ShapeDtypeStruct(shape, jnp.int16)] * len(flips),
        scratch_shapes=[pltpu.VMEM((top, 2 * HALF), F32)],
        compiler_params=params(),
        cost_estimate=cost(2 * shape[0] * 256 * 256 * 3, 4 * shape[0] * 512),
        name="spread_rest",
    )(vector.reshape(blocks, BLOCK), *both, *table)


def lines_kernel(place_ref, coeff_ref, *refs):
    out_ref = refs[-1]
    lanes = lax.broadcasted_iota(jnp.int32, (8, REGION), 1)

    def body(group, carry):
        at = pl.multiple_of(group * 16, 16)
        coeff = [coeff_ref[pl.ds(at + 8 * q, 8), :] for q in range(2)]
        for local in range(GROUP):
            panel = group * GROUP + local
            depth = place_ref[1, panel]
            shift = (depth - 4 * local) & (REGION - 1)
            inside = in_window(lanes, depth)
            for q in range(2):
                first = pl.multiple_of(panel * 16 + 8 * q, 8)
                out_ref[pl.ds(first, 8), :] = jnp.where(inside, pltpu.roll(coeff[q], shift, 1), 0.0)
        return carry

    lax.fori_loop(0, place_ref.shape[1] // GROUP, body, 0)


def place_lines(places, coeff, awaited):
    count = places.shape[1]
    shape = (count * 16, REGION)
    return pl.pallas_call(
        lines_kernel,
        in_specs=[in_smem(), whole_vmem()] + [anywhere()] * len(awaited),
        out_specs=whole_vmem(),
        out_shape=jax.ShapeDtypeStruct(shape, F32),
        compiler_params=params(),
        cost_estimate=cost(16 * count * REGION, 4 * 16 * count * REGION),
        name="place_lines",
    )(places, coeff, *awaited)


def stack_pieces(parts, reach_x, reach_y, top, opened, stacked):
    half = reach_x // 2
    pitch = up_to(reach_y, 8)
    tall = len(parts) * pitch
    chip = lax.axis_index("narrow")
    for flip, part in enumerate(parts):
        first = from_short(part[:top, :])
        opened[...] = from_short(part[top:, :]) * unit(first[0:1], first[1:2])
        place = (chip ^ flip) * pitch
        for i in range(half):
            stacked[pl.ds(pl.multiple_of(i * tall + place, 8), reach_y), :] = opened[
                i * reach_y : (i + 1) * reach_y, :
            ]


def transform_pieces(table, stacked, before, spectrum):
    half = spectrum.shape[0]
    tall = stacked.shape[0] // half

    def tripled(values):
        high, low = split(values)
        return jnp.concatenate([high, low, high], axis=0)

    for i in range(0, half, 2):
        places = range(i, min(i + 2, half))
        held = jnp.concatenate([stacked[j * tall : (j + 1) * tall, :] for j in places], axis=1)
        result = dot(table, tripled(held))
        for j in places:
            made = result[:, (j - i) * 2 * HALF : (j - i + 1) * 2 * HALF]
            spectrum[j] = made if before is None else before[j] + made


def forward_early_kernel(reach_x, reach_y, chips, *refs):
    parts = refs[:chips]
    table_ref, spectrum, opened, stacked = refs[chips:]
    top = parts[0].shape[0] - opened.shape[0]
    stacked[...] = jnp.zeros_like(stacked)
    stack_pieces(parts, reach_x, reach_y, top, opened, stacked)
    transform_pieces(table_ref[lax.axis_index("pair")], stacked, None, spectrum)


def stacking_scratch(chips, reach_x, reach_y):
    half = reach_x // 2
    return [
        pltpu.VMEM((up_to(half * reach_y, 16), 2 * HALF), F32),
        pltpu.VMEM((half * chips * up_to(reach_y, 8), 2 * HALF), F32),
    ]


def forward_early(parts, table, reach_x, reach_y):
    half = reach_x // 2
    chips = len(parts)
    return pl.pallas_call(
        functools.partial(forward_early_kernel, reach_x, reach_y, chips),
        in_specs=[whole_vmem()] * (chips + 1),
        out_specs=whole_vmem(),
        out_shape=jax.ShapeDtypeStruct((half, GRID, 2 * HALF), F32),
        scratch_shapes=stacking_scratch(chips, reach_x, reach_y),
        compiler_params=params(),
        cost_estimate=cost(EARLY_FLOPS, 4 * half * GRID * 2 * HALF * 2),
        name="forward_early",
    )(*parts, table)


def forward_kernel(reach_x, reach_y, blocks, pieces, awaited, *refs):
    parts = refs[:pieces]
    early_ref, table_ref, modes_ref = refs[pieces : pieces + 3]
    refs = refs[: pieces + 3] + refs[pieces + 3 + awaited :]
    spectrum, even_out, layers_out, odd_out, own_out, peers_out, inner_out, *refs = refs[pieces + 3 :]
    opened, stacked, slabs, head = refs
    half = reach_x // 2
    pair = lax.axis_size("pair")
    top = parts[0].shape[0] - opened.shape[0]
    stacked[...] = jnp.zeros_like(stacked)
    head[...] = jnp.zeros_like(head)
    for piece in range(pieces):
        first = from_short(parts[piece][:top, :])
        mantissa, exponent = first[2 : 2 + blocks], first[2 + blocks : 2 + 2 * blocks]
        peers_out[piece * blocks : (piece + 1) * blocks, :] = decode_rounded(mantissa, exponent)
        at = 6 + 2 * piece * blocks
        head[at : at + blocks, :] = mantissa
        head[at + blocks : at + 2 * blocks, :] = exponent
    before = early_ref
    for core in range(1, pair):
        stack_pieces(parts[core::pair], reach_x, reach_y, top, opened, stacked)
        transform_pieces(table_ref[lax.axis_index("pair") ^ core], stacked, before, spectrum)
        before = spectrum

    chunk = 32

    def body(index, largest):
        rows = pl.ds(pl.multiple_of(index * chunk, chunk), chunk)
        low = low_lanes(chunk)
        decay = modes_ref[0, rows, :]
        log_decay = modes_ref[1, rows, :]
        across_half = jnp.exp(half * log_decay)
        across_cut = jnp.exp((half - 4) * log_decay)
        layers = [spectrum[i, rows, :] for i in range(half)]
        run = layers[0]
        cut_right = run
        for i in range(1, half):
            run = decay * run + layers[i]
            if i == half - 5:
                cut_right = run
        right = run
        run = layers[half - 1]
        cut_left = run
        for i in range(half - 2, -1, -1):
            run = decay * run + layers[i]
            if i == 4:
                cut_left = run
        left = run
        inner_out[rows, :] = jnp.where(low, right, left)
        swapped_right, swapped_left = swap(right), swap(left)
        own = jnp.where(low, left + across_half * swapped_left, right + across_half * swapped_right)
        made = [
            jnp.where(low, swap(layers[half - 4]), layers[half - 3]),
            jnp.where(low, swap(layers[half - 2]), layers[half - 1]),
            jnp.where(low, own, cut_right + across_cut * swapped_right),
            jnp.where(low, layers[0], swap(layers[1])),
            jnp.where(low, layers[2], swap(layers[3])),
            jnp.where(low, cut_left + across_cut * swapped_left, own),
            own,
        ]
        own_out[rows, :] = own
        for slab, values in enumerate(made):
            slabs[slab, rows, :] = values
        return tuple(
            jnp.maximum(old, jnp.max(jnp.abs(values).reshape(chunk // 8, 8, 2 * HALF), axis=0))
            for old, values in zip(largest, made)
        )

    zero = jnp.zeros((8, 2 * HALF), F32)
    largest = lax.fori_loop(0, GRID // chunk, body, (zero,) * 7)
    scales = [fit_scale(jnp.max(value, axis=0, keepdims=True)) for value in largest]
    head_rows = head.shape[0]

    def send(out, top, which):
        for place, slab in enumerate(which):
            exponent, fraction = scales[slab]
            head[2 * place : 2 * place + 1, :] = exponent
            head[2 * place + 1 : 2 * place + 2, :] = fraction
            at = top + place * GRID
            out[at : at + GRID, :] = quantize(slabs[slab], exponent, fraction)
        out[:top, :] = to_short(head[:top, :])

    on_left = lax.axis_index("wide") & 1
    for side, (even, odd) in enumerate(((0, 3), (3, 0))):

        @pl.when(on_left == side)
        def _():
            send(even_out, head_rows, (even + 2, 6))
            send(layers_out, 16, (even, even + 1))
            send(odd_out, head_rows, (odd + 2, odd, odd + 1))


def forward(parts, early, table, modes, reach_x, reach_y, blocks, awaited):
    pieces = len(parts)
    half = reach_x // 2
    lanes = 2 * HALF
    head = up_to(6 + 2 * pieces * blocks, 16)
    short = lambda rows: jax.ShapeDtypeStruct((rows, lanes), jnp.int16)
    return pl.pallas_call(
        functools.partial(
            forward_kernel, reach_x, reach_y, blocks, pieces, len(awaited)
        ),
        in_specs=[whole_vmem()] * (pieces + 3) + [anywhere()] * len(awaited),
        out_specs=[whole_vmem()] * 7,
        out_shape=[
            jax.ShapeDtypeStruct((half, GRID, lanes), F32),
            short(head + 2 * GRID),
            short(16 + 2 * GRID),
            short(head + 3 * GRID),
            jax.ShapeDtypeStruct((GRID, lanes), F32),
            jax.ShapeDtypeStruct((pieces * blocks, BLOCK), F32),
            jax.ShapeDtypeStruct((GRID, lanes), F32),
        ],
        scratch_shapes=stacking_scratch(pieces // table.shape[0], reach_x, reach_y)
        + [
            pltpu.VMEM((7, GRID, lanes), F32),
            pltpu.VMEM((head, lanes), F32),
        ],
        compiler_params=params(),
        cost_estimate=cost(2 * half * 256 * 256 * 128, 4 * half * GRID * lanes * 2),
        name="forward",
    )(*parts, early, table, modes, *awaited)


def opened_slabs(ref, count, head_rows):
    first = from_short(ref[:16, :])
    for slab in range(count):
        scale = unit(first[2 * slab : 2 * slab + 1], first[2 * slab + 1 : 2 * slab + 2])
        at = head_rows + slab * GRID
        yield from_short(ref[at : at + GRID, :]) * scale


def pair_kernel(reach_x, flips, own_ref, even_ref, modes_ref, *refs):
    outs, head = refs[:-1], refs[-1]
    span = reach_x - 4
    here = lax.axis_index("wide")
    low = low_lanes(GRID)
    log_decay = modes_ref[1]
    own = own_ref[...]
    _, partner = opened_slabs(even_ref, 2, even_ref.shape[0] - 2 * GRID)

    def weight(distances):
        powers = []
        for distance in distances:
            ahead = span * distance - reach_x
            powers.append(jnp.where(distance >= 2, ahead, ahead + GRID).astype(F32))
        return jnp.exp(jnp.where(low, *powers) * log_decay)

    head[...] = jnp.zeros_like(head)
    for flip, out in zip(flips, outs):
        behind = (here ^ flip) - here
        message = own * weight((-behind, behind))
        behind = (here ^ flip) - (here ^ 1)
        beside = jnp.where(jnp.abs(behind) == 1, 0.0, 1.0)
        send_piece(out, head, message + partner * (weight((-behind, behind)) * beside))


def pair_messages(own, from_even, modes, reach_x, flips):
    return pl.pallas_call(
        functools.partial(pair_kernel, reach_x, flips),
        in_specs=[whole_vmem()] * 3,
        out_specs=[whole_vmem()] * len(flips),
        out_shape=[jax.ShapeDtypeStruct((16 + GRID, 2 * HALF), jnp.int16)] * len(flips),
        scratch_shapes=[pltpu.VMEM((16, 2 * HALF), F32)],
        compiler_params=params(),
        cost_estimate=cost(16 * GRID * 2 * HALF, 4 * GRID * 2 * HALF * (6 + len(flips))),
        name="pair_messages",
    )(own, from_even, modes)


def send_fields(outs, flips, reach_y, field_high, field_low, high_ref, low_ref, ready, head):
    half = field_high.shape[0]
    mine = y_position()
    pitch = up_to(reach_y, 16)
    pick = lambda ref: jnp.concatenate([ref[mine ^ flip] for flip in flips], axis=0)
    table = (pick(high_ref), pick(low_ref))
    for i in range(0, half, 2):
        many = min(2, half - i)
        join = lambda ref: jnp.concatenate([ref[i + j] for j in range(many)], axis=1)
        result = dot_three(table, (join(field_high), join(field_low)))
        for j in range(many):
            for piece in range(len(flips)):
                ready[piece, (i + j) * reach_y : (i + j + 1) * reach_y, :] = result[
                    piece * pitch : piece * pitch + reach_y, j * 2 * HALF : (j + 1) * 2 * HALF
                ]
    head[...] = jnp.zeros_like(head)
    for piece, out in enumerate(outs):
        if ready.shape[1] > half * reach_y:
            ready[piece, half * reach_y :, :] = jnp.zeros_like(ready[piece, half * reach_y :, :])
        send_piece(out, head, ready[piece])


def inverse_kernel(reach_x, reach_y, flips, fars, *refs):
    spectrum, from_even, even_layers, from_odd, own_ref, inner_ref, *far_refs = refs[: 6 + fars]
    refs = refs[6 + fars :]
    high_ref, low_ref, modes_ref = refs[:3]
    outs = refs[3 : 3 + len(flips)]
    field_high, field_low, ready, head = refs[3 + len(flips) :]
    half = reach_x // 2
    span = reach_x - 4
    chunk = 32
    head_rows = from_even.shape[0] - 2 * GRID
    on_left = (lax.axis_index("wide") & 1) == 1
    even_places = (from_even, head_rows, 0), (even_layers, 16, 0), (even_layers, 16, 1)
    odd_places = tuple((from_odd, head_rows, place) for place in range(3))

    def slab_unit(place):
        ref, _, at = place
        first = from_short(ref[:16, :])
        return unit(first[2 * at : 2 * at + 1], first[2 * at + 1 : 2 * at + 2])

    both_units = [[slab_unit(place) for place in places] for places in (even_places, odd_places)]

    def sided(even, odd):
        return jnp.where(on_left, even, odd), jnp.where(on_left, odd, even)

    far_units = []
    for ref in far_refs:
        first = from_short(ref[:16, :])
        far_units.append(unit(first[0:1], first[1:2]))

    def body(index, carry):
        first = pl.multiple_of(index * chunk, chunk)
        rows = pl.ds(first, chunk)
        low = low_lanes(chunk)
        decay = modes_ref[0, rows, :]
        log_decay = modes_ref[1, rows, :]
        ring = modes_ref[2, rows, :]
        gain = modes_ref[3, rows, :]
        across_half = jnp.exp(half * log_decay)
        across_cut = jnp.exp((half - 4) * log_decay)
        around = jnp.exp((GRID - 4) * log_decay)
        beside = jnp.exp((GRID - reach_x - span) * log_decay)
        layers = [spectrum[i, rows, :] for i in range(half)]

        def slab(which):
            found = []
            for places, units in zip((even_places, odd_places), both_units):
                ref, top, place = places[which]
                at = pl.multiple_of(top + place * GRID + index * chunk, 16)
                found.append(from_short(ref[pl.ds(at, chunk), :]) * units[which])
            return sided(*found)

        left_moments, right_moments = slab(0)
        head_layers, tail_layers = zip(slab(1), slab(2))
        zero = jnp.zeros_like(decay)
        from_head = [head_layers[0], swap(head_layers[0]), head_layers[1], swap(head_layers[1])]
        from_tail = [swap(tail_layers[0]), tail_layers[0], swap(tail_layers[1]), tail_layers[1]]
        head_sum = from_head[0]
        for i in range(1, 4):
            head_sum = decay * head_sum + from_head[i]
        tail_sum = from_tail[3]
        for i in range(2, -1, -1):
            tail_sum = decay * tail_sum + from_tail[i]
        for i in range(4):
            layers[i] = layers[i] + jnp.where(low, from_head[i], zero)
        for i in range(4):
            place = half - 4 + i
            layers[place] = layers[place] + jnp.where(low, zero, from_tail[i])
        total = own_ref[rows, :] * jnp.exp((GRID - reach_x) * log_decay)
        at = pl.ds(pl.multiple_of(16 + index * chunk, 16), chunk)
        for ref, scale in zip(far_refs, far_units):
            total = total + from_short(ref[at, :]) * scale
        one = jnp.ones_like(decay)
        total = total + left_moments * jnp.where(low, beside, one)
        total = total + right_moments * jnp.where(low, one, beside)
        shared = jnp.where(low, head_sum, tail_sum)
        entering = (swap(total) + around * shared) * ring
        leaving = swap(across_half * entering + across_cut * shared + inner_ref[rows, :])
        run = jnp.where(low, entering, leaving)
        forward_runs = []
        for i in range(half):
            run = decay * run + layers[i]
            forward_runs.append(run)
        run = jnp.where(low, leaving, entering)
        for i in range(half - 1, -1, -1):
            ahead = decay * run
            high, rest = split(gain * (forward_runs[i] + ahead))
            field_high[i, rows, :] = high
            field_low[i, rows, :] = rest
            run = ahead + layers[i]
        return carry

    lax.fori_loop(0, GRID // chunk, body, 0)
    send_fields(outs, flips, reach_y, field_high, field_low, high_ref, low_ref, ready, head)


def inverse(
    spectrum,
    from_even,
    even_layers,
    from_odd,
    own,
    inner,
    fars,
    table,
    modes,
    reach_x,
    reach_y,
    flips,
):
    half = reach_x // 2
    lanes = 2 * HALF
    body = up_to(half * reach_y, 16)
    shapes = [jax.ShapeDtypeStruct((16 + body, lanes), jnp.int16)] * len(flips)
    shapes += [jax.ShapeDtypeStruct((half, GRID, lanes), BF16)] * 2
    return pl.pallas_call(
        functools.partial(inverse_kernel, reach_x, reach_y, flips, len(fars)),
        in_specs=[whole_vmem()] * (9 + len(fars)),
        out_specs=[whole_vmem()] * len(shapes),
        out_shape=shapes,
        scratch_shapes=[
            pltpu.VMEM((len(flips), body, lanes), F32),
            pltpu.VMEM((16, lanes), F32),
        ],
        compiler_params=params(),
        cost_estimate=cost(2 * half * 256 * 256 * 128, 4 * half * GRID * lanes * 2),
        name="inverse",
    )(spectrum, from_even, even_layers, from_odd, own, inner, *fars, *table, modes)


def inverse_rest_kernel(reach_y, flips, field_high, field_low, high_ref, low_ref, *refs):
    outs, (ready, head) = refs[: len(flips)], refs[len(flips) :]
    send_fields(outs, flips, reach_y, field_high, field_low, high_ref, low_ref, ready, head)


def inverse_rest(field, table, reach_y, flips):
    half = field[0].shape[0]
    lanes = 2 * HALF
    body = up_to(half * reach_y, 16)
    return pl.pallas_call(
        functools.partial(inverse_rest_kernel, reach_y, flips),
        in_specs=[whole_vmem()] * 4,
        out_specs=[whole_vmem()] * len(flips),
        out_shape=[jax.ShapeDtypeStruct((16 + body, lanes), jnp.int16)] * len(flips),
        scratch_shapes=[
            pltpu.VMEM((len(flips), body, lanes), F32),
            pltpu.VMEM((16, lanes), F32),
        ],
        compiler_params=params(),
        cost_estimate=cost(2 * half * 256 * 256 * 128, 4 * half * GRID * lanes * 2),
        name="inverse_rest",
    )(*field, *table)


def sum_rows(values):
    row = lax.broadcasted_iota(jnp.int32, values[0].shape, 0)
    for step in (4, 2, 1):
        low = (row & step) == 0
        paired = []
        for one, other in zip(values[: len(values) // 2], values[len(values) // 2 :]):
            kept = jnp.where(low, one, other)
            moved = jnp.where(low, other, one)
            if step == 4:
                moved = pltpu.roll(moved, 4, 0)
            else:
                moved = jnp.where(low, pltpu.roll(moved, 8 - step, 0), pltpu.roll(moved, step, 0))
            paired.append(kept + moved)
        values = paired
    return values[0]


def z_lines(parts, flips, high_ref, low_ref):
    mine = y_position()
    opened = []
    for part in parts:
        first = from_short(part[:16, :])
        opened.append(from_short(part[16:, :]) * unit(first[0:1], first[1:2]))
    values = split(jnp.concatenate(opened, axis=1))
    pick = lambda ref: jnp.concatenate([ref[mine ^ flip] for flip in flips], axis=0)
    return dot_three(values, (pick(high_ref), pick(low_ref)))


def sample_early_kernel(flips, *refs):
    *parts, high_ref, low_ref, out_ref = refs
    out_ref[...] = z_lines(parts, flips, high_ref, low_ref)


def sample_early(parts, flips, table):
    rows = parts[0].shape[0] - 16
    return pl.pallas_call(
        functools.partial(sample_early_kernel, flips),
        in_specs=[whole_vmem()] * (len(parts) + 2),
        out_specs=whole_vmem(),
        out_shape=jax.ShapeDtypeStruct((rows, 2 * REGION), F32),
        compiler_params=params(),
        cost_estimate=cost(EARLY_FLOPS, 4 * rows * 512),
        name="sample_early",
    )(*parts, *table)


def sample_kernel(last, reach_x, reach_y, flips, place_ref, *refs):
    parts = refs[: len(flips)]
    early_ref, high_ref, low_ref, line_ref, own_ref, vector_ref, near_ref, out_ref = refs[
        len(flips) : len(flips) + 8
    ]
    flat, field, sums = refs[len(flips) + 8 :]
    half_rows = reach_x * reach_y // 2
    both = early_ref[...] + z_lines(parts, flips, high_ref, low_ref)
    flat[:half_rows, :] = both[:half_rows, :REGION]
    flat[half_rows:, :] = both[:half_rows, REGION:]
    for x in range(reach_x):
        layer = flat[x * reach_y : (x + 1) * reach_y, :]
        for row in pair_rows(x, reach_x, reach_y):
            field[pl.ds(row, reach_y, stride=2), :] = layer
    count = place_ref.shape[1]

    def body(group, carry):
        for eight in range(0, GROUP, 8):
            totals = []
            for local in range(eight, eight + 8):
                panel = group * GROUP + local
                row = place_ref[0, panel]
                first = pl.multiple_of(panel * 16, 16)
                totals.append(
                    field[pl.ds(row, 8), :] * line_ref[pl.ds(first, 8), :]
                    + field[pl.ds(row + 2 * reach_y, 8), :] * line_ref[pl.ds(first + 8, 8), :]
                )
            sums[pl.ds(pl.multiple_of(group * GROUP + eight, 8), 8), :] = sum_rows(totals)
        return carry

    lax.fori_loop(0, count // GROUP, body, 0)
    sampled = lax.dot_general(
        jnp.ones((8, REGION), F32),
        sums[...],
        (((1,), (1,)), ((), ())),
        precision=lax.Precision.HIGHEST,
        preferred_element_type=F32,
    )
    for block in range(count // BLOCK):
        lane = slice(block * BLOCK, (block + 1) * BLOCK)
        row = slice(block, block + 1)
        vector = vector_ref[row, :]
        image = jnp.where(own_ref[row, :] == 1, 0.0, 0.5 * vector) + sampled[:1, lane]
        image = image + near_ref[row, :]
        if last:
            out_ref[0:1, lane] = vector
            out_ref[1:2, lane] = image
        else:
            out_ref[row, :] = image


def sample(last, places, parts, flips, early, table, lines, flag, vector, near, reach_x, reach_y):
    count = places.shape[1]
    blocks = count // BLOCK
    shape = (2, count) if last else (blocks, BLOCK)
    return pl.pallas_call(
        functools.partial(sample_kernel, last, reach_x, reach_y, flips),
        in_specs=[in_smem()] + [whole_vmem()] * (len(parts) + 7),
        out_specs=whole_vmem(),
        out_shape=jax.ShapeDtypeStruct(shape, F32),
        scratch_shapes=[
            pltpu.VMEM((reach_x * reach_y, REGION), F32),
            pltpu.VMEM((pair_count(reach_x, reach_y), REGION), F32),
            pltpu.VMEM((count, REGION), F32),
        ],
        compiler_params=params(),
        cost_estimate=cost(reach_x * reach_y * 256 * 512, 4 * 16 * count * REGION),
        name="sample",
    )(
        places,
        *parts,
        early,
        *table,
        lines,
        flag.reshape(blocks, BLOCK),
        vector.reshape(blocks, BLOCK),
        near,
    )


def near_kernel(slots, blocks, place_ref, target_ref, *refs):
    even_ref, odd_ref, peers_ref, tile_ref = refs[:4]
    out_ref, held = refs[-2:]
    count = peers_ref.shape[0]
    held[count : 2 * count, :] = peers_ref[...]
    on_left = lax.axis_index("wide") & 1
    for side, ref in ((1 - on_left, even_ref), (on_left, odd_ref)):
        top = from_short(ref[...])
        for piece in range(count // blocks):
            at = 6 + 2 * piece * blocks
            held[pl.ds(side * (2 * count) + piece * blocks, blocks), :] = decode_rounded(
                top[at : at + blocks], top[at + blocks : at + 2 * blocks]
            )
    out_ref[...] = jnp.zeros_like(out_ref)
    for slot in range(slots):
        picked = held[pl.ds(place_ref[slot], 1), :]
        picked = jnp.broadcast_to(picked, (16, BLOCK)).astype(BF16)
        product = lax.dot_general(
            picked,
            tile_ref[slot],
            (((1,), (1,)), ((), ())),
            preferred_element_type=F32,
        )
        target = pl.ds(target_ref[slot], 1)
        out_ref[target, :] = out_ref[target, :] + product[:1]


def near_field(places, targets, from_even, from_odd, peers, tiles, blocks, out_rows, awaited):
    slots = tiles.shape[0]
    head = from_even.shape[0] - 2 * GRID
    constant = lambda shape: pl.BlockSpec(shape, lambda i: (0,) * len(shape))
    return pl.pallas_call(
        functools.partial(near_kernel, slots, blocks),
        grid=(1,),
        in_specs=[
            in_smem(),
            in_smem(),
            constant((head, BLOCK)),
            constant((head, BLOCK)),
            constant(peers.shape),
            constant(tiles.shape),
        ]
        + [anywhere()] * len(awaited),
        out_specs=constant((out_rows, BLOCK)),
        out_shape=jax.ShapeDtypeStruct((out_rows, BLOCK), F32),
        scratch_shapes=[pltpu.VMEM((3 * peers.shape[0], BLOCK), F32)],
        compiler_params=params(),
        cost_estimate=cost(2 * slots * 16 * BLOCK * BLOCK, 2 * slots * BLOCK * BLOCK),
        name="near_field",
    )(places, targets, from_even, from_odd, peers, tiles, *awaited)


def shards(
    density,
    surface_flag,
    stencil_base,
    sample_weights,
    dipole_weights,
    near_target,
    near_source,
    near_tiles,
):
    x_count = lax.axis_size("wide")
    y_count = lax.axis_size(Y_AXES)
    y_index = lax.axis_index(Y_AXES)
    pair = lax.axis_size("pair")
    span_x = REGION // x_count
    span_y = REGION // y_count
    reach_x = span_x + 4
    reach_y = span_y + 4
    count = density.shape[0]
    blocks = count // BLOCK

    z_forward, z_inverse, y_forward, y_inverse, modes = tables(y_count, pair, span_y)
    modes = lax.dynamic_index_in_dim(jnp.asarray(modes), y_index, 0, keepdims=False)

    neighbour = near_source // blocks
    flip = (y_index + neighbour % 3 - 1) ^ y_index
    sources = ((neighbour // 3) * y_count + flip) * blocks + near_source % blocks
    out_rows = up_to(blocks + 1, 8)
    live = near_target >= 0
    sources = jnp.where(live, sources, 0)
    targets = jnp.where(live, near_target, out_rows - 1)

    swaps = lambda pairs: [(i, j) for i, j in pairs] + [(j, i) for i, j in pairs]
    even_swap = swaps([(i, i + 1) for i in range(0, x_count - 1, 2)])
    odd_swap = swaps([(i, i + 1) for i in range(1, x_count - 1, 2)])
    far_flips = list(range(2, x_count, 2))

    first = list(range(pair, y_count, pair))
    rest = [flip for flip in range(y_count) if flip not in first]
    same_core = list(range(0, y_count, pair))
    other_core = [flip for flip in range(y_count) if flip not in same_core]

    def turned(sent, then):
        arrived = [None] * y_count
        for flip, part in zip(first + rest, list(sent) + list(then)):
            swap_pairs = [(i, i ^ flip) for i in range(y_count)]
            arrived[flip] = part if flip == 0 else lax.ppermute(part, Y_AXES, swap_pairs)
        return arrived

    def chosen(parts, flips):
        return [parts[flip] for flip in flips]

    def convolve_and_sample(last, vector, sent, both, places, sample_lines, awaited):
        arrived = turned(sent, spread_rest(vector, both, z_forward, rest))
        early = forward_early(chosen(arrived, same_core), y_forward, reach_x, reach_y)
        spectrum, even_message, layers, odd_message, own, peers, inner = forward(
            arrived, early, y_forward, modes, reach_x, reach_y, blocks, awaited
        )
        from_even = lax.ppermute(even_message, "wide", even_swap)
        from_odd = lax.ppermute(odd_message, "wide", odd_swap)
        even_layers = lax.ppermute(layers, "wide", even_swap)
        fars = [
            lax.ppermute(message, "wide", [(i, i ^ flip) for i in range(x_count)])
            for flip, message in zip(
                far_flips, pair_messages(own, from_even, modes, reach_x, far_flips)
            )
        ]
        *sent, high, low = inverse(
            spectrum,
            from_even,
            even_layers,
            from_odd,
            own,
            inner,
            fars,
            y_inverse,
            modes,
            reach_x,
            reach_y,
            first,
        )
        then = inverse_rest((high, low), y_inverse, reach_y, rest)
        near_part = near_field(
            sources, targets, from_even, from_odd, peers, near_tiles, blocks, out_rows, then[:1]
        )
        arrived = turned(sent, then)
        image = sample(
            last,
            places,
            chosen(arrived, other_core),
            other_core,
            sample_early(chosen(arrived, same_core), same_core, z_inverse),
            z_inverse,
            sample_lines,
            surface_flag,
            vector,
            near_part,
            reach_x,
            reach_y,
        )
        return image, near_part

    raw = (stencil_base, surface_flag, sample_weights, dipole_weights)
    *sent, high, low, source_coeff, sample_coeff, places = spread(
        density, z_forward, None, raw, reach_x, reach_y, first
    )
    sample_lines = place_lines(places, sample_coeff, [])
    first_image, near_part = convolve_and_sample(
        False, density, sent, (high, low), places, sample_lines, [sample_lines]
    )
    first_image = first_image.reshape(-1)
    source_lines = place_lines(places, source_coeff, [near_part])
    *sent, high, low = spread(
        first_image, z_forward, (places, source_lines), None, reach_x, reach_y, first
    )
    both_images, _ = convolve_and_sample(
        True, first_image, sent, (high, low), places, sample_lines, []
    )
    return both_images


def solution(mesh):
    panels = P(("groups",) + ALL_AXES)
    columns = P(None, ("groups",) + ALL_AXES)
    in_specs = (
        panels,
        panels,
        columns,
        columns,
        columns,
        panels,
        panels,
        P(("groups",) + ALL_AXES, None, None),
    )
    return jax.shard_map(
        shards, mesh=mesh, in_specs=in_specs, out_specs=columns, check_vma=False
    )
```

```python
import functools
import math

import jax
import jax.numpy as jnp
import numpy as np
from jax import lax
from jax.experimental import pallas as pl
from jax.experimental.pallas import tpu as pltpu
from jax.sharding import PartitionSpec as P

GRID = 256
REGION = 128
BLOCK = 128
HALF = 64
KERNEL_GAIN = 4.0
SCREEN = 1.0 / 1024.0
LN2 = math.log(2.0)
Y_AXES = ("narrow", "pair")
ALL_AXES = ("wide", "narrow", "pair")
F32 = jnp.float32
BF16 = jnp.bfloat16
VMEM_LIMIT = 24 * 1024 * 1024
START_LIMIT = VMEM_LIMIT
EARLY_FLOPS = 5 * 10**9
GROUP = 32
CHAINS = 2


def cas(angles):
    return np.cos(angles) + np.sin(angles)


def up_to(count, multiple):
    return -(-count // multiple) * multiple


def low_lanes(rows):
    return lax.broadcasted_iota(jnp.int32, (rows, 2 * HALF), 1) < HALF


def swap(values):
    return pltpu.roll(values, HALF, 1)


def split(values):
    high = values.astype(BF16)
    return high, (values - high.astype(F32)).astype(BF16)


def dot(left, right):
    return jnp.dot(left, right, preferred_element_type=F32)


def dot_three(left, right):
    return dot(left[0], right[0]) + (dot(left[0], right[1]) + dot(left[1], right[0]))


def params():
    return pltpu.CompilerParams(vmem_limit_bytes=VMEM_LIMIT)


def whole_vmem():
    return pl.BlockSpec(memory_space=pltpu.VMEM)


def anywhere():
    return pl.BlockSpec(memory_space=pl.ANY)


def in_smem():
    return pl.BlockSpec(memory_space=pltpu.SMEM)


def cost(flops, moved):
    return pl.CostEstimate(flops=flops, bytes_accessed=moved, transcendentals=0)


def full_scale(exponent, fraction):
    return fraction * jnp.exp(exponent * LN2) * (1.0 / 1024.0)


def fit_scale(largest):
    largest = jnp.maximum(largest, 1e-30)
    exponent = jnp.floor(jnp.log(largest) * (1.0 / LN2))
    fraction = jnp.ceil(largest * jnp.exp(-exponent * LN2) * 1024.0) + 1.0
    return exponent, fraction


def to_short(values):
    return values.astype(jnp.int32).astype(jnp.int16)


def from_short(values):
    return values.astype(jnp.int32).astype(F32)


def quantize(values, exponent, fraction):
    return to_short(jnp.round(values * (32767.0 / full_scale(exponent, fraction))))


def unit(exponent, fraction):
    return full_scale(exponent, fraction) * (1.0 / 32767.0)


def encode_rounded(values):
    rounded = values.astype(BF16).astype(F32)
    size = jnp.maximum(jnp.abs(rounded), 1e-30)
    exponent = jnp.floor(jnp.log(size) * (1.0 / LN2))
    return jnp.round(rounded * jnp.exp((10.0 - exponent) * LN2)), exponent


def decode_rounded(mantissa, exponent):
    return (mantissa * jnp.exp((exponent - 10.0) * LN2)).astype(BF16).astype(F32)


def send_piece(out, head, values):
    exponent, fraction = fit_scale(jnp.max(jnp.abs(values), axis=0, keepdims=True))
    head[0:1, :] = exponent
    head[1:2, :] = fraction
    top = head.shape[0]
    out[:top, :] = to_short(head[...])
    out[top:, :] = quantize(values, exponent, fraction)


def y_position():
    return lax.axis_index("narrow") * lax.axis_size("pair") + lax.axis_index("pair")


def halves(table):
    high = table.astype(jnp.bfloat16)
    return high, (table - high.astype(np.float64)).astype(jnp.bfloat16)


def tables(y_count, pair, span_y):
    depth = GRID // y_count
    reach = span_y + 4
    waves = np.arange(GRID)
    step = 2.0 * np.pi / GRID
    z_table = cas(step * np.outer(np.arange(REGION), waves))
    z_forward = np.zeros((y_count, 2 * REGION, 2 * HALF))
    z_inverse = np.zeros((y_count, 2 * HALF, 2 * REGION))
    symbols = 4.0 * np.sin(np.pi * waves / GRID) ** 2
    shift = np.full((y_count, GRID, 2 * HALF), 1.0)
    y_forward = np.zeros((GRID, y_count, up_to(reach, 8)))
    y_inverse = np.zeros((y_count, up_to(reach, 16), GRID))
    for block in range(y_count):
        mine = z_table[:, block * depth : (block + 1) * depth]
        for half in range(2):
            rows = slice(half * REGION, (half + 1) * REGION)
            lanes = slice(half * HALF, half * HALF + depth)
            z_forward[block, rows, lanes] = mine
            z_inverse[block, lanes, rows] = mine.T / GRID
            shift[block, :, lanes] = (
                SCREEN + symbols[:, None] + symbols[None, block * depth : (block + 1) * depth]
            )
        cells = block * span_y - 2 + np.arange(reach)
        y_table = cas(step * np.outer(waves, cells))
        y_forward[:, block, :reach] = y_table
        y_inverse[block, :reach] = y_table.T / GRID
    y_forward = y_forward.reshape(GRID, y_count // pair, pair, -1).transpose(2, 0, 1, 3)
    y_forward = halves(y_forward.reshape(pair, GRID, -1))
    y_forward = np.concatenate([y_forward[0], y_forward[0], y_forward[1]], axis=2)
    root = np.sqrt(shift * (shift + 4.0))
    decay = 2.0 / (2.0 + shift + root)
    log_decay = np.log(decay)
    ring = 1.0 / (1.0 - np.exp(GRID * log_decay))
    gain = KERNEL_GAIN / root
    modes = np.stack([decay, log_decay, ring, gain], axis=1).astype(np.float32)
    return (
        halves(z_forward),
        halves(z_inverse),
        y_forward,
        halves(y_inverse),
        modes,
    )


def mixing_matrix():
    place = lax.broadcasted_iota(jnp.int32, (4 * BLOCK, 4 * BLOCK), 0)
    lane = lax.broadcasted_iota(jnp.int32, (4 * BLOCK, 4 * BLOCK), 1)
    return jnp.where(lane == 4 * (place % BLOCK) + place // BLOCK, 1.0, 0.0).astype(BF16)


def weave(tiles, mixing, out):
    weights = jnp.concatenate([jnp.concatenate(tile, axis=1) for tile in tiles], axis=0)
    first, rest = split(weights)
    second, third = split(weights - first.astype(F32))
    woven = dot(first, mixing) + (dot(second, mixing) + dot(third, mixing))
    for tile in range(len(tiles)):
        for part in range(BLOCK // GROUP):
            at = (tile * (BLOCK // GROUP) + part) * 16
            lanes = slice(part * BLOCK, (part + 1) * BLOCK)
            for a in range(4):
                row = tile * 16 + 4 * a
                out[pl.ds(at + 8 * (a // 2) + a % 2, 4, stride=2), :] = woven[row : row + 4, lanes]


def by_depth(ref):
    return [ref[pl.ds(depth, 16, stride=4), :] for depth in range(4)]


def pair_rows(x, reach_x, reach_y):
    even = (x // 2) * 2 * reach_y + x % 2
    if x == 0 or x == reach_x - 1:
        return [even]
    return [even, reach_x * reach_y + ((x - 1) // 2) * 2 * reach_y + (x - 1) % 2]


def pair_count(reach_x, reach_y):
    return (2 * reach_x - 2) * reach_y


def in_window(lanes, depth):
    return ((lanes - depth) & -4) == 0


def add_panels(reach, woven, vector_ref, place_ref, weight_ref, grids):
    lanes = lax.broadcasted_iota(jnp.int32, (8, REGION), 1)

    def body(group, carry):
        at = pl.multiple_of(group * 16, 16)
        coeff = [weight_ref[pl.ds(at + 8 * q, 8), :] for q in range(2)] if woven else None
        for local in range(GROUP):
            panel = group * GROUP + local
            grid = grids[local % len(grids)]
            row = place_ref[0, panel]
            value = vector_ref[panel]
            if woven:
                depth = place_ref[1, panel]
                shift = (depth - 4 * local) & (REGION - 1)
                value = jnp.where(in_window(lanes, depth), value, 0.0)
                lines = [pltpu.roll(coeff[q], shift, 1) for q in range(2)]
            else:
                first = pl.multiple_of(panel * 16, 16)
                lines = [weight_ref[pl.ds(first + 8 * q, 8), :] for q in range(2)]
            places = [pl.ds(row, 8), pl.ds(row + 2 * reach, 8)]
            held = [grid[place, :] for place in places]
            for q in range(2):
                grid[places[q], :] = held[q] + lines[q] * value
        return carry

    lax.fori_loop(0, vector_ref.shape[0] // GROUP, body, 0)


def send_pieces(outs, flips, head, rounded, both, high_ref, low_ref):
    blocks = rounded.shape[0]
    mantissa, exponent = encode_rounded(rounded)
    head[...] = jnp.zeros_like(head)
    head[2 : 2 + blocks, :] = mantissa
    head[2 + blocks : 2 + 2 * blocks, :] = exponent
    mine = y_position()
    for at in range(0, len(flips), 2):
        pick = lambda ref: jnp.concatenate([ref[mine ^ flip] for flip in flips[at : at + 2]], axis=1)
        result = dot_three(both, (pick(high_ref), pick(low_ref)))
        for i, out in enumerate(outs[at : at + 2]):
            send_piece(out, head, result[:, i * 2 * HALF : (i + 1) * 2 * HALF])


def spread_grid(reach_x, reach_y, rounded, tables, outs, flips, wides, head, total, grids):
    for x in range(reach_x):
        parts = [
            grid[pl.ds(row, reach_y, stride=2), :]
            for row in pair_rows(x, reach_x, reach_y)
            for grid in grids
        ]
        total[x * reach_y : (x + 1) * reach_y, :] = sum(parts[1:], parts[0])
    half = reach_x * reach_y // 2
    both = jnp.concatenate([total[:half, :], total[half:, :]], axis=1)
    extra = wides[0].shape[0] - half
    if extra:
        both = jnp.concatenate([both, jnp.zeros((extra, 2 * REGION), F32)], axis=0)
    both = split(both)
    for wide, values in zip(wides, both):
        wide[...] = values
    send_pieces(outs, flips, head, rounded, both, *tables)


def start_kernel(reach_x, reach_y, flips, *refs):
    vector_ref, *remote = refs[:8]
    refs = refs[8:]
    outs, refs = refs[: len(flips)], refs[len(flips) :]
    wides, (weight_ref, places_out), refs = refs[:2], refs[2:4], refs[4:]
    rounded, high, low, stencil, flag, samples, dipoles = refs[:7]
    place_ref, sems, head, total = refs[7:11]
    grids = refs[11:]
    tiles = samples.shape[0]
    copies = []
    fetch = lambda source, target: copies.append(
        pltpu.make_async_copy(source, target, sems.at[len(copies)])
    )
    rounded_in, high_in, low_in, stencil_in, flag_in, sample_in, dipole_in = remote
    fetch(stencil_in, stencil)
    fetch(flag_in, flag)
    for tile in range(tiles):
        lanes = pl.ds(tile * BLOCK, BLOCK)
        fetch(sample_in.at[:, lanes], samples.at[tile])
        fetch(dipole_in.at[:, lanes], dipoles.at[tile])
    needed_first = len(copies)
    fetch(rounded_in, rounded)
    fetch(high_in, high)
    fetch(low_in, low)
    for copy in copies:
        copy.start()
    for grid in grids:
        grid[...] = jnp.zeros_like(grid)
    mixing = mixing_matrix()
    copies[0].wait()
    span_x, span_y = reach_x - 4, reach_y - 4
    local_x = stencil[0:1, :] - (lax.axis_index("wide") * span_x - 2)
    local_y = stencil[1:2, :] - (y_position() * span_y - 2)
    odd = local_x & 1
    places_out[0:1, :] = odd * (reach_x * reach_y) + (local_x >> 1) * (2 * reach_y) + 2 * local_y
    places_out[1:2, :] = stencil[2:3, :]
    to_scalar = pltpu.make_async_copy(places_out, place_ref, sems.at[len(copies)])
    to_scalar.start()
    for copy in copies[1:needed_first]:
        copy.wait()
    sources = []
    for tile in range(tiles):
        charged = flag[:, tile * BLOCK : (tile + 1) * BLOCK] == 1
        pairs = zip(by_depth(samples.at[tile]), by_depth(dipoles.at[tile]))
        sources.append([jnp.where(charged, -sample, dipole) for sample, dipole in pairs])
    weave(sources, mixing, weight_ref)
    to_scalar.wait()
    add_panels(reach_y, True, vector_ref, place_ref, weight_ref, grids)
    for copy in copies[needed_first:]:
        copy.wait()
    spread_grid(
        reach_x, reach_y, rounded[...], (high, low), outs, flips, wides, head, total, grids
    )


def spread_kernel(reach_x, reach_y, flips, *refs):
    vector_ref, place_ref, rounded_ref, high_ref, low_ref, line_ref = refs[:6]
    refs = refs[6:]
    outs, wides, (head, total), grids = (
        refs[: len(flips)],
        refs[len(flips) : len(flips) + 2],
        refs[len(flips) + 2 : len(flips) + 4],
        refs[len(flips) + 4 :],
    )
    for grid in grids:
        grid[...] = jnp.zeros_like(grid)
    add_panels(reach_y, False, vector_ref, place_ref, line_ref, grids)
    spread_grid(
        reach_x,
        reach_y,
        rounded_ref[...],
        (high_ref, low_ref),
        outs,
        flips,
        wides,
        head,
        total,
        grids,
    )


def spread(vector, table, placed, raw, reach_x, reach_y, flips):
    count = vector.shape[0]
    half = reach_x * reach_y // 2
    blocks = count // BLOCK
    top = up_to(2 + 2 * blocks, 16)
    lanes = 2 * HALF
    body = up_to(half, 16)
    woven = (count // GROUP * 16, BLOCK)
    out_shapes = [jax.ShapeDtypeStruct((top + body, lanes), jnp.int16)] * len(flips)
    out_shapes += [jax.ShapeDtypeStruct((body, 2 * REGION), BF16)] * 2
    rounded = vector.reshape(blocks, BLOCK)
    work = [
        pltpu.VMEM((top, lanes), F32),
        pltpu.VMEM((reach_x * reach_y, REGION), F32),
    ] + [pltpu.VMEM((pair_count(reach_x, reach_y), REGION), F32)] * CHAINS
    if placed is None:
        stencil, flag, sample, dipole = raw
        operands = [vector, rounded, *table, stencil, flag.reshape(1, -1), sample, dipole]
        pinned = [pltpu.with_memory_space_constraint(value, pltpu.HBM) for value in operands[1:]]
        operands = [vector] + pinned
        in_specs = [in_smem()] + [pl.BlockSpec(memory_space=pltpu.HBM)] * 7
        out_shapes += [jax.ShapeDtypeStruct(woven, F32)]
        out_shapes += [jax.ShapeDtypeStruct((2, count), jnp.int32)]
        out_shapes += [jax.ShapeDtypeStruct(rounded.shape, F32)]
        out_shapes += [jax.ShapeDtypeStruct(values.shape, BF16) for values in table]
        tiled = pltpu.VMEM((blocks, 64, BLOCK), F32)
        work = [
            pltpu.VMEM(stencil.shape, jnp.int32),
            pltpu.VMEM((1, count), jnp.int32),
            tiled,
            tiled,
            pltpu.SMEM((2, count), jnp.int32),
            pltpu.SemaphoreType.DMA((6 + 2 * blocks,)),
        ] + work
    else:
        operands = [vector, placed[0], rounded, *table, placed[1]]
        in_specs = [in_smem()] * 2 + [whole_vmem()] * 4
    return pl.pallas_call(
        functools.partial(
            start_kernel if placed is None else spread_kernel, reach_x, reach_y, flips
        ),
        in_specs=in_specs,
        out_specs=[whole_vmem()] * len(out_shapes),
        out_shape=out_shapes,
        scratch_shapes=work,
        compiler_params=pltpu.CompilerParams(
            vmem_limit_bytes=START_LIMIT if placed is None else VMEM_LIMIT
        ),
        cost_estimate=cost(2 * half * 256 * 512, 4 * 16 * count * REGION),
        name="start" if placed is None else "spread",
    )(*operands)


def spread_rest_kernel(flips, rounded_ref, wide_high, wide_low, high_ref, low_ref, *refs):
    outs, head = refs[:-1], refs[-1]
    both = (wide_high[...], wide_low[...])
    send_pieces(outs, flips, head, rounded_ref[...], both, high_ref, low_ref)


def spread_rest(rounded, both, table, flips):
    blocks = rounded.shape[0]
    top = up_to(2 + 2 * blocks, 16)
    shape = (top + both[0].shape[0], 2 * HALF)
    return pl.pallas_call(
        functools.partial(spread_rest_kernel, flips),
        in_specs=[whole_vmem()] * 5,
        out_specs=[whole_vmem()] * len(flips),
        out_shape=[jax.ShapeDtypeStruct(shape, jnp.int16)] * len(flips),
        scratch_shapes=[pltpu.VMEM((top, 2 * HALF), F32)],
        compiler_params=params(),
        cost_estimate=cost(2 * shape[0] * 256 * 256 * 3, 4 * shape[0] * 512),
        name="spread_rest",
    )(rounded, *both, *table)


def lines_kernel(place_ref, coeff_ref, *refs):
    out_ref = refs[-1]
    lanes = lax.broadcasted_iota(jnp.int32, (8, REGION), 1)

    def body(group, carry):
        at = pl.multiple_of(group * 16, 16)
        coeff = [coeff_ref[pl.ds(at + 8 * q, 8), :] for q in range(2)]
        for local in range(GROUP):
            panel = group * GROUP + local
            depth = place_ref[1, panel]
            shift = (depth - 4 * local) & (REGION - 1)
            inside = in_window(lanes, depth)
            for q in range(2):
                first = pl.multiple_of(panel * 16 + 8 * q, 8)
                out_ref[pl.ds(first, 8), :] = jnp.where(inside, pltpu.roll(coeff[q], shift, 1), 0.0)
        return carry

    lax.fori_loop(0, place_ref.shape[1] // GROUP, body, 0)


def sample_lines_kernel(tiles, place_ref, *refs):
    out_ref, coeff = refs[-2:]
    weave([by_depth(ref) for ref in refs[:tiles]], mixing_matrix(), coeff)
    lines_kernel(place_ref, coeff, out_ref)


def place_sample_lines(places, sample):
    count = places.shape[1]
    blocks = count // BLOCK
    tile = lambda t: pl.BlockSpec((64, BLOCK), lambda i: (0, t))
    shape = (count * 16, REGION)
    return pl.pallas_call(
        functools.partial(sample_lines_kernel, blocks),
        grid=(1,),
        in_specs=[in_smem()] + [tile(t) for t in range(blocks)],
        out_specs=pl.BlockSpec(shape, lambda i: (0, 0)),
        out_shape=jax.ShapeDtypeStruct(shape, F32),
        scratch_shapes=[pltpu.VMEM((count // GROUP * 16, BLOCK), F32)],
        compiler_params=params(),
        cost_estimate=cost(16 * count * REGION, 4 * 16 * count * REGION),
        name="place_sample_lines",
    )(places, *[sample] * blocks)


def place_lines(places, coeff, awaited):
    count = places.shape[1]
    shape = (count * 16, REGION)
    return pl.pallas_call(
        lines_kernel,
        in_specs=[in_smem(), whole_vmem()] + [anywhere()] * len(awaited),
        out_specs=whole_vmem(),
        out_shape=jax.ShapeDtypeStruct(shape, F32),
        compiler_params=params(),
        cost_estimate=cost(16 * count * REGION, 4 * 16 * count * REGION),
        name="place_lines",
    )(places, coeff, *awaited)


def stack_pieces(parts, reach_x, reach_y, top, opened, stacked):
    half = reach_x // 2
    pitch = up_to(reach_y, 8)
    tall = len(parts) * pitch
    chip = lax.axis_index("narrow")
    for flip, part in enumerate(parts):
        first = from_short(part[:top, :])
        opened[...] = from_short(part[top:, :]) * unit(first[0:1], first[1:2])
        place = (chip ^ flip) * pitch
        for i in range(half):
            stacked[pl.ds(pl.multiple_of(i * tall + place, 8), reach_y), :] = opened[
                i * reach_y : (i + 1) * reach_y, :
            ]


def transform_pieces(table, stacked, before, spectrum):
    half = spectrum.shape[0]
    tall = stacked.shape[0] // half

    def tripled(values):
        high, low = split(values)
        return jnp.concatenate([high, low, high], axis=0)

    for i in range(0, half, 2):
        places = range(i, min(i + 2, half))
        held = jnp.concatenate([stacked[j * tall : (j + 1) * tall, :] for j in places], axis=1)
        result = dot(table, tripled(held))
        for j in places:
            made = result[:, (j - i) * 2 * HALF : (j - i + 1) * 2 * HALF]
            spectrum[j] = made if before is None else before[j] + made


def forward_early_kernel(reach_x, reach_y, chips, *refs):
    parts = refs[:chips]
    table_ref, spectrum, opened, stacked = refs[chips:]
    top = parts[0].shape[0] - opened.shape[0]
    stacked[...] = jnp.zeros_like(stacked)
    stack_pieces(parts, reach_x, reach_y, top, opened, stacked)
    transform_pieces(table_ref[lax.axis_index("pair")], stacked, None, spectrum)


def stacking_scratch(chips, reach_x, reach_y):
    half = reach_x // 2
    return [
        pltpu.VMEM((up_to(half * reach_y, 16), 2 * HALF), F32),
        pltpu.VMEM((half * chips * up_to(reach_y, 8), 2 * HALF), F32),
    ]


def forward_early(parts, table, reach_x, reach_y):
    half = reach_x // 2
    chips = len(parts)
    return pl.pallas_call(
        functools.partial(forward_early_kernel, reach_x, reach_y, chips),
        in_specs=[whole_vmem()] * (chips + 1),
        out_specs=whole_vmem(),
        out_shape=jax.ShapeDtypeStruct((half, GRID, 2 * HALF), F32),
        scratch_shapes=stacking_scratch(chips, reach_x, reach_y),
        compiler_params=params(),
        cost_estimate=cost(EARLY_FLOPS, 4 * half * GRID * 2 * HALF * 2),
        name="forward_early",
    )(*parts, table)


def forward_kernel(reach_x, reach_y, blocks, pieces, awaited, *refs):
    parts = refs[:pieces]
    early_ref, table_ref, modes_ref = refs[pieces : pieces + 3]
    refs = refs[: pieces + 3] + refs[pieces + 3 + awaited :]
    spectrum, even_out, layers_out, odd_out, own_out, peers_out, inner_out, *refs = refs[pieces + 3 :]
    opened, stacked, slabs, head = refs
    half = reach_x // 2
    pair = lax.axis_size("pair")
    top = parts[0].shape[0] - opened.shape[0]
    stacked[...] = jnp.zeros_like(stacked)
    head[...] = jnp.zeros_like(head)
    for piece in range(pieces):
        first = from_short(parts[piece][:top, :])
        mantissa, exponent = first[2 : 2 + blocks], first[2 + blocks : 2 + 2 * blocks]
        peers_out[piece * blocks : (piece + 1) * blocks, :] = decode_rounded(mantissa, exponent)
        at = 6 + 2 * piece * blocks
        head[at : at + blocks, :] = mantissa
        head[at + blocks : at + 2 * blocks, :] = exponent
    before = early_ref
    for core in range(1, pair):
        stack_pieces(parts[core::pair], reach_x, reach_y, top, opened, stacked)
        transform_pieces(table_ref[lax.axis_index("pair") ^ core], stacked, before, spectrum)
        before = spectrum

    chunk = 32

    def body(index, largest):
        rows = pl.ds(pl.multiple_of(index * chunk, chunk), chunk)
        low = low_lanes(chunk)
        decay = modes_ref[0, rows, :]
        log_decay = modes_ref[1, rows, :]
        across_half = jnp.exp(half * log_decay)
        across_cut = jnp.exp((half - 4) * log_decay)
        layers = [spectrum[i, rows, :] for i in range(half)]
        run = layers[0]
        cut_right = run
        for i in range(1, half):
            run = decay * run + layers[i]
            if i == half - 5:
                cut_right = run
        right = run
        run = layers[half - 1]
        cut_left = run
        for i in range(half - 2, -1, -1):
            run = decay * run + layers[i]
            if i == 4:
                cut_left = run
        left = run
        inner_out[rows, :] = jnp.where(low, right, left)
        swapped_right, swapped_left = swap(right), swap(left)
        own = jnp.where(low, left + across_half * swapped_left, right + across_half * swapped_right)
        made = [
            jnp.where(low, swap(layers[half - 4]), layers[half - 3]),
            jnp.where(low, swap(layers[half - 2]), layers[half - 1]),
            jnp.where(low, own, cut_right + across_cut * swapped_right),
            jnp.where(low, layers[0], swap(layers[1])),
            jnp.where(low, layers[2], swap(layers[3])),
            jnp.where(low, cut_left + across_cut * swapped_left, own),
            own,
        ]
        own_out[rows, :] = own
        for slab, values in enumerate(made):
            slabs[slab, rows, :] = values
        return tuple(
            jnp.maximum(old, jnp.max(jnp.abs(values).reshape(chunk // 8, 8, 2 * HALF), axis=0))
            for old, values in zip(largest, made)
        )

    zero = jnp.zeros((8, 2 * HALF), F32)
    largest = lax.fori_loop(0, GRID // chunk, body, (zero,) * 7)
    scales = [fit_scale(jnp.max(value, axis=0, keepdims=True)) for value in largest]
    head_rows = head.shape[0]

    def send(out, top, which):
        for place, slab in enumerate(which):
            exponent, fraction = scales[slab]
            head[2 * place : 2 * place + 1, :] = exponent
            head[2 * place + 1 : 2 * place + 2, :] = fraction
            at = top + place * GRID
            out[at : at + GRID, :] = quantize(slabs[slab], exponent, fraction)
        out[:top, :] = to_short(head[:top, :])

    on_left = lax.axis_index("wide") & 1
    for side, (even, odd) in enumerate(((0, 3), (3, 0))):

        @pl.when(on_left == side)
        def _():
            send(even_out, head_rows, (even + 2, 6))
            send(layers_out, 16, (even, even + 1))
            send(odd_out, head_rows, (odd + 2, odd, odd + 1))


def forward(parts, early, table, modes, reach_x, reach_y, blocks, awaited):
    pieces = len(parts)
    half = reach_x // 2
    lanes = 2 * HALF
    head = up_to(6 + 2 * pieces * blocks, 16)
    short = lambda rows: jax.ShapeDtypeStruct((rows, lanes), jnp.int16)
    return pl.pallas_call(
        functools.partial(
            forward_kernel, reach_x, reach_y, blocks, pieces, len(awaited)
        ),
        in_specs=[whole_vmem()] * (pieces + 3) + [anywhere()] * len(awaited),
        out_specs=[whole_vmem()] * 7,
        out_shape=[
            jax.ShapeDtypeStruct((half, GRID, lanes), F32),
            short(head + 2 * GRID),
            short(16 + 2 * GRID),
            short(head + 3 * GRID),
            jax.ShapeDtypeStruct((GRID, lanes), F32),
            jax.ShapeDtypeStruct((pieces * blocks, BLOCK), F32),
            jax.ShapeDtypeStruct((GRID, lanes), F32),
        ],
        scratch_shapes=stacking_scratch(pieces // table.shape[0], reach_x, reach_y)
        + [
            pltpu.VMEM((7, GRID, lanes), F32),
            pltpu.VMEM((head, lanes), F32),
        ],
        compiler_params=params(),
        cost_estimate=cost(2 * half * 256 * 256 * 128, 4 * half * GRID * lanes * 2),
        name="forward",
    )(*parts, early, table, modes, *awaited)


def opened_slabs(ref, count, head_rows):
    first = from_short(ref[:16, :])
    for slab in range(count):
        scale = unit(first[2 * slab : 2 * slab + 1], first[2 * slab + 1 : 2 * slab + 2])
        at = head_rows + slab * GRID
        yield from_short(ref[at : at + GRID, :]) * scale


def pair_kernel(reach_x, flips, own_ref, even_ref, modes_ref, *refs):
    outs, head = refs[:-1], refs[-1]
    span = reach_x - 4
    here = lax.axis_index("wide")
    low = low_lanes(GRID)
    log_decay = modes_ref[1]
    own = own_ref[...]
    _, partner = opened_slabs(even_ref, 2, even_ref.shape[0] - 2 * GRID)

    def weight(distances):
        powers = []
        for distance in distances:
            ahead = span * distance - reach_x
            powers.append(jnp.where(distance >= 2, ahead, ahead + GRID).astype(F32))
        return jnp.exp(jnp.where(low, *powers) * log_decay)

    head[...] = jnp.zeros_like(head)
    for flip, out in zip(flips, outs):
        behind = (here ^ flip) - here
        message = own * weight((-behind, behind))
        behind = (here ^ flip) - (here ^ 1)
        beside = jnp.where(jnp.abs(behind) == 1, 0.0, 1.0)
        send_piece(out, head, message + partner * (weight((-behind, behind)) * beside))


def pair_messages(own, from_even, modes, reach_x, flips):
    return pl.pallas_call(
        functools.partial(pair_kernel, reach_x, flips),
        in_specs=[whole_vmem()] * 3,
        out_specs=[whole_vmem()] * len(flips),
        out_shape=[jax.ShapeDtypeStruct((16 + GRID, 2 * HALF), jnp.int16)] * len(flips),
        scratch_shapes=[pltpu.VMEM((16, 2 * HALF), F32)],
        compiler_params=params(),
        cost_estimate=cost(16 * GRID * 2 * HALF, 4 * GRID * 2 * HALF * (6 + len(flips))),
        name="pair_messages",
    )(own, from_even, modes)


def send_fields(outs, flips, reach_y, field_high, field_low, high_ref, low_ref, ready, head):
    half = field_high.shape[0]
    mine = y_position()
    pitch = up_to(reach_y, 16)
    pick = lambda ref: jnp.concatenate([ref[mine ^ flip] for flip in flips], axis=0)
    table = (pick(high_ref), pick(low_ref))
    for i in range(0, half, 2):
        many = min(2, half - i)
        join = lambda ref: jnp.concatenate([ref[i + j] for j in range(many)], axis=1)
        result = dot_three(table, (join(field_high), join(field_low)))
        for j in range(many):
            for piece in range(len(flips)):
                ready[piece, (i + j) * reach_y : (i + j + 1) * reach_y, :] = result[
                    piece * pitch : piece * pitch + reach_y, j * 2 * HALF : (j + 1) * 2 * HALF
                ]
    head[...] = jnp.zeros_like(head)
    for piece, out in enumerate(outs):
        if ready.shape[1] > half * reach_y:
            ready[piece, half * reach_y :, :] = jnp.zeros_like(ready[piece, half * reach_y :, :])
        send_piece(out, head, ready[piece])


def inverse_kernel(reach_x, reach_y, flips, fars, *refs):
    spectrum, from_even, even_layers, from_odd, own_ref, inner_ref, *far_refs = refs[: 6 + fars]
    refs = refs[6 + fars :]
    high_ref, low_ref, modes_ref = refs[:3]
    outs = refs[3 : 3 + len(flips)]
    field_high, field_low, ready, head = refs[3 + len(flips) :]
    half = reach_x // 2
    span = reach_x - 4
    chunk = 32
    head_rows = from_even.shape[0] - 2 * GRID
    on_left = (lax.axis_index("wide") & 1) == 1
    even_places = (from_even, head_rows, 0), (even_layers, 16, 0), (even_layers, 16, 1)
    odd_places = tuple((from_odd, head_rows, place) for place in range(3))

    def slab_unit(place):
        ref, _, at = place
        first = from_short(ref[:16, :])
        return unit(first[2 * at : 2 * at + 1], first[2 * at + 1 : 2 * at + 2])

    both_units = [[slab_unit(place) for place in places] for places in (even_places, odd_places)]

    def sided(even, odd):
        return jnp.where(on_left, even, odd), jnp.where(on_left, odd, even)

    far_units = []
    for ref in far_refs:
        first = from_short(ref[:16, :])
        far_units.append(unit(first[0:1], first[1:2]))

    def body(index, carry):
        first = pl.multiple_of(index * chunk, chunk)
        rows = pl.ds(first, chunk)
        low = low_lanes(chunk)
        decay = modes_ref[0, rows, :]
        log_decay = modes_ref[1, rows, :]
        ring = modes_ref[2, rows, :]
        gain = modes_ref[3, rows, :]
        across_half = jnp.exp(half * log_decay)
        across_cut = jnp.exp((half - 4) * log_decay)
        around = jnp.exp((GRID - 4) * log_decay)
        beside = jnp.exp((GRID - reach_x - span) * log_decay)
        layers = [spectrum[i, rows, :] for i in range(half)]

        def slab(which):
            found = []
            for places, units in zip((even_places, odd_places), both_units):
                ref, top, place = places[which]
                at = pl.multiple_of(top + place * GRID + index * chunk, 16)
                found.append(from_short(ref[pl.ds(at, chunk), :]) * units[which])
            return sided(*found)

        left_moments, right_moments = slab(0)
        head_layers, tail_layers = zip(slab(1), slab(2))
        zero = jnp.zeros_like(decay)
        from_head = [head_layers[0], swap(head_layers[0]), head_layers[1], swap(head_layers[1])]
        from_tail = [swap(tail_layers[0]), tail_layers[0], swap(tail_layers[1]), tail_layers[1]]
        head_sum = from_head[0]
        for i in range(1, 4):
            head_sum = decay * head_sum + from_head[i]
        tail_sum = from_tail[3]
        for i in range(2, -1, -1):
            tail_sum = decay * tail_sum + from_tail[i]
        for i in range(4):
            layers[i] = layers[i] + jnp.where(low, from_head[i], zero)
        for i in range(4):
            place = half - 4 + i
            layers[place] = layers[place] + jnp.where(low, zero, from_tail[i])
        total = own_ref[rows, :] * jnp.exp((GRID - reach_x) * log_decay)
        at = pl.ds(pl.multiple_of(16 + index * chunk, 16), chunk)
        for ref, scale in zip(far_refs, far_units):
            total = total + from_short(ref[at, :]) * scale
        one = jnp.ones_like(decay)
        total = total + left_moments * jnp.where(low, beside, one)
        total = total + right_moments * jnp.where(low, one, beside)
        shared = jnp.where(low, head_sum, tail_sum)
        entering = (swap(total) + around * shared) * ring
        leaving = swap(across_half * entering + across_cut * shared + inner_ref[rows, :])
        run = jnp.where(low, entering, leaving)
        forward_runs = []
        for i in range(half):
            run = decay * run + layers[i]
            forward_runs.append(run)
        run = jnp.where(low, leaving, entering)
        for i in range(half - 1, -1, -1):
            ahead = decay * run
            high, rest = split(gain * (forward_runs[i] + ahead))
            field_high[i, rows, :] = high
            field_low[i, rows, :] = rest
            run = ahead + layers[i]
        return carry

    lax.fori_loop(0, GRID // chunk, body, 0)
    send_fields(outs, flips, reach_y, field_high, field_low, high_ref, low_ref, ready, head)


def inverse(
    spectrum,
    from_even,
    even_layers,
    from_odd,
    own,
    inner,
    fars,
    table,
    modes,
    reach_x,
    reach_y,
    flips,
):
    half = reach_x // 2
    lanes = 2 * HALF
    body = up_to(half * reach_y, 16)
    shapes = [jax.ShapeDtypeStruct((16 + body, lanes), jnp.int16)] * len(flips)
    shapes += [jax.ShapeDtypeStruct((half, GRID, lanes), BF16)] * 2
    return pl.pallas_call(
        functools.partial(inverse_kernel, reach_x, reach_y, flips, len(fars)),
        in_specs=[whole_vmem()] * (9 + len(fars)),
        out_specs=[whole_vmem()] * len(shapes),
        out_shape=shapes,
        scratch_shapes=[
            pltpu.VMEM((len(flips), body, lanes), F32),
            pltpu.VMEM((16, lanes), F32),
        ],
        compiler_params=params(),
        cost_estimate=cost(2 * half * 256 * 256 * 128, 4 * half * GRID * lanes * 2),
        name="inverse",
    )(spectrum, from_even, even_layers, from_odd, own, inner, *fars, *table, modes)


def inverse_rest_kernel(reach_y, flips, field_high, field_low, high_ref, low_ref, *refs):
    outs, (ready, head) = refs[: len(flips)], refs[len(flips) :]
    send_fields(outs, flips, reach_y, field_high, field_low, high_ref, low_ref, ready, head)


def inverse_rest(field, table, reach_y, flips):
    half = field[0].shape[0]
    lanes = 2 * HALF
    body = up_to(half * reach_y, 16)
    return pl.pallas_call(
        functools.partial(inverse_rest_kernel, reach_y, flips),
        in_specs=[whole_vmem()] * 4,
        out_specs=[whole_vmem()] * len(flips),
        out_shape=[jax.ShapeDtypeStruct((16 + body, lanes), jnp.int16)] * len(flips),
        scratch_shapes=[
            pltpu.VMEM((len(flips), body, lanes), F32),
            pltpu.VMEM((16, lanes), F32),
        ],
        compiler_params=params(),
        cost_estimate=cost(2 * half * 256 * 256 * 128, 4 * half * GRID * lanes * 2),
        name="inverse_rest",
    )(*field, *table)


def sum_rows(values):
    row = lax.broadcasted_iota(jnp.int32, values[0].shape, 0)
    for step in (4, 2, 1):
        low = (row & step) == 0
        paired = []
        for one, other in zip(values[: len(values) // 2], values[len(values) // 2 :]):
            kept = jnp.where(low, one, other)
            moved = jnp.where(low, other, one)
            if step == 4:
                moved = pltpu.roll(moved, 4, 0)
            else:
                moved = jnp.where(low, pltpu.roll(moved, 8 - step, 0), pltpu.roll(moved, step, 0))
            paired.append(kept + moved)
        values = paired
    return values[0]


def z_lines(parts, flips, high_ref, low_ref):
    mine = y_position()
    opened = []
    for part in parts:
        first = from_short(part[:16, :])
        opened.append(from_short(part[16:, :]) * unit(first[0:1], first[1:2]))
    values = split(jnp.concatenate(opened, axis=1))
    pick = lambda ref: jnp.concatenate([ref[mine ^ flip] for flip in flips], axis=0)
    return dot_three(values, (pick(high_ref), pick(low_ref)))


def sample_early_kernel(flips, *refs):
    *parts, high_ref, low_ref, out_ref = refs
    out_ref[...] = z_lines(parts, flips, high_ref, low_ref)


def sample_early(parts, flips, table):
    rows = parts[0].shape[0] - 16
    return pl.pallas_call(
        functools.partial(sample_early_kernel, flips),
        in_specs=[whole_vmem()] * (len(parts) + 2),
        out_specs=whole_vmem(),
        out_shape=jax.ShapeDtypeStruct((rows, 2 * REGION), F32),
        compiler_params=params(),
        cost_estimate=cost(EARLY_FLOPS, 4 * rows * 512),
        name="sample_early",
    )(*parts, *table)


def sample_kernel(last, reach_x, reach_y, flips, place_ref, *refs):
    parts = refs[: len(flips)]
    early_ref, high_ref, low_ref, line_ref, own_ref, vector_ref, near_ref, out_ref = refs[
        len(flips) : len(flips) + 8
    ]
    flat, field, sums = refs[len(flips) + 8 :]
    half_rows = reach_x * reach_y // 2
    both = early_ref[...] + z_lines(parts, flips, high_ref, low_ref)
    flat[:half_rows, :] = both[:half_rows, :REGION]
    flat[half_rows:, :] = both[:half_rows, REGION:]
    for x in range(reach_x):
        layer = flat[x * reach_y : (x + 1) * reach_y, :]
        for row in pair_rows(x, reach_x, reach_y):
            field[pl.ds(row, reach_y, stride=2), :] = layer
    count = place_ref.shape[1]

    def body(group, carry):
        for eight in range(0, GROUP, 8):
            totals = []
            for local in range(eight, eight + 8):
                panel = group * GROUP + local
                row = place_ref[0, panel]
                first = pl.multiple_of(panel * 16, 16)
                totals.append(
                    field[pl.ds(row, 8), :] * line_ref[pl.ds(first, 8), :]
                    + field[pl.ds(row + 2 * reach_y, 8), :] * line_ref[pl.ds(first + 8, 8), :]
                )
            sums[pl.ds(pl.multiple_of(group * GROUP + eight, 8), 8), :] = sum_rows(totals)
        return carry

    lax.fori_loop(0, count // GROUP, body, 0)
    sampled = lax.dot_general(
        jnp.ones((8, REGION), F32),
        sums[...],
        (((1,), (1,)), ((), ())),
        precision=lax.Precision.HIGHEST,
        preferred_element_type=F32,
    )
    for block in range(count // BLOCK):
        lane = slice(block * BLOCK, (block + 1) * BLOCK)
        row = slice(block, block + 1)
        vector = vector_ref[row, :]
        image = jnp.where(own_ref[row, :] == 1, 0.0, 0.5 * vector) + sampled[:1, lane]
        image = image + near_ref[row, :]
        if last:
            out_ref[0:1, lane] = vector
            out_ref[1:2, lane] = image
        else:
            out_ref[row, :] = image


def sample(last, places, parts, flips, early, table, lines, flag, vector, near, reach_x, reach_y):
    count = places.shape[1]
    blocks = count // BLOCK
    shape = (2, count) if last else (blocks, BLOCK)
    return pl.pallas_call(
        functools.partial(sample_kernel, last, reach_x, reach_y, flips),
        in_specs=[in_smem()] + [whole_vmem()] * (len(parts) + 7),
        out_specs=whole_vmem(),
        out_shape=jax.ShapeDtypeStruct(shape, F32),
        scratch_shapes=[
            pltpu.VMEM((reach_x * reach_y, REGION), F32),
            pltpu.VMEM((pair_count(reach_x, reach_y), REGION), F32),
            pltpu.VMEM((count, REGION), F32),
        ],
        compiler_params=params(),
        cost_estimate=cost(reach_x * reach_y * 256 * 512, 4 * 16 * count * REGION),
        name="sample",
    )(
        places,
        *parts,
        early,
        *table,
        lines,
        flag.reshape(blocks, BLOCK),
        vector.reshape(blocks, BLOCK),
        near,
    )


def near_kernel(slots, blocks, place_ref, target_ref, *refs):
    even_ref, odd_ref, peers_ref, tile_ref = refs[:4]
    out_ref, held = refs[-2:]
    count = peers_ref.shape[0]
    held[count : 2 * count, :] = peers_ref[...]
    on_left = lax.axis_index("wide") & 1
    for side, ref in ((1 - on_left, even_ref), (on_left, odd_ref)):
        top = from_short(ref[...])
        for piece in range(count // blocks):
            at = 6 + 2 * piece * blocks
            held[pl.ds(side * (2 * count) + piece * blocks, blocks), :] = decode_rounded(
                top[at : at + blocks], top[at + blocks : at + 2 * blocks]
            )
    out_ref[...] = jnp.zeros_like(out_ref)
    for slot in range(slots):
        picked = held[pl.ds(place_ref[slot], 1), :]
        picked = jnp.broadcast_to(picked, (16, BLOCK)).astype(BF16)
        product = lax.dot_general(
            picked,
            tile_ref[slot],
            (((1,), (1,)), ((), ())),
            preferred_element_type=F32,
        )
        target = pl.ds(target_ref[slot], 1)
        out_ref[target, :] = out_ref[target, :] + product[:1]


def near_field(places, targets, from_even, from_odd, peers, tiles, blocks, out_rows, awaited):
    slots = tiles.shape[0]
    head = from_even.shape[0] - 2 * GRID
    constant = lambda shape: pl.BlockSpec(shape, lambda i: (0,) * len(shape))
    return pl.pallas_call(
        functools.partial(near_kernel, slots, blocks),
        grid=(1,),
        in_specs=[
            in_smem(),
            in_smem(),
            constant((head, BLOCK)),
            constant((head, BLOCK)),
            constant(peers.shape),
            constant(tiles.shape),
        ]
        + [anywhere()] * len(awaited),
        out_specs=constant((out_rows, BLOCK)),
        out_shape=jax.ShapeDtypeStruct((out_rows, BLOCK), F32),
        scratch_shapes=[pltpu.VMEM((3 * peers.shape[0], BLOCK), F32)],
        compiler_params=params(),
        cost_estimate=cost(2 * slots * 16 * BLOCK * BLOCK, 2 * slots * BLOCK * BLOCK),
        name="near_field",
    )(places, targets, from_even, from_odd, peers, tiles, *awaited)


def shards(
    density,
    surface_flag,
    stencil_base,
    sample_weights,
    dipole_weights,
    near_target,
    near_source,
    near_tiles,
):
    x_count = lax.axis_size("wide")
    y_count = lax.axis_size(Y_AXES)
    y_index = lax.axis_index(Y_AXES)
    pair = lax.axis_size("pair")
    span_x = REGION // x_count
    span_y = REGION // y_count
    reach_x = span_x + 4
    reach_y = span_y + 4
    count = density.shape[0]
    blocks = count // BLOCK

    z_forward, z_inverse, y_forward, y_inverse, modes = tables(y_count, pair, span_y)
    modes = lax.dynamic_index_in_dim(jnp.asarray(modes), y_index, 0, keepdims=False)

    neighbour = near_source // blocks
    flip = (y_index + neighbour % 3 - 1) ^ y_index
    sources = ((neighbour // 3) * y_count + flip) * blocks + near_source % blocks
    out_rows = up_to(blocks + 1, 8)
    live = near_target >= 0
    sources = jnp.where(live, sources, 0)
    targets = jnp.where(live, near_target, out_rows - 1)

    swaps = lambda pairs: [(i, j) for i, j in pairs] + [(j, i) for i, j in pairs]
    even_swap = swaps([(i, i + 1) for i in range(0, x_count - 1, 2)])
    odd_swap = swaps([(i, i + 1) for i in range(1, x_count - 1, 2)])
    far_flips = list(range(2, x_count, 2))

    first, rest = list(range(pair, y_count)), list(range(pair))
    same_core = list(range(0, y_count, pair))
    other_core = [flip for flip in range(y_count) if flip not in same_core]

    def turned(sent, then):
        arrived = [None] * y_count
        for flip, part in zip(first + rest, list(sent) + list(then)):
            swap_pairs = [(i, i ^ flip) for i in range(y_count)]
            arrived[flip] = part if flip == 0 else lax.ppermute(part, Y_AXES, swap_pairs)
        return arrived

    def chosen(parts, flips):
        return [parts[flip] for flip in flips]

    def convolve_and_sample(last, vector, sent, both, table, places, sample_lines, awaited):
        arrived = turned(sent, spread_rest(vector, both, table, rest))
        early = forward_early(chosen(arrived, same_core), y_forward, reach_x, reach_y)
        spectrum, even_message, layers, odd_message, own, peers, inner = forward(
            arrived, early, y_forward, modes, reach_x, reach_y, blocks, awaited
        )
        from_even = lax.ppermute(even_message, "wide", even_swap)
        from_odd = lax.ppermute(odd_message, "wide", odd_swap)
        even_layers = lax.ppermute(layers, "wide", even_swap)
        fars = [
            lax.ppermute(message, "wide", [(i, i ^ flip) for i in range(x_count)])
            for flip, message in zip(
                far_flips, pair_messages(own, from_even, modes, reach_x, far_flips)
            )
        ]
        *sent, high, low = inverse(
            spectrum,
            from_even,
            even_layers,
            from_odd,
            own,
            inner,
            fars,
            y_inverse,
            modes,
            reach_x,
            reach_y,
            first,
        )
        then = inverse_rest((high, low), y_inverse, reach_y, rest)
        near_part = near_field(
            sources, targets, from_even, from_odd, peers, near_tiles, blocks, out_rows, then[:1]
        )
        arrived = turned(sent, then)
        image = sample(
            last,
            places,
            chosen(arrived, other_core),
            other_core,
            sample_early(chosen(arrived, same_core), same_core, z_inverse),
            z_inverse,
            sample_lines,
            surface_flag,
            vector,
            near_part,
            reach_x,
            reach_y,
        )
        return image, near_part

    raw = (stencil_base, surface_flag, sample_weights, dipole_weights)
    *sent, wide_high, wide_low, source_coeff, places, vector, high, low = spread(
        density, z_forward, None, raw, reach_x, reach_y, first
    )
    z_forward = (high, low)
    sample_lines = place_sample_lines(places, sample_weights)
    vector, near_part = convolve_and_sample(
        False,
        vector,
        sent,
        (wide_high, wide_low),
        z_forward,
        places,
        sample_lines,
        [sample_lines],
    )
    source_lines = place_lines(places, source_coeff, [near_part])
    *sent, wide_high, wide_low = spread(
        vector.reshape(-1), z_forward, (places, source_lines), None, reach_x, reach_y, first
    )
    both_images, _ = convolve_and_sample(
        True, vector, sent, (wide_high, wide_low), z_forward, places, sample_lines, []
    )
    return both_images


def solution(mesh):
    panels = P(("groups",) + ALL_AXES)
    columns = P(None, ("groups",) + ALL_AXES)
    in_specs = (
        panels,
        panels,
        columns,
        columns,
        columns,
        panels,
        panels,
        P(("groups",) + ALL_AXES, None, None),
    )
    return jax.shard_map(
        shards, mesh=mesh, in_specs=in_specs, out_specs=columns, check_vma=False
    )
```

```python
import functools
import math

import jax
import jax.numpy as jnp
import numpy as np
from jax import lax
from jax.experimental import pallas as pl
from jax.experimental.pallas import tpu as pltpu
from jax.sharding import PartitionSpec as P

GRID = 256
REGION = 128
BLOCK = 128
HALF = 64
KERNEL_GAIN = 4.0
SCREEN = 1.0 / 1024.0
LN2 = math.log(2.0)
Y_AXES = ("narrow", "pair")
ALL_AXES = ("wide", "narrow", "pair")
F32 = jnp.float32
BF16 = jnp.bfloat16
VMEM_LIMIT = 24 * 1024 * 1024
START_LIMIT = VMEM_LIMIT
EARLY_FLOPS = 5 * 10**9
GROUP = 32
CHAINS = 2


def cas(angles):
    return np.cos(angles) + np.sin(angles)


def up_to(count, multiple):
    return -(-count // multiple) * multiple


def low_lanes(rows):
    return lax.broadcasted_iota(jnp.int32, (rows, 2 * HALF), 1) < HALF


def swap(values):
    return pltpu.roll(values, HALF, 1)


def split(values):
    high = values.astype(BF16)
    return high, (values - high.astype(F32)).astype(BF16)


def dot(left, right):
    return jnp.dot(left, right, preferred_element_type=F32)


def dot_three(left, right):
    return dot(left[0], right[0]) + (dot(left[0], right[1]) + dot(left[1], right[0]))


def params():
    return pltpu.CompilerParams(vmem_limit_bytes=VMEM_LIMIT)


def whole_vmem():
    return pl.BlockSpec(memory_space=pltpu.VMEM)


def anywhere():
    return pl.BlockSpec(memory_space=pl.ANY)


def in_smem():
    return pl.BlockSpec(memory_space=pltpu.SMEM)


def cost(flops, moved):
    return pl.CostEstimate(flops=flops, bytes_accessed=moved, transcendentals=0)


def full_scale(exponent, fraction):
    return fraction * jnp.exp(exponent * LN2) * (1.0 / 1024.0)


def fit_scale(largest):
    largest = jnp.maximum(largest, 1e-30)
    exponent = jnp.floor(jnp.log(largest) * (1.0 / LN2))
    fraction = jnp.ceil(largest * jnp.exp(-exponent * LN2) * 1024.0) + 1.0
    return exponent, fraction


def to_short(values):
    return values.astype(jnp.int32).astype(jnp.int16)


def from_short(values):
    return values.astype(jnp.int32).astype(F32)


def quantize(values, exponent, fraction):
    return to_short(jnp.round(values * (32767.0 / full_scale(exponent, fraction))))


def unit(exponent, fraction):
    return full_scale(exponent, fraction) * (1.0 / 32767.0)


def encode_rounded(values):
    rounded = values.astype(BF16).astype(F32)
    size = jnp.maximum(jnp.abs(rounded), 1e-30)
    exponent = jnp.floor(jnp.log(size) * (1.0 / LN2))
    return jnp.round(rounded * jnp.exp((10.0 - exponent) * LN2)), exponent


def decode_rounded(mantissa, exponent):
    return (mantissa * jnp.exp((exponent - 10.0) * LN2)).astype(BF16).astype(F32)


def send_piece(out, head, values):
    exponent, fraction = fit_scale(jnp.max(jnp.abs(values), axis=0, keepdims=True))
    head[0:1, :] = exponent
    head[1:2, :] = fraction
    top = head.shape[0]
    out[:top, :] = to_short(head[...])
    out[top:, :] = quantize(values, exponent, fraction)


def y_position():
    return lax.axis_index("narrow") * lax.axis_size("pair") + lax.axis_index("pair")


def halves(table):
    high = table.astype(jnp.bfloat16)
    return high, (table - high.astype(np.float64)).astype(jnp.bfloat16)


def tables(y_count, pair, span_y):
    depth = GRID // y_count
    reach = span_y + 4
    waves = np.arange(GRID)
    step = 2.0 * np.pi / GRID
    z_table = cas(step * np.outer(np.arange(REGION), waves))
    z_forward = np.zeros((y_count, 2 * REGION, 2 * HALF))
    z_inverse = np.zeros((y_count, 2 * HALF, 2 * REGION))
    symbols = 4.0 * np.sin(np.pi * waves / GRID) ** 2
    shift = np.full((y_count, GRID, 2 * HALF), 1.0)
    y_forward = np.zeros((GRID, y_count, up_to(reach, 8)))
    y_inverse = np.zeros((y_count, up_to(reach, 16), GRID))
    for block in range(y_count):
        mine = z_table[:, block * depth : (block + 1) * depth]
        for half in range(2):
            rows = slice(half * REGION, (half + 1) * REGION)
            lanes = slice(half * HALF, half * HALF + depth)
            z_forward[block, rows, lanes] = mine
            z_inverse[block, lanes, rows] = mine.T / GRID
            shift[block, :, lanes] = (
                SCREEN + symbols[:, None] + symbols[None, block * depth : (block + 1) * depth]
            )
        cells = block * span_y - 2 + np.arange(reach)
        y_table = cas(step * np.outer(waves, cells))
        y_forward[:, block, :reach] = y_table
        y_inverse[block, :reach] = y_table.T / GRID
    y_forward = y_forward.reshape(GRID, y_count // pair, pair, -1).transpose(2, 0, 1, 3)
    y_forward = halves(y_forward.reshape(pair, GRID, -1))
    y_forward = np.concatenate([y_forward[0], y_forward[0], y_forward[1]], axis=2)
    root = np.sqrt(shift * (shift + 4.0))
    decay = 2.0 / (2.0 + shift + root)
    log_decay = np.log(decay)
    ring = 1.0 / (1.0 - np.exp(GRID * log_decay))
    gain = KERNEL_GAIN / root
    modes = np.stack([decay, log_decay, ring, gain], axis=1).astype(np.float32)
    return (
        halves(z_forward),
        halves(z_inverse),
        y_forward,
        halves(y_inverse),
        modes,
    )


def mixing_matrix():
    place = lax.broadcasted_iota(jnp.int32, (4 * BLOCK, 4 * BLOCK), 0)
    lane = lax.broadcasted_iota(jnp.int32, (4 * BLOCK, 4 * BLOCK), 1)
    return jnp.where(lane == 4 * (place % BLOCK) + place // BLOCK, 1.0, 0.0).astype(BF16)


def weave(tiles, mixing, out):
    weights = jnp.concatenate([jnp.concatenate(tile, axis=1) for tile in tiles], axis=0)
    first, rest = split(weights)
    second, third = split(weights - first.astype(F32))
    woven = dot(first, mixing) + (dot(second, mixing) + dot(third, mixing))
    for tile in range(len(tiles)):
        for part in range(BLOCK // GROUP):
            at = (tile * (BLOCK // GROUP) + part) * 16
            lanes = slice(part * BLOCK, (part + 1) * BLOCK)
            for a in range(4):
                row = tile * 16 + 4 * a
                out[pl.ds(at + 8 * (a // 2) + a % 2, 4, stride=2), :] = woven[row : row + 4, lanes]


def by_depth(ref):
    return [ref[pl.ds(depth, 16, stride=4), :] for depth in range(4)]


def pair_rows(x, reach_x, reach_y):
    even = (x // 2) * 2 * reach_y + x % 2
    if x == 0 or x == reach_x - 1:
        return [even]
    return [even, reach_x * reach_y + ((x - 1) // 2) * 2 * reach_y + (x - 1) % 2]


def pair_count(reach_x, reach_y):
    return (2 * reach_x - 2) * reach_y


def in_window(lanes, depth):
    return ((lanes - depth) & -4) == 0


def add_panels(reach, woven, vector_ref, place_ref, weight_ref, grids):
    lanes = lax.broadcasted_iota(jnp.int32, (8, REGION), 1)

    def body(group, carry):
        at = pl.multiple_of(group * 16, 16)
        coeff = [weight_ref[pl.ds(at + 8 * q, 8), :] for q in range(2)] if woven else None
        for local in range(GROUP):
            panel = group * GROUP + local
            grid = grids[local % len(grids)]
            row = place_ref[0, panel]
            value = vector_ref[panel]
            if woven:
                depth = place_ref[1, panel]
                shift = (depth - 4 * local) & (REGION - 1)
                value = jnp.where(in_window(lanes, depth), value, 0.0)
                lines = [pltpu.roll(coeff[q], shift, 1) for q in range(2)]
            else:
                first = pl.multiple_of(panel * 16, 16)
                lines = [weight_ref[pl.ds(first + 8 * q, 8), :] for q in range(2)]
            places = [pl.ds(row, 8), pl.ds(row + 2 * reach, 8)]
            held = [grid[place, :] for place in places]
            for q in range(2):
                grid[places[q], :] = held[q] + lines[q] * value
        return carry

    lax.fori_loop(0, vector_ref.shape[0] // GROUP, body, 0)


def send_pieces(outs, flips, head, rounded, both, high_ref, low_ref):
    blocks = rounded.shape[0]
    mantissa, exponent = encode_rounded(rounded)
    head[...] = jnp.zeros_like(head)
    head[2 : 2 + blocks, :] = mantissa
    head[2 + blocks : 2 + 2 * blocks, :] = exponent
    mine = y_position()
    for at in range(0, len(flips), 2):
        pick = lambda ref: jnp.concatenate([ref[mine ^ flip] for flip in flips[at : at + 2]], axis=1)
        result = dot_three(both, (pick(high_ref), pick(low_ref)))
        for i, out in enumerate(outs[at : at + 2]):
            send_piece(out, head, result[:, i * 2 * HALF : (i + 1) * 2 * HALF])


def spread_grid(reach_x, reach_y, rounded, tables, outs, flips, wides, head, total, grids):
    for x in range(reach_x):
        parts = [
            grid[pl.ds(row, reach_y, stride=2), :]
            for row in pair_rows(x, reach_x, reach_y)
            for grid in grids
        ]
        total[x * reach_y : (x + 1) * reach_y, :] = sum(parts[1:], parts[0])
    half = reach_x * reach_y // 2
    both = jnp.concatenate([total[:half, :], total[half:, :]], axis=1)
    extra = wides[0].shape[0] - half
    if extra:
        both = jnp.concatenate([both, jnp.zeros((extra, 2 * REGION), F32)], axis=0)
    both = split(both)
    for wide, values in zip(wides, both):
        wide[...] = values
    send_pieces(outs, flips, head, rounded, both, *tables)


def start_kernel(reach_x, reach_y, flips, *refs):
    vector_ref, *remote = refs[:8]
    refs = refs[8:]
    outs, refs = refs[: len(flips)], refs[len(flips) :]
    wides, (weight_ref, places_out), refs = refs[:2], refs[2:4], refs[4:]
    rounded, high, low, stencil, flag, samples, dipoles = refs[:7]
    place_ref, sems, head, total = refs[7:11]
    grids = refs[11:]
    tiles = samples.shape[0]
    copies = []
    fetch = lambda source, target: copies.append(
        pltpu.make_async_copy(source, target, sems.at[len(copies)])
    )
    rounded_in, high_in, low_in, stencil_in, flag_in, sample_in, dipole_in = remote
    fetch(stencil_in, stencil)
    fetch(flag_in, flag)
    for tile in range(tiles):
        lanes = pl.ds(tile * BLOCK, BLOCK)
        fetch(sample_in.at[:, lanes], samples.at[tile])
        fetch(dipole_in.at[:, lanes], dipoles.at[tile])
    needed_first = len(copies)
    fetch(rounded_in, rounded)
    fetch(high_in, high)
    fetch(low_in, low)
    for copy in copies:
        copy.start()
    for grid in grids:
        grid[...] = jnp.zeros_like(grid)
    mixing = mixing_matrix()
    copies[0].wait()
    span_x, span_y = reach_x - 4, reach_y - 4
    local_x = stencil[0:1, :] - (lax.axis_index("wide") * span_x - 2)
    local_y = stencil[1:2, :] - (y_position() * span_y - 2)
    odd = local_x & 1
    places_out[0:1, :] = odd * (reach_x * reach_y) + (local_x >> 1) * (2 * reach_y) + 2 * local_y
    places_out[1:2, :] = stencil[2:3, :]
    to_scalar = pltpu.make_async_copy(places_out, place_ref, sems.at[len(copies)])
    to_scalar.start()
    for copy in copies[1:needed_first]:
        copy.wait()
    sources = []
    for tile in range(tiles):
        charged = flag[:, tile * BLOCK : (tile + 1) * BLOCK] == 1
        pairs = zip(by_depth(samples.at[tile]), by_depth(dipoles.at[tile]))
        sources.append([jnp.where(charged, -sample, dipole) for sample, dipole in pairs])
    weave(sources, mixing, weight_ref)
    to_scalar.wait()
    add_panels(reach_y, True, vector_ref, place_ref, weight_ref, grids)
    for copy in copies[needed_first:]:
        copy.wait()
    spread_grid(
        reach_x, reach_y, rounded[...], (high, low), outs, flips, wides, head, total, grids
    )


def spread_kernel(reach_x, reach_y, flips, *refs):
    vector_ref, place_ref, rounded_ref, high_ref, low_ref, line_ref = refs[:6]
    refs = refs[6:]
    outs, wides, (head, total), grids = (
        refs[: len(flips)],
        refs[len(flips) : len(flips) + 2],
        refs[len(flips) + 2 : len(flips) + 4],
        refs[len(flips) + 4 :],
    )
    for grid in grids:
        grid[...] = jnp.zeros_like(grid)
    add_panels(reach_y, False, vector_ref, place_ref, line_ref, grids)
    spread_grid(
        reach_x,
        reach_y,
        rounded_ref[...],
        (high_ref, low_ref),
        outs,
        flips,
        wides,
        head,
        total,
        grids,
    )


def spread(vector, table, placed, raw, reach_x, reach_y, flips):
    count = vector.shape[0]
    half = reach_x * reach_y // 2
    blocks = count // BLOCK
    top = up_to(2 + 2 * blocks, 16)
    lanes = 2 * HALF
    body = up_to(half, 16)
    woven = (count // GROUP * 16, BLOCK)
    out_shapes = [jax.ShapeDtypeStruct((top + body, lanes), jnp.int16)] * len(flips)
    out_shapes += [jax.ShapeDtypeStruct((body, 2 * REGION), BF16)] * 2
    rounded = vector.reshape(blocks, BLOCK)
    work = [
        pltpu.VMEM((top, lanes), F32),
        pltpu.VMEM((reach_x * reach_y, REGION), F32),
    ] + [pltpu.VMEM((pair_count(reach_x, reach_y), REGION), F32)] * CHAINS
    if placed is None:
        stencil, flag, sample, dipole = raw
        operands = [vector, rounded, *table, stencil, flag.reshape(1, -1), sample, dipole]
        pinned = [pltpu.with_memory_space_constraint(value, pltpu.HBM) for value in operands[1:]]
        operands = [vector] + pinned
        in_specs = [in_smem()] + [pl.BlockSpec(memory_space=pltpu.HBM)] * 7
        out_shapes += [jax.ShapeDtypeStruct(woven, F32)]
        out_shapes += [jax.ShapeDtypeStruct((2, count), jnp.int32)]
        out_shapes += [jax.ShapeDtypeStruct(rounded.shape, F32)]
        out_shapes += [jax.ShapeDtypeStruct(values.shape, BF16) for values in table]
        tiled = pltpu.VMEM((blocks, 64, BLOCK), F32)
        work = [
            pltpu.VMEM(stencil.shape, jnp.int32),
            pltpu.VMEM((1, count), jnp.int32),
            tiled,
            tiled,
            pltpu.SMEM((2, count), jnp.int32),
            pltpu.SemaphoreType.DMA((6 + 2 * blocks,)),
        ] + work
    else:
        operands = [vector, placed[0], rounded, *table, placed[1]]
        in_specs = [in_smem()] * 2 + [whole_vmem()] * 4
    return pl.pallas_call(
        functools.partial(
            start_kernel if placed is None else spread_kernel, reach_x, reach_y, flips
        ),
        in_specs=in_specs,
        out_specs=[whole_vmem()] * len(out_shapes),
        out_shape=out_shapes,
        scratch_shapes=work,
        compiler_params=pltpu.CompilerParams(
            vmem_limit_bytes=START_LIMIT if placed is None else VMEM_LIMIT
        ),
        cost_estimate=cost(2 * half * 256 * 512, 4 * 16 * count * REGION),
        name="start" if placed is None else "spread",
    )(*operands)


def spread_rest_kernel(flips, rounded_ref, wide_high, wide_low, high_ref, low_ref, *refs):
    outs, head = refs[:-1], refs[-1]
    both = (wide_high[...], wide_low[...])
    send_pieces(outs, flips, head, rounded_ref[...], both, high_ref, low_ref)


def spread_rest(rounded, both, table, flips):
    blocks = rounded.shape[0]
    top = up_to(2 + 2 * blocks, 16)
    shape = (top + both[0].shape[0], 2 * HALF)
    return pl.pallas_call(
        functools.partial(spread_rest_kernel, flips),
        in_specs=[whole_vmem()] * 5,
        out_specs=[whole_vmem()] * len(flips),
        out_shape=[jax.ShapeDtypeStruct(shape, jnp.int16)] * len(flips),
        scratch_shapes=[pltpu.VMEM((top, 2 * HALF), F32)],
        compiler_params=params(),
        cost_estimate=cost(2 * shape[0] * 256 * 256 * 3, 4 * shape[0] * 512),
        name="spread_rest",
    )(rounded, *both, *table)


def lines_kernel(place_ref, coeff_ref, *refs):
    out_ref = refs[-1]
    lanes = lax.broadcasted_iota(jnp.int32, (8, REGION), 1)

    def body(group, carry):
        at = pl.multiple_of(group * 16, 16)
        coeff = [coeff_ref[pl.ds(at + 8 * q, 8), :] for q in range(2)]
        for local in range(GROUP):
            panel = group * GROUP + local
            depth = place_ref[1, panel]
            shift = (depth - 4 * local) & (REGION - 1)
            inside = in_window(lanes, depth)
            for q in range(2):
                first = pl.multiple_of(panel * 16 + 8 * q, 8)
                out_ref[pl.ds(first, 8), :] = jnp.where(inside, pltpu.roll(coeff[q], shift, 1), 0.0)
        return carry

    lax.fori_loop(0, place_ref.shape[1] // GROUP, body, 0)


def sample_lines_kernel(tiles, place_ref, *refs):
    out_ref, coeff = refs[-2:]
    weave([by_depth(ref) for ref in refs[:tiles]], mixing_matrix(), coeff)
    lines_kernel(place_ref, coeff, out_ref)


def place_sample_lines(places, sample):
    count = places.shape[1]
    blocks = count // BLOCK
    tile = lambda t: pl.BlockSpec((64, BLOCK), lambda i: (0, t))
    shape = (count * 16, REGION)
    return pl.pallas_call(
        functools.partial(sample_lines_kernel, blocks),
        grid=(1,),
        in_specs=[in_smem()] + [tile(t) for t in range(blocks)],
        out_specs=pl.BlockSpec(shape, lambda i: (0, 0)),
        out_shape=jax.ShapeDtypeStruct(shape, F32),
        scratch_shapes=[pltpu.VMEM((count // GROUP * 16, BLOCK), F32)],
        compiler_params=params(),
        cost_estimate=cost(16 * count * REGION, 4 * 16 * count * REGION),
        name="place_sample_lines",
    )(places, *[sample] * blocks)


def place_lines(places, coeff, awaited):
    count = places.shape[1]
    shape = (count * 16, REGION)
    return pl.pallas_call(
        lines_kernel,
        in_specs=[in_smem(), whole_vmem()] + [anywhere()] * len(awaited),
        out_specs=whole_vmem(),
        out_shape=jax.ShapeDtypeStruct(shape, F32),
        compiler_params=params(),
        cost_estimate=cost(16 * count * REGION, 4 * 16 * count * REGION),
        name="place_lines",
    )(places, coeff, *awaited)


def put_edges(opened, reach_x, reach_y, edges, first):
    half = reach_x // 2
    low = low_lanes(reach_y)
    layer = lambda i: opened[i * reach_y : (i + 1) * reach_y, :]
    for two in range(2):
        place = slice(first + two * reach_y, first + (two + 1) * reach_y)
        edges[0, place, :] = jnp.where(low, layer(2 * two), swap(layer(2 * two + 1)))
        last = half - 4 + 2 * two
        edges[1, place, :] = jnp.where(low, swap(layer(last)), layer(last + 1))


def stack_layers(layers, at, reach_y, stacked):
    tall = stacked.shape[0] // len(layers)
    place = at * up_to(reach_y, 8)
    for i, layer in enumerate(layers):
        stacked[pl.ds(pl.multiple_of(i * tall + place, 8), reach_y), :] = layer


def stack_pieces(parts, reach_x, reach_y, top, opened, stacked, edges, places):
    chip = lax.axis_index("narrow")
    for flip, (part, place) in enumerate(zip(parts, places)):
        first = from_short(part[:top, :])
        opened[...] = from_short(part[top:, :]) * unit(first[0:1], first[1:2])
        layers = [opened[i * reach_y : (i + 1) * reach_y, :] for i in range(reach_x // 2)]
        stack_layers(layers, chip ^ flip, reach_y, stacked)
        put_edges(opened, reach_x, reach_y, edges, place * 2 * reach_y)


def transform_pieces(table, stacked, before, spectrum):
    half = spectrum.shape[0]
    tall = stacked.shape[0] // half

    def tripled(values):
        high, low = split(values)
        return jnp.concatenate([high, low, high], axis=0)

    for i in range(0, half, 2):
        places = range(i, min(i + 2, half))
        held = jnp.concatenate([stacked[j * tall : (j + 1) * tall, :] for j in places], axis=1)
        result = dot(table, tripled(held))
        for j in places:
            made = result[:, (j - i) * 2 * HALF : (j - i + 1) * 2 * HALF]
            spectrum[j] = made if before is None else before[j] + made


def forward_early_kernel(reach_x, reach_y, chips, *refs):
    parts = refs[:chips]
    table_ref, spectrum, edges, opened, stacked = refs[chips:]
    top = parts[0].shape[0] - opened.shape[0]
    stacked[...] = jnp.zeros_like(stacked)
    stack_pieces(parts, reach_x, reach_y, top, opened, stacked, edges, range(chips))
    transform_pieces(table_ref[lax.axis_index("pair")], stacked, None, spectrum)


def stacking_scratch(chips, reach_x, reach_y):
    half = reach_x // 2
    return [
        pltpu.VMEM((up_to(half * reach_y, 16), 2 * HALF), F32),
        pltpu.VMEM((half * chips * up_to(reach_y, 8), 2 * HALF), F32),
    ]


def forward_early(parts, table, reach_x, reach_y):
    half = reach_x // 2
    chips = len(parts)
    return pl.pallas_call(
        functools.partial(forward_early_kernel, reach_x, reach_y, chips),
        in_specs=[whole_vmem()] * (chips + 1),
        out_specs=[whole_vmem()] * 2,
        out_shape=[
            jax.ShapeDtypeStruct((half, GRID, 2 * HALF), F32),
            jax.ShapeDtypeStruct((2, chips * 2 * reach_y, 2 * HALF), F32),
        ],
        scratch_shapes=stacking_scratch(chips, reach_x, reach_y),
        compiler_params=params(),
        cost_estimate=cost(EARLY_FLOPS, 4 * half * GRID * 2 * HALF * 2),
        name="forward_early",
    )(*parts, table)


def forward_kernel(reach_x, reach_y, blocks, pieces, awaited, *refs):
    parts = refs[:pieces]
    early_ref, early_edges, table_ref, modes_ref = refs[pieces : pieces + 4]
    refs = refs[pieces + 4 + awaited :]
    spectrum, even_out, layers_out, odd_out, own_out, peers_out, inner_out, *refs = refs
    opened, stacked, edges, slabs, head = refs
    half = reach_x // 2
    pair = lax.axis_size("pair")
    top = parts[0].shape[0] - opened.shape[0]
    stacked[...] = jnp.zeros_like(stacked)
    head[...] = jnp.zeros_like(head)
    for piece in range(pieces):
        first = from_short(parts[piece][:top, :])
        mantissa, exponent = first[2 : 2 + blocks], first[2 + blocks : 2 + 2 * blocks]
        peers_out[piece * blocks : (piece + 1) * blocks, :] = decode_rounded(mantissa, exponent)
        at = 6 + 2 * piece * blocks
        head[at : at + blocks, :] = mantissa
        head[at + blocks : at + 2 * blocks, :] = exponent
    rows = 2 * reach_y
    for chip in range(pieces // pair):
        place = chip * pair * rows
        edges[:, place : place + rows, :] = early_edges[:, chip * rows : (chip + 1) * rows, :]
    before = early_ref
    for core in range(1, pair):
        places = range(core, pieces, pair)
        stack_pieces(parts[core::pair], reach_x, reach_y, top, opened, stacked, edges, places)
        transform_pieces(table_ref[lax.axis_index("pair") ^ core], stacked, before, spectrum)
        before = spectrum

    chunk = 32

    def body(index, largest):
        rows = pl.ds(pl.multiple_of(index * chunk, chunk), chunk)
        low = low_lanes(chunk)
        decay = modes_ref[0, rows, :]
        log_decay = modes_ref[1, rows, :]
        across_half = jnp.exp(half * log_decay)
        across_cut = jnp.exp((half - 4) * log_decay)
        layers = [spectrum[i, rows, :] for i in range(half)]
        run = layers[0]
        cut_right = run
        for i in range(1, half):
            run = decay * run + layers[i]
            if i == half - 5:
                cut_right = run
        right = run
        run = layers[half - 1]
        cut_left = run
        for i in range(half - 2, -1, -1):
            run = decay * run + layers[i]
            if i == 4:
                cut_left = run
        left = run
        inner_out[rows, :] = jnp.where(low, right, left)
        swapped_right, swapped_left = swap(right), swap(left)
        own = jnp.where(low, left + across_half * swapped_left, right + across_half * swapped_right)
        own_out[rows, :] = own
        made = [
            jnp.where(low, own, cut_right + across_cut * swapped_right),
            jnp.where(low, cut_left + across_cut * swapped_left, own),
        ]
        for slab, values in enumerate(made):
            slabs[slab, rows, :] = values
        return tuple(
            jnp.maximum(old, jnp.max(jnp.abs(values).reshape(chunk // 8, 8, 2 * HALF), axis=0))
            for old, values in zip(largest, made)
        )

    zero = jnp.zeros((8, 2 * HALF), F32)
    largest = lax.fori_loop(0, GRID // chunk, body, (zero,) * 2)
    top = head.shape[0]
    low = low_lanes(GRID // 2)
    upper, lower = own_out[: GRID // 2, :], own_out[GRID // 2 :, :]
    packed = [jnp.where(low, swap(upper), lower), jnp.where(low, upper, swap(lower))]

    def send(out, first, parts):
        place = first
        for index, (values, most) in enumerate(parts):
            exponent, fraction = fit_scale(jnp.max(most, axis=0, keepdims=True))
            head[2 * index : 2 * index + 1, :] = exponent
            head[2 * index + 1 : 2 * index + 2, :] = fraction
            out[place : place + values.shape[0], :] = quantize(values, exponent, fraction)
            place += values.shape[0]
        out[:first, :] = to_short(head[:first, :])

    with_most = lambda values: (values, jnp.abs(values))
    on_left = lax.axis_index("wide") & 1
    for side, (even, odd) in enumerate(((0, 1), (1, 0))):

        @pl.when(on_left == side)
        def _():
            send(even_out, top, [(slabs[even], largest[even]), with_most(packed[even])])
            send(layers_out, 16, [with_most(edges[1 - even])])
            send(odd_out, top, [(slabs[odd], largest[odd]), with_most(edges[1 - odd])])


def forward(parts, early, early_edges, table, modes, reach_x, reach_y, blocks, awaited):
    pieces = len(parts)
    half = reach_x // 2
    lanes = 2 * HALF
    head = up_to(6 + 2 * pieces * blocks, 16)
    border = pieces * 2 * reach_y
    short = lambda rows: jax.ShapeDtypeStruct((rows, lanes), jnp.int16)
    return pl.pallas_call(
        functools.partial(
            forward_kernel, reach_x, reach_y, blocks, pieces, len(awaited)
        ),
        in_specs=[whole_vmem()] * (pieces + 4) + [anywhere()] * len(awaited),
        out_specs=[whole_vmem()] * 7,
        out_shape=[
            jax.ShapeDtypeStruct((half, GRID, lanes), F32),
            short(head + GRID + GRID // 2),
            short(16 + border),
            short(head + GRID + border),
            jax.ShapeDtypeStruct((GRID, lanes), F32),
            jax.ShapeDtypeStruct((pieces * blocks, BLOCK), F32),
            jax.ShapeDtypeStruct((GRID, lanes), F32),
        ],
        scratch_shapes=stacking_scratch(pieces // table.shape[0], reach_x, reach_y)
        + [
            pltpu.VMEM((2, border, lanes), F32),
            pltpu.VMEM((2, GRID, lanes), F32),
            pltpu.VMEM((head, lanes), F32),
        ],
        compiler_params=params(),
        cost_estimate=cost(2 * half * 256 * 256 * 128, 4 * half * GRID * lanes * 2),
        name="forward",
    )(*parts, early, early_edges, table, modes, *awaited)


def opened_part(ref, index, first, rows):
    head = from_short(ref[:16, :])
    scale = unit(head[2 * index : 2 * index + 1], head[2 * index + 1 : 2 * index + 2])
    return from_short(ref[first : first + rows, :]) * scale


def pair_kernel(reach_x, flips, own_ref, even_ref, modes_ref, *refs):
    outs, head = refs[:-1], refs[-1]
    span = reach_x - 4
    here = lax.axis_index("wide")
    low = low_lanes(GRID)
    log_decay = modes_ref[1]
    own = own_ref[...]
    top = even_ref.shape[0] - GRID - GRID // 2
    cut = opened_part(even_ref, 0, top, GRID)
    packed = opened_part(even_ref, 1, top + GRID, GRID // 2)
    from_left = jnp.where(low, cut, jnp.concatenate([swap(packed), packed], axis=0))
    from_right = jnp.where(low, jnp.concatenate([packed, swap(packed)], axis=0), cut)
    partner = jnp.where((here & 1) == 1, from_left, from_right)

    def weight(distances):
        powers = []
        for distance in distances:
            ahead = span * distance - reach_x
            powers.append(jnp.where(distance >= 2, ahead, ahead + GRID).astype(F32))
        return jnp.exp(jnp.where(low, *powers) * log_decay)

    head[...] = jnp.zeros_like(head)
    for flip, out in zip(flips, outs):
        behind = (here ^ flip) - here
        message = own * weight((-behind, behind))
        behind = (here ^ flip) - (here ^ 1)
        beside = jnp.where(jnp.abs(behind) == 1, 0.0, 1.0)
        send_piece(out, head, message + partner * (weight((-behind, behind)) * beside))


def pair_messages(own, from_even, modes, reach_x, flips):
    return pl.pallas_call(
        functools.partial(pair_kernel, reach_x, flips),
        in_specs=[whole_vmem()] * 3,
        out_specs=[whole_vmem()] * len(flips),
        out_shape=[jax.ShapeDtypeStruct((16 + GRID, 2 * HALF), jnp.int16)] * len(flips),
        scratch_shapes=[pltpu.VMEM((16, 2 * HALF), F32)],
        compiler_params=params(),
        cost_estimate=cost(16 * GRID * 2 * HALF, 4 * GRID * 2 * HALF * (6 + len(flips))),
        name="pair_messages",
    )(own, from_even, modes)


def borders_kernel(reach_y, pieces, layers_ref, odd_ref, table_ref, out_ref, stacked, partial):
    on_left = (lax.axis_index("wide") & 1) == 1
    pair = lax.axis_size("pair")
    rows = pieces * 2 * reach_y
    even = opened_part(layers_ref, 0, 16, rows)
    odd = opened_part(odd_ref, 1, odd_ref.shape[0] - rows, rows)
    left, right = jnp.where(on_left, even, odd), jnp.where(on_left, odd, even)
    low = low_lanes(rows)
    both = [jnp.where(low, left, swap(right)), jnp.where(low, swap(left), right)]
    core = lax.axis_index("pair")
    chip = lax.axis_index("narrow")
    stacked[...] = jnp.zeros_like(stacked)
    before = None
    for other in range(pair):
        for flip in range(pieces // pair):
            first = (flip * pair + other) * 2 * reach_y
            layers = [
                values[first + two * reach_y : first + (two + 1) * reach_y]
                for two in range(2)
                for values in both
            ]
            stack_layers(layers, chip ^ flip, reach_y, stacked)
        target = out_ref if other == pair - 1 else partial
        transform_pieces(table_ref[core ^ other], stacked, before, target)
        before = target


def borders(layers, from_odd, table, reach_y, pieces):
    chips = pieces // table.shape[0]
    shape = (4, GRID, 2 * HALF)
    return pl.pallas_call(
        functools.partial(borders_kernel, reach_y, pieces),
        in_specs=[whole_vmem()] * 3,
        out_specs=whole_vmem(),
        out_shape=jax.ShapeDtypeStruct(shape, F32),
        scratch_shapes=[
            pltpu.VMEM((4 * chips * up_to(reach_y, 8), 2 * HALF), F32),
            pltpu.VMEM(shape, F32),
        ],
        compiler_params=params(),
        cost_estimate=cost(2 * 4 * 256 * 256 * 128, 4 * 6 * GRID * 2 * HALF),
        name="borders",
    )(layers, from_odd, table)


def send_fields(outs, flips, reach_y, field_high, field_low, high_ref, low_ref, ready, head):
    half = field_high.shape[0]
    mine = y_position()
    pitch = up_to(reach_y, 16)
    pick = lambda ref: jnp.concatenate([ref[mine ^ flip] for flip in flips], axis=0)
    table = (pick(high_ref), pick(low_ref))
    for i in range(0, half, 2):
        many = min(2, half - i)
        join = lambda ref: jnp.concatenate([ref[i + j] for j in range(many)], axis=1)
        result = dot_three(table, (join(field_high), join(field_low)))
        for j in range(many):
            for piece in range(len(flips)):
                ready[piece, (i + j) * reach_y : (i + j + 1) * reach_y, :] = result[
                    piece * pitch : piece * pitch + reach_y, j * 2 * HALF : (j + 1) * 2 * HALF
                ]
    head[...] = jnp.zeros_like(head)
    for piece, out in enumerate(outs):
        if ready.shape[1] > half * reach_y:
            ready[piece, half * reach_y :, :] = jnp.zeros_like(ready[piece, half * reach_y :, :])
        send_piece(out, head, ready[piece])


def inverse_kernel(reach_x, reach_y, flips, fars, *refs):
    spectrum, border_ref, from_even, from_odd, own_ref, inner_ref, *far_refs = refs[: 6 + fars]
    refs = refs[6 + fars :]
    high_ref, low_ref, modes_ref = refs[:3]
    outs = refs[3 : 3 + len(flips)]
    field_high, field_low, ready, head = refs[3 + len(flips) :]
    half = reach_x // 2
    span = reach_x - 4
    chunk = 32
    head_rows = from_even.shape[0] - GRID - GRID // 2
    on_left = (lax.axis_index("wide") & 1) == 1
    moment_units = []
    for ref in (from_even, from_odd):
        first = from_short(ref[:16, :])
        moment_units.append(unit(first[0:1], first[1:2]))

    far_units = []
    for ref in far_refs:
        first = from_short(ref[:16, :])
        far_units.append(unit(first[0:1], first[1:2]))

    def body(index, carry):
        first = pl.multiple_of(index * chunk, chunk)
        rows = pl.ds(first, chunk)
        low = low_lanes(chunk)
        decay = modes_ref[0, rows, :]
        log_decay = modes_ref[1, rows, :]
        ring = modes_ref[2, rows, :]
        gain = modes_ref[3, rows, :]
        across_half = jnp.exp(half * log_decay)
        across_cut = jnp.exp((half - 4) * log_decay)
        around = jnp.exp((GRID - 4) * log_decay)
        beside = jnp.exp((GRID - reach_x - span) * log_decay)
        layers = [spectrum[i, rows, :] for i in range(half)]

        at = pl.ds(pl.multiple_of(head_rows + index * chunk, 16), chunk)
        even, odd = (
            from_short(ref[at, :]) * scale for ref, scale in zip((from_even, from_odd), moment_units)
        )
        left_moments, right_moments = jnp.where(on_left, even, odd), jnp.where(on_left, odd, even)
        border = [border_ref[i, rows, :] for i in range(4)]
        zero = jnp.zeros_like(decay)
        head_sum = border[0]
        for i in range(1, 4):
            head_sum = decay * head_sum + border[i]
        tail_sum = border[3]
        for i in range(2, -1, -1):
            tail_sum = decay * tail_sum + border[i]
        for i in range(4):
            layers[i] = layers[i] + jnp.where(low, border[i], zero)
        for i in range(4):
            place = half - 4 + i
            layers[place] = layers[place] + jnp.where(low, zero, border[i])
        total = own_ref[rows, :] * jnp.exp((GRID - reach_x) * log_decay)
        at = pl.ds(pl.multiple_of(16 + index * chunk, 16), chunk)
        for ref, scale in zip(far_refs, far_units):
            total = total + from_short(ref[at, :]) * scale
        one = jnp.ones_like(decay)
        total = total + left_moments * jnp.where(low, beside, one)
        total = total + right_moments * jnp.where(low, one, beside)
        shared = jnp.where(low, head_sum, tail_sum)
        entering = (swap(total) + around * shared) * ring
        leaving = swap(across_half * entering + across_cut * shared + inner_ref[rows, :])
        run = jnp.where(low, entering, leaving)
        forward_runs = []
        for i in range(half):
            run = decay * run + layers[i]
            forward_runs.append(run)
        run = jnp.where(low, leaving, entering)
        for i in range(half - 1, -1, -1):
            ahead = decay * run
            high, rest = split(gain * (forward_runs[i] + ahead))
            field_high[i, rows, :] = high
            field_low[i, rows, :] = rest
            run = ahead + layers[i]
        return carry

    lax.fori_loop(0, GRID // chunk, body, 0)
    send_fields(outs, flips, reach_y, field_high, field_low, high_ref, low_ref, ready, head)


def inverse(
    spectrum, border, from_even, from_odd, own, inner, fars, table, modes, reach_x, reach_y, flips
):
    half = reach_x // 2
    lanes = 2 * HALF
    body = up_to(half * reach_y, 16)
    shapes = [jax.ShapeDtypeStruct((16 + body, lanes), jnp.int16)] * len(flips)
    shapes += [jax.ShapeDtypeStruct((half, GRID, lanes), BF16)] * 2
    return pl.pallas_call(
        functools.partial(inverse_kernel, reach_x, reach_y, flips, len(fars)),
        in_specs=[whole_vmem()] * (9 + len(fars)),
        out_specs=[whole_vmem()] * len(shapes),
        out_shape=shapes,
        scratch_shapes=[
            pltpu.VMEM((len(flips), body, lanes), F32),
            pltpu.VMEM((16, lanes), F32),
        ],
        compiler_params=params(),
        cost_estimate=cost(2 * half * 256 * 256 * 128, 4 * half * GRID * lanes * 2),
        name="inverse",
    )(spectrum, border, from_even, from_odd, own, inner, *fars, *table, modes)


def inverse_rest_kernel(reach_y, flips, field_high, field_low, high_ref, low_ref, *refs):
    outs, (ready, head) = refs[: len(flips)], refs[len(flips) :]
    send_fields(outs, flips, reach_y, field_high, field_low, high_ref, low_ref, ready, head)


def inverse_rest(field, table, reach_y, flips):
    half = field[0].shape[0]
    lanes = 2 * HALF
    body = up_to(half * reach_y, 16)
    return pl.pallas_call(
        functools.partial(inverse_rest_kernel, reach_y, flips),
        in_specs=[whole_vmem()] * 4,
        out_specs=[whole_vmem()] * len(flips),
        out_shape=[jax.ShapeDtypeStruct((16 + body, lanes), jnp.int16)] * len(flips),
        scratch_shapes=[
            pltpu.VMEM((len(flips), body, lanes), F32),
            pltpu.VMEM((16, lanes), F32),
        ],
        compiler_params=params(),
        cost_estimate=cost(2 * half * 256 * 256 * 128, 4 * half * GRID * lanes * 2),
        name="inverse_rest",
    )(*field, *table)


def sum_rows(values):
    row = lax.broadcasted_iota(jnp.int32, values[0].shape, 0)
    for step in (4, 2, 1):
        low = (row & step) == 0
        paired = []
        for one, other in zip(values[: len(values) // 2], values[len(values) // 2 :]):
            kept = jnp.where(low, one, other)
            moved = jnp.where(low, other, one)
            if step == 4:
                moved = pltpu.roll(moved, 4, 0)
            else:
                moved = jnp.where(low, pltpu.roll(moved, 8 - step, 0), pltpu.roll(moved, step, 0))
            paired.append(kept + moved)
        values = paired
    return values[0]


def z_lines(parts, flips, high_ref, low_ref):
    mine = y_position()
    opened = []
    for part in parts:
        first = from_short(part[:16, :])
        opened.append(from_short(part[16:, :]) * unit(first[0:1], first[1:2]))
    values = split(jnp.concatenate(opened, axis=1))
    pick = lambda ref: jnp.concatenate([ref[mine ^ flip] for flip in flips], axis=0)
    return dot_three(values, (pick(high_ref), pick(low_ref)))


def sample_early_kernel(flips, *refs):
    *parts, high_ref, low_ref, out_ref = refs
    out_ref[...] = z_lines(parts, flips, high_ref, low_ref)


def sample_early(parts, flips, table):
    rows = parts[0].shape[0] - 16
    return pl.pallas_call(
        functools.partial(sample_early_kernel, flips),
        in_specs=[whole_vmem()] * (len(parts) + 2),
        out_specs=whole_vmem(),
        out_shape=jax.ShapeDtypeStruct((rows, 2 * REGION), F32),
        compiler_params=params(),
        cost_estimate=cost(EARLY_FLOPS, 4 * rows * 512),
        name="sample_early",
    )(*parts, *table)


def sample_kernel(last, reach_x, reach_y, flips, place_ref, *refs):
    parts = refs[: len(flips)]
    early_ref, high_ref, low_ref, line_ref, own_ref, vector_ref, near_ref, out_ref = refs[
        len(flips) : len(flips) + 8
    ]
    flat, field, sums = refs[len(flips) + 8 :]
    half_rows = reach_x * reach_y // 2
    both = early_ref[...] + z_lines(parts, flips, high_ref, low_ref)
    flat[:half_rows, :] = both[:half_rows, :REGION]
    flat[half_rows:, :] = both[:half_rows, REGION:]
    for x in range(reach_x):
        layer = flat[x * reach_y : (x + 1) * reach_y, :]
        for row in pair_rows(x, reach_x, reach_y):
            field[pl.ds(row, reach_y, stride=2), :] = layer
    count = place_ref.shape[1]

    def body(group, carry):
        for eight in range(0, GROUP, 8):
            totals = []
            for local in range(eight, eight + 8):
                panel = group * GROUP + local
                row = place_ref[0, panel]
                first = pl.multiple_of(panel * 16, 16)
                totals.append(
                    field[pl.ds(row, 8), :] * line_ref[pl.ds(first, 8), :]
                    + field[pl.ds(row + 2 * reach_y, 8), :] * line_ref[pl.ds(first + 8, 8), :]
                )
            sums[pl.ds(pl.multiple_of(group * GROUP + eight, 8), 8), :] = sum_rows(totals)
        return carry

    lax.fori_loop(0, count // GROUP, body, 0)
    sampled = lax.dot_general(
        jnp.ones((8, REGION), F32),
        sums[...],
        (((1,), (1,)), ((), ())),
        precision=lax.Precision.HIGHEST,
        preferred_element_type=F32,
    )
    for block in range(count // BLOCK):
        lane = slice(block * BLOCK, (block + 1) * BLOCK)
        row = slice(block, block + 1)
        vector = vector_ref[row, :]
        image = jnp.where(own_ref[row, :] == 1, 0.0, 0.5 * vector) + sampled[:1, lane]
        image = image + near_ref[row, :]
        if last:
            out_ref[0:1, lane] = vector
            out_ref[1:2, lane] = image
        else:
            out_ref[row, :] = image


def sample(last, places, parts, flips, early, table, lines, flag, vector, near, reach_x, reach_y):
    count = places.shape[1]
    blocks = count // BLOCK
    shape = (2, count) if last else (blocks, BLOCK)
    return pl.pallas_call(
        functools.partial(sample_kernel, last, reach_x, reach_y, flips),
        in_specs=[in_smem()] + [whole_vmem()] * (len(parts) + 7),
        out_specs=whole_vmem(),
        out_shape=jax.ShapeDtypeStruct(shape, F32),
        scratch_shapes=[
            pltpu.VMEM((reach_x * reach_y, REGION), F32),
            pltpu.VMEM((pair_count(reach_x, reach_y), REGION), F32),
            pltpu.VMEM((count, REGION), F32),
        ],
        compiler_params=params(),
        cost_estimate=cost(reach_x * reach_y * 256 * 512, 4 * 16 * count * REGION),
        name="sample",
    )(
        places,
        *parts,
        early,
        *table,
        lines,
        flag.reshape(blocks, BLOCK),
        vector.reshape(blocks, BLOCK),
        near,
    )


def near_kernel(slots, blocks, place_ref, target_ref, *refs):
    even_ref, odd_ref, peers_ref, tile_ref = refs[:4]
    out_ref, held = refs[-2:]
    count = peers_ref.shape[0]
    held[count : 2 * count, :] = peers_ref[...]
    on_left = lax.axis_index("wide") & 1
    for side, ref in ((1 - on_left, even_ref), (on_left, odd_ref)):
        top = from_short(ref[...])
        for piece in range(count // blocks):
            at = 6 + 2 * piece * blocks
            held[pl.ds(side * (2 * count) + piece * blocks, blocks), :] = decode_rounded(
                top[at : at + blocks], top[at + blocks : at + 2 * blocks]
            )
    out_ref[...] = jnp.zeros_like(out_ref)
    for slot in range(slots):
        picked = held[pl.ds(place_ref[slot], 1), :]
        picked = jnp.broadcast_to(picked, (16, BLOCK)).astype(BF16)
        product = lax.dot_general(
            picked,
            tile_ref[slot],
            (((1,), (1,)), ((), ())),
            preferred_element_type=F32,
        )
        target = pl.ds(target_ref[slot], 1)
        out_ref[target, :] = out_ref[target, :] + product[:1]


def near_field(places, targets, from_even, from_odd, peers, tiles, blocks, out_rows, awaited):
    slots = tiles.shape[0]
    head = up_to(6 + 2 * peers.shape[0], 16)
    constant = lambda shape: pl.BlockSpec(shape, lambda i: (0,) * len(shape))
    return pl.pallas_call(
        functools.partial(near_kernel, slots, blocks),
        grid=(1,),
        in_specs=[
            in_smem(),
            in_smem(),
            constant((head, BLOCK)),
            constant((head, BLOCK)),
            constant(peers.shape),
            constant(tiles.shape),
        ]
        + [anywhere()] * len(awaited),
        out_specs=constant((out_rows, BLOCK)),
        out_shape=jax.ShapeDtypeStruct((out_rows, BLOCK), F32),
        scratch_shapes=[pltpu.VMEM((3 * peers.shape[0], BLOCK), F32)],
        compiler_params=params(),
        cost_estimate=cost(2 * slots * 16 * BLOCK * BLOCK, 2 * slots * BLOCK * BLOCK),
        name="near_field",
    )(places, targets, from_even, from_odd, peers, tiles, *awaited)


def shards(
    density,
    surface_flag,
    stencil_base,
    sample_weights,
    dipole_weights,
    near_target,
    near_source,
    near_tiles,
):
    x_count = lax.axis_size("wide")
    y_count = lax.axis_size(Y_AXES)
    y_index = lax.axis_index(Y_AXES)
    pair = lax.axis_size("pair")
    span_x = REGION // x_count
    span_y = REGION // y_count
    reach_x = span_x + 4
    reach_y = span_y + 4
    count = density.shape[0]
    blocks = count // BLOCK

    z_forward, z_inverse, y_forward, y_inverse, modes = tables(y_count, pair, span_y)
    modes = lax.dynamic_index_in_dim(jnp.asarray(modes), y_index, 0, keepdims=False)

    neighbour = near_source // blocks
    flip = (y_index + neighbour % 3 - 1) ^ y_index
    sources = ((neighbour // 3) * y_count + flip) * blocks + near_source % blocks
    out_rows = up_to(blocks + 1, 8)
    live = near_target >= 0
    sources = jnp.where(live, sources, 0)
    targets = jnp.where(live, near_target, out_rows - 1)

    swaps = lambda pairs: [(i, j) for i, j in pairs] + [(j, i) for i, j in pairs]
    even_swap = swaps([(i, i + 1) for i in range(0, x_count - 1, 2)])
    odd_swap = swaps([(i, i + 1) for i in range(1, x_count - 1, 2)])
    far_flips = list(range(2, x_count, 2))

    first, rest = list(range(pair, y_count)), list(range(pair))
    same_core = list(range(0, y_count, pair))
    other_core = [flip for flip in range(y_count) if flip not in same_core]

    def turned(sent, then):
        arrived = [None] * y_count
        for flip, part in zip(first + rest, list(sent) + list(then)):
            swap_pairs = [(i, i ^ flip) for i in range(y_count)]
            arrived[flip] = part if flip == 0 else lax.ppermute(part, Y_AXES, swap_pairs)
        return arrived

    def chosen(parts, flips):
        return [parts[flip] for flip in flips]

    def convolve_and_sample(last, vector, sent, both, table, places, sample_lines, awaited):
        arrived = turned(sent, spread_rest(vector, both, table, rest))
        early, edges = forward_early(chosen(arrived, same_core), y_forward, reach_x, reach_y)
        spectrum, even_message, layers, odd_message, own, peers, inner = forward(
            arrived, early, edges, y_forward, modes, reach_x, reach_y, blocks, awaited
        )
        from_even = lax.ppermute(even_message, "wide", even_swap)
        from_odd = lax.ppermute(odd_message, "wide", odd_swap)
        even_layers = lax.ppermute(layers, "wide", even_swap)
        fars = [
            lax.ppermute(message, "wide", [(i, i ^ flip) for i in range(x_count)])
            for flip, message in zip(
                far_flips, pair_messages(own, from_even, modes, reach_x, far_flips)
            )
        ]
        *sent, high, low = inverse(
            spectrum,
            borders(even_layers, from_odd, y_forward, reach_y, y_count),
            from_even,
            from_odd,
            own,
            inner,
            fars,
            y_inverse,
            modes,
            reach_x,
            reach_y,
            first,
        )
        then = inverse_rest((high, low), y_inverse, reach_y, rest)
        near_part = near_field(
            sources, targets, from_even, from_odd, peers, near_tiles, blocks, out_rows, then[:1]
        )
        arrived = turned(sent, then)
        image = sample(
            last,
            places,
            chosen(arrived, other_core),
            other_core,
            sample_early(chosen(arrived, same_core), same_core, z_inverse),
            z_inverse,
            sample_lines,
            surface_flag,
            vector,
            near_part,
            reach_x,
            reach_y,
        )
        return image, near_part

    raw = (stencil_base, surface_flag, sample_weights, dipole_weights)
    *sent, wide_high, wide_low, source_coeff, places, vector, high, low = spread(
        density, z_forward, None, raw, reach_x, reach_y, first
    )
    z_forward = (high, low)
    sample_lines = place_sample_lines(places, sample_weights)
    vector, near_part = convolve_and_sample(
        False,
        vector,
        sent,
        (wide_high, wide_low),
        z_forward,
        places,
        sample_lines,
        [sample_lines],
    )
    source_lines = place_lines(places, source_coeff, [near_part])
    *sent, wide_high, wide_low = spread(
        vector.reshape(-1), z_forward, (places, source_lines), None, reach_x, reach_y, first
    )
    both_images, _ = convolve_and_sample(
        True, vector, sent, (wide_high, wide_low), z_forward, places, sample_lines, []
    )
    return both_images


def solution(mesh):
    panels = P(("groups",) + ALL_AXES)
    columns = P(None, ("groups",) + ALL_AXES)
    in_specs = (
        panels,
        panels,
        columns,
        columns,
        columns,
        panels,
        panels,
        P(("groups",) + ALL_AXES, None, None),
    )
    return jax.shard_map(
        shards, mesh=mesh, in_specs=in_specs, out_specs=columns, check_vma=False
    )
```

```python
import functools
import math

import jax
import jax.numpy as jnp
import numpy as np
from jax import lax
from jax.experimental import pallas as pl
from jax.experimental.pallas import tpu as pltpu
from jax.sharding import PartitionSpec as P

GRID = 256
REGION = 128
BLOCK = 128
HALF = 64
KERNEL_GAIN = 4.0
SCREEN = 1.0 / 1024.0
LN2 = math.log(2.0)
Y_AXES = ("narrow", "pair")
ALL_AXES = ("wide", "narrow", "pair")
F32 = jnp.float32
BF16 = jnp.bfloat16
VMEM_LIMIT = 24 * 1024 * 1024
START_LIMIT = VMEM_LIMIT
EARLY_FLOPS = 5 * 10**9
GROUP = 32
CHAINS = 2


def cas(angles):
    return np.cos(angles) + np.sin(angles)


def up_to(count, multiple):
    return -(-count // multiple) * multiple


def low_lanes(rows):
    return lax.broadcasted_iota(jnp.int32, (rows, 2 * HALF), 1) < HALF


def swap(values):
    return pltpu.roll(values, HALF, 1)


def split(values):
    high = values.astype(BF16)
    return high, (values - high.astype(F32)).astype(BF16)


def dot(left, right):
    return jnp.dot(left, right, preferred_element_type=F32)


def dot_three(left, right):
    return dot(left[0], right[0]) + (dot(left[0], right[1]) + dot(left[1], right[0]))


def params():
    return pltpu.CompilerParams(vmem_limit_bytes=VMEM_LIMIT)


def whole_vmem():
    return pl.BlockSpec(memory_space=pltpu.VMEM)


def anywhere():
    return pl.BlockSpec(memory_space=pl.ANY)


def in_smem():
    return pl.BlockSpec(memory_space=pltpu.SMEM)


def cost(flops, moved):
    return pl.CostEstimate(flops=flops, bytes_accessed=moved, transcendentals=0)


def full_scale(exponent, fraction):
    return fraction * jnp.exp(exponent * LN2) * (1.0 / 1024.0)


def fit_scale(largest):
    largest = jnp.maximum(largest, 1e-30)
    exponent = jnp.floor(jnp.log(largest) * (1.0 / LN2))
    fraction = jnp.ceil(largest * jnp.exp(-exponent * LN2) * 1024.0) + 1.0
    return exponent, fraction


def to_short(values):
    return values.astype(jnp.int32).astype(jnp.int16)


def from_short(values):
    return values.astype(jnp.int32).astype(F32)


def quantize(values, exponent, fraction):
    return to_short(jnp.round(values * (32767.0 / full_scale(exponent, fraction))))


def unit(exponent, fraction):
    return full_scale(exponent, fraction) * (1.0 / 32767.0)


def encode_rounded(values):
    rounded = values.astype(BF16).astype(F32)
    size = jnp.maximum(jnp.abs(rounded), 1e-30)
    exponent = jnp.floor(jnp.log(size) * (1.0 / LN2))
    return jnp.round(rounded * jnp.exp((10.0 - exponent) * LN2)), exponent


def decode_rounded(mantissa, exponent):
    return (mantissa * jnp.exp((exponent - 10.0) * LN2)).astype(BF16).astype(F32)


def send_piece(out, head, values):
    exponent, fraction = fit_scale(jnp.max(jnp.abs(values), axis=0, keepdims=True))
    head[0:1, :] = exponent
    head[1:2, :] = fraction
    top = head.shape[0]
    out[:top, :] = to_short(head[...])
    out[top:, :] = quantize(values, exponent, fraction)


def y_position():
    return lax.axis_index("narrow") * lax.axis_size("pair") + lax.axis_index("pair")


def halves(table):
    high = table.astype(jnp.bfloat16)
    return high, (table - high.astype(np.float64)).astype(jnp.bfloat16)


def tables(y_count, pair, span_y):
    depth = GRID // y_count
    reach = span_y + 4
    waves = np.arange(GRID)
    step = 2.0 * np.pi / GRID
    z_table = cas(step * np.outer(np.arange(REGION), waves))
    z_forward = np.zeros((y_count, 2 * REGION, 2 * HALF))
    z_inverse = np.zeros((y_count, 2 * HALF, 2 * REGION))
    symbols = 4.0 * np.sin(np.pi * waves / GRID) ** 2
    shift = np.full((y_count, GRID, 2 * HALF), 1.0)
    y_forward = np.zeros((GRID, y_count, up_to(reach, 8)))
    y_inverse = np.zeros((y_count, up_to(reach, 16), GRID))
    for block in range(y_count):
        mine = z_table[:, block * depth : (block + 1) * depth]
        for half in range(2):
            rows = slice(half * REGION, (half + 1) * REGION)
            lanes = slice(half * HALF, half * HALF + depth)
            z_forward[block, rows, lanes] = mine
            z_inverse[block, lanes, rows] = mine.T / GRID
            shift[block, :, lanes] = (
                SCREEN + symbols[:, None] + symbols[None, block * depth : (block + 1) * depth]
            )
        cells = block * span_y - 2 + np.arange(reach)
        y_table = cas(step * np.outer(waves, cells))
        y_forward[:, block, :reach] = y_table
        y_inverse[block, :reach] = y_table.T / GRID
    y_forward = y_forward.reshape(GRID, y_count // pair, pair, -1).transpose(2, 0, 1, 3)
    y_forward = halves(y_forward.reshape(pair, GRID, -1))
    y_forward = np.concatenate([y_forward[0], y_forward[0], y_forward[1]], axis=2)
    root = np.sqrt(shift * (shift + 4.0))
    decay = 2.0 / (2.0 + shift + root)
    log_decay = np.log(decay)
    ring = 1.0 / (1.0 - np.exp(GRID * log_decay))
    gain = KERNEL_GAIN / root
    modes = np.stack([decay, log_decay, ring, gain], axis=1).astype(np.float32)
    return (
        halves(z_forward),
        halves(z_inverse),
        y_forward,
        halves(y_inverse),
        modes,
    )


def mixing_matrix():
    place = lax.broadcasted_iota(jnp.int32, (4 * BLOCK, 4 * BLOCK), 0)
    lane = lax.broadcasted_iota(jnp.int32, (4 * BLOCK, 4 * BLOCK), 1)
    return jnp.where(lane == 4 * (place % BLOCK) + place // BLOCK, 1.0, 0.0).astype(BF16)


def weave(tiles, mixing, out):
    weights = jnp.concatenate([jnp.concatenate(tile, axis=1) for tile in tiles], axis=0)
    first, rest = split(weights)
    second, third = split(weights - first.astype(F32))
    woven = dot(first, mixing) + (dot(second, mixing) + dot(third, mixing))
    for tile in range(len(tiles)):
        for part in range(BLOCK // GROUP):
            at = (tile * (BLOCK // GROUP) + part) * 16
            lanes = slice(part * BLOCK, (part + 1) * BLOCK)
            for a in range(4):
                row = tile * 16 + 4 * a
                out[pl.ds(at + 8 * (a // 2) + a % 2, 4, stride=2), :] = woven[row : row + 4, lanes]


def by_depth(ref):
    return [ref[pl.ds(depth, 16, stride=4), :] for depth in range(4)]


def pair_rows(x, reach_x, reach_y):
    even = (x // 2) * 2 * reach_y + x % 2
    if x == 0 or x == reach_x - 1:
        return [even]
    return [even, reach_x * reach_y + ((x - 1) // 2) * 2 * reach_y + (x - 1) % 2]


def pair_count(reach_x, reach_y):
    return (2 * reach_x - 2) * reach_y


def in_window(lanes, depth):
    return ((lanes - depth) & -4) == 0


def add_panels(reach, woven, vector_ref, place_ref, weight_ref, grids):
    lanes = lax.broadcasted_iota(jnp.int32, (8, REGION), 1)

    def body(group, carry):
        at = pl.multiple_of(group * 16, 16)
        coeff = [weight_ref[pl.ds(at + 8 * q, 8), :] for q in range(2)] if woven else None
        for local in range(GROUP):
            panel = group * GROUP + local
            grid = grids[local % len(grids)]
            row = place_ref[0, panel]
            value = vector_ref[panel]
            if woven:
                depth = place_ref[1, panel]
                shift = (depth - 4 * local) & (REGION - 1)
                value = jnp.where(in_window(lanes, depth), value, 0.0)
                lines = [pltpu.roll(coeff[q], shift, 1) for q in range(2)]
            else:
                first = pl.multiple_of(panel * 16, 16)
                lines = [weight_ref[pl.ds(first + 8 * q, 8), :] for q in range(2)]
            places = [pl.ds(row, 8), pl.ds(row + 2 * reach, 8)]
            held = [grid[place, :] for place in places]
            for q in range(2):
                grid[places[q], :] = held[q] + lines[q] * value
        return carry

    lax.fori_loop(0, vector_ref.shape[0] // GROUP, body, 0)


def send_pieces(outs, flips, head, rounded, both, high_ref, low_ref):
    blocks = rounded.shape[0]
    mantissa, exponent = encode_rounded(rounded)
    head[...] = jnp.zeros_like(head)
    head[2 : 2 + blocks, :] = mantissa
    head[2 + blocks : 2 + 2 * blocks, :] = exponent
    mine = y_position()
    for at in range(0, len(flips), 2):
        pick = lambda ref: jnp.concatenate([ref[mine ^ flip] for flip in flips[at : at + 2]], axis=1)
        result = dot_three(both, (pick(high_ref), pick(low_ref)))
        for i, out in enumerate(outs[at : at + 2]):
            send_piece(out, head, result[:, i * 2 * HALF : (i + 1) * 2 * HALF])


def spread_grid(reach_x, reach_y, rounded, tables, outs, flips, wides, head, total, grids):
    for x in range(reach_x):
        parts = [
            grid[pl.ds(row, reach_y, stride=2), :]
            for row in pair_rows(x, reach_x, reach_y)
            for grid in grids
        ]
        total[x * reach_y : (x + 1) * reach_y, :] = sum(parts[1:], parts[0])
    half = reach_x * reach_y // 2
    both = jnp.concatenate([total[:half, :], total[half:, :]], axis=1)
    extra = wides[0].shape[0] - half
    if extra:
        both = jnp.concatenate([both, jnp.zeros((extra, 2 * REGION), F32)], axis=0)
    both = split(both)
    for wide, values in zip(wides, both):
        wide[...] = values
    send_pieces(outs, flips, head, rounded, both, *tables)


def start_kernel(reach_x, reach_y, flips, *refs):
    vector_ref, *remote = refs[:9]
    refs = refs[9:]
    outs, refs = refs[: len(flips)], refs[len(flips) :]
    wides, (weight_ref, places_out), refs = refs[:2], refs[2:4], refs[4:]
    rounded, high, low, modes, samples, stencil, flag, dipoles = refs[:8]
    place_ref, sems, head, total = refs[8:12]
    grids = refs[12:]
    tiles = samples.shape[0]
    copies = []
    fetch = lambda source, target: copies.append(
        pltpu.make_async_copy(source, target, sems.at[len(copies)])
    )
    rounded_in, high_in, low_in, stencil_in, flag_in, sample_in, dipole_in, modes_in = remote
    fetch(stencil_in, stencil)
    fetch(flag_in, flag)
    for tile in range(tiles):
        lanes = pl.ds(tile * BLOCK, BLOCK)
        fetch(sample_in.at[:, lanes], samples.at[tile])
        fetch(dipole_in.at[:, lanes], dipoles.at[tile])
    needed_first = len(copies)
    fetch(rounded_in, rounded)
    fetch(high_in, high)
    fetch(low_in, low)
    fetch(modes_in.at[y_position()], modes)
    for copy in copies:
        copy.start()
    for grid in grids:
        grid[...] = jnp.zeros_like(grid)
    mixing = mixing_matrix()
    copies[0].wait()
    span_x, span_y = reach_x - 4, reach_y - 4
    local_x = stencil[0:1, :] - (lax.axis_index("wide") * span_x - 2)
    local_y = stencil[1:2, :] - (y_position() * span_y - 2)
    odd = local_x & 1
    places_out[0:1, :] = odd * (reach_x * reach_y) + (local_x >> 1) * (2 * reach_y) + 2 * local_y
    places_out[1:2, :] = stencil[2:3, :]
    to_scalar = pltpu.make_async_copy(places_out, place_ref, sems.at[len(copies)])
    to_scalar.start()
    for copy in copies[1:needed_first]:
        copy.wait()
    sources = []
    for tile in range(tiles):
        charged = flag[:, tile * BLOCK : (tile + 1) * BLOCK] == 1
        pairs = zip(by_depth(samples.at[tile]), by_depth(dipoles.at[tile]))
        sources.append([jnp.where(charged, -sample, dipole) for sample, dipole in pairs])
    weave(sources, mixing, weight_ref)
    to_scalar.wait()
    add_panels(reach_y, True, vector_ref, place_ref, weight_ref, grids)
    for copy in copies[needed_first:]:
        copy.wait()
    spread_grid(
        reach_x, reach_y, rounded[...], (high, low), outs, flips, wides, head, total, grids
    )


def spread_kernel(reach_x, reach_y, flips, *refs):
    vector_ref, place_ref, rounded_ref, high_ref, low_ref, line_ref = refs[:6]
    refs = refs[6:]
    outs, wides, (head, total), grids = (
        refs[: len(flips)],
        refs[len(flips) : len(flips) + 2],
        refs[len(flips) + 2 : len(flips) + 4],
        refs[len(flips) + 4 :],
    )
    for grid in grids:
        grid[...] = jnp.zeros_like(grid)
    add_panels(reach_y, False, vector_ref, place_ref, line_ref, grids)
    spread_grid(
        reach_x,
        reach_y,
        rounded_ref[...],
        (high_ref, low_ref),
        outs,
        flips,
        wides,
        head,
        total,
        grids,
    )


def spread(vector, table, placed, raw, reach_x, reach_y, flips):
    count = vector.shape[0]
    half = reach_x * reach_y // 2
    blocks = count // BLOCK
    top = up_to(2 + 2 * blocks, 16)
    lanes = 2 * HALF
    body = up_to(half, 16)
    woven = (count // GROUP * 16, BLOCK)
    out_shapes = [jax.ShapeDtypeStruct((top + body, lanes), jnp.int16)] * len(flips)
    out_shapes += [jax.ShapeDtypeStruct((body, 2 * REGION), BF16)] * 2
    rounded = vector.reshape(blocks, BLOCK)
    work = [
        pltpu.VMEM((top, lanes), F32),
        pltpu.VMEM((reach_x * reach_y, REGION), F32),
    ] + [pltpu.VMEM((pair_count(reach_x, reach_y), REGION), F32)] * CHAINS
    if placed is None:
        stencil, flag, sample, dipole, modes = raw
        operands = [vector, rounded, *table, stencil, flag.reshape(1, -1), sample, dipole, modes]
        pinned = [pltpu.with_memory_space_constraint(value, pltpu.HBM) for value in operands[1:]]
        operands = [vector] + pinned
        in_specs = [in_smem()] + [pl.BlockSpec(memory_space=pltpu.HBM)] * 8
        out_shapes += [jax.ShapeDtypeStruct(woven, F32)]
        out_shapes += [jax.ShapeDtypeStruct((2, count), jnp.int32)]
        out_shapes += [jax.ShapeDtypeStruct(rounded.shape, F32)]
        out_shapes += [jax.ShapeDtypeStruct(values.shape, BF16) for values in table]
        out_shapes += [jax.ShapeDtypeStruct(modes.shape[1:], F32)]
        out_shapes += [jax.ShapeDtypeStruct((blocks, 64, BLOCK), F32)]
        work = [
            pltpu.VMEM(stencil.shape, jnp.int32),
            pltpu.VMEM((1, count), jnp.int32),
            pltpu.VMEM((blocks, 64, BLOCK), F32),
            pltpu.SMEM((2, count), jnp.int32),
            pltpu.SemaphoreType.DMA((7 + 2 * blocks,)),
        ] + work
    else:
        operands = [vector, placed[0], rounded, *table, placed[1]]
        in_specs = [in_smem()] * 2 + [whole_vmem()] * 4
    return pl.pallas_call(
        functools.partial(
            start_kernel if placed is None else spread_kernel, reach_x, reach_y, flips
        ),
        in_specs=in_specs,
        out_specs=[whole_vmem()] * len(out_shapes),
        out_shape=out_shapes,
        scratch_shapes=work,
        compiler_params=pltpu.CompilerParams(
            vmem_limit_bytes=START_LIMIT if placed is None else VMEM_LIMIT
        ),
        cost_estimate=cost(2 * half * 256 * 512, 4 * 16 * count * REGION),
        name="start" if placed is None else "spread",
    )(*operands)


def spread_rest_kernel(flips, rounded_ref, wide_high, wide_low, high_ref, low_ref, *refs):
    outs, head = refs[:-1], refs[-1]
    both = (wide_high[...], wide_low[...])
    send_pieces(outs, flips, head, rounded_ref[...], both, high_ref, low_ref)


def spread_rest(rounded, both, table, flips):
    blocks = rounded.shape[0]
    top = up_to(2 + 2 * blocks, 16)
    shape = (top + both[0].shape[0], 2 * HALF)
    return pl.pallas_call(
        functools.partial(spread_rest_kernel, flips),
        in_specs=[whole_vmem()] * 5,
        out_specs=[whole_vmem()] * len(flips),
        out_shape=[jax.ShapeDtypeStruct(shape, jnp.int16)] * len(flips),
        scratch_shapes=[pltpu.VMEM((top, 2 * HALF), F32)],
        compiler_params=params(),
        cost_estimate=cost(2 * shape[0] * 256 * 256 * 3, 4 * shape[0] * 512),
        name="spread_rest",
    )(rounded, *both, *table)


def lines_kernel(place_ref, coeff_ref, *refs):
    out_ref = refs[-1]
    lanes = lax.broadcasted_iota(jnp.int32, (8, REGION), 1)

    def body(group, carry):
        at = pl.multiple_of(group * 16, 16)
        coeff = [coeff_ref[pl.ds(at + 8 * q, 8), :] for q in range(2)]
        for local in range(GROUP):
            panel = group * GROUP + local
            depth = place_ref[1, panel]
            shift = (depth - 4 * local) & (REGION - 1)
            inside = in_window(lanes, depth)
            for q in range(2):
                first = pl.multiple_of(panel * 16 + 8 * q, 8)
                out_ref[pl.ds(first, 8), :] = jnp.where(inside, pltpu.roll(coeff[q], shift, 1), 0.0)
        return carry

    lax.fori_loop(0, place_ref.shape[1] // GROUP, body, 0)


def sample_lines_kernel(place_ref, sample_ref, out_ref, coeff):
    tiles = [by_depth(sample_ref.at[tile]) for tile in range(sample_ref.shape[0])]
    weave(tiles, mixing_matrix(), coeff)
    lines_kernel(place_ref, coeff, out_ref)


def place_sample_lines(places, sample):
    count = places.shape[1]
    shape = (count * 16, REGION)
    return pl.pallas_call(
        sample_lines_kernel,
        in_specs=[in_smem(), whole_vmem()],
        out_specs=whole_vmem(),
        out_shape=jax.ShapeDtypeStruct(shape, F32),
        scratch_shapes=[pltpu.VMEM((count // GROUP * 16, BLOCK), F32)],
        compiler_params=params(),
        cost_estimate=cost(16 * count * REGION, 4 * 16 * count * REGION),
        name="place_sample_lines",
    )(places, sample)


def place_lines(places, coeff, awaited):
    count = places.shape[1]
    shape = (count * 16, REGION)
    return pl.pallas_call(
        lines_kernel,
        in_specs=[in_smem(), whole_vmem()] + [anywhere()] * len(awaited),
        out_specs=whole_vmem(),
        out_shape=jax.ShapeDtypeStruct(shape, F32),
        compiler_params=params(),
        cost_estimate=cost(16 * count * REGION, 4 * 16 * count * REGION),
        name="place_lines",
    )(places, coeff, *awaited)


def open_kernel(part_ref, out_ref):
    top = part_ref.shape[0] - out_ref.shape[0]
    first = from_short(part_ref[:top, :])
    out_ref[...] = from_short(part_ref[top:, :]) * unit(first[0:1], first[1:2])


def open_piece(part, rows):
    return pl.pallas_call(
        open_kernel,
        in_specs=[whole_vmem()],
        out_specs=whole_vmem(),
        out_shape=jax.ShapeDtypeStruct((rows, 2 * HALF), F32),
        compiler_params=params(),
        cost_estimate=cost(EARLY_FLOPS, 6 * rows * 2 * HALF),
        name="open_piece",
    )(part)


def put_edges(opened, reach_x, reach_y, edges, first):
    half = reach_x // 2
    low = low_lanes(reach_y)
    layer = lambda i: opened[i * reach_y : (i + 1) * reach_y, :]
    for two in range(2):
        place = slice(first + two * reach_y, first + (two + 1) * reach_y)
        edges[0, place, :] = jnp.where(low, layer(2 * two), swap(layer(2 * two + 1)))
        last = half - 4 + 2 * two
        edges[1, place, :] = jnp.where(low, swap(layer(last)), layer(last + 1))


def stack_layers(layers, at, reach_y, stacked):
    tall = stacked.shape[0] // len(layers)
    place = at * up_to(reach_y, 8)
    for i, layer in enumerate(layers):
        stacked[pl.ds(pl.multiple_of(i * tall + place, 8), reach_y), :] = layer


def stack_pieces(parts, reach_x, reach_y, top, opened, stacked, edges, places):
    chip = lax.axis_index("narrow")
    for flip, (part, place) in enumerate(zip(parts, places)):
        if part.dtype == F32:
            values = part
        else:
            values = opened
            first = from_short(part[:top, :])
            values[...] = from_short(part[top:, :]) * unit(first[0:1], first[1:2])
        layers = [values[i * reach_y : (i + 1) * reach_y, :] for i in range(reach_x // 2)]
        stack_layers(layers, chip ^ flip, reach_y, stacked)
        put_edges(values, reach_x, reach_y, edges, place * 2 * reach_y)


def transform_pieces(table, stacked, before, spectrum):
    half = spectrum.shape[0]
    tall = stacked.shape[0] // half

    def tripled(values):
        high, low = split(values)
        return jnp.concatenate([high, low, high], axis=0)

    for i in range(0, half, 2):
        places = range(i, min(i + 2, half))
        held = jnp.concatenate([stacked[j * tall : (j + 1) * tall, :] for j in places], axis=1)
        result = dot(table, tripled(held))
        for j in places:
            made = result[:, (j - i) * 2 * HALF : (j - i + 1) * 2 * HALF]
            spectrum[j] = made if before is None else before[j] + made


def forward_early_kernel(reach_x, reach_y, chips, *refs):
    parts = refs[:chips]
    table_ref, spectrum, edges, opened, stacked = refs[chips:]
    top = parts[0].shape[0] - opened.shape[0]
    stacked[...] = jnp.zeros_like(stacked)
    stack_pieces(parts, reach_x, reach_y, top, opened, stacked, edges, range(chips))
    transform_pieces(table_ref[lax.axis_index("pair")], stacked, None, spectrum)


def stacking_scratch(chips, reach_x, reach_y):
    half = reach_x // 2
    return [
        pltpu.VMEM((up_to(half * reach_y, 16), 2 * HALF), F32),
        pltpu.VMEM((half * chips * up_to(reach_y, 8), 2 * HALF), F32),
    ]


def forward_early(parts, table, reach_x, reach_y):
    half = reach_x // 2
    chips = len(parts)
    return pl.pallas_call(
        functools.partial(forward_early_kernel, reach_x, reach_y, chips),
        in_specs=[whole_vmem()] * (chips + 1),
        out_specs=[whole_vmem()] * 2,
        out_shape=[
            jax.ShapeDtypeStruct((half, GRID, 2 * HALF), F32),
            jax.ShapeDtypeStruct((2, chips * 2 * reach_y, 2 * HALF), F32),
        ],
        scratch_shapes=stacking_scratch(chips, reach_x, reach_y),
        compiler_params=params(),
        cost_estimate=cost(EARLY_FLOPS, 4 * half * GRID * 2 * HALF * 2),
        name="forward_early",
    )(*parts, table)


def forward_kernel(reach_x, reach_y, blocks, pieces, before_opened, awaited, *refs):
    parts = refs[:pieces]
    ready = dict(zip(before_opened, refs[pieces:]))
    refs = refs[:pieces] + refs[pieces + len(before_opened) :]
    early_ref, early_edges, table_ref, modes_ref = refs[pieces : pieces + 4]
    refs = refs[pieces + 4 + awaited :]
    spectrum, even_out, layers_out, odd_out, own_out, peers_out, inner_out, *refs = refs
    opened, stacked, edges, slabs, head = refs
    half = reach_x // 2
    pair = lax.axis_size("pair")
    top = parts[0].shape[0] - opened.shape[0]
    stacked[...] = jnp.zeros_like(stacked)
    head[...] = jnp.zeros_like(head)
    for piece in range(pieces):
        first = from_short(parts[piece][:top, :])
        mantissa, exponent = first[2 : 2 + blocks], first[2 + blocks : 2 + 2 * blocks]
        peers_out[piece * blocks : (piece + 1) * blocks, :] = decode_rounded(mantissa, exponent)
        at = 6 + 2 * piece * blocks
        head[at : at + blocks, :] = mantissa
        head[at + blocks : at + 2 * blocks, :] = exponent
    rows = 2 * reach_y
    for chip in range(pieces // pair):
        place = chip * pair * rows
        edges[:, place : place + rows, :] = early_edges[:, chip * rows : (chip + 1) * rows, :]
    before = early_ref
    for core in range(1, pair):
        places = range(core, pieces, pair)
        held = [ready.get(flip, parts[flip]) for flip in places]
        stack_pieces(held, reach_x, reach_y, top, opened, stacked, edges, places)
        transform_pieces(table_ref[lax.axis_index("pair") ^ core], stacked, before, spectrum)
        before = spectrum

    chunk = 32

    def body(index, largest):
        rows = pl.ds(pl.multiple_of(index * chunk, chunk), chunk)
        low = low_lanes(chunk)
        decay = modes_ref[0, rows, :]
        log_decay = modes_ref[1, rows, :]
        across_half = jnp.exp(half * log_decay)
        across_cut = jnp.exp((half - 4) * log_decay)
        layers = [spectrum[i, rows, :] for i in range(half)]
        run = layers[0]
        cut_right = run
        for i in range(1, half):
            run = decay * run + layers[i]
            if i == half - 5:
                cut_right = run
        right = run
        run = layers[half - 1]
        cut_left = run
        for i in range(half - 2, -1, -1):
            run = decay * run + layers[i]
            if i == 4:
                cut_left = run
        left = run
        inner_out[rows, :] = jnp.where(low, right, left)
        swapped_right, swapped_left = swap(right), swap(left)
        own = jnp.where(low, left + across_half * swapped_left, right + across_half * swapped_right)
        own_out[rows, :] = own
        made = [
            jnp.where(low, own, cut_right + across_cut * swapped_right),
            jnp.where(low, cut_left + across_cut * swapped_left, own),
        ]
        for slab, values in enumerate(made):
            slabs[slab, rows, :] = values
        return tuple(
            jnp.maximum(old, jnp.max(jnp.abs(values).reshape(chunk // 8, 8, 2 * HALF), axis=0))
            for old, values in zip(largest, made)
        )

    zero = jnp.zeros((8, 2 * HALF), F32)
    largest = lax.fori_loop(0, GRID // chunk, body, (zero,) * 2)
    top = head.shape[0]
    low = low_lanes(GRID // 2)
    upper, lower = own_out[: GRID // 2, :], own_out[GRID // 2 :, :]
    packed = [jnp.where(low, swap(upper), lower), jnp.where(low, upper, swap(lower))]

    def send(out, first, parts):
        place = first
        for index, (values, most) in enumerate(parts):
            exponent, fraction = fit_scale(jnp.max(most, axis=0, keepdims=True))
            head[2 * index : 2 * index + 1, :] = exponent
            head[2 * index + 1 : 2 * index + 2, :] = fraction
            out[place : place + values.shape[0], :] = quantize(values, exponent, fraction)
            place += values.shape[0]
        out[:first, :] = to_short(head[:first, :])

    with_most = lambda values: (values, jnp.abs(values))
    on_left = lax.axis_index("wide") & 1
    for side, (even, odd) in enumerate(((0, 1), (1, 0))):

        @pl.when(on_left == side)
        def _():
            send(even_out, top, [(slabs[even], largest[even]), with_most(packed[even])])
            send(layers_out, 16, [with_most(edges[1 - even])])
            send(odd_out, top, [(slabs[odd], largest[odd]), with_most(edges[1 - odd])])


def forward(
    parts, ready, early, early_edges, table, modes, reach_x, reach_y, blocks, awaited
):
    pieces = len(parts)
    half = reach_x // 2
    lanes = 2 * HALF
    head = up_to(6 + 2 * pieces * blocks, 16)
    border = pieces * 2 * reach_y
    short = lambda rows: jax.ShapeDtypeStruct((rows, lanes), jnp.int16)
    return pl.pallas_call(
        functools.partial(
            forward_kernel, reach_x, reach_y, blocks, pieces, list(ready), len(awaited)
        ),
        in_specs=[whole_vmem()] * (pieces + len(ready) + 4) + [anywhere()] * len(awaited),
        out_specs=[whole_vmem()] * 7,
        out_shape=[
            jax.ShapeDtypeStruct((half, GRID, lanes), F32),
            short(head + GRID + GRID // 2),
            short(16 + border),
            short(head + GRID + border),
            jax.ShapeDtypeStruct((GRID, lanes), F32),
            jax.ShapeDtypeStruct((pieces * blocks, BLOCK), F32),
            jax.ShapeDtypeStruct((GRID, lanes), F32),
        ],
        scratch_shapes=stacking_scratch(pieces // table.shape[0], reach_x, reach_y)
        + [
            pltpu.VMEM((2, border, lanes), F32),
            pltpu.VMEM((2, GRID, lanes), F32),
            pltpu.VMEM((head, lanes), F32),
        ],
        compiler_params=params(),
        cost_estimate=cost(2 * half * 256 * 256 * 128, 4 * half * GRID * lanes * 2),
        name="forward",
    )(*parts, *ready.values(), early, early_edges, table, modes, *awaited)


def opened_part(ref, index, first, rows):
    head = from_short(ref[:16, :])
    scale = unit(head[2 * index : 2 * index + 1], head[2 * index + 1 : 2 * index + 2])
    return from_short(ref[first : first + rows, :]) * scale


def pair_kernel(reach_x, flips, own_ref, even_ref, modes_ref, *refs):
    outs, head = refs[:-1], refs[-1]
    span = reach_x - 4
    here = lax.axis_index("wide")
    low = low_lanes(GRID)
    log_decay = modes_ref[1]
    own = own_ref[...]
    top = even_ref.shape[0] - GRID - GRID // 2
    cut = opened_part(even_ref, 0, top, GRID)
    packed = opened_part(even_ref, 1, top + GRID, GRID // 2)
    from_left = jnp.where(low, cut, jnp.concatenate([swap(packed), packed], axis=0))
    from_right = jnp.where(low, jnp.concatenate([packed, swap(packed)], axis=0), cut)
    partner = jnp.where((here & 1) == 1, from_left, from_right)

    def weight(distances):
        powers = []
        for distance in distances:
            ahead = span * distance - reach_x
            powers.append(jnp.where(distance >= 2, ahead, ahead + GRID).astype(F32))
        return jnp.exp(jnp.where(low, *powers) * log_decay)

    head[...] = jnp.zeros_like(head)
    for flip, out in zip(flips, outs):
        behind = (here ^ flip) - here
        message = own * weight((-behind, behind))
        behind = (here ^ flip) - (here ^ 1)
        beside = jnp.where(jnp.abs(behind) == 1, 0.0, 1.0)
        send_piece(out, head, message + partner * (weight((-behind, behind)) * beside))


def pair_messages(own, from_even, modes, reach_x, flips):
    return pl.pallas_call(
        functools.partial(pair_kernel, reach_x, flips),
        in_specs=[whole_vmem()] * 3,
        out_specs=[whole_vmem()] * len(flips),
        out_shape=[jax.ShapeDtypeStruct((16 + GRID, 2 * HALF), jnp.int16)] * len(flips),
        scratch_shapes=[pltpu.VMEM((16, 2 * HALF), F32)],
        compiler_params=params(),
        cost_estimate=cost(16 * GRID * 2 * HALF, 4 * GRID * 2 * HALF * (6 + len(flips))),
        name="pair_messages",
    )(own, from_even, modes)


def borders_kernel(reach_y, pieces, layers_ref, odd_ref, table_ref, out_ref, stacked, partial):
    on_left = (lax.axis_index("wide") & 1) == 1
    pair = lax.axis_size("pair")
    rows = pieces * 2 * reach_y
    even = opened_part(layers_ref, 0, 16, rows)
    odd = opened_part(odd_ref, 1, odd_ref.shape[0] - rows, rows)
    left, right = jnp.where(on_left, even, odd), jnp.where(on_left, odd, even)
    low = low_lanes(rows)
    both = [jnp.where(low, left, swap(right)), jnp.where(low, swap(left), right)]
    core = lax.axis_index("pair")
    chip = lax.axis_index("narrow")
    stacked[...] = jnp.zeros_like(stacked)
    before = None
    for other in range(pair):
        for flip in range(pieces // pair):
            first = (flip * pair + other) * 2 * reach_y
            layers = [
                values[first + two * reach_y : first + (two + 1) * reach_y]
                for two in range(2)
                for values in both
            ]
            stack_layers(layers, chip ^ flip, reach_y, stacked)
        target = out_ref if other == pair - 1 else partial
        transform_pieces(table_ref[core ^ other], stacked, before, target)
        before = target


def borders(layers, from_odd, table, reach_y, pieces):
    chips = pieces // table.shape[0]
    shape = (4, GRID, 2 * HALF)
    return pl.pallas_call(
        functools.partial(borders_kernel, reach_y, pieces),
        in_specs=[whole_vmem()] * 3,
        out_specs=whole_vmem(),
        out_shape=jax.ShapeDtypeStruct(shape, F32),
        scratch_shapes=[
            pltpu.VMEM((4 * chips * up_to(reach_y, 8), 2 * HALF), F32),
            pltpu.VMEM(shape, F32),
        ],
        compiler_params=params(),
        cost_estimate=cost(2 * 4 * 256 * 256 * 128, 4 * 6 * GRID * 2 * HALF),
        name="borders",
    )(layers, from_odd, table)


def send_fields(outs, flips, reach_y, field_high, field_low, high_ref, low_ref, ready, head):
    half = field_high.shape[0]
    mine = y_position()
    pitch = up_to(reach_y, 16)
    pick = lambda ref: jnp.concatenate([ref[mine ^ flip] for flip in flips], axis=0)
    table = (pick(high_ref), pick(low_ref))
    for i in range(0, half, 2):
        many = min(2, half - i)
        join = lambda ref: jnp.concatenate([ref[i + j] for j in range(many)], axis=1)
        result = dot_three(table, (join(field_high), join(field_low)))
        for j in range(many):
            for piece in range(len(flips)):
                ready[piece, (i + j) * reach_y : (i + j + 1) * reach_y, :] = result[
                    piece * pitch : piece * pitch + reach_y, j * 2 * HALF : (j + 1) * 2 * HALF
                ]
    head[...] = jnp.zeros_like(head)
    for piece, out in enumerate(outs):
        if ready.shape[1] > half * reach_y:
            ready[piece, half * reach_y :, :] = jnp.zeros_like(ready[piece, half * reach_y :, :])
        send_piece(out, head, ready[piece])


def inverse_kernel(reach_x, reach_y, flips, fars, *refs):
    spectrum, border_ref, from_even, from_odd, own_ref, inner_ref, *far_refs = refs[: 6 + fars]
    refs = refs[6 + fars :]
    high_ref, low_ref, modes_ref = refs[:3]
    outs = refs[3 : 3 + len(flips)]
    field_high, field_low, ready, head = refs[3 + len(flips) :]
    half = reach_x // 2
    span = reach_x - 4
    chunk = 32
    head_rows = from_even.shape[0] - GRID - GRID // 2
    on_left = (lax.axis_index("wide") & 1) == 1
    moment_units = []
    for ref in (from_even, from_odd):
        first = from_short(ref[:16, :])
        moment_units.append(unit(first[0:1], first[1:2]))

    far_units = []
    for ref in far_refs:
        first = from_short(ref[:16, :])
        far_units.append(unit(first[0:1], first[1:2]))

    def body(index, carry):
        first = pl.multiple_of(index * chunk, chunk)
        rows = pl.ds(first, chunk)
        low = low_lanes(chunk)
        decay = modes_ref[0, rows, :]
        log_decay = modes_ref[1, rows, :]
        ring = modes_ref[2, rows, :]
        gain = modes_ref[3, rows, :]
        across_half = jnp.exp(half * log_decay)
        across_cut = jnp.exp((half - 4) * log_decay)
        around = jnp.exp((GRID - 4) * log_decay)
        beside = jnp.exp((GRID - reach_x - span) * log_decay)
        layers = [spectrum[i, rows, :] for i in range(half)]

        at = pl.ds(pl.multiple_of(head_rows + index * chunk, 16), chunk)
        even, odd = (
            from_short(ref[at, :]) * scale for ref, scale in zip((from_even, from_odd), moment_units)
        )
        left_moments, right_moments = jnp.where(on_left, even, odd), jnp.where(on_left, odd, even)
        border = [border_ref[i, rows, :] for i in range(4)]
        zero = jnp.zeros_like(decay)
        head_sum = border[0]
        for i in range(1, 4):
            head_sum = decay * head_sum + border[i]
        tail_sum = border[3]
        for i in range(2, -1, -1):
            tail_sum = decay * tail_sum + border[i]
        for i in range(4):
            layers[i] = layers[i] + jnp.where(low, border[i], zero)
        for i in range(4):
            place = half - 4 + i
            layers[place] = layers[place] + jnp.where(low, zero, border[i])
        total = own_ref[rows, :] * jnp.exp((GRID - reach_x) * log_decay)
        at = pl.ds(pl.multiple_of(16 + index * chunk, 16), chunk)
        for ref, scale in zip(far_refs, far_units):
            total = total + from_short(ref[at, :]) * scale
        one = jnp.ones_like(decay)
        total = total + left_moments * jnp.where(low, beside, one)
        total = total + right_moments * jnp.where(low, one, beside)
        shared = jnp.where(low, head_sum, tail_sum)
        entering = (swap(total) + around * shared) * ring
        leaving = swap(across_half * entering + across_cut * shared + inner_ref[rows, :])
        run = jnp.where(low, entering, leaving)
        forward_runs = []
        for i in range(half):
            run = decay * run + layers[i]
            forward_runs.append(run)
        run = jnp.where(low, leaving, entering)
        for i in range(half - 1, -1, -1):
            ahead = decay * run
            high, rest = split(gain * (forward_runs[i] + ahead))
            field_high[i, rows, :] = high
            field_low[i, rows, :] = rest
            run = ahead + layers[i]
        return carry

    lax.fori_loop(0, GRID // chunk, body, 0)
    send_fields(outs, flips, reach_y, field_high, field_low, high_ref, low_ref, ready, head)


def inverse(
    spectrum, border, from_even, from_odd, own, inner, fars, table, modes, reach_x, reach_y, flips
):
    half = reach_x // 2
    lanes = 2 * HALF
    body = up_to(half * reach_y, 16)
    shapes = [jax.ShapeDtypeStruct((16 + body, lanes), jnp.int16)] * len(flips)
    shapes += [jax.ShapeDtypeStruct((half, GRID, lanes), BF16)] * 2
    return pl.pallas_call(
        functools.partial(inverse_kernel, reach_x, reach_y, flips, len(fars)),
        in_specs=[whole_vmem()] * (9 + len(fars)),
        out_specs=[whole_vmem()] * len(shapes),
        out_shape=shapes,
        scratch_shapes=[
            pltpu.VMEM((len(flips), body, lanes), F32),
            pltpu.VMEM((16, lanes), F32),
        ],
        compiler_params=params(),
        cost_estimate=cost(2 * half * 256 * 256 * 128, 4 * half * GRID * lanes * 2),
        name="inverse",
    )(spectrum, border, from_even, from_odd, own, inner, *fars, *table, modes)


def inverse_rest_kernel(reach_y, flips, field_high, field_low, high_ref, low_ref, *refs):
    outs, (ready, head) = refs[: len(flips)], refs[len(flips) :]
    send_fields(outs, flips, reach_y, field_high, field_low, high_ref, low_ref, ready, head)


def inverse_rest(field, table, reach_y, flips):
    half = field[0].shape[0]
    lanes = 2 * HALF
    body = up_to(half * reach_y, 16)
    return pl.pallas_call(
        functools.partial(inverse_rest_kernel, reach_y, flips),
        in_specs=[whole_vmem()] * 4,
        out_specs=[whole_vmem()] * len(flips),
        out_shape=[jax.ShapeDtypeStruct((16 + body, lanes), jnp.int16)] * len(flips),
        scratch_shapes=[
            pltpu.VMEM((len(flips), body, lanes), F32),
            pltpu.VMEM((16, lanes), F32),
        ],
        compiler_params=params(),
        cost_estimate=cost(2 * half * 256 * 256 * 128, 4 * half * GRID * lanes * 2),
        name="inverse_rest",
    )(*field, *table)


def sum_rows(values):
    row = lax.broadcasted_iota(jnp.int32, values[0].shape, 0)
    for step in (4, 2, 1):
        low = (row & step) == 0
        paired = []
        for one, other in zip(values[: len(values) // 2], values[len(values) // 2 :]):
            kept = jnp.where(low, one, other)
            moved = jnp.where(low, other, one)
            if step == 4:
                moved = pltpu.roll(moved, 4, 0)
            else:
                moved = jnp.where(low, pltpu.roll(moved, 8 - step, 0), pltpu.roll(moved, step, 0))
            paired.append(kept + moved)
        values = paired
    return values[0]


def z_lines(parts, flips, high_ref, low_ref):
    mine = y_position()
    opened = []
    for part in parts:
        if part.dtype == F32:
            opened.append(part[...])
        else:
            first = from_short(part[:16, :])
            opened.append(from_short(part[16:, :]) * unit(first[0:1], first[1:2]))
    values = split(jnp.concatenate(opened, axis=1))
    pick = lambda ref: jnp.concatenate([ref[mine ^ flip] for flip in flips], axis=0)
    return dot_three(values, (pick(high_ref), pick(low_ref)))


def sample_early_kernel(flips, *refs):
    *parts, high_ref, low_ref, out_ref = refs
    out_ref[...] = z_lines(parts, flips, high_ref, low_ref)


def sample_early(parts, flips, table):
    rows = parts[0].shape[0] - 16
    return pl.pallas_call(
        functools.partial(sample_early_kernel, flips),
        in_specs=[whole_vmem()] * (len(parts) + 2),
        out_specs=whole_vmem(),
        out_shape=jax.ShapeDtypeStruct((rows, 2 * REGION), F32),
        compiler_params=params(),
        cost_estimate=cost(EARLY_FLOPS, 4 * rows * 512),
        name="sample_early",
    )(*parts, *table)


def sample_kernel(last, reach_x, reach_y, flips, place_ref, *refs):
    parts = refs[: len(flips)]
    early_ref, high_ref, low_ref, line_ref, own_ref, vector_ref, near_ref, out_ref = refs[
        len(flips) : len(flips) + 8
    ]
    flat, field, sums = refs[len(flips) + 8 :]
    half_rows = reach_x * reach_y // 2
    both = early_ref[...] + z_lines(parts, flips, high_ref, low_ref)
    flat[:half_rows, :] = both[:half_rows, :REGION]
    flat[half_rows:, :] = both[:half_rows, REGION:]
    for x in range(reach_x):
        layer = flat[x * reach_y : (x + 1) * reach_y, :]
        for row in pair_rows(x, reach_x, reach_y):
            field[pl.ds(row, reach_y, stride=2), :] = layer
    count = place_ref.shape[1]

    def body(group, carry):
        for eight in range(0, GROUP, 8):
            totals = []
            for local in range(eight, eight + 8):
                panel = group * GROUP + local
                row = place_ref[0, panel]
                first = pl.multiple_of(panel * 16, 16)
                totals.append(
                    field[pl.ds(row, 8), :] * line_ref[pl.ds(first, 8), :]
                    + field[pl.ds(row + 2 * reach_y, 8), :] * line_ref[pl.ds(first + 8, 8), :]
                )
            sums[pl.ds(pl.multiple_of(group * GROUP + eight, 8), 8), :] = sum_rows(totals)
        return carry

    lax.fori_loop(0, count // GROUP, body, 0)
    sampled = lax.dot_general(
        jnp.ones((8, REGION), F32),
        sums[...],
        (((1,), (1,)), ((), ())),
        precision=lax.Precision.HIGHEST,
        preferred_element_type=F32,
    )
    for block in range(count // BLOCK):
        lane = slice(block * BLOCK, (block + 1) * BLOCK)
        row = slice(block, block + 1)
        vector = vector_ref[row, :]
        image = jnp.where(own_ref[row, :] == 1, 0.0, 0.5 * vector) + sampled[:1, lane]
        image = image + near_ref[row, :]
        if last:
            out_ref[0:1, lane] = vector
            out_ref[1:2, lane] = image
        else:
            out_ref[row, :] = image


def sample(last, places, parts, flips, early, table, lines, flag, vector, near, reach_x, reach_y):
    count = places.shape[1]
    blocks = count // BLOCK
    shape = (2, count) if last else (blocks, BLOCK)
    return pl.pallas_call(
        functools.partial(sample_kernel, last, reach_x, reach_y, flips),
        in_specs=[in_smem()] + [whole_vmem()] * (len(parts) + 7),
        out_specs=whole_vmem(),
        out_shape=jax.ShapeDtypeStruct(shape, F32),
        scratch_shapes=[
            pltpu.VMEM((reach_x * reach_y, REGION), F32),
            pltpu.VMEM((pair_count(reach_x, reach_y), REGION), F32),
            pltpu.VMEM((count, REGION), F32),
        ],
        compiler_params=params(),
        cost_estimate=cost(reach_x * reach_y * 256 * 512, 4 * 16 * count * REGION),
        name="sample",
    )(
        places,
        *parts,
        early,
        *table,
        lines,
        flag.reshape(blocks, BLOCK),
        vector.reshape(blocks, BLOCK),
        near,
    )


def near_kernel(slots, blocks, place_ref, target_ref, *refs):
    even_ref, odd_ref, peers_ref, tile_ref = refs[:4]
    out_ref, held = refs[-2:]
    count = peers_ref.shape[0]
    held[count : 2 * count, :] = peers_ref[...]
    on_left = lax.axis_index("wide") & 1
    for side, ref in ((1 - on_left, even_ref), (on_left, odd_ref)):
        top = from_short(ref[...])
        for piece in range(count // blocks):
            at = 6 + 2 * piece * blocks
            held[pl.ds(side * (2 * count) + piece * blocks, blocks), :] = decode_rounded(
                top[at : at + blocks], top[at + blocks : at + 2 * blocks]
            )
    out_ref[...] = jnp.zeros_like(out_ref)
    for slot in range(slots):
        picked = held[pl.ds(place_ref[slot], 1), :]
        picked = jnp.broadcast_to(picked, (16, BLOCK)).astype(BF16)
        product = lax.dot_general(
            picked,
            tile_ref[slot],
            (((1,), (1,)), ((), ())),
            preferred_element_type=F32,
        )
        target = pl.ds(target_ref[slot], 1)
        out_ref[target, :] = out_ref[target, :] + product[:1]


def near_field(places, targets, from_even, from_odd, peers, tiles, blocks, out_rows, awaited):
    slots = tiles.shape[0]
    head = up_to(6 + 2 * peers.shape[0], 16)
    constant = lambda shape: pl.BlockSpec(shape, lambda i: (0,) * len(shape))
    return pl.pallas_call(
        functools.partial(near_kernel, slots, blocks),
        grid=(1,),
        in_specs=[
            in_smem(),
            in_smem(),
            constant((head, BLOCK)),
            constant((head, BLOCK)),
            constant(peers.shape),
            constant(tiles.shape),
        ]
        + [anywhere()] * len(awaited),
        out_specs=constant((out_rows, BLOCK)),
        out_shape=jax.ShapeDtypeStruct((out_rows, BLOCK), F32),
        scratch_shapes=[pltpu.VMEM((3 * peers.shape[0], BLOCK), F32)],
        compiler_params=params(),
        cost_estimate=cost(2 * slots * 16 * BLOCK * BLOCK, 2 * slots * BLOCK * BLOCK),
        name="near_field",
    )(places, targets, from_even, from_odd, peers, tiles, *awaited)


def shards(
    density,
    surface_flag,
    stencil_base,
    sample_weights,
    dipole_weights,
    near_target,
    near_source,
    near_tiles,
):
    x_count = lax.axis_size("wide")
    y_count = lax.axis_size(Y_AXES)
    y_index = lax.axis_index(Y_AXES)
    pair = lax.axis_size("pair")
    span_x = REGION // x_count
    span_y = REGION // y_count
    reach_x = span_x + 4
    reach_y = span_y + 4
    count = density.shape[0]
    blocks = count // BLOCK

    z_forward, z_inverse, y_forward, y_inverse, modes = tables(y_count, pair, span_y)

    neighbour = near_source // blocks
    flip = (y_index + neighbour % 3 - 1) ^ y_index
    sources = ((neighbour // 3) * y_count + flip) * blocks + near_source % blocks
    out_rows = up_to(blocks + 1, 8)
    live = near_target >= 0
    sources = jnp.where(live, sources, 0)
    targets = jnp.where(live, near_target, out_rows - 1)

    swaps = lambda pairs: [(i, j) for i, j in pairs] + [(j, i) for i, j in pairs]
    even_swap = swaps([(i, i + 1) for i in range(0, x_count - 1, 2)])
    odd_swap = swaps([(i, i + 1) for i in range(1, x_count - 1, 2)])
    far_flips = list(range(2, x_count, 2))

    first, rest = list(range(pair, y_count)), list(range(pair))
    same_core = list(range(0, y_count, pair))
    other_core = [flip for flip in range(y_count) if flip not in same_core]

    def turned(sent, then):
        arrived = [None] * y_count
        for flip, part in zip(first + rest, list(sent) + list(then)):
            swap_pairs = [(i, i ^ flip) for i in range(y_count)]
            arrived[flip] = part if flip == 0 else lax.ppermute(part, Y_AXES, swap_pairs)
        return arrived

    def chosen(parts, flips):
        return [parts[flip] for flip in flips]

    def opened(parts):
        rows = up_to(reach_x * reach_y // 2, 16)
        return {flip: open_piece(parts[flip], rows) for flip in first if flip in other_core}

    def convolve_and_sample(last, vector, sent, both, table, modes, places, sample_lines, awaited):
        arrived = turned(sent, spread_rest(vector, both, table, rest))
        early, edges = forward_early(chosen(arrived, same_core), y_forward, reach_x, reach_y)
        spectrum, even_message, layers, odd_message, own, peers, inner = forward(
            arrived,
            opened(arrived),
            early,
            edges,
            y_forward,
            modes,
            reach_x,
            reach_y,
            blocks,
            awaited,
        )
        from_even = lax.ppermute(even_message, "wide", even_swap)
        from_odd = lax.ppermute(odd_message, "wide", odd_swap)
        even_layers = lax.ppermute(layers, "wide", even_swap)
        fars = [
            lax.ppermute(message, "wide", [(i, i ^ flip) for i in range(x_count)])
            for flip, message in zip(
                far_flips, pair_messages(own, from_even, modes, reach_x, far_flips)
            )
        ]
        *sent, high, low = inverse(
            spectrum,
            borders(even_layers, from_odd, y_forward, reach_y, y_count),
            from_even,
            from_odd,
            own,
            inner,
            fars,
            y_inverse,
            modes,
            reach_x,
            reach_y,
            first,
        )
        then = inverse_rest((high, low), y_inverse, reach_y, rest)
        near_part = near_field(
            sources, targets, from_even, from_odd, peers, near_tiles, blocks, out_rows, then[:1]
        )
        arrived = turned(sent, then)
        ready = opened(arrived)
        image = sample(
            last,
            places,
            [ready.get(flip, arrived[flip]) for flip in other_core],
            other_core,
            sample_early(chosen(arrived, same_core), same_core, z_inverse),
            z_inverse,
            sample_lines,
            surface_flag,
            vector,
            near_part,
            reach_x,
            reach_y,
        )
        return image, near_part

    raw = (stencil_base, surface_flag, sample_weights, dipole_weights, jnp.asarray(modes))
    *sent, wide_high, wide_low, source_coeff, places, vector, high, low, modes, samples = spread(
        density, z_forward, None, raw, reach_x, reach_y, first
    )
    z_forward = (high, low)
    sample_lines = place_sample_lines(places, samples)
    vector, near_part = convolve_and_sample(
        False,
        vector,
        sent,
        (wide_high, wide_low),
        z_forward,
        modes,
        places,
        sample_lines,
        [sample_lines],
    )
    source_lines = place_lines(places, source_coeff, [near_part])
    *sent, wide_high, wide_low = spread(
        vector.reshape(-1), z_forward, (places, source_lines), None, reach_x, reach_y, first
    )
    both_images, _ = convolve_and_sample(
        True, vector, sent, (wide_high, wide_low), z_forward, modes, places, sample_lines, []
    )
    return both_images


def solution(mesh):
    panels = P(("groups",) + ALL_AXES)
    columns = P(None, ("groups",) + ALL_AXES)
    in_specs = (
        panels,
        panels,
        columns,
        columns,
        columns,
        panels,
        panels,
        P(("groups",) + ALL_AXES, None, None),
    )
    return jax.shard_map(
        shards, mesh=mesh, in_specs=in_specs, out_specs=columns, check_vma=False
    )
```

```python
import functools
import math

import jax
import jax.numpy as jnp
import numpy as np
from jax import lax
from jax.experimental import pallas as pl
from jax.experimental.pallas import tpu as pltpu
from jax.sharding import PartitionSpec as P

GRID = 256
REGION = 128
BLOCK = 128
HALF = 64
KERNEL_GAIN = 4.0
SCREEN = 1.0 / 1024.0
LN2 = math.log(2.0)
Y_AXES = ("narrow", "pair")
ALL_AXES = ("wide", "narrow", "pair")
F32 = jnp.float32
BF16 = jnp.bfloat16
VMEM_LIMIT = 24 * 1024 * 1024
START_LIMIT = VMEM_LIMIT
EARLY_FLOPS = 5 * 10**9
GROUP = 32
CHAINS = 2


def cas(angles):
    return np.cos(angles) + np.sin(angles)


def up_to(count, multiple):
    return -(-count // multiple) * multiple


def low_lanes(rows):
    return lax.broadcasted_iota(jnp.int32, (rows, 2 * HALF), 1) < HALF


def swap(values):
    return pltpu.roll(values, HALF, 1)


def split(values):
    high = values.astype(BF16)
    return high, (values - high.astype(F32)).astype(BF16)


def dot(left, right):
    return jnp.dot(left, right, preferred_element_type=F32)


def dot_three(left, right):
    return dot(left[0], right[0]) + (dot(left[0], right[1]) + dot(left[1], right[0]))


def params():
    return pltpu.CompilerParams(vmem_limit_bytes=VMEM_LIMIT)


def whole_vmem():
    return pl.BlockSpec(memory_space=pltpu.VMEM)


def anywhere():
    return pl.BlockSpec(memory_space=pl.ANY)


def in_smem():
    return pl.BlockSpec(memory_space=pltpu.SMEM)


def cost(flops, moved):
    return pl.CostEstimate(flops=flops, bytes_accessed=moved, transcendentals=0)


def full_scale(exponent, fraction):
    return fraction * jnp.exp(exponent * LN2) * (1.0 / 1024.0)


def fit_scale(largest):
    largest = jnp.maximum(largest, 1e-30)
    exponent = jnp.floor(jnp.log(largest) * (1.0 / LN2))
    fraction = jnp.ceil(largest * jnp.exp(-exponent * LN2) * 1024.0) + 1.0
    return exponent, fraction


def to_short(values):
    return values.astype(jnp.int32).astype(jnp.int16)


def from_short(values):
    return values.astype(jnp.int32).astype(F32)


def quantize(values, exponent, fraction):
    return to_short(jnp.round(values * (32767.0 / full_scale(exponent, fraction))))


def unit(exponent, fraction):
    return full_scale(exponent, fraction) * (1.0 / 32767.0)


def encode_rounded(values):
    rounded = values.astype(BF16).astype(F32)
    size = jnp.maximum(jnp.abs(rounded), 1e-30)
    exponent = jnp.floor(jnp.log(size) * (1.0 / LN2))
    return jnp.round(rounded * jnp.exp((10.0 - exponent) * LN2)), exponent


def decode_rounded(mantissa, exponent):
    return (mantissa * jnp.exp((exponent - 10.0) * LN2)).astype(BF16).astype(F32)


def send_piece(out, head, values):
    exponent, fraction = fit_scale(jnp.max(jnp.abs(values), axis=0, keepdims=True))
    head[0:1, :] = exponent
    head[1:2, :] = fraction
    top = head.shape[0]
    out[:top, :] = to_short(head[...])
    out[top:, :] = quantize(values, exponent, fraction)


def y_position():
    return lax.axis_index("narrow") * lax.axis_size("pair") + lax.axis_index("pair")


def halves(table):
    high = table.astype(jnp.bfloat16)
    return high, (table - high.astype(np.float64)).astype(jnp.bfloat16)


def tables(y_count, pair, span_y):
    depth = GRID // y_count
    reach = span_y + 4
    waves = np.arange(GRID)
    step = 2.0 * np.pi / GRID
    z_table = cas(step * np.outer(np.arange(REGION), waves))
    z_forward = np.zeros((y_count, 2 * REGION, 2 * HALF))
    z_inverse = np.zeros((y_count, 2 * HALF, 2 * REGION))
    symbols = 4.0 * np.sin(np.pi * waves / GRID) ** 2
    shift = np.full((y_count, GRID, 2 * HALF), 1.0)
    y_forward = np.zeros((GRID, y_count, up_to(reach, 8)))
    y_inverse = np.zeros((y_count, up_to(reach, 16), GRID))
    for block in range(y_count):
        mine = z_table[:, block * depth : (block + 1) * depth]
        for half in range(2):
            rows = slice(half * REGION, (half + 1) * REGION)
            lanes = slice(half * HALF, half * HALF + depth)
            z_forward[block, rows, lanes] = mine
            z_inverse[block, lanes, rows] = mine.T / GRID
            shift[block, :, lanes] = (
                SCREEN + symbols[:, None] + symbols[None, block * depth : (block + 1) * depth]
            )
        cells = block * span_y - 2 + np.arange(reach)
        y_table = cas(step * np.outer(waves, cells))
        y_forward[:, block, :reach] = y_table
        y_inverse[block, :reach] = y_table.T / GRID
    y_forward = y_forward.reshape(GRID, y_count // pair, pair, -1).transpose(2, 0, 1, 3)
    y_forward = halves(y_forward.reshape(pair, GRID, -1))
    y_forward = np.concatenate([y_forward[0], y_forward[0], y_forward[1]], axis=2)
    root = np.sqrt(shift * (shift + 4.0))
    decay = 2.0 / (2.0 + shift + root)
    log_decay = np.log(decay)
    ring = 1.0 / (1.0 - np.exp(GRID * log_decay))
    gain = KERNEL_GAIN / root
    modes = np.stack([decay, log_decay, ring, gain], axis=1).astype(np.float32)
    return (
        halves(z_forward),
        halves(z_inverse),
        y_forward,
        halves(y_inverse),
        modes,
    )


def mixing_matrix():
    place = lax.broadcasted_iota(jnp.int32, (4 * BLOCK, 4 * BLOCK), 0)
    lane = lax.broadcasted_iota(jnp.int32, (4 * BLOCK, 4 * BLOCK), 1)
    return jnp.where(lane == 4 * (place % BLOCK) + place // BLOCK, 1.0, 0.0).astype(BF16)


def weave(tiles, mixing, out):
    weights = jnp.concatenate([jnp.concatenate(tile, axis=1) for tile in tiles], axis=0)
    first, rest = split(weights)
    second, third = split(weights - first.astype(F32))
    woven = dot(first, mixing) + (dot(second, mixing) + dot(third, mixing))
    for tile in range(len(tiles)):
        for part in range(BLOCK // GROUP):
            at = (tile * (BLOCK // GROUP) + part) * 16
            lanes = slice(part * BLOCK, (part + 1) * BLOCK)
            for a in range(4):
                row = tile * 16 + 4 * a
                out[pl.ds(at + 8 * (a // 2) + a % 2, 4, stride=2), :] = woven[row : row + 4, lanes]


def by_depth(ref):
    return [ref[pl.ds(depth, 16, stride=4), :] for depth in range(4)]


def pair_rows(x, reach_x, reach_y):
    even = (x // 2) * 2 * reach_y + x % 2
    if x == 0 or x == reach_x - 1:
        return [even]
    return [even, reach_x * reach_y + ((x - 1) // 2) * 2 * reach_y + (x - 1) % 2]


def pair_count(reach_x, reach_y):
    return (2 * reach_x - 2) * reach_y


def in_window(lanes, depth):
    return ((lanes - depth) & -4) == 0


def add_panels(reach, woven, vector_ref, place_ref, weight_ref, grids):
    lanes = lax.broadcasted_iota(jnp.int32, (8, REGION), 1)

    def body(group, carry):
        at = pl.multiple_of(group * 16, 16)
        coeff = [weight_ref[pl.ds(at + 8 * q, 8), :] for q in range(2)] if woven else None
        for local in range(GROUP):
            panel = group * GROUP + local
            grid = grids[local % len(grids)]
            row = place_ref[0, panel]
            value = vector_ref[panel]
            if woven:
                depth = place_ref[1, panel]
                shift = (depth - 4 * local) & (REGION - 1)
                value = jnp.where(in_window(lanes, depth), value, 0.0)
                lines = [pltpu.roll(coeff[q], shift, 1) for q in range(2)]
            else:
                first = pl.multiple_of(panel * 16, 16)
                lines = [weight_ref[pl.ds(first + 8 * q, 8), :] for q in range(2)]
            places = [pl.ds(row, 8), pl.ds(row + 2 * reach, 8)]
            held = [grid[place, :] for place in places]
            for q in range(2):
                grid[places[q], :] = held[q] + lines[q] * value
        return carry

    lax.fori_loop(0, vector_ref.shape[0] // GROUP, body, 0)


def send_pieces(outs, flips, head, rounded, both, high_ref, low_ref):
    blocks = rounded.shape[0]
    mantissa, exponent = encode_rounded(rounded)
    head[...] = jnp.zeros_like(head)
    head[2 : 2 + blocks, :] = mantissa
    head[2 + blocks : 2 + 2 * blocks, :] = exponent
    mine = y_position()
    for at in range(0, len(flips), 2):
        pick = lambda ref: jnp.concatenate([ref[mine ^ flip] for flip in flips[at : at + 2]], axis=1)
        result = dot_three(both, (pick(high_ref), pick(low_ref)))
        for i, out in enumerate(outs[at : at + 2]):
            send_piece(out, head, result[:, i * 2 * HALF : (i + 1) * 2 * HALF])


def spread_grid(reach_x, reach_y, rounded, tables, outs, flips, wides, head, total, grids):
    for x in range(reach_x):
        parts = [
            grid[pl.ds(row, reach_y, stride=2), :]
            for row in pair_rows(x, reach_x, reach_y)
            for grid in grids
        ]
        total[x * reach_y : (x + 1) * reach_y, :] = sum(parts[1:], parts[0])
    half = reach_x * reach_y // 2
    both = jnp.concatenate([total[:half, :], total[half:, :]], axis=1)
    extra = wides[0].shape[0] - half
    if extra:
        both = jnp.concatenate([both, jnp.zeros((extra, 2 * REGION), F32)], axis=0)
    both = split(both)
    for wide, values in zip(wides, both):
        wide[...] = values
    send_pieces(outs, flips, head, rounded, both, *tables)


def start_kernel(reach_x, reach_y, flips, *refs):
    vector_ref, *remote = refs[:8]
    refs = refs[8:]
    outs, refs = refs[: len(flips)], refs[len(flips) :]
    wides, (weight_ref, places_out), refs = refs[:2], refs[2:4], refs[4:]
    rounded, high, low, stencil, flag, samples, dipoles = refs[:7]
    place_ref, sems, head, total = refs[7:11]
    grids = refs[11:]
    tiles = samples.shape[0]
    copies = []
    fetch = lambda source, target: copies.append(
        pltpu.make_async_copy(source, target, sems.at[len(copies)])
    )
    rounded_in, high_in, low_in, stencil_in, flag_in, sample_in, dipole_in = remote
    fetch(stencil_in, stencil)
    fetch(flag_in, flag)
    for tile in range(tiles):
        lanes = pl.ds(tile * BLOCK, BLOCK)
        fetch(sample_in.at[:, lanes], samples.at[tile])
        fetch(dipole_in.at[:, lanes], dipoles.at[tile])
    needed_first = len(copies)
    fetch(rounded_in, rounded)
    fetch(high_in, high)
    fetch(low_in, low)
    for copy in copies:
        copy.start()
    for grid in grids:
        grid[...] = jnp.zeros_like(grid)
    mixing = mixing_matrix()
    copies[0].wait()
    span_x, span_y = reach_x - 4, reach_y - 4
    local_x = stencil[0:1, :] - (lax.axis_index("wide") * span_x - 2)
    local_y = stencil[1:2, :] - (y_position() * span_y - 2)
    odd = local_x & 1
    places_out[0:1, :] = odd * (reach_x * reach_y) + (local_x >> 1) * (2 * reach_y) + 2 * local_y
    places_out[1:2, :] = stencil[2:3, :]
    to_scalar = pltpu.make_async_copy(places_out, place_ref, sems.at[len(copies)])
    to_scalar.start()
    for copy in copies[1:needed_first]:
        copy.wait()
    sources = []
    for tile in range(tiles):
        charged = flag[:, tile * BLOCK : (tile + 1) * BLOCK] == 1
        pairs = zip(by_depth(samples.at[tile]), by_depth(dipoles.at[tile]))
        sources.append([jnp.where(charged, -sample, dipole) for sample, dipole in pairs])
    weave(sources, mixing, weight_ref)
    to_scalar.wait()
    add_panels(reach_y, True, vector_ref, place_ref, weight_ref, grids)
    for copy in copies[needed_first:]:
        copy.wait()
    spread_grid(
        reach_x, reach_y, rounded[...], (high, low), outs, flips, wides, head, total, grids
    )


def spread_kernel(reach_x, reach_y, flips, *refs):
    vector_in, place_in, rounded_ref, high_ref, low_ref, line_ref = refs[:6]
    refs = refs[6:]
    outs, wides, (vector_ref, place_ref, sems, head, total), grids = (
        refs[: len(flips)],
        refs[len(flips) : len(flips) + 2],
        refs[len(flips) + 2 : len(flips) + 7],
        refs[len(flips) + 7 :],
    )
    copies = [
        pltpu.make_async_copy(vector_in, vector_ref, sems.at[0]),
        pltpu.make_async_copy(place_in, place_ref, sems.at[1]),
    ]
    for copy in copies:
        copy.start()
    for grid in grids:
        grid[...] = jnp.zeros_like(grid)
    for copy in copies:
        copy.wait()
    add_panels(reach_y, False, vector_ref, place_ref, line_ref, grids)
    spread_grid(
        reach_x,
        reach_y,
        rounded_ref[...],
        (high_ref, low_ref),
        outs,
        flips,
        wides,
        head,
        total,
        grids,
    )


def spread(vector, table, placed, raw, reach_x, reach_y, flips):
    count = vector.shape[0]
    half = reach_x * reach_y // 2
    blocks = count // BLOCK
    top = up_to(2 + 2 * blocks, 16)
    lanes = 2 * HALF
    body = up_to(half, 16)
    woven = (count // GROUP * 16, BLOCK)
    out_shapes = [jax.ShapeDtypeStruct((top + body, lanes), jnp.int16)] * len(flips)
    out_shapes += [jax.ShapeDtypeStruct((body, 2 * REGION), BF16)] * 2
    rounded = vector.reshape(blocks, BLOCK)
    work = [
        pltpu.VMEM((top, lanes), F32),
        pltpu.VMEM((reach_x * reach_y, REGION), F32),
    ] + [pltpu.VMEM((pair_count(reach_x, reach_y), REGION), F32)] * CHAINS
    if placed is None:
        stencil, flag, sample, dipole = raw
        operands = [vector, rounded, *table, stencil, flag.reshape(1, -1), sample, dipole]
        pinned = [pltpu.with_memory_space_constraint(value, pltpu.HBM) for value in operands[1:]]
        operands = [vector] + pinned
        in_specs = [in_smem()] + [pl.BlockSpec(memory_space=pltpu.HBM)] * 7
        out_shapes += [jax.ShapeDtypeStruct(woven, F32)]
        out_shapes += [jax.ShapeDtypeStruct((2, count), jnp.int32)]
        out_shapes += [jax.ShapeDtypeStruct(rounded.shape, F32)]
        out_shapes += [jax.ShapeDtypeStruct(values.shape, BF16) for values in table]
        tiled = pltpu.VMEM((blocks, 64, BLOCK), F32)
        work = [
            pltpu.VMEM(stencil.shape, jnp.int32),
            pltpu.VMEM((1, count), jnp.int32),
            tiled,
            tiled,
            pltpu.SMEM((2, count), jnp.int32),
            pltpu.SemaphoreType.DMA((6 + 2 * blocks,)),
        ] + work
    else:
        operands = [vector, placed[0], rounded, *table, placed[1]]
        in_specs = [anywhere()] * 2 + [whole_vmem()] * 4
        work = [
            pltpu.SMEM((count,), F32),
            pltpu.SMEM((2, count), jnp.int32),
            pltpu.SemaphoreType.DMA((2,)),
        ] + work
    return pl.pallas_call(
        functools.partial(
            start_kernel if placed is None else spread_kernel, reach_x, reach_y, flips
        ),
        in_specs=in_specs,
        out_specs=[whole_vmem()] * len(out_shapes),
        out_shape=out_shapes,
        scratch_shapes=work,
        compiler_params=pltpu.CompilerParams(
            vmem_limit_bytes=START_LIMIT if placed is None else VMEM_LIMIT
        ),
        cost_estimate=cost(2 * half * 256 * 512, 4 * 16 * count * REGION),
        name="start" if placed is None else "spread",
    )(*operands)


def spread_rest_kernel(flips, rounded_ref, wide_high, wide_low, high_ref, low_ref, *refs):
    outs, head = refs[:-1], refs[-1]
    both = (wide_high[...], wide_low[...])
    send_pieces(outs, flips, head, rounded_ref[...], both, high_ref, low_ref)


def spread_rest(rounded, both, table, flips):
    blocks = rounded.shape[0]
    top = up_to(2 + 2 * blocks, 16)
    shape = (top + both[0].shape[0], 2 * HALF)
    return pl.pallas_call(
        functools.partial(spread_rest_kernel, flips),
        in_specs=[whole_vmem()] * 5,
        out_specs=[whole_vmem()] * len(flips),
        out_shape=[jax.ShapeDtypeStruct(shape, jnp.int16)] * len(flips),
        scratch_shapes=[pltpu.VMEM((top, 2 * HALF), F32)],
        compiler_params=params(),
        cost_estimate=cost(2 * shape[0] * 256 * 256 * 3, 4 * shape[0] * 512),
        name="spread_rest",
    )(rounded, *both, *table)


def lines_kernel(place_ref, coeff_ref, *refs):
    out_ref = refs[-1]
    lanes = lax.broadcasted_iota(jnp.int32, (8, REGION), 1)

    def body(group, carry):
        at = pl.multiple_of(group * 16, 16)
        coeff = [coeff_ref[pl.ds(at + 8 * q, 8), :] for q in range(2)]
        for local in range(GROUP):
            panel = group * GROUP + local
            depth = place_ref[1, panel]
            shift = (depth - 4 * local) & (REGION - 1)
            inside = in_window(lanes, depth)
            for q in range(2):
                first = pl.multiple_of(panel * 16 + 8 * q, 8)
                out_ref[pl.ds(first, 8), :] = jnp.where(inside, pltpu.roll(coeff[q], shift, 1), 0.0)
        return carry

    lax.fori_loop(0, place_ref.shape[1] // GROUP, body, 0)


def sample_lines_kernel(tiles, place_ref, *refs):
    out_ref, coeff = refs[-2:]
    weave([by_depth(ref) for ref in refs[:tiles]], mixing_matrix(), coeff)
    lines_kernel(place_ref, coeff, out_ref)


def place_sample_lines(places, sample):
    count = places.shape[1]
    blocks = count // BLOCK
    tile = lambda t: pl.BlockSpec((64, BLOCK), lambda i: (0, t))
    shape = (count * 16, REGION)
    return pl.pallas_call(
        functools.partial(sample_lines_kernel, blocks),
        grid=(1,),
        in_specs=[in_smem()] + [tile(t) for t in range(blocks)],
        out_specs=pl.BlockSpec(shape, lambda i: (0, 0)),
        out_shape=jax.ShapeDtypeStruct(shape, F32),
        scratch_shapes=[pltpu.VMEM((count // GROUP * 16, BLOCK), F32)],
        compiler_params=params(),
        cost_estimate=cost(16 * count * REGION, 4 * 16 * count * REGION),
        name="place_sample_lines",
    )(places, *[sample] * blocks)


def place_lines(places, coeff, awaited):
    count = places.shape[1]
    shape = (count * 16, REGION)
    return pl.pallas_call(
        lines_kernel,
        in_specs=[in_smem(), whole_vmem()] + [anywhere()] * len(awaited),
        out_specs=whole_vmem(),
        out_shape=jax.ShapeDtypeStruct(shape, F32),
        compiler_params=params(),
        cost_estimate=cost(16 * count * REGION, 4 * 16 * count * REGION),
        name="place_lines",
    )(places, coeff, *awaited)


def put_edges(opened, reach_x, reach_y, edges, first):
    half = reach_x // 2
    low = low_lanes(reach_y)
    layer = lambda i: opened[i * reach_y : (i + 1) * reach_y, :]
    for two in range(2):
        place = slice(first + two * reach_y, first + (two + 1) * reach_y)
        edges[0, place, :] = jnp.where(low, layer(2 * two), swap(layer(2 * two + 1)))
        last = half - 4 + 2 * two
        edges[1, place, :] = jnp.where(low, swap(layer(last)), layer(last + 1))


def stack_layers(layers, at, reach_y, stacked):
    tall = stacked.shape[0] // len(layers)
    place = at * up_to(reach_y, 8)
    for i, layer in enumerate(layers):
        stacked[pl.ds(pl.multiple_of(i * tall + place, 8), reach_y), :] = layer


def stack_pieces(parts, reach_x, reach_y, top, opened, stacked, edges, places):
    chip = lax.axis_index("narrow")
    for flip, (part, place) in enumerate(zip(parts, places)):
        first = from_short(part[:top, :])
        opened[...] = from_short(part[top:, :]) * unit(first[0:1], first[1:2])
        layers = [opened[i * reach_y : (i + 1) * reach_y, :] for i in range(reach_x // 2)]
        stack_layers(layers, chip ^ flip, reach_y, stacked)
        put_edges(opened, reach_x, reach_y, edges, place * 2 * reach_y)


def transform_pieces(table, stacked, before, spectrum):
    half = spectrum.shape[0]
    tall = stacked.shape[0] // half

    def tripled(values):
        high, low = split(values)
        return jnp.concatenate([high, low, high], axis=0)

    for i in range(0, half, 2):
        places = range(i, min(i + 2, half))
        held = jnp.concatenate([stacked[j * tall : (j + 1) * tall, :] for j in places], axis=1)
        result = dot(table, tripled(held))
        for j in places:
            made = result[:, (j - i) * 2 * HALF : (j - i + 1) * 2 * HALF]
            spectrum[j] = made if before is None else before[j] + made


def forward_early_kernel(reach_x, reach_y, chips, *refs):
    parts = refs[:chips]
    table_ref, spectrum, edges, opened, stacked = refs[chips:]
    top = parts[0].shape[0] - opened.shape[0]
    stacked[...] = jnp.zeros_like(stacked)
    stack_pieces(parts, reach_x, reach_y, top, opened, stacked, edges, range(chips))
    transform_pieces(table_ref[lax.axis_index("pair")], stacked, None, spectrum)


def stacking_scratch(chips, reach_x, reach_y):
    half = reach_x // 2
    return [
        pltpu.VMEM((up_to(half * reach_y, 16), 2 * HALF), F32),
        pltpu.VMEM((half * chips * up_to(reach_y, 8), 2 * HALF), F32),
    ]


def forward_early(parts, table, reach_x, reach_y):
    half = reach_x // 2
    chips = len(parts)
    return pl.pallas_call(
        functools.partial(forward_early_kernel, reach_x, reach_y, chips),
        in_specs=[whole_vmem()] * (chips + 1),
        out_specs=[whole_vmem()] * 2,
        out_shape=[
            jax.ShapeDtypeStruct((half, GRID, 2 * HALF), F32),
            jax.ShapeDtypeStruct((2, chips * 2 * reach_y, 2 * HALF), F32),
        ],
        scratch_shapes=stacking_scratch(chips, reach_x, reach_y),
        compiler_params=params(),
        cost_estimate=cost(EARLY_FLOPS, 4 * half * GRID * 2 * HALF * 2),
        name="forward_early",
    )(*parts, table)


def forward_kernel(reach_x, reach_y, blocks, pieces, awaited, *refs):
    parts = refs[:pieces]
    early_ref, early_edges, table_ref, modes_ref = refs[pieces : pieces + 4]
    refs = refs[pieces + 4 + awaited :]
    spectrum, even_out, layers_out, odd_out, own_out, peers_out, inner_out, *refs = refs
    opened, stacked, edges, slabs, head = refs
    half = reach_x // 2
    pair = lax.axis_size("pair")
    top = parts[0].shape[0] - opened.shape[0]
    stacked[...] = jnp.zeros_like(stacked)
    head[...] = jnp.zeros_like(head)
    for piece in range(pieces):
        first = from_short(parts[piece][:top, :])
        mantissa, exponent = first[2 : 2 + blocks], first[2 + blocks : 2 + 2 * blocks]
        peers_out[piece * blocks : (piece + 1) * blocks, :] = decode_rounded(mantissa, exponent)
        at = 6 + 2 * piece * blocks
        head[at : at + blocks, :] = mantissa
        head[at + blocks : at + 2 * blocks, :] = exponent
    rows = 2 * reach_y
    for chip in range(pieces // pair):
        place = chip * pair * rows
        edges[:, place : place + rows, :] = early_edges[:, chip * rows : (chip + 1) * rows, :]
    before = early_ref
    for core in range(1, pair):
        places = range(core, pieces, pair)
        stack_pieces(parts[core::pair], reach_x, reach_y, top, opened, stacked, edges, places)
        transform_pieces(table_ref[lax.axis_index("pair") ^ core], stacked, before, spectrum)
        before = spectrum

    chunk = 64

    def body(index, largest):
        rows = pl.ds(pl.multiple_of(index * chunk, chunk), chunk)
        low = low_lanes(chunk)
        decay = modes_ref[0, rows, :]
        log_decay = modes_ref[1, rows, :]
        across_half = jnp.exp(half * log_decay)
        across_cut = jnp.exp((half - 4) * log_decay)
        layers = [spectrum[i, rows, :] for i in range(half)]
        run = layers[0]
        cut_right = run
        for i in range(1, half):
            run = decay * run + layers[i]
            if i == half - 5:
                cut_right = run
        right = run
        run = layers[half - 1]
        cut_left = run
        for i in range(half - 2, -1, -1):
            run = decay * run + layers[i]
            if i == 4:
                cut_left = run
        left = run
        inner_out[rows, :] = jnp.where(low, right, left)
        swapped_right, swapped_left = swap(right), swap(left)
        own = jnp.where(low, left + across_half * swapped_left, right + across_half * swapped_right)
        own_out[rows, :] = own
        made = [
            jnp.where(low, own, cut_right + across_cut * swapped_right),
            jnp.where(low, cut_left + across_cut * swapped_left, own),
        ]
        for slab, values in enumerate(made):
            slabs[slab, rows, :] = values
        return tuple(
            jnp.maximum(old, jnp.max(jnp.abs(values).reshape(chunk // 8, 8, 2 * HALF), axis=0))
            for old, values in zip(largest, made)
        )

    zero = jnp.zeros((8, 2 * HALF), F32)
    largest = lax.fori_loop(0, GRID // chunk, body, (zero,) * 2)
    top = head.shape[0]
    low = low_lanes(GRID // 2)
    upper, lower = own_out[: GRID // 2, :], own_out[GRID // 2 :, :]
    packed = [jnp.where(low, swap(upper), lower), jnp.where(low, upper, swap(lower))]

    def send(out, first, parts):
        place = first
        for index, (values, most) in enumerate(parts):
            exponent, fraction = fit_scale(jnp.max(most, axis=0, keepdims=True))
            head[2 * index : 2 * index + 1, :] = exponent
            head[2 * index + 1 : 2 * index + 2, :] = fraction
            out[place : place + values.shape[0], :] = quantize(values, exponent, fraction)
            place += values.shape[0]
        out[:first, :] = to_short(head[:first, :])

    with_most = lambda values: (values, jnp.abs(values))
    on_left = lax.axis_index("wide") & 1
    for side, (even, odd) in enumerate(((0, 1), (1, 0))):

        @pl.when(on_left == side)
        def _():
            send(even_out, top, [(slabs[even], largest[even]), with_most(packed[even])])
            send(layers_out, 16, [with_most(edges[1 - even])])
            send(odd_out, top, [(slabs[odd], largest[odd]), with_most(edges[1 - odd])])


def forward(parts, early, early_edges, table, modes, reach_x, reach_y, blocks, awaited):
    pieces = len(parts)
    half = reach_x // 2
    lanes = 2 * HALF
    head = up_to(6 + 2 * pieces * blocks, 16)
    border = pieces * 2 * reach_y
    short = lambda rows: jax.ShapeDtypeStruct((rows, lanes), jnp.int16)
    return pl.pallas_call(
        functools.partial(
            forward_kernel, reach_x, reach_y, blocks, pieces, len(awaited)
        ),
        in_specs=[whole_vmem()] * (pieces + 4) + [anywhere()] * len(awaited),
        out_specs=[whole_vmem()] * 7,
        out_shape=[
            jax.ShapeDtypeStruct((half, GRID, lanes), F32),
            short(head + GRID + GRID // 2),
            short(16 + border),
            short(head + GRID + border),
            jax.ShapeDtypeStruct((GRID, lanes), F32),
            jax.ShapeDtypeStruct((pieces * blocks, BLOCK), F32),
            jax.ShapeDtypeStruct((GRID, lanes), F32),
        ],
        scratch_shapes=stacking_scratch(pieces // table.shape[0], reach_x, reach_y)
        + [
            pltpu.VMEM((2, border, lanes), F32),
            pltpu.VMEM((2, GRID, lanes), F32),
            pltpu.VMEM((head, lanes), F32),
        ],
        compiler_params=params(),
        cost_estimate=cost(2 * half * 256 * 256 * 128, 4 * half * GRID * lanes * 2),
        name="forward",
    )(*parts, early, early_edges, table, modes, *awaited)


def opened_part(ref, index, first, rows):
    head = from_short(ref[:16, :])
    scale = unit(head[2 * index : 2 * index + 1], head[2 * index + 1 : 2 * index + 2])
    return from_short(ref[first : first + rows, :]) * scale


def pair_kernel(reach_x, flips, own_ref, even_ref, modes_ref, *refs):
    outs, head = refs[:-1], refs[-1]
    span = reach_x - 4
    here = lax.axis_index("wide")
    low = low_lanes(GRID)
    log_decay = modes_ref[1]
    own = own_ref[...]
    top = even_ref.shape[0] - GRID - GRID // 2
    cut = opened_part(even_ref, 0, top, GRID)
    packed = opened_part(even_ref, 1, top + GRID, GRID // 2)
    from_left = jnp.where(low, cut, jnp.concatenate([swap(packed), packed], axis=0))
    from_right = jnp.where(low, jnp.concatenate([packed, swap(packed)], axis=0), cut)
    partner = jnp.where((here & 1) == 1, from_left, from_right)

    def weight(distances):
        powers = []
        for distance in distances:
            ahead = span * distance - reach_x
            powers.append(jnp.where(distance >= 2, ahead, ahead + GRID).astype(F32))
        return jnp.exp(jnp.where(low, *powers) * log_decay)

    head[...] = jnp.zeros_like(head)
    for flip, out in zip(flips, outs):
        behind = (here ^ flip) - here
        message = own * weight((-behind, behind))
        behind = (here ^ flip) - (here ^ 1)
        beside = jnp.where(jnp.abs(behind) == 1, 0.0, 1.0)
        send_piece(out, head, message + partner * (weight((-behind, behind)) * beside))


def pair_messages(own, from_even, modes, reach_x, flips):
    return pl.pallas_call(
        functools.partial(pair_kernel, reach_x, flips),
        in_specs=[whole_vmem()] * 3,
        out_specs=[whole_vmem()] * len(flips),
        out_shape=[jax.ShapeDtypeStruct((16 + GRID, 2 * HALF), jnp.int16)] * len(flips),
        scratch_shapes=[pltpu.VMEM((16, 2 * HALF), F32)],
        compiler_params=params(),
        cost_estimate=cost(16 * GRID * 2 * HALF, 4 * GRID * 2 * HALF * (6 + len(flips))),
        name="pair_messages",
    )(own, from_even, modes)


def borders_kernel(reach_y, pieces, layers_ref, odd_ref, table_ref, out_ref, stacked, partial):
    on_left = (lax.axis_index("wide") & 1) == 1
    pair = lax.axis_size("pair")
    rows = pieces * 2 * reach_y
    even = opened_part(layers_ref, 0, 16, rows)
    odd = opened_part(odd_ref, 1, odd_ref.shape[0] - rows, rows)
    left, right = jnp.where(on_left, even, odd), jnp.where(on_left, odd, even)
    low = low_lanes(rows)
    both = [jnp.where(low, left, swap(right)), jnp.where(low, swap(left), right)]
    core = lax.axis_index("pair")
    chip = lax.axis_index("narrow")
    stacked[...] = jnp.zeros_like(stacked)
    before = None
    for other in range(pair):
        for flip in range(pieces // pair):
            first = (flip * pair + other) * 2 * reach_y
            layers = [
                values[first + two * reach_y : first + (two + 1) * reach_y]
                for two in range(2)
                for values in both
            ]
            stack_layers(layers, chip ^ flip, reach_y, stacked)
        target = out_ref if other == pair - 1 else partial
        transform_pieces(table_ref[core ^ other], stacked, before, target)
        before = target


def borders(layers, from_odd, table, reach_y, pieces):
    chips = pieces // table.shape[0]
    shape = (4, GRID, 2 * HALF)
    return pl.pallas_call(
        functools.partial(borders_kernel, reach_y, pieces),
        in_specs=[whole_vmem()] * 3,
        out_specs=whole_vmem(),
        out_shape=jax.ShapeDtypeStruct(shape, F32),
        scratch_shapes=[
            pltpu.VMEM((4 * chips * up_to(reach_y, 8), 2 * HALF), F32),
            pltpu.VMEM(shape, F32),
        ],
        compiler_params=params(),
        cost_estimate=cost(2 * 4 * 256 * 256 * 128, 4 * 6 * GRID * 2 * HALF),
        name="borders",
    )(layers, from_odd, table)


def send_fields(outs, flips, reach_y, field_high, field_low, high_ref, low_ref, ready, head):
    half = field_high.shape[0]
    mine = y_position()
    pitch = up_to(reach_y, 16)
    pick = lambda ref: jnp.concatenate([ref[mine ^ flip] for flip in flips], axis=0)
    table = (pick(high_ref), pick(low_ref))
    for i in range(0, half, 2):
        many = min(2, half - i)
        join = lambda ref: jnp.concatenate([ref[i + j] for j in range(many)], axis=1)
        result = dot_three(table, (join(field_high), join(field_low)))
        for j in range(many):
            for piece in range(len(flips)):
                ready[piece, (i + j) * reach_y : (i + j + 1) * reach_y, :] = result[
                    piece * pitch : piece * pitch + reach_y, j * 2 * HALF : (j + 1) * 2 * HALF
                ]
    head[...] = jnp.zeros_like(head)
    for piece, out in enumerate(outs):
        if ready.shape[1] > half * reach_y:
            ready[piece, half * reach_y :, :] = jnp.zeros_like(ready[piece, half * reach_y :, :])
        send_piece(out, head, ready[piece])


def inverse_kernel(reach_x, reach_y, flips, fars, *refs):
    spectrum, border_ref, from_even, from_odd, own_ref, inner_ref, *far_refs = refs[: 6 + fars]
    refs = refs[6 + fars :]
    high_ref, low_ref, modes_ref = refs[:3]
    outs = refs[3 : 3 + len(flips)]
    field_high, field_low, ready, head = refs[3 + len(flips) :]
    half = reach_x // 2
    span = reach_x - 4
    chunk = 64
    head_rows = from_even.shape[0] - GRID - GRID // 2
    on_left = (lax.axis_index("wide") & 1) == 1
    moment_units = []
    for ref in (from_even, from_odd):
        first = from_short(ref[:16, :])
        moment_units.append(unit(first[0:1], first[1:2]))

    far_units = []
    for ref in far_refs:
        first = from_short(ref[:16, :])
        far_units.append(unit(first[0:1], first[1:2]))

    def body(index, carry):
        first = pl.multiple_of(index * chunk, chunk)
        rows = pl.ds(first, chunk)
        low = low_lanes(chunk)
        decay = modes_ref[0, rows, :]
        log_decay = modes_ref[1, rows, :]
        ring = modes_ref[2, rows, :]
        gain = modes_ref[3, rows, :]
        across_half = jnp.exp(half * log_decay)
        across_cut = jnp.exp((half - 4) * log_decay)
        around = jnp.exp((GRID - 4) * log_decay)
        beside = jnp.exp((GRID - reach_x - span) * log_decay)
        layers = [spectrum[i, rows, :] for i in range(half)]

        at = pl.ds(pl.multiple_of(head_rows + index * chunk, 16), chunk)
        even, odd = (
            from_short(ref[at, :]) * scale for ref, scale in zip((from_even, from_odd), moment_units)
        )
        left_moments, right_moments = jnp.where(on_left, even, odd), jnp.where(on_left, odd, even)
        border = [border_ref[i, rows, :] for i in range(4)]
        zero = jnp.zeros_like(decay)
        head_sum = border[0]
        for i in range(1, 4):
            head_sum = decay * head_sum + border[i]
        tail_sum = border[3]
        for i in range(2, -1, -1):
            tail_sum = decay * tail_sum + border[i]
        for i in range(4):
            layers[i] = layers[i] + jnp.where(low, border[i], zero)
        for i in range(4):
            place = half - 4 + i
            layers[place] = layers[place] + jnp.where(low, zero, border[i])
        total = own_ref[rows, :] * jnp.exp((GRID - reach_x) * log_decay)
        at = pl.ds(pl.multiple_of(16 + index * chunk, 16), chunk)
        for ref, scale in zip(far_refs, far_units):
            total = total + from_short(ref[at, :]) * scale
        one = jnp.ones_like(decay)
        total = total + left_moments * jnp.where(low, beside, one)
        total = total + right_moments * jnp.where(low, one, beside)
        shared = jnp.where(low, head_sum, tail_sum)
        entering = (swap(total) + around * shared) * ring
        leaving = swap(across_half * entering + across_cut * shared + inner_ref[rows, :])
        run = jnp.where(low, entering, leaving)
        forward_runs = []
        for i in range(half):
            run = decay * run + layers[i]
            forward_runs.append(run)
        run = jnp.where(low, leaving, entering)
        for i in range(half - 1, -1, -1):
            ahead = decay * run
            high, rest = split(gain * (forward_runs[i] + ahead))
            field_high[i, rows, :] = high
            field_low[i, rows, :] = rest
            run = ahead + layers[i]
        return carry

    lax.fori_loop(0, GRID // chunk, body, 0)
    send_fields(outs, flips, reach_y, field_high, field_low, high_ref, low_ref, ready, head)


def inverse(
    spectrum, border, from_even, from_odd, own, inner, fars, table, modes, reach_x, reach_y, flips
):
    half = reach_x // 2
    lanes = 2 * HALF
    body = up_to(half * reach_y, 16)
    shapes = [jax.ShapeDtypeStruct((16 + body, lanes), jnp.int16)] * len(flips)
    shapes += [jax.ShapeDtypeStruct((half, GRID, lanes), BF16)] * 2
    return pl.pallas_call(
        functools.partial(inverse_kernel, reach_x, reach_y, flips, len(fars)),
        in_specs=[whole_vmem()] * (9 + len(fars)),
        out_specs=[whole_vmem()] * len(shapes),
        out_shape=shapes,
        scratch_shapes=[
            pltpu.VMEM((len(flips), body, lanes), F32),
            pltpu.VMEM((16, lanes), F32),
        ],
        compiler_params=params(),
        cost_estimate=cost(2 * half * 256 * 256 * 128, 4 * half * GRID * lanes * 2),
        name="inverse",
    )(spectrum, border, from_even, from_odd, own, inner, *fars, *table, modes)


def inverse_rest_kernel(reach_y, flips, field_high, field_low, high_ref, low_ref, *refs):
    outs, (ready, head) = refs[: len(flips)], refs[len(flips) :]
    send_fields(outs, flips, reach_y, field_high, field_low, high_ref, low_ref, ready, head)


def inverse_rest(field, table, reach_y, flips):
    half = field[0].shape[0]
    lanes = 2 * HALF
    body = up_to(half * reach_y, 16)
    return pl.pallas_call(
        functools.partial(inverse_rest_kernel, reach_y, flips),
        in_specs=[whole_vmem()] * 4,
        out_specs=[whole_vmem()] * len(flips),
        out_shape=[jax.ShapeDtypeStruct((16 + body, lanes), jnp.int16)] * len(flips),
        scratch_shapes=[
            pltpu.VMEM((len(flips), body, lanes), F32),
            pltpu.VMEM((16, lanes), F32),
        ],
        compiler_params=params(),
        cost_estimate=cost(2 * half * 256 * 256 * 128, 4 * half * GRID * lanes * 2),
        name="inverse_rest",
    )(*field, *table)


def sum_rows(values):
    row = lax.broadcasted_iota(jnp.int32, values[0].shape, 0)
    for step in (4, 2, 1):
        low = (row & step) == 0
        paired = []
        for one, other in zip(values[: len(values) // 2], values[len(values) // 2 :]):
            kept = jnp.where(low, one, other)
            moved = jnp.where(low, other, one)
            if step == 4:
                moved = pltpu.roll(moved, 4, 0)
            else:
                moved = jnp.where(low, pltpu.roll(moved, 8 - step, 0), pltpu.roll(moved, step, 0))
            paired.append(kept + moved)
        values = paired
    return values[0]


def z_lines(parts, flips, high_ref, low_ref):
    mine = y_position()
    opened = []
    for part in parts:
        first = from_short(part[:16, :])
        opened.append(from_short(part[16:, :]) * unit(first[0:1], first[1:2]))
    values = split(jnp.concatenate(opened, axis=1))
    pick = lambda ref: jnp.concatenate([ref[mine ^ flip] for flip in flips], axis=0)
    return dot_three(values, (pick(high_ref), pick(low_ref)))


def sample_early_kernel(flips, *refs):
    *parts, high_ref, low_ref, out_ref = refs
    out_ref[...] = z_lines(parts, flips, high_ref, low_ref)


def sample_early(parts, flips, table):
    rows = parts[0].shape[0] - 16
    return pl.pallas_call(
        functools.partial(sample_early_kernel, flips),
        in_specs=[whole_vmem()] * (len(parts) + 2),
        out_specs=whole_vmem(),
        out_shape=jax.ShapeDtypeStruct((rows, 2 * REGION), F32),
        compiler_params=params(),
        cost_estimate=cost(EARLY_FLOPS, 4 * rows * 512),
        name="sample_early",
    )(*parts, *table)


def sample_kernel(last, reach_x, reach_y, flips, place_in, *refs):
    parts = refs[: len(flips)]
    early_ref, high_ref, low_ref, line_ref, own_ref, vector_ref, near_ref, out_ref = refs[
        len(flips) : len(flips) + 8
    ]
    flat, field, sums, place_ref, sem = refs[len(flips) + 8 :]
    copy = pltpu.make_async_copy(place_in, place_ref, sem)
    copy.start()
    half_rows = reach_x * reach_y // 2
    both = early_ref[...] + z_lines(parts, flips, high_ref, low_ref)
    flat[:half_rows, :] = both[:half_rows, :REGION]
    flat[half_rows:, :] = both[:half_rows, REGION:]
    for x in range(reach_x):
        layer = flat[x * reach_y : (x + 1) * reach_y, :]
        for row in pair_rows(x, reach_x, reach_y):
            field[pl.ds(row, reach_y, stride=2), :] = layer
    count = place_ref.shape[1]

    def body(group, carry):
        for eight in range(0, GROUP, 8):
            totals = []
            for local in range(eight, eight + 8):
                panel = group * GROUP + local
                row = place_ref[0, panel]
                first = pl.multiple_of(panel * 16, 16)
                totals.append(
                    field[pl.ds(row, 8), :] * line_ref[pl.ds(first, 8), :]
                    + field[pl.ds(row + 2 * reach_y, 8), :] * line_ref[pl.ds(first + 8, 8), :]
                )
            sums[pl.ds(pl.multiple_of(group * GROUP + eight, 8), 8), :] = sum_rows(totals)
        return carry

    copy.wait()
    lax.fori_loop(0, count // GROUP, body, 0)
    first, rest = split(sums[...])
    second, third = split(sums[...] - first.astype(F32))
    across = lambda values: lax.dot_general(
        jnp.ones((16, REGION), BF16),
        values,
        (((1,), (1,)), ((), ())),
        preferred_element_type=F32,
    )
    sampled = across(first) + (across(second) + across(third))
    for block in range(count // BLOCK):
        lane = slice(block * BLOCK, (block + 1) * BLOCK)
        row = slice(block, block + 1)
        vector = vector_ref[row, :]
        image = jnp.where(own_ref[row, :] == 1, 0.0, 0.5 * vector) + sampled[:1, lane]
        image = image + near_ref[row, :]
        if last:
            out_ref[0:1, lane] = vector
            out_ref[1:2, lane] = image
        else:
            out_ref[row, :] = image


def sample(last, places, parts, flips, early, table, lines, flag, vector, near, reach_x, reach_y):
    count = places.shape[1]
    blocks = count // BLOCK
    shape = (2, count) if last else (blocks, BLOCK)
    return pl.pallas_call(
        functools.partial(sample_kernel, last, reach_x, reach_y, flips),
        in_specs=[anywhere()] + [whole_vmem()] * (len(parts) + 7),
        out_specs=whole_vmem(),
        out_shape=jax.ShapeDtypeStruct(shape, F32),
        scratch_shapes=[
            pltpu.VMEM((reach_x * reach_y, REGION), F32),
            pltpu.VMEM((pair_count(reach_x, reach_y), REGION), F32),
            pltpu.VMEM((count, REGION), F32),
            pltpu.SMEM((2, count), jnp.int32),
            pltpu.SemaphoreType.DMA,
        ],
        compiler_params=params(),
        cost_estimate=cost(reach_x * reach_y * 256 * 512, 4 * 16 * count * REGION),
        name="sample",
    )(
        places,
        *parts,
        early,
        *table,
        lines,
        flag.reshape(blocks, BLOCK),
        vector.reshape(blocks, BLOCK),
        near,
    )


def near_kernel(slots, blocks, place_ref, target_ref, *refs):
    even_ref, odd_ref, peers_ref, tile_ref = refs[:4]
    out_ref, held = refs[-2:]
    count = peers_ref.shape[0]
    held[count : 2 * count, :] = peers_ref[...]
    on_left = lax.axis_index("wide") & 1
    for side, ref in ((1 - on_left, even_ref), (on_left, odd_ref)):
        top = from_short(ref[...])
        for piece in range(count // blocks):
            at = 6 + 2 * piece * blocks
            held[pl.ds(side * (2 * count) + piece * blocks, blocks), :] = decode_rounded(
                top[at : at + blocks], top[at + blocks : at + 2 * blocks]
            )
    out_ref[...] = jnp.zeros_like(out_ref)
    for slot in range(slots):
        picked = held[pl.ds(place_ref[slot], 1), :]
        picked = jnp.broadcast_to(picked, (16, BLOCK)).astype(BF16)
        product = lax.dot_general(
            picked,
            tile_ref[slot],
            (((1,), (1,)), ((), ())),
            preferred_element_type=F32,
        )
        target = pl.ds(target_ref[slot], 1)
        out_ref[target, :] = out_ref[target, :] + product[:1]


def near_field(places, targets, from_even, from_odd, peers, tiles, blocks, out_rows, awaited):
    slots = tiles.shape[0]
    head = up_to(6 + 2 * peers.shape[0], 16)
    constant = lambda shape: pl.BlockSpec(shape, lambda i: (0,) * len(shape))
    return pl.pallas_call(
        functools.partial(near_kernel, slots, blocks),
        grid=(1,),
        in_specs=[
            in_smem(),
            in_smem(),
            constant((head, BLOCK)),
            constant((head, BLOCK)),
            constant(peers.shape),
            constant(tiles.shape),
        ]
        + [anywhere()] * len(awaited),
        out_specs=constant((out_rows, BLOCK)),
        out_shape=jax.ShapeDtypeStruct((out_rows, BLOCK), F32),
        scratch_shapes=[pltpu.VMEM((3 * peers.shape[0], BLOCK), F32)],
        compiler_params=params(),
        cost_estimate=cost(2 * slots * 16 * BLOCK * BLOCK, 2 * slots * BLOCK * BLOCK),
        name="near_field",
    )(places, targets, from_even, from_odd, peers, tiles, *awaited)


def shards(
    density,
    surface_flag,
    stencil_base,
    sample_weights,
    dipole_weights,
    near_target,
    near_source,
    near_tiles,
):
    x_count = lax.axis_size("wide")
    y_count = lax.axis_size(Y_AXES)
    y_index = lax.axis_index(Y_AXES)
    pair = lax.axis_size("pair")
    span_x = REGION // x_count
    span_y = REGION // y_count
    reach_x = span_x + 4
    reach_y = span_y + 4
    count = density.shape[0]
    blocks = count // BLOCK

    z_forward, z_inverse, y_forward, y_inverse, modes = tables(y_count, pair, span_y)
    modes = lax.dynamic_index_in_dim(jnp.asarray(modes), y_index, 0, keepdims=False)

    neighbour = near_source // blocks
    flip = (y_index + neighbour % 3 - 1) ^ y_index
    sources = ((neighbour // 3) * y_count + flip) * blocks + near_source % blocks
    out_rows = up_to(blocks + 1, 8)
    live = near_target >= 0
    sources = jnp.where(live, sources, 0)
    targets = jnp.where(live, near_target, out_rows - 1)

    swaps = lambda pairs: [(i, j) for i, j in pairs] + [(j, i) for i, j in pairs]
    even_swap = swaps([(i, i + 1) for i in range(0, x_count - 1, 2)])
    odd_swap = swaps([(i, i + 1) for i in range(1, x_count - 1, 2)])
    far_flips = list(range(2, x_count, 2))

    first, rest = list(range(pair, y_count)), list(range(pair))
    same_core = list(range(0, y_count, pair))
    other_core = [flip for flip in range(y_count) if flip not in same_core]

    def turned(sent, then):
        arrived = [None] * y_count
        for flip, part in zip(first + rest, list(sent) + list(then)):
            swap_pairs = [(i, i ^ flip) for i in range(y_count)]
            arrived[flip] = part if flip == 0 else lax.ppermute(part, Y_AXES, swap_pairs)
        return arrived

    def chosen(parts, flips):
        return [parts[flip] for flip in flips]

    def convolve_and_sample(last, vector, sent, both, table, places, sample_lines, awaited):
        arrived = turned(sent, spread_rest(vector, both, table, rest))
        early, edges = forward_early(chosen(arrived, same_core), y_forward, reach_x, reach_y)
        spectrum, even_message, layers, odd_message, own, peers, inner = forward(
            arrived, early, edges, y_forward, modes, reach_x, reach_y, blocks, awaited
        )
        from_even = lax.ppermute(even_message, "wide", even_swap)
        from_odd = lax.ppermute(odd_message, "wide", odd_swap)
        even_layers = lax.ppermute(layers, "wide", even_swap)
        fars = [
            lax.ppermute(message, "wide", [(i, i ^ flip) for i in range(x_count)])
            for flip, message in zip(
                far_flips, pair_messages(own, from_even, modes, reach_x, far_flips)
            )
        ]
        *sent, high, low = inverse(
            spectrum,
            borders(even_layers, from_odd, y_forward, reach_y, y_count),
            from_even,
            from_odd,
            own,
            inner,
            fars,
            y_inverse,
            modes,
            reach_x,
            reach_y,
            first,
        )
        then = inverse_rest((high, low), y_inverse, reach_y, rest)
        near_part = near_field(
            sources, targets, from_even, from_odd, peers, near_tiles, blocks, out_rows, then[:1]
        )
        arrived = turned(sent, then)
        image = sample(
            last,
            places,
            chosen(arrived, other_core),
            other_core,
            sample_early(chosen(arrived, same_core), same_core, z_inverse),
            z_inverse,
            sample_lines,
            surface_flag,
            vector,
            near_part,
            reach_x,
            reach_y,
        )
        return image, near_part

    raw = (stencil_base, surface_flag, sample_weights, dipole_weights)
    *sent, wide_high, wide_low, source_coeff, places, vector, high, low = spread(
        density, z_forward, None, raw, reach_x, reach_y, first
    )
    z_forward = (high, low)
    sample_lines = place_sample_lines(places, sample_weights)
    vector, near_part = convolve_and_sample(
        False,
        vector,
        sent,
        (wide_high, wide_low),
        z_forward,
        places,
        sample_lines,
        [sample_lines],
    )
    source_lines = place_lines(places, source_coeff, [near_part])
    *sent, wide_high, wide_low = spread(
        vector.reshape(-1), z_forward, (places, source_lines), None, reach_x, reach_y, first
    )
    both_images, _ = convolve_and_sample(
        True, vector, sent, (wide_high, wide_low), z_forward, places, sample_lines, []
    )
    return both_images


def solution(mesh):
    panels = P(("groups",) + ALL_AXES)
    columns = P(None, ("groups",) + ALL_AXES)
    in_specs = (
        panels,
        panels,
        columns,
        columns,
        columns,
        panels,
        panels,
        P(("groups",) + ALL_AXES, None, None),
    )
    return jax.shard_map(
        shards, mesh=mesh, in_specs=in_specs, out_specs=columns, check_vma=False
    )
```

```python
import functools
import math

import jax
import jax.numpy as jnp
import numpy as np
from jax import lax
from jax.experimental import pallas as pl
from jax.experimental.pallas import tpu as pltpu
from jax.sharding import PartitionSpec as P

GRID = 256
REGION = 128
BLOCK = 128
HALF = 64
KERNEL_GAIN = 4.0
SCREEN = 1.0 / 1024.0
LN2 = math.log(2.0)
Y_AXES = ("narrow", "pair")
ALL_AXES = ("wide", "narrow", "pair")
F32 = jnp.float32
BF16 = jnp.bfloat16
VMEM_LIMIT = 24 * 1024 * 1024
START_LIMIT = VMEM_LIMIT
EARLY_FLOPS = 5 * 10**9
GROUP = 32
CHAINS = 2


def cas(angles):
    return np.cos(angles) + np.sin(angles)


def up_to(count, multiple):
    return -(-count // multiple) * multiple


def low_lanes(rows):
    return lax.broadcasted_iota(jnp.int32, (rows, 2 * HALF), 1) < HALF


def swap(values):
    return pltpu.roll(values, HALF, 1)


def split(values):
    high = values.astype(BF16)
    return high, (values - high.astype(F32)).astype(BF16)


def dot(left, right):
    return jnp.dot(left, right, preferred_element_type=F32)


def dot_three(left, right):
    return dot(left[0], right[0]) + (dot(left[0], right[1]) + dot(left[1], right[0]))


def params():
    return pltpu.CompilerParams(vmem_limit_bytes=VMEM_LIMIT)


def whole_vmem():
    return pl.BlockSpec(memory_space=pltpu.VMEM)


def anywhere():
    return pl.BlockSpec(memory_space=pl.ANY)


def in_smem():
    return pl.BlockSpec(memory_space=pltpu.SMEM)


def cost(flops, moved):
    return pl.CostEstimate(flops=flops, bytes_accessed=moved, transcendentals=0)


def full_scale(exponent, fraction):
    return fraction * jnp.exp(exponent * LN2) * (1.0 / 1024.0)


def fit_scale(largest):
    largest = jnp.maximum(largest, 1e-30)
    exponent = jnp.floor(jnp.log(largest) * (1.0 / LN2))
    fraction = jnp.ceil(largest * jnp.exp(-exponent * LN2) * 1024.0) + 1.0
    return exponent, fraction


def to_short(values):
    return values.astype(jnp.int32).astype(jnp.int16)


def from_short(values):
    return values.astype(jnp.int32).astype(F32)


def quantize(values, exponent, fraction):
    return to_short(jnp.round(values * (32767.0 / full_scale(exponent, fraction))))


def unit(exponent, fraction):
    return full_scale(exponent, fraction) * (1.0 / 32767.0)


def encode_rounded(values):
    rounded = values.astype(BF16).astype(F32)
    size = jnp.maximum(jnp.abs(rounded), 1e-30)
    exponent = jnp.floor(jnp.log(size) * (1.0 / LN2))
    return jnp.round(rounded * jnp.exp((10.0 - exponent) * LN2)), exponent


def decode_rounded(mantissa, exponent):
    return (mantissa * jnp.exp((exponent - 10.0) * LN2)).astype(BF16).astype(F32)


def send_piece(out, head, values):
    exponent, fraction = fit_scale(jnp.max(jnp.abs(values), axis=0, keepdims=True))
    head[0:1, :] = exponent
    head[1:2, :] = fraction
    top = head.shape[0]
    out[:top, :] = to_short(head[...])
    out[top:, :] = quantize(values, exponent, fraction)


def y_position():
    return lax.axis_index("narrow") * lax.axis_size("pair") + lax.axis_index("pair")


def halves(table):
    high = table.astype(jnp.bfloat16)
    return high, (table - high.astype(np.float64)).astype(jnp.bfloat16)


def tables(y_count, pair, span_y):
    depth = GRID // y_count
    reach = span_y + 4
    waves = np.arange(GRID)
    step = 2.0 * np.pi / GRID
    z_table = cas(step * np.outer(np.arange(REGION), waves))
    z_forward = np.zeros((y_count, 2 * REGION, 2 * HALF))
    z_inverse = np.zeros((y_count, 2 * HALF, 2 * REGION))
    symbols = 4.0 * np.sin(np.pi * waves / GRID) ** 2
    shift = np.full((y_count, GRID, 2 * HALF), 1.0)
    y_forward = np.zeros((GRID, y_count, up_to(reach, 8)))
    y_inverse = np.zeros((y_count, up_to(reach, 16), GRID))
    for block in range(y_count):
        mine = z_table[:, block * depth : (block + 1) * depth]
        for half in range(2):
            rows = slice(half * REGION, (half + 1) * REGION)
            lanes = slice(half * HALF, half * HALF + depth)
            z_forward[block, rows, lanes] = mine
            z_inverse[block, lanes, rows] = mine.T / GRID
            shift[block, :, lanes] = (
                SCREEN + symbols[:, None] + symbols[None, block * depth : (block + 1) * depth]
            )
        cells = block * span_y - 2 + np.arange(reach)
        y_table = cas(step * np.outer(waves, cells))
        y_forward[:, block, :reach] = y_table
        y_inverse[block, :reach] = y_table.T / GRID
    y_forward = y_forward.reshape(GRID, y_count // pair, pair, -1).transpose(2, 0, 1, 3)
    y_forward = halves(y_forward.reshape(pair, GRID, -1))
    y_forward = np.concatenate([y_forward[0], y_forward[0], y_forward[1]], axis=2)
    root = np.sqrt(shift * (shift + 4.0))
    decay = 2.0 / (2.0 + shift + root)
    log_decay = np.log(decay)
    ring = 1.0 / (1.0 - np.exp(GRID * log_decay))
    gain = KERNEL_GAIN / root
    modes = np.stack([decay, log_decay, ring, gain], axis=1).astype(np.float32)
    return (
        halves(z_forward),
        halves(z_inverse),
        y_forward,
        halves(y_inverse),
        modes,
    )


def mixing_matrix():
    place = lax.broadcasted_iota(jnp.int32, (4 * BLOCK, 4 * BLOCK), 0)
    lane = lax.broadcasted_iota(jnp.int32, (4 * BLOCK, 4 * BLOCK), 1)
    return jnp.where(lane == 4 * (place % BLOCK) + place // BLOCK, 1.0, 0.0).astype(BF16)


def weave(tiles, mixing, out):
    weights = jnp.concatenate([jnp.concatenate(tile, axis=1) for tile in tiles], axis=0)
    first, rest = split(weights)
    second, third = split(weights - first.astype(F32))
    woven = dot(first, mixing) + (dot(second, mixing) + dot(third, mixing))
    for tile in range(len(tiles)):
        for part in range(BLOCK // GROUP):
            at = (tile * (BLOCK // GROUP) + part) * 16
            lanes = slice(part * BLOCK, (part + 1) * BLOCK)
            for a in range(4):
                row = tile * 16 + 4 * a
                out[pl.ds(at + 8 * (a // 2) + a % 2, 4, stride=2), :] = woven[row : row + 4, lanes]


def by_depth(ref):
    return [ref[pl.ds(depth, 16, stride=4), :] for depth in range(4)]


def pair_rows(x, reach_x, reach_y):
    even = (x // 2) * 2 * reach_y + x % 2
    if x == 0 or x == reach_x - 1:
        return [even]
    return [even, reach_x * reach_y + ((x - 1) // 2) * 2 * reach_y + (x - 1) % 2]


def pair_count(reach_x, reach_y):
    return (2 * reach_x - 2) * reach_y


def in_window(lanes, depth):
    return ((lanes - depth) & -4) == 0


def add_panels(reach, woven, vector_ref, place_ref, weight_ref, grids):
    lanes = lax.broadcasted_iota(jnp.int32, (8, REGION), 1)

    def body(group, carry):
        at = pl.multiple_of(group * 16, 16)
        coeff = [weight_ref[pl.ds(at + 8 * q, 8), :] for q in range(2)] if woven else None
        for local in range(GROUP):
            panel = group * GROUP + local
            grid = grids[local % len(grids)]
            row = place_ref[0, panel]
            value = vector_ref[panel]
            if woven:
                depth = place_ref[1, panel]
                shift = (depth - 4 * local) & (REGION - 1)
                value = jnp.where(in_window(lanes, depth), value, 0.0)
                lines = [pltpu.roll(coeff[q], shift, 1) for q in range(2)]
            else:
                first = pl.multiple_of(panel * 16, 16)
                lines = [weight_ref[pl.ds(first + 8 * q, 8), :] for q in range(2)]
            places = [pl.ds(row, 8), pl.ds(row + 2 * reach, 8)]
            held = [grid[place, :] for place in places]
            for q in range(2):
                grid[places[q], :] = held[q] + lines[q] * value
        return carry

    lax.fori_loop(0, vector_ref.shape[0] // GROUP, body, 0)


def send_pieces(outs, flips, head, rounded, both, high_ref, low_ref):
    blocks = rounded.shape[0]
    mantissa, exponent = encode_rounded(rounded)
    head[...] = jnp.zeros_like(head)
    head[2 : 2 + blocks, :] = mantissa
    head[2 + blocks : 2 + 2 * blocks, :] = exponent
    mine = y_position()
    for at in range(0, len(flips), 2):
        pick = lambda ref: jnp.concatenate([ref[mine ^ flip] for flip in flips[at : at + 2]], axis=1)
        result = dot_three(both, (pick(high_ref), pick(low_ref)))
        for i, out in enumerate(outs[at : at + 2]):
            send_piece(out, head, result[:, i * 2 * HALF : (i + 1) * 2 * HALF])


def spread_grid(reach_x, reach_y, rounded, tables, outs, flips, wides, head, total, grids):
    for x in range(reach_x):
        parts = [
            grid[pl.ds(row, reach_y, stride=2), :]
            for row in pair_rows(x, reach_x, reach_y)
            for grid in grids
        ]
        total[x * reach_y : (x + 1) * reach_y, :] = sum(parts[1:], parts[0])
    half = reach_x * reach_y // 2
    both = jnp.concatenate([total[:half, :], total[half:, :]], axis=1)
    extra = wides[0].shape[0] - half
    if extra:
        both = jnp.concatenate([both, jnp.zeros((extra, 2 * REGION), F32)], axis=0)
    both = split(both)
    for wide, values in zip(wides, both):
        wide[...] = values
    send_pieces(outs, flips, head, rounded, both, *tables)


def start_kernel(reach_x, reach_y, flips, *refs):
    vector_in, *remote = refs[:8]
    refs = refs[8:]
    outs, refs = refs[: len(flips)], refs[len(flips) :]
    wides, (weight_ref, places_out), refs = refs[:2], refs[2:4], refs[4:]
    rounded, high, low, stencil, flag, samples, dipoles, vector_ref = refs[:8]
    place_ref, sems, head, total = refs[8:12]
    grids = refs[12:]
    tiles = samples.shape[0]
    copies = []
    fetch = lambda source, target: copies.append(
        pltpu.make_async_copy(source, target, sems.at[len(copies)])
    )
    rounded_in, high_in, low_in, stencil_in, flag_in, sample_in, dipole_in = remote
    fetch(stencil_in, stencil)
    fetch(flag_in, flag)
    fetch(vector_in, vector_ref)
    for tile in range(tiles):
        lanes = pl.ds(tile * BLOCK, BLOCK)
        fetch(sample_in.at[:, lanes], samples.at[tile])
        fetch(dipole_in.at[:, lanes], dipoles.at[tile])
    needed_first = len(copies)
    fetch(rounded_in, rounded)
    fetch(high_in, high)
    fetch(low_in, low)
    for copy in copies:
        copy.start()
    for grid in grids:
        grid[...] = jnp.zeros_like(grid)
    mixing = mixing_matrix()
    copies[0].wait()
    span_x, span_y = reach_x - 4, reach_y - 4
    local_x = stencil[0:1, :] - (lax.axis_index("wide") * span_x - 2)
    local_y = stencil[1:2, :] - (y_position() * span_y - 2)
    odd = local_x & 1
    places_out[0:1, :] = odd * (reach_x * reach_y) + (local_x >> 1) * (2 * reach_y) + 2 * local_y
    places_out[1:2, :] = stencil[2:3, :]
    to_scalar = pltpu.make_async_copy(places_out, place_ref, sems.at[len(copies)])
    to_scalar.start()
    for copy in copies[1:needed_first]:
        copy.wait()
    sources = []
    for tile in range(tiles):
        charged = flag[:, tile * BLOCK : (tile + 1) * BLOCK] == 1
        pairs = zip(by_depth(samples.at[tile]), by_depth(dipoles.at[tile]))
        sources.append([jnp.where(charged, -sample, dipole) for sample, dipole in pairs])
    weave(sources, mixing, weight_ref)
    to_scalar.wait()
    add_panels(reach_y, True, vector_ref, place_ref, weight_ref, grids)
    for copy in copies[needed_first:]:
        copy.wait()
    spread_grid(
        reach_x, reach_y, rounded[...], (high, low), outs, flips, wides, head, total, grids
    )


def spread_kernel(reach_x, reach_y, flips, *refs):
    vector_in, place_in, rounded_ref, high_ref, low_ref, line_ref = refs[:6]
    refs = refs[6:]
    outs, wides, (vector_ref, place_ref, sems, head, total), grids = (
        refs[: len(flips)],
        refs[len(flips) : len(flips) + 2],
        refs[len(flips) + 2 : len(flips) + 7],
        refs[len(flips) + 7 :],
    )
    copies = [
        pltpu.make_async_copy(vector_in, vector_ref, sems.at[0]),
        pltpu.make_async_copy(place_in, place_ref, sems.at[1]),
    ]
    for copy in copies:
        copy.start()
    for grid in grids:
        grid[...] = jnp.zeros_like(grid)
    for copy in copies:
        copy.wait()
    add_panels(reach_y, False, vector_ref, place_ref, line_ref, grids)
    spread_grid(
        reach_x,
        reach_y,
        rounded_ref[...],
        (high_ref, low_ref),
        outs,
        flips,
        wides,
        head,
        total,
        grids,
    )


def spread(vector, table, placed, raw, reach_x, reach_y, flips):
    count = vector.shape[0]
    half = reach_x * reach_y // 2
    blocks = count // BLOCK
    top = up_to(2 + 2 * blocks, 16)
    lanes = 2 * HALF
    body = up_to(half, 16)
    woven = (count // GROUP * 16, BLOCK)
    out_shapes = [jax.ShapeDtypeStruct((top + body, lanes), jnp.int16)] * len(flips)
    out_shapes += [jax.ShapeDtypeStruct((body, 2 * REGION), BF16)] * 2
    rounded = vector.reshape(blocks, BLOCK)
    work = [
        pltpu.VMEM((top, lanes), F32),
        pltpu.VMEM((reach_x * reach_y, REGION), F32),
    ] + [pltpu.VMEM((pair_count(reach_x, reach_y), REGION), F32)] * CHAINS
    if placed is None:
        stencil, flag, sample, dipole = raw
        operands = [vector, rounded, *table, stencil, flag.reshape(1, -1), sample, dipole]
        operands = [pltpu.with_memory_space_constraint(value, pltpu.HBM) for value in operands]
        in_specs = [pl.BlockSpec(memory_space=pltpu.HBM)] * 8
        out_shapes += [jax.ShapeDtypeStruct(woven, F32)]
        out_shapes += [jax.ShapeDtypeStruct((2, count), jnp.int32)]
        out_shapes += [jax.ShapeDtypeStruct(rounded.shape, F32)]
        out_shapes += [jax.ShapeDtypeStruct(values.shape, BF16) for values in table]
        tiled = pltpu.VMEM((blocks, 64, BLOCK), F32)
        work = [
            pltpu.VMEM(stencil.shape, jnp.int32),
            pltpu.VMEM((1, count), jnp.int32),
            tiled,
            tiled,
            pltpu.SMEM((count,), F32),
            pltpu.SMEM((2, count), jnp.int32),
            pltpu.SemaphoreType.DMA((7 + 2 * blocks,)),
        ] + work
    else:
        operands = [vector, placed[0], rounded, *table, placed[1]]
        in_specs = [anywhere()] * 2 + [whole_vmem()] * 4
        work = [
            pltpu.SMEM((count,), F32),
            pltpu.SMEM((2, count), jnp.int32),
            pltpu.SemaphoreType.DMA((2,)),
        ] + work
    return pl.pallas_call(
        functools.partial(
            start_kernel if placed is None else spread_kernel, reach_x, reach_y, flips
        ),
        in_specs=in_specs,
        out_specs=[whole_vmem()] * len(out_shapes),
        out_shape=out_shapes,
        scratch_shapes=work,
        compiler_params=pltpu.CompilerParams(
            vmem_limit_bytes=START_LIMIT if placed is None else VMEM_LIMIT
        ),
        cost_estimate=cost(2 * half * 256 * 512, 4 * 16 * count * REGION),
        name="start" if placed is None else "spread",
    )(*operands)


def spread_rest_kernel(flips, rounded_ref, wide_high, wide_low, high_ref, low_ref, *refs):
    outs, head = refs[:-1], refs[-1]
    both = (wide_high[...], wide_low[...])
    send_pieces(outs, flips, head, rounded_ref[...], both, high_ref, low_ref)


def spread_rest(rounded, both, table, flips):
    blocks = rounded.shape[0]
    top = up_to(2 + 2 * blocks, 16)
    shape = (top + both[0].shape[0], 2 * HALF)
    return pl.pallas_call(
        functools.partial(spread_rest_kernel, flips),
        in_specs=[whole_vmem()] * 5,
        out_specs=[whole_vmem()] * len(flips),
        out_shape=[jax.ShapeDtypeStruct(shape, jnp.int16)] * len(flips),
        scratch_shapes=[pltpu.VMEM((top, 2 * HALF), F32)],
        compiler_params=params(),
        cost_estimate=cost(2 * shape[0] * 256 * 256 * 3, 4 * shape[0] * 512),
        name="spread_rest",
    )(rounded, *both, *table)


def lines_kernel(place_ref, coeff_ref, *refs):
    out_ref = refs[-1]
    lanes = lax.broadcasted_iota(jnp.int32, (8, REGION), 1)

    def body(group, carry):
        at = pl.multiple_of(group * 16, 16)
        coeff = [coeff_ref[pl.ds(at + 8 * q, 8), :] for q in range(2)]
        for local in range(GROUP):
            panel = group * GROUP + local
            depth = place_ref[1, panel]
            shift = (depth - 4 * local) & (REGION - 1)
            inside = in_window(lanes, depth)
            for q in range(2):
                first = pl.multiple_of(panel * 16 + 8 * q, 8)
                out_ref[pl.ds(first, 8), :] = jnp.where(inside, pltpu.roll(coeff[q], shift, 1), 0.0)
        return carry

    lax.fori_loop(0, place_ref.shape[1] // GROUP, body, 0)


def sample_lines_kernel(tiles, place_ref, *refs):
    out_ref, coeff = refs[-2:]
    weave([by_depth(ref) for ref in refs[:tiles]], mixing_matrix(), coeff)
    lines_kernel(place_ref, coeff, out_ref)


def place_sample_lines(places, sample):
    count = places.shape[1]
    blocks = count // BLOCK
    tile = lambda t: pl.BlockSpec((64, BLOCK), lambda i: (0, t))
    shape = (count * 16, REGION)
    return pl.pallas_call(
        functools.partial(sample_lines_kernel, blocks),
        grid=(1,),
        in_specs=[in_smem()] + [tile(t) for t in range(blocks)],
        out_specs=pl.BlockSpec(shape, lambda i: (0, 0)),
        out_shape=jax.ShapeDtypeStruct(shape, F32),
        scratch_shapes=[pltpu.VMEM((count // GROUP * 16, BLOCK), F32)],
        compiler_params=params(),
        cost_estimate=cost(16 * count * REGION, 4 * 16 * count * REGION),
        name="place_sample_lines",
    )(places, *[sample] * blocks)


def place_lines(places, coeff, awaited):
    count = places.shape[1]
    shape = (count * 16, REGION)
    return pl.pallas_call(
        lines_kernel,
        in_specs=[in_smem(), whole_vmem()] + [anywhere()] * len(awaited),
        out_specs=whole_vmem(),
        out_shape=jax.ShapeDtypeStruct(shape, F32),
        compiler_params=params(),
        cost_estimate=cost(16 * count * REGION, 4 * 16 * count * REGION),
        name="place_lines",
    )(places, coeff, *awaited)


def put_edges(opened, reach_x, reach_y, edges, first):
    half = reach_x // 2
    low = low_lanes(reach_y)
    layer = lambda i: opened[i * reach_y : (i + 1) * reach_y, :]
    for two in range(2):
        place = slice(first + two * reach_y, first + (two + 1) * reach_y)
        edges[0, place, :] = jnp.where(low, layer(2 * two), swap(layer(2 * two + 1)))
        last = half - 4 + 2 * two
        edges[1, place, :] = jnp.where(low, swap(layer(last)), layer(last + 1))


def stack_layers(layers, at, reach_y, stacked):
    tall = stacked.shape[0] // len(layers)
    place = at * up_to(reach_y, 8)
    for i, layer in enumerate(layers):
        stacked[pl.ds(pl.multiple_of(i * tall + place, 8), reach_y), :] = layer


def stack_pieces(parts, reach_x, reach_y, top, opened, stacked, edges, places):
    chip = lax.axis_index("narrow")
    for flip, (part, place) in enumerate(zip(parts, places)):
        first = from_short(part[:top, :])
        opened[...] = from_short(part[top:, :]) * unit(first[0:1], first[1:2])
        layers = [opened[i * reach_y : (i + 1) * reach_y, :] for i in range(reach_x // 2)]
        stack_layers(layers, chip ^ flip, reach_y, stacked)
        put_edges(opened, reach_x, reach_y, edges, place * 2 * reach_y)


def transform_pieces(table, stacked, before, spectrum):
    half = spectrum.shape[0]
    tall = stacked.shape[0] // half

    def tripled(values):
        high, low = split(values)
        return jnp.concatenate([high, low, high], axis=0)

    for i in range(0, half, 2):
        places = range(i, min(i + 2, half))
        held = jnp.concatenate([stacked[j * tall : (j + 1) * tall, :] for j in places], axis=1)
        result = dot(table, tripled(held))
        for j in places:
            made = result[:, (j - i) * 2 * HALF : (j - i + 1) * 2 * HALF]
            spectrum[j] = made if before is None else before[j] + made


def forward_early_kernel(reach_x, reach_y, chips, *refs):
    parts = refs[:chips]
    table_ref, spectrum, edges, opened, stacked = refs[chips:]
    top = parts[0].shape[0] - opened.shape[0]
    stacked[...] = jnp.zeros_like(stacked)
    stack_pieces(parts, reach_x, reach_y, top, opened, stacked, edges, range(chips))
    transform_pieces(table_ref[lax.axis_index("pair")], stacked, None, spectrum)


def stacking_scratch(chips, reach_x, reach_y):
    half = reach_x // 2
    return [
        pltpu.VMEM((up_to(half * reach_y, 16), 2 * HALF), F32),
        pltpu.VMEM((half * chips * up_to(reach_y, 8), 2 * HALF), F32),
    ]


def forward_early(parts, table, reach_x, reach_y):
    half = reach_x // 2
    chips = len(parts)
    return pl.pallas_call(
        functools.partial(forward_early_kernel, reach_x, reach_y, chips),
        in_specs=[whole_vmem()] * (chips + 1),
        out_specs=[whole_vmem()] * 2,
        out_shape=[
            jax.ShapeDtypeStruct((half, GRID, 2 * HALF), F32),
            jax.ShapeDtypeStruct((2, chips * 2 * reach_y, 2 * HALF), F32),
        ],
        scratch_shapes=stacking_scratch(chips, reach_x, reach_y),
        compiler_params=params(),
        cost_estimate=cost(EARLY_FLOPS, 4 * half * GRID * 2 * HALF * 2),
        name="forward_early",
    )(*parts, table)


def forward_kernel(reach_x, reach_y, blocks, pieces, awaited, *refs):
    parts = refs[:pieces]
    early_ref, early_edges, table_ref, modes_ref = refs[pieces : pieces + 4]
    refs = refs[pieces + 4 + awaited :]
    spectrum, even_out, layers_out, odd_out, own_out, peers_out, inner_out, *refs = refs
    opened, stacked, edges, slabs, head = refs
    half = reach_x // 2
    pair = lax.axis_size("pair")
    top = parts[0].shape[0] - opened.shape[0]
    stacked[...] = jnp.zeros_like(stacked)
    head[...] = jnp.zeros_like(head)
    for piece in range(pieces):
        first = from_short(parts[piece][:top, :])
        mantissa, exponent = first[2 : 2 + blocks], first[2 + blocks : 2 + 2 * blocks]
        peers_out[piece * blocks : (piece + 1) * blocks, :] = decode_rounded(mantissa, exponent)
        at = 6 + 2 * piece * blocks
        head[at : at + blocks, :] = mantissa
        head[at + blocks : at + 2 * blocks, :] = exponent
    rows = 2 * reach_y
    for chip in range(pieces // pair):
        place = chip * pair * rows
        edges[:, place : place + rows, :] = early_edges[:, chip * rows : (chip + 1) * rows, :]
    before = early_ref
    for core in range(1, pair):
        places = range(core, pieces, pair)
        stack_pieces(parts[core::pair], reach_x, reach_y, top, opened, stacked, edges, places)
        transform_pieces(table_ref[lax.axis_index("pair") ^ core], stacked, before, spectrum)
        before = spectrum

    chunk = 128

    def body(index, largest):
        rows = pl.ds(pl.multiple_of(index * chunk, chunk), chunk)
        low = low_lanes(chunk)
        decay = modes_ref[0, rows, :]
        log_decay = modes_ref[1, rows, :]
        across_half = jnp.exp(half * log_decay)
        across_cut = jnp.exp((half - 4) * log_decay)
        layers = [spectrum[i, rows, :] for i in range(half)]
        run = layers[0]
        cut_right = run
        for i in range(1, half):
            run = decay * run + layers[i]
            if i == half - 5:
                cut_right = run
        right = run
        run = layers[half - 1]
        cut_left = run
        for i in range(half - 2, -1, -1):
            run = decay * run + layers[i]
            if i == 4:
                cut_left = run
        left = run
        inner_out[rows, :] = jnp.where(low, right, left)
        swapped_right, swapped_left = swap(right), swap(left)
        own = jnp.where(low, left + across_half * swapped_left, right + across_half * swapped_right)
        own_out[rows, :] = own
        made = [
            jnp.where(low, own, cut_right + across_cut * swapped_right),
            jnp.where(low, cut_left + across_cut * swapped_left, own),
        ]
        for slab, values in enumerate(made):
            slabs[slab, rows, :] = values
        return tuple(
            jnp.maximum(old, jnp.max(jnp.abs(values).reshape(chunk // 8, 8, 2 * HALF), axis=0))
            for old, values in zip(largest, made)
        )

    zero = jnp.zeros((8, 2 * HALF), F32)
    largest = lax.fori_loop(0, GRID // chunk, body, (zero,) * 2)
    top = head.shape[0]
    low = low_lanes(GRID // 2)
    upper, lower = own_out[: GRID // 2, :], own_out[GRID // 2 :, :]
    packed = [jnp.where(low, swap(upper), lower), jnp.where(low, upper, swap(lower))]

    def send(out, first, parts):
        place = first
        for index, (values, most) in enumerate(parts):
            exponent, fraction = fit_scale(jnp.max(most, axis=0, keepdims=True))
            head[2 * index : 2 * index + 1, :] = exponent
            head[2 * index + 1 : 2 * index + 2, :] = fraction
            out[place : place + values.shape[0], :] = quantize(values, exponent, fraction)
            place += values.shape[0]
        out[:first, :] = to_short(head[:first, :])

    with_most = lambda values: (values, jnp.abs(values))
    on_left = lax.axis_index("wide") & 1
    for side, (even, odd) in enumerate(((0, 1), (1, 0))):

        @pl.when(on_left == side)
        def _():
            send(even_out, top, [(slabs[even], largest[even]), with_most(packed[even])])
            send(layers_out, 16, [with_most(edges[1 - even])])
            send(odd_out, top, [(slabs[odd], largest[odd]), with_most(edges[1 - odd])])


def forward(parts, early, early_edges, table, modes, reach_x, reach_y, blocks, awaited):
    pieces = len(parts)
    half = reach_x // 2
    lanes = 2 * HALF
    head = up_to(6 + 2 * pieces * blocks, 16)
    border = pieces * 2 * reach_y
    short = lambda rows: jax.ShapeDtypeStruct((rows, lanes), jnp.int16)
    return pl.pallas_call(
        functools.partial(
            forward_kernel, reach_x, reach_y, blocks, pieces, len(awaited)
        ),
        in_specs=[whole_vmem()] * (pieces + 4) + [anywhere()] * len(awaited),
        out_specs=[whole_vmem()] * 7,
        out_shape=[
            jax.ShapeDtypeStruct((half, GRID, lanes), F32),
            short(head + GRID + GRID // 2),
            short(16 + border),
            short(head + GRID + border),
            jax.ShapeDtypeStruct((GRID, lanes), F32),
            jax.ShapeDtypeStruct((pieces * blocks, BLOCK), F32),
            jax.ShapeDtypeStruct((GRID, lanes), F32),
        ],
        scratch_shapes=stacking_scratch(pieces // table.shape[0], reach_x, reach_y)
        + [
            pltpu.VMEM((2, border, lanes), F32),
            pltpu.VMEM((2, GRID, lanes), F32),
            pltpu.VMEM((head, lanes), F32),
        ],
        compiler_params=params(),
        cost_estimate=cost(2 * half * 256 * 256 * 128, 4 * half * GRID * lanes * 2),
        name="forward",
    )(*parts, early, early_edges, table, modes, *awaited)


def opened_part(ref, index, first, rows):
    head = from_short(ref[:16, :])
    scale = unit(head[2 * index : 2 * index + 1], head[2 * index + 1 : 2 * index + 2])
    return from_short(ref[first : first + rows, :]) * scale


def pair_kernel(reach_x, flips, own_ref, even_ref, modes_ref, *refs):
    outs, head = refs[:-1], refs[-1]
    span = reach_x - 4
    here = lax.axis_index("wide")
    low = low_lanes(GRID)
    log_decay = modes_ref[1]
    own = own_ref[...]
    top = even_ref.shape[0] - GRID - GRID // 2
    cut = opened_part(even_ref, 0, top, GRID)
    packed = opened_part(even_ref, 1, top + GRID, GRID // 2)
    from_left = jnp.where(low, cut, jnp.concatenate([swap(packed), packed], axis=0))
    from_right = jnp.where(low, jnp.concatenate([packed, swap(packed)], axis=0), cut)
    partner = jnp.where((here & 1) == 1, from_left, from_right)

    def weight(distances):
        powers = []
        for distance in distances:
            ahead = span * distance - reach_x
            powers.append(jnp.where(distance >= 2, ahead, ahead + GRID).astype(F32))
        return jnp.exp(jnp.where(low, *powers) * log_decay)

    head[...] = jnp.zeros_like(head)
    for flip, out in zip(flips, outs):
        behind = (here ^ flip) - here
        message = own * weight((-behind, behind))
        behind = (here ^ flip) - (here ^ 1)
        beside = jnp.where(jnp.abs(behind) == 1, 0.0, 1.0)
        send_piece(out, head, message + partner * (weight((-behind, behind)) * beside))


def pair_messages(own, from_even, modes, reach_x, flips):
    return pl.pallas_call(
        functools.partial(pair_kernel, reach_x, flips),
        in_specs=[whole_vmem()] * 3,
        out_specs=[whole_vmem()] * len(flips),
        out_shape=[jax.ShapeDtypeStruct((16 + GRID, 2 * HALF), jnp.int16)] * len(flips),
        scratch_shapes=[pltpu.VMEM((16, 2 * HALF), F32)],
        compiler_params=params(),
        cost_estimate=cost(16 * GRID * 2 * HALF, 4 * GRID * 2 * HALF * (6 + len(flips))),
        name="pair_messages",
    )(own, from_even, modes)


def borders_kernel(reach_y, pieces, layers_ref, odd_ref, table_ref, out_ref, stacked, partial):
    on_left = (lax.axis_index("wide") & 1) == 1
    pair = lax.axis_size("pair")
    rows = pieces * 2 * reach_y
    even = opened_part(layers_ref, 0, 16, rows)
    odd = opened_part(odd_ref, 1, odd_ref.shape[0] - rows, rows)
    left, right = jnp.where(on_left, even, odd), jnp.where(on_left, odd, even)
    low = low_lanes(rows)
    both = [jnp.where(low, left, swap(right)), jnp.where(low, swap(left), right)]
    core = lax.axis_index("pair")
    chip = lax.axis_index("narrow")
    stacked[...] = jnp.zeros_like(stacked)
    before = None
    for other in range(pair):
        for flip in range(pieces // pair):
            first = (flip * pair + other) * 2 * reach_y
            layers = [
                values[first + two * reach_y : first + (two + 1) * reach_y]
                for two in range(2)
                for values in both
            ]
            stack_layers(layers, chip ^ flip, reach_y, stacked)
        target = out_ref if other == pair - 1 else partial
        transform_pieces(table_ref[core ^ other], stacked, before, target)
        before = target


def borders(layers, from_odd, table, reach_y, pieces):
    chips = pieces // table.shape[0]
    shape = (4, GRID, 2 * HALF)
    return pl.pallas_call(
        functools.partial(borders_kernel, reach_y, pieces),
        in_specs=[whole_vmem()] * 3,
        out_specs=whole_vmem(),
        out_shape=jax.ShapeDtypeStruct(shape, F32),
        scratch_shapes=[
            pltpu.VMEM((4 * chips * up_to(reach_y, 8), 2 * HALF), F32),
            pltpu.VMEM(shape, F32),
        ],
        compiler_params=params(),
        cost_estimate=cost(2 * 4 * 256 * 256 * 128, 4 * 6 * GRID * 2 * HALF),
        name="borders",
    )(layers, from_odd, table)


def send_fields(outs, flips, reach_y, field_high, field_low, high_ref, low_ref, ready, head):
    half = field_high.shape[0]
    mine = y_position()
    pitch = up_to(reach_y, 16)
    pick = lambda ref: jnp.concatenate([ref[mine ^ flip] for flip in flips], axis=0)
    table = (pick(high_ref), pick(low_ref))
    for i in range(0, half, 2):
        many = min(2, half - i)
        join = lambda ref: jnp.concatenate([ref[i + j] for j in range(many)], axis=1)
        result = dot_three(table, (join(field_high), join(field_low)))
        for j in range(many):
            for piece in range(len(flips)):
                ready[piece, (i + j) * reach_y : (i + j + 1) * reach_y, :] = result[
                    piece * pitch : piece * pitch + reach_y, j * 2 * HALF : (j + 1) * 2 * HALF
                ]
    head[...] = jnp.zeros_like(head)
    for piece, out in enumerate(outs):
        if ready.shape[1] > half * reach_y:
            ready[piece, half * reach_y :, :] = jnp.zeros_like(ready[piece, half * reach_y :, :])
        send_piece(out, head, ready[piece])


def inverse_kernel(reach_x, reach_y, flips, fars, *refs):
    spectrum, border_ref, from_even, from_odd, own_ref, inner_ref, *far_refs = refs[: 6 + fars]
    refs = refs[6 + fars :]
    high_ref, low_ref, modes_ref = refs[:3]
    outs = refs[3 : 3 + len(flips)]
    field_high, field_low, ready, head = refs[3 + len(flips) :]
    half = reach_x // 2
    span = reach_x - 4
    chunk = 128
    head_rows = from_even.shape[0] - GRID - GRID // 2
    on_left = (lax.axis_index("wide") & 1) == 1
    moment_units = []
    for ref in (from_even, from_odd):
        first = from_short(ref[:16, :])
        moment_units.append(unit(first[0:1], first[1:2]))

    far_units = []
    for ref in far_refs:
        first = from_short(ref[:16, :])
        far_units.append(unit(first[0:1], first[1:2]))

    def body(index, carry):
        first = pl.multiple_of(index * chunk, chunk)
        rows = pl.ds(first, chunk)
        low = low_lanes(chunk)
        decay = modes_ref[0, rows, :]
        log_decay = modes_ref[1, rows, :]
        ring = modes_ref[2, rows, :]
        gain = modes_ref[3, rows, :]
        across_half = jnp.exp(half * log_decay)
        across_cut = jnp.exp((half - 4) * log_decay)
        around = jnp.exp((GRID - 4) * log_decay)
        beside = jnp.exp((GRID - reach_x - span) * log_decay)
        layers = [spectrum[i, rows, :] for i in range(half)]

        at = pl.ds(pl.multiple_of(head_rows + index * chunk, 16), chunk)
        even, odd = (
            from_short(ref[at, :]) * scale for ref, scale in zip((from_even, from_odd), moment_units)
        )
        left_moments, right_moments = jnp.where(on_left, even, odd), jnp.where(on_left, odd, even)
        border = [border_ref[i, rows, :] for i in range(4)]
        zero = jnp.zeros_like(decay)
        head_sum = border[0]
        for i in range(1, 4):
            head_sum = decay * head_sum + border[i]
        tail_sum = border[3]
        for i in range(2, -1, -1):
            tail_sum = decay * tail_sum + border[i]
        for i in range(4):
            layers[i] = layers[i] + jnp.where(low, border[i], zero)
        for i in range(4):
            place = half - 4 + i
            layers[place] = layers[place] + jnp.where(low, zero, border[i])
        total = own_ref[rows, :] * jnp.exp((GRID - reach_x) * log_decay)
        at = pl.ds(pl.multiple_of(16 + index * chunk, 16), chunk)
        for ref, scale in zip(far_refs, far_units):
            total = total + from_short(ref[at, :]) * scale
        one = jnp.ones_like(decay)
        total = total + left_moments * jnp.where(low, beside, one)
        total = total + right_moments * jnp.where(low, one, beside)
        shared = jnp.where(low, head_sum, tail_sum)
        entering = (swap(total) + around * shared) * ring
        leaving = swap(across_half * entering + across_cut * shared + inner_ref[rows, :])
        run = jnp.where(low, entering, leaving)
        forward_runs = []
        for i in range(half):
            run = decay * run + layers[i]
            forward_runs.append(run)
        run = jnp.where(low, leaving, entering)
        for i in range(half - 1, -1, -1):
            ahead = decay * run
            high, rest = split(gain * (forward_runs[i] + ahead))
            field_high[i, rows, :] = high
            field_low[i, rows, :] = rest
            run = ahead + layers[i]
        return carry

    lax.fori_loop(0, GRID // chunk, body, 0)
    send_fields(outs, flips, reach_y, field_high, field_low, high_ref, low_ref, ready, head)


def inverse(
    spectrum, border, from_even, from_odd, own, inner, fars, table, modes, reach_x, reach_y, flips
):
    half = reach_x // 2
    lanes = 2 * HALF
    body = up_to(half * reach_y, 16)
    shapes = [jax.ShapeDtypeStruct((16 + body, lanes), jnp.int16)] * len(flips)
    shapes += [jax.ShapeDtypeStruct((half, GRID, lanes), BF16)] * 2
    return pl.pallas_call(
        functools.partial(inverse_kernel, reach_x, reach_y, flips, len(fars)),
        in_specs=[whole_vmem()] * (9 + len(fars)),
        out_specs=[whole_vmem()] * len(shapes),
        out_shape=shapes,
        scratch_shapes=[
            pltpu.VMEM((len(flips), body, lanes), F32),
            pltpu.VMEM((16, lanes), F32),
        ],
        compiler_params=params(),
        cost_estimate=cost(2 * half * 256 * 256 * 128, 4 * half * GRID * lanes * 2),
        name="inverse",
    )(spectrum, border, from_even, from_odd, own, inner, *fars, *table, modes)


def inverse_rest_kernel(reach_y, flips, field_high, field_low, high_ref, low_ref, *refs):
    outs, (ready, head) = refs[: len(flips)], refs[len(flips) :]
    send_fields(outs, flips, reach_y, field_high, field_low, high_ref, low_ref, ready, head)


def inverse_rest(field, table, reach_y, flips):
    half = field[0].shape[0]
    lanes = 2 * HALF
    body = up_to(half * reach_y, 16)
    return pl.pallas_call(
        functools.partial(inverse_rest_kernel, reach_y, flips),
        in_specs=[whole_vmem()] * 4,
        out_specs=[whole_vmem()] * len(flips),
        out_shape=[jax.ShapeDtypeStruct((16 + body, lanes), jnp.int16)] * len(flips),
        scratch_shapes=[
            pltpu.VMEM((len(flips), body, lanes), F32),
            pltpu.VMEM((16, lanes), F32),
        ],
        compiler_params=params(),
        cost_estimate=cost(2 * half * 256 * 256 * 128, 4 * half * GRID * lanes * 2),
        name="inverse_rest",
    )(*field, *table)


def sum_rows(values):
    row = lax.broadcasted_iota(jnp.int32, values[0].shape, 0)
    for step in (4, 2, 1):
        low = (row & step) == 0
        paired = []
        for one, other in zip(values[: len(values) // 2], values[len(values) // 2 :]):
            kept = jnp.where(low, one, other)
            moved = jnp.where(low, other, one)
            if step == 4:
                moved = pltpu.roll(moved, 4, 0)
            else:
                moved = jnp.where(low, pltpu.roll(moved, 8 - step, 0), pltpu.roll(moved, step, 0))
            paired.append(kept + moved)
        values = paired
    return values[0]


def z_lines(parts, flips, high_ref, low_ref):
    mine = y_position()
    opened = []
    for part in parts:
        first = from_short(part[:16, :])
        opened.append(from_short(part[16:, :]) * unit(first[0:1], first[1:2]))
    values = split(jnp.concatenate(opened, axis=1))
    pick = lambda ref: jnp.concatenate([ref[mine ^ flip] for flip in flips], axis=0)
    return dot_three(values, (pick(high_ref), pick(low_ref)))


def sample_early_kernel(flips, *refs):
    *parts, high_ref, low_ref, out_ref = refs
    out_ref[...] = z_lines(parts, flips, high_ref, low_ref)


def sample_early(parts, flips, table):
    rows = parts[0].shape[0] - 16
    return pl.pallas_call(
        functools.partial(sample_early_kernel, flips),
        in_specs=[whole_vmem()] * (len(parts) + 2),
        out_specs=whole_vmem(),
        out_shape=jax.ShapeDtypeStruct((rows, 2 * REGION), F32),
        compiler_params=params(),
        cost_estimate=cost(EARLY_FLOPS, 4 * rows * 512),
        name="sample_early",
    )(*parts, *table)


def sample_kernel(last, reach_x, reach_y, flips, place_in, *refs):
    parts = refs[: len(flips)]
    early_ref, high_ref, low_ref, line_ref, own_ref, vector_ref, near_ref, out_ref = refs[
        len(flips) : len(flips) + 8
    ]
    flat, field, sums, place_ref, sem = refs[len(flips) + 8 :]
    copy = pltpu.make_async_copy(place_in, place_ref, sem)
    copy.start()
    half_rows = reach_x * reach_y // 2
    both = early_ref[...] + z_lines(parts, flips, high_ref, low_ref)
    flat[:half_rows, :] = both[:half_rows, :REGION]
    flat[half_rows:, :] = both[:half_rows, REGION:]
    for x in range(reach_x):
        layer = flat[x * reach_y : (x + 1) * reach_y, :]
        for row in pair_rows(x, reach_x, reach_y):
            field[pl.ds(row, reach_y, stride=2), :] = layer
    count = place_ref.shape[1]

    def body(group, carry):
        for eight in range(0, GROUP, 8):
            totals = []
            for local in range(eight, eight + 8):
                panel = group * GROUP + local
                row = place_ref[0, panel]
                first = pl.multiple_of(panel * 16, 16)
                totals.append(
                    field[pl.ds(row, 8), :] * line_ref[pl.ds(first, 8), :]
                    + field[pl.ds(row + 2 * reach_y, 8), :] * line_ref[pl.ds(first + 8, 8), :]
                )
            sums[pl.ds(pl.multiple_of(group * GROUP + eight, 8), 8), :] = sum_rows(totals)
        return carry

    copy.wait()
    lax.fori_loop(0, count // GROUP, body, 0)
    first, rest = split(sums[...])
    second, third = split(sums[...] - first.astype(F32))
    across = lambda values: lax.dot_general(
        jnp.ones((16, REGION), BF16),
        values,
        (((1,), (1,)), ((), ())),
        preferred_element_type=F32,
    )
    sampled = across(first) + (across(second) + across(third))
    for block in range(count // BLOCK):
        lane = slice(block * BLOCK, (block + 1) * BLOCK)
        row = slice(block, block + 1)
        vector = vector_ref[row, :]
        image = jnp.where(own_ref[row, :] == 1, 0.0, 0.5 * vector) + sampled[:1, lane]
        image = image + near_ref[row, :]
        if last:
            out_ref[0:1, lane] = vector
            out_ref[1:2, lane] = image
        else:
            out_ref[row, :] = image


def sample(last, places, parts, flips, early, table, lines, flag, vector, near, reach_x, reach_y):
    count = places.shape[1]
    blocks = count // BLOCK
    shape = (2, count) if last else (blocks, BLOCK)
    return pl.pallas_call(
        functools.partial(sample_kernel, last, reach_x, reach_y, flips),
        in_specs=[anywhere()] + [whole_vmem()] * (len(parts) + 7),
        out_specs=whole_vmem(),
        out_shape=jax.ShapeDtypeStruct(shape, F32),
        scratch_shapes=[
            pltpu.VMEM((reach_x * reach_y, REGION), F32),
            pltpu.VMEM((pair_count(reach_x, reach_y), REGION), F32),
            pltpu.VMEM((count, REGION), F32),
            pltpu.SMEM((2, count), jnp.int32),
            pltpu.SemaphoreType.DMA,
        ],
        compiler_params=params(),
        cost_estimate=cost(reach_x * reach_y * 256 * 512, 4 * 16 * count * REGION),
        name="sample",
    )(
        places,
        *parts,
        early,
        *table,
        lines,
        flag.reshape(blocks, BLOCK),
        vector.reshape(blocks, BLOCK),
        near,
    )


def near_kernel(slots, blocks, place_ref, target_ref, *refs):
    even_ref, odd_ref, peers_ref, tile_ref = refs[:4]
    out_ref, held = refs[-2:]
    count = peers_ref.shape[0]
    held[count : 2 * count, :] = peers_ref[...]
    on_left = lax.axis_index("wide") & 1
    for side, ref in ((1 - on_left, even_ref), (on_left, odd_ref)):
        top = from_short(ref[...])
        for piece in range(count // blocks):
            at = 6 + 2 * piece * blocks
            held[pl.ds(side * (2 * count) + piece * blocks, blocks), :] = decode_rounded(
                top[at : at + blocks], top[at + blocks : at + 2 * blocks]
            )
    out_ref[...] = jnp.zeros_like(out_ref)
    for slot in range(slots):
        picked = held[pl.ds(place_ref[slot], 1), :]
        picked = jnp.broadcast_to(picked, (16, BLOCK)).astype(BF16)
        product = lax.dot_general(
            picked,
            tile_ref[slot],
            (((1,), (1,)), ((), ())),
            preferred_element_type=F32,
        )
        target = pl.ds(target_ref[slot], 1)
        out_ref[target, :] = out_ref[target, :] + product[:1]


def near_field(places, targets, from_even, from_odd, peers, tiles, blocks, out_rows, awaited):
    slots = tiles.shape[0]
    head = up_to(6 + 2 * peers.shape[0], 16)
    constant = lambda shape: pl.BlockSpec(shape, lambda i: (0,) * len(shape))
    return pl.pallas_call(
        functools.partial(near_kernel, slots, blocks),
        grid=(1,),
        in_specs=[
            in_smem(),
            in_smem(),
            constant((head, BLOCK)),
            constant((head, BLOCK)),
            constant(peers.shape),
            constant(tiles.shape),
        ]
        + [anywhere()] * len(awaited),
        out_specs=constant((out_rows, BLOCK)),
        out_shape=jax.ShapeDtypeStruct((out_rows, BLOCK), F32),
        scratch_shapes=[pltpu.VMEM((3 * peers.shape[0], BLOCK), F32)],
        compiler_params=params(),
        cost_estimate=cost(2 * slots * 16 * BLOCK * BLOCK, 2 * slots * BLOCK * BLOCK),
        name="near_field",
    )(places, targets, from_even, from_odd, peers, tiles, *awaited)


def shards(
    density,
    surface_flag,
    stencil_base,
    sample_weights,
    dipole_weights,
    near_target,
    near_source,
    near_tiles,
):
    x_count = lax.axis_size("wide")
    y_count = lax.axis_size(Y_AXES)
    y_index = lax.axis_index(Y_AXES)
    pair = lax.axis_size("pair")
    span_x = REGION // x_count
    span_y = REGION // y_count
    reach_x = span_x + 4
    reach_y = span_y + 4
    count = density.shape[0]
    blocks = count // BLOCK

    z_forward, z_inverse, y_forward, y_inverse, modes = tables(y_count, pair, span_y)
    modes = lax.dynamic_index_in_dim(jnp.asarray(modes), y_index, 0, keepdims=False)

    neighbour = near_source // blocks
    flip = (y_index + neighbour % 3 - 1) ^ y_index
    sources = ((neighbour // 3) * y_count + flip) * blocks + near_source % blocks
    out_rows = up_to(blocks + 1, 8)
    live = near_target >= 0
    sources = jnp.where(live, sources, 0)
    targets = jnp.where(live, near_target, out_rows - 1)

    swaps = lambda pairs: [(i, j) for i, j in pairs] + [(j, i) for i, j in pairs]
    even_swap = swaps([(i, i + 1) for i in range(0, x_count - 1, 2)])
    odd_swap = swaps([(i, i + 1) for i in range(1, x_count - 1, 2)])
    far_flips = list(range(2, x_count, 2))

    first, rest = list(range(pair, y_count)), list(range(pair))
    same_core = list(range(0, y_count, pair))
    other_core = [flip for flip in range(y_count) if flip not in same_core]

    def turned(sent, then):
        arrived = [None] * y_count
        for flip, part in zip(first + rest, list(sent) + list(then)):
            swap_pairs = [(i, i ^ flip) for i in range(y_count)]
            arrived[flip] = part if flip == 0 else lax.ppermute(part, Y_AXES, swap_pairs)
        return arrived

    def chosen(parts, flips):
        return [parts[flip] for flip in flips]

    def convolve_and_sample(last, vector, sent, both, table, places, sample_lines, awaited):
        arrived = turned(sent, spread_rest(vector, both, table, rest))
        early, edges = forward_early(chosen(arrived, same_core), y_forward, reach_x, reach_y)
        spectrum, even_message, layers, odd_message, own, peers, inner = forward(
            arrived, early, edges, y_forward, modes, reach_x, reach_y, blocks, awaited
        )
        from_even = lax.ppermute(even_message, "wide", even_swap)
        from_odd = lax.ppermute(odd_message, "wide", odd_swap)
        even_layers = lax.ppermute(layers, "wide", even_swap)
        fars = [
            lax.ppermute(message, "wide", [(i, i ^ flip) for i in range(x_count)])
            for flip, message in zip(
                far_flips, pair_messages(own, from_even, modes, reach_x, far_flips)
            )
        ]
        *sent, high, low = inverse(
            spectrum,
            borders(even_layers, from_odd, y_forward, reach_y, y_count),
            from_even,
            from_odd,
            own,
            inner,
            fars,
            y_inverse,
            modes,
            reach_x,
            reach_y,
            first,
        )
        then = inverse_rest((high, low), y_inverse, reach_y, rest)
        near_part = near_field(
            sources, targets, from_even, from_odd, peers, near_tiles, blocks, out_rows, then[:1]
        )
        arrived = turned(sent, then)
        image = sample(
            last,
            places,
            chosen(arrived, other_core),
            other_core,
            sample_early(chosen(arrived, same_core), same_core, z_inverse),
            z_inverse,
            sample_lines,
            surface_flag,
            vector,
            near_part,
            reach_x,
            reach_y,
        )
        return image, near_part

    raw = (stencil_base, surface_flag, sample_weights, dipole_weights)
    *sent, wide_high, wide_low, source_coeff, places, vector, high, low = spread(
        density, z_forward, None, raw, reach_x, reach_y, first
    )
    z_forward = (high, low)
    sample_lines = place_sample_lines(places, sample_weights)
    vector, near_part = convolve_and_sample(
        False,
        vector,
        sent,
        (wide_high, wide_low),
        z_forward,
        places,
        sample_lines,
        [sample_lines],
    )
    source_lines = place_lines(places, source_coeff, [near_part])
    *sent, wide_high, wide_low = spread(
        vector.reshape(-1), z_forward, (places, source_lines), None, reach_x, reach_y, first
    )
    both_images, _ = convolve_and_sample(
        True, vector, sent, (wide_high, wide_low), z_forward, places, sample_lines, []
    )
    return both_images


def solution(mesh):
    panels = P(("groups",) + ALL_AXES)
    columns = P(None, ("groups",) + ALL_AXES)
    in_specs = (
        panels,
        panels,
        columns,
        columns,
        columns,
        panels,
        panels,
        P(("groups",) + ALL_AXES, None, None),
    )
    return jax.shard_map(
        shards, mesh=mesh, in_specs=in_specs, out_specs=columns, check_vma=False
    )
```

```python
import functools
import math

import jax
import jax.numpy as jnp
import numpy as np
from jax import lax
from jax.experimental import pallas as pl
from jax.experimental.pallas import tpu as pltpu
from jax.sharding import PartitionSpec as P

GRID = 256
REGION = 128
BLOCK = 128
HALF = 64
KERNEL_GAIN = 4.0
SCREEN = 1.0 / 1024.0
LN2 = math.log(2.0)
Y_AXES = ("narrow", "pair")
ALL_AXES = ("wide", "narrow", "pair")
F32 = jnp.float32
BF16 = jnp.bfloat16
VMEM_LIMIT = 24 * 1024 * 1024
START_LIMIT = VMEM_LIMIT
EARLY_FLOPS = 5 * 10**9
GROUP = 32
CHAINS = 2


def cas(angles):
    return np.cos(angles) + np.sin(angles)


def up_to(count, multiple):
    return -(-count // multiple) * multiple


def low_lanes(rows):
    return lax.broadcasted_iota(jnp.int32, (rows, 2 * HALF), 1) < HALF


def swap(values):
    return pltpu.roll(values, HALF, 1)


def split(values):
    high = values.astype(BF16)
    return high, (values - high.astype(F32)).astype(BF16)


def dot(left, right):
    return jnp.dot(left, right, preferred_element_type=F32)


def dot_three(left, right):
    return dot(left[0], right[0]) + (dot(left[0], right[1]) + dot(left[1], right[0]))


def params():
    return pltpu.CompilerParams(vmem_limit_bytes=VMEM_LIMIT)


def whole_vmem():
    return pl.BlockSpec(memory_space=pltpu.VMEM)


def anywhere():
    return pl.BlockSpec(memory_space=pl.ANY)


def in_smem():
    return pl.BlockSpec(memory_space=pltpu.SMEM)


def cost(flops, moved):
    return pl.CostEstimate(flops=flops, bytes_accessed=moved, transcendentals=0)


def full_scale(exponent, fraction):
    return fraction * jnp.exp(exponent * LN2) * (1.0 / 1024.0)


def fit_scale(largest):
    largest = jnp.maximum(largest, 1e-30)
    exponent = jnp.floor(jnp.log(largest) * (1.0 / LN2))
    fraction = jnp.ceil(largest * jnp.exp(-exponent * LN2) * 1024.0) + 1.0
    return exponent, fraction


def to_short(values):
    return values.astype(jnp.int32).astype(jnp.int16)


def from_short(values):
    return values.astype(jnp.int32).astype(F32)


def quantize(values, exponent, fraction):
    return to_short(jnp.round(values * (32767.0 / full_scale(exponent, fraction))))


def unit(exponent, fraction):
    return full_scale(exponent, fraction) * (1.0 / 32767.0)


def encode_rounded(values):
    rounded = values.astype(BF16).astype(F32)
    size = jnp.maximum(jnp.abs(rounded), 1e-30)
    exponent = jnp.floor(jnp.log(size) * (1.0 / LN2))
    return jnp.round(rounded * jnp.exp((10.0 - exponent) * LN2)), exponent


def decode_rounded(mantissa, exponent):
    return (mantissa * jnp.exp((exponent - 10.0) * LN2)).astype(BF16).astype(F32)


def send_piece(out, head, values):
    exponent, fraction = fit_scale(jnp.max(jnp.abs(values), axis=0, keepdims=True))
    head[0:1, :] = exponent
    head[1:2, :] = fraction
    top = head.shape[0]
    out[:top, :] = to_short(head[...])
    out[top:, :] = quantize(values, exponent, fraction)


def y_position():
    return lax.axis_index("narrow") * lax.axis_size("pair") + lax.axis_index("pair")


def halves(table):
    high = table.astype(jnp.bfloat16)
    return high, (table - high.astype(np.float64)).astype(jnp.bfloat16)


def tables(y_count, pair, span_y):
    depth = GRID // y_count
    reach = span_y + 4
    waves = np.arange(GRID)
    step = 2.0 * np.pi / GRID
    z_table = cas(step * np.outer(np.arange(REGION), waves))
    z_forward = np.zeros((y_count, 2 * REGION, 2 * HALF))
    z_inverse = np.zeros((y_count, 2 * HALF, 2 * REGION))
    symbols = 4.0 * np.sin(np.pi * waves / GRID) ** 2
    shift = np.full((y_count, GRID, 2 * HALF), 1.0)
    y_forward = np.zeros((GRID, y_count, up_to(reach, 8)))
    y_inverse = np.zeros((y_count, up_to(reach, 16), GRID))
    for block in range(y_count):
        mine = z_table[:, block * depth : (block + 1) * depth]
        for half in range(2):
            rows = slice(half * REGION, (half + 1) * REGION)
            lanes = slice(half * HALF, half * HALF + depth)
            z_forward[block, rows, lanes] = mine
            z_inverse[block, lanes, rows] = mine.T / GRID
            shift[block, :, lanes] = (
                SCREEN + symbols[:, None] + symbols[None, block * depth : (block + 1) * depth]
            )
        cells = block * span_y - 2 + np.arange(reach)
        y_table = cas(step * np.outer(waves, cells))
        y_forward[:, block, :reach] = y_table
        y_inverse[block, :reach] = y_table.T / GRID
    y_forward = y_forward.reshape(GRID, y_count // pair, pair, -1).transpose(2, 0, 1, 3)
    y_forward = halves(y_forward.reshape(pair, GRID, -1))
    y_forward = np.concatenate([y_forward[0], y_forward[0], y_forward[1]], axis=2)
    root = np.sqrt(shift * (shift + 4.0))
    decay = 2.0 / (2.0 + shift + root)
    log_decay = np.log(decay)
    ring = 1.0 / (1.0 - np.exp(GRID * log_decay))
    gain = KERNEL_GAIN / root
    modes = np.stack([decay, log_decay, ring, gain], axis=1).astype(np.float32)
    return (
        halves(z_forward),
        halves(z_inverse),
        y_forward,
        halves(y_inverse),
        modes,
    )


def mixing_matrix():
    place = lax.broadcasted_iota(jnp.int32, (4 * BLOCK, 4 * BLOCK), 0)
    lane = lax.broadcasted_iota(jnp.int32, (4 * BLOCK, 4 * BLOCK), 1)
    return jnp.where(lane == 4 * (place % BLOCK) + place // BLOCK, 1.0, 0.0).astype(BF16)


def weave(tiles, mixing, out):
    weights = jnp.concatenate([jnp.concatenate(tile, axis=1) for tile in tiles], axis=0)
    first, rest = split(weights)
    second, third = split(weights - first.astype(F32))
    woven = dot(first, mixing) + (dot(second, mixing) + dot(third, mixing))
    for tile in range(len(tiles)):
        for part in range(BLOCK // GROUP):
            at = (tile * (BLOCK // GROUP) + part) * 16
            lanes = slice(part * BLOCK, (part + 1) * BLOCK)
            for a in range(4):
                row = tile * 16 + 4 * a
                out[pl.ds(at + 8 * (a // 2) + a % 2, 4, stride=2), :] = woven[row : row + 4, lanes]


def by_depth(ref):
    return [ref[pl.ds(depth, 16, stride=4), :] for depth in range(4)]


def pair_rows(x, reach_x, reach_y):
    even = (x // 2) * 2 * reach_y + x % 2
    if x == 0 or x == reach_x - 1:
        return [even]
    return [even, reach_x * reach_y + ((x - 1) // 2) * 2 * reach_y + (x - 1) % 2]


def pair_count(reach_x, reach_y):
    return (2 * reach_x - 2) * reach_y


def in_window(lanes, depth):
    return ((lanes - depth) & -4) == 0


def add_panels(reach, woven, vector_ref, place_ref, weight_ref, grids):
    lanes = lax.broadcasted_iota(jnp.int32, (8, REGION), 1)

    def body(group, carry):
        at = pl.multiple_of(group * 16, 16)
        coeff = [weight_ref[pl.ds(at + 8 * q, 8), :] for q in range(2)] if woven else None
        for local in range(GROUP):
            panel = group * GROUP + local
            grid = grids[local % len(grids)]
            row = place_ref[0, panel]
            value = vector_ref[panel]
            if woven:
                depth = place_ref[1, panel]
                shift = (depth - 4 * local) & (REGION - 1)
                value = jnp.where(in_window(lanes, depth), value, 0.0)
                lines = [pltpu.roll(coeff[q], shift, 1) for q in range(2)]
            else:
                first = pl.multiple_of(panel * 16, 16)
                lines = [weight_ref[pl.ds(first + 8 * q, 8), :] for q in range(2)]
            places = [pl.ds(row, 8), pl.ds(row + 2 * reach, 8)]
            held = [grid[place, :] for place in places]
            for q in range(2):
                grid[places[q], :] = held[q] + lines[q] * value
        return carry

    lax.fori_loop(0, vector_ref.shape[0] // GROUP, body, 0)


def send_pieces(outs, flips, head, rounded, both, high_ref, low_ref):
    blocks = rounded.shape[0]
    mantissa, exponent = encode_rounded(rounded)
    head[...] = jnp.zeros_like(head)
    head[2 : 2 + blocks, :] = mantissa
    head[2 + blocks : 2 + 2 * blocks, :] = exponent
    mine = y_position()
    for at in range(0, len(flips), 2):
        pick = lambda ref: jnp.concatenate([ref[mine ^ flip] for flip in flips[at : at + 2]], axis=1)
        result = dot_three(both, (pick(high_ref), pick(low_ref)))
        for i, out in enumerate(outs[at : at + 2]):
            send_piece(out, head, result[:, i * 2 * HALF : (i + 1) * 2 * HALF])


def spread_grid(reach_x, reach_y, rounded, tables, outs, flips, wides, head, total, grids):
    for x in range(reach_x):
        parts = [
            grid[pl.ds(row, reach_y, stride=2), :]
            for row in pair_rows(x, reach_x, reach_y)
            for grid in grids
        ]
        total[x * reach_y : (x + 1) * reach_y, :] = sum(parts[1:], parts[0])
    half = reach_x * reach_y // 2
    both = jnp.concatenate([total[:half, :], total[half:, :]], axis=1)
    extra = wides[0].shape[0] - half
    if extra:
        both = jnp.concatenate([both, jnp.zeros((extra, 2 * REGION), F32)], axis=0)
    both = split(both)
    for wide, values in zip(wides, both):
        wide[...] = values
    send_pieces(outs, flips, head, rounded, both, *tables)


def start_kernel(reach_x, reach_y, flips, *refs):
    vector_in, *remote = refs[:8]
    refs = refs[8:]
    outs, refs = refs[: len(flips)], refs[len(flips) :]
    wides, (weight_ref, places_out), refs = refs[:2], refs[2:4], refs[4:]
    rounded, high, low, stencil, flag, samples, dipoles, vector_ref = refs[:8]
    place_ref, sems, head, total = refs[8:12]
    grids = refs[12:]
    tiles = samples.shape[0]
    copies = []
    fetch = lambda source, target: copies.append(
        pltpu.make_async_copy(source, target, sems.at[len(copies)])
    )
    rounded_in, high_in, low_in, stencil_in, flag_in, sample_in, dipole_in = remote
    fetch(stencil_in, stencil)
    fetch(flag_in, flag)
    fetch(vector_in, vector_ref)
    for tile in range(tiles):
        lanes = pl.ds(tile * BLOCK, BLOCK)
        fetch(sample_in.at[:, lanes], samples.at[tile])
        fetch(dipole_in.at[:, lanes], dipoles.at[tile])
    needed_first = len(copies)
    fetch(rounded_in, rounded)
    fetch(high_in, high)
    fetch(low_in, low)
    for copy in copies:
        copy.start()
    for grid in grids:
        grid[...] = jnp.zeros_like(grid)
    mixing = mixing_matrix()
    copies[0].wait()
    span_x, span_y = reach_x - 4, reach_y - 4
    local_x = stencil[0:1, :] - (lax.axis_index("wide") * span_x - 2)
    local_y = stencil[1:2, :] - (y_position() * span_y - 2)
    odd = local_x & 1
    places_out[0:1, :] = odd * (reach_x * reach_y) + (local_x >> 1) * (2 * reach_y) + 2 * local_y
    places_out[1:2, :] = stencil[2:3, :]
    to_scalar = pltpu.make_async_copy(places_out, place_ref, sems.at[len(copies)])
    to_scalar.start()
    for copy in copies[1:needed_first]:
        copy.wait()
    sources = []
    for tile in range(tiles):
        charged = flag[:, tile * BLOCK : (tile + 1) * BLOCK] == 1
        pairs = zip(by_depth(samples.at[tile]), by_depth(dipoles.at[tile]))
        sources.append([jnp.where(charged, -sample, dipole) for sample, dipole in pairs])
    weave(sources, mixing, weight_ref)
    to_scalar.wait()
    add_panels(reach_y, True, vector_ref, place_ref, weight_ref, grids)
    for copy in copies[needed_first:]:
        copy.wait()
    spread_grid(
        reach_x, reach_y, rounded[...], (high, low), outs, flips, wides, head, total, grids
    )


def spread_kernel(reach_x, reach_y, flips, *refs):
    vector_in, place_in, rounded_ref, high_ref, low_ref, line_ref = refs[:6]
    refs = refs[6:]
    outs, wides, (vector_ref, place_ref, sems, head, total), grids = (
        refs[: len(flips)],
        refs[len(flips) : len(flips) + 2],
        refs[len(flips) + 2 : len(flips) + 7],
        refs[len(flips) + 7 :],
    )
    copies = [
        pltpu.make_async_copy(vector_in, vector_ref, sems.at[0]),
        pltpu.make_async_copy(place_in, place_ref, sems.at[1]),
    ]
    for copy in copies:
        copy.start()
    for grid in grids:
        grid[...] = jnp.zeros_like(grid)
    for copy in copies:
        copy.wait()
    add_panels(reach_y, False, vector_ref, place_ref, line_ref, grids)
    spread_grid(
        reach_x,
        reach_y,
        rounded_ref[...],
        (high_ref, low_ref),
        outs,
        flips,
        wides,
        head,
        total,
        grids,
    )


def spread(vector, table, placed, raw, reach_x, reach_y, flips):
    count = vector.shape[0]
    half = reach_x * reach_y // 2
    blocks = count // BLOCK
    top = up_to(2 + 2 * blocks, 16)
    lanes = 2 * HALF
    body = up_to(half, 16)
    woven = (count // GROUP * 16, BLOCK)
    out_shapes = [jax.ShapeDtypeStruct((top + body, lanes), jnp.int16)] * len(flips)
    out_shapes += [jax.ShapeDtypeStruct((body, 2 * REGION), BF16)] * 2
    rounded = vector.reshape(blocks, BLOCK)
    work = [
        pltpu.VMEM((top, lanes), F32),
        pltpu.VMEM((reach_x * reach_y, REGION), F32),
    ] + [pltpu.VMEM((pair_count(reach_x, reach_y), REGION), F32)] * CHAINS
    if placed is None:
        stencil, flag, sample, dipole = raw
        operands = [vector, rounded, *table, stencil, flag.reshape(1, -1), sample, dipole]
        operands = [pltpu.with_memory_space_constraint(value, pltpu.HBM) for value in operands]
        in_specs = [pl.BlockSpec(memory_space=pltpu.HBM)] * 8
        out_shapes += [jax.ShapeDtypeStruct(woven, F32)]
        out_shapes += [jax.ShapeDtypeStruct((2, count), jnp.int32)]
        out_shapes += [jax.ShapeDtypeStruct(rounded.shape, F32)]
        out_shapes += [jax.ShapeDtypeStruct(values.shape, BF16) for values in table]
        tiled = pltpu.VMEM((blocks, 64, BLOCK), F32)
        work = [
            pltpu.VMEM(stencil.shape, jnp.int32),
            pltpu.VMEM((1, count), jnp.int32),
            tiled,
            tiled,
            pltpu.SMEM((count,), F32),
            pltpu.SMEM((2, count), jnp.int32),
            pltpu.SemaphoreType.DMA((7 + 2 * blocks,)),
        ] + work
    else:
        operands = [vector, placed[0], rounded, *table, placed[1]]
        in_specs = [anywhere()] * 2 + [whole_vmem()] * 4
        work = [
            pltpu.SMEM((count,), F32),
            pltpu.SMEM((2, count), jnp.int32),
            pltpu.SemaphoreType.DMA((2,)),
        ] + work
    return pl.pallas_call(
        functools.partial(
            start_kernel if placed is None else spread_kernel, reach_x, reach_y, flips
        ),
        in_specs=in_specs,
        out_specs=[whole_vmem()] * len(out_shapes),
        out_shape=out_shapes,
        scratch_shapes=work,
        compiler_params=pltpu.CompilerParams(
            vmem_limit_bytes=START_LIMIT if placed is None else VMEM_LIMIT
        ),
        cost_estimate=cost(2 * half * 256 * 512, 4 * 16 * count * REGION),
        name="start" if placed is None else "spread",
    )(*operands)


def spread_rest_kernel(flips, rounded_ref, wide_high, wide_low, high_ref, low_ref, *refs):
    outs, head = refs[:-1], refs[-1]
    both = (wide_high[...], wide_low[...])
    send_pieces(outs, flips, head, rounded_ref[...], both, high_ref, low_ref)


def spread_rest(rounded, both, table, flips):
    blocks = rounded.shape[0]
    top = up_to(2 + 2 * blocks, 16)
    shape = (top + both[0].shape[0], 2 * HALF)
    return pl.pallas_call(
        functools.partial(spread_rest_kernel, flips),
        in_specs=[whole_vmem()] * 5,
        out_specs=[whole_vmem()] * len(flips),
        out_shape=[jax.ShapeDtypeStruct(shape, jnp.int16)] * len(flips),
        scratch_shapes=[pltpu.VMEM((top, 2 * HALF), F32)],
        compiler_params=params(),
        cost_estimate=cost(2 * shape[0] * 256 * 256 * 3, 4 * shape[0] * 512),
        name="spread_rest",
    )(rounded, *both, *table)


def lines_kernel(place_ref, coeff_ref, *refs):
    out_ref = refs[-1]
    lanes = lax.broadcasted_iota(jnp.int32, (8, REGION), 1)

    def body(group, carry):
        at = pl.multiple_of(group * 16, 16)
        coeff = [coeff_ref[pl.ds(at + 8 * q, 8), :] for q in range(2)]
        for local in range(GROUP):
            panel = group * GROUP + local
            depth = place_ref[1, panel]
            shift = (depth - 4 * local) & (REGION - 1)
            inside = in_window(lanes, depth)
            for q in range(2):
                first = pl.multiple_of(panel * 16 + 8 * q, 8)
                out_ref[pl.ds(first, 8), :] = jnp.where(inside, pltpu.roll(coeff[q], shift, 1), 0.0)
        return carry

    lax.fori_loop(0, place_ref.shape[1] // GROUP, body, 0)


def sample_lines_kernel(tiles, place_ref, *refs):
    out_ref, coeff = refs[-2:]
    weave([by_depth(ref) for ref in refs[:tiles]], mixing_matrix(), coeff)
    lines_kernel(place_ref, coeff, out_ref)


def place_sample_lines(places, sample):
    count = places.shape[1]
    blocks = count // BLOCK
    tile = lambda t: pl.BlockSpec((64, BLOCK), lambda i: (0, t))
    shape = (count * 16, REGION)
    return pl.pallas_call(
        functools.partial(sample_lines_kernel, blocks),
        grid=(1,),
        in_specs=[in_smem()] + [tile(t) for t in range(blocks)],
        out_specs=pl.BlockSpec(shape, lambda i: (0, 0)),
        out_shape=jax.ShapeDtypeStruct(shape, F32),
        scratch_shapes=[pltpu.VMEM((count // GROUP * 16, BLOCK), F32)],
        compiler_params=params(),
        cost_estimate=cost(16 * count * REGION, 4 * 16 * count * REGION),
        name="place_sample_lines",
    )(places, *[sample] * blocks)


def place_lines(places, coeff, awaited):
    count = places.shape[1]
    shape = (count * 16, REGION)
    return pl.pallas_call(
        lines_kernel,
        in_specs=[in_smem(), whole_vmem()] + [anywhere()] * len(awaited),
        out_specs=whole_vmem(),
        out_shape=jax.ShapeDtypeStruct(shape, F32),
        compiler_params=params(),
        cost_estimate=cost(16 * count * REGION, 4 * 16 * count * REGION),
        name="place_lines",
    )(places, coeff, *awaited)


def put_edges(opened, reach_x, reach_y, edges, first):
    half = reach_x // 2
    low = low_lanes(reach_y)
    layer = lambda i: opened[i * reach_y : (i + 1) * reach_y, :]
    for two in range(2):
        place = slice(first + two * reach_y, first + (two + 1) * reach_y)
        edges[0, place, :] = jnp.where(low, layer(2 * two), swap(layer(2 * two + 1)))
        last = half - 4 + 2 * two
        edges[1, place, :] = jnp.where(low, swap(layer(last)), layer(last + 1))


def stack_layers(layers, at, reach_y, stacked):
    tall = stacked.shape[0] // len(layers)
    place = at * up_to(reach_y, 8)
    for i, layer in enumerate(layers):
        stacked[pl.ds(pl.multiple_of(i * tall + place, 8), reach_y), :] = layer


def transform_flips(parts, flips, reach_x, reach_y, table_ref, before, spectrum, edges, scratch):
    opened, stacked = scratch
    top = parts[0].shape[0] - opened.shape[0]
    pair = lax.axis_size("pair")
    chip = lax.axis_index("narrow")
    for core in range(pair):
        mine = [(flip, part) for flip, part in zip(flips, parts) if flip % pair == core]
        if not mine:
            continue
        stacked[...] = jnp.zeros_like(stacked)
        for flip, part in mine:
            first = from_short(part[:top, :])
            opened[...] = from_short(part[top:, :]) * unit(first[0:1], first[1:2])
            layers = [opened[i * reach_y : (i + 1) * reach_y, :] for i in range(reach_x // 2)]
            stack_layers(layers, chip ^ (flip // pair), reach_y, stacked)
            put_edges(opened, reach_x, reach_y, edges, flip * 2 * reach_y)
        transform_pieces(table_ref[lax.axis_index("pair") ^ core], stacked, before, spectrum)
        before = spectrum


def transform_pieces(table, stacked, before, spectrum):
    half = spectrum.shape[0]
    tall = stacked.shape[0] // half

    def tripled(values):
        high, low = split(values)
        return jnp.concatenate([high, low, high], axis=0)

    for i in range(0, half, 2):
        places = range(i, min(i + 2, half))
        held = jnp.concatenate([stacked[j * tall : (j + 1) * tall, :] for j in places], axis=1)
        result = dot(table, tripled(held))
        for j in places:
            made = result[:, (j - i) * 2 * HALF : (j - i + 1) * 2 * HALF]
            spectrum[j] = made if before is None else before[j] + made


def forward_early_kernel(reach_x, reach_y, flips, *refs):
    parts = refs[: len(flips)]
    table_ref, spectrum, edges, *scratch = refs[len(flips) :]
    edges[...] = jnp.zeros_like(edges)
    transform_flips(parts, flips, reach_x, reach_y, table_ref, None, spectrum, edges, scratch)


def stacking_scratch(chips, reach_x, reach_y):
    half = reach_x // 2
    return [
        pltpu.VMEM((up_to(half * reach_y, 16), 2 * HALF), F32),
        pltpu.VMEM((half * chips * up_to(reach_y, 8), 2 * HALF), F32),
    ]


def forward_early(parts, flips, pieces, table, reach_x, reach_y):
    half = reach_x // 2
    return pl.pallas_call(
        functools.partial(forward_early_kernel, reach_x, reach_y, flips),
        in_specs=[whole_vmem()] * (len(flips) + 1),
        out_specs=[whole_vmem()] * 2,
        out_shape=[
            jax.ShapeDtypeStruct((half, GRID, 2 * HALF), F32),
            jax.ShapeDtypeStruct((2, pieces * 2 * reach_y, 2 * HALF), F32),
        ],
        scratch_shapes=stacking_scratch(pieces // table.shape[0], reach_x, reach_y),
        compiler_params=params(),
        cost_estimate=cost(EARLY_FLOPS, 4 * half * GRID * 2 * HALF * 2),
        name="forward_early",
    )(*parts, table)


def forward_kernel(reach_x, reach_y, blocks, pieces, late, awaited, *refs):
    parts = refs[:pieces]
    early_ref, early_edges, table_ref, modes_ref = refs[pieces : pieces + 4]
    refs = refs[pieces + 4 + awaited :]
    spectrum, even_out, layers_out, odd_out, own_out, peers_out, inner_out, *refs = refs
    opened, stacked, edges, slabs, head = refs
    half = reach_x // 2
    top = parts[0].shape[0] - opened.shape[0]
    head[...] = jnp.zeros_like(head)
    for piece in range(pieces):
        first = from_short(parts[piece][:top, :])
        mantissa, exponent = first[2 : 2 + blocks], first[2 + blocks : 2 + 2 * blocks]
        peers_out[piece * blocks : (piece + 1) * blocks, :] = decode_rounded(mantissa, exponent)
        at = 6 + 2 * piece * blocks
        head[at : at + blocks, :] = mantissa
        head[at + blocks : at + 2 * blocks, :] = exponent
    edges[...] = early_edges[...]
    held = [parts[flip] for flip in late]
    scratch = (opened, stacked)
    transform_flips(held, late, reach_x, reach_y, table_ref, early_ref, spectrum, edges, scratch)

    chunk = 256

    def body(index, largest):
        rows = pl.ds(pl.multiple_of(index * chunk, chunk), chunk)
        low = low_lanes(chunk)
        decay = modes_ref[0, rows, :]
        log_decay = modes_ref[1, rows, :]
        across_half = jnp.exp(half * log_decay)
        across_cut = jnp.exp((half - 4) * log_decay)
        layers = [spectrum[i, rows, :] for i in range(half)]
        run = layers[0]
        cut_right = run
        for i in range(1, half):
            run = decay * run + layers[i]
            if i == half - 5:
                cut_right = run
        right = run
        run = layers[half - 1]
        cut_left = run
        for i in range(half - 2, -1, -1):
            run = decay * run + layers[i]
            if i == 4:
                cut_left = run
        left = run
        inner_out[rows, :] = jnp.where(low, right, left)
        swapped_right, swapped_left = swap(right), swap(left)
        own = jnp.where(low, left + across_half * swapped_left, right + across_half * swapped_right)
        own_out[rows, :] = own
        made = [
            jnp.where(low, own, cut_right + across_cut * swapped_right),
            jnp.where(low, cut_left + across_cut * swapped_left, own),
        ]
        for slab, values in enumerate(made):
            slabs[slab, rows, :] = values
        return tuple(
            jnp.maximum(old, jnp.max(jnp.abs(values).reshape(chunk // 8, 8, 2 * HALF), axis=0))
            for old, values in zip(largest, made)
        )

    zero = jnp.zeros((8, 2 * HALF), F32)
    largest = lax.fori_loop(0, GRID // chunk, body, (zero,) * 2)
    top = head.shape[0]
    low = low_lanes(GRID // 2)
    upper, lower = own_out[: GRID // 2, :], own_out[GRID // 2 :, :]
    packed = [jnp.where(low, swap(upper), lower), jnp.where(low, upper, swap(lower))]

    def send(out, first, parts):
        place = first
        for index, (values, most) in enumerate(parts):
            exponent, fraction = fit_scale(jnp.max(most, axis=0, keepdims=True))
            head[2 * index : 2 * index + 1, :] = exponent
            head[2 * index + 1 : 2 * index + 2, :] = fraction
            out[place : place + values.shape[0], :] = quantize(values, exponent, fraction)
            place += values.shape[0]
        out[:first, :] = to_short(head[:first, :])

    with_most = lambda values: (values, jnp.abs(values))
    on_left = lax.axis_index("wide") & 1
    for side, (even, odd) in enumerate(((0, 1), (1, 0))):

        @pl.when(on_left == side)
        def _():
            send(even_out, top, [(slabs[even], largest[even]), with_most(packed[even])])
            send(layers_out, 16, [with_most(edges[1 - even])])
            send(odd_out, top, [(slabs[odd], largest[odd]), with_most(edges[1 - odd])])


def forward(parts, late, early, early_edges, table, modes, reach_x, reach_y, blocks, awaited):
    pieces = len(parts)
    half = reach_x // 2
    lanes = 2 * HALF
    head = up_to(6 + 2 * pieces * blocks, 16)
    border = pieces * 2 * reach_y
    short = lambda rows: jax.ShapeDtypeStruct((rows, lanes), jnp.int16)
    return pl.pallas_call(
        functools.partial(
            forward_kernel, reach_x, reach_y, blocks, pieces, late, len(awaited)
        ),
        in_specs=[whole_vmem()] * (pieces + 4) + [anywhere()] * len(awaited),
        out_specs=[whole_vmem()] * 7,
        out_shape=[
            jax.ShapeDtypeStruct((half, GRID, lanes), F32),
            short(head + GRID + GRID // 2),
            short(16 + border),
            short(head + GRID + border),
            jax.ShapeDtypeStruct((GRID, lanes), F32),
            jax.ShapeDtypeStruct((pieces * blocks, BLOCK), F32),
            jax.ShapeDtypeStruct((GRID, lanes), F32),
        ],
        scratch_shapes=stacking_scratch(pieces // table.shape[0], reach_x, reach_y)
        + [
            pltpu.VMEM((2, border, lanes), F32),
            pltpu.VMEM((2, GRID, lanes), F32),
            pltpu.VMEM((head, lanes), F32),
        ],
        compiler_params=params(),
        cost_estimate=cost(2 * half * 256 * 256 * 128, 4 * half * GRID * lanes * 2),
        name="forward",
    )(*parts, early, early_edges, table, modes, *awaited)


def opened_part(ref, index, first, rows):
    head = from_short(ref[:16, :])
    scale = unit(head[2 * index : 2 * index + 1], head[2 * index + 1 : 2 * index + 2])
    return from_short(ref[first : first + rows, :]) * scale


def pair_kernel(reach_x, flips, own_ref, even_ref, modes_ref, *refs):
    outs, head = refs[:-1], refs[-1]
    span = reach_x - 4
    here = lax.axis_index("wide")
    low = low_lanes(GRID)
    log_decay = modes_ref[1]
    own = own_ref[...]
    top = even_ref.shape[0] - GRID - GRID // 2
    cut = opened_part(even_ref, 0, top, GRID)
    packed = opened_part(even_ref, 1, top + GRID, GRID // 2)
    from_left = jnp.where(low, cut, jnp.concatenate([swap(packed), packed], axis=0))
    from_right = jnp.where(low, jnp.concatenate([packed, swap(packed)], axis=0), cut)
    partner = jnp.where((here & 1) == 1, from_left, from_right)

    def weight(distances):
        powers = []
        for distance in distances:
            ahead = span * distance - reach_x
            powers.append(jnp.where(distance >= 2, ahead, ahead + GRID).astype(F32))
        return jnp.exp(jnp.where(low, *powers) * log_decay)

    head[...] = jnp.zeros_like(head)
    for flip, out in zip(flips, outs):
        behind = (here ^ flip) - here
        message = own * weight((-behind, behind))
        behind = (here ^ flip) - (here ^ 1)
        beside = jnp.where(jnp.abs(behind) == 1, 0.0, 1.0)
        send_piece(out, head, message + partner * (weight((-behind, behind)) * beside))


def pair_messages(own, from_even, modes, reach_x, flips):
    return pl.pallas_call(
        functools.partial(pair_kernel, reach_x, flips),
        in_specs=[whole_vmem()] * 3,
        out_specs=[whole_vmem()] * len(flips),
        out_shape=[jax.ShapeDtypeStruct((16 + GRID, 2 * HALF), jnp.int16)] * len(flips),
        scratch_shapes=[pltpu.VMEM((16, 2 * HALF), F32)],
        compiler_params=params(),
        cost_estimate=cost(16 * GRID * 2 * HALF, 4 * GRID * 2 * HALF * (6 + len(flips))),
        name="pair_messages",
    )(own, from_even, modes)


def borders_kernel(reach_y, pieces, layers_ref, odd_ref, table_ref, out_ref, stacked, partial):
    on_left = (lax.axis_index("wide") & 1) == 1
    pair = lax.axis_size("pair")
    rows = pieces * 2 * reach_y
    even = opened_part(layers_ref, 0, 16, rows)
    odd = opened_part(odd_ref, 1, odd_ref.shape[0] - rows, rows)
    left, right = jnp.where(on_left, even, odd), jnp.where(on_left, odd, even)
    low = low_lanes(rows)
    both = [jnp.where(low, left, swap(right)), jnp.where(low, swap(left), right)]
    core = lax.axis_index("pair")
    chip = lax.axis_index("narrow")
    stacked[...] = jnp.zeros_like(stacked)
    before = None
    for other in range(pair):
        for flip in range(pieces // pair):
            first = (flip * pair + other) * 2 * reach_y
            layers = [
                values[first + two * reach_y : first + (two + 1) * reach_y]
                for two in range(2)
                for values in both
            ]
            stack_layers(layers, chip ^ flip, reach_y, stacked)
        target = out_ref if other == pair - 1 else partial
        transform_pieces(table_ref[core ^ other], stacked, before, target)
        before = target


def borders(layers, from_odd, table, reach_y, pieces):
    chips = pieces // table.shape[0]
    shape = (4, GRID, 2 * HALF)
    return pl.pallas_call(
        functools.partial(borders_kernel, reach_y, pieces),
        in_specs=[whole_vmem()] * 3,
        out_specs=whole_vmem(),
        out_shape=jax.ShapeDtypeStruct(shape, F32),
        scratch_shapes=[
            pltpu.VMEM((4 * chips * up_to(reach_y, 8), 2 * HALF), F32),
            pltpu.VMEM(shape, F32),
        ],
        compiler_params=params(),
        cost_estimate=cost(2 * 4 * 256 * 256 * 128, 4 * 6 * GRID * 2 * HALF),
        name="borders",
    )(layers, from_odd, table)


def send_fields(outs, flips, reach_y, field_high, field_low, high_ref, low_ref, ready, head):
    half = field_high.shape[0]
    mine = y_position()
    pitch = up_to(reach_y, 16)
    pick = lambda ref: jnp.concatenate([ref[mine ^ flip] for flip in flips], axis=0)
    table = (pick(high_ref), pick(low_ref))
    for i in range(0, half, 2):
        many = min(2, half - i)
        join = lambda ref: jnp.concatenate([ref[i + j] for j in range(many)], axis=1)
        result = dot_three(table, (join(field_high), join(field_low)))
        for j in range(many):
            for piece in range(len(flips)):
                ready[piece, (i + j) * reach_y : (i + j + 1) * reach_y, :] = result[
                    piece * pitch : piece * pitch + reach_y, j * 2 * HALF : (j + 1) * 2 * HALF
                ]
    head[...] = jnp.zeros_like(head)
    for piece, out in enumerate(outs):
        if ready.shape[1] > half * reach_y:
            ready[piece, half * reach_y :, :] = jnp.zeros_like(ready[piece, half * reach_y :, :])
        send_piece(out, head, ready[piece])


def inverse_kernel(reach_x, reach_y, flips, fars, *refs):
    spectrum, border_ref, from_even, from_odd, own_ref, inner_ref, *far_refs = refs[: 6 + fars]
    refs = refs[6 + fars :]
    high_ref, low_ref, modes_ref = refs[:3]
    outs = refs[3 : 3 + len(flips)]
    field_high, field_low, ready, head = refs[3 + len(flips) :]
    half = reach_x // 2
    span = reach_x - 4
    chunk = 256
    head_rows = from_even.shape[0] - GRID - GRID // 2
    on_left = (lax.axis_index("wide") & 1) == 1
    moment_units = []
    for ref in (from_even, from_odd):
        first = from_short(ref[:16, :])
        moment_units.append(unit(first[0:1], first[1:2]))

    far_units = []
    for ref in far_refs:
        first = from_short(ref[:16, :])
        far_units.append(unit(first[0:1], first[1:2]))

    def body(index, carry):
        first = pl.multiple_of(index * chunk, chunk)
        rows = pl.ds(first, chunk)
        low = low_lanes(chunk)
        decay = modes_ref[0, rows, :]
        log_decay = modes_ref[1, rows, :]
        ring = modes_ref[2, rows, :]
        gain = modes_ref[3, rows, :]
        across_half = jnp.exp(half * log_decay)
        across_cut = jnp.exp((half - 4) * log_decay)
        around = jnp.exp((GRID - 4) * log_decay)
        beside = jnp.exp((GRID - reach_x - span) * log_decay)
        layers = [spectrum[i, rows, :] for i in range(half)]

        at = pl.ds(pl.multiple_of(head_rows + index * chunk, 16), chunk)
        even, odd = (
            from_short(ref[at, :]) * scale for ref, scale in zip((from_even, from_odd), moment_units)
        )
        left_moments, right_moments = jnp.where(on_left, even, odd), jnp.where(on_left, odd, even)
        border = [border_ref[i, rows, :] for i in range(4)]
        zero = jnp.zeros_like(decay)
        head_sum = border[0]
        for i in range(1, 4):
            head_sum = decay * head_sum + border[i]
        tail_sum = border[3]
        for i in range(2, -1, -1):
            tail_sum = decay * tail_sum + border[i]
        for i in range(4):
            layers[i] = layers[i] + jnp.where(low, border[i], zero)
        for i in range(4):
            place = half - 4 + i
            layers[place] = layers[place] + jnp.where(low, zero, border[i])
        total = own_ref[rows, :] * jnp.exp((GRID - reach_x) * log_decay)
        at = pl.ds(pl.multiple_of(16 + index * chunk, 16), chunk)
        for ref, scale in zip(far_refs, far_units):
            total = total + from_short(ref[at, :]) * scale
        one = jnp.ones_like(decay)
        total = total + left_moments * jnp.where(low, beside, one)
        total = total + right_moments * jnp.where(low, one, beside)
        shared = jnp.where(low, head_sum, tail_sum)
        entering = (swap(total) + around * shared) * ring
        leaving = swap(across_half * entering + across_cut * shared + inner_ref[rows, :])
        run = jnp.where(low, entering, leaving)
        forward_runs = []
        for i in range(half):
            run = decay * run + layers[i]
            forward_runs.append(run)
        run = jnp.where(low, leaving, entering)
        for i in range(half - 1, -1, -1):
            ahead = decay * run
            high, rest = split(gain * (forward_runs[i] + ahead))
            field_high[i, rows, :] = high
            field_low[i, rows, :] = rest
            run = ahead + layers[i]
        return carry

    lax.fori_loop(0, GRID // chunk, body, 0)
    send_fields(outs, flips, reach_y, field_high, field_low, high_ref, low_ref, ready, head)


def inverse(
    spectrum, border, from_even, from_odd, own, inner, fars, table, modes, reach_x, reach_y, flips
):
    half = reach_x // 2
    lanes = 2 * HALF
    body = up_to(half * reach_y, 16)
    shapes = [jax.ShapeDtypeStruct((16 + body, lanes), jnp.int16)] * len(flips)
    shapes += [jax.ShapeDtypeStruct((half, GRID, lanes), BF16)] * 2
    return pl.pallas_call(
        functools.partial(inverse_kernel, reach_x, reach_y, flips, len(fars)),
        in_specs=[whole_vmem()] * (9 + len(fars)),
        out_specs=[whole_vmem()] * len(shapes),
        out_shape=shapes,
        scratch_shapes=[
            pltpu.VMEM((len(flips), body, lanes), F32),
            pltpu.VMEM((16, lanes), F32),
        ],
        compiler_params=params(),
        cost_estimate=cost(2 * half * 256 * 256 * 128, 4 * half * GRID * lanes * 2),
        name="inverse",
    )(spectrum, border, from_even, from_odd, own, inner, *fars, *table, modes)


def inverse_rest_kernel(reach_y, flips, field_high, field_low, high_ref, low_ref, *refs):
    outs, (ready, head) = refs[: len(flips)], refs[len(flips) :]
    send_fields(outs, flips, reach_y, field_high, field_low, high_ref, low_ref, ready, head)


def inverse_rest(field, table, reach_y, flips):
    half = field[0].shape[0]
    lanes = 2 * HALF
    body = up_to(half * reach_y, 16)
    return pl.pallas_call(
        functools.partial(inverse_rest_kernel, reach_y, flips),
        in_specs=[whole_vmem()] * 4,
        out_specs=[whole_vmem()] * len(flips),
        out_shape=[jax.ShapeDtypeStruct((16 + body, lanes), jnp.int16)] * len(flips),
        scratch_shapes=[
            pltpu.VMEM((len(flips), body, lanes), F32),
            pltpu.VMEM((16, lanes), F32),
        ],
        compiler_params=params(),
        cost_estimate=cost(2 * half * 256 * 256 * 128, 4 * half * GRID * lanes * 2),
        name="inverse_rest",
    )(*field, *table)


def sum_rows(values):
    row = lax.broadcasted_iota(jnp.int32, values[0].shape, 0)
    for step in (4, 2, 1):
        low = (row & step) == 0
        paired = []
        for one, other in zip(values[: len(values) // 2], values[len(values) // 2 :]):
            kept = jnp.where(low, one, other)
            moved = jnp.where(low, other, one)
            if step == 4:
                moved = pltpu.roll(moved, 4, 0)
            else:
                moved = jnp.where(low, pltpu.roll(moved, 8 - step, 0), pltpu.roll(moved, step, 0))
            paired.append(kept + moved)
        values = paired
    return values[0]


def z_lines(parts, flips, high_ref, low_ref):
    mine = y_position()
    opened = []
    for part in parts:
        first = from_short(part[:16, :])
        opened.append(from_short(part[16:, :]) * unit(first[0:1], first[1:2]))
    values = split(jnp.concatenate(opened, axis=1))
    pick = lambda ref: jnp.concatenate([ref[mine ^ flip] for flip in flips], axis=0)
    return dot_three(values, (pick(high_ref), pick(low_ref)))


def sample_early_kernel(flips, *refs):
    *parts, high_ref, low_ref, out_ref = refs
    out_ref[...] = z_lines(parts, flips, high_ref, low_ref)


def sample_early(parts, flips, table):
    rows = parts[0].shape[0] - 16
    return pl.pallas_call(
        functools.partial(sample_early_kernel, flips),
        in_specs=[whole_vmem()] * (len(parts) + 2),
        out_specs=whole_vmem(),
        out_shape=jax.ShapeDtypeStruct((rows, 2 * REGION), F32),
        compiler_params=params(),
        cost_estimate=cost(EARLY_FLOPS, 4 * rows * 512),
        name="sample_early",
    )(*parts, *table)


def sample_kernel(last, reach_x, reach_y, flips, place_in, *refs):
    parts = refs[: len(flips)]
    early_ref, high_ref, low_ref, line_ref, own_ref, vector_ref, near_ref, out_ref = refs[
        len(flips) : len(flips) + 8
    ]
    flat, field, sums, place_ref, sem = refs[len(flips) + 8 :]
    copy = pltpu.make_async_copy(place_in, place_ref, sem)
    copy.start()
    half_rows = reach_x * reach_y // 2
    both = early_ref[...] + z_lines(parts, flips, high_ref, low_ref)
    flat[:half_rows, :] = both[:half_rows, :REGION]
    flat[half_rows:, :] = both[:half_rows, REGION:]
    for x in range(reach_x):
        layer = flat[x * reach_y : (x + 1) * reach_y, :]
        for row in pair_rows(x, reach_x, reach_y):
            field[pl.ds(row, reach_y, stride=2), :] = layer
    count = place_ref.shape[1]

    def body(group, carry):
        for eight in range(0, GROUP, 8):
            totals = []
            for local in range(eight, eight + 8):
                panel = group * GROUP + local
                row = place_ref[0, panel]
                first = pl.multiple_of(panel * 16, 16)
                totals.append(
                    field[pl.ds(row, 8), :] * line_ref[pl.ds(first, 8), :]
                    + field[pl.ds(row + 2 * reach_y, 8), :] * line_ref[pl.ds(first + 8, 8), :]
                )
            sums[pl.ds(pl.multiple_of(group * GROUP + eight, 8), 8), :] = sum_rows(totals)
        return carry

    copy.wait()
    lax.fori_loop(0, count // GROUP, body, 0)
    first, rest = split(sums[...])
    second, third = split(sums[...] - first.astype(F32))
    across = lambda values: lax.dot_general(
        jnp.ones((16, REGION), BF16),
        values,
        (((1,), (1,)), ((), ())),
        preferred_element_type=F32,
    )
    sampled = across(first) + (across(second) + across(third))
    for block in range(count // BLOCK):
        lane = slice(block * BLOCK, (block + 1) * BLOCK)
        row = slice(block, block + 1)
        vector = vector_ref[row, :]
        image = jnp.where(own_ref[row, :] == 1, 0.0, 0.5 * vector) + sampled[:1, lane]
        image = image + near_ref[row, :]
        if last:
            out_ref[0:1, lane] = vector
            out_ref[1:2, lane] = image
        else:
            out_ref[row, :] = image


def sample(last, places, parts, flips, early, table, lines, flag, vector, near, reach_x, reach_y):
    count = places.shape[1]
    blocks = count // BLOCK
    shape = (2, count) if last else (blocks, BLOCK)
    return pl.pallas_call(
        functools.partial(sample_kernel, last, reach_x, reach_y, flips),
        in_specs=[anywhere()] + [whole_vmem()] * (len(parts) + 7),
        out_specs=whole_vmem(),
        out_shape=jax.ShapeDtypeStruct(shape, F32),
        scratch_shapes=[
            pltpu.VMEM((reach_x * reach_y, REGION), F32),
            pltpu.VMEM((pair_count(reach_x, reach_y), REGION), F32),
            pltpu.VMEM((count, REGION), F32),
            pltpu.SMEM((2, count), jnp.int32),
            pltpu.SemaphoreType.DMA,
        ],
        compiler_params=params(),
        cost_estimate=cost(reach_x * reach_y * 256 * 512, 4 * 16 * count * REGION),
        name="sample",
    )(
        places,
        *parts,
        early,
        *table,
        lines,
        flag.reshape(blocks, BLOCK),
        vector.reshape(blocks, BLOCK),
        near,
    )


def near_kernel(slots, blocks, place_ref, target_ref, *refs):
    even_ref, odd_ref, peers_ref, tile_ref = refs[:4]
    out_ref, held = refs[-2:]
    count = peers_ref.shape[0]
    held[count : 2 * count, :] = peers_ref[...]
    on_left = lax.axis_index("wide") & 1
    for side, ref in ((1 - on_left, even_ref), (on_left, odd_ref)):
        top = from_short(ref[...])
        for piece in range(count // blocks):
            at = 6 + 2 * piece * blocks
            held[pl.ds(side * (2 * count) + piece * blocks, blocks), :] = decode_rounded(
                top[at : at + blocks], top[at + blocks : at + 2 * blocks]
            )
    out_ref[...] = jnp.zeros_like(out_ref)
    for slot in range(slots):
        picked = held[pl.ds(place_ref[slot], 1), :]
        picked = jnp.broadcast_to(picked, (16, BLOCK)).astype(BF16)
        product = lax.dot_general(
            picked,
            tile_ref[slot],
            (((1,), (1,)), ((), ())),
            preferred_element_type=F32,
        )
        target = pl.ds(target_ref[slot], 1)
        out_ref[target, :] = out_ref[target, :] + product[:1]


def near_field(places, targets, from_even, from_odd, peers, tiles, blocks, out_rows, awaited):
    slots = tiles.shape[0]
    head = up_to(6 + 2 * peers.shape[0], 16)
    constant = lambda shape: pl.BlockSpec(shape, lambda i: (0,) * len(shape))
    return pl.pallas_call(
        functools.partial(near_kernel, slots, blocks),
        grid=(1,),
        in_specs=[
            in_smem(),
            in_smem(),
            constant((head, BLOCK)),
            constant((head, BLOCK)),
            constant(peers.shape),
            constant(tiles.shape),
        ]
        + [anywhere()] * len(awaited),
        out_specs=constant((out_rows, BLOCK)),
        out_shape=jax.ShapeDtypeStruct((out_rows, BLOCK), F32),
        scratch_shapes=[pltpu.VMEM((3 * peers.shape[0], BLOCK), F32)],
        compiler_params=params(),
        cost_estimate=cost(2 * slots * 16 * BLOCK * BLOCK, 2 * slots * BLOCK * BLOCK),
        name="near_field",
    )(places, targets, from_even, from_odd, peers, tiles, *awaited)


def shards(
    density,
    surface_flag,
    stencil_base,
    sample_weights,
    dipole_weights,
    near_target,
    near_source,
    near_tiles,
):
    x_count = lax.axis_size("wide")
    y_count = lax.axis_size(Y_AXES)
    y_index = lax.axis_index(Y_AXES)
    pair = lax.axis_size("pair")
    span_x = REGION // x_count
    span_y = REGION // y_count
    reach_x = span_x + 4
    reach_y = span_y + 4
    count = density.shape[0]
    blocks = count // BLOCK

    z_forward, z_inverse, y_forward, y_inverse, modes = tables(y_count, pair, span_y)
    modes = lax.dynamic_index_in_dim(jnp.asarray(modes), y_index, 0, keepdims=False)

    neighbour = near_source // blocks
    flip = (y_index + neighbour % 3 - 1) ^ y_index
    sources = ((neighbour // 3) * y_count + flip) * blocks + near_source % blocks
    out_rows = up_to(blocks + 1, 8)
    live = near_target >= 0
    sources = jnp.where(live, sources, 0)
    targets = jnp.where(live, near_target, out_rows - 1)

    swaps = lambda pairs: [(i, j) for i, j in pairs] + [(j, i) for i, j in pairs]
    even_swap = swaps([(i, i + 1) for i in range(0, x_count - 1, 2)])
    odd_swap = swaps([(i, i + 1) for i in range(1, x_count - 1, 2)])
    far_flips = list(range(2, x_count, 2))

    first, rest = list(range(1, y_count)), [0]
    early_flips, late_flips = list(range(y_count - 1)), [y_count - 1]

    def turned(sent, then):
        arrived = [None] * y_count
        for flip, part in zip(first + rest, list(sent) + list(then)):
            swap_pairs = [(i, i ^ flip) for i in range(y_count)]
            arrived[flip] = part if flip == 0 else lax.ppermute(part, Y_AXES, swap_pairs)
        return arrived

    def chosen(parts, flips):
        return [parts[flip] for flip in flips]

    def convolve_and_sample(last, vector, sent, both, table, places, sample_lines, awaited):
        arrived = turned(sent, spread_rest(vector, both, table, rest))
        early, edges = forward_early(
            chosen(arrived, early_flips), early_flips, y_count, y_forward, reach_x, reach_y
        )
        spectrum, even_message, layers, odd_message, own, peers, inner = forward(
            arrived,
            late_flips,
            early,
            edges,
            y_forward,
            modes,
            reach_x,
            reach_y,
            blocks,
            awaited,
        )
        from_even = lax.ppermute(even_message, "wide", even_swap)
        from_odd = lax.ppermute(odd_message, "wide", odd_swap)
        even_layers = lax.ppermute(layers, "wide", even_swap)
        fars = [
            lax.ppermute(message, "wide", [(i, i ^ flip) for i in range(x_count)])
            for flip, message in zip(
                far_flips, pair_messages(own, from_even, modes, reach_x, far_flips)
            )
        ]
        *sent, high, low = inverse(
            spectrum,
            borders(even_layers, from_odd, y_forward, reach_y, y_count),
            from_even,
            from_odd,
            own,
            inner,
            fars,
            y_inverse,
            modes,
            reach_x,
            reach_y,
            first,
        )
        then = inverse_rest((high, low), y_inverse, reach_y, rest)
        near_part = near_field(
            sources, targets, from_even, from_odd, peers, near_tiles, blocks, out_rows, then[:1]
        )
        arrived = turned(sent, then)
        image = sample(
            last,
            places,
            chosen(arrived, late_flips),
            late_flips,
            sample_early(chosen(arrived, early_flips), early_flips, z_inverse),
            z_inverse,
            sample_lines,
            surface_flag,
            vector,
            near_part,
            reach_x,
            reach_y,
        )
        return image, near_part

    raw = (stencil_base, surface_flag, sample_weights, dipole_weights)
    *sent, wide_high, wide_low, source_coeff, places, vector, high, low = spread(
        density, z_forward, None, raw, reach_x, reach_y, first
    )
    z_forward = (high, low)
    sample_lines = place_sample_lines(places, sample_weights)
    vector, near_part = convolve_and_sample(
        False,
        vector,
        sent,
        (wide_high, wide_low),
        z_forward,
        places,
        sample_lines,
        [sample_lines],
    )
    source_lines = place_lines(places, source_coeff, [near_part])
    *sent, wide_high, wide_low = spread(
        vector.reshape(-1), z_forward, (places, source_lines), None, reach_x, reach_y, first
    )
    both_images, _ = convolve_and_sample(
        True, vector, sent, (wide_high, wide_low), z_forward, places, sample_lines, []
    )
    return both_images


def solution(mesh):
    panels = P(("groups",) + ALL_AXES)
    columns = P(None, ("groups",) + ALL_AXES)
    in_specs = (
        panels,
        panels,
        columns,
        columns,
        columns,
        panels,
        panels,
        P(("groups",) + ALL_AXES, None, None),
    )
    return jax.shard_map(
        shards, mesh=mesh, in_specs=in_specs, out_specs=columns, check_vma=False
    )
```

```python
import functools
import math

import jax
import jax.numpy as jnp
import numpy as np
from jax import lax
from jax.experimental import pallas as pl
from jax.experimental.pallas import tpu as pltpu
from jax.sharding import PartitionSpec as P

GRID = 256
REGION = 128
BLOCK = 128
HALF = 64
KERNEL_GAIN = 4.0
SCREEN = 1.0 / 1024.0
LN2 = math.log(2.0)
Y_AXES = ("narrow", "pair")
ALL_AXES = ("wide", "narrow", "pair")
F32 = jnp.float32
BF16 = jnp.bfloat16
VMEM_LIMIT = 24 * 1024 * 1024
START_LIMIT = VMEM_LIMIT
EARLY_FLOPS = 5 * 10**9
GROUP = 32
CHAINS = 2


def cas(angles):
    return np.cos(angles) + np.sin(angles)


def up_to(count, multiple):
    return -(-count // multiple) * multiple


def low_lanes(rows):
    return lax.broadcasted_iota(jnp.int32, (rows, 2 * HALF), 1) < HALF


def swap(values):
    return pltpu.roll(values, HALF, 1)


def split(values):
    high = values.astype(BF16)
    return high, (values - high.astype(F32)).astype(BF16)


def dot(left, right):
    return jnp.dot(left, right, preferred_element_type=F32)


def dot_three(left, right):
    return dot(left[0], right[0]) + (dot(left[0], right[1]) + dot(left[1], right[0]))


def params():
    return pltpu.CompilerParams(vmem_limit_bytes=VMEM_LIMIT)


def whole_vmem():
    return pl.BlockSpec(memory_space=pltpu.VMEM)


def anywhere():
    return pl.BlockSpec(memory_space=pl.ANY)


def in_smem():
    return pl.BlockSpec(memory_space=pltpu.SMEM)


def cost(flops, moved):
    return pl.CostEstimate(flops=flops, bytes_accessed=moved, transcendentals=0)


def full_scale(exponent, fraction):
    return fraction * jnp.exp(exponent * LN2) * (1.0 / 1024.0)


def fit_scale(largest):
    largest = jnp.maximum(largest, 1e-30)
    exponent = jnp.floor(jnp.log(largest) * (1.0 / LN2))
    fraction = jnp.ceil(largest * jnp.exp(-exponent * LN2) * 1024.0) + 1.0
    return exponent, fraction


def to_short(values):
    return values.astype(jnp.int32).astype(jnp.int16)


def from_short(values):
    return values.astype(jnp.int32).astype(F32)


def quantize(values, exponent, fraction):
    return to_short(jnp.round(values * (32767.0 / full_scale(exponent, fraction))))


def unit(exponent, fraction):
    return full_scale(exponent, fraction) * (1.0 / 32767.0)


def encode_rounded(values):
    rounded = values.astype(BF16).astype(F32)
    size = jnp.maximum(jnp.abs(rounded), 1e-30)
    exponent = jnp.floor(jnp.log(size) * (1.0 / LN2))
    return jnp.round(rounded * jnp.exp((10.0 - exponent) * LN2)), exponent


def decode_rounded(mantissa, exponent):
    return (mantissa * jnp.exp((exponent - 10.0) * LN2)).astype(BF16).astype(F32)


def send_piece(out, head, values):
    exponent, fraction = fit_scale(jnp.max(jnp.abs(values), axis=0, keepdims=True))
    head[0:1, :] = exponent
    head[1:2, :] = fraction
    top = head.shape[0]
    out[:top, :] = to_short(head[...])
    out[top:, :] = quantize(values, exponent, fraction)


def y_position():
    return lax.axis_index("narrow") * lax.axis_size("pair") + lax.axis_index("pair")


def halves(table):
    high = table.astype(jnp.bfloat16)
    return high, (table - high.astype(np.float64)).astype(jnp.bfloat16)


def tables(y_count, pair, span_y):
    depth = GRID // y_count
    reach = span_y + 4
    waves = np.arange(GRID)
    step = 2.0 * np.pi / GRID
    z_table = cas(step * np.outer(np.arange(REGION), waves))
    z_forward = np.zeros((y_count, 2 * REGION, 2 * HALF))
    z_inverse = np.zeros((y_count, 2 * HALF, 2 * REGION))
    symbols = 4.0 * np.sin(np.pi * waves / GRID) ** 2
    shift = np.full((y_count, GRID, 2 * HALF), 1.0)
    y_forward = np.zeros((GRID, y_count, up_to(reach, 8)))
    y_inverse = np.zeros((y_count, up_to(reach, 16), GRID))
    for block in range(y_count):
        mine = z_table[:, block * depth : (block + 1) * depth]
        for half in range(2):
            rows = slice(half * REGION, (half + 1) * REGION)
            lanes = slice(half * HALF, half * HALF + depth)
            z_forward[block, rows, lanes] = mine
            z_inverse[block, lanes, rows] = mine.T / GRID
            shift[block, :, lanes] = (
                SCREEN + symbols[:, None] + symbols[None, block * depth : (block + 1) * depth]
            )
        cells = block * span_y - 2 + np.arange(reach)
        y_table = cas(step * np.outer(waves, cells))
        y_forward[:, block, :reach] = y_table
        y_inverse[block, :reach] = y_table.T / GRID
    y_forward = y_forward.reshape(GRID, y_count // pair, pair, -1).transpose(2, 0, 1, 3)
    y_forward = halves(y_forward.reshape(pair, GRID, -1))
    y_forward = np.concatenate([y_forward[0], y_forward[0], y_forward[1]], axis=2)
    root = np.sqrt(shift * (shift + 4.0))
    decay = 2.0 / (2.0 + shift + root)
    log_decay = np.log(decay)
    ring = 1.0 / (1.0 - np.exp(GRID * log_decay))
    gain = KERNEL_GAIN / root
    modes = np.stack([decay, log_decay, ring, gain], axis=1).astype(np.float32)
    return (
        halves(z_forward),
        halves(z_inverse),
        y_forward,
        halves(y_inverse),
        modes,
    )


def mixing_matrix():
    place = lax.broadcasted_iota(jnp.int32, (4 * BLOCK, 4 * BLOCK), 0)
    lane = lax.broadcasted_iota(jnp.int32, (4 * BLOCK, 4 * BLOCK), 1)
    return jnp.where(lane == 4 * (place % BLOCK) + place // BLOCK, 1.0, 0.0).astype(BF16)


def weave(tiles, mixing, out):
    weights = jnp.concatenate([jnp.concatenate(tile, axis=1) for tile in tiles], axis=0)
    first, rest = split(weights)
    second, third = split(weights - first.astype(F32))
    woven = dot(first, mixing) + (dot(second, mixing) + dot(third, mixing))
    for tile in range(len(tiles)):
        for part in range(BLOCK // GROUP):
            at = (tile * (BLOCK // GROUP) + part) * 16
            lanes = slice(part * BLOCK, (part + 1) * BLOCK)
            for a in range(4):
                row = tile * 16 + 4 * a
                out[pl.ds(at + 8 * (a // 2) + a % 2, 4, stride=2), :] = woven[row : row + 4, lanes]


def by_depth(ref):
    return [ref[pl.ds(depth, 16, stride=4), :] for depth in range(4)]


def pair_rows(x, reach_x, reach_y):
    even = (x // 2) * 2 * reach_y + x % 2
    if x == 0 or x == reach_x - 1:
        return [even]
    return [even, reach_x * reach_y + ((x - 1) // 2) * 2 * reach_y + (x - 1) % 2]


def pair_count(reach_x, reach_y):
    return (2 * reach_x - 2) * reach_y


def in_window(lanes, depth):
    return ((lanes - depth) & -4) == 0


def add_panels(reach, woven, vector_ref, place_ref, weight_ref, grids):
    lanes = lax.broadcasted_iota(jnp.int32, (8, REGION), 1)

    def body(group, carry):
        at = pl.multiple_of(group * 16, 16)
        coeff = [weight_ref[pl.ds(at + 8 * q, 8), :] for q in range(2)] if woven else None
        for local in range(GROUP):
            panel = group * GROUP + local
            grid = grids[local % len(grids)]
            row = place_ref[0, panel]
            value = vector_ref[panel]
            if woven:
                depth = place_ref[1, panel]
                shift = (depth - 4 * local) & (REGION - 1)
                value = jnp.where(in_window(lanes, depth), value, 0.0)
                lines = [pltpu.roll(coeff[q], shift, 1) for q in range(2)]
            else:
                first = pl.multiple_of(panel * 16, 16)
                lines = [weight_ref[pl.ds(first + 8 * q, 8), :] for q in range(2)]
            places = [pl.ds(row, 8), pl.ds(row + 2 * reach, 8)]
            held = [grid[place, :] for place in places]
            for q in range(2):
                grid[places[q], :] = held[q] + lines[q] * value
        return carry

    lax.fori_loop(0, vector_ref.shape[0] // GROUP, body, 0)


def send_pieces(outs, flips, head, rounded, both, high_ref, low_ref):
    blocks = rounded.shape[0]
    mantissa, exponent = encode_rounded(rounded)
    head[...] = jnp.zeros_like(head)
    head[2 : 2 + blocks, :] = mantissa
    head[2 + blocks : 2 + 2 * blocks, :] = exponent
    mine = y_position()
    for at in range(0, len(flips), 2):
        pick = lambda ref: jnp.concatenate([ref[mine ^ flip] for flip in flips[at : at + 2]], axis=1)
        result = dot_three(both, (pick(high_ref), pick(low_ref)))
        for i, out in enumerate(outs[at : at + 2]):
            send_piece(out, head, result[:, i * 2 * HALF : (i + 1) * 2 * HALF])


def spread_grid(reach_x, reach_y, rounded, tables, outs, flips, wides, head, total, grids):
    for x in range(reach_x):
        parts = [
            grid[pl.ds(row, reach_y, stride=2), :]
            for row in pair_rows(x, reach_x, reach_y)
            for grid in grids
        ]
        total[x * reach_y : (x + 1) * reach_y, :] = sum(parts[1:], parts[0])
    half = reach_x * reach_y // 2
    both = jnp.concatenate([total[:half, :], total[half:, :]], axis=1)
    extra = wides[0].shape[0] - half
    if extra:
        both = jnp.concatenate([both, jnp.zeros((extra, 2 * REGION), F32)], axis=0)
    both = split(both)
    for wide, values in zip(wides, both):
        wide[...] = values
    send_pieces(outs, flips, head, rounded, both, *tables)


def start_kernel(reach_x, reach_y, flips, *refs):
    vector_in, *remote = refs[:8]
    refs = refs[8:]
    outs, refs = refs[: len(flips)], refs[len(flips) :]
    wides, (weight_ref, places_out), refs = refs[:2], refs[2:4], refs[4:]
    rounded, high, low, stencil, flag, samples, dipoles, vector_ref = refs[:8]
    place_ref, sems, head, total = refs[8:12]
    grids = refs[12:]
    tiles = samples.shape[0]
    copies = []
    fetch = lambda source, target: copies.append(
        pltpu.make_async_copy(source, target, sems.at[len(copies)])
    )
    rounded_in, high_in, low_in, stencil_in, flag_in, sample_in, dipole_in = remote
    fetch(stencil_in, stencil)
    fetch(flag_in, flag)
    fetch(vector_in, vector_ref)
    for tile in range(tiles):
        lanes = pl.ds(tile * BLOCK, BLOCK)
        fetch(sample_in.at[:, lanes], samples.at[tile])
        fetch(dipole_in.at[:, lanes], dipoles.at[tile])
    needed_first = len(copies)
    fetch(rounded_in, rounded)
    fetch(high_in, high)
    fetch(low_in, low)
    for copy in copies:
        copy.start()
    for grid in grids:
        grid[...] = jnp.zeros_like(grid)
    mixing = mixing_matrix()
    copies[0].wait()
    span_x, span_y = reach_x - 4, reach_y - 4
    local_x = stencil[0:1, :] - (lax.axis_index("wide") * span_x - 2)
    local_y = stencil[1:2, :] - (y_position() * span_y - 2)
    odd = local_x & 1
    places_out[0:1, :] = odd * (reach_x * reach_y) + (local_x >> 1) * (2 * reach_y) + 2 * local_y
    places_out[1:2, :] = stencil[2:3, :]
    to_scalar = pltpu.make_async_copy(places_out, place_ref, sems.at[len(copies)])
    to_scalar.start()
    for copy in copies[1:needed_first]:
        copy.wait()
    sources = []
    for tile in range(tiles):
        charged = flag[:, tile * BLOCK : (tile + 1) * BLOCK] == 1
        pairs = zip(by_depth(samples.at[tile]), by_depth(dipoles.at[tile]))
        sources.append([jnp.where(charged, -sample, dipole) for sample, dipole in pairs])
    weave(sources, mixing, weight_ref)
    to_scalar.wait()
    add_panels(reach_y, True, vector_ref, place_ref, weight_ref, grids)
    for copy in copies[needed_first:]:
        copy.wait()
    spread_grid(
        reach_x, reach_y, rounded[...], (high, low), outs, flips, wides, head, total, grids
    )


def spread_kernel(reach_x, reach_y, flips, *refs):
    vector_in, place_in, rounded_ref, high_ref, low_ref, line_ref = refs[:6]
    refs = refs[6:]
    outs, wides, (vector_ref, place_ref, sems, head, total), grids = (
        refs[: len(flips)],
        refs[len(flips) : len(flips) + 2],
        refs[len(flips) + 2 : len(flips) + 7],
        refs[len(flips) + 7 :],
    )
    copies = [
        pltpu.make_async_copy(vector_in, vector_ref, sems.at[0]),
        pltpu.make_async_copy(place_in, place_ref, sems.at[1]),
    ]
    for copy in copies:
        copy.start()
    for grid in grids:
        grid[...] = jnp.zeros_like(grid)
    for copy in copies:
        copy.wait()
    add_panels(reach_y, False, vector_ref, place_ref, line_ref, grids)
    spread_grid(
        reach_x,
        reach_y,
        rounded_ref[...],
        (high_ref, low_ref),
        outs,
        flips,
        wides,
        head,
        total,
        grids,
    )


def spread(vector, table, placed, raw, reach_x, reach_y, flips):
    count = vector.shape[0]
    half = reach_x * reach_y // 2
    blocks = count // BLOCK
    top = up_to(2 + 2 * blocks, 16)
    lanes = 2 * HALF
    body = up_to(half, 16)
    woven = (count // GROUP * 16, BLOCK)
    out_shapes = [jax.ShapeDtypeStruct((top + body, lanes), jnp.int16)] * len(flips)
    out_shapes += [jax.ShapeDtypeStruct((body, 2 * REGION), BF16)] * 2
    rounded = vector.reshape(blocks, BLOCK)
    work = [
        pltpu.VMEM((top, lanes), F32),
        pltpu.VMEM((reach_x * reach_y, REGION), F32),
    ] + [pltpu.VMEM((pair_count(reach_x, reach_y), REGION), F32)] * CHAINS
    if placed is None:
        stencil, flag, sample, dipole = raw
        operands = [vector, rounded, *table, stencil, flag.reshape(1, -1), sample, dipole]
        operands = [pltpu.with_memory_space_constraint(value, pltpu.HBM) for value in operands]
        in_specs = [pl.BlockSpec(memory_space=pltpu.HBM)] * 8
        out_shapes += [jax.ShapeDtypeStruct(woven, F32)]
        out_shapes += [jax.ShapeDtypeStruct((2, count), jnp.int32)]
        out_shapes += [jax.ShapeDtypeStruct(rounded.shape, F32)]
        out_shapes += [jax.ShapeDtypeStruct(values.shape, BF16) for values in table]
        tiled = pltpu.VMEM((blocks, 64, BLOCK), F32)
        work = [
            pltpu.VMEM(stencil.shape, jnp.int32),
            pltpu.VMEM((1, count), jnp.int32),
            tiled,
            tiled,
            pltpu.SMEM((count,), F32),
            pltpu.SMEM((2, count), jnp.int32),
            pltpu.SemaphoreType.DMA((7 + 2 * blocks,)),
        ] + work
    else:
        operands = [vector, placed[0], rounded, *table, placed[1]]
        in_specs = [anywhere()] * 2 + [whole_vmem()] * 4
        work = [
            pltpu.SMEM((count,), F32),
            pltpu.SMEM((2, count), jnp.int32),
            pltpu.SemaphoreType.DMA((2,)),
        ] + work
    return pl.pallas_call(
        functools.partial(
            start_kernel if placed is None else spread_kernel, reach_x, reach_y, flips
        ),
        in_specs=in_specs,
        out_specs=[whole_vmem()] * len(out_shapes),
        out_shape=out_shapes,
        scratch_shapes=work,
        compiler_params=pltpu.CompilerParams(
            vmem_limit_bytes=START_LIMIT if placed is None else VMEM_LIMIT
        ),
        cost_estimate=cost(2 * half * 256 * 512, 4 * 16 * count * REGION),
        name="start" if placed is None else "spread",
    )(*operands)


def spread_rest_kernel(flips, rounded_ref, wide_high, wide_low, high_ref, low_ref, *refs):
    outs, head = refs[:-1], refs[-1]
    both = (wide_high[...], wide_low[...])
    send_pieces(outs, flips, head, rounded_ref[...], both, high_ref, low_ref)


def spread_rest(rounded, both, table, flips):
    blocks = rounded.shape[0]
    top = up_to(2 + 2 * blocks, 16)
    shape = (top + both[0].shape[0], 2 * HALF)
    return pl.pallas_call(
        functools.partial(spread_rest_kernel, flips),
        in_specs=[whole_vmem()] * 5,
        out_specs=[whole_vmem()] * len(flips),
        out_shape=[jax.ShapeDtypeStruct(shape, jnp.int16)] * len(flips),
        scratch_shapes=[pltpu.VMEM((top, 2 * HALF), F32)],
        compiler_params=params(),
        cost_estimate=cost(2 * shape[0] * 256 * 256 * 3, 4 * shape[0] * 512),
        name="spread_rest",
    )(rounded, *both, *table)


def lines_kernel(place_ref, coeff_ref, *refs):
    out_ref = refs[-1]
    lanes = lax.broadcasted_iota(jnp.int32, (8, REGION), 1)

    def body(group, carry):
        at = pl.multiple_of(group * 16, 16)
        coeff = [coeff_ref[pl.ds(at + 8 * q, 8), :] for q in range(2)]
        for local in range(GROUP):
            panel = group * GROUP + local
            depth = place_ref[1, panel]
            shift = (depth - 4 * local) & (REGION - 1)
            inside = in_window(lanes, depth)
            for q in range(2):
                first = pl.multiple_of(panel * 16 + 8 * q, 8)
                out_ref[pl.ds(first, 8), :] = jnp.where(inside, pltpu.roll(coeff[q], shift, 1), 0.0)
        return carry

    lax.fori_loop(0, place_ref.shape[1] // GROUP, body, 0)


def sample_lines_kernel(tiles, place_ref, *refs):
    out_ref, coeff = refs[-2:]
    weave([by_depth(ref) for ref in refs[:tiles]], mixing_matrix(), coeff)
    lines_kernel(place_ref, coeff, out_ref)


def place_sample_lines(places, sample):
    count = places.shape[1]
    blocks = count // BLOCK
    tile = lambda t: pl.BlockSpec((64, BLOCK), lambda i: (0, t))
    shape = (count * 16, REGION)
    return pl.pallas_call(
        functools.partial(sample_lines_kernel, blocks),
        grid=(1,),
        in_specs=[in_smem()] + [tile(t) for t in range(blocks)],
        out_specs=pl.BlockSpec(shape, lambda i: (0, 0)),
        out_shape=jax.ShapeDtypeStruct(shape, F32),
        scratch_shapes=[pltpu.VMEM((count // GROUP * 16, BLOCK), F32)],
        compiler_params=params(),
        cost_estimate=cost(16 * count * REGION, 4 * 16 * count * REGION),
        name="place_sample_lines",
    )(places, *[sample] * blocks)


def place_lines(places, coeff, awaited):
    count = places.shape[1]
    shape = (count * 16, REGION)
    return pl.pallas_call(
        lines_kernel,
        in_specs=[in_smem(), whole_vmem()] + [anywhere()] * len(awaited),
        out_specs=whole_vmem(),
        out_shape=jax.ShapeDtypeStruct(shape, F32),
        compiler_params=params(),
        cost_estimate=cost(16 * count * REGION, 4 * 16 * count * REGION),
        name="place_lines",
    )(places, coeff, *awaited)


def put_edges(opened, reach_x, reach_y, edges, first):
    half = reach_x // 2
    low = low_lanes(reach_y)
    layer = lambda i: opened[i * reach_y : (i + 1) * reach_y, :]
    for two in range(2):
        place = slice(first + two * reach_y, first + (two + 1) * reach_y)
        edges[0, place, :] = jnp.where(low, layer(2 * two), swap(layer(2 * two + 1)))
        last = half - 4 + 2 * two
        edges[1, place, :] = jnp.where(low, swap(layer(last)), layer(last + 1))


def stack_layers(layers, at, reach_y, stacked):
    tall = stacked.shape[0] // len(layers)
    place = at * up_to(reach_y, 8)
    for i, layer in enumerate(layers):
        stacked[pl.ds(pl.multiple_of(i * tall + place, 8), reach_y), :] = layer


def stack_pieces(parts, reach_x, reach_y, top, opened, stacked, edges, places):
    chip = lax.axis_index("narrow")
    for flip, (part, place) in enumerate(zip(parts, places)):
        first = from_short(part[:top, :])
        opened[...] = from_short(part[top:, :]) * unit(first[0:1], first[1:2])
        layers = [opened[i * reach_y : (i + 1) * reach_y, :] for i in range(reach_x // 2)]
        stack_layers(layers, chip ^ flip, reach_y, stacked)
        put_edges(opened, reach_x, reach_y, edges, place * 2 * reach_y)


def transform_pieces(table, stacked, before, spectrum):
    half = spectrum.shape[0]
    tall = stacked.shape[0] // half

    def tripled(values):
        high, low = split(values)
        return jnp.concatenate([high, low, high], axis=0)

    for i in range(0, half, 2):
        places = range(i, min(i + 2, half))
        held = jnp.concatenate([stacked[j * tall : (j + 1) * tall, :] for j in places], axis=1)
        result = dot(table, tripled(held))
        for j in places:
            made = result[:, (j - i) * 2 * HALF : (j - i + 1) * 2 * HALF]
            spectrum[j] = made if before is None else before[j] + made


def forward_early_kernel(reach_x, reach_y, chips, *refs):
    parts = refs[:chips]
    table_ref, spectrum, edges, opened, stacked = refs[chips:]
    top = parts[0].shape[0] - opened.shape[0]
    stacked[...] = jnp.zeros_like(stacked)
    stack_pieces(parts, reach_x, reach_y, top, opened, stacked, edges, range(chips))
    transform_pieces(table_ref[lax.axis_index("pair")], stacked, None, spectrum)


def stacking_scratch(chips, reach_x, reach_y):
    half = reach_x // 2
    return [
        pltpu.VMEM((up_to(half * reach_y, 16), 2 * HALF), F32),
        pltpu.VMEM((half * chips * up_to(reach_y, 8), 2 * HALF), F32),
    ]


def forward_early(parts, table, reach_x, reach_y):
    half = reach_x // 2
    chips = len(parts)
    return pl.pallas_call(
        functools.partial(forward_early_kernel, reach_x, reach_y, chips),
        in_specs=[whole_vmem()] * (chips + 1),
        out_specs=[whole_vmem()] * 2,
        out_shape=[
            jax.ShapeDtypeStruct((half, GRID, 2 * HALF), F32),
            jax.ShapeDtypeStruct((2, chips * 2 * reach_y, 2 * HALF), F32),
        ],
        scratch_shapes=stacking_scratch(chips, reach_x, reach_y),
        compiler_params=params(),
        cost_estimate=cost(EARLY_FLOPS, 4 * half * GRID * 2 * HALF * 2),
        name="forward_early",
    )(*parts, table)


def forward_kernel(reach_x, reach_y, blocks, pieces, awaited, *refs):
    parts = refs[:pieces]
    early_ref, early_edges, table_ref, modes_ref = refs[pieces : pieces + 4]
    refs = refs[pieces + 4 + awaited :]
    spectrum, even_out, layers_out, odd_out, own_out, peers_out, inner_out, *refs = refs
    opened, stacked, edges, slabs, head = refs
    half = reach_x // 2
    pair = lax.axis_size("pair")
    top = parts[0].shape[0] - opened.shape[0]
    stacked[...] = jnp.zeros_like(stacked)
    head[...] = jnp.zeros_like(head)
    for piece in range(pieces):
        first = from_short(parts[piece][:top, :])
        mantissa, exponent = first[2 : 2 + blocks], first[2 + blocks : 2 + 2 * blocks]
        peers_out[piece * blocks : (piece + 1) * blocks, :] = decode_rounded(mantissa, exponent)
        at = 6 + 2 * piece * blocks
        head[at : at + blocks, :] = mantissa
        head[at + blocks : at + 2 * blocks, :] = exponent
    rows = 2 * reach_y
    for chip in range(pieces // pair):
        place = chip * pair * rows
        edges[:, place : place + rows, :] = early_edges[:, chip * rows : (chip + 1) * rows, :]
    before = early_ref
    for core in range(1, pair):
        places = range(core, pieces, pair)
        stack_pieces(parts[core::pair], reach_x, reach_y, top, opened, stacked, edges, places)
        transform_pieces(table_ref[lax.axis_index("pair") ^ core], stacked, before, spectrum)
        before = spectrum

    chunk = 256

    def body(index, largest):
        rows = pl.ds(pl.multiple_of(index * chunk, chunk), chunk)
        low = low_lanes(chunk)
        decay = modes_ref[0, rows, :]
        log_decay = modes_ref[1, rows, :]
        across_half = jnp.exp(half * log_decay)
        across_cut = jnp.exp((half - 4) * log_decay)
        layers = [spectrum[i, rows, :] for i in range(half)]
        run = layers[0]
        cut_right = run
        for i in range(1, half):
            run = decay * run + layers[i]
            if i == half - 5:
                cut_right = run
        right = run
        run = layers[half - 1]
        cut_left = run
        for i in range(half - 2, -1, -1):
            run = decay * run + layers[i]
            if i == 4:
                cut_left = run
        left = run
        inner_out[rows, :] = jnp.where(low, right, left)
        swapped_right, swapped_left = swap(right), swap(left)
        own = jnp.where(low, left + across_half * swapped_left, right + across_half * swapped_right)
        own_out[rows, :] = own
        made = [
            jnp.where(low, own, cut_right + across_cut * swapped_right),
            jnp.where(low, cut_left + across_cut * swapped_left, own),
        ]
        for slab, values in enumerate(made):
            slabs[slab, rows, :] = values
        return tuple(
            jnp.maximum(old, jnp.max(jnp.abs(values).reshape(chunk // 8, 8, 2 * HALF), axis=0))
            for old, values in zip(largest, made)
        )

    zero = jnp.zeros((8, 2 * HALF), F32)
    largest = lax.fori_loop(0, GRID // chunk, body, (zero,) * 2)
    top = head.shape[0]
    low = low_lanes(GRID // 2)
    upper, lower = own_out[: GRID // 2, :], own_out[GRID // 2 :, :]
    packed = [jnp.where(low, swap(upper), lower), jnp.where(low, upper, swap(lower))]

    def send(out, first, parts):
        place = first
        for index, (values, most) in enumerate(parts):
            exponent, fraction = fit_scale(jnp.max(most, axis=0, keepdims=True))
            head[2 * index : 2 * index + 1, :] = exponent
            head[2 * index + 1 : 2 * index + 2, :] = fraction
            out[place : place + values.shape[0], :] = quantize(values, exponent, fraction)
            place += values.shape[0]
        out[:first, :] = to_short(head[:first, :])

    with_most = lambda values: (values, jnp.abs(values))
    on_left = lax.axis_index("wide") & 1
    for side, (even, odd) in enumerate(((0, 1), (1, 0))):

        @pl.when(on_left == side)
        def _():
            send(even_out, top, [(slabs[even], largest[even]), with_most(packed[even])])
            send(layers_out, 16, [with_most(edges[1 - even])])
            send(odd_out, top, [(slabs[odd], largest[odd]), with_most(edges[1 - odd])])


def forward(parts, early, early_edges, table, modes, reach_x, reach_y, blocks, awaited):
    pieces = len(parts)
    half = reach_x // 2
    lanes = 2 * HALF
    head = up_to(6 + 2 * pieces * blocks, 16)
    border = pieces * 2 * reach_y
    short = lambda rows: jax.ShapeDtypeStruct((rows, lanes), jnp.int16)
    return pl.pallas_call(
        functools.partial(
            forward_kernel, reach_x, reach_y, blocks, pieces, len(awaited)
        ),
        in_specs=[whole_vmem()] * (pieces + 4) + [anywhere()] * len(awaited),
        out_specs=[whole_vmem()] * 7,
        out_shape=[
            jax.ShapeDtypeStruct((half, GRID, lanes), F32),
            short(head + GRID + GRID // 2),
            short(16 + border),
            short(head + GRID + border),
            jax.ShapeDtypeStruct((GRID, lanes), F32),
            jax.ShapeDtypeStruct((pieces * blocks, BLOCK), F32),
            jax.ShapeDtypeStruct((GRID, lanes), F32),
        ],
        scratch_shapes=stacking_scratch(pieces // table.shape[0], reach_x, reach_y)
        + [
            pltpu.VMEM((2, border, lanes), F32),
            pltpu.VMEM((2, GRID, lanes), F32),
            pltpu.VMEM((head, lanes), F32),
        ],
        compiler_params=params(),
        cost_estimate=cost(2 * half * 256 * 256 * 128, 4 * half * GRID * lanes * 2),
        name="forward",
    )(*parts, early, early_edges, table, modes, *awaited)


def opened_part(ref, index, first, rows):
    head = from_short(ref[:16, :])
    scale = unit(head[2 * index : 2 * index + 1], head[2 * index + 1 : 2 * index + 2])
    return from_short(ref[first : first + rows, :]) * scale


def pair_kernel(reach_x, flips, own_ref, even_ref, modes_ref, *refs):
    outs, head = refs[:-1], refs[-1]
    span = reach_x - 4
    here = lax.axis_index("wide")
    low = low_lanes(GRID)
    log_decay = modes_ref[1]
    own = own_ref[...]
    top = even_ref.shape[0] - GRID - GRID // 2
    cut = opened_part(even_ref, 0, top, GRID)
    packed = opened_part(even_ref, 1, top + GRID, GRID // 2)
    from_left = jnp.where(low, cut, jnp.concatenate([swap(packed), packed], axis=0))
    from_right = jnp.where(low, jnp.concatenate([packed, swap(packed)], axis=0), cut)
    partner = jnp.where((here & 1) == 1, from_left, from_right)

    def weight(distances):
        powers = []
        for distance in distances:
            ahead = span * distance - reach_x
            powers.append(jnp.where(distance >= 2, ahead, ahead + GRID).astype(F32))
        return jnp.exp(jnp.where(low, *powers) * log_decay)

    head[...] = jnp.zeros_like(head)
    for flip, out in zip(flips, outs):
        behind = (here ^ flip) - here
        message = own * weight((-behind, behind))
        behind = (here ^ flip) - (here ^ 1)
        beside = jnp.where(jnp.abs(behind) == 1, 0.0, 1.0)
        send_piece(out, head, message + partner * (weight((-behind, behind)) * beside))


def pair_messages(own, from_even, modes, reach_x, flips):
    return pl.pallas_call(
        functools.partial(pair_kernel, reach_x, flips),
        in_specs=[whole_vmem()] * 3,
        out_specs=[whole_vmem()] * len(flips),
        out_shape=[jax.ShapeDtypeStruct((16 + GRID, 2 * HALF), jnp.int16)] * len(flips),
        scratch_shapes=[pltpu.VMEM((16, 2 * HALF), F32)],
        compiler_params=params(),
        cost_estimate=cost(16 * GRID * 2 * HALF, 4 * GRID * 2 * HALF * (6 + len(flips))),
        name="pair_messages",
    )(own, from_even, modes)


def odd_kernel(odd_ref, moments_out, edges_out):
    rows = edges_out.shape[0]
    first = odd_ref.shape[0] - rows - GRID
    moments_out[...] = opened_part(odd_ref, 0, first, GRID)
    edges_out[...] = opened_part(odd_ref, 1, first + GRID, rows)


def open_odd(from_odd, border):
    lanes = 2 * HALF
    return pl.pallas_call(
        odd_kernel,
        in_specs=[whole_vmem()],
        out_specs=[whole_vmem()] * 2,
        out_shape=[
            jax.ShapeDtypeStruct((GRID, lanes), F32),
            jax.ShapeDtypeStruct((border, lanes), F32),
        ],
        compiler_params=params(),
        cost_estimate=cost(4 * GRID * lanes, 6 * (GRID + border) * lanes),
        name="open_odd",
    )(from_odd)


def far_kernel(fars, *refs):
    total = opened_part(refs[0], 0, 16, GRID)
    for ref in refs[1:fars]:
        total = total + opened_part(ref, 0, 16, GRID)
    refs[-1][...] = total


def far_moments(fars, awaited):
    return pl.pallas_call(
        functools.partial(far_kernel, len(fars)),
        in_specs=[whole_vmem()] * len(fars) + [anywhere()] * len(awaited),
        out_specs=whole_vmem(),
        out_shape=jax.ShapeDtypeStruct((GRID, 2 * HALF), F32),
        compiler_params=params(),
        cost_estimate=cost(EARLY_FLOPS, 2 * GRID * 2 * HALF * (2 + len(fars))),
        name="far_moments",
    )(*fars, *awaited)


def borders_kernel(reach_y, pieces, layers_ref, edges_ref, table_ref, *refs):
    out_ref, stacked, partial = refs[-3:]
    on_left = (lax.axis_index("wide") & 1) == 1
    pair = lax.axis_size("pair")
    rows = pieces * 2 * reach_y
    even = opened_part(layers_ref, 0, 16, rows)
    odd = edges_ref[...]
    left, right = jnp.where(on_left, even, odd), jnp.where(on_left, odd, even)
    low = low_lanes(rows)
    both = [jnp.where(low, left, swap(right)), jnp.where(low, swap(left), right)]
    core = lax.axis_index("pair")
    chip = lax.axis_index("narrow")
    stacked[...] = jnp.zeros_like(stacked)
    before = None
    for other in range(pair):
        for flip in range(pieces // pair):
            first = (flip * pair + other) * 2 * reach_y
            layers = [
                values[first + two * reach_y : first + (two + 1) * reach_y]
                for two in range(2)
                for values in both
            ]
            stack_layers(layers, chip ^ flip, reach_y, stacked)
        target = out_ref if other == pair - 1 else partial
        transform_pieces(table_ref[core ^ other], stacked, before, target)
        before = target


def borders(layers, odd_edges, table, reach_y, pieces, awaited):
    chips = pieces // table.shape[0]
    shape = (4, GRID, 2 * HALF)
    return pl.pallas_call(
        functools.partial(borders_kernel, reach_y, pieces),
        in_specs=[whole_vmem()] * 3 + [anywhere()] * len(awaited),
        out_specs=whole_vmem(),
        out_shape=jax.ShapeDtypeStruct(shape, F32),
        scratch_shapes=[
            pltpu.VMEM((4 * chips * up_to(reach_y, 8), 2 * HALF), F32),
            pltpu.VMEM(shape, F32),
        ],
        compiler_params=params(),
        cost_estimate=cost(2 * 4 * 256 * 256 * 128, 4 * 6 * GRID * 2 * HALF),
        name="borders",
    )(layers, odd_edges, table, *awaited)


def send_fields(outs, flips, reach_y, field_high, field_low, high_ref, low_ref, ready, head):
    half = field_high.shape[0]
    mine = y_position()
    pitch = up_to(reach_y, 16)
    pick = lambda ref: jnp.concatenate([ref[mine ^ flip] for flip in flips], axis=0)
    table = (pick(high_ref), pick(low_ref))
    for i in range(0, half, 2):
        many = min(2, half - i)
        join = lambda ref: jnp.concatenate([ref[i + j] for j in range(many)], axis=1)
        result = dot_three(table, (join(field_high), join(field_low)))
        for j in range(many):
            for piece in range(len(flips)):
                ready[piece, (i + j) * reach_y : (i + j + 1) * reach_y, :] = result[
                    piece * pitch : piece * pitch + reach_y, j * 2 * HALF : (j + 1) * 2 * HALF
                ]
    head[...] = jnp.zeros_like(head)
    for piece, out in enumerate(outs):
        if ready.shape[1] > half * reach_y:
            ready[piece, half * reach_y :, :] = jnp.zeros_like(ready[piece, half * reach_y :, :])
        send_piece(out, head, ready[piece])


def inverse_kernel(reach_x, reach_y, flips, *refs):
    spectrum, border_ref, from_even, odd_ref, own_ref, inner_ref, far_ref = refs[:7]
    refs = refs[7:]
    high_ref, low_ref, modes_ref = refs[:3]
    outs = refs[3 : 3 + len(flips)]
    field_high, field_low, ready, head = refs[3 + len(flips) :]
    half = reach_x // 2
    span = reach_x - 4
    chunk = 256
    head_rows = from_even.shape[0] - GRID - GRID // 2
    on_left = (lax.axis_index("wide") & 1) == 1
    first = from_short(from_even[:16, :])
    even_unit = unit(first[0:1], first[1:2])

    def body(index, carry):
        first = pl.multiple_of(index * chunk, chunk)
        rows = pl.ds(first, chunk)
        low = low_lanes(chunk)
        decay = modes_ref[0, rows, :]
        log_decay = modes_ref[1, rows, :]
        ring = modes_ref[2, rows, :]
        gain = modes_ref[3, rows, :]
        across_half = jnp.exp(half * log_decay)
        across_cut = jnp.exp((half - 4) * log_decay)
        around = jnp.exp((GRID - 4) * log_decay)
        beside = jnp.exp((GRID - reach_x - span) * log_decay)
        layers = [spectrum[i, rows, :] for i in range(half)]

        at = pl.ds(pl.multiple_of(head_rows + index * chunk, 16), chunk)
        even, odd = from_short(from_even[at, :]) * even_unit, odd_ref[rows, :]
        left_moments, right_moments = jnp.where(on_left, even, odd), jnp.where(on_left, odd, even)
        border = [border_ref[i, rows, :] for i in range(4)]
        zero = jnp.zeros_like(decay)
        head_sum = border[0]
        for i in range(1, 4):
            head_sum = decay * head_sum + border[i]
        tail_sum = border[3]
        for i in range(2, -1, -1):
            tail_sum = decay * tail_sum + border[i]
        for i in range(4):
            layers[i] = layers[i] + jnp.where(low, border[i], zero)
        for i in range(4):
            place = half - 4 + i
            layers[place] = layers[place] + jnp.where(low, zero, border[i])
        total = own_ref[rows, :] * jnp.exp((GRID - reach_x) * log_decay)
        total = total + far_ref[rows, :]
        one = jnp.ones_like(decay)
        total = total + left_moments * jnp.where(low, beside, one)
        total = total + right_moments * jnp.where(low, one, beside)
        shared = jnp.where(low, head_sum, tail_sum)
        entering = (swap(total) + around * shared) * ring
        leaving = swap(across_half * entering + across_cut * shared + inner_ref[rows, :])
        run = jnp.where(low, entering, leaving)
        forward_runs = []
        for i in range(half):
            run = decay * run + layers[i]
            forward_runs.append(run)
        run = jnp.where(low, leaving, entering)
        for i in range(half - 1, -1, -1):
            ahead = decay * run
            high, rest = split(gain * (forward_runs[i] + ahead))
            field_high[i, rows, :] = high
            field_low[i, rows, :] = rest
            run = ahead + layers[i]
        return carry

    lax.fori_loop(0, GRID // chunk, body, 0)
    send_fields(outs, flips, reach_y, field_high, field_low, high_ref, low_ref, ready, head)


def inverse(
    spectrum, border, from_even, odd, own, inner, far, table, modes, reach_x, reach_y, flips
):
    half = reach_x // 2
    lanes = 2 * HALF
    body = up_to(half * reach_y, 16)
    shapes = [jax.ShapeDtypeStruct((16 + body, lanes), jnp.int16)] * len(flips)
    shapes += [jax.ShapeDtypeStruct((half, GRID, lanes), BF16)] * 2
    return pl.pallas_call(
        functools.partial(inverse_kernel, reach_x, reach_y, flips),
        in_specs=[whole_vmem()] * 10,
        out_specs=[whole_vmem()] * len(shapes),
        out_shape=shapes,
        scratch_shapes=[
            pltpu.VMEM((len(flips), body, lanes), F32),
            pltpu.VMEM((16, lanes), F32),
        ],
        compiler_params=params(),
        cost_estimate=cost(2 * half * 256 * 256 * 128, 4 * half * GRID * lanes * 2),
        name="inverse",
    )(spectrum, border, from_even, odd, own, inner, far, *table, modes)


def inverse_rest_kernel(reach_y, flips, field_high, field_low, high_ref, low_ref, *refs):
    outs, (ready, head) = refs[: len(flips)], refs[len(flips) :]
    send_fields(outs, flips, reach_y, field_high, field_low, high_ref, low_ref, ready, head)


def inverse_rest(field, table, reach_y, flips):
    half = field[0].shape[0]
    lanes = 2 * HALF
    body = up_to(half * reach_y, 16)
    return pl.pallas_call(
        functools.partial(inverse_rest_kernel, reach_y, flips),
        in_specs=[whole_vmem()] * 4,
        out_specs=[whole_vmem()] * len(flips),
        out_shape=[jax.ShapeDtypeStruct((16 + body, lanes), jnp.int16)] * len(flips),
        scratch_shapes=[
            pltpu.VMEM((len(flips), body, lanes), F32),
            pltpu.VMEM((16, lanes), F32),
        ],
        compiler_params=params(),
        cost_estimate=cost(2 * half * 256 * 256 * 128, 4 * half * GRID * lanes * 2),
        name="inverse_rest",
    )(*field, *table)


def sum_rows(values):
    row = lax.broadcasted_iota(jnp.int32, values[0].shape, 0)
    for step in (4, 2, 1):
        low = (row & step) == 0
        paired = []
        for one, other in zip(values[: len(values) // 2], values[len(values) // 2 :]):
            kept = jnp.where(low, one, other)
            moved = jnp.where(low, other, one)
            if step == 4:
                moved = pltpu.roll(moved, 4, 0)
            else:
                moved = jnp.where(low, pltpu.roll(moved, 8 - step, 0), pltpu.roll(moved, step, 0))
            paired.append(kept + moved)
        values = paired
    return values[0]


def z_lines(parts, flips, high_ref, low_ref):
    mine = y_position()
    opened = []
    for part in parts:
        first = from_short(part[:16, :])
        opened.append(from_short(part[16:, :]) * unit(first[0:1], first[1:2]))
    values = split(jnp.concatenate(opened, axis=1))
    pick = lambda ref: jnp.concatenate([ref[mine ^ flip] for flip in flips], axis=0)
    return dot_three(values, (pick(high_ref), pick(low_ref)))


def sample_early_kernel(flips, *refs):
    *parts, high_ref, low_ref, out_ref = refs
    out_ref[...] = z_lines(parts, flips, high_ref, low_ref)


def sample_early(parts, flips, table):
    rows = parts[0].shape[0] - 16
    return pl.pallas_call(
        functools.partial(sample_early_kernel, flips),
        in_specs=[whole_vmem()] * (len(parts) + 2),
        out_specs=whole_vmem(),
        out_shape=jax.ShapeDtypeStruct((rows, 2 * REGION), F32),
        compiler_params=params(),
        cost_estimate=cost(EARLY_FLOPS, 4 * rows * 512),
        name="sample_early",
    )(*parts, *table)


def sample_kernel(last, reach_x, reach_y, flips, place_in, *refs):
    parts = refs[: len(flips)]
    early_ref, high_ref, low_ref, line_ref, own_ref, vector_ref, near_ref, out_ref = refs[
        len(flips) : len(flips) + 8
    ]
    flat, field, sums, place_ref, sem = refs[len(flips) + 8 :]
    copy = pltpu.make_async_copy(place_in, place_ref, sem)
    copy.start()
    half_rows = reach_x * reach_y // 2
    both = early_ref[...] + z_lines(parts, flips, high_ref, low_ref)
    flat[:half_rows, :] = both[:half_rows, :REGION]
    flat[half_rows:, :] = both[:half_rows, REGION:]
    for x in range(reach_x):
        layer = flat[x * reach_y : (x + 1) * reach_y, :]
        for row in pair_rows(x, reach_x, reach_y):
            field[pl.ds(row, reach_y, stride=2), :] = layer
    count = place_ref.shape[1]

    def body(group, carry):
        for eight in range(0, GROUP, 8):
            totals = []
            for local in range(eight, eight + 8):
                panel = group * GROUP + local
                row = place_ref[0, panel]
                first = pl.multiple_of(panel * 16, 16)
                totals.append(
                    field[pl.ds(row, 8), :] * line_ref[pl.ds(first, 8), :]
                    + field[pl.ds(row + 2 * reach_y, 8), :] * line_ref[pl.ds(first + 8, 8), :]
                )
            sums[pl.ds(pl.multiple_of(group * GROUP + eight, 8), 8), :] = sum_rows(totals)
        return carry

    copy.wait()
    lax.fori_loop(0, count // GROUP, body, 0)
    first, rest = split(sums[...])
    second, third = split(sums[...] - first.astype(F32))
    across = lambda values: lax.dot_general(
        jnp.ones((16, REGION), BF16),
        values,
        (((1,), (1,)), ((), ())),
        preferred_element_type=F32,
    )
    sampled = across(first) + (across(second) + across(third))
    for block in range(count // BLOCK):
        lane = slice(block * BLOCK, (block + 1) * BLOCK)
        row = slice(block, block + 1)
        vector = vector_ref[row, :]
        image = jnp.where(own_ref[row, :] == 1, 0.0, 0.5 * vector) + sampled[:1, lane]
        image = image + near_ref[row, :]
        if last:
            out_ref[0:1, lane] = vector
            out_ref[1:2, lane] = image
        else:
            out_ref[row, :] = image


def sample(last, places, parts, flips, early, table, lines, flag, vector, near, reach_x, reach_y):
    count = places.shape[1]
    blocks = count // BLOCK
    shape = (2, count) if last else (blocks, BLOCK)
    return pl.pallas_call(
        functools.partial(sample_kernel, last, reach_x, reach_y, flips),
        in_specs=[anywhere()] + [whole_vmem()] * (len(parts) + 7),
        out_specs=whole_vmem(),
        out_shape=jax.ShapeDtypeStruct(shape, F32),
        scratch_shapes=[
            pltpu.VMEM((reach_x * reach_y, REGION), F32),
            pltpu.VMEM((pair_count(reach_x, reach_y), REGION), F32),
            pltpu.VMEM((count, REGION), F32),
            pltpu.SMEM((2, count), jnp.int32),
            pltpu.SemaphoreType.DMA,
        ],
        compiler_params=params(),
        cost_estimate=cost(reach_x * reach_y * 256 * 512, 4 * 16 * count * REGION),
        name="sample",
    )(
        places,
        *parts,
        early,
        *table,
        lines,
        flag.reshape(blocks, BLOCK),
        vector.reshape(blocks, BLOCK),
        near,
    )


def near_kernel(slots, blocks, place_ref, target_ref, *refs):
    even_ref, odd_ref, peers_ref, tile_ref = refs[:4]
    out_ref, held = refs[-2:]
    count = peers_ref.shape[0]
    held[count : 2 * count, :] = peers_ref[...]
    on_left = lax.axis_index("wide") & 1
    for side, ref in ((1 - on_left, even_ref), (on_left, odd_ref)):
        top = from_short(ref[...])
        for piece in range(count // blocks):
            at = 6 + 2 * piece * blocks
            held[pl.ds(side * (2 * count) + piece * blocks, blocks), :] = decode_rounded(
                top[at : at + blocks], top[at + blocks : at + 2 * blocks]
            )
    out_ref[...] = jnp.zeros_like(out_ref)
    for slot in range(slots):
        picked = held[pl.ds(place_ref[slot], 1), :]
        picked = jnp.broadcast_to(picked, (16, BLOCK)).astype(BF16)
        product = lax.dot_general(
            picked,
            tile_ref[slot],
            (((1,), (1,)), ((), ())),
            preferred_element_type=F32,
        )
        target = pl.ds(target_ref[slot], 1)
        out_ref[target, :] = out_ref[target, :] + product[:1]


def near_field(places, targets, from_even, from_odd, peers, tiles, blocks, out_rows, awaited):
    slots = tiles.shape[0]
    head = up_to(6 + 2 * peers.shape[0], 16)
    constant = lambda shape: pl.BlockSpec(shape, lambda i: (0,) * len(shape))
    return pl.pallas_call(
        functools.partial(near_kernel, slots, blocks),
        grid=(1,),
        in_specs=[
            in_smem(),
            in_smem(),
            constant((head, BLOCK)),
            constant((head, BLOCK)),
            constant(peers.shape),
            constant(tiles.shape),
        ]
        + [anywhere()] * len(awaited),
        out_specs=constant((out_rows, BLOCK)),
        out_shape=jax.ShapeDtypeStruct((out_rows, BLOCK), F32),
        scratch_shapes=[pltpu.VMEM((3 * peers.shape[0], BLOCK), F32)],
        compiler_params=params(),
        cost_estimate=cost(2 * slots * 16 * BLOCK * BLOCK, 2 * slots * BLOCK * BLOCK),
        name="near_field",
    )(places, targets, from_even, from_odd, peers, tiles, *awaited)


def shards(
    density,
    surface_flag,
    stencil_base,
    sample_weights,
    dipole_weights,
    near_target,
    near_source,
    near_tiles,
):
    x_count = lax.axis_size("wide")
    y_count = lax.axis_size(Y_AXES)
    y_index = lax.axis_index(Y_AXES)
    pair = lax.axis_size("pair")
    span_x = REGION // x_count
    span_y = REGION // y_count
    reach_x = span_x + 4
    reach_y = span_y + 4
    count = density.shape[0]
    blocks = count // BLOCK

    z_forward, z_inverse, y_forward, y_inverse, modes = tables(y_count, pair, span_y)
    modes = lax.dynamic_index_in_dim(jnp.asarray(modes), y_index, 0, keepdims=False)

    neighbour = near_source // blocks
    flip = (y_index + neighbour % 3 - 1) ^ y_index
    sources = ((neighbour // 3) * y_count + flip) * blocks + near_source % blocks
    out_rows = up_to(blocks + 1, 8)
    live = near_target >= 0
    sources = jnp.where(live, sources, 0)
    targets = jnp.where(live, near_target, out_rows - 1)

    swaps = lambda pairs: [(i, j) for i, j in pairs] + [(j, i) for i, j in pairs]
    even_swap = swaps([(i, i + 1) for i in range(0, x_count - 1, 2)])
    odd_swap = swaps([(i, i + 1) for i in range(1, x_count - 1, 2)])
    far_flips = list(range(2, x_count, 2))

    first, rest = list(range(pair, y_count)), list(range(pair))
    same_core = list(range(0, y_count, pair))
    other_core = [flip for flip in range(y_count) if flip not in same_core]

    def turned(sent, then):
        arrived = [None] * y_count
        for flip, part in zip(first + rest, list(sent) + list(then)):
            swap_pairs = [(i, i ^ flip) for i in range(y_count)]
            arrived[flip] = part if flip == 0 else lax.ppermute(part, Y_AXES, swap_pairs)
        return arrived

    def chosen(parts, flips):
        return [parts[flip] for flip in flips]

    def convolve_and_sample(last, vector, sent, both, table, places, sample_lines, awaited):
        arrived = turned(sent, spread_rest(vector, both, table, rest))
        early, edges = forward_early(chosen(arrived, same_core), y_forward, reach_x, reach_y)
        spectrum, even_message, layers, odd_message, own, peers, inner = forward(
            arrived, early, edges, y_forward, modes, reach_x, reach_y, blocks, awaited
        )
        from_even = lax.ppermute(even_message, "wide", even_swap)
        from_odd = lax.ppermute(odd_message, "wide", odd_swap)
        even_layers = lax.ppermute(layers, "wide", even_swap)
        fars = [
            lax.ppermute(message, "wide", [(i, i ^ flip) for i in range(x_count)])
            for flip, message in zip(
                far_flips, pair_messages(own, from_even, modes, reach_x, far_flips)
            )
        ]
        odd_moments, odd_edges = open_odd(from_odd, y_count * 2 * reach_y)
        far = far_moments(fars, [odd_moments]) if fars else jnp.zeros_like(own)
        *sent, high, low = inverse(
            spectrum,
            borders(even_layers, odd_edges, y_forward, reach_y, y_count, [far]),
            from_even,
            odd_moments,
            own,
            inner,
            far,
            y_inverse,
            modes,
            reach_x,
            reach_y,
            first,
        )
        then = inverse_rest((high, low), y_inverse, reach_y, rest)
        near_part = near_field(
            sources, targets, from_even, from_odd, peers, near_tiles, blocks, out_rows, then[:1]
        )
        arrived = turned(sent, then)
        image = sample(
            last,
            places,
            chosen(arrived, other_core),
            other_core,
            sample_early(chosen(arrived, same_core), same_core, z_inverse),
            z_inverse,
            sample_lines,
            surface_flag,
            vector,
            near_part,
            reach_x,
            reach_y,
        )
        return image, near_part

    raw = (stencil_base, surface_flag, sample_weights, dipole_weights)
    *sent, wide_high, wide_low, source_coeff, places, vector, high, low = spread(
        density, z_forward, None, raw, reach_x, reach_y, first
    )
    z_forward = (high, low)
    sample_lines = place_sample_lines(places, sample_weights)
    vector, near_part = convolve_and_sample(
        False,
        vector,
        sent,
        (wide_high, wide_low),
        z_forward,
        places,
        sample_lines,
        [sample_lines],
    )
    source_lines = place_lines(places, source_coeff, [near_part])
    *sent, wide_high, wide_low = spread(
        vector.reshape(-1), z_forward, (places, source_lines), None, reach_x, reach_y, first
    )
    both_images, _ = convolve_and_sample(
        True, vector, sent, (wide_high, wide_low), z_forward, places, sample_lines, []
    )
    return both_images


def solution(mesh):
    panels = P(("groups",) + ALL_AXES)
    columns = P(None, ("groups",) + ALL_AXES)
    in_specs = (
        panels,
        panels,
        columns,
        columns,
        columns,
        panels,
        panels,
        P(("groups",) + ALL_AXES, None, None),
    )
    return jax.shard_map(
        shards, mesh=mesh, in_specs=in_specs, out_specs=columns, check_vma=False
    )
```

```python
import functools
import math

import jax
import jax.numpy as jnp
import numpy as np
from jax import lax
from jax.experimental import pallas as pl
from jax.experimental.pallas import tpu as pltpu
from jax.sharding import PartitionSpec as P

GRID = 256
REGION = 128
BLOCK = 128
HALF = 64
KERNEL_GAIN = 4.0
SCREEN = 1.0 / 1024.0
LN2 = math.log(2.0)
ROUNDING = 1.5 * 2.0**23
Y_AXES = ("narrow", "pair")
ALL_AXES = ("wide", "narrow", "pair")
F32 = jnp.float32
BF16 = jnp.bfloat16
VMEM_LIMIT = 24 * 1024 * 1024
START_LIMIT = VMEM_LIMIT
EARLY_FLOPS = 5 * 10**9
GROUP = 32
CHAINS = 2


def cas(angles):
    return np.cos(angles) + np.sin(angles)


def up_to(count, multiple):
    return -(-count // multiple) * multiple


def low_lanes(rows):
    return lax.broadcasted_iota(jnp.int32, (rows, 2 * HALF), 1) < HALF


def swap(values):
    return pltpu.roll(values, HALF, 1)


def split(values):
    high = values.astype(BF16)
    return high, (values - high.astype(F32)).astype(BF16)


def dot(left, right):
    return jnp.dot(left, right, preferred_element_type=F32)


def dot_three(left, right):
    return dot(left[0], right[0]) + (dot(left[0], right[1]) + dot(left[1], right[0]))


def params():
    return pltpu.CompilerParams(vmem_limit_bytes=VMEM_LIMIT)


def whole_vmem():
    return pl.BlockSpec(memory_space=pltpu.VMEM)


def anywhere():
    return pl.BlockSpec(memory_space=pl.ANY)


def in_smem():
    return pl.BlockSpec(memory_space=pltpu.SMEM)


def cost(flops, moved):
    return pl.CostEstimate(flops=flops, bytes_accessed=moved, transcendentals=0)


def full_scale(exponent, fraction):
    return fraction * jnp.exp(exponent * LN2) * (1.0 / 1024.0)


def fit_scale(largest):
    largest = jnp.maximum(largest, 1e-30)
    exponent = jnp.floor(jnp.log(largest) * (1.0 / LN2))
    fraction = jnp.ceil(largest * jnp.exp(-exponent * LN2) * 1024.0) + 1.0
    return exponent, fraction


def to_short(values):
    return values.astype(jnp.int32).astype(jnp.int16)


def from_short(values):
    return values.astype(jnp.int32).astype(F32)


def quantize(values, exponent, fraction):
    scaled = values * (32767.0 / full_scale(exponent, fraction))
    return to_short((scaled + ROUNDING) - ROUNDING)


def unit(exponent, fraction):
    return full_scale(exponent, fraction) * (1.0 / 32767.0)


def encode_rounded(values):
    rounded = values.astype(BF16).astype(F32)
    size = jnp.maximum(jnp.abs(rounded), 1e-30)
    exponent = jnp.floor(jnp.log(size) * (1.0 / LN2))
    return jnp.round(rounded * jnp.exp((10.0 - exponent) * LN2)), exponent


def decode_rounded(mantissa, exponent):
    return (mantissa * jnp.exp((exponent - 10.0) * LN2)).astype(BF16).astype(F32)


def send_piece(out, head, values):
    exponent, fraction = fit_scale(jnp.max(jnp.abs(values), axis=0, keepdims=True))
    head[0:1, :] = exponent
    head[1:2, :] = fraction
    top = head.shape[0]
    out[:top, :] = to_short(head[...])
    out[top:, :] = quantize(values, exponent, fraction)


def y_position():
    return lax.axis_index("narrow") * lax.axis_size("pair") + lax.axis_index("pair")


def halves(table):
    high = table.astype(jnp.bfloat16)
    return high, (table - high.astype(np.float64)).astype(jnp.bfloat16)


def tables(y_count, pair, span_y):
    depth = GRID // y_count
    reach = span_y + 4
    waves = np.arange(GRID)
    step = 2.0 * np.pi / GRID
    z_table = cas(step * np.outer(np.arange(REGION), waves))
    z_forward = np.zeros((y_count, 2 * REGION, 2 * HALF))
    z_inverse = np.zeros((y_count, 2 * HALF, 2 * REGION))
    symbols = 4.0 * np.sin(np.pi * waves / GRID) ** 2
    shift = np.full((y_count, GRID, 2 * HALF), 1.0)
    y_forward = np.zeros((GRID, y_count, up_to(reach, 8)))
    y_inverse = np.zeros((y_count, up_to(reach, 16), GRID))
    for block in range(y_count):
        mine = z_table[:, block * depth : (block + 1) * depth]
        for half in range(2):
            rows = slice(half * REGION, (half + 1) * REGION)
            lanes = slice(half * HALF, half * HALF + depth)
            z_forward[block, rows, lanes] = mine
            z_inverse[block, lanes, rows] = mine.T / GRID
            shift[block, :, lanes] = (
                SCREEN + symbols[:, None] + symbols[None, block * depth : (block + 1) * depth]
            )
        cells = block * span_y - 2 + np.arange(reach)
        y_table = cas(step * np.outer(waves, cells))
        y_forward[:, block, :reach] = y_table
        y_inverse[block, :reach] = y_table.T / GRID
    y_forward = y_forward.reshape(GRID, y_count // pair, pair, -1).transpose(2, 0, 1, 3)
    y_forward = halves(y_forward.reshape(pair, GRID, -1))
    y_forward = np.concatenate([y_forward[0], y_forward[0], y_forward[1]], axis=2)
    root = np.sqrt(shift * (shift + 4.0))
    decay = 2.0 / (2.0 + shift + root)
    log_decay = np.log(decay)
    ring = 1.0 / (1.0 - np.exp(GRID * log_decay))
    gain = KERNEL_GAIN / root
    modes = np.stack([decay, log_decay, ring, gain], axis=1).astype(np.float32)
    return (
        halves(z_forward),
        halves(z_inverse),
        y_forward,
        halves(y_inverse),
        modes,
    )


def mixing_matrix():
    place = lax.broadcasted_iota(jnp.int32, (4 * BLOCK, 4 * BLOCK), 0)
    lane = lax.broadcasted_iota(jnp.int32, (4 * BLOCK, 4 * BLOCK), 1)
    return jnp.where(lane == 4 * (place % BLOCK) + place // BLOCK, 1.0, 0.0).astype(BF16)


def weave(tiles, mixing, out):
    weights = jnp.concatenate([jnp.concatenate(tile, axis=1) for tile in tiles], axis=0)
    first, rest = split(weights)
    second, third = split(weights - first.astype(F32))
    woven = dot(first, mixing) + (dot(second, mixing) + dot(third, mixing))
    for tile in range(len(tiles)):
        for part in range(BLOCK // GROUP):
            at = (tile * (BLOCK // GROUP) + part) * 16
            lanes = slice(part * BLOCK, (part + 1) * BLOCK)
            for a in range(4):
                row = tile * 16 + 4 * a
                out[pl.ds(at + 8 * (a // 2) + a % 2, 4, stride=2), :] = woven[row : row + 4, lanes]


def by_depth(ref):
    return [ref[pl.ds(depth, 16, stride=4), :] for depth in range(4)]


def pair_rows(x, reach_x, reach_y):
    even = (x // 2) * 2 * reach_y + x % 2
    if x == 0 or x == reach_x - 1:
        return [even]
    return [even, reach_x * reach_y + ((x - 1) // 2) * 2 * reach_y + (x - 1) % 2]


def pair_count(reach_x, reach_y):
    return (2 * reach_x - 2) * reach_y


def in_window(lanes, depth):
    return ((lanes - depth) & -4) == 0


def add_panels(reach, woven, vector_ref, place_ref, weight_ref, grids):
    lanes = lax.broadcasted_iota(jnp.int32, (8, REGION), 1)

    def body(group, carry):
        at = pl.multiple_of(group * 16, 16)
        coeff = [weight_ref[pl.ds(at + 8 * q, 8), :] for q in range(2)] if woven else None
        for local in range(GROUP):
            panel = group * GROUP + local
            grid = grids[local % len(grids)]
            row = place_ref[0, panel]
            value = vector_ref[panel]
            if woven:
                depth = place_ref[1, panel]
                shift = (depth - 4 * local) & (REGION - 1)
                value = jnp.where(in_window(lanes, depth), value, 0.0)
                lines = [pltpu.roll(coeff[q], shift, 1) for q in range(2)]
            else:
                first = pl.multiple_of(panel * 16, 16)
                lines = [weight_ref[pl.ds(first + 8 * q, 8), :] for q in range(2)]
            places = [pl.ds(row, 8), pl.ds(row + 2 * reach, 8)]
            held = [grid[place, :] for place in places]
            for q in range(2):
                grid[places[q], :] = held[q] + lines[q] * value
        return carry

    lax.fori_loop(0, vector_ref.shape[0] // GROUP, body, 0)


def send_pieces(outs, flips, head, rounded, both, high_ref, low_ref):
    blocks = rounded.shape[0]
    mantissa, exponent = encode_rounded(rounded)
    head[...] = jnp.zeros_like(head)
    head[2 : 2 + blocks, :] = mantissa
    head[2 + blocks : 2 + 2 * blocks, :] = exponent
    mine = y_position()
    for at in range(0, len(flips), 2):
        pick = lambda ref: jnp.concatenate([ref[mine ^ flip] for flip in flips[at : at + 2]], axis=1)
        result = dot_three(both, (pick(high_ref), pick(low_ref)))
        for i, out in enumerate(outs[at : at + 2]):
            send_piece(out, head, result[:, i * 2 * HALF : (i + 1) * 2 * HALF])


def spread_grid(reach_x, reach_y, rounded, tables, outs, flips, wides, head, total, grids):
    for x in range(reach_x):
        parts = [
            grid[pl.ds(row, reach_y, stride=2), :]
            for row in pair_rows(x, reach_x, reach_y)
            for grid in grids
        ]
        total[x * reach_y : (x + 1) * reach_y, :] = sum(parts[1:], parts[0])
    half = reach_x * reach_y // 2
    both = jnp.concatenate([total[:half, :], total[half:, :]], axis=1)
    extra = wides[0].shape[0] - half
    if extra:
        both = jnp.concatenate([both, jnp.zeros((extra, 2 * REGION), F32)], axis=0)
    both = split(both)
    for wide, values in zip(wides, both):
        wide[...] = values
    send_pieces(outs, flips, head, rounded, both, *tables)


def start_kernel(reach_x, reach_y, flips, *refs):
    vector_in, *remote = refs[:8]
    refs = refs[8:]
    outs, refs = refs[: len(flips)], refs[len(flips) :]
    wides, (weight_ref, places_out), refs = refs[:2], refs[2:4], refs[4:]
    rounded, high, low, stencil, flag, samples, dipoles, vector_ref = refs[:8]
    place_ref, sems, head, total = refs[8:12]
    grids = refs[12:]
    tiles = samples.shape[0]
    copies = []
    fetch = lambda source, target: copies.append(
        pltpu.make_async_copy(source, target, sems.at[len(copies)])
    )
    rounded_in, high_in, low_in, stencil_in, flag_in, sample_in, dipole_in = remote
    fetch(stencil_in, stencil)
    fetch(flag_in, flag)
    fetch(vector_in, vector_ref)
    for tile in range(tiles):
        lanes = pl.ds(tile * BLOCK, BLOCK)
        fetch(sample_in.at[:, lanes], samples.at[tile])
        fetch(dipole_in.at[:, lanes], dipoles.at[tile])
    needed_first = len(copies)
    fetch(rounded_in, rounded)
    fetch(high_in, high)
    fetch(low_in, low)
    for copy in copies:
        copy.start()
    for grid in grids:
        grid[...] = jnp.zeros_like(grid)
    mixing = mixing_matrix()
    copies[0].wait()
    span_x, span_y = reach_x - 4, reach_y - 4
    local_x = stencil[0:1, :] - (lax.axis_index("wide") * span_x - 2)
    local_y = stencil[1:2, :] - (y_position() * span_y - 2)
    odd = local_x & 1
    places_out[0:1, :] = odd * (reach_x * reach_y) + (local_x >> 1) * (2 * reach_y) + 2 * local_y
    places_out[1:2, :] = stencil[2:3, :]
    to_scalar = pltpu.make_async_copy(places_out, place_ref, sems.at[len(copies)])
    to_scalar.start()
    for copy in copies[1:needed_first]:
        copy.wait()
    sources = []
    for tile in range(tiles):
        charged = flag[:, tile * BLOCK : (tile + 1) * BLOCK] == 1
        pairs = zip(by_depth(samples.at[tile]), by_depth(dipoles.at[tile]))
        sources.append([jnp.where(charged, -sample, dipole) for sample, dipole in pairs])
    weave(sources, mixing, weight_ref)
    to_scalar.wait()
    add_panels(reach_y, True, vector_ref, place_ref, weight_ref, grids)
    for copy in copies[needed_first:]:
        copy.wait()
    spread_grid(
        reach_x, reach_y, rounded[...], (high, low), outs, flips, wides, head, total, grids
    )


def spread_kernel(reach_x, reach_y, flips, *refs):
    vector_in, place_in, rounded_ref, high_ref, low_ref, line_ref = refs[:6]
    refs = refs[6:]
    outs, wides, (vector_ref, place_ref, sems, head, total), grids = (
        refs[: len(flips)],
        refs[len(flips) : len(flips) + 2],
        refs[len(flips) + 2 : len(flips) + 7],
        refs[len(flips) + 7 :],
    )
    copies = [
        pltpu.make_async_copy(vector_in, vector_ref, sems.at[0]),
        pltpu.make_async_copy(place_in, place_ref, sems.at[1]),
    ]
    for copy in copies:
        copy.start()
    for grid in grids:
        grid[...] = jnp.zeros_like(grid)
    for copy in copies:
        copy.wait()
    add_panels(reach_y, False, vector_ref, place_ref, line_ref, grids)
    spread_grid(
        reach_x,
        reach_y,
        rounded_ref[...],
        (high_ref, low_ref),
        outs,
        flips,
        wides,
        head,
        total,
        grids,
    )


def spread(vector, table, placed, raw, reach_x, reach_y, flips):
    count = vector.shape[0]
    half = reach_x * reach_y // 2
    blocks = count // BLOCK
    top = up_to(2 + 2 * blocks, 16)
    lanes = 2 * HALF
    body = up_to(half, 16)
    woven = (count // GROUP * 16, BLOCK)
    out_shapes = [jax.ShapeDtypeStruct((top + body, lanes), jnp.int16)] * len(flips)
    out_shapes += [jax.ShapeDtypeStruct((body, 2 * REGION), BF16)] * 2
    rounded = vector.reshape(blocks, BLOCK)
    work = [
        pltpu.VMEM((top, lanes), F32),
        pltpu.VMEM((reach_x * reach_y, REGION), F32),
    ] + [pltpu.VMEM((pair_count(reach_x, reach_y), REGION), F32)] * CHAINS
    if placed is None:
        stencil, flag, sample, dipole = raw
        operands = [vector, rounded, *table, stencil, flag.reshape(1, -1), sample, dipole]
        operands = [pltpu.with_memory_space_constraint(value, pltpu.HBM) for value in operands]
        in_specs = [pl.BlockSpec(memory_space=pltpu.HBM)] * 8
        out_shapes += [jax.ShapeDtypeStruct(woven, F32)]
        out_shapes += [jax.ShapeDtypeStruct((2, count), jnp.int32)]
        out_shapes += [jax.ShapeDtypeStruct(rounded.shape, F32)]
        out_shapes += [jax.ShapeDtypeStruct(values.shape, BF16) for values in table]
        tiled = pltpu.VMEM((blocks, 64, BLOCK), F32)
        work = [
            pltpu.VMEM(stencil.shape, jnp.int32),
            pltpu.VMEM((1, count), jnp.int32),
            tiled,
            tiled,
            pltpu.SMEM((count,), F32),
            pltpu.SMEM((2, count), jnp.int32),
            pltpu.SemaphoreType.DMA((7 + 2 * blocks,)),
        ] + work
    else:
        operands = [vector, placed[0], rounded, *table, placed[1]]
        in_specs = [anywhere()] * 2 + [whole_vmem()] * 4
        work = [
            pltpu.SMEM((count,), F32),
            pltpu.SMEM((2, count), jnp.int32),
            pltpu.SemaphoreType.DMA((2,)),
        ] + work
    return pl.pallas_call(
        functools.partial(
            start_kernel if placed is None else spread_kernel, reach_x, reach_y, flips
        ),
        in_specs=in_specs,
        out_specs=[whole_vmem()] * len(out_shapes),
        out_shape=out_shapes,
        scratch_shapes=work,
        compiler_params=pltpu.CompilerParams(
            vmem_limit_bytes=START_LIMIT if placed is None else VMEM_LIMIT
        ),
        cost_estimate=cost(2 * half * 256 * 512, 4 * 16 * count * REGION),
        name="start" if placed is None else "spread",
    )(*operands)


def spread_rest_kernel(flips, rounded_ref, wide_high, wide_low, high_ref, low_ref, *refs):
    outs, head = refs[:-1], refs[-1]
    both = (wide_high[...], wide_low[...])
    send_pieces(outs, flips, head, rounded_ref[...], both, high_ref, low_ref)


def spread_rest(rounded, both, table, flips):
    blocks = rounded.shape[0]
    top = up_to(2 + 2 * blocks, 16)
    shape = (top + both[0].shape[0], 2 * HALF)
    return pl.pallas_call(
        functools.partial(spread_rest_kernel, flips),
        in_specs=[whole_vmem()] * 5,
        out_specs=[whole_vmem()] * len(flips),
        out_shape=[jax.ShapeDtypeStruct(shape, jnp.int16)] * len(flips),
        scratch_shapes=[pltpu.VMEM((top, 2 * HALF), F32)],
        compiler_params=params(),
        cost_estimate=cost(2 * shape[0] * 256 * 256 * 3, 4 * shape[0] * 512),
        name="spread_rest",
    )(rounded, *both, *table)


def lines_kernel(place_ref, coeff_ref, *refs):
    out_ref = refs[-1]
    lanes = lax.broadcasted_iota(jnp.int32, (8, REGION), 1)

    def body(group, carry):
        at = pl.multiple_of(group * 16, 16)
        coeff = [coeff_ref[pl.ds(at + 8 * q, 8), :] for q in range(2)]
        for local in range(GROUP):
            panel = group * GROUP + local
            depth = place_ref[1, panel]
            shift = (depth - 4 * local) & (REGION - 1)
            inside = in_window(lanes, depth)
            for q in range(2):
                first = pl.multiple_of(panel * 16 + 8 * q, 8)
                out_ref[pl.ds(first, 8), :] = jnp.where(inside, pltpu.roll(coeff[q], shift, 1), 0.0)
        return carry

    lax.fori_loop(0, place_ref.shape[1] // GROUP, body, 0)


def sample_lines_kernel(tiles, place_ref, *refs):
    out_ref, coeff = refs[-2:]
    weave([by_depth(ref) for ref in refs[:tiles]], mixing_matrix(), coeff)
    lines_kernel(place_ref, coeff, out_ref)


def place_sample_lines(places, sample):
    count = places.shape[1]
    blocks = count // BLOCK
    tile = lambda t: pl.BlockSpec((64, BLOCK), lambda i: (0, t))
    shape = (count * 16, REGION)
    return pl.pallas_call(
        functools.partial(sample_lines_kernel, blocks),
        grid=(1,),
        in_specs=[in_smem()] + [tile(t) for t in range(blocks)],
        out_specs=pl.BlockSpec(shape, lambda i: (0, 0)),
        out_shape=jax.ShapeDtypeStruct(shape, F32),
        scratch_shapes=[pltpu.VMEM((count // GROUP * 16, BLOCK), F32)],
        compiler_params=params(),
        cost_estimate=cost(16 * count * REGION, 4 * 16 * count * REGION),
        name="place_sample_lines",
    )(places, *[sample] * blocks)


def place_lines(places, coeff, awaited):
    count = places.shape[1]
    shape = (count * 16, REGION)
    return pl.pallas_call(
        lines_kernel,
        in_specs=[in_smem(), whole_vmem()] + [anywhere()] * len(awaited),
        out_specs=whole_vmem(),
        out_shape=jax.ShapeDtypeStruct(shape, F32),
        compiler_params=params(),
        cost_estimate=cost(16 * count * REGION, 4 * 16 * count * REGION),
        name="place_lines",
    )(places, coeff, *awaited)


def put_edges(opened, reach_x, reach_y, edges, first):
    half = reach_x // 2
    low = low_lanes(reach_y)
    layer = lambda i: opened[i * reach_y : (i + 1) * reach_y, :]
    for two in range(2):
        place = slice(first + two * reach_y, first + (two + 1) * reach_y)
        edges[0, place, :] = jnp.where(low, layer(2 * two), swap(layer(2 * two + 1)))
        last = half - 4 + 2 * two
        edges[1, place, :] = jnp.where(low, swap(layer(last)), layer(last + 1))


def stack_layers(layers, at, reach_y, stacked):
    tall = stacked.shape[0] // len(layers)
    place = at * up_to(reach_y, 8)
    for i, layer in enumerate(layers):
        stacked[pl.ds(pl.multiple_of(i * tall + place, 8), reach_y), :] = layer


def stack_pieces(parts, reach_x, reach_y, top, opened, stacked, edges, places):
    chip = lax.axis_index("narrow")
    for flip, (part, place) in enumerate(zip(parts, places)):
        first = from_short(part[:top, :])
        opened[...] = from_short(part[top:, :]) * unit(first[0:1], first[1:2])
        layers = [opened[i * reach_y : (i + 1) * reach_y, :] for i in range(reach_x // 2)]
        stack_layers(layers, chip ^ flip, reach_y, stacked)
        put_edges(opened, reach_x, reach_y, edges, place * 2 * reach_y)


def transform_pieces(table, stacked, before, spectrum):
    half = spectrum.shape[0]
    tall = stacked.shape[0] // half

    def tripled(values):
        high, low = split(values)
        return jnp.concatenate([high, low, high], axis=0)

    for i in range(0, half, 2):
        places = range(i, min(i + 2, half))
        held = jnp.concatenate([stacked[j * tall : (j + 1) * tall, :] for j in places], axis=1)
        result = dot(table, tripled(held))
        for j in places:
            made = result[:, (j - i) * 2 * HALF : (j - i + 1) * 2 * HALF]
            spectrum[j] = made if before is None else before[j] + made


def forward_early_kernel(reach_x, reach_y, chips, *refs):
    parts = refs[:chips]
    table_ref, spectrum, edges, opened, stacked = refs[chips:]
    top = parts[0].shape[0] - opened.shape[0]
    stacked[...] = jnp.zeros_like(stacked)
    stack_pieces(parts, reach_x, reach_y, top, opened, stacked, edges, range(chips))
    transform_pieces(table_ref[lax.axis_index("pair")], stacked, None, spectrum)


def stacking_scratch(chips, reach_x, reach_y):
    half = reach_x // 2
    return [
        pltpu.VMEM((up_to(half * reach_y, 16), 2 * HALF), F32),
        pltpu.VMEM((half * chips * up_to(reach_y, 8), 2 * HALF), F32),
    ]


def forward_early(parts, table, reach_x, reach_y):
    half = reach_x // 2
    chips = len(parts)
    return pl.pallas_call(
        functools.partial(forward_early_kernel, reach_x, reach_y, chips),
        in_specs=[whole_vmem()] * (chips + 1),
        out_specs=[whole_vmem()] * 2,
        out_shape=[
            jax.ShapeDtypeStruct((half, GRID, 2 * HALF), F32),
            jax.ShapeDtypeStruct((2, chips * 2 * reach_y, 2 * HALF), F32),
        ],
        scratch_shapes=stacking_scratch(chips, reach_x, reach_y),
        compiler_params=params(),
        cost_estimate=cost(EARLY_FLOPS, 4 * half * GRID * 2 * HALF * 2),
        name="forward_early",
    )(*parts, table)


def forward_kernel(reach_x, reach_y, blocks, pieces, awaited, *refs):
    parts = refs[:pieces]
    early_ref, early_edges, table_ref, modes_ref = refs[pieces : pieces + 4]
    refs = refs[pieces + 4 + awaited :]
    spectrum, even_out, layers_out, odd_out, own_out, peers_out, inner_out, *refs = refs
    opened, stacked, edges, slabs, head = refs
    half = reach_x // 2
    pair = lax.axis_size("pair")
    top = parts[0].shape[0] - opened.shape[0]
    stacked[...] = jnp.zeros_like(stacked)
    head[...] = jnp.zeros_like(head)
    for piece in range(pieces):
        first = from_short(parts[piece][:top, :])
        mantissa, exponent = first[2 : 2 + blocks], first[2 + blocks : 2 + 2 * blocks]
        peers_out[piece * blocks : (piece + 1) * blocks, :] = decode_rounded(mantissa, exponent)
        at = 6 + 2 * piece * blocks
        head[at : at + blocks, :] = mantissa
        head[at + blocks : at + 2 * blocks, :] = exponent
    rows = 2 * reach_y
    for chip in range(pieces // pair):
        place = chip * pair * rows
        edges[:, place : place + rows, :] = early_edges[:, chip * rows : (chip + 1) * rows, :]
    before = early_ref
    for core in range(1, pair):
        places = range(core, pieces, pair)
        stack_pieces(parts[core::pair], reach_x, reach_y, top, opened, stacked, edges, places)
        transform_pieces(table_ref[lax.axis_index("pair") ^ core], stacked, before, spectrum)
        before = spectrum

    chunk = 256

    def body(index, largest):
        rows = pl.ds(pl.multiple_of(index * chunk, chunk), chunk)
        low = low_lanes(chunk)
        decay = modes_ref[0, rows, :]
        log_decay = modes_ref[1, rows, :]
        across_half = jnp.exp(half * log_decay)
        across_cut = jnp.exp((half - 4) * log_decay)
        layers = [spectrum[i, rows, :] for i in range(half)]
        run = layers[0]
        cut_right = run
        for i in range(1, half):
            run = decay * run + layers[i]
            if i == half - 5:
                cut_right = run
        right = run
        run = layers[half - 1]
        cut_left = run
        for i in range(half - 2, -1, -1):
            run = decay * run + layers[i]
            if i == 4:
                cut_left = run
        left = run
        inner_out[rows, :] = jnp.where(low, right, left)
        swapped_right, swapped_left = swap(right), swap(left)
        own = jnp.where(low, left + across_half * swapped_left, right + across_half * swapped_right)
        own_out[rows, :] = own
        made = [
            jnp.where(low, own, cut_right + across_cut * swapped_right),
            jnp.where(low, cut_left + across_cut * swapped_left, own),
        ]
        for slab, values in enumerate(made):
            slabs[slab, rows, :] = values
        return tuple(
            jnp.maximum(old, jnp.max(jnp.abs(values).reshape(chunk // 8, 8, 2 * HALF), axis=0))
            for old, values in zip(largest, made)
        )

    zero = jnp.zeros((8, 2 * HALF), F32)
    largest = lax.fori_loop(0, GRID // chunk, body, (zero,) * 2)
    top = head.shape[0]
    low = low_lanes(GRID // 2)
    upper, lower = own_out[: GRID // 2, :], own_out[GRID // 2 :, :]
    packed = [jnp.where(low, swap(upper), lower), jnp.where(low, upper, swap(lower))]

    def send(out, first, parts):
        place = first
        for index, (values, most) in enumerate(parts):
            exponent, fraction = fit_scale(jnp.max(most, axis=0, keepdims=True))
            head[2 * index : 2 * index + 1, :] = exponent
            head[2 * index + 1 : 2 * index + 2, :] = fraction
            out[place : place + values.shape[0], :] = quantize(values, exponent, fraction)
            place += values.shape[0]
        out[:first, :] = to_short(head[:first, :])

    with_most = lambda values: (values, jnp.abs(values))
    on_left = lax.axis_index("wide") & 1
    for side, (even, odd) in enumerate(((0, 1), (1, 0))):

        @pl.when(on_left == side)
        def _():
            send(even_out, 16, [(slabs[even], largest[even]), with_most(packed[even])])
            send(layers_out, top, [with_most(edges[1 - even])])
            send(odd_out, top, [(slabs[odd], largest[odd]), with_most(edges[1 - odd])])


def forward(parts, early, early_edges, table, modes, reach_x, reach_y, blocks, awaited):
    pieces = len(parts)
    half = reach_x // 2
    lanes = 2 * HALF
    head = up_to(6 + 2 * pieces * blocks, 16)
    border = pieces * 2 * reach_y
    short = lambda rows: jax.ShapeDtypeStruct((rows, lanes), jnp.int16)
    return pl.pallas_call(
        functools.partial(
            forward_kernel, reach_x, reach_y, blocks, pieces, len(awaited)
        ),
        in_specs=[whole_vmem()] * (pieces + 4) + [anywhere()] * len(awaited),
        out_specs=[whole_vmem()] * 7,
        out_shape=[
            jax.ShapeDtypeStruct((half, GRID, lanes), F32),
            short(16 + GRID + GRID // 2),
            short(head + border),
            short(head + GRID + border),
            jax.ShapeDtypeStruct((GRID, lanes), F32),
            jax.ShapeDtypeStruct((pieces * blocks, BLOCK), F32),
            jax.ShapeDtypeStruct((GRID, lanes), F32),
        ],
        scratch_shapes=stacking_scratch(pieces // table.shape[0], reach_x, reach_y)
        + [
            pltpu.VMEM((2, border, lanes), F32),
            pltpu.VMEM((2, GRID, lanes), F32),
            pltpu.VMEM((head, lanes), F32),
        ],
        compiler_params=params(),
        cost_estimate=cost(2 * half * 256 * 256 * 128, 4 * half * GRID * lanes * 2),
        name="forward",
    )(*parts, early, early_edges, table, modes, *awaited)


def opened_part(ref, index, first, rows):
    head = from_short(ref[:16, :])
    scale = unit(head[2 * index : 2 * index + 1], head[2 * index + 1 : 2 * index + 2])
    return from_short(ref[first : first + rows, :]) * scale


def pair_kernel(reach_x, flips, own_ref, even_ref, modes_ref, *refs):
    outs, head = refs[:-1], refs[-1]
    span = reach_x - 4
    here = lax.axis_index("wide")
    low = low_lanes(GRID)
    log_decay = modes_ref[1]
    own = own_ref[...]
    top = even_ref.shape[0] - GRID - GRID // 2
    cut = opened_part(even_ref, 0, top, GRID)
    packed = opened_part(even_ref, 1, top + GRID, GRID // 2)
    from_left = jnp.where(low, cut, jnp.concatenate([swap(packed), packed], axis=0))
    from_right = jnp.where(low, jnp.concatenate([packed, swap(packed)], axis=0), cut)
    partner = jnp.where((here & 1) == 1, from_left, from_right)

    def weight(distances):
        powers = []
        for distance in distances:
            ahead = span * distance - reach_x
            powers.append(jnp.where(distance >= 2, ahead, ahead + GRID).astype(F32))
        return jnp.exp(jnp.where(low, *powers) * log_decay)

    head[...] = jnp.zeros_like(head)
    for flip, out in zip(flips, outs):
        behind = (here ^ flip) - here
        message = own * weight((-behind, behind))
        behind = (here ^ flip) - (here ^ 1)
        beside = jnp.where(jnp.abs(behind) == 1, 0.0, 1.0)
        send_piece(out, head, message + partner * (weight((-behind, behind)) * beside))


def pair_messages(own, from_even, modes, reach_x, flips):
    return pl.pallas_call(
        functools.partial(pair_kernel, reach_x, flips),
        in_specs=[whole_vmem()] * 3,
        out_specs=[whole_vmem()] * len(flips),
        out_shape=[jax.ShapeDtypeStruct((16 + GRID, 2 * HALF), jnp.int16)] * len(flips),
        scratch_shapes=[pltpu.VMEM((16, 2 * HALF), F32)],
        compiler_params=params(),
        cost_estimate=cost(16 * GRID * 2 * HALF, 4 * GRID * 2 * HALF * (6 + len(flips))),
        name="pair_messages",
    )(own, from_even, modes)


def borders_kernel(reach_y, pieces, layers_ref, odd_ref, table_ref, out_ref, stacked, partial):
    on_left = (lax.axis_index("wide") & 1) == 1
    pair = lax.axis_size("pair")
    rows = pieces * 2 * reach_y
    even = opened_part(layers_ref, 0, layers_ref.shape[0] - rows, rows)
    odd = opened_part(odd_ref, 1, odd_ref.shape[0] - rows, rows)
    left, right = jnp.where(on_left, even, odd), jnp.where(on_left, odd, even)
    low = low_lanes(rows)
    both = [jnp.where(low, left, swap(right)), jnp.where(low, swap(left), right)]
    core = lax.axis_index("pair")
    chip = lax.axis_index("narrow")
    stacked[...] = jnp.zeros_like(stacked)
    before = None
    for other in range(pair):
        for flip in range(pieces // pair):
            first = (flip * pair + other) * 2 * reach_y
            layers = [
                values[first + two * reach_y : first + (two + 1) * reach_y]
                for two in range(2)
                for values in both
            ]
            stack_layers(layers, chip ^ flip, reach_y, stacked)
        target = out_ref if other == pair - 1 else partial
        transform_pieces(table_ref[core ^ other], stacked, before, target)
        before = target


def borders(layers, from_odd, table, reach_y, pieces):
    chips = pieces // table.shape[0]
    shape = (4, GRID, 2 * HALF)
    return pl.pallas_call(
        functools.partial(borders_kernel, reach_y, pieces),
        in_specs=[whole_vmem()] * 3,
        out_specs=whole_vmem(),
        out_shape=jax.ShapeDtypeStruct(shape, F32),
        scratch_shapes=[
            pltpu.VMEM((4 * chips * up_to(reach_y, 8), 2 * HALF), F32),
            pltpu.VMEM(shape, F32),
        ],
        compiler_params=params(),
        cost_estimate=cost(2 * 4 * 256 * 256 * 128, 4 * 6 * GRID * 2 * HALF),
        name="borders",
    )(layers, from_odd, table)


def send_fields(outs, flips, reach_y, field_high, field_low, high_ref, low_ref, ready, head):
    half = field_high.shape[0]
    mine = y_position()
    pitch = up_to(reach_y, 16)
    pick = lambda ref: jnp.concatenate([ref[mine ^ flip] for flip in flips], axis=0)
    table = (pick(high_ref), pick(low_ref))
    for i in range(0, half, 2):
        many = min(2, half - i)
        join = lambda ref: jnp.concatenate([ref[i + j] for j in range(many)], axis=1)
        result = dot_three(table, (join(field_high), join(field_low)))
        for j in range(many):
            for piece in range(len(flips)):
                ready[piece, (i + j) * reach_y : (i + j + 1) * reach_y, :] = result[
                    piece * pitch : piece * pitch + reach_y, j * 2 * HALF : (j + 1) * 2 * HALF
                ]
    head[...] = jnp.zeros_like(head)
    for piece, out in enumerate(outs):
        if ready.shape[1] > half * reach_y:
            ready[piece, half * reach_y :, :] = jnp.zeros_like(ready[piece, half * reach_y :, :])
        send_piece(out, head, ready[piece])


def inverse_kernel(reach_x, reach_y, flips, fars, *refs):
    spectrum, border_ref, from_even, from_odd, own_ref, inner_ref, *far_refs = refs[: 6 + fars]
    refs = refs[6 + fars :]
    high_ref, low_ref, modes_ref = refs[:3]
    outs = refs[3 : 3 + len(flips)]
    field_high, field_low, ready, head = refs[3 + len(flips) :]
    half = reach_x // 2
    span = reach_x - 4
    chunk = 256
    border_rows = lax.axis_size("narrow") * lax.axis_size("pair") * 2 * reach_y
    tops = from_even.shape[0] - GRID - GRID // 2, from_odd.shape[0] - GRID - border_rows
    on_left = (lax.axis_index("wide") & 1) == 1
    moment_units = []
    for ref in (from_even, from_odd):
        first = from_short(ref[:16, :])
        moment_units.append(unit(first[0:1], first[1:2]))

    far_units = []
    for ref in far_refs:
        first = from_short(ref[:16, :])
        far_units.append(unit(first[0:1], first[1:2]))

    def body(index, carry):
        first = pl.multiple_of(index * chunk, chunk)
        rows = pl.ds(first, chunk)
        low = low_lanes(chunk)
        decay = modes_ref[0, rows, :]
        log_decay = modes_ref[1, rows, :]
        ring = modes_ref[2, rows, :]
        gain = modes_ref[3, rows, :]
        across_half = jnp.exp(half * log_decay)
        across_cut = jnp.exp((half - 4) * log_decay)
        around = jnp.exp((GRID - 4) * log_decay)
        beside = jnp.exp((GRID - reach_x - span) * log_decay)
        layers = [spectrum[i, rows, :] for i in range(half)]

        even, odd = (
            from_short(ref[pl.ds(pl.multiple_of(top + index * chunk, 16), chunk), :]) * scale
            for ref, top, scale in zip((from_even, from_odd), tops, moment_units)
        )
        left_moments, right_moments = jnp.where(on_left, even, odd), jnp.where(on_left, odd, even)
        border = [border_ref[i, rows, :] for i in range(4)]
        zero = jnp.zeros_like(decay)
        head_sum = border[0]
        for i in range(1, 4):
            head_sum = decay * head_sum + border[i]
        tail_sum = border[3]
        for i in range(2, -1, -1):
            tail_sum = decay * tail_sum + border[i]
        for i in range(4):
            layers[i] = layers[i] + jnp.where(low, border[i], zero)
        for i in range(4):
            place = half - 4 + i
            layers[place] = layers[place] + jnp.where(low, zero, border[i])
        total = own_ref[rows, :] * jnp.exp((GRID - reach_x) * log_decay)
        at = pl.ds(pl.multiple_of(16 + index * chunk, 16), chunk)
        for ref, scale in zip(far_refs, far_units):
            total = total + from_short(ref[at, :]) * scale
        one = jnp.ones_like(decay)
        total = total + left_moments * jnp.where(low, beside, one)
        total = total + right_moments * jnp.where(low, one, beside)
        shared = jnp.where(low, head_sum, tail_sum)
        entering = (swap(total) + around * shared) * ring
        leaving = swap(across_half * entering + across_cut * shared + inner_ref[rows, :])
        run = jnp.where(low, entering, leaving)
        forward_runs = []
        for i in range(half):
            run = decay * run + layers[i]
            forward_runs.append(run)
        run = jnp.where(low, leaving, entering)
        for i in range(half - 1, -1, -1):
            ahead = decay * run
            high, rest = split(gain * (forward_runs[i] + ahead))
            field_high[i, rows, :] = high
            field_low[i, rows, :] = rest
            run = ahead + layers[i]
        return carry

    lax.fori_loop(0, GRID // chunk, body, 0)
    send_fields(outs, flips, reach_y, field_high, field_low, high_ref, low_ref, ready, head)


def inverse(
    spectrum, border, from_even, from_odd, own, inner, fars, table, modes, reach_x, reach_y, flips
):
    half = reach_x // 2
    lanes = 2 * HALF
    body = up_to(half * reach_y, 16)
    shapes = [jax.ShapeDtypeStruct((16 + body, lanes), jnp.int16)] * len(flips)
    shapes += [jax.ShapeDtypeStruct((half, GRID, lanes), BF16)] * 2
    return pl.pallas_call(
        functools.partial(inverse_kernel, reach_x, reach_y, flips, len(fars)),
        in_specs=[whole_vmem()] * (9 + len(fars)),
        out_specs=[whole_vmem()] * len(shapes),
        out_shape=shapes,
        scratch_shapes=[
            pltpu.VMEM((len(flips), body, lanes), F32),
            pltpu.VMEM((16, lanes), F32),
        ],
        compiler_params=params(),
        cost_estimate=cost(2 * half * 256 * 256 * 128, 4 * half * GRID * lanes * 2),
        name="inverse",
    )(spectrum, border, from_even, from_odd, own, inner, *fars, *table, modes)


def inverse_rest_kernel(reach_y, flips, field_high, field_low, high_ref, low_ref, *refs):
    outs, (ready, head) = refs[: len(flips)], refs[len(flips) :]
    send_fields(outs, flips, reach_y, field_high, field_low, high_ref, low_ref, ready, head)


def inverse_rest(field, table, reach_y, flips):
    half = field[0].shape[0]
    lanes = 2 * HALF
    body = up_to(half * reach_y, 16)
    return pl.pallas_call(
        functools.partial(inverse_rest_kernel, reach_y, flips),
        in_specs=[whole_vmem()] * 4,
        out_specs=[whole_vmem()] * len(flips),
        out_shape=[jax.ShapeDtypeStruct((16 + body, lanes), jnp.int16)] * len(flips),
        scratch_shapes=[
            pltpu.VMEM((len(flips), body, lanes), F32),
            pltpu.VMEM((16, lanes), F32),
        ],
        compiler_params=params(),
        cost_estimate=cost(2 * half * 256 * 256 * 128, 4 * half * GRID * lanes * 2),
        name="inverse_rest",
    )(*field, *table)


def sum_rows(values):
    row = lax.broadcasted_iota(jnp.int32, values[0].shape, 0)
    for step in (4, 2, 1):
        low = (row & step) == 0
        paired = []
        for one, other in zip(values[: len(values) // 2], values[len(values) // 2 :]):
            kept = jnp.where(low, one, other)
            moved = jnp.where(low, other, one)
            if step == 4:
                moved = pltpu.roll(moved, 4, 0)
            else:
                moved = jnp.where(low, pltpu.roll(moved, 8 - step, 0), pltpu.roll(moved, step, 0))
            paired.append(kept + moved)
        values = paired
    return values[0]


def z_lines(parts, flips, high_ref, low_ref):
    mine = y_position()
    opened = []
    for part in parts:
        first = from_short(part[:16, :])
        opened.append(from_short(part[16:, :]) * unit(first[0:1], first[1:2]))
    values = split(jnp.concatenate(opened, axis=1))
    pick = lambda ref: jnp.concatenate([ref[mine ^ flip] for flip in flips], axis=0)
    return dot_three(values, (pick(high_ref), pick(low_ref)))


def sample_early_kernel(flips, *refs):
    *parts, high_ref, low_ref, out_ref = refs
    out_ref[...] = z_lines(parts, flips, high_ref, low_ref)


def sample_early(parts, flips, table):
    rows = parts[0].shape[0] - 16
    return pl.pallas_call(
        functools.partial(sample_early_kernel, flips),
        in_specs=[whole_vmem()] * (len(parts) + 2),
        out_specs=whole_vmem(),
        out_shape=jax.ShapeDtypeStruct((rows, 2 * REGION), F32),
        compiler_params=params(),
        cost_estimate=cost(EARLY_FLOPS, 4 * rows * 512),
        name="sample_early",
    )(*parts, *table)


def sample_kernel(last, reach_x, reach_y, flips, place_in, *refs):
    parts = refs[: len(flips)]
    early_ref, high_ref, low_ref, line_ref, own_ref, vector_ref, near_ref, out_ref = refs[
        len(flips) : len(flips) + 8
    ]
    flat, field, sums, place_ref, sem = refs[len(flips) + 8 :]
    copy = pltpu.make_async_copy(place_in, place_ref, sem)
    copy.start()
    half_rows = reach_x * reach_y // 2
    both = early_ref[...] + z_lines(parts, flips, high_ref, low_ref)
    flat[:half_rows, :] = both[:half_rows, :REGION]
    flat[half_rows:, :] = both[:half_rows, REGION:]
    for x in range(reach_x):
        layer = flat[x * reach_y : (x + 1) * reach_y, :]
        for row in pair_rows(x, reach_x, reach_y):
            field[pl.ds(row, reach_y, stride=2), :] = layer
    count = place_ref.shape[1]

    def body(group, carry):
        for eight in range(0, GROUP, 8):
            totals = []
            for local in range(eight, eight + 8):
                panel = group * GROUP + local
                row = place_ref[0, panel]
                first = pl.multiple_of(panel * 16, 16)
                totals.append(
                    field[pl.ds(row, 8), :] * line_ref[pl.ds(first, 8), :]
                    + field[pl.ds(row + 2 * reach_y, 8), :] * line_ref[pl.ds(first + 8, 8), :]
                )
            sums[pl.ds(pl.multiple_of(group * GROUP + eight, 8), 8), :] = sum_rows(totals)
        return carry

    copy.wait()
    lax.fori_loop(0, count // GROUP, body, 0)
    first, rest = split(sums[...])
    second, third = split(sums[...] - first.astype(F32))
    across = lambda values: lax.dot_general(
        jnp.ones((16, REGION), BF16),
        values,
        (((1,), (1,)), ((), ())),
        preferred_element_type=F32,
    )
    sampled = across(first) + (across(second) + across(third))
    for block in range(count // BLOCK):
        lane = slice(block * BLOCK, (block + 1) * BLOCK)
        row = slice(block, block + 1)
        vector = vector_ref[row, :]
        image = jnp.where(own_ref[row, :] == 1, 0.0, 0.5 * vector) + sampled[:1, lane]
        image = image + near_ref[row, :]
        if last:
            out_ref[0:1, lane] = vector
            out_ref[1:2, lane] = image
        else:
            out_ref[row, :] = image


def sample(last, places, parts, flips, early, table, lines, flag, vector, near, reach_x, reach_y):
    count = places.shape[1]
    blocks = count // BLOCK
    shape = (2, count) if last else (blocks, BLOCK)
    return pl.pallas_call(
        functools.partial(sample_kernel, last, reach_x, reach_y, flips),
        in_specs=[anywhere()] + [whole_vmem()] * (len(parts) + 7),
        out_specs=whole_vmem(),
        out_shape=jax.ShapeDtypeStruct(shape, F32),
        scratch_shapes=[
            pltpu.VMEM((reach_x * reach_y, REGION), F32),
            pltpu.VMEM((pair_count(reach_x, reach_y), REGION), F32),
            pltpu.VMEM((count, REGION), F32),
            pltpu.SMEM((2, count), jnp.int32),
            pltpu.SemaphoreType.DMA,
        ],
        compiler_params=params(),
        cost_estimate=cost(reach_x * reach_y * 256 * 512, 4 * 16 * count * REGION),
        name="sample",
    )(
        places,
        *parts,
        early,
        *table,
        lines,
        flag.reshape(blocks, BLOCK),
        vector.reshape(blocks, BLOCK),
        near,
    )


def near_kernel(slots, blocks, place_ref, target_ref, *refs):
    even_ref, odd_ref, peers_ref, tile_ref = refs[:4]
    out_ref, held = refs[-2:]
    count = peers_ref.shape[0]
    held[count : 2 * count, :] = peers_ref[...]
    on_left = lax.axis_index("wide") & 1
    for side, ref in ((1 - on_left, even_ref), (on_left, odd_ref)):
        top = from_short(ref[...])
        for piece in range(count // blocks):
            at = 6 + 2 * piece * blocks
            held[pl.ds(side * (2 * count) + piece * blocks, blocks), :] = decode_rounded(
                top[at : at + blocks], top[at + blocks : at + 2 * blocks]
            )
    out_ref[...] = jnp.zeros_like(out_ref)
    for slot in range(slots):
        picked = held[pl.ds(place_ref[slot], 1), :]
        picked = jnp.broadcast_to(picked, (16, BLOCK)).astype(BF16)
        product = lax.dot_general(
            picked,
            tile_ref[slot],
            (((1,), (1,)), ((), ())),
            preferred_element_type=F32,
        )
        target = pl.ds(target_ref[slot], 1)
        out_ref[target, :] = out_ref[target, :] + product[:1]


def near_field(places, targets, from_even, from_odd, peers, tiles, blocks, out_rows, awaited):
    slots = tiles.shape[0]
    head = up_to(6 + 2 * peers.shape[0], 16)
    constant = lambda shape: pl.BlockSpec(shape, lambda i: (0,) * len(shape))
    return pl.pallas_call(
        functools.partial(near_kernel, slots, blocks),
        grid=(1,),
        in_specs=[
            in_smem(),
            in_smem(),
            constant((head, BLOCK)),
            constant((head, BLOCK)),
            constant(peers.shape),
            constant(tiles.shape),
        ]
        + [anywhere()] * len(awaited),
        out_specs=constant((out_rows, BLOCK)),
        out_shape=jax.ShapeDtypeStruct((out_rows, BLOCK), F32),
        scratch_shapes=[pltpu.VMEM((3 * peers.shape[0], BLOCK), F32)],
        compiler_params=params(),
        cost_estimate=cost(2 * slots * 16 * BLOCK * BLOCK, 2 * slots * BLOCK * BLOCK),
        name="near_field",
    )(places, targets, from_even, from_odd, peers, tiles, *awaited)


def shards(
    density,
    surface_flag,
    stencil_base,
    sample_weights,
    dipole_weights,
    near_target,
    near_source,
    near_tiles,
):
    x_count = lax.axis_size("wide")
    y_count = lax.axis_size(Y_AXES)
    y_index = lax.axis_index(Y_AXES)
    pair = lax.axis_size("pair")
    span_x = REGION // x_count
    span_y = REGION // y_count
    reach_x = span_x + 4
    reach_y = span_y + 4
    count = density.shape[0]
    blocks = count // BLOCK

    z_forward, z_inverse, y_forward, y_inverse, modes = tables(y_count, pair, span_y)
    modes = lax.dynamic_index_in_dim(jnp.asarray(modes), y_index, 0, keepdims=False)

    neighbour = near_source // blocks
    flip = (y_index + neighbour % 3 - 1) ^ y_index
    sources = ((neighbour // 3) * y_count + flip) * blocks + near_source % blocks
    out_rows = up_to(blocks + 1, 8)
    live = near_target >= 0
    sources = jnp.where(live, sources, 0)
    targets = jnp.where(live, near_target, out_rows - 1)

    swaps = lambda pairs: [(i, j) for i, j in pairs] + [(j, i) for i, j in pairs]
    even_swap = swaps([(i, i + 1) for i in range(0, x_count - 1, 2)])
    odd_swap = swaps([(i, i + 1) for i in range(1, x_count - 1, 2)])
    far_flips = list(range(2, x_count, 2))

    first, rest = list(range(pair, y_count)), list(range(pair))
    same_core = list(range(0, y_count, pair))
    other_core = [flip for flip in range(y_count) if flip not in same_core]

    def turned(sent, then):
        arrived = [None] * y_count
        for flip, part in zip(first + rest, list(sent) + list(then)):
            swap_pairs = [(i, i ^ flip) for i in range(y_count)]
            arrived[flip] = part if flip == 0 else lax.ppermute(part, Y_AXES, swap_pairs)
        return arrived

    def chosen(parts, flips):
        return [parts[flip] for flip in flips]

    def convolve_and_sample(last, vector, sent, both, table, places, sample_lines, awaited):
        arrived = turned(sent, spread_rest(vector, both, table, rest))
        early, edges = forward_early(chosen(arrived, same_core), y_forward, reach_x, reach_y)
        spectrum, even_message, layers, odd_message, own, peers, inner = forward(
            arrived, early, edges, y_forward, modes, reach_x, reach_y, blocks, awaited
        )
        from_even = lax.ppermute(even_message, "wide", even_swap)
        from_odd = lax.ppermute(odd_message, "wide", odd_swap)
        even_layers = lax.ppermute(layers, "wide", even_swap)
        fars = [
            lax.ppermute(message, "wide", [(i, i ^ flip) for i in range(x_count)])
            for flip, message in zip(
                far_flips, pair_messages(own, from_even, modes, reach_x, far_flips)
            )
        ]
        *sent, high, low = inverse(
            spectrum,
            borders(even_layers, from_odd, y_forward, reach_y, y_count),
            from_even,
            from_odd,
            own,
            inner,
            fars,
            y_inverse,
            modes,
            reach_x,
            reach_y,
            first,
        )
        then = inverse_rest((high, low), y_inverse, reach_y, rest)
        near_part = near_field(
            sources, targets, even_layers, from_odd, peers, near_tiles, blocks, out_rows, then[:1]
        )
        arrived = turned(sent, then)
        image = sample(
            last,
            places,
            chosen(arrived, other_core),
            other_core,
            sample_early(chosen(arrived, same_core), same_core, z_inverse),
            z_inverse,
            sample_lines,
            surface_flag,
            vector,
            near_part,
            reach_x,
            reach_y,
        )
        return image, near_part

    raw = (stencil_base, surface_flag, sample_weights, dipole_weights)
    *sent, wide_high, wide_low, source_coeff, places, vector, high, low = spread(
        density, z_forward, None, raw, reach_x, reach_y, first
    )
    z_forward = (high, low)
    sample_lines = place_sample_lines(places, sample_weights)
    vector, near_part = convolve_and_sample(
        False,
        vector,
        sent,
        (wide_high, wide_low),
        z_forward,
        places,
        sample_lines,
        [sample_lines],
    )
    source_lines = place_lines(places, source_coeff, [near_part])
    *sent, wide_high, wide_low = spread(
        vector.reshape(-1), z_forward, (places, source_lines), None, reach_x, reach_y, first
    )
    both_images, _ = convolve_and_sample(
        True, vector, sent, (wide_high, wide_low), z_forward, places, sample_lines, []
    )
    return both_images


def solution(mesh):
    panels = P(("groups",) + ALL_AXES)
    columns = P(None, ("groups",) + ALL_AXES)
    in_specs = (
        panels,
        panels,
        columns,
        columns,
        columns,
        panels,
        panels,
        P(("groups",) + ALL_AXES, None, None),
    )
    return jax.shard_map(
        shards, mesh=mesh, in_specs=in_specs, out_specs=columns, check_vma=False
    )
```

```python
import functools
import math

import jax
import jax.numpy as jnp
import numpy as np
from jax import lax
from jax.experimental import pallas as pl
from jax.experimental.pallas import tpu as pltpu
from jax.sharding import PartitionSpec as P

GRID = 256
REGION = 128
BLOCK = 128
HALF = 64
KERNEL_GAIN = 4.0
SCREEN = 1.0 / 1024.0
LN2 = math.log(2.0)
Y_AXES = ("narrow", "pair")
ALL_AXES = ("wide", "narrow", "pair")
F32 = jnp.float32
BF16 = jnp.bfloat16
VMEM_LIMIT = 24 * 1024 * 1024
START_LIMIT = VMEM_LIMIT
EARLY_FLOPS = 5 * 10**9
GROUP = 32
CHAINS = 2


def cas(angles):
    return np.cos(angles) + np.sin(angles)


def up_to(count, multiple):
    return -(-count // multiple) * multiple


def low_lanes(rows):
    return lax.broadcasted_iota(jnp.int32, (rows, 2 * HALF), 1) < HALF


def swap(values):
    return pltpu.roll(values, HALF, 1)


def split(values):
    high = values.astype(BF16)
    return high, (values - high.astype(F32)).astype(BF16)


def dot(left, right):
    return jnp.dot(left, right, preferred_element_type=F32)


def dot_three(left, right):
    return dot(left[0], right[0]) + (dot(left[0], right[1]) + dot(left[1], right[0]))


def params():
    return pltpu.CompilerParams(vmem_limit_bytes=VMEM_LIMIT)


def whole_vmem():
    return pl.BlockSpec(memory_space=pltpu.VMEM)


def anywhere():
    return pl.BlockSpec(memory_space=pl.ANY)


def in_smem():
    return pl.BlockSpec(memory_space=pltpu.SMEM)


def cost(flops, moved):
    return pl.CostEstimate(flops=flops, bytes_accessed=moved, transcendentals=0)


def full_scale(exponent, fraction):
    return fraction * jnp.exp(exponent * LN2) * (1.0 / 1024.0)


def fit_scale(largest):
    largest = jnp.maximum(largest, 1e-30)
    exponent = jnp.floor(jnp.log(largest) * (1.0 / LN2))
    fraction = jnp.ceil(largest * jnp.exp(-exponent * LN2) * 1024.0) + 1.0
    return exponent, fraction


def to_short(values):
    return values.astype(jnp.int32).astype(jnp.int16)


def from_short(values):
    return values.astype(jnp.int32).astype(F32)


def quantize(values, exponent, fraction):
    return to_short(jnp.round(values * (32767.0 / full_scale(exponent, fraction))))


def unit(exponent, fraction):
    return full_scale(exponent, fraction) * (1.0 / 32767.0)


def encode_rounded(values):
    rounded = values.astype(BF16).astype(F32)
    size = jnp.maximum(jnp.abs(rounded), 1e-30)
    exponent = jnp.floor(jnp.log(size) * (1.0 / LN2))
    return jnp.round(rounded * jnp.exp((10.0 - exponent) * LN2)), exponent


def decode_rounded(mantissa, exponent):
    return (mantissa * jnp.exp((exponent - 10.0) * LN2)).astype(BF16).astype(F32)


def send_piece(out, head, values):
    exponent, fraction = fit_scale(jnp.max(jnp.abs(values), axis=0, keepdims=True))
    head[0:1, :] = exponent
    head[1:2, :] = fraction
    top = head.shape[0]
    out[:top, :] = to_short(head[...])
    out[top:, :] = quantize(values, exponent, fraction)


def y_position():
    return lax.axis_index("narrow") * lax.axis_size("pair") + lax.axis_index("pair")


def halves(table):
    high = table.astype(jnp.bfloat16)
    return high, (table - high.astype(np.float64)).astype(jnp.bfloat16)


def tables(y_count, pair, span_y):
    depth = GRID // y_count
    reach = span_y + 4
    waves = np.arange(GRID)
    step = 2.0 * np.pi / GRID
    z_table = cas(step * np.outer(np.arange(REGION), waves))
    z_forward = np.zeros((y_count, 2 * REGION, 2 * HALF))
    z_inverse = np.zeros((y_count, 2 * HALF, 2 * REGION))
    symbols = 4.0 * np.sin(np.pi * waves / GRID) ** 2
    shift = np.full((y_count, GRID, 2 * HALF), 1.0)
    y_forward = np.zeros((GRID, y_count, up_to(reach, 8)))
    y_inverse = np.zeros((y_count, up_to(reach, 16), GRID))
    for block in range(y_count):
        mine = z_table[:, block * depth : (block + 1) * depth]
        for half in range(2):
            rows = slice(half * REGION, (half + 1) * REGION)
            lanes = slice(half * HALF, half * HALF + depth)
            z_forward[block, rows, lanes] = mine
            z_inverse[block, lanes, rows] = mine.T / GRID
            shift[block, :, lanes] = (
                SCREEN + symbols[:, None] + symbols[None, block * depth : (block + 1) * depth]
            )
        cells = block * span_y - 2 + np.arange(reach)
        y_table = cas(step * np.outer(waves, cells))
        y_forward[:, block, :reach] = y_table
        y_inverse[block, :reach] = y_table.T / GRID
    y_forward = y_forward.reshape(GRID, y_count // pair, pair, -1).transpose(2, 0, 1, 3)
    y_forward = halves(y_forward.reshape(pair, GRID, -1))
    y_forward = np.concatenate([y_forward[0], y_forward[0], y_forward[1]], axis=2)
    root = np.sqrt(shift * (shift + 4.0))
    decay = 2.0 / (2.0 + shift + root)
    log_decay = np.log(decay)
    ring = 1.0 / (1.0 - np.exp(GRID * log_decay))
    gain = KERNEL_GAIN / root
    modes = np.stack([decay, log_decay, ring, gain], axis=1).astype(np.float32)
    return (
        halves(z_forward),
        halves(z_inverse),
        y_forward,
        halves(y_inverse),
        modes,
    )


def mixing_matrix():
    place = lax.broadcasted_iota(jnp.int32, (4 * BLOCK, 4 * BLOCK), 0)
    lane = lax.broadcasted_iota(jnp.int32, (4 * BLOCK, 4 * BLOCK), 1)
    return jnp.where(lane == 4 * (place % BLOCK) + place // BLOCK, 1.0, 0.0).astype(BF16)


def weave(tiles, mixing, out):
    weights = jnp.concatenate([jnp.concatenate(tile, axis=1) for tile in tiles], axis=0)
    first, rest = split(weights)
    second, third = split(weights - first.astype(F32))
    woven = dot(first, mixing) + (dot(second, mixing) + dot(third, mixing))
    for tile in range(len(tiles)):
        for part in range(BLOCK // GROUP):
            at = (tile * (BLOCK // GROUP) + part) * 16
            lanes = slice(part * BLOCK, (part + 1) * BLOCK)
            for a in range(4):
                row = tile * 16 + 4 * a
                out[pl.ds(at + 8 * (a // 2) + a % 2, 4, stride=2), :] = woven[row : row + 4, lanes]


def by_depth(ref):
    return [ref[pl.ds(depth, 16, stride=4), :] for depth in range(4)]


def pair_rows(x, reach_x, reach_y):
    even = (x // 2) * 2 * reach_y + x % 2
    if x == 0 or x == reach_x - 1:
        return [even]
    return [even, reach_x * reach_y + ((x - 1) // 2) * 2 * reach_y + (x - 1) % 2]


def pair_count(reach_x, reach_y):
    return (2 * reach_x - 2) * reach_y


def in_window(lanes, depth):
    return ((lanes - depth) & -4) == 0


def add_panels(reach, woven, vector_ref, place_ref, weight_ref, grids):
    lanes = lax.broadcasted_iota(jnp.int32, (8, REGION), 1)

    def body(group, carry):
        at = pl.multiple_of(group * 16, 16)
        coeff = [weight_ref[pl.ds(at + 8 * q, 8), :] for q in range(2)] if woven else None
        for local in range(GROUP):
            panel = group * GROUP + local
            grid = grids[local % len(grids)]
            row = place_ref[0, panel]
            value = vector_ref[panel]
            if woven:
                depth = place_ref[1, panel]
                shift = (depth - 4 * local) & (REGION - 1)
                value = jnp.where(in_window(lanes, depth), value, 0.0)
                lines = [pltpu.roll(coeff[q], shift, 1) for q in range(2)]
            else:
                first = pl.multiple_of(panel * 16, 16)
                lines = [weight_ref[pl.ds(first + 8 * q, 8), :] for q in range(2)]
            places = [pl.ds(row, 8), pl.ds(row + 2 * reach, 8)]
            held = [grid[place, :] for place in places]
            for q in range(2):
                grid[places[q], :] = held[q] + lines[q] * value
        return carry

    lax.fori_loop(0, vector_ref.shape[0] // GROUP, body, 0)


def send_pieces(outs, flips, head, rounded, both, high_ref, low_ref):
    blocks = rounded.shape[0]
    mantissa, exponent = encode_rounded(rounded)
    head[...] = jnp.zeros_like(head)
    head[2 : 2 + blocks, :] = mantissa
    head[2 + blocks : 2 + 2 * blocks, :] = exponent
    mine = y_position()
    for at in range(0, len(flips), 2):
        pick = lambda ref: jnp.concatenate([ref[mine ^ flip] for flip in flips[at : at + 2]], axis=1)
        result = dot_three(both, (pick(high_ref), pick(low_ref)))
        for i, out in enumerate(outs[at : at + 2]):
            send_piece(out, head, result[:, i * 2 * HALF : (i + 1) * 2 * HALF])


def spread_grid(reach_x, reach_y, rounded, tables, outs, flips, wides, head, total, grids):
    for x in range(reach_x):
        parts = [
            grid[pl.ds(row, reach_y, stride=2), :]
            for row in pair_rows(x, reach_x, reach_y)
            for grid in grids
        ]
        total[x * reach_y : (x + 1) * reach_y, :] = sum(parts[1:], parts[0])
    half = reach_x * reach_y // 2
    both = jnp.concatenate([total[:half, :], total[half:, :]], axis=1)
    extra = wides[0].shape[0] - half
    if extra:
        both = jnp.concatenate([both, jnp.zeros((extra, 2 * REGION), F32)], axis=0)
    both = split(both)
    for wide, values in zip(wides, both):
        wide[...] = values
    send_pieces(outs, flips, head, rounded, both, *tables)


def start_kernel(reach_x, reach_y, flips, *refs):
    vector_in, *remote = refs[:8]
    refs = refs[8:]
    outs, refs = refs[: len(flips)], refs[len(flips) :]
    wides, (weight_ref, places_out), refs = refs[:2], refs[2:4], refs[4:]
    rounded, high, low, stencil, flag, samples, dipoles, vector_ref = refs[:8]
    place_ref, sems, head, total = refs[8:12]
    grids = refs[12:]
    tiles = samples.shape[0]
    copies = []
    fetch = lambda source, target: copies.append(
        pltpu.make_async_copy(source, target, sems.at[len(copies)])
    )
    rounded_in, high_in, low_in, stencil_in, flag_in, sample_in, dipole_in = remote
    fetch(stencil_in, stencil)
    fetch(flag_in, flag)
    fetch(vector_in, vector_ref)
    for tile in range(tiles):
        lanes = pl.ds(tile * BLOCK, BLOCK)
        fetch(sample_in.at[:, lanes], samples.at[tile])
        fetch(dipole_in.at[:, lanes], dipoles.at[tile])
    needed_first = len(copies)
    fetch(rounded_in, rounded)
    fetch(high_in, high)
    fetch(low_in, low)
    for copy in copies:
        copy.start()
    for grid in grids:
        grid[...] = jnp.zeros_like(grid)
    mixing = mixing_matrix()
    copies[0].wait()
    span_x, span_y = reach_x - 4, reach_y - 4
    local_x = stencil[0:1, :] - (lax.axis_index("wide") * span_x - 2)
    local_y = stencil[1:2, :] - (y_position() * span_y - 2)
    odd = local_x & 1
    places_out[0:1, :] = odd * (reach_x * reach_y) + (local_x >> 1) * (2 * reach_y) + 2 * local_y
    places_out[1:2, :] = stencil[2:3, :]
    to_scalar = pltpu.make_async_copy(places_out, place_ref, sems.at[len(copies)])
    to_scalar.start()
    for copy in copies[1:needed_first]:
        copy.wait()
    sources = []
    for tile in range(tiles):
        charged = flag[:, tile * BLOCK : (tile + 1) * BLOCK] == 1
        pairs = zip(by_depth(samples.at[tile]), by_depth(dipoles.at[tile]))
        sources.append([jnp.where(charged, -sample, dipole) for sample, dipole in pairs])
    weave(sources, mixing, weight_ref)
    to_scalar.wait()
    add_panels(reach_y, True, vector_ref, place_ref, weight_ref, grids)
    for copy in copies[needed_first:]:
        copy.wait()
    spread_grid(
        reach_x, reach_y, rounded[...], (high, low), outs, flips, wides, head, total, grids
    )


def spread_kernel(reach_x, reach_y, flips, *refs):
    vector_in, place_in, rounded_ref, high_ref, low_ref, line_ref = refs[:6]
    refs = refs[6:]
    outs, wides, (vector_ref, place_ref, sems, head, total), grids = (
        refs[: len(flips)],
        refs[len(flips) : len(flips) + 2],
        refs[len(flips) + 2 : len(flips) + 7],
        refs[len(flips) + 7 :],
    )
    copies = [
        pltpu.make_async_copy(vector_in, vector_ref, sems.at[0]),
        pltpu.make_async_copy(place_in, place_ref, sems.at[1]),
    ]
    for copy in copies:
        copy.start()
    for grid in grids:
        grid[...] = jnp.zeros_like(grid)
    for copy in copies:
        copy.wait()
    add_panels(reach_y, False, vector_ref, place_ref, line_ref, grids)
    spread_grid(
        reach_x,
        reach_y,
        rounded_ref[...],
        (high_ref, low_ref),
        outs,
        flips,
        wides,
        head,
        total,
        grids,
    )


def spread(vector, table, placed, raw, reach_x, reach_y, flips):
    count = vector.shape[0]
    half = reach_x * reach_y // 2
    blocks = count // BLOCK
    top = up_to(2 + 2 * blocks, 16)
    lanes = 2 * HALF
    body = up_to(half, 16)
    woven = (count // GROUP * 16, BLOCK)
    out_shapes = [jax.ShapeDtypeStruct((top + body, lanes), jnp.int16)] * len(flips)
    out_shapes += [jax.ShapeDtypeStruct((body, 2 * REGION), BF16)] * 2
    rounded = vector.reshape(blocks, BLOCK)
    work = [
        pltpu.VMEM((top, lanes), F32),
        pltpu.VMEM((reach_x * reach_y, REGION), F32),
    ] + [pltpu.VMEM((pair_count(reach_x, reach_y), REGION), F32)] * CHAINS
    if placed is None:
        stencil, flag, sample, dipole = raw
        operands = [vector, rounded, *table, stencil, flag.reshape(1, -1), sample, dipole]
        operands = [pltpu.with_memory_space_constraint(value, pltpu.HBM) for value in operands]
        in_specs = [pl.BlockSpec(memory_space=pltpu.HBM)] * 8
        out_shapes += [jax.ShapeDtypeStruct(woven, F32)]
        out_shapes += [jax.ShapeDtypeStruct((2, count), jnp.int32)]
        out_shapes += [jax.ShapeDtypeStruct(rounded.shape, F32)]
        out_shapes += [jax.ShapeDtypeStruct(values.shape, BF16) for values in table]
        tiled = pltpu.VMEM((blocks, 64, BLOCK), F32)
        work = [
            pltpu.VMEM(stencil.shape, jnp.int32),
            pltpu.VMEM((1, count), jnp.int32),
            tiled,
            tiled,
            pltpu.SMEM((count,), F32),
            pltpu.SMEM((2, count), jnp.int32),
            pltpu.SemaphoreType.DMA((7 + 2 * blocks,)),
        ] + work
    else:
        operands = [vector, placed[0], rounded, *table, placed[1]]
        in_specs = [anywhere()] * 2 + [whole_vmem()] * 4
        work = [
            pltpu.SMEM((count,), F32),
            pltpu.SMEM((2, count), jnp.int32),
            pltpu.SemaphoreType.DMA((2,)),
        ] + work
    return pl.pallas_call(
        functools.partial(
            start_kernel if placed is None else spread_kernel, reach_x, reach_y, flips
        ),
        in_specs=in_specs,
        out_specs=[whole_vmem()] * len(out_shapes),
        out_shape=out_shapes,
        scratch_shapes=work,
        compiler_params=pltpu.CompilerParams(
            vmem_limit_bytes=START_LIMIT if placed is None else VMEM_LIMIT
        ),
        cost_estimate=cost(2 * half * 256 * 512, 4 * 16 * count * REGION),
        name="start" if placed is None else "spread",
    )(*operands)


def spread_rest_kernel(flips, rounded_ref, wide_high, wide_low, high_ref, low_ref, *refs):
    outs, head = refs[:-1], refs[-1]
    both = (wide_high[...], wide_low[...])
    send_pieces(outs, flips, head, rounded_ref[...], both, high_ref, low_ref)


def spread_rest(rounded, both, table, flips):
    blocks = rounded.shape[0]
    top = up_to(2 + 2 * blocks, 16)
    shape = (top + both[0].shape[0], 2 * HALF)
    return pl.pallas_call(
        functools.partial(spread_rest_kernel, flips),
        in_specs=[whole_vmem()] * 5,
        out_specs=[whole_vmem()] * len(flips),
        out_shape=[jax.ShapeDtypeStruct(shape, jnp.int16)] * len(flips),
        scratch_shapes=[pltpu.VMEM((top, 2 * HALF), F32)],
        compiler_params=params(),
        cost_estimate=cost(2 * shape[0] * 256 * 256 * 3, 4 * shape[0] * 512),
        name="spread_rest",
    )(rounded, *both, *table)


def lines_kernel(place_ref, coeff_ref, *refs):
    out_ref = refs[-1]
    lanes = lax.broadcasted_iota(jnp.int32, (8, REGION), 1)

    def body(group, carry):
        at = pl.multiple_of(group * 16, 16)
        coeff = [coeff_ref[pl.ds(at + 8 * q, 8), :] for q in range(2)]
        for local in range(GROUP):
            panel = group * GROUP + local
            depth = place_ref[1, panel]
            shift = (depth - 4 * local) & (REGION - 1)
            inside = in_window(lanes, depth)
            for q in range(2):
                first = pl.multiple_of(panel * 16 + 8 * q, 8)
                out_ref[pl.ds(first, 8), :] = jnp.where(inside, pltpu.roll(coeff[q], shift, 1), 0.0)
        return carry

    lax.fori_loop(0, place_ref.shape[1] // GROUP, body, 0)


def sample_lines_kernel(tiles, place_ref, *refs):
    out_ref, coeff = refs[-2:]
    weave([by_depth(ref) for ref in refs[:tiles]], mixing_matrix(), coeff)
    lines_kernel(place_ref, coeff, out_ref)


def place_sample_lines(places, sample):
    count = places.shape[1]
    blocks = count // BLOCK
    tile = lambda t: pl.BlockSpec((64, BLOCK), lambda i: (0, t))
    shape = (count * 16, REGION)
    return pl.pallas_call(
        functools.partial(sample_lines_kernel, blocks),
        grid=(1,),
        in_specs=[in_smem()] + [tile(t) for t in range(blocks)],
        out_specs=pl.BlockSpec(shape, lambda i: (0, 0)),
        out_shape=jax.ShapeDtypeStruct(shape, F32),
        scratch_shapes=[pltpu.VMEM((count // GROUP * 16, BLOCK), F32)],
        compiler_params=params(),
        cost_estimate=cost(16 * count * REGION, 4 * 16 * count * REGION),
        name="place_sample_lines",
    )(places, *[sample] * blocks)


def place_lines(places, coeff, awaited):
    count = places.shape[1]
    shape = (count * 16, REGION)
    return pl.pallas_call(
        lines_kernel,
        in_specs=[in_smem(), whole_vmem()] + [anywhere()] * len(awaited),
        out_specs=whole_vmem(),
        out_shape=jax.ShapeDtypeStruct(shape, F32),
        compiler_params=params(),
        cost_estimate=cost(16 * count * REGION, 4 * 16 * count * REGION),
        name="place_lines",
    )(places, coeff, *awaited)


def put_edges(opened, reach_x, reach_y, edges, first):
    half = reach_x // 2
    low = low_lanes(reach_y)
    layer = lambda i: opened[i * reach_y : (i + 1) * reach_y, :]
    for two in range(2):
        place = slice(first + two * reach_y, first + (two + 1) * reach_y)
        edges[0, place, :] = jnp.where(low, layer(2 * two), swap(layer(2 * two + 1)))
        last = half - 4 + 2 * two
        edges[1, place, :] = jnp.where(low, swap(layer(last)), layer(last + 1))


def stack_layers(layers, at, reach_y, stacked):
    tall = stacked.shape[0] // len(layers)
    place = at * up_to(reach_y, 8)
    for i, layer in enumerate(layers):
        stacked[pl.ds(pl.multiple_of(i * tall + place, 8), reach_y), :] = layer


def stack_pieces(parts, reach_x, reach_y, top, opened, stacked, edges, places):
    chip = lax.axis_index("narrow")
    for flip, (part, place) in enumerate(zip(parts, places)):
        first = from_short(part[:top, :])
        opened[...] = from_short(part[top:, :]) * unit(first[0:1], first[1:2])
        layers = [opened[i * reach_y : (i + 1) * reach_y, :] for i in range(reach_x // 2)]
        stack_layers(layers, chip ^ flip, reach_y, stacked)
        put_edges(opened, reach_x, reach_y, edges, place * 2 * reach_y)


def transform_pieces(table, stacked, before, spectrum):
    half = spectrum.shape[0]
    tall = stacked.shape[0] // half

    def tripled(values):
        high, low = split(values)
        return jnp.concatenate([high, low, high], axis=0)

    for i in range(0, half, 2):
        places = range(i, min(i + 2, half))
        held = jnp.concatenate([stacked[j * tall : (j + 1) * tall, :] for j in places], axis=1)
        result = dot(table, tripled(held))
        for j in places:
            made = result[:, (j - i) * 2 * HALF : (j - i + 1) * 2 * HALF]
            spectrum[j] = made if before is None else before[j] + made


def forward_early_kernel(reach_x, reach_y, chips, *refs):
    parts = refs[:chips]
    table_ref, spectrum, edges, opened, stacked = refs[chips:]
    top = parts[0].shape[0] - opened.shape[0]
    stacked[...] = jnp.zeros_like(stacked)
    stack_pieces(parts, reach_x, reach_y, top, opened, stacked, edges, range(chips))
    transform_pieces(table_ref[lax.axis_index("pair")], stacked, None, spectrum)


def stacking_scratch(chips, reach_x, reach_y):
    half = reach_x // 2
    return [
        pltpu.VMEM((up_to(half * reach_y, 16), 2 * HALF), F32),
        pltpu.VMEM((half * chips * up_to(reach_y, 8), 2 * HALF), F32),
    ]


def forward_early(parts, table, reach_x, reach_y):
    half = reach_x // 2
    chips = len(parts)
    return pl.pallas_call(
        functools.partial(forward_early_kernel, reach_x, reach_y, chips),
        in_specs=[whole_vmem()] * (chips + 1),
        out_specs=[whole_vmem()] * 2,
        out_shape=[
            jax.ShapeDtypeStruct((half, GRID, 2 * HALF), F32),
            jax.ShapeDtypeStruct((2, chips * 2 * reach_y, 2 * HALF), F32),
        ],
        scratch_shapes=stacking_scratch(chips, reach_x, reach_y),
        compiler_params=params(),
        cost_estimate=cost(EARLY_FLOPS, 4 * half * GRID * 2 * HALF * 2),
        name="forward_early",
    )(*parts, table)


def forward_kernel(reach_x, reach_y, blocks, pieces, awaited, *refs):
    parts = refs[:pieces]
    early_ref, early_edges, table_ref, modes_ref = refs[pieces : pieces + 4]
    refs = refs[pieces + 4 + awaited :]
    spectrum, even_out, layers_out, odd_out, own_out, peers_out, inner_out, *refs = refs
    opened, stacked, edges, slabs, head = refs
    half = reach_x // 2
    pair = lax.axis_size("pair")
    top = parts[0].shape[0] - opened.shape[0]
    stacked[...] = jnp.zeros_like(stacked)
    head[...] = jnp.zeros_like(head)
    for piece in range(pieces):
        first = from_short(parts[piece][:top, :])
        mantissa, exponent = first[2 : 2 + blocks], first[2 + blocks : 2 + 2 * blocks]
        peers_out[piece * blocks : (piece + 1) * blocks, :] = decode_rounded(mantissa, exponent)
        at = 6 + 2 * piece * blocks
        head[at : at + blocks, :] = mantissa
        head[at + blocks : at + 2 * blocks, :] = exponent
    rows = 2 * reach_y
    for chip in range(pieces // pair):
        place = chip * pair * rows
        edges[:, place : place + rows, :] = early_edges[:, chip * rows : (chip + 1) * rows, :]
    before = early_ref
    for core in range(1, pair):
        places = range(core, pieces, pair)
        stack_pieces(parts[core::pair], reach_x, reach_y, top, opened, stacked, edges, places)
        transform_pieces(table_ref[lax.axis_index("pair") ^ core], stacked, before, spectrum)
        before = spectrum

    chunk = 256

    def body(index, largest):
        rows = pl.ds(pl.multiple_of(index * chunk, chunk), chunk)
        low = low_lanes(chunk)
        decay = modes_ref[0, rows, :]
        log_decay = modes_ref[1, rows, :]
        across_half = jnp.exp(half * log_decay)
        across_cut = jnp.exp((half - 4) * log_decay)
        layers = [spectrum[i, rows, :] for i in range(half)]
        run = layers[0]
        cut_right = run
        for i in range(1, half):
            run = decay * run + layers[i]
            if i == half - 5:
                cut_right = run
        right = run
        run = layers[half - 1]
        cut_left = run
        for i in range(half - 2, -1, -1):
            run = decay * run + layers[i]
            if i == 4:
                cut_left = run
        left = run
        inner_out[rows, :] = jnp.where(low, right, left)
        swapped_right, swapped_left = swap(right), swap(left)
        own = jnp.where(low, left + across_half * swapped_left, right + across_half * swapped_right)
        own_out[rows, :] = own
        made = [
            jnp.where(low, own, cut_right + across_cut * swapped_right),
            jnp.where(low, cut_left + across_cut * swapped_left, own),
        ]
        for slab, values in enumerate(made):
            slabs[slab, rows, :] = values
        return tuple(
            jnp.maximum(old, jnp.max(jnp.abs(values).reshape(chunk // 8, 8, 2 * HALF), axis=0))
            for old, values in zip(largest, made)
        )

    zero = jnp.zeros((8, 2 * HALF), F32)
    largest = lax.fori_loop(0, GRID // chunk, body, (zero,) * 2)
    top = head.shape[0]
    low = low_lanes(GRID // 2)
    upper, lower = own_out[: GRID // 2, :], own_out[GRID // 2 :, :]
    packed = [jnp.where(low, swap(upper), lower), jnp.where(low, upper, swap(lower))]

    def send(out, first, parts):
        place = first
        for index, (values, most) in enumerate(parts):
            exponent, fraction = fit_scale(jnp.max(most, axis=0, keepdims=True))
            head[2 * index : 2 * index + 1, :] = exponent
            head[2 * index + 1 : 2 * index + 2, :] = fraction
            out[place : place + values.shape[0], :] = quantize(values, exponent, fraction)
            place += values.shape[0]
        out[:first, :] = to_short(head[:first, :])

    with_most = lambda values: (values, jnp.abs(values))
    on_left = lax.axis_index("wide") & 1
    for side, (even, odd) in enumerate(((0, 1), (1, 0))):

        @pl.when(on_left == side)
        def _():
            send(even_out, 16, [(slabs[even], largest[even]), with_most(packed[even])])
            send(layers_out, top, [with_most(edges[1 - even])])
            send(odd_out, top, [(slabs[odd], largest[odd]), with_most(edges[1 - odd])])


def forward(parts, early, early_edges, table, modes, reach_x, reach_y, blocks, awaited):
    pieces = len(parts)
    half = reach_x // 2
    lanes = 2 * HALF
    head = up_to(6 + 2 * pieces * blocks, 16)
    border = pieces * 2 * reach_y
    short = lambda rows: jax.ShapeDtypeStruct((rows, lanes), jnp.int16)
    return pl.pallas_call(
        functools.partial(
            forward_kernel, reach_x, reach_y, blocks, pieces, len(awaited)
        ),
        in_specs=[whole_vmem()] * (pieces + 4) + [anywhere()] * len(awaited),
        out_specs=[whole_vmem()] * 7,
        out_shape=[
            jax.ShapeDtypeStruct((half, GRID, lanes), F32),
            short(16 + GRID + GRID // 2),
            short(head + border),
            short(head + GRID + border),
            jax.ShapeDtypeStruct((GRID, lanes), F32),
            jax.ShapeDtypeStruct((pieces * blocks, BLOCK), F32),
            jax.ShapeDtypeStruct((GRID, lanes), F32),
        ],
        scratch_shapes=stacking_scratch(pieces // table.shape[0], reach_x, reach_y)
        + [
            pltpu.VMEM((2, border, lanes), F32),
            pltpu.VMEM((2, GRID, lanes), F32),
            pltpu.VMEM((head, lanes), F32),
        ],
        compiler_params=params(),
        cost_estimate=cost(2 * half * 256 * 256 * 128, 4 * half * GRID * lanes * 2),
        name="forward",
    )(*parts, early, early_edges, table, modes, *awaited)


def opened_part(ref, index, first, rows):
    head = from_short(ref[:16, :])
    scale = unit(head[2 * index : 2 * index + 1], head[2 * index + 1 : 2 * index + 2])
    return from_short(ref[first : first + rows, :]) * scale


def pair_kernel(reach_x, flips, own_ref, even_ref, modes_ref, *refs):
    outs, head = refs[:-1], refs[-1]
    span = reach_x - 4
    here = lax.axis_index("wide")
    low = low_lanes(GRID)
    log_decay = modes_ref[1]
    own = own_ref[...]
    top = even_ref.shape[0] - GRID - GRID // 2
    cut = opened_part(even_ref, 0, top, GRID)
    packed = opened_part(even_ref, 1, top + GRID, GRID // 2)
    from_left = jnp.where(low, cut, jnp.concatenate([swap(packed), packed], axis=0))
    from_right = jnp.where(low, jnp.concatenate([packed, swap(packed)], axis=0), cut)
    partner = jnp.where((here & 1) == 1, from_left, from_right)

    def weight(distances):
        powers = []
        for distance in distances:
            ahead = span * distance - reach_x
            powers.append(jnp.where(distance >= 2, ahead, ahead + GRID).astype(F32))
        return jnp.exp(jnp.where(low, *powers) * log_decay)

    head[...] = jnp.zeros_like(head)
    for flip, out in zip(flips, outs):
        behind = (here ^ flip) - here
        message = own * weight((-behind, behind))
        behind = (here ^ flip) - (here ^ 1)
        beside = jnp.where(jnp.abs(behind) == 1, 0.0, 1.0)
        send_piece(out, head, message + partner * (weight((-behind, behind)) * beside))


def pair_messages(own, from_even, modes, reach_x, flips):
    return pl.pallas_call(
        functools.partial(pair_kernel, reach_x, flips),
        in_specs=[whole_vmem()] * 3,
        out_specs=[whole_vmem()] * len(flips),
        out_shape=[jax.ShapeDtypeStruct((16 + GRID, 2 * HALF), jnp.int16)] * len(flips),
        scratch_shapes=[pltpu.VMEM((16, 2 * HALF), F32)],
        compiler_params=params(),
        cost_estimate=cost(16 * GRID * 2 * HALF, 4 * GRID * 2 * HALF * (6 + len(flips))),
        name="pair_messages",
    )(own, from_even, modes)


def borders_kernel(reach_y, pieces, layers_ref, odd_ref, table_ref, out_ref, stacked, partial):
    on_left = (lax.axis_index("wide") & 1) == 1
    pair = lax.axis_size("pair")
    rows = pieces * 2 * reach_y
    even = opened_part(layers_ref, 0, layers_ref.shape[0] - rows, rows)
    odd = opened_part(odd_ref, 1, odd_ref.shape[0] - rows, rows)
    left, right = jnp.where(on_left, even, odd), jnp.where(on_left, odd, even)
    low = low_lanes(rows)
    both = [jnp.where(low, left, swap(right)), jnp.where(low, swap(left), right)]
    core = lax.axis_index("pair")
    chip = lax.axis_index("narrow")
    stacked[...] = jnp.zeros_like(stacked)
    before = None
    for other in range(pair):
        for flip in range(pieces // pair):
            first = (flip * pair + other) * 2 * reach_y
            layers = [
                values[first + two * reach_y : first + (two + 1) * reach_y]
                for two in range(2)
                for values in both
            ]
            stack_layers(layers, chip ^ flip, reach_y, stacked)
        target = out_ref if other == pair - 1 else partial
        transform_pieces(table_ref[core ^ other], stacked, before, target)
        before = target


def borders(layers, from_odd, table, reach_y, pieces):
    chips = pieces // table.shape[0]
    shape = (4, GRID, 2 * HALF)
    return pl.pallas_call(
        functools.partial(borders_kernel, reach_y, pieces),
        in_specs=[whole_vmem()] * 3,
        out_specs=whole_vmem(),
        out_shape=jax.ShapeDtypeStruct(shape, F32),
        scratch_shapes=[
            pltpu.VMEM((4 * chips * up_to(reach_y, 8), 2 * HALF), F32),
            pltpu.VMEM(shape, F32),
        ],
        compiler_params=params(),
        cost_estimate=cost(2 * 4 * 256 * 256 * 128, 4 * 6 * GRID * 2 * HALF),
        name="borders",
    )(layers, from_odd, table)


def send_fields(outs, flips, reach_y, field_high, field_low, high_ref, low_ref, ready, head):
    half = field_high.shape[0]
    mine = y_position()
    pitch = up_to(reach_y, 16)
    pick = lambda ref: jnp.concatenate([ref[mine ^ flip] for flip in flips], axis=0)
    table = (pick(high_ref), pick(low_ref))
    for i in range(0, half, 2):
        many = min(2, half - i)
        join = lambda ref: jnp.concatenate([ref[i + j] for j in range(many)], axis=1)
        result = dot_three(table, (join(field_high), join(field_low)))
        for j in range(many):
            for piece in range(len(flips)):
                ready[piece, (i + j) * reach_y : (i + j + 1) * reach_y, :] = result[
                    piece * pitch : piece * pitch + reach_y, j * 2 * HALF : (j + 1) * 2 * HALF
                ]
    head[...] = jnp.zeros_like(head)
    for piece, out in enumerate(outs):
        if ready.shape[1] > half * reach_y:
            ready[piece, half * reach_y :, :] = jnp.zeros_like(ready[piece, half * reach_y :, :])
        send_piece(out, head, ready[piece])


def inverse_kernel(reach_x, reach_y, flips, fars, *refs):
    spectrum, border_ref, from_even, from_odd, own_ref, inner_ref, *far_refs = refs[: 6 + fars]
    refs = refs[6 + fars :]
    high_ref, low_ref, modes_ref = refs[:3]
    outs = refs[3 : 3 + len(flips)]
    field_high, field_low, ready, head = refs[3 + len(flips) :]
    half = reach_x // 2
    span = reach_x - 4
    chunk = 256
    border_rows = lax.axis_size("narrow") * lax.axis_size("pair") * 2 * reach_y
    tops = from_even.shape[0] - GRID - GRID // 2, from_odd.shape[0] - GRID - border_rows
    on_left = (lax.axis_index("wide") & 1) == 1
    moment_units = []
    for ref in (from_even, from_odd):
        first = from_short(ref[:16, :])
        moment_units.append(unit(first[0:1], first[1:2]))

    far_units = []
    for ref in far_refs:
        first = from_short(ref[:16, :])
        far_units.append(unit(first[0:1], first[1:2]))

    def body(index, carry):
        first = pl.multiple_of(index * chunk, chunk)
        rows = pl.ds(first, chunk)
        low = low_lanes(chunk)
        decay = modes_ref[0, rows, :]
        log_decay = modes_ref[1, rows, :]
        ring = modes_ref[2, rows, :]
        gain = modes_ref[3, rows, :]
        across_half = jnp.exp(half * log_decay)
        across_cut = jnp.exp((half - 4) * log_decay)
        around = jnp.exp((GRID - 4) * log_decay)
        beside = jnp.exp((GRID - reach_x - span) * log_decay)
        layers = [spectrum[i, rows, :] for i in range(half)]

        even, odd = (
            from_short(ref[pl.ds(pl.multiple_of(top + index * chunk, 16), chunk), :]) * scale
            for ref, top, scale in zip((from_even, from_odd), tops, moment_units)
        )
        left_moments, right_moments = jnp.where(on_left, even, odd), jnp.where(on_left, odd, even)
        border = [border_ref[i, rows, :] for i in range(4)]
        zero = jnp.zeros_like(decay)
        head_sum = border[0]
        for i in range(1, 4):
            head_sum = decay * head_sum + border[i]
        tail_sum = border[3]
        for i in range(2, -1, -1):
            tail_sum = decay * tail_sum + border[i]
        for i in range(4):
            layers[i] = layers[i] + jnp.where(low, border[i], zero)
        for i in range(4):
            place = half - 4 + i
            layers[place] = layers[place] + jnp.where(low, zero, border[i])
        total = own_ref[rows, :] * jnp.exp((GRID - reach_x) * log_decay)
        at = pl.ds(pl.multiple_of(16 + index * chunk, 16), chunk)
        for ref, scale in zip(far_refs, far_units):
            total = total + from_short(ref[at, :]) * scale
        one = jnp.ones_like(decay)
        total = total + left_moments * jnp.where(low, beside, one)
        total = total + right_moments * jnp.where(low, one, beside)
        shared = jnp.where(low, head_sum, tail_sum)
        entering = (swap(total) + around * shared) * ring
        leaving = swap(across_half * entering + across_cut * shared + inner_ref[rows, :])
        run = jnp.where(low, entering, leaving)
        forward_runs = []
        for i in range(half):
            run = decay * run + layers[i]
            forward_runs.append(run)
        run = jnp.where(low, leaving, entering)
        for i in range(half - 1, -1, -1):
            ahead = decay * run
            high, rest = split(gain * (forward_runs[i] + ahead))
            field_high[i, rows, :] = high
            field_low[i, rows, :] = rest
            run = ahead + layers[i]
        return carry

    lax.fori_loop(0, GRID // chunk, body, 0)
    send_fields(outs, flips, reach_y, field_high, field_low, high_ref, low_ref, ready, head)


def inverse(
    spectrum, border, from_even, from_odd, own, inner, fars, table, modes, reach_x, reach_y, flips
):
    half = reach_x // 2
    lanes = 2 * HALF
    body = up_to(half * reach_y, 16)
    shapes = [jax.ShapeDtypeStruct((16 + body, lanes), jnp.int16)] * len(flips)
    shapes += [jax.ShapeDtypeStruct((half, GRID, lanes), BF16)] * 2
    return pl.pallas_call(
        functools.partial(inverse_kernel, reach_x, reach_y, flips, len(fars)),
        in_specs=[whole_vmem()] * (9 + len(fars)),
        out_specs=[whole_vmem()] * len(shapes),
        out_shape=shapes,
        scratch_shapes=[
            pltpu.VMEM((len(flips), body, lanes), F32),
            pltpu.VMEM((16, lanes), F32),
        ],
        compiler_params=params(),
        cost_estimate=cost(2 * half * 256 * 256 * 128, 4 * half * GRID * lanes * 2),
        name="inverse",
    )(spectrum, border, from_even, from_odd, own, inner, *fars, *table, modes)


def inverse_rest_kernel(reach_y, flips, field_high, field_low, high_ref, low_ref, *refs):
    outs, (ready, head) = refs[: len(flips)], refs[len(flips) :]
    send_fields(outs, flips, reach_y, field_high, field_low, high_ref, low_ref, ready, head)


def inverse_rest(field, table, reach_y, flips):
    half = field[0].shape[0]
    lanes = 2 * HALF
    body = up_to(half * reach_y, 16)
    return pl.pallas_call(
        functools.partial(inverse_rest_kernel, reach_y, flips),
        in_specs=[whole_vmem()] * 4,
        out_specs=[whole_vmem()] * len(flips),
        out_shape=[jax.ShapeDtypeStruct((16 + body, lanes), jnp.int16)] * len(flips),
        scratch_shapes=[
            pltpu.VMEM((len(flips), body, lanes), F32),
            pltpu.VMEM((16, lanes), F32),
        ],
        compiler_params=params(),
        cost_estimate=cost(2 * half * 256 * 256 * 128, 4 * half * GRID * lanes * 2),
        name="inverse_rest",
    )(*field, *table)


def sum_rows(values):
    row = lax.broadcasted_iota(jnp.int32, values[0].shape, 0)
    for step in (4, 2, 1):
        low = (row & step) == 0
        paired = []
        for one, other in zip(values[: len(values) // 2], values[len(values) // 2 :]):
            kept = jnp.where(low, one, other)
            moved = jnp.where(low, other, one)
            if step == 4:
                moved = pltpu.roll(moved, 4, 0)
            else:
                moved = jnp.where(low, pltpu.roll(moved, 8 - step, 0), pltpu.roll(moved, step, 0))
            paired.append(kept + moved)
        values = paired
    return values[0]


def z_lines(parts, flips, high_ref, low_ref):
    mine = y_position()
    opened = []
    for part in parts:
        first = from_short(part[:16, :])
        opened.append(from_short(part[16:, :]) * unit(first[0:1], first[1:2]))
    values = split(jnp.concatenate(opened, axis=1))
    pick = lambda ref: jnp.concatenate([ref[mine ^ flip] for flip in flips], axis=0)
    return dot_three(values, (pick(high_ref), pick(low_ref)))


def sample_early_kernel(flips, *refs):
    *parts, high_ref, low_ref, out_ref = refs
    out_ref[...] = z_lines(parts, flips, high_ref, low_ref)


def sample_early(parts, flips, table):
    rows = parts[0].shape[0] - 16
    return pl.pallas_call(
        functools.partial(sample_early_kernel, flips),
        in_specs=[whole_vmem()] * (len(parts) + 2),
        out_specs=whole_vmem(),
        out_shape=jax.ShapeDtypeStruct((rows, 2 * REGION), F32),
        compiler_params=params(),
        cost_estimate=cost(EARLY_FLOPS, 4 * rows * 512),
        name="sample_early",
    )(*parts, *table)


def sample_kernel(last, reach_x, reach_y, flips, place_in, *refs):
    parts = refs[: len(flips)]
    early_ref, high_ref, low_ref, line_ref, own_ref, vector_ref, near_ref, out_ref = refs[
        len(flips) : len(flips) + 8
    ]
    flat, field, sums, place_ref, sem = refs[len(flips) + 8 :]
    copy = pltpu.make_async_copy(place_in, place_ref, sem)
    copy.start()
    half_rows = reach_x * reach_y // 2
    both = early_ref[...] + z_lines(parts, flips, high_ref, low_ref)
    flat[:half_rows, :] = both[:half_rows, :REGION]
    flat[half_rows:, :] = both[:half_rows, REGION:]
    for x in range(reach_x):
        layer = flat[x * reach_y : (x + 1) * reach_y, :]
        for row in pair_rows(x, reach_x, reach_y):
            field[pl.ds(row, reach_y, stride=2), :] = layer
    count = place_ref.shape[1]

    def body(group, carry):
        for eight in range(0, GROUP, 8):
            totals = []
            for local in range(eight, eight + 8):
                panel = group * GROUP + local
                row = place_ref[0, panel]
                first = pl.multiple_of(panel * 16, 16)
                totals.append(
                    field[pl.ds(row, 8), :] * line_ref[pl.ds(first, 8), :]
                    + field[pl.ds(row + 2 * reach_y, 8), :] * line_ref[pl.ds(first + 8, 8), :]
                )
            sums[pl.ds(pl.multiple_of(group * GROUP + eight, 8), 8), :] = sum_rows(totals)
        return carry

    copy.wait()
    lax.fori_loop(0, count // GROUP, body, 0)
    first, rest = split(sums[...])
    second, third = split(sums[...] - first.astype(F32))
    across = lambda values: lax.dot_general(
        jnp.ones((16, REGION), BF16),
        values,
        (((1,), (1,)), ((), ())),
        preferred_element_type=F32,
    )
    sampled = across(first) + (across(second) + across(third))
    for block in range(count // BLOCK):
        lane = slice(block * BLOCK, (block + 1) * BLOCK)
        row = slice(block, block + 1)
        vector = vector_ref[row, :]
        image = jnp.where(own_ref[row, :] == 1, 0.0, 0.5 * vector) + sampled[:1, lane]
        image = image + near_ref[row, :]
        if last:
            out_ref[0:1, lane] = vector
            out_ref[1:2, lane] = image
        else:
            out_ref[row, :] = image


def sample(last, places, parts, flips, early, table, lines, flag, vector, near, reach_x, reach_y):
    count = places.shape[1]
    blocks = count // BLOCK
    shape = (2, count) if last else (blocks, BLOCK)
    return pl.pallas_call(
        functools.partial(sample_kernel, last, reach_x, reach_y, flips),
        in_specs=[anywhere()] + [whole_vmem()] * (len(parts) + 7),
        out_specs=whole_vmem(),
        out_shape=jax.ShapeDtypeStruct(shape, F32),
        scratch_shapes=[
            pltpu.VMEM((reach_x * reach_y, REGION), F32),
            pltpu.VMEM((pair_count(reach_x, reach_y), REGION), F32),
            pltpu.VMEM((count, REGION), F32),
            pltpu.SMEM((2, count), jnp.int32),
            pltpu.SemaphoreType.DMA,
        ],
        compiler_params=params(),
        cost_estimate=cost(reach_x * reach_y * 256 * 512, 4 * 16 * count * REGION),
        name="sample",
    )(
        places,
        *parts,
        early,
        *table,
        lines,
        flag.reshape(blocks, BLOCK),
        vector.reshape(blocks, BLOCK),
        near,
    )


def near_kernel(slots, blocks, place_ref, target_ref, *refs):
    even_ref, odd_ref, peers_ref, tile_ref = refs[:4]
    out_ref, held = refs[-2:]
    count = peers_ref.shape[0]
    held[count : 2 * count, :] = peers_ref[...]
    on_left = lax.axis_index("wide") & 1
    for side, ref in ((1 - on_left, even_ref), (on_left, odd_ref)):
        top = from_short(ref[...])
        for piece in range(count // blocks):
            at = 6 + 2 * piece * blocks
            held[pl.ds(side * (2 * count) + piece * blocks, blocks), :] = decode_rounded(
                top[at : at + blocks], top[at + blocks : at + 2 * blocks]
            )
    out_ref[...] = jnp.zeros_like(out_ref)
    for slot in range(slots):
        picked = held[pl.ds(place_ref[slot], 1), :]
        picked = jnp.broadcast_to(picked, (16, BLOCK)).astype(BF16)
        product = lax.dot_general(
            picked,
            tile_ref[slot],
            (((1,), (1,)), ((), ())),
            preferred_element_type=F32,
        )
        target = pl.ds(target_ref[slot], 1)
        out_ref[target, :] = out_ref[target, :] + product[:1]


def near_field(places, targets, from_even, from_odd, peers, tiles, blocks, out_rows, awaited):
    slots = tiles.shape[0]
    head = up_to(6 + 2 * peers.shape[0], 16)
    constant = lambda shape: pl.BlockSpec(shape, lambda i: (0,) * len(shape))
    return pl.pallas_call(
        functools.partial(near_kernel, slots, blocks),
        grid=(1,),
        in_specs=[
            in_smem(),
            in_smem(),
            constant((head, BLOCK)),
            constant((head, BLOCK)),
            constant(peers.shape),
            constant(tiles.shape),
        ]
        + [anywhere()] * len(awaited),
        out_specs=constant((out_rows, BLOCK)),
        out_shape=jax.ShapeDtypeStruct((out_rows, BLOCK), F32),
        scratch_shapes=[pltpu.VMEM((3 * peers.shape[0], BLOCK), F32)],
        compiler_params=params(),
        cost_estimate=cost(2 * slots * 16 * BLOCK * BLOCK, 2 * slots * BLOCK * BLOCK),
        name="near_field",
    )(places, targets, from_even, from_odd, peers, tiles, *awaited)


def shards(
    density,
    surface_flag,
    stencil_base,
    sample_weights,
    dipole_weights,
    near_target,
    near_source,
    near_tiles,
):
    x_count = lax.axis_size("wide")
    y_count = lax.axis_size(Y_AXES)
    y_index = lax.axis_index(Y_AXES)
    pair = lax.axis_size("pair")
    span_x = REGION // x_count
    span_y = REGION // y_count
    reach_x = span_x + 4
    reach_y = span_y + 4
    count = density.shape[0]
    blocks = count // BLOCK

    z_forward, z_inverse, y_forward, y_inverse, modes = tables(y_count, pair, span_y)
    modes = lax.dynamic_index_in_dim(jnp.asarray(modes), y_index, 0, keepdims=False)

    neighbour = near_source // blocks
    flip = (y_index + neighbour % 3 - 1) ^ y_index
    sources = ((neighbour // 3) * y_count + flip) * blocks + near_source % blocks
    out_rows = up_to(blocks + 1, 8)
    live = near_target >= 0
    sources = jnp.where(live, sources, 0)
    targets = jnp.where(live, near_target, out_rows - 1)

    swaps = lambda pairs: [(i, j) for i, j in pairs] + [(j, i) for i, j in pairs]
    even_swap = swaps([(i, i + 1) for i in range(0, x_count - 1, 2)])
    odd_swap = swaps([(i, i + 1) for i in range(1, x_count - 1, 2)])
    far_flips = list(range(2, x_count, 2))

    first, inside, local = list(range(pair, y_count)), list(range(1, pair)), [0]
    same_core = list(range(0, y_count, pair))
    other_core = [flip for flip in range(y_count) if flip not in same_core]

    def turned(sent, then):
        arrived = [None] * y_count
        for flip, part in zip(first + inside + local, list(sent) + list(then)):
            swap_pairs = [(i, i ^ flip) for i in range(y_count)]
            arrived[flip] = part if flip == 0 else lax.ppermute(part, Y_AXES, swap_pairs)
        return arrived

    def chosen(parts, flips):
        return [parts[flip] for flip in flips]

    def convolve_and_sample(last, vector, sent, both, table, places, sample_lines, awaited):
        then = [part for flips in (inside, local) for part in spread_rest(vector, both, table, flips)]
        arrived = turned(sent, then)
        early, edges = forward_early(chosen(arrived, same_core), y_forward, reach_x, reach_y)
        spectrum, even_message, layers, odd_message, own, peers, inner = forward(
            arrived, early, edges, y_forward, modes, reach_x, reach_y, blocks, awaited
        )
        from_even = lax.ppermute(even_message, "wide", even_swap)
        from_odd = lax.ppermute(odd_message, "wide", odd_swap)
        even_layers = lax.ppermute(layers, "wide", even_swap)
        fars = [
            lax.ppermute(message, "wide", [(i, i ^ flip) for i in range(x_count)])
            for flip, message in zip(
                far_flips, pair_messages(own, from_even, modes, reach_x, far_flips)
            )
        ]
        *sent, high, low = inverse(
            spectrum,
            borders(even_layers, from_odd, y_forward, reach_y, y_count),
            from_even,
            from_odd,
            own,
            inner,
            fars,
            y_inverse,
            modes,
            reach_x,
            reach_y,
            first,
        )
        then = [
            part
            for flips in (inside, local)
            for part in inverse_rest((high, low), y_inverse, reach_y, flips)
        ]
        near_part = near_field(
            sources, targets, even_layers, from_odd, peers, near_tiles, blocks, out_rows, then[:1]
        )
        arrived = turned(sent, then)
        image = sample(
            last,
            places,
            chosen(arrived, other_core),
            other_core,
            sample_early(chosen(arrived, same_core), same_core, z_inverse),
            z_inverse,
            sample_lines,
            surface_flag,
            vector,
            near_part,
            reach_x,
            reach_y,
        )
        return image, near_part

    raw = (stencil_base, surface_flag, sample_weights, dipole_weights)
    *sent, wide_high, wide_low, source_coeff, places, vector, high, low = spread(
        density, z_forward, None, raw, reach_x, reach_y, first
    )
    z_forward = (high, low)
    sample_lines = place_sample_lines(places, sample_weights)
    vector, near_part = convolve_and_sample(
        False,
        vector,
        sent,
        (wide_high, wide_low),
        z_forward,
        places,
        sample_lines,
        [sample_lines],
    )
    source_lines = place_lines(places, source_coeff, [near_part])
    *sent, wide_high, wide_low = spread(
        vector.reshape(-1), z_forward, (places, source_lines), None, reach_x, reach_y, first
    )
    both_images, _ = convolve_and_sample(
        True, vector, sent, (wide_high, wide_low), z_forward, places, sample_lines, []
    )
    return both_images


def solution(mesh):
    panels = P(("groups",) + ALL_AXES)
    columns = P(None, ("groups",) + ALL_AXES)
    in_specs = (
        panels,
        panels,
        columns,
        columns,
        columns,
        panels,
        panels,
        P(("groups",) + ALL_AXES, None, None),
    )
    return jax.shard_map(
        shards, mesh=mesh, in_specs=in_specs, out_specs=columns, check_vma=False
    )
```

```python
import functools
import math

import jax
import jax.numpy as jnp
import numpy as np
from jax import lax
from jax.experimental import pallas as pl
from jax.experimental.pallas import tpu as pltpu
from jax.sharding import PartitionSpec as P

GRID = 256
REGION = 128
BLOCK = 128
HALF = 64
KERNEL_GAIN = 4.0
SCREEN = 1.0 / 1024.0
LN2 = math.log(2.0)
SPARE = 16
Y_AXES = ("narrow", "pair")
ALL_AXES = ("wide", "narrow", "pair")
F32 = jnp.float32
BF16 = jnp.bfloat16
VMEM_LIMIT = 24 * 1024 * 1024
START_LIMIT = VMEM_LIMIT
EARLY_FLOPS = 5 * 10**9
GROUP = 32
CHAINS = 2


def cas(angles):
    return np.cos(angles) + np.sin(angles)


def up_to(count, multiple):
    return -(-count // multiple) * multiple


def low_lanes(rows):
    return lax.broadcasted_iota(jnp.int32, (rows, 2 * HALF), 1) < HALF


def swap(values):
    return pltpu.roll(values, HALF, 1)


def split(values):
    high = values.astype(BF16)
    return high, (values - high.astype(F32)).astype(BF16)


def dot(left, right):
    return jnp.dot(left, right, preferred_element_type=F32)


def dot_three(left, right):
    return dot(left[0], right[0]) + (dot(left[0], right[1]) + dot(left[1], right[0]))


def params():
    return pltpu.CompilerParams(vmem_limit_bytes=VMEM_LIMIT)


def whole_vmem():
    return pl.BlockSpec(memory_space=pltpu.VMEM)


def anywhere():
    return pl.BlockSpec(memory_space=pl.ANY)


def in_smem():
    return pl.BlockSpec(memory_space=pltpu.SMEM)


def cost(flops, moved):
    return pl.CostEstimate(flops=flops, bytes_accessed=moved, transcendentals=0)


def full_scale(exponent, fraction):
    return fraction * jnp.exp(exponent * LN2) * (1.0 / 1024.0)


def fit_scale(largest):
    largest = jnp.maximum(largest, 1e-30)
    exponent = jnp.floor(jnp.log(largest) * (1.0 / LN2))
    fraction = jnp.ceil(largest * jnp.exp(-exponent * LN2) * 1024.0) + 1.0
    return exponent, fraction


def to_short(values):
    return values.astype(jnp.int32).astype(jnp.int16)


def from_short(values):
    return values.astype(jnp.int32).astype(F32)


def quantize(values, exponent, fraction):
    return to_short(jnp.round(values * (32767.0 / full_scale(exponent, fraction))))


def unit(exponent, fraction):
    return full_scale(exponent, fraction) * (1.0 / 32767.0)


def encode_rounded(values):
    rounded = values.astype(BF16).astype(F32)
    size = jnp.maximum(jnp.abs(rounded), 1e-30)
    exponent = jnp.floor(jnp.log(size) * (1.0 / LN2))
    return jnp.round(rounded * jnp.exp((10.0 - exponent) * LN2)), exponent


def decode_rounded(mantissa, exponent):
    return (mantissa * jnp.exp((exponent - 10.0) * LN2)).astype(BF16).astype(F32)


def send_piece(out, head, values):
    exponent, fraction = fit_scale(jnp.max(jnp.abs(values), axis=0, keepdims=True))
    head[0:1, :] = exponent
    head[1:2, :] = fraction
    top = head.shape[0]
    out[:top, :] = to_short(head[...])
    out[top:, :] = quantize(values, exponent, fraction)


def y_position():
    return lax.axis_index("narrow") * lax.axis_size("pair") + lax.axis_index("pair")


def halves(table):
    high = table.astype(jnp.bfloat16)
    return high, (table - high.astype(np.float64)).astype(jnp.bfloat16)


def tables(y_count, pair, span_y):
    depth = GRID // y_count
    reach = span_y + 4
    waves = np.arange(GRID)
    step = 2.0 * np.pi / GRID
    z_table = cas(step * np.outer(np.arange(REGION), waves))
    z_forward = np.zeros((y_count, 2 * REGION, 2 * HALF))
    z_inverse = np.zeros((y_count, 2 * HALF, 2 * REGION))
    symbols = 4.0 * np.sin(np.pi * waves / GRID) ** 2
    shift = np.full((y_count, GRID, 2 * HALF), 1.0)
    y_forward = np.zeros((GRID, y_count, up_to(reach, 8)))
    y_inverse = np.zeros((y_count, up_to(reach, 16), GRID))
    for block in range(y_count):
        mine = z_table[:, block * depth : (block + 1) * depth]
        for half in range(2):
            rows = slice(half * REGION, (half + 1) * REGION)
            lanes = slice(half * HALF, half * HALF + depth)
            z_forward[block, rows, lanes] = mine
            z_inverse[block, lanes, rows] = mine.T / GRID
            shift[block, :, lanes] = (
                SCREEN + symbols[:, None] + symbols[None, block * depth : (block + 1) * depth]
            )
        cells = block * span_y - 2 + np.arange(reach)
        y_table = cas(step * np.outer(waves, cells))
        y_forward[:, block, :reach] = y_table
        y_inverse[block, :reach] = y_table.T / GRID
    y_forward = y_forward.reshape(GRID, y_count // pair, pair, -1).transpose(2, 0, 1, 3)
    y_forward = halves(y_forward.reshape(pair, GRID, -1))
    y_forward = np.concatenate([y_forward[0], y_forward[0], y_forward[1]], axis=2)
    root = np.sqrt(shift * (shift + 4.0))
    decay = 2.0 / (2.0 + shift + root)
    log_decay = np.log(decay)
    modes = np.stack([decay, log_decay], axis=1).astype(np.float32)
    return (
        halves(z_forward),
        halves(z_inverse),
        y_forward,
        halves(y_inverse),
        modes,
    )


def mixing_matrix():
    place = lax.broadcasted_iota(jnp.int32, (4 * BLOCK, 4 * BLOCK), 0)
    lane = lax.broadcasted_iota(jnp.int32, (4 * BLOCK, 4 * BLOCK), 1)
    return jnp.where(lane == 4 * (place % BLOCK) + place // BLOCK, 1.0, 0.0).astype(BF16)


def weave(tiles, mixing, out):
    weights = jnp.concatenate([jnp.concatenate(tile, axis=1) for tile in tiles], axis=0)
    first, rest = split(weights)
    second, third = split(weights - first.astype(F32))
    woven = dot(first, mixing) + (dot(second, mixing) + dot(third, mixing))
    for tile in range(len(tiles)):
        for part in range(BLOCK // GROUP):
            at = (tile * (BLOCK // GROUP) + part) * 16
            lanes = slice(part * BLOCK, (part + 1) * BLOCK)
            for a in range(4):
                row = tile * 16 + 4 * a
                out[pl.ds(at + 8 * (a // 2) + a % 2, 4, stride=2), :] = woven[row : row + 4, lanes]


def by_depth(ref):
    return [ref[pl.ds(depth, 16, stride=4), :] for depth in range(4)]


def pair_rows(x, reach_x, reach_y):
    even = (x // 2) * 2 * reach_y + x % 2
    if x == 0 or x == reach_x - 1:
        return [even]
    return [even, reach_x * reach_y + ((x - 1) // 2) * 2 * reach_y + (x - 1) % 2]


def pair_count(reach_x, reach_y):
    return (2 * reach_x - 2) * reach_y + SPARE


def in_window(lanes, depth):
    return ((lanes - depth) & -4) == 0


def add_panels(reach, woven, vector_ref, place_ref, weight_ref, grids):
    lanes = lax.broadcasted_iota(jnp.int32, (8, REGION), 1)

    def body(group, carry):
        at = pl.multiple_of(group * 16, 16)
        coeff = [weight_ref[pl.ds(at + 8 * q, 8), :] for q in range(2)] if woven else None
        for local in range(GROUP):
            panel = group * GROUP + local
            grid = grids[local % len(grids)]
            row = place_ref[0, panel]
            value = vector_ref[panel]
            if woven:
                depth = place_ref[1, panel]
                shift = (depth - 4 * local) & (REGION - 1)
                value = jnp.where(in_window(lanes, depth), value, 0.0)
                lines = [pltpu.roll(coeff[q], shift, 1) for q in range(2)]
            else:
                first = pl.multiple_of(panel * 16, 16)
                lines = [weight_ref[pl.ds(first + 8 * q, 8), :] for q in range(2)]
            places = [pl.ds(row, 8), pl.ds(row + 2 * reach, 8)]
            held = [grid[place, :] for place in places]
            for q in range(2):
                grid[places[q], :] = held[q] + lines[q] * value
        return carry

    lax.fori_loop(0, vector_ref.shape[0] // GROUP, body, 0)


def send_pieces(outs, flips, head, rounded, both, high_ref, low_ref):
    blocks = rounded.shape[0]
    mantissa, exponent = encode_rounded(rounded)
    head[...] = jnp.zeros_like(head)
    head[2 : 2 + blocks, :] = mantissa
    head[2 + blocks : 2 + 2 * blocks, :] = exponent
    mine = y_position()
    for at in range(0, len(flips), 2):
        pick = lambda ref: jnp.concatenate([ref[mine ^ flip] for flip in flips[at : at + 2]], axis=1)
        result = dot_three(both, (pick(high_ref), pick(low_ref)))
        for i, out in enumerate(outs[at : at + 2]):
            send_piece(out, head, result[:, i * 2 * HALF : (i + 1) * 2 * HALF])


def spread_grid(reach_x, reach_y, rounded, tables, outs, flips, wides, head, total, grids):
    for x in range(reach_x):
        parts = [
            grid[pl.ds(row, reach_y, stride=2), :]
            for row in pair_rows(x, reach_x, reach_y)
            for grid in grids
        ]
        total[x * reach_y : (x + 1) * reach_y, :] = sum(parts[1:], parts[0])
    half = reach_x * reach_y // 2
    both = jnp.concatenate([total[:half, :], total[half : 2 * half, :]], axis=1)
    extra = wides[0].shape[0] - half
    if extra:
        both = jnp.concatenate([both, jnp.zeros((extra, 2 * REGION), F32)], axis=0)
    both = split(both)
    for wide, values in zip(wides, both):
        wide[...] = values
    send_pieces(outs, flips, head, rounded, both, *tables)


def start_kernel(reach_x, reach_y, flips, *refs):
    vector_in, *remote = refs[:8]
    refs = refs[8:]
    outs, refs = refs[: len(flips)], refs[len(flips) :]
    wides, (weight_ref, places_out), refs = refs[:2], refs[2:4], refs[4:]
    rounded, high, low, stencil, flag, samples, dipoles, vector_ref = refs[:8]
    place_ref, sems, head, total = refs[8:12]
    grids = refs[12:]
    tiles = samples.shape[0]
    copies = []
    fetch = lambda source, target: copies.append(
        pltpu.make_async_copy(source, target, sems.at[len(copies)])
    )
    rounded_in, high_in, low_in, stencil_in, flag_in, sample_in, dipole_in = remote
    fetch(stencil_in, stencil)
    fetch(flag_in, flag)
    fetch(vector_in, vector_ref)
    for tile in range(tiles):
        lanes = pl.ds(tile * BLOCK, BLOCK)
        fetch(sample_in.at[:, lanes], samples.at[tile, pl.ds(0, 64)])
        fetch(dipole_in.at[:, lanes], dipoles.at[tile, pl.ds(0, 64)])
    needed_first = len(copies)
    fetch(rounded_in, rounded)
    fetch(high_in, high)
    fetch(low_in, low)
    for copy in copies:
        copy.start()
    for grid in grids:
        grid[...] = jnp.zeros_like(grid)
    mixing = mixing_matrix()
    copies[0].wait()
    span_x, span_y = reach_x - 4, reach_y - 4
    local_x = stencil[0:1, :] - (lax.axis_index("wide") * span_x - 2)
    local_y = stencil[1:2, :] - (y_position() * span_y - 2)
    odd = local_x & 1
    places_out[0:1, :] = odd * (reach_x * reach_y) + (local_x >> 1) * (2 * reach_y) + 2 * local_y
    places_out[1:2, :] = stencil[2:3, :]
    to_scalar = pltpu.make_async_copy(places_out, place_ref, sems.at[len(copies)])
    to_scalar.start()
    for copy in copies[1:needed_first]:
        copy.wait()
    sources = []
    for tile in range(tiles):
        charged = flag[:, tile * BLOCK : (tile + 1) * BLOCK] == 1
        pairs = zip(by_depth(samples.at[tile]), by_depth(dipoles.at[tile]))
        sources.append([jnp.where(charged, -sample, dipole) for sample, dipole in pairs])
    weave(sources, mixing, weight_ref)
    to_scalar.wait()
    add_panels(reach_y, True, vector_ref, place_ref, weight_ref, grids)
    for copy in copies[needed_first:]:
        copy.wait()
    spread_grid(
        reach_x, reach_y, rounded[...], (high, low), outs, flips, wides, head, total, grids
    )


def spread_kernel(reach_x, reach_y, flips, *refs):
    vector_in, place_in, rounded_ref, high_ref, low_ref, line_ref = refs[:6]
    refs = refs[6:]
    outs, wides, (vector_ref, place_ref, sems, head, total), grids = (
        refs[: len(flips)],
        refs[len(flips) : len(flips) + 2],
        refs[len(flips) + 2 : len(flips) + 7],
        refs[len(flips) + 7 :],
    )
    copies = [
        pltpu.make_async_copy(vector_in, vector_ref, sems.at[0]),
        pltpu.make_async_copy(place_in, place_ref, sems.at[1]),
    ]
    for copy in copies:
        copy.start()
    for grid in grids:
        grid[...] = jnp.zeros_like(grid)
    for copy in copies:
        copy.wait()
    add_panels(reach_y, False, vector_ref, place_ref, line_ref, grids)
    spread_grid(
        reach_x,
        reach_y,
        rounded_ref[...],
        (high_ref, low_ref),
        outs,
        flips,
        wides,
        head,
        total,
        grids,
    )


def spread(vector, table, placed, raw, reach_x, reach_y, flips):
    count = vector.shape[0]
    half = reach_x * reach_y // 2
    blocks = count // BLOCK
    top = up_to(2 + 2 * blocks, 16)
    lanes = 2 * HALF
    body = up_to(half, 16)
    woven = (count // GROUP * 16 + SPARE, BLOCK)
    out_shapes = [jax.ShapeDtypeStruct((top + body, lanes), jnp.int16)] * len(flips)
    out_shapes += [jax.ShapeDtypeStruct((body, 2 * REGION), BF16)] * 2
    rounded = vector.reshape(blocks, BLOCK)
    work = [
        pltpu.VMEM((top, lanes), F32),
        pltpu.VMEM((reach_x * reach_y + SPARE, REGION), F32),
    ] + [pltpu.VMEM((pair_count(reach_x, reach_y), REGION), F32)] * CHAINS
    if placed is None:
        stencil, flag, sample, dipole = raw
        operands = [vector, rounded, *table, stencil, flag.reshape(1, -1), sample, dipole]
        operands = [pltpu.with_memory_space_constraint(value, pltpu.HBM) for value in operands]
        in_specs = [pl.BlockSpec(memory_space=pltpu.HBM)] * 8
        out_shapes += [jax.ShapeDtypeStruct(woven, F32)]
        out_shapes += [jax.ShapeDtypeStruct((2, count), jnp.int32)]
        out_shapes += [jax.ShapeDtypeStruct(rounded.shape, F32)]
        out_shapes += [jax.ShapeDtypeStruct(values.shape, BF16) for values in table]
        tiled = pltpu.VMEM((blocks, 64 + SPARE, BLOCK), F32)
        work = [
            pltpu.VMEM(stencil.shape, jnp.int32),
            pltpu.VMEM((1, count), jnp.int32),
            tiled,
            tiled,
            pltpu.SMEM((count,), F32),
            pltpu.SMEM((2, count), jnp.int32),
            pltpu.SemaphoreType.DMA((7 + 2 * blocks,)),
        ] + work
    else:
        operands = [vector, placed[0], rounded, *table, placed[1]]
        in_specs = [anywhere()] * 2 + [whole_vmem()] * 4
        work = [
            pltpu.SMEM((count,), F32),
            pltpu.SMEM((2, count), jnp.int32),
            pltpu.SemaphoreType.DMA((2,)),
        ] + work
    return pl.pallas_call(
        functools.partial(
            start_kernel if placed is None else spread_kernel, reach_x, reach_y, flips
        ),
        in_specs=in_specs,
        out_specs=[whole_vmem()] * len(out_shapes),
        out_shape=out_shapes,
        scratch_shapes=work,
        compiler_params=pltpu.CompilerParams(
            vmem_limit_bytes=START_LIMIT if placed is None else VMEM_LIMIT
        ),
        cost_estimate=cost(2 * half * 256 * 512, 4 * 16 * count * REGION),
        name="start" if placed is None else "spread",
    )(*operands)


def spread_rest_kernel(flips, rounded_ref, wide_high, wide_low, high_ref, low_ref, *refs):
    outs, head = refs[:-1], refs[-1]
    both = (wide_high[...], wide_low[...])
    send_pieces(outs, flips, head, rounded_ref[...], both, high_ref, low_ref)


def spread_rest(rounded, both, table, flips):
    blocks = rounded.shape[0]
    top = up_to(2 + 2 * blocks, 16)
    shape = (top + both[0].shape[0], 2 * HALF)
    return pl.pallas_call(
        functools.partial(spread_rest_kernel, flips),
        in_specs=[whole_vmem()] * 5,
        out_specs=[whole_vmem()] * len(flips),
        out_shape=[jax.ShapeDtypeStruct(shape, jnp.int16)] * len(flips),
        scratch_shapes=[pltpu.VMEM((top, 2 * HALF), F32)],
        compiler_params=params(),
        cost_estimate=cost(2 * shape[0] * 256 * 256 * 3, 4 * shape[0] * 512),
        name="spread_rest",
    )(rounded, *both, *table)


def lines_kernel(place_ref, coeff_ref, *refs):
    out_ref = refs[-1]
    lanes = lax.broadcasted_iota(jnp.int32, (8, REGION), 1)

    def body(group, carry):
        at = pl.multiple_of(group * 16, 16)
        coeff = [coeff_ref[pl.ds(at + 8 * q, 8), :] for q in range(2)]
        for local in range(GROUP):
            panel = group * GROUP + local
            depth = place_ref[1, panel]
            shift = (depth - 4 * local) & (REGION - 1)
            inside = in_window(lanes, depth)
            for q in range(2):
                first = pl.multiple_of(panel * 16 + 8 * q, 8)
                out_ref[pl.ds(first, 8), :] = jnp.where(inside, pltpu.roll(coeff[q], shift, 1), 0.0)
        return carry

    lax.fori_loop(0, place_ref.shape[1] // GROUP, body, 0)


def sample_lines_kernel(tiles, place_ref, *refs):
    out_ref, coeff, held = refs[-3:]
    for tile, ref in enumerate(refs[:tiles]):
        held[tile, :64, :] = ref[...]
    weave([by_depth(held.at[tile]) for tile in range(tiles)], mixing_matrix(), coeff)
    lines_kernel(place_ref, coeff, out_ref)


def place_sample_lines(places, sample):
    count = places.shape[1]
    blocks = count // BLOCK
    tile = lambda t: pl.BlockSpec((64, BLOCK), lambda i: (0, t))
    shape = (count * 16, REGION)
    return pl.pallas_call(
        functools.partial(sample_lines_kernel, blocks),
        grid=(1,),
        in_specs=[in_smem()] + [tile(t) for t in range(blocks)],
        out_specs=pl.BlockSpec(shape, lambda i: (0, 0)),
        out_shape=jax.ShapeDtypeStruct(shape, F32),
        scratch_shapes=[
            pltpu.VMEM((count // GROUP * 16 + SPARE, BLOCK), F32),
            pltpu.VMEM((blocks, 64 + SPARE, BLOCK), F32),
        ],
        compiler_params=params(),
        cost_estimate=cost(16 * count * REGION, 4 * 16 * count * REGION),
        name="place_sample_lines",
    )(places, *[sample] * blocks)


def place_lines(places, coeff, awaited):
    count = places.shape[1]
    shape = (count * 16, REGION)
    return pl.pallas_call(
        lines_kernel,
        in_specs=[in_smem(), whole_vmem()] + [anywhere()] * len(awaited),
        out_specs=whole_vmem(),
        out_shape=jax.ShapeDtypeStruct(shape, F32),
        compiler_params=params(),
        cost_estimate=cost(16 * count * REGION, 4 * 16 * count * REGION),
        name="place_lines",
    )(places, coeff, *awaited)


def put_edges(opened, reach_x, reach_y, edges, first):
    half = reach_x // 2
    low = low_lanes(reach_y)
    layer = lambda i: opened[i * reach_y : (i + 1) * reach_y, :]
    for two in range(2):
        place = slice(first + two * reach_y, first + (two + 1) * reach_y)
        edges[0, place, :] = jnp.where(low, layer(2 * two), swap(layer(2 * two + 1)))
        last = half - 4 + 2 * two
        edges[1, place, :] = jnp.where(low, swap(layer(last)), layer(last + 1))


def stack_layers(layers, at, reach_y, stacked):
    tall = stacked.shape[0] // len(layers)
    place = at * up_to(reach_y, 8)
    for i, layer in enumerate(layers):
        stacked[pl.ds(pl.multiple_of(i * tall + place, 8), reach_y), :] = layer


def stack_pieces(parts, reach_x, reach_y, top, opened, stacked, edges, places):
    chip = lax.axis_index("narrow")
    for flip, (part, place) in enumerate(zip(parts, places)):
        first = from_short(part[:top, :])
        opened[...] = from_short(part[top:, :]) * unit(first[0:1], first[1:2])
        layers = [opened[i * reach_y : (i + 1) * reach_y, :] for i in range(reach_x // 2)]
        stack_layers(layers, chip ^ flip, reach_y, stacked)
        put_edges(opened, reach_x, reach_y, edges, place * 2 * reach_y)


def transform_pieces(table, stacked, before, spectrum):
    half = spectrum.shape[0]
    tall = stacked.shape[0] // half

    def tripled(values):
        high, low = split(values)
        return jnp.concatenate([high, low, high], axis=0)

    for i in range(0, half, 2):
        places = range(i, min(i + 2, half))
        held = jnp.concatenate([stacked[j * tall : (j + 1) * tall, :] for j in places], axis=1)
        result = dot(table, tripled(held))
        for j in places:
            made = result[:, (j - i) * 2 * HALF : (j - i + 1) * 2 * HALF]
            spectrum[j] = made if before is None else before[j] + made


def forward_early_kernel(reach_x, reach_y, chips, *refs):
    parts = refs[:chips]
    table_ref, spectrum, edges, opened, stacked = refs[chips:]
    top = parts[0].shape[0] - opened.shape[0]
    stacked[...] = jnp.zeros_like(stacked)
    stack_pieces(parts, reach_x, reach_y, top, opened, stacked, edges, range(chips))
    transform_pieces(table_ref[lax.axis_index("pair")], stacked, None, spectrum)


def stacking_scratch(chips, reach_x, reach_y):
    half = reach_x // 2
    return [
        pltpu.VMEM((up_to(half * reach_y, 16), 2 * HALF), F32),
        pltpu.VMEM((half * chips * up_to(reach_y, 8), 2 * HALF), F32),
    ]


def forward_early(parts, table, reach_x, reach_y):
    half = reach_x // 2
    chips = len(parts)
    return pl.pallas_call(
        functools.partial(forward_early_kernel, reach_x, reach_y, chips),
        in_specs=[whole_vmem()] * (chips + 1),
        out_specs=[whole_vmem()] * 2,
        out_shape=[
            jax.ShapeDtypeStruct((half, GRID, 2 * HALF), F32),
            jax.ShapeDtypeStruct((2, chips * 2 * reach_y + SPARE, 2 * HALF), F32),
        ],
        scratch_shapes=stacking_scratch(chips, reach_x, reach_y),
        compiler_params=params(),
        cost_estimate=cost(EARLY_FLOPS, 4 * half * GRID * 2 * HALF * 2),
        name="forward_early",
    )(*parts, table)


def forward_kernel(reach_x, reach_y, blocks, pieces, awaited, *refs):
    parts = refs[:pieces]
    early_ref, early_edges, table_ref, modes_ref = refs[pieces : pieces + 4]
    refs = refs[pieces + 4 + awaited :]
    spectrum, even_out, layers_out, odd_out, own_out, peers_out, inner_out, *refs = refs
    opened, stacked, edges, slabs, head = refs
    half = reach_x // 2
    pair = lax.axis_size("pair")
    top = parts[0].shape[0] - opened.shape[0]
    stacked[...] = jnp.zeros_like(stacked)
    head[...] = jnp.zeros_like(head)
    for piece in range(pieces):
        first = from_short(parts[piece][:top, :])
        mantissa, exponent = first[2 : 2 + blocks], first[2 + blocks : 2 + 2 * blocks]
        peers_out[piece * blocks : (piece + 1) * blocks, :] = decode_rounded(mantissa, exponent)
        at = 6 + 2 * piece * blocks
        head[at : at + blocks, :] = mantissa
        head[at + blocks : at + 2 * blocks, :] = exponent
    rows = 2 * reach_y
    for chip in range(pieces // pair):
        place = chip * pair * rows
        edges[:, place : place + rows, :] = early_edges[:, chip * rows : (chip + 1) * rows, :]
    before = early_ref
    for core in range(1, pair):
        places = range(core, pieces, pair)
        stack_pieces(parts[core::pair], reach_x, reach_y, top, opened, stacked, edges, places)
        transform_pieces(table_ref[lax.axis_index("pair") ^ core], stacked, before, spectrum)
        before = spectrum

    chunk = 256

    def body(index, largest):
        rows = pl.ds(pl.multiple_of(index * chunk, chunk), chunk)
        low = low_lanes(chunk)
        decay = modes_ref[0, rows, :]
        log_decay = modes_ref[1, rows, :]
        across_half = jnp.exp(half * log_decay)
        across_cut = jnp.exp((half - 4) * log_decay)
        layers = [spectrum[i, rows, :] for i in range(half)]
        run = layers[0]
        cut_right = run
        for i in range(1, half):
            run = decay * run + layers[i]
            if i == half - 5:
                cut_right = run
        right = run
        run = layers[half - 1]
        cut_left = run
        for i in range(half - 2, -1, -1):
            run = decay * run + layers[i]
            if i == 4:
                cut_left = run
        left = run
        inner_out[rows, :] = jnp.where(low, right, left)
        swapped_right, swapped_left = swap(right), swap(left)
        own = jnp.where(low, left + across_half * swapped_left, right + across_half * swapped_right)
        own_out[rows, :] = own
        made = [
            jnp.where(low, own, cut_right + across_cut * swapped_right),
            jnp.where(low, cut_left + across_cut * swapped_left, own),
        ]
        for slab, values in enumerate(made):
            slabs[slab, rows, :] = values
        return tuple(
            jnp.maximum(old, jnp.max(jnp.abs(values).reshape(chunk // 8, 8, 2 * HALF), axis=0))
            for old, values in zip(largest, made)
        )

    zero = jnp.zeros((8, 2 * HALF), F32)
    largest = lax.fori_loop(0, GRID // chunk, body, (zero,) * 2)
    top = head.shape[0]
    low = low_lanes(GRID // 2)
    upper, lower = own_out[: GRID // 2, :], own_out[GRID // 2 :, :]
    packed = [jnp.where(low, swap(upper), lower), jnp.where(low, upper, swap(lower))]

    def send(out, first, parts):
        place = first
        for index, (values, most) in enumerate(parts):
            exponent, fraction = fit_scale(jnp.max(most, axis=0, keepdims=True))
            head[2 * index : 2 * index + 1, :] = exponent
            head[2 * index + 1 : 2 * index + 2, :] = fraction
            out[place : place + values.shape[0], :] = quantize(values, exponent, fraction)
            place += values.shape[0]
        out[:first, :] = to_short(head[:first, :])

    with_most = lambda values: (values, jnp.abs(values))
    border = pieces * 2 * reach_y
    on_left = lax.axis_index("wide") & 1
    for side, (even, odd) in enumerate(((0, 1), (1, 0))):

        @pl.when(on_left == side)
        def _():
            send(even_out, 16, [(slabs[even], largest[even]), with_most(packed[even])])
            send(layers_out, top, [with_most(edges[1 - even, :border, :])])
            send(odd_out, top, [(slabs[odd], largest[odd]), with_most(edges[1 - odd, :border, :])])


def forward(parts, early, early_edges, table, modes, reach_x, reach_y, blocks, awaited):
    pieces = len(parts)
    half = reach_x // 2
    lanes = 2 * HALF
    head = up_to(6 + 2 * pieces * blocks, 16)
    border = pieces * 2 * reach_y
    short = lambda rows: jax.ShapeDtypeStruct((rows, lanes), jnp.int16)
    return pl.pallas_call(
        functools.partial(
            forward_kernel, reach_x, reach_y, blocks, pieces, len(awaited)
        ),
        in_specs=[whole_vmem()] * (pieces + 4) + [anywhere()] * len(awaited),
        out_specs=[whole_vmem()] * 7,
        out_shape=[
            jax.ShapeDtypeStruct((half, GRID, lanes), F32),
            short(16 + GRID + GRID // 2),
            short(head + border),
            short(head + GRID + border),
            jax.ShapeDtypeStruct((GRID, lanes), F32),
            jax.ShapeDtypeStruct((pieces * blocks, BLOCK), F32),
            jax.ShapeDtypeStruct((GRID, lanes), F32),
        ],
        scratch_shapes=stacking_scratch(pieces // table.shape[0], reach_x, reach_y)
        + [
            pltpu.VMEM((2, border + SPARE, lanes), F32),
            pltpu.VMEM((2, GRID, lanes), F32),
            pltpu.VMEM((head, lanes), F32),
        ],
        compiler_params=params(),
        cost_estimate=cost(2 * half * 256 * 256 * 128, 4 * half * GRID * lanes * 2),
        name="forward",
    )(*parts, early, early_edges, table, modes, *awaited)


def opened_part(ref, index, first, rows):
    head = from_short(ref[:16, :])
    scale = unit(head[2 * index : 2 * index + 1], head[2 * index + 1 : 2 * index + 2])
    return from_short(ref[first : first + rows, :]) * scale


def pair_kernel(reach_x, flips, own_ref, even_ref, modes_ref, *refs):
    outs, head = refs[:-1], refs[-1]
    span = reach_x - 4
    here = lax.axis_index("wide")
    low = low_lanes(GRID)
    log_decay = modes_ref[1]
    own = own_ref[...]
    top = even_ref.shape[0] - GRID - GRID // 2
    cut = opened_part(even_ref, 0, top, GRID)
    packed = opened_part(even_ref, 1, top + GRID, GRID // 2)
    from_left = jnp.where(low, cut, jnp.concatenate([swap(packed), packed], axis=0))
    from_right = jnp.where(low, jnp.concatenate([packed, swap(packed)], axis=0), cut)
    partner = jnp.where((here & 1) == 1, from_left, from_right)

    def weight(distances):
        powers = []
        for distance in distances:
            ahead = span * distance - reach_x
            powers.append(jnp.where(distance >= 2, ahead, ahead + GRID).astype(F32))
        return jnp.exp(jnp.where(low, *powers) * log_decay)

    head[...] = jnp.zeros_like(head)
    for flip, out in zip(flips, outs):
        behind = (here ^ flip) - here
        message = own * weight((-behind, behind))
        behind = (here ^ flip) - (here ^ 1)
        beside = jnp.where(jnp.abs(behind) == 1, 0.0, 1.0)
        send_piece(out, head, message + partner * (weight((-behind, behind)) * beside))


def pair_messages(own, from_even, modes, reach_x, flips):
    return pl.pallas_call(
        functools.partial(pair_kernel, reach_x, flips),
        in_specs=[whole_vmem()] * 3,
        out_specs=[whole_vmem()] * len(flips),
        out_shape=[jax.ShapeDtypeStruct((16 + GRID, 2 * HALF), jnp.int16)] * len(flips),
        scratch_shapes=[pltpu.VMEM((16, 2 * HALF), F32)],
        compiler_params=params(),
        cost_estimate=cost(16 * GRID * 2 * HALF, 4 * GRID * 2 * HALF * (6 + len(flips))),
        name="pair_messages",
    )(own, from_even, modes)


def borders_kernel(reach_y, pieces, layers_ref, odd_ref, table_ref, out_ref, stacked, partial):
    on_left = (lax.axis_index("wide") & 1) == 1
    pair = lax.axis_size("pair")
    rows = pieces * 2 * reach_y
    even = opened_part(layers_ref, 0, layers_ref.shape[0] - rows, rows)
    odd = opened_part(odd_ref, 1, odd_ref.shape[0] - rows, rows)
    left, right = jnp.where(on_left, even, odd), jnp.where(on_left, odd, even)
    low = low_lanes(rows)
    both = [jnp.where(low, left, swap(right)), jnp.where(low, swap(left), right)]
    core = lax.axis_index("pair")
    chip = lax.axis_index("narrow")
    stacked[...] = jnp.zeros_like(stacked)
    before = None
    for other in range(pair):
        for flip in range(pieces // pair):
            first = (flip * pair + other) * 2 * reach_y
            layers = [
                values[first + two * reach_y : first + (two + 1) * reach_y]
                for two in range(2)
                for values in both
            ]
            stack_layers(layers, chip ^ flip, reach_y, stacked)
        target = out_ref if other == pair - 1 else partial
        transform_pieces(table_ref[core ^ other], stacked, before, target)
        before = target


def borders(layers, from_odd, table, reach_y, pieces):
    chips = pieces // table.shape[0]
    shape = (4, GRID, 2 * HALF)
    return pl.pallas_call(
        functools.partial(borders_kernel, reach_y, pieces),
        in_specs=[whole_vmem()] * 3,
        out_specs=whole_vmem(),
        out_shape=jax.ShapeDtypeStruct(shape, F32),
        scratch_shapes=[
            pltpu.VMEM((4 * chips * up_to(reach_y, 8), 2 * HALF), F32),
            pltpu.VMEM(shape, F32),
        ],
        compiler_params=params(),
        cost_estimate=cost(2 * 4 * 256 * 256 * 128, 4 * 6 * GRID * 2 * HALF),
        name="borders",
    )(layers, from_odd, table)


def send_fields(outs, flips, reach_y, field_high, field_low, high_ref, low_ref, ready, head):
    half = field_high.shape[0]
    mine = y_position()
    pitch = up_to(reach_y, 16)
    pick = lambda ref: jnp.concatenate([ref[mine ^ flip] for flip in flips], axis=0)
    table = (pick(high_ref), pick(low_ref))
    for i in range(0, half, 2):
        many = min(2, half - i)
        join = lambda ref: jnp.concatenate([ref[i + j] for j in range(many)], axis=1)
        result = dot_three(table, (join(field_high), join(field_low)))
        for j in range(many):
            for piece in range(len(flips)):
                ready[piece, (i + j) * reach_y : (i + j + 1) * reach_y, :] = result[
                    piece * pitch : piece * pitch + reach_y, j * 2 * HALF : (j + 1) * 2 * HALF
                ]
    head[...] = jnp.zeros_like(head)
    for piece, out in enumerate(outs):
        if ready.shape[1] > half * reach_y:
            ready[piece, half * reach_y :, :] = jnp.zeros_like(ready[piece, half * reach_y :, :])
        send_piece(out, head, ready[piece])


def inverse_kernel(reach_x, reach_y, flips, fars, *refs):
    spectrum, border_ref, from_even, from_odd, own_ref, inner_ref, *far_refs = refs[: 6 + fars]
    refs = refs[6 + fars :]
    high_ref, low_ref, modes_ref = refs[:3]
    outs = refs[3 : 3 + len(flips)]
    field_high, field_low, ready, head = refs[3 + len(flips) :]
    half = reach_x // 2
    span = reach_x - 4
    chunk = 256
    border_rows = lax.axis_size("narrow") * lax.axis_size("pair") * 2 * reach_y
    tops = from_even.shape[0] - GRID - GRID // 2, from_odd.shape[0] - GRID - border_rows
    on_left = (lax.axis_index("wide") & 1) == 1
    moment_units = []
    for ref in (from_even, from_odd):
        first = from_short(ref[:16, :])
        moment_units.append(unit(first[0:1], first[1:2]))

    far_units = []
    for ref in far_refs:
        first = from_short(ref[:16, :])
        far_units.append(unit(first[0:1], first[1:2]))

    def body(index, carry):
        first = pl.multiple_of(index * chunk, chunk)
        rows = pl.ds(first, chunk)
        low = low_lanes(chunk)
        decay = modes_ref[0, rows, :]
        log_decay = modes_ref[1, rows, :]
        ring = 1.0 / (1.0 - jnp.exp(GRID * log_decay))
        gain = KERNEL_GAIN * decay / ((1.0 - decay) * (1.0 + decay))
        across_half = jnp.exp(half * log_decay)
        across_cut = jnp.exp((half - 4) * log_decay)
        around = jnp.exp((GRID - 4) * log_decay)
        beside = jnp.exp((GRID - reach_x - span) * log_decay)
        layers = [spectrum[i, rows, :] for i in range(half)]

        even, odd = (
            from_short(ref[pl.ds(pl.multiple_of(top + index * chunk, 16), chunk), :]) * scale
            for ref, top, scale in zip((from_even, from_odd), tops, moment_units)
        )
        left_moments, right_moments = jnp.where(on_left, even, odd), jnp.where(on_left, odd, even)
        border = [border_ref[i, rows, :] for i in range(4)]
        zero = jnp.zeros_like(decay)
        head_sum = border[0]
        for i in range(1, 4):
            head_sum = decay * head_sum + border[i]
        tail_sum = border[3]
        for i in range(2, -1, -1):
            tail_sum = decay * tail_sum + border[i]
        for i in range(4):
            layers[i] = layers[i] + jnp.where(low, border[i], zero)
        for i in range(4):
            place = half - 4 + i
            layers[place] = layers[place] + jnp.where(low, zero, border[i])
        total = own_ref[rows, :] * jnp.exp((GRID - reach_x) * log_decay)
        at = pl.ds(pl.multiple_of(16 + index * chunk, 16), chunk)
        for ref, scale in zip(far_refs, far_units):
            total = total + from_short(ref[at, :]) * scale
        one = jnp.ones_like(decay)
        total = total + left_moments * jnp.where(low, beside, one)
        total = total + right_moments * jnp.where(low, one, beside)
        shared = jnp.where(low, head_sum, tail_sum)
        entering = (swap(total) + around * shared) * ring
        leaving = swap(across_half * entering + across_cut * shared + inner_ref[rows, :])
        run = jnp.where(low, entering, leaving)
        forward_runs = []
        for i in range(half):
            run = decay * run + layers[i]
            forward_runs.append(run)
        run = jnp.where(low, leaving, entering)
        for i in range(half - 1, -1, -1):
            ahead = decay * run
            high, rest = split(gain * (forward_runs[i] + ahead))
            field_high[i, rows, :] = high
            field_low[i, rows, :] = rest
            run = ahead + layers[i]
        return carry

    lax.fori_loop(0, GRID // chunk, body, 0)
    send_fields(outs, flips, reach_y, field_high, field_low, high_ref, low_ref, ready, head)


def inverse(
    spectrum, border, from_even, from_odd, own, inner, fars, table, modes, reach_x, reach_y, flips
):
    half = reach_x // 2
    lanes = 2 * HALF
    body = up_to(half * reach_y, 16)
    shapes = [jax.ShapeDtypeStruct((16 + body, lanes), jnp.int16)] * len(flips)
    shapes += [jax.ShapeDtypeStruct((half, GRID, lanes), BF16)] * 2
    return pl.pallas_call(
        functools.partial(inverse_kernel, reach_x, reach_y, flips, len(fars)),
        in_specs=[whole_vmem()] * (9 + len(fars)),
        out_specs=[whole_vmem()] * len(shapes),
        out_shape=shapes,
        scratch_shapes=[
            pltpu.VMEM((len(flips), body, lanes), F32),
            pltpu.VMEM((16, lanes), F32),
        ],
        compiler_params=params(),
        cost_estimate=cost(2 * half * 256 * 256 * 128, 4 * half * GRID * lanes * 2),
        name="inverse",
    )(spectrum, border, from_even, from_odd, own, inner, *fars, *table, modes)


def inverse_rest_kernel(reach_y, flips, field_high, field_low, high_ref, low_ref, *refs):
    outs, (ready, head) = refs[: len(flips)], refs[len(flips) :]
    send_fields(outs, flips, reach_y, field_high, field_low, high_ref, low_ref, ready, head)


def inverse_rest(field, table, reach_y, flips):
    half = field[0].shape[0]
    lanes = 2 * HALF
    body = up_to(half * reach_y, 16)
    return pl.pallas_call(
        functools.partial(inverse_rest_kernel, reach_y, flips),
        in_specs=[whole_vmem()] * 4,
        out_specs=[whole_vmem()] * len(flips),
        out_shape=[jax.ShapeDtypeStruct((16 + body, lanes), jnp.int16)] * len(flips),
        scratch_shapes=[
            pltpu.VMEM((len(flips), body, lanes), F32),
            pltpu.VMEM((16, lanes), F32),
        ],
        compiler_params=params(),
        cost_estimate=cost(2 * half * 256 * 256 * 128, 4 * half * GRID * lanes * 2),
        name="inverse_rest",
    )(*field, *table)


def sum_rows(values):
    row = lax.broadcasted_iota(jnp.int32, values[0].shape, 0)
    for step in (4, 2, 1):
        low = (row & step) == 0
        paired = []
        for one, other in zip(values[: len(values) // 2], values[len(values) // 2 :]):
            kept = jnp.where(low, one, other)
            moved = jnp.where(low, other, one)
            if step == 4:
                moved = pltpu.roll(moved, 4, 0)
            else:
                moved = jnp.where(low, pltpu.roll(moved, 8 - step, 0), pltpu.roll(moved, step, 0))
            paired.append(kept + moved)
        values = paired
    return values[0]


def z_lines(parts, flips, high_ref, low_ref):
    mine = y_position()
    opened = []
    for part in parts:
        first = from_short(part[:16, :])
        opened.append(from_short(part[16:, :]) * unit(first[0:1], first[1:2]))
    values = split(jnp.concatenate(opened, axis=1))
    pick = lambda ref: jnp.concatenate([ref[mine ^ flip] for flip in flips], axis=0)
    return dot_three(values, (pick(high_ref), pick(low_ref)))


def sample_early_kernel(flips, *refs):
    *parts, high_ref, low_ref, out_ref = refs
    out_ref[...] = z_lines(parts, flips, high_ref, low_ref)


def sample_early(parts, flips, table):
    rows = parts[0].shape[0] - 16
    return pl.pallas_call(
        functools.partial(sample_early_kernel, flips),
        in_specs=[whole_vmem()] * (len(parts) + 2),
        out_specs=whole_vmem(),
        out_shape=jax.ShapeDtypeStruct((rows, 2 * REGION), F32),
        compiler_params=params(),
        cost_estimate=cost(EARLY_FLOPS, 4 * rows * 512),
        name="sample_early",
    )(*parts, *table)


def sample_kernel(last, reach_x, reach_y, flips, place_in, *refs):
    parts = refs[: len(flips)]
    early_ref, high_ref, low_ref, line_ref, own_ref, vector_ref, near_ref, out_ref = refs[
        len(flips) : len(flips) + 8
    ]
    flat, field, sums, place_ref, sem = refs[len(flips) + 8 :]
    copy = pltpu.make_async_copy(place_in, place_ref, sem)
    copy.start()
    half_rows = reach_x * reach_y // 2
    both = early_ref[...] + z_lines(parts, flips, high_ref, low_ref)
    flat[:half_rows, :] = both[:half_rows, :REGION]
    flat[half_rows : 2 * half_rows, :] = both[:half_rows, REGION:]
    for x in range(reach_x):
        layer = flat[x * reach_y : (x + 1) * reach_y, :]
        for row in pair_rows(x, reach_x, reach_y):
            field[pl.ds(row, reach_y, stride=2), :] = layer
    count = place_ref.shape[1]

    def body(group, carry):
        for eight in range(0, GROUP, 8):
            totals = []
            for local in range(eight, eight + 8):
                panel = group * GROUP + local
                row = place_ref[0, panel]
                first = pl.multiple_of(panel * 16, 16)
                totals.append(
                    field[pl.ds(row, 8), :] * line_ref[pl.ds(first, 8), :]
                    + field[pl.ds(row + 2 * reach_y, 8), :] * line_ref[pl.ds(first + 8, 8), :]
                )
            sums[pl.ds(pl.multiple_of(group * GROUP + eight, 8), 8), :] = sum_rows(totals)
        return carry

    copy.wait()
    lax.fori_loop(0, count // GROUP, body, 0)
    first, rest = split(sums[...])
    second, third = split(sums[...] - first.astype(F32))
    across = lambda values: lax.dot_general(
        jnp.ones((16, REGION), BF16),
        values,
        (((1,), (1,)), ((), ())),
        preferred_element_type=F32,
    )
    sampled = across(first) + (across(second) + across(third))
    for block in range(count // BLOCK):
        lane = slice(block * BLOCK, (block + 1) * BLOCK)
        row = slice(block, block + 1)
        vector = vector_ref[row, :]
        image = jnp.where(own_ref[row, :] == 1, 0.0, 0.5 * vector) + sampled[:1, lane]
        image = image + near_ref[row, :]
        if last:
            out_ref[0:1, lane] = vector
            out_ref[1:2, lane] = image
        else:
            out_ref[row, :] = image


def sample(last, places, parts, flips, early, table, lines, flag, vector, near, reach_x, reach_y):
    count = places.shape[1]
    blocks = count // BLOCK
    shape = (2, count) if last else (blocks, BLOCK)
    return pl.pallas_call(
        functools.partial(sample_kernel, last, reach_x, reach_y, flips),
        in_specs=[anywhere()] + [whole_vmem()] * (len(parts) + 7),
        out_specs=whole_vmem(),
        out_shape=jax.ShapeDtypeStruct(shape, F32),
        scratch_shapes=[
            pltpu.VMEM((reach_x * reach_y + SPARE, REGION), F32),
            pltpu.VMEM((pair_count(reach_x, reach_y), REGION), F32),
            pltpu.VMEM((count, REGION), F32),
            pltpu.SMEM((2, count), jnp.int32),
            pltpu.SemaphoreType.DMA,
        ],
        compiler_params=params(),
        cost_estimate=cost(reach_x * reach_y * 256 * 512, 4 * 16 * count * REGION),
        name="sample",
    )(
        places,
        *parts,
        early,
        *table,
        lines,
        flag.reshape(blocks, BLOCK),
        vector.reshape(blocks, BLOCK),
        near,
    )


def near_kernel(slots, blocks, place_ref, target_ref, *refs):
    even_ref, odd_ref, peers_ref, tile_ref = refs[:4]
    out_ref, held = refs[-2:]
    count = peers_ref.shape[0]
    held[count : 2 * count, :] = peers_ref[...]
    on_left = lax.axis_index("wide") & 1
    for side, ref in ((1 - on_left, even_ref), (on_left, odd_ref)):
        top = from_short(ref[...])
        for piece in range(count // blocks):
            at = 6 + 2 * piece * blocks
            held[pl.ds(side * (2 * count) + piece * blocks, blocks), :] = decode_rounded(
                top[at : at + blocks], top[at + blocks : at + 2 * blocks]
            )
    out_ref[...] = jnp.zeros_like(out_ref)
    for slot in range(slots):
        picked = held[pl.ds(place_ref[slot], 1), :]
        picked = jnp.broadcast_to(picked, (16, BLOCK)).astype(BF16)
        product = lax.dot_general(
            picked,
            tile_ref[slot],
            (((1,), (1,)), ((), ())),
            preferred_element_type=F32,
        )
        target = pl.ds(target_ref[slot], 1)
        out_ref[target, :] = out_ref[target, :] + product[:1]


def near_field(places, targets, from_even, from_odd, peers, tiles, blocks, out_rows, awaited):
    slots = tiles.shape[0]
    head = up_to(6 + 2 * peers.shape[0], 16)
    constant = lambda shape: pl.BlockSpec(shape, lambda i: (0,) * len(shape))
    return pl.pallas_call(
        functools.partial(near_kernel, slots, blocks),
        grid=(1,),
        in_specs=[
            in_smem(),
            in_smem(),
            constant((head, BLOCK)),
            constant((head, BLOCK)),
            constant(peers.shape),
            constant(tiles.shape),
        ]
        + [anywhere()] * len(awaited),
        out_specs=constant((out_rows, BLOCK)),
        out_shape=jax.ShapeDtypeStruct((out_rows, BLOCK), F32),
        scratch_shapes=[pltpu.VMEM((3 * peers.shape[0] + SPARE, BLOCK), F32)],
        compiler_params=params(),
        cost_estimate=cost(2 * slots * 16 * BLOCK * BLOCK, 2 * slots * BLOCK * BLOCK),
        name="near_field",
    )(places, targets, from_even, from_odd, peers, tiles, *awaited)


def shards(
    density,
    surface_flag,
    stencil_base,
    sample_weights,
    dipole_weights,
    near_target,
    near_source,
    near_tiles,
):
    x_count = lax.axis_size("wide")
    y_count = lax.axis_size(Y_AXES)
    y_index = lax.axis_index(Y_AXES)
    pair = lax.axis_size("pair")
    span_x = REGION // x_count
    span_y = REGION // y_count
    reach_x = span_x + 4
    reach_y = span_y + 4
    count = density.shape[0]
    blocks = count // BLOCK

    z_forward, z_inverse, y_forward, y_inverse, modes = tables(y_count, pair, span_y)
    modes = lax.dynamic_index_in_dim(jnp.asarray(modes), y_index, 0, keepdims=False)

    neighbour = near_source // blocks
    flip = (y_index + neighbour % 3 - 1) ^ y_index
    sources = ((neighbour // 3) * y_count + flip) * blocks + near_source % blocks
    out_rows = up_to(blocks + 1, 8)
    live = near_target >= 0
    sources = jnp.where(live, sources, 0)
    targets = jnp.where(live, near_target, out_rows - 1)

    swaps = lambda pairs: [(i, j) for i, j in pairs] + [(j, i) for i, j in pairs]
    even_swap = swaps([(i, i + 1) for i in range(0, x_count - 1, 2)])
    odd_swap = swaps([(i, i + 1) for i in range(1, x_count - 1, 2)])
    far_flips = list(range(2, x_count, 2))

    first, inside, local = list(range(pair, y_count)), list(range(1, pair)), [0]
    same_core = list(range(0, y_count, pair))
    other_core = [flip for flip in range(y_count) if flip not in same_core]

    def turned(sent, then):
        arrived = [None] * y_count
        for flip, part in zip(first + inside + local, list(sent) + list(then)):
            swap_pairs = [(i, i ^ flip) for i in range(y_count)]
            arrived[flip] = part if flip == 0 else lax.ppermute(part, Y_AXES, swap_pairs)
        return arrived

    def chosen(parts, flips):
        return [parts[flip] for flip in flips]

    def convolve_and_sample(last, vector, sent, both, table, places, sample_lines, awaited):
        then = [part for flips in (inside, local) for part in spread_rest(vector, both, table, flips)]
        arrived = turned(sent, then)
        early, edges = forward_early(chosen(arrived, same_core), y_forward, reach_x, reach_y)
        spectrum, even_message, layers, odd_message, own, peers, inner = forward(
            arrived, early, edges, y_forward, modes, reach_x, reach_y, blocks, awaited
        )
        from_even = lax.ppermute(even_message, "wide", even_swap)
        from_odd = lax.ppermute(odd_message, "wide", odd_swap)
        even_layers = lax.ppermute(layers, "wide", even_swap)
        fars = [
            lax.ppermute(message, "wide", [(i, i ^ flip) for i in range(x_count)])
            for flip, message in zip(
                far_flips, pair_messages(own, from_even, modes, reach_x, far_flips)
            )
        ]
        *sent, high, low = inverse(
            spectrum,
            borders(even_layers, from_odd, y_forward, reach_y, y_count),
            from_even,
            from_odd,
            own,
            inner,
            fars,
            y_inverse,
            modes,
            reach_x,
            reach_y,
            first,
        )
        then = [
            part
            for flips in (inside, local)
            for part in inverse_rest((high, low), y_inverse, reach_y, flips)
        ]
        near_part = near_field(
            sources, targets, even_layers, from_odd, peers, near_tiles, blocks, out_rows, then[:1]
        )
        arrived = turned(sent, then)
        image = sample(
            last,
            places,
            chosen(arrived, other_core),
            other_core,
            sample_early(chosen(arrived, same_core), same_core, z_inverse),
            z_inverse,
            sample_lines,
            surface_flag,
            vector,
            near_part,
            reach_x,
            reach_y,
        )
        return image, near_part

    raw = (stencil_base, surface_flag, sample_weights, dipole_weights)
    *sent, wide_high, wide_low, source_coeff, places, vector, high, low = spread(
        density, z_forward, None, raw, reach_x, reach_y, first
    )
    z_forward = (high, low)
    sample_lines = place_sample_lines(places, sample_weights)
    vector, near_part = convolve_and_sample(
        False,
        vector,
        sent,
        (wide_high, wide_low),
        z_forward,
        places,
        sample_lines,
        [sample_lines],
    )
    source_lines = place_lines(places, source_coeff, [near_part])
    *sent, wide_high, wide_low = spread(
        vector.reshape(-1), z_forward, (places, source_lines), None, reach_x, reach_y, first
    )
    both_images, _ = convolve_and_sample(
        True, vector, sent, (wide_high, wide_low), z_forward, places, sample_lines, []
    )
    return both_images


def solution(mesh):
    panels = P(("groups",) + ALL_AXES)
    columns = P(None, ("groups",) + ALL_AXES)
    in_specs = (
        panels,
        panels,
        columns,
        columns,
        columns,
        panels,
        panels,
        P(("groups",) + ALL_AXES, None, None),
    )
    return jax.shard_map(
        shards, mesh=mesh, in_specs=in_specs, out_specs=columns, check_vma=False
    )
```

```python
import functools
import math

import jax
import jax.numpy as jnp
import numpy as np
from jax import lax
from jax.experimental import pallas as pl
from jax.experimental.pallas import tpu as pltpu
from jax.sharding import PartitionSpec as P

GRID = 256
REGION = 128
BLOCK = 128
HALF = 64
KERNEL_GAIN = 4.0
SCREEN = 1.0 / 1024.0
LN2 = math.log(2.0)
SPARE = 16
Y_AXES = ("narrow", "pair")
ALL_AXES = ("wide", "narrow", "pair")
F32 = jnp.float32
BF16 = jnp.bfloat16
VMEM_LIMIT = 24 * 1024 * 1024
START_LIMIT = VMEM_LIMIT
EARLY_FLOPS = 5 * 10**9
GROUP = 32
CHAINS = 2


def cas(angles):
    return np.cos(angles) + np.sin(angles)


def up_to(count, multiple):
    return -(-count // multiple) * multiple


def low_lanes(rows):
    return lax.broadcasted_iota(jnp.int32, (rows, 2 * HALF), 1) < HALF


def swap(values):
    return pltpu.roll(values, HALF, 1)


def split(values):
    high = values.astype(BF16)
    return high, (values - high.astype(F32)).astype(BF16)


def dot(left, right):
    return jnp.dot(left, right, preferred_element_type=F32)


def dot_three(left, right):
    return dot(left[0], right[0]) + (dot(left[0], right[1]) + dot(left[1], right[0]))


def params():
    return pltpu.CompilerParams(vmem_limit_bytes=VMEM_LIMIT)


def whole_vmem():
    return pl.BlockSpec(memory_space=pltpu.VMEM)


def anywhere():
    return pl.BlockSpec(memory_space=pl.ANY)


def in_smem():
    return pl.BlockSpec(memory_space=pltpu.SMEM)


def cost(flops, moved):
    return pl.CostEstimate(flops=flops, bytes_accessed=moved, transcendentals=0)


def full_scale(exponent, fraction):
    return fraction * jnp.exp(exponent * LN2) * (1.0 / 1024.0)


def fit_scale(largest):
    largest = jnp.maximum(largest, 1e-30)
    exponent = jnp.floor(jnp.log(largest) * (1.0 / LN2))
    fraction = jnp.ceil(largest * jnp.exp(-exponent * LN2) * 1024.0) + 1.0
    return exponent, fraction


def to_short(values):
    return values.astype(jnp.int32).astype(jnp.int16)


def from_short(values):
    return values.astype(jnp.int32).astype(F32)


def quantize(values, exponent, fraction):
    return to_short(jnp.round(values * (32767.0 / full_scale(exponent, fraction))))


def unit(exponent, fraction):
    return full_scale(exponent, fraction) * (1.0 / 32767.0)


def encode_rounded(values):
    rounded = values.astype(BF16).astype(F32)
    size = jnp.maximum(jnp.abs(rounded), 1e-30)
    exponent = jnp.floor(jnp.log(size) * (1.0 / LN2))
    return jnp.round(rounded * jnp.exp((10.0 - exponent) * LN2)), exponent


def decode_rounded(mantissa, exponent):
    return (mantissa * jnp.exp((exponent - 10.0) * LN2)).astype(BF16).astype(F32)


def send_piece(out, head, values):
    exponent, fraction = fit_scale(jnp.max(jnp.abs(values), axis=0, keepdims=True))
    head[0:1, :] = exponent
    head[1:2, :] = fraction
    top = head.shape[0]
    out[:top, :] = to_short(head[...])
    out[top:, :] = quantize(values, exponent, fraction)


def y_position():
    return lax.axis_index("narrow") * lax.axis_size("pair") + lax.axis_index("pair")


def halves(table):
    high = table.astype(jnp.bfloat16)
    return high, (table - high.astype(np.float64)).astype(jnp.bfloat16)


def tables(y_count, pair, span_y):
    depth = GRID // y_count
    reach = span_y + 4
    waves = np.arange(GRID)
    step = 2.0 * np.pi / GRID
    z_table = cas(step * np.outer(np.arange(REGION), waves))
    z_forward = np.zeros((y_count, 2 * REGION, 2 * HALF))
    z_inverse = np.zeros((y_count, 2 * HALF, 2 * REGION))
    symbols = 4.0 * np.sin(np.pi * waves / GRID) ** 2
    shift = np.full((y_count, GRID, 2 * HALF), 1.0)
    y_forward = np.zeros((GRID, y_count, up_to(reach, 8)))
    y_inverse = np.zeros((y_count, up_to(reach, 16), GRID))
    for block in range(y_count):
        mine = z_table[:, block * depth : (block + 1) * depth]
        for half in range(2):
            rows = slice(half * REGION, (half + 1) * REGION)
            lanes = slice(half * HALF, half * HALF + depth)
            z_forward[block, rows, lanes] = mine
            z_inverse[block, lanes, rows] = mine.T / GRID
            shift[block, :, lanes] = (
                SCREEN + symbols[:, None] + symbols[None, block * depth : (block + 1) * depth]
            )
        cells = block * span_y - 2 + np.arange(reach)
        y_table = cas(step * np.outer(waves, cells))
        y_forward[:, block, :reach] = y_table
        y_inverse[block, :reach] = y_table.T / GRID
    y_forward = y_forward.reshape(GRID, y_count // pair, pair, -1).transpose(2, 0, 1, 3)
    y_forward = halves(y_forward.reshape(pair, GRID, -1))
    y_forward = np.concatenate([y_forward[0], y_forward[0], y_forward[1]], axis=2)
    root = np.sqrt(shift * (shift + 4.0))
    decay = 2.0 / (2.0 + shift + root)
    log_decay = np.log(decay)
    modes = np.stack([decay, log_decay], axis=1).astype(np.float32)
    return (
        halves(z_forward),
        halves(z_inverse),
        y_forward,
        halves(y_inverse),
        modes,
    )


def mixing_matrix():
    place = lax.broadcasted_iota(jnp.int32, (4 * BLOCK, 4 * BLOCK), 0)
    lane = lax.broadcasted_iota(jnp.int32, (4 * BLOCK, 4 * BLOCK), 1)
    return jnp.where(lane == 4 * (place % BLOCK) + place // BLOCK, 1.0, 0.0).astype(BF16)


def weave(tiles, mixing, out):
    weights = jnp.concatenate([jnp.concatenate(tile, axis=1) for tile in tiles], axis=0)
    first, rest = split(weights)
    second, third = split(weights - first.astype(F32))
    woven = dot(first, mixing) + (dot(second, mixing) + dot(third, mixing))
    for tile in range(len(tiles)):
        for part in range(BLOCK // GROUP):
            at = (tile * (BLOCK // GROUP) + part) * 16
            lanes = slice(part * BLOCK, (part + 1) * BLOCK)
            for a in range(4):
                row = tile * 16 + 4 * a
                out[pl.ds(at + 8 * (a // 2) + a % 2, 4, stride=2), :] = woven[row : row + 4, lanes]


def by_depth(ref):
    return [ref[pl.ds(depth, 16, stride=4), :] for depth in range(4)]


def pair_rows(x, reach_x, reach_y):
    even = (x // 2) * 2 * reach_y + x % 2
    if x == 0 or x == reach_x - 1:
        return [even]
    return [even, reach_x * reach_y + ((x - 1) // 2) * 2 * reach_y + (x - 1) % 2]


def pair_count(reach_x, reach_y):
    return (2 * reach_x - 2) * reach_y + SPARE


def in_window(lanes, depth):
    return ((lanes - depth) & -4) == 0


def add_panels(reach, woven, vector_ref, place_ref, weight_ref, grids):
    lanes = lax.broadcasted_iota(jnp.int32, (8, REGION), 1)

    def body(group, carry):
        at = pl.multiple_of(group * 16, 16)
        coeff = [weight_ref[pl.ds(at + 8 * q, 8), :] for q in range(2)] if woven else None
        for local in range(GROUP):
            panel = group * GROUP + local
            grid = grids[local % len(grids)]
            row = place_ref[0, panel]
            value = vector_ref[panel]
            if woven:
                depth = place_ref[1, panel]
                shift = (depth - 4 * local) & (REGION - 1)
                value = jnp.where(in_window(lanes, depth), value, 0.0)
                lines = [pltpu.roll(coeff[q], shift, 1) for q in range(2)]
            else:
                first = pl.multiple_of(panel * 16, 16)
                lines = [weight_ref[pl.ds(first + 8 * q, 8), :] for q in range(2)]
            places = [pl.ds(row, 8), pl.ds(row + 2 * reach, 8)]
            held = [grid[place, :] for place in places]
            for q in range(2):
                grid[places[q], :] = held[q] + lines[q] * value
        return carry

    lax.fori_loop(0, vector_ref.shape[0] // GROUP, body, 0)


def send_pieces(outs, flips, head, rounded, both, high_ref, low_ref):
    blocks = rounded.shape[0]
    mantissa, exponent = encode_rounded(rounded)
    head[...] = jnp.zeros_like(head)
    head[2 : 2 + blocks, :] = mantissa
    head[2 + blocks : 2 + 2 * blocks, :] = exponent
    mine = y_position()
    for at in range(0, len(flips), 2):
        pick = lambda ref: jnp.concatenate([ref[mine ^ flip] for flip in flips[at : at + 2]], axis=1)
        result = dot_three(both, (pick(high_ref), pick(low_ref)))
        for i, out in enumerate(outs[at : at + 2]):
            send_piece(out, head, result[:, i * 2 * HALF : (i + 1) * 2 * HALF])


def spread_grid(reach_x, reach_y, rounded, tables, outs, flips, wides, head, total, grids):
    for x in range(reach_x):
        parts = [
            grid[pl.ds(row, reach_y, stride=2), :]
            for row in pair_rows(x, reach_x, reach_y)
            for grid in grids
        ]
        total[x * reach_y : (x + 1) * reach_y, :] = sum(parts[1:], parts[0])
    half = reach_x * reach_y // 2
    both = jnp.concatenate([total[:half, :], total[half : 2 * half, :]], axis=1)
    extra = wides[0].shape[0] - half
    if extra:
        both = jnp.concatenate([both, jnp.zeros((extra, 2 * REGION), F32)], axis=0)
    both = split(both)
    for wide, values in zip(wides, both):
        wide[...] = values
    send_pieces(outs, flips, head, rounded, both, *tables)


def start_kernel(reach_x, reach_y, flips, *refs):
    vector_in, *remote = refs[:8]
    refs = refs[8:]
    outs, refs = refs[: len(flips)], refs[len(flips) :]
    wides, (weight_ref, places_out), refs = refs[:2], refs[2:4], refs[4:]
    rounded, high, low, stencil, flag, samples, dipoles, vector_ref = refs[:8]
    place_ref, sems, head, total = refs[8:12]
    grids = refs[12:]
    tiles = samples.shape[0]
    copies = []
    fetch = lambda source, target: copies.append(
        pltpu.make_async_copy(source, target, sems.at[len(copies)])
    )
    rounded_in, high_in, low_in, stencil_in, flag_in, sample_in, dipole_in = remote
    fetch(stencil_in, stencil)
    fetch(flag_in, flag)
    fetch(vector_in, vector_ref)
    for tile in range(tiles):
        lanes = pl.ds(tile * BLOCK, BLOCK)
        fetch(sample_in.at[:, lanes], samples.at[tile, pl.ds(0, 64)])
        fetch(dipole_in.at[:, lanes], dipoles.at[tile, pl.ds(0, 64)])
    needed_first = len(copies)
    fetch(rounded_in, rounded)
    fetch(high_in, high)
    fetch(low_in, low)
    for copy in copies:
        copy.start()
    for grid in grids:
        grid[...] = jnp.zeros_like(grid)
    mixing = mixing_matrix()
    copies[0].wait()
    span_x, span_y = reach_x - 4, reach_y - 4
    local_x = stencil[0:1, :] - (lax.axis_index("wide") * span_x - 2)
    local_y = stencil[1:2, :] - (y_position() * span_y - 2)
    odd = local_x & 1
    places_out[0:1, :] = odd * (reach_x * reach_y) + (local_x >> 1) * (2 * reach_y) + 2 * local_y
    places_out[1:2, :] = stencil[2:3, :]
    to_scalar = pltpu.make_async_copy(places_out, place_ref, sems.at[len(copies)])
    to_scalar.start()
    for copy in copies[1:needed_first]:
        copy.wait()
    sources = []
    for tile in range(tiles):
        charged = flag[:, tile * BLOCK : (tile + 1) * BLOCK] == 1
        pairs = zip(by_depth(samples.at[tile]), by_depth(dipoles.at[tile]))
        sources.append([jnp.where(charged, -sample, dipole) for sample, dipole in pairs])
    weave(sources, mixing, weight_ref)
    to_scalar.wait()
    add_panels(reach_y, True, vector_ref, place_ref, weight_ref, grids)
    for copy in copies[needed_first:]:
        copy.wait()
    spread_grid(
        reach_x, reach_y, rounded[...], (high, low), outs, flips, wides, head, total, grids
    )


def spread_kernel(reach_x, reach_y, flips, *refs):
    vector_in, place_in, rounded_ref, high_ref, low_ref, line_ref = refs[:6]
    refs = refs[6:]
    outs, wides, (vector_ref, place_ref, sems, head, total), grids = (
        refs[: len(flips)],
        refs[len(flips) : len(flips) + 2],
        refs[len(flips) + 2 : len(flips) + 7],
        refs[len(flips) + 7 :],
    )
    copies = [
        pltpu.make_async_copy(vector_in, vector_ref, sems.at[0]),
        pltpu.make_async_copy(place_in, place_ref, sems.at[1]),
    ]
    for copy in copies:
        copy.start()
    for grid in grids:
        grid[...] = jnp.zeros_like(grid)
    for copy in copies:
        copy.wait()
    add_panels(reach_y, False, vector_ref, place_ref, line_ref, grids)
    spread_grid(
        reach_x,
        reach_y,
        rounded_ref[...],
        (high_ref, low_ref),
        outs,
        flips,
        wides,
        head,
        total,
        grids,
    )


def spread(vector, table, placed, raw, reach_x, reach_y, flips):
    count = vector.shape[0]
    half = reach_x * reach_y // 2
    blocks = count // BLOCK
    top = up_to(2 + 2 * blocks, 16)
    lanes = 2 * HALF
    body = up_to(half, 16)
    woven = (count // GROUP * 16 + SPARE, BLOCK)
    out_shapes = [jax.ShapeDtypeStruct((top + body, lanes), jnp.int16)] * len(flips)
    out_shapes += [jax.ShapeDtypeStruct((body, 2 * REGION), BF16)] * 2
    rounded = vector.reshape(blocks, BLOCK)
    work = [
        pltpu.VMEM((top, lanes), F32),
        pltpu.VMEM((reach_x * reach_y + SPARE, REGION), F32),
    ] + [pltpu.VMEM((pair_count(reach_x, reach_y), REGION), F32)] * CHAINS
    if placed is None:
        stencil, flag, sample, dipole = raw
        operands = [vector, rounded, *table, stencil, flag.reshape(1, -1), sample, dipole]
        operands = [pltpu.with_memory_space_constraint(value, pltpu.HBM) for value in operands]
        in_specs = [pl.BlockSpec(memory_space=pltpu.HBM)] * 8
        out_shapes += [jax.ShapeDtypeStruct(woven, F32)]
        out_shapes += [jax.ShapeDtypeStruct((2, count), jnp.int32)]
        out_shapes += [jax.ShapeDtypeStruct(rounded.shape, F32)]
        out_shapes += [jax.ShapeDtypeStruct(values.shape, BF16) for values in table]
        tiled = pltpu.VMEM((blocks, 64 + SPARE, BLOCK), F32)
        work = [
            pltpu.VMEM(stencil.shape, jnp.int32),
            pltpu.VMEM((1, count), jnp.int32),
            tiled,
            tiled,
            pltpu.SMEM((count,), F32),
            pltpu.SMEM((2, count), jnp.int32),
            pltpu.SemaphoreType.DMA((7 + 2 * blocks,)),
        ] + work
    else:
        operands = [vector, placed[0], rounded, *table, placed[1]]
        in_specs = [anywhere()] * 2 + [whole_vmem()] * 4
        work = [
            pltpu.SMEM((count,), F32),
            pltpu.SMEM((2, count), jnp.int32),
            pltpu.SemaphoreType.DMA((2,)),
        ] + work
    return pl.pallas_call(
        functools.partial(
            start_kernel if placed is None else spread_kernel, reach_x, reach_y, flips
        ),
        in_specs=in_specs,
        out_specs=[whole_vmem()] * len(out_shapes),
        out_shape=out_shapes,
        scratch_shapes=work,
        compiler_params=pltpu.CompilerParams(
            vmem_limit_bytes=START_LIMIT if placed is None else VMEM_LIMIT
        ),
        cost_estimate=cost(2 * half * 256 * 512, 4 * 16 * count * REGION),
        name="start" if placed is None else "spread",
    )(*operands)


def spread_rest_kernel(flips, rounded_ref, wide_high, wide_low, high_ref, low_ref, *refs):
    outs, head = refs[:-1], refs[-1]
    both = (wide_high[...], wide_low[...])
    send_pieces(outs, flips, head, rounded_ref[...], both, high_ref, low_ref)


def spread_rest(rounded, both, table, flips):
    blocks = rounded.shape[0]
    top = up_to(2 + 2 * blocks, 16)
    shape = (top + both[0].shape[0], 2 * HALF)
    return pl.pallas_call(
        functools.partial(spread_rest_kernel, flips),
        in_specs=[whole_vmem()] * 5,
        out_specs=[whole_vmem()] * len(flips),
        out_shape=[jax.ShapeDtypeStruct(shape, jnp.int16)] * len(flips),
        scratch_shapes=[pltpu.VMEM((top, 2 * HALF), F32)],
        compiler_params=params(),
        cost_estimate=cost(2 * shape[0] * 256 * 256 * 3, 4 * shape[0] * 512),
        name="spread_rest",
    )(rounded, *both, *table)


def lines_kernel(place_ref, coeff_ref, *refs):
    out_ref = refs[-1]
    lanes = lax.broadcasted_iota(jnp.int32, (8, REGION), 1)

    def body(group, carry):
        at = pl.multiple_of(group * 16, 16)
        coeff = [coeff_ref[pl.ds(at + 8 * q, 8), :] for q in range(2)]
        for local in range(GROUP):
            panel = group * GROUP + local
            depth = place_ref[1, panel]
            shift = (depth - 4 * local) & (REGION - 1)
            inside = in_window(lanes, depth)
            for q in range(2):
                first = pl.multiple_of(panel * 16 + 8 * q, 8)
                out_ref[pl.ds(first, 8), :] = jnp.where(inside, pltpu.roll(coeff[q], shift, 1), 0.0)
        return carry

    lax.fori_loop(0, place_ref.shape[1] // GROUP, body, 0)


def sample_lines_kernel(tiles, place_ref, *refs):
    out_ref, coeff, held = refs[-3:]
    for tile, ref in enumerate(refs[:tiles]):
        held[tile, :64, :] = ref[...]
    weave([by_depth(held.at[tile]) for tile in range(tiles)], mixing_matrix(), coeff)
    lines_kernel(place_ref, coeff, out_ref)


def place_sample_lines(places, sample):
    count = places.shape[1]
    blocks = count // BLOCK
    tile = lambda t: pl.BlockSpec((64, BLOCK), lambda i: (0, t))
    shape = (count * 16, REGION)
    return pl.pallas_call(
        functools.partial(sample_lines_kernel, blocks),
        grid=(1,),
        in_specs=[in_smem()] + [tile(t) for t in range(blocks)],
        out_specs=pl.BlockSpec(shape, lambda i: (0, 0)),
        out_shape=jax.ShapeDtypeStruct(shape, F32),
        scratch_shapes=[
            pltpu.VMEM((count // GROUP * 16 + SPARE, BLOCK), F32),
            pltpu.VMEM((blocks, 64 + SPARE, BLOCK), F32),
        ],
        compiler_params=params(),
        cost_estimate=cost(16 * count * REGION, 4 * 16 * count * REGION),
        name="place_sample_lines",
    )(places, *[sample] * blocks)


def place_lines(places, coeff, awaited):
    count = places.shape[1]
    shape = (count * 16, REGION)
    return pl.pallas_call(
        lines_kernel,
        in_specs=[in_smem(), whole_vmem()] + [anywhere()] * len(awaited),
        out_specs=whole_vmem(),
        out_shape=jax.ShapeDtypeStruct(shape, F32),
        compiler_params=params(),
        cost_estimate=cost(16 * count * REGION, 4 * 16 * count * REGION),
        name="place_lines",
    )(places, coeff, *awaited)


def put_edges(opened, reach_x, reach_y, edges, first):
    half = reach_x // 2
    low = low_lanes(reach_y)
    layer = lambda i: opened[i * reach_y : (i + 1) * reach_y, :]
    for two in range(2):
        place = slice(first + two * reach_y, first + (two + 1) * reach_y)
        edges[0, place, :] = jnp.where(low, layer(2 * two), swap(layer(2 * two + 1)))
        last = half - 4 + 2 * two
        edges[1, place, :] = jnp.where(low, swap(layer(last)), layer(last + 1))


def stack_layers(layers, at, reach_y, stacked):
    tall = stacked.shape[0] // len(layers)
    place = at * up_to(reach_y, 8)
    for i, layer in enumerate(layers):
        stacked[pl.ds(pl.multiple_of(i * tall + place, 8), reach_y), :] = layer


def stack_pieces(parts, reach_x, reach_y, top, opened, stacked, edges, places):
    chip = lax.axis_index("narrow")
    for flip, (part, place) in enumerate(zip(parts, places)):
        first = from_short(part[:top, :])
        opened[...] = from_short(part[top:, :]) * unit(first[0:1], first[1:2])
        layers = [opened[i * reach_y : (i + 1) * reach_y, :] for i in range(reach_x // 2)]
        stack_layers(layers, chip ^ flip, reach_y, stacked)
        put_edges(opened, reach_x, reach_y, edges, place * 2 * reach_y)


def transform_pieces(table, stacked, before, spectrum):
    half = spectrum.shape[0]
    tall = stacked.shape[0] // half

    def tripled(values):
        high, low = split(values)
        return jnp.concatenate([high, low, high], axis=0)

    for i in range(0, half, 2):
        places = range(i, min(i + 2, half))
        held = jnp.concatenate([stacked[j * tall : (j + 1) * tall, :] for j in places], axis=1)
        result = dot(table, tripled(held))
        for j in places:
            made = result[:, (j - i) * 2 * HALF : (j - i + 1) * 2 * HALF]
            spectrum[j] = made if before is None else before[j] + made


def forward_early_kernel(reach_x, reach_y, chips, *refs):
    parts = refs[:chips]
    table_ref, spectrum, edges, opened, stacked = refs[chips:]
    top = parts[0].shape[0] - opened.shape[0]
    stacked[...] = jnp.zeros_like(stacked)
    stack_pieces(parts, reach_x, reach_y, top, opened, stacked, edges, range(chips))
    transform_pieces(table_ref[lax.axis_index("pair")], stacked, None, spectrum)


def stacking_scratch(chips, reach_x, reach_y):
    half = reach_x // 2
    return [
        pltpu.VMEM((up_to(half * reach_y, 16), 2 * HALF), F32),
        pltpu.VMEM((half * chips * up_to(reach_y, 8), 2 * HALF), F32),
    ]


def forward_early(parts, table, reach_x, reach_y):
    half = reach_x // 2
    chips = len(parts)
    return pl.pallas_call(
        functools.partial(forward_early_kernel, reach_x, reach_y, chips),
        in_specs=[whole_vmem()] * (chips + 1),
        out_specs=[whole_vmem()] * 2,
        out_shape=[
            jax.ShapeDtypeStruct((half, GRID, 2 * HALF), F32),
            jax.ShapeDtypeStruct((2, chips * 2 * reach_y + SPARE, 2 * HALF), F32),
        ],
        scratch_shapes=stacking_scratch(chips, reach_x, reach_y),
        compiler_params=params(),
        cost_estimate=cost(EARLY_FLOPS, 4 * half * GRID * 2 * HALF * 2),
        name="forward_early",
    )(*parts, table)


def forward_kernel(reach_x, reach_y, blocks, pieces, awaited, *refs):
    parts = refs[:pieces]
    early_ref, early_edges, table_ref, modes_ref = refs[pieces : pieces + 4]
    refs = refs[pieces + 4 + awaited :]
    spectrum, even_out, layers_out, odd_out, own_out, peers_out, inner_out, *refs = refs
    opened, stacked, edges, slabs, head = refs
    half = reach_x // 2
    pair = lax.axis_size("pair")
    top = parts[0].shape[0] - opened.shape[0]
    stacked[...] = jnp.zeros_like(stacked)
    head[...] = jnp.zeros_like(head)
    for piece in range(pieces):
        first = from_short(parts[piece][:top, :])
        mantissa, exponent = first[2 : 2 + blocks], first[2 + blocks : 2 + 2 * blocks]
        peers_out[piece * blocks : (piece + 1) * blocks, :] = decode_rounded(mantissa, exponent)
        at = 6 + 2 * piece * blocks
        head[at : at + blocks, :] = mantissa
        head[at + blocks : at + 2 * blocks, :] = exponent
    rows = 2 * reach_y
    for chip in range(pieces // pair):
        place = chip * pair * rows
        edges[:, place : place + rows, :] = early_edges[:, chip * rows : (chip + 1) * rows, :]
    before = early_ref
    for core in range(1, pair):
        places = range(core, pieces, pair)
        stack_pieces(parts[core::pair], reach_x, reach_y, top, opened, stacked, edges, places)
        transform_pieces(table_ref[lax.axis_index("pair") ^ core], stacked, before, spectrum)
        before = spectrum

    chunk = 256

    def body(index, largest):
        rows = pl.ds(pl.multiple_of(index * chunk, chunk), chunk)
        low = low_lanes(chunk)
        decay = modes_ref[y_position(), 0, rows, :]
        log_decay = modes_ref[y_position(), 1, rows, :]
        across_half = jnp.exp(half * log_decay)
        across_cut = jnp.exp((half - 4) * log_decay)
        layers = [spectrum[i, rows, :] for i in range(half)]
        run = layers[0]
        cut_right = run
        for i in range(1, half):
            run = decay * run + layers[i]
            if i == half - 5:
                cut_right = run
        right = run
        run = layers[half - 1]
        cut_left = run
        for i in range(half - 2, -1, -1):
            run = decay * run + layers[i]
            if i == 4:
                cut_left = run
        left = run
        inner_out[rows, :] = jnp.where(low, right, left)
        swapped_right, swapped_left = swap(right), swap(left)
        own = jnp.where(low, left + across_half * swapped_left, right + across_half * swapped_right)
        own_out[rows, :] = own
        made = [
            jnp.where(low, own, cut_right + across_cut * swapped_right),
            jnp.where(low, cut_left + across_cut * swapped_left, own),
        ]
        for slab, values in enumerate(made):
            slabs[slab, rows, :] = values
        return tuple(
            jnp.maximum(old, jnp.max(jnp.abs(values).reshape(chunk // 8, 8, 2 * HALF), axis=0))
            for old, values in zip(largest, made)
        )

    zero = jnp.zeros((8, 2 * HALF), F32)
    largest = lax.fori_loop(0, GRID // chunk, body, (zero,) * 2)
    top = head.shape[0]
    low = low_lanes(GRID // 2)
    upper, lower = own_out[: GRID // 2, :], own_out[GRID // 2 :, :]
    packed = [jnp.where(low, swap(upper), lower), jnp.where(low, upper, swap(lower))]

    def send(out, first, parts):
        place = first
        for index, (values, most) in enumerate(parts):
            exponent, fraction = fit_scale(jnp.max(most, axis=0, keepdims=True))
            head[2 * index : 2 * index + 1, :] = exponent
            head[2 * index + 1 : 2 * index + 2, :] = fraction
            out[place : place + values.shape[0], :] = quantize(values, exponent, fraction)
            place += values.shape[0]
        out[:first, :] = to_short(head[:first, :])

    with_most = lambda values: (values, jnp.abs(values))
    border = pieces * 2 * reach_y
    on_left = lax.axis_index("wide") & 1
    for side, (even, odd) in enumerate(((0, 1), (1, 0))):

        @pl.when(on_left == side)
        def _():
            send(even_out, 16, [(slabs[even], largest[even]), with_most(packed[even])])
            send(layers_out, top, [with_most(edges[1 - even, :border, :])])
            send(odd_out, top, [(slabs[odd], largest[odd]), with_most(edges[1 - odd, :border, :])])


def forward(parts, early, early_edges, table, modes, reach_x, reach_y, blocks, awaited):
    pieces = len(parts)
    half = reach_x // 2
    lanes = 2 * HALF
    head = up_to(6 + 2 * pieces * blocks, 16)
    border = pieces * 2 * reach_y
    short = lambda rows: jax.ShapeDtypeStruct((rows, lanes), jnp.int16)
    return pl.pallas_call(
        functools.partial(
            forward_kernel, reach_x, reach_y, blocks, pieces, len(awaited)
        ),
        in_specs=[whole_vmem()] * (pieces + 4) + [anywhere()] * len(awaited),
        out_specs=[whole_vmem()] * 7,
        out_shape=[
            jax.ShapeDtypeStruct((half, GRID, lanes), F32),
            short(16 + GRID + GRID // 2),
            short(head + border),
            short(head + GRID + border),
            jax.ShapeDtypeStruct((GRID, lanes), F32),
            jax.ShapeDtypeStruct((pieces * blocks, BLOCK), F32),
            jax.ShapeDtypeStruct((GRID, lanes), F32),
        ],
        scratch_shapes=stacking_scratch(pieces // table.shape[0], reach_x, reach_y)
        + [
            pltpu.VMEM((2, border + SPARE, lanes), F32),
            pltpu.VMEM((2, GRID, lanes), F32),
            pltpu.VMEM((head, lanes), F32),
        ],
        compiler_params=params(),
        cost_estimate=cost(2 * half * 256 * 256 * 128, 4 * half * GRID * lanes * 2),
        name="forward",
    )(*parts, early, early_edges, table, modes, *awaited)


def opened_part(ref, index, first, rows):
    head = from_short(ref[:16, :])
    scale = unit(head[2 * index : 2 * index + 1], head[2 * index + 1 : 2 * index + 2])
    return from_short(ref[first : first + rows, :]) * scale


def pair_kernel(reach_x, flips, own_ref, even_ref, modes_ref, *refs):
    outs, head = refs[:-1], refs[-1]
    span = reach_x - 4
    here = lax.axis_index("wide")
    low = low_lanes(GRID)
    log_decay = modes_ref[y_position(), 1]
    own = own_ref[...]
    top = even_ref.shape[0] - GRID - GRID // 2
    cut = opened_part(even_ref, 0, top, GRID)
    packed = opened_part(even_ref, 1, top + GRID, GRID // 2)
    from_left = jnp.where(low, cut, jnp.concatenate([swap(packed), packed], axis=0))
    from_right = jnp.where(low, jnp.concatenate([packed, swap(packed)], axis=0), cut)
    partner = jnp.where((here & 1) == 1, from_left, from_right)

    def weight(distances):
        powers = []
        for distance in distances:
            ahead = span * distance - reach_x
            powers.append(jnp.where(distance >= 2, ahead, ahead + GRID).astype(F32))
        return jnp.exp(jnp.where(low, *powers) * log_decay)

    head[...] = jnp.zeros_like(head)
    for flip, out in zip(flips, outs):
        behind = (here ^ flip) - here
        message = own * weight((-behind, behind))
        behind = (here ^ flip) - (here ^ 1)
        beside = jnp.where(jnp.abs(behind) == 1, 0.0, 1.0)
        send_piece(out, head, message + partner * (weight((-behind, behind)) * beside))


def pair_messages(own, from_even, modes, reach_x, flips):
    return pl.pallas_call(
        functools.partial(pair_kernel, reach_x, flips),
        in_specs=[whole_vmem()] * 3,
        out_specs=[whole_vmem()] * len(flips),
        out_shape=[jax.ShapeDtypeStruct((16 + GRID, 2 * HALF), jnp.int16)] * len(flips),
        scratch_shapes=[pltpu.VMEM((16, 2 * HALF), F32)],
        compiler_params=params(),
        cost_estimate=cost(16 * GRID * 2 * HALF, 4 * GRID * 2 * HALF * (6 + len(flips))),
        name="pair_messages",
    )(own, from_even, modes)


def borders_kernel(reach_y, pieces, layers_ref, odd_ref, table_ref, out_ref, stacked, partial):
    on_left = (lax.axis_index("wide") & 1) == 1
    pair = lax.axis_size("pair")
    rows = pieces * 2 * reach_y
    even = opened_part(layers_ref, 0, layers_ref.shape[0] - rows, rows)
    odd = opened_part(odd_ref, 1, odd_ref.shape[0] - rows, rows)
    left, right = jnp.where(on_left, even, odd), jnp.where(on_left, odd, even)
    low = low_lanes(rows)
    both = [jnp.where(low, left, swap(right)), jnp.where(low, swap(left), right)]
    core = lax.axis_index("pair")
    chip = lax.axis_index("narrow")
    stacked[...] = jnp.zeros_like(stacked)
    before = None
    for other in range(pair):
        for flip in range(pieces // pair):
            first = (flip * pair + other) * 2 * reach_y
            layers = [
                values[first + two * reach_y : first + (two + 1) * reach_y]
                for two in range(2)
                for values in both
            ]
            stack_layers(layers, chip ^ flip, reach_y, stacked)
        target = out_ref if other == pair - 1 else partial
        transform_pieces(table_ref[core ^ other], stacked, before, target)
        before = target


def borders(layers, from_odd, table, reach_y, pieces):
    chips = pieces // table.shape[0]
    shape = (4, GRID, 2 * HALF)
    return pl.pallas_call(
        functools.partial(borders_kernel, reach_y, pieces),
        in_specs=[whole_vmem()] * 3,
        out_specs=whole_vmem(),
        out_shape=jax.ShapeDtypeStruct(shape, F32),
        scratch_shapes=[
            pltpu.VMEM((4 * chips * up_to(reach_y, 8), 2 * HALF), F32),
            pltpu.VMEM(shape, F32),
        ],
        compiler_params=params(),
        cost_estimate=cost(2 * 4 * 256 * 256 * 128, 4 * 6 * GRID * 2 * HALF),
        name="borders",
    )(layers, from_odd, table)


def send_fields(outs, flips, reach_y, field_high, field_low, high_ref, low_ref, ready, head):
    half = field_high.shape[0]
    mine = y_position()
    pitch = up_to(reach_y, 16)
    pick = lambda ref: jnp.concatenate([ref[mine ^ flip] for flip in flips], axis=0)
    table = (pick(high_ref), pick(low_ref))
    for i in range(0, half, 2):
        many = min(2, half - i)
        join = lambda ref: jnp.concatenate([ref[i + j] for j in range(many)], axis=1)
        result = dot_three(table, (join(field_high), join(field_low)))
        for j in range(many):
            for piece in range(len(flips)):
                ready[piece, (i + j) * reach_y : (i + j + 1) * reach_y, :] = result[
                    piece * pitch : piece * pitch + reach_y, j * 2 * HALF : (j + 1) * 2 * HALF
                ]
    head[...] = jnp.zeros_like(head)
    for piece, out in enumerate(outs):
        if ready.shape[1] > half * reach_y:
            ready[piece, half * reach_y :, :] = jnp.zeros_like(ready[piece, half * reach_y :, :])
        send_piece(out, head, ready[piece])


def inverse_kernel(reach_x, reach_y, flips, fars, *refs):
    spectrum, border_ref, from_even, from_odd, own_ref, inner_ref, *far_refs = refs[: 6 + fars]
    refs = refs[6 + fars :]
    high_ref, low_ref, modes_ref = refs[:3]
    outs = refs[3 : 3 + len(flips)]
    field_high, field_low, ready, head = refs[3 + len(flips) :]
    half = reach_x // 2
    span = reach_x - 4
    chunk = 256
    border_rows = lax.axis_size("narrow") * lax.axis_size("pair") * 2 * reach_y
    tops = from_even.shape[0] - GRID - GRID // 2, from_odd.shape[0] - GRID - border_rows
    on_left = (lax.axis_index("wide") & 1) == 1
    moment_units = []
    for ref in (from_even, from_odd):
        first = from_short(ref[:16, :])
        moment_units.append(unit(first[0:1], first[1:2]))

    far_units = []
    for ref in far_refs:
        first = from_short(ref[:16, :])
        far_units.append(unit(first[0:1], first[1:2]))

    def body(index, carry):
        first = pl.multiple_of(index * chunk, chunk)
        rows = pl.ds(first, chunk)
        low = low_lanes(chunk)
        decay = modes_ref[y_position(), 0, rows, :]
        log_decay = modes_ref[y_position(), 1, rows, :]
        ring = 1.0 / (1.0 - jnp.exp(GRID * log_decay))
        gain = KERNEL_GAIN * decay / ((1.0 - decay) * (1.0 + decay))
        across_half = jnp.exp(half * log_decay)
        across_cut = jnp.exp((half - 4) * log_decay)
        around = jnp.exp((GRID - 4) * log_decay)
        beside = jnp.exp((GRID - reach_x - span) * log_decay)
        layers = [spectrum[i, rows, :] for i in range(half)]

        even, odd = (
            from_short(ref[pl.ds(pl.multiple_of(top + index * chunk, 16), chunk), :]) * scale
            for ref, top, scale in zip((from_even, from_odd), tops, moment_units)
        )
        left_moments, right_moments = jnp.where(on_left, even, odd), jnp.where(on_left, odd, even)
        border = [border_ref[i, rows, :] for i in range(4)]
        zero = jnp.zeros_like(decay)
        head_sum = border[0]
        for i in range(1, 4):
            head_sum = decay * head_sum + border[i]
        tail_sum = border[3]
        for i in range(2, -1, -1):
            tail_sum = decay * tail_sum + border[i]
        for i in range(4):
            layers[i] = layers[i] + jnp.where(low, border[i], zero)
        for i in range(4):
            place = half - 4 + i
            layers[place] = layers[place] + jnp.where(low, zero, border[i])
        total = own_ref[rows, :] * jnp.exp((GRID - reach_x) * log_decay)
        at = pl.ds(pl.multiple_of(16 + index * chunk, 16), chunk)
        for ref, scale in zip(far_refs, far_units):
            total = total + from_short(ref[at, :]) * scale
        one = jnp.ones_like(decay)
        total = total + left_moments * jnp.where(low, beside, one)
        total = total + right_moments * jnp.where(low, one, beside)
        shared = jnp.where(low, head_sum, tail_sum)
        entering = (swap(total) + around * shared) * ring
        leaving = swap(across_half * entering + across_cut * shared + inner_ref[rows, :])
        run = jnp.where(low, entering, leaving)
        forward_runs = []
        for i in range(half):
            run = decay * run + layers[i]
            forward_runs.append(run)
        run = jnp.where(low, leaving, entering)
        for i in range(half - 1, -1, -1):
            ahead = decay * run
            high, rest = split(gain * (forward_runs[i] + ahead))
            field_high[i, rows, :] = high
            field_low[i, rows, :] = rest
            run = ahead + layers[i]
        return carry

    lax.fori_loop(0, GRID // chunk, body, 0)
    send_fields(outs, flips, reach_y, field_high, field_low, high_ref, low_ref, ready, head)


def inverse(
    spectrum, border, from_even, from_odd, own, inner, fars, table, modes, reach_x, reach_y, flips
):
    half = reach_x // 2
    lanes = 2 * HALF
    body = up_to(half * reach_y, 16)
    shapes = [jax.ShapeDtypeStruct((16 + body, lanes), jnp.int16)] * len(flips)
    shapes += [jax.ShapeDtypeStruct((half, GRID, lanes), BF16)] * 2
    return pl.pallas_call(
        functools.partial(inverse_kernel, reach_x, reach_y, flips, len(fars)),
        in_specs=[whole_vmem()] * (9 + len(fars)),
        out_specs=[whole_vmem()] * len(shapes),
        out_shape=shapes,
        scratch_shapes=[
            pltpu.VMEM((len(flips), body, lanes), F32),
            pltpu.VMEM((16, lanes), F32),
        ],
        compiler_params=params(),
        cost_estimate=cost(2 * half * 256 * 256 * 128, 4 * half * GRID * lanes * 2),
        name="inverse",
    )(spectrum, border, from_even, from_odd, own, inner, *fars, *table, modes)


def inverse_rest_kernel(reach_y, flips, field_high, field_low, high_ref, low_ref, *refs):
    outs, (ready, head) = refs[: len(flips)], refs[len(flips) :]
    send_fields(outs, flips, reach_y, field_high, field_low, high_ref, low_ref, ready, head)


def inverse_rest(field, table, reach_y, flips):
    half = field[0].shape[0]
    lanes = 2 * HALF
    body = up_to(half * reach_y, 16)
    return pl.pallas_call(
        functools.partial(inverse_rest_kernel, reach_y, flips),
        in_specs=[whole_vmem()] * 4,
        out_specs=[whole_vmem()] * len(flips),
        out_shape=[jax.ShapeDtypeStruct((16 + body, lanes), jnp.int16)] * len(flips),
        scratch_shapes=[
            pltpu.VMEM((len(flips), body, lanes), F32),
            pltpu.VMEM((16, lanes), F32),
        ],
        compiler_params=params(),
        cost_estimate=cost(2 * half * 256 * 256 * 128, 4 * half * GRID * lanes * 2),
        name="inverse_rest",
    )(*field, *table)


def sum_rows(values):
    row = lax.broadcasted_iota(jnp.int32, values[0].shape, 0)
    for step in (4, 2, 1):
        low = (row & step) == 0
        paired = []
        for one, other in zip(values[: len(values) // 2], values[len(values) // 2 :]):
            kept = jnp.where(low, one, other)
            moved = jnp.where(low, other, one)
            if step == 4:
                moved = pltpu.roll(moved, 4, 0)
            else:
                moved = jnp.where(low, pltpu.roll(moved, 8 - step, 0), pltpu.roll(moved, step, 0))
            paired.append(kept + moved)
        values = paired
    return values[0]


def z_lines(parts, flips, high_ref, low_ref):
    mine = y_position()
    opened = []
    for part in parts:
        first = from_short(part[:16, :])
        opened.append(from_short(part[16:, :]) * unit(first[0:1], first[1:2]))
    values = split(jnp.concatenate(opened, axis=1))
    pick = lambda ref: jnp.concatenate([ref[mine ^ flip] for flip in flips], axis=0)
    return dot_three(values, (pick(high_ref), pick(low_ref)))


def sample_early_kernel(flips, *refs):
    *parts, high_ref, low_ref, out_ref = refs
    out_ref[...] = z_lines(parts, flips, high_ref, low_ref)


def sample_early(parts, flips, table):
    rows = parts[0].shape[0] - 16
    return pl.pallas_call(
        functools.partial(sample_early_kernel, flips),
        in_specs=[whole_vmem()] * (len(parts) + 2),
        out_specs=whole_vmem(),
        out_shape=jax.ShapeDtypeStruct((rows, 2 * REGION), F32),
        compiler_params=params(),
        cost_estimate=cost(EARLY_FLOPS, 4 * rows * 512),
        name="sample_early",
    )(*parts, *table)


def sample_kernel(last, reach_x, reach_y, flips, place_in, *refs):
    parts = refs[: len(flips)]
    early_ref, high_ref, low_ref, line_ref, own_ref, vector_ref, near_ref, out_ref = refs[
        len(flips) : len(flips) + 8
    ]
    flat, field, sums, place_ref, sem = refs[len(flips) + 8 :]
    copy = pltpu.make_async_copy(place_in, place_ref, sem)
    copy.start()
    half_rows = reach_x * reach_y // 2
    both = early_ref[...] + z_lines(parts, flips, high_ref, low_ref)
    flat[:half_rows, :] = both[:half_rows, :REGION]
    flat[half_rows : 2 * half_rows, :] = both[:half_rows, REGION:]
    for x in range(reach_x):
        layer = flat[x * reach_y : (x + 1) * reach_y, :]
        for row in pair_rows(x, reach_x, reach_y):
            field[pl.ds(row, reach_y, stride=2), :] = layer
    count = place_ref.shape[1]

    def body(group, carry):
        for eight in range(0, GROUP, 8):
            totals = []
            for local in range(eight, eight + 8):
                panel = group * GROUP + local
                row = place_ref[0, panel]
                first = pl.multiple_of(panel * 16, 16)
                totals.append(
                    field[pl.ds(row, 8), :] * line_ref[pl.ds(first, 8), :]
                    + field[pl.ds(row + 2 * reach_y, 8), :] * line_ref[pl.ds(first + 8, 8), :]
                )
            sums[pl.ds(pl.multiple_of(group * GROUP + eight, 8), 8), :] = sum_rows(totals)
        return carry

    copy.wait()
    lax.fori_loop(0, count // GROUP, body, 0)
    first, rest = split(sums[...])
    second, third = split(sums[...] - first.astype(F32))
    across = lambda values: lax.dot_general(
        jnp.ones((16, REGION), BF16),
        values,
        (((1,), (1,)), ((), ())),
        preferred_element_type=F32,
    )
    sampled = across(first) + (across(second) + across(third))
    for block in range(count // BLOCK):
        lane = slice(block * BLOCK, (block + 1) * BLOCK)
        row = slice(block, block + 1)
        vector = vector_ref[row, :]
        image = jnp.where(own_ref[row, :] == 1, 0.0, 0.5 * vector) + sampled[:1, lane]
        image = image + near_ref[row, :]
        if last:
            out_ref[0:1, lane] = vector
            out_ref[1:2, lane] = image
        else:
            out_ref[row, :] = image


def sample(last, places, parts, flips, early, table, lines, flag, vector, near, reach_x, reach_y):
    count = places.shape[1]
    blocks = count // BLOCK
    shape = (2, count) if last else (blocks, BLOCK)
    return pl.pallas_call(
        functools.partial(sample_kernel, last, reach_x, reach_y, flips),
        in_specs=[anywhere()] + [whole_vmem()] * (len(parts) + 7),
        out_specs=whole_vmem(),
        out_shape=jax.ShapeDtypeStruct(shape, F32),
        scratch_shapes=[
            pltpu.VMEM((reach_x * reach_y + SPARE, REGION), F32),
            pltpu.VMEM((pair_count(reach_x, reach_y), REGION), F32),
            pltpu.VMEM((count, REGION), F32),
            pltpu.SMEM((2, count), jnp.int32),
            pltpu.SemaphoreType.DMA,
        ],
        compiler_params=params(),
        cost_estimate=cost(reach_x * reach_y * 256 * 512, 4 * 16 * count * REGION),
        name="sample",
    )(
        places,
        *parts,
        early,
        *table,
        lines,
        flag.reshape(blocks, BLOCK),
        vector.reshape(blocks, BLOCK),
        near,
    )


def near_kernel(slots, blocks, place_ref, target_ref, *refs):
    even_ref, odd_ref, peers_ref, tile_ref = refs[:4]
    out_ref, held = refs[-2:]
    count = peers_ref.shape[0]
    held[count : 2 * count, :] = peers_ref[...]
    on_left = lax.axis_index("wide") & 1
    for side, ref in ((1 - on_left, even_ref), (on_left, odd_ref)):
        top = from_short(ref[...])
        for piece in range(count // blocks):
            at = 6 + 2 * piece * blocks
            held[pl.ds(side * (2 * count) + piece * blocks, blocks), :] = decode_rounded(
                top[at : at + blocks], top[at + blocks : at + 2 * blocks]
            )
    out_ref[...] = jnp.zeros_like(out_ref)
    for slot in range(slots):
        picked = held[pl.ds(place_ref[slot], 1), :]
        picked = jnp.broadcast_to(picked, (16, BLOCK)).astype(BF16)
        product = lax.dot_general(
            picked,
            tile_ref[slot],
            (((1,), (1,)), ((), ())),
            preferred_element_type=F32,
        )
        target = pl.ds(target_ref[slot], 1)
        out_ref[target, :] = out_ref[target, :] + product[:1]


def near_field(places, targets, from_even, from_odd, peers, tiles, blocks, out_rows, awaited):
    slots = tiles.shape[0]
    head = up_to(6 + 2 * peers.shape[0], 16)
    constant = lambda shape: pl.BlockSpec(shape, lambda i: (0,) * len(shape))
    return pl.pallas_call(
        functools.partial(near_kernel, slots, blocks),
        grid=(1,),
        in_specs=[
            in_smem(),
            in_smem(),
            constant((head, BLOCK)),
            constant((head, BLOCK)),
            constant(peers.shape),
            constant(tiles.shape),
        ]
        + [anywhere()] * len(awaited),
        out_specs=constant((out_rows, BLOCK)),
        out_shape=jax.ShapeDtypeStruct((out_rows, BLOCK), F32),
        scratch_shapes=[pltpu.VMEM((3 * peers.shape[0] + SPARE, BLOCK), F32)],
        compiler_params=params(),
        cost_estimate=cost(2 * slots * 16 * BLOCK * BLOCK, 2 * slots * BLOCK * BLOCK),
        name="near_field",
    )(places, targets, from_even, from_odd, peers, tiles, *awaited)


def shards(
    density,
    surface_flag,
    stencil_base,
    sample_weights,
    dipole_weights,
    near_target,
    near_source,
    near_tiles,
):
    x_count = lax.axis_size("wide")
    y_count = lax.axis_size(Y_AXES)
    y_index = lax.axis_index(Y_AXES)
    pair = lax.axis_size("pair")
    span_x = REGION // x_count
    span_y = REGION // y_count
    reach_x = span_x + 4
    reach_y = span_y + 4
    count = density.shape[0]
    blocks = count // BLOCK

    z_forward, z_inverse, y_forward, y_inverse, modes = tables(y_count, pair, span_y)

    neighbour = near_source // blocks
    flip = (y_index + neighbour % 3 - 1) ^ y_index
    sources = ((neighbour // 3) * y_count + flip) * blocks + near_source % blocks
    out_rows = up_to(blocks + 1, 8)
    live = near_target >= 0
    sources = jnp.where(live, sources, 0)
    targets = jnp.where(live, near_target, out_rows - 1)

    swaps = lambda pairs: [(i, j) for i, j in pairs] + [(j, i) for i, j in pairs]
    even_swap = swaps([(i, i + 1) for i in range(0, x_count - 1, 2)])
    odd_swap = swaps([(i, i + 1) for i in range(1, x_count - 1, 2)])
    far_flips = list(range(2, x_count, 2))

    first, inside, local = list(range(pair, y_count)), list(range(1, pair)), [0]
    same_core = list(range(0, y_count, pair))
    other_core = [flip for flip in range(y_count) if flip not in same_core]

    def turned(sent, then):
        arrived = [None] * y_count
        for flip, part in zip(first + inside + local, list(sent) + list(then)):
            swap_pairs = [(i, i ^ flip) for i in range(y_count)]
            arrived[flip] = part if flip == 0 else lax.ppermute(part, Y_AXES, swap_pairs)
        return arrived

    def chosen(parts, flips):
        return [parts[flip] for flip in flips]

    def convolve_and_sample(last, vector, sent, both, table, places, sample_lines, awaited):
        then = [part for flips in (inside, local) for part in spread_rest(vector, both, table, flips)]
        arrived = turned(sent, then)
        early, edges = forward_early(chosen(arrived, same_core), y_forward, reach_x, reach_y)
        spectrum, even_message, layers, odd_message, own, peers, inner = forward(
            arrived, early, edges, y_forward, modes, reach_x, reach_y, blocks, awaited
        )
        from_even = lax.ppermute(even_message, "wide", even_swap)
        from_odd = lax.ppermute(odd_message, "wide", odd_swap)
        even_layers = lax.ppermute(layers, "wide", even_swap)
        fars = [
            lax.ppermute(message, "wide", [(i, i ^ flip) for i in range(x_count)])
            for flip, message in zip(
                far_flips, pair_messages(own, from_even, modes, reach_x, far_flips)
            )
        ]
        *sent, high, low = inverse(
            spectrum,
            borders(even_layers, from_odd, y_forward, reach_y, y_count),
            from_even,
            from_odd,
            own,
            inner,
            fars,
            y_inverse,
            modes,
            reach_x,
            reach_y,
            first,
        )
        then = [
            part
            for flips in (inside, local)
            for part in inverse_rest((high, low), y_inverse, reach_y, flips)
        ]
        near_part = near_field(
            sources, targets, even_layers, from_odd, peers, near_tiles, blocks, out_rows, then[:1]
        )
        arrived = turned(sent, then)
        image = sample(
            last,
            places,
            chosen(arrived, other_core),
            other_core,
            sample_early(chosen(arrived, same_core), same_core, z_inverse),
            z_inverse,
            sample_lines,
            surface_flag,
            vector,
            near_part,
            reach_x,
            reach_y,
        )
        return image, near_part

    raw = (stencil_base, surface_flag, sample_weights, dipole_weights)
    *sent, wide_high, wide_low, source_coeff, places, vector, high, low = spread(
        density, z_forward, None, raw, reach_x, reach_y, first
    )
    z_forward = (high, low)
    sample_lines = place_sample_lines(places, sample_weights)
    vector, near_part = convolve_and_sample(
        False,
        vector,
        sent,
        (wide_high, wide_low),
        z_forward,
        places,
        sample_lines,
        [sample_lines],
    )
    source_lines = place_lines(places, source_coeff, [near_part])
    *sent, wide_high, wide_low = spread(
        vector.reshape(-1), z_forward, (places, source_lines), None, reach_x, reach_y, first
    )
    both_images, _ = convolve_and_sample(
        True, vector, sent, (wide_high, wide_low), z_forward, places, sample_lines, []
    )
    return both_images


def solution(mesh):
    panels = P(("groups",) + ALL_AXES)
    columns = P(None, ("groups",) + ALL_AXES)
    in_specs = (
        panels,
        panels,
        columns,
        columns,
        columns,
        panels,
        panels,
        P(("groups",) + ALL_AXES, None, None),
    )
    return jax.shard_map(
        shards, mesh=mesh, in_specs=in_specs, out_specs=columns, check_vma=False
    )
```

```python
import functools
import math

import jax
import jax.numpy as jnp
import numpy as np
from jax import lax
from jax.experimental import pallas as pl
from jax.experimental.pallas import tpu as pltpu
from jax.sharding import PartitionSpec as P

GRID = 256
REGION = 128
BLOCK = 128
HALF = 64
KERNEL_GAIN = 4.0
SCREEN = 1.0 / 1024.0
LN2 = math.log(2.0)
SPARE = 16
Y_AXES = ("narrow", "pair")
ALL_AXES = ("wide", "narrow", "pair")
F32 = jnp.float32
BF16 = jnp.bfloat16
VMEM_LIMIT = 24 * 1024 * 1024
START_LIMIT = VMEM_LIMIT
EARLY_FLOPS = 5 * 10**9
GROUP = 32
CHAINS = 2


def cas(angles):
    return np.cos(angles) + np.sin(angles)


def up_to(count, multiple):
    return -(-count // multiple) * multiple


def low_lanes(rows):
    return lax.broadcasted_iota(jnp.int32, (rows, 2 * HALF), 1) < HALF


def swap(values):
    return pltpu.roll(values, HALF, 1)


def split(values):
    high = values.astype(BF16)
    return high, (values - high.astype(F32)).astype(BF16)


def dot(left, right):
    return jnp.dot(left, right, preferred_element_type=F32)


def dot_three(left, right):
    return dot(left[0], right[0]) + (dot(left[0], right[1]) + dot(left[1], right[0]))


def params():
    return pltpu.CompilerParams(vmem_limit_bytes=VMEM_LIMIT)


def whole_vmem():
    return pl.BlockSpec(memory_space=pltpu.VMEM)


def anywhere():
    return pl.BlockSpec(memory_space=pl.ANY)


def in_smem():
    return pl.BlockSpec(memory_space=pltpu.SMEM)


def cost(flops, moved):
    return pl.CostEstimate(flops=flops, bytes_accessed=moved, transcendentals=0)


def full_scale(exponent, fraction):
    return fraction * jnp.exp(exponent * LN2) * (1.0 / 1024.0)


def fit_scale(largest):
    largest = jnp.maximum(largest, 1e-30)
    exponent = jnp.floor(jnp.log(largest) * (1.0 / LN2))
    fraction = jnp.ceil(largest * jnp.exp(-exponent * LN2) * 1024.0) + 1.0
    return exponent, fraction


def to_short(values):
    return values.astype(jnp.int32).astype(jnp.int16)


def from_short(values):
    return values.astype(jnp.int32).astype(F32)


def quantize(values, exponent, fraction):
    return to_short(jnp.round(values * (32767.0 / full_scale(exponent, fraction))))


def unit(exponent, fraction):
    return full_scale(exponent, fraction) * (1.0 / 32767.0)


def encode_rounded(values):
    rounded = values.astype(BF16).astype(F32)
    size = jnp.maximum(jnp.abs(rounded), 1e-30)
    exponent = jnp.floor(jnp.log(size) * (1.0 / LN2))
    return jnp.round(rounded * jnp.exp((10.0 - exponent) * LN2)), exponent


def decode_rounded(mantissa, exponent):
    return (mantissa * jnp.exp((exponent - 10.0) * LN2)).astype(BF16).astype(F32)


def send_piece(out, head, values):
    exponent, fraction = fit_scale(jnp.max(jnp.abs(values), axis=0, keepdims=True))
    head[0:1, :] = exponent
    head[1:2, :] = fraction
    top = head.shape[0]
    out[:top, :] = to_short(head[...])
    out[top:, :] = quantize(values, exponent, fraction)


def y_position():
    return lax.axis_index("narrow") * lax.axis_size("pair") + lax.axis_index("pair")


def halves(table):
    high = table.astype(jnp.bfloat16)
    return high, (table - high.astype(np.float64)).astype(jnp.bfloat16)


def tables(y_count, pair, span_y):
    depth = GRID // y_count
    reach = span_y + 4
    waves = np.arange(GRID)
    step = 2.0 * np.pi / GRID
    z_table = cas(step * np.outer(np.arange(REGION), waves))
    z_forward = np.zeros((y_count, 2 * REGION, 2 * HALF))
    z_inverse = np.zeros((y_count, 2 * HALF, 2 * REGION))
    symbols = 4.0 * np.sin(np.pi * waves / GRID) ** 2
    shift = np.full((y_count, GRID, 2 * HALF), 1.0)
    y_forward = np.zeros((GRID, y_count, up_to(reach, 8)))
    y_inverse = np.zeros((y_count, up_to(reach, 16), GRID))
    for block in range(y_count):
        mine = z_table[:, block * depth : (block + 1) * depth]
        for half in range(2):
            rows = slice(half * REGION, (half + 1) * REGION)
            lanes = slice(half * HALF, half * HALF + depth)
            z_forward[block, rows, lanes] = mine
            z_inverse[block, lanes, rows] = mine.T / GRID
            shift[block, :, lanes] = (
                SCREEN + symbols[:, None] + symbols[None, block * depth : (block + 1) * depth]
            )
        cells = block * span_y - 2 + np.arange(reach)
        y_table = cas(step * np.outer(waves, cells))
        y_forward[:, block, :reach] = y_table
        y_inverse[block, :reach] = y_table.T / GRID
    y_forward = y_forward.reshape(GRID, y_count // pair, pair, -1).transpose(2, 0, 1, 3)
    y_forward = halves(y_forward.reshape(pair, GRID, -1))
    y_forward = np.concatenate([y_forward[0], y_forward[0], y_forward[1]], axis=2)
    root = np.sqrt(shift * (shift + 4.0))
    decay = 2.0 / (2.0 + shift + root)
    log_decay = np.log(decay)
    ring = 1.0 / (1.0 - np.exp(GRID * log_decay))
    gain = KERNEL_GAIN / root
    modes = np.stack([decay, log_decay, ring, gain], axis=1).astype(np.float32)
    return (
        halves(z_forward),
        halves(z_inverse),
        y_forward,
        halves(y_inverse),
        modes,
    )


def mixing_matrix():
    place = lax.broadcasted_iota(jnp.int32, (4 * BLOCK, 4 * BLOCK), 0)
    lane = lax.broadcasted_iota(jnp.int32, (4 * BLOCK, 4 * BLOCK), 1)
    return jnp.where(lane == 4 * (place % BLOCK) + place // BLOCK, 1.0, 0.0).astype(BF16)


def weave(tiles, mixing, out):
    weights = jnp.concatenate([jnp.concatenate(tile, axis=1) for tile in tiles], axis=0)
    first, rest = split(weights)
    second, third = split(weights - first.astype(F32))
    woven = dot(first, mixing) + (dot(second, mixing) + dot(third, mixing))
    for tile in range(len(tiles)):
        for part in range(BLOCK // GROUP):
            at = (tile * (BLOCK // GROUP) + part) * 16
            lanes = slice(part * BLOCK, (part + 1) * BLOCK)
            for a in range(4):
                row = tile * 16 + 4 * a
                out[pl.ds(at + 8 * (a // 2) + a % 2, 4, stride=2), :] = woven[row : row + 4, lanes]


def by_depth(ref):
    return [ref[pl.ds(depth, 16, stride=4), :] for depth in range(4)]


def pair_rows(x, reach_x, reach_y):
    even = (x // 2) * 2 * reach_y + x % 2
    if x == 0 or x == reach_x - 1:
        return [even]
    return [even, reach_x * reach_y + ((x - 1) // 2) * 2 * reach_y + (x - 1) % 2]


def pair_count(reach_x, reach_y):
    return (2 * reach_x - 2) * reach_y + SPARE


def in_window(lanes, depth):
    return ((lanes - depth) & -4) == 0


def add_panels(reach, woven, vector_ref, place_ref, weight_ref, grids):
    lanes = lax.broadcasted_iota(jnp.int32, (8, REGION), 1)

    def body(group, carry):
        at = pl.multiple_of(group * 16, 16)
        coeff = [weight_ref[pl.ds(at + 8 * q, 8), :] for q in range(2)] if woven else None
        for local in range(GROUP):
            panel = group * GROUP + local
            grid = grids[local % len(grids)]
            row = place_ref[0, panel]
            value = vector_ref[panel]
            if woven:
                depth = place_ref[1, panel]
                shift = (depth - 4 * local) & (REGION - 1)
                value = jnp.where(in_window(lanes, depth), value, 0.0)
                lines = [pltpu.roll(coeff[q], shift, 1) for q in range(2)]
            else:
                first = pl.multiple_of(panel * 16, 16)
                lines = [weight_ref[pl.ds(first + 8 * q, 8), :] for q in range(2)]
            places = [pl.ds(row, 8), pl.ds(row + 2 * reach, 8)]
            held = [grid[place, :] for place in places]
            for q in range(2):
                grid[places[q], :] = held[q] + lines[q] * value
        return carry

    lax.fori_loop(0, vector_ref.shape[0] // GROUP, body, 0)


def send_pieces(outs, flips, head, rounded, both, high_ref, low_ref):
    blocks = rounded.shape[0]
    mantissa, exponent = encode_rounded(rounded)
    head[...] = jnp.zeros_like(head)
    head[2 : 2 + blocks, :] = mantissa
    head[2 + blocks : 2 + 2 * blocks, :] = exponent
    mine = y_position()
    for at in range(0, len(flips), 2):
        pick = lambda ref: jnp.concatenate([ref[mine ^ flip] for flip in flips[at : at + 2]], axis=1)
        result = dot_three(both, (pick(high_ref), pick(low_ref)))
        for i, out in enumerate(outs[at : at + 2]):
            send_piece(out, head, result[:, i * 2 * HALF : (i + 1) * 2 * HALF])


def spread_grid(reach_x, reach_y, rounded, tables, outs, flips, wides, head, total, grids):
    for x in range(reach_x):
        parts = [
            grid[pl.ds(row, reach_y, stride=2), :]
            for row in pair_rows(x, reach_x, reach_y)
            for grid in grids
        ]
        total[x * reach_y : (x + 1) * reach_y, :] = sum(parts[1:], parts[0])
    half = reach_x * reach_y // 2
    both = jnp.concatenate([total[:half, :], total[half : 2 * half, :]], axis=1)
    extra = wides[0].shape[0] - half
    if extra:
        both = jnp.concatenate([both, jnp.zeros((extra, 2 * REGION), F32)], axis=0)
    both = split(both)
    for wide, values in zip(wides, both):
        wide[...] = values
    send_pieces(outs, flips, head, rounded, both, *tables)


def start_kernel(reach_x, reach_y, flips, *refs):
    vector_in, *remote = refs[:8]
    refs = refs[8:]
    outs, refs = refs[: len(flips)], refs[len(flips) :]
    wides, (weight_ref, places_out), refs = refs[:2], refs[2:4], refs[4:]
    rounded, high, low, stencil, flag, samples, dipoles, vector_ref = refs[:8]
    place_ref, sems, head, total = refs[8:12]
    grids = refs[12:]
    tiles = samples.shape[0]
    copies = []
    fetch = lambda source, target: copies.append(
        pltpu.make_async_copy(source, target, sems.at[len(copies)])
    )
    rounded_in, high_in, low_in, stencil_in, flag_in, sample_in, dipole_in = remote
    fetch(stencil_in, stencil)
    fetch(flag_in, flag)
    fetch(vector_in, vector_ref)
    for tile in range(tiles):
        lanes = pl.ds(tile * BLOCK, BLOCK)
        fetch(sample_in.at[:, lanes], samples.at[tile, pl.ds(0, 64)])
        fetch(dipole_in.at[:, lanes], dipoles.at[tile, pl.ds(0, 64)])
    needed_first = len(copies)
    fetch(rounded_in, rounded)
    fetch(high_in, high)
    fetch(low_in, low)
    for copy in copies:
        copy.start()
    for grid in grids:
        grid[...] = jnp.zeros_like(grid)
    mixing = mixing_matrix()
    copies[0].wait()
    span_x, span_y = reach_x - 4, reach_y - 4
    local_x = stencil[0:1, :] - (lax.axis_index("wide") * span_x - 2)
    local_y = stencil[1:2, :] - (y_position() * span_y - 2)
    odd = local_x & 1
    places_out[0:1, :] = odd * (reach_x * reach_y) + (local_x >> 1) * (2 * reach_y) + 2 * local_y
    places_out[1:2, :] = stencil[2:3, :]
    to_scalar = pltpu.make_async_copy(places_out, place_ref, sems.at[len(copies)])
    to_scalar.start()
    for copy in copies[1:needed_first]:
        copy.wait()
    sources = []
    for tile in range(tiles):
        charged = flag[:, tile * BLOCK : (tile + 1) * BLOCK] == 1
        pairs = zip(by_depth(samples.at[tile]), by_depth(dipoles.at[tile]))
        sources.append([jnp.where(charged, -sample, dipole) for sample, dipole in pairs])
    weave(sources, mixing, weight_ref)
    to_scalar.wait()
    add_panels(reach_y, True, vector_ref, place_ref, weight_ref, grids)
    for copy in copies[needed_first:]:
        copy.wait()
    spread_grid(
        reach_x, reach_y, rounded[...], (high, low), outs, flips, wides, head, total, grids
    )


def spread_kernel(reach_x, reach_y, flips, *refs):
    vector_in, place_in, rounded_ref, high_ref, low_ref, line_ref = refs[:6]
    refs = refs[6:]
    outs, wides, (vector_ref, place_ref, sems, head, total), grids = (
        refs[: len(flips)],
        refs[len(flips) : len(flips) + 2],
        refs[len(flips) + 2 : len(flips) + 7],
        refs[len(flips) + 7 :],
    )
    copies = [
        pltpu.make_async_copy(vector_in, vector_ref, sems.at[0]),
        pltpu.make_async_copy(place_in, place_ref, sems.at[1]),
    ]
    for copy in copies:
        copy.start()
    for grid in grids:
        grid[...] = jnp.zeros_like(grid)
    for copy in copies:
        copy.wait()
    add_panels(reach_y, False, vector_ref, place_ref, line_ref, grids)
    spread_grid(
        reach_x,
        reach_y,
        rounded_ref[...],
        (high_ref, low_ref),
        outs,
        flips,
        wides,
        head,
        total,
        grids,
    )


def spread(vector, table, placed, raw, reach_x, reach_y, flips):
    count = vector.shape[0]
    half = reach_x * reach_y // 2
    blocks = count // BLOCK
    top = up_to(2 + 2 * blocks, 16)
    lanes = 2 * HALF
    body = up_to(half, 16)
    woven = (count // GROUP * 16 + SPARE, BLOCK)
    out_shapes = [jax.ShapeDtypeStruct((top + body, lanes), jnp.int16)] * len(flips)
    out_shapes += [jax.ShapeDtypeStruct((body, 2 * REGION), BF16)] * 2
    rounded = vector.reshape(blocks, BLOCK)
    work = [
        pltpu.VMEM((top, lanes), F32),
        pltpu.VMEM((reach_x * reach_y + SPARE, REGION), F32),
    ] + [pltpu.VMEM((pair_count(reach_x, reach_y), REGION), F32)] * CHAINS
    if placed is None:
        stencil, flag, sample, dipole = raw
        operands = [vector, rounded, *table, stencil, flag.reshape(1, -1), sample, dipole]
        operands = [pltpu.with_memory_space_constraint(value, pltpu.HBM) for value in operands]
        in_specs = [pl.BlockSpec(memory_space=pltpu.HBM)] * 8
        out_shapes += [jax.ShapeDtypeStruct(woven, F32)]
        out_shapes += [jax.ShapeDtypeStruct((2, count), jnp.int32)]
        out_shapes += [jax.ShapeDtypeStruct(rounded.shape, F32)]
        out_shapes += [jax.ShapeDtypeStruct(values.shape, BF16) for values in table]
        tiled = pltpu.VMEM((blocks, 64 + SPARE, BLOCK), F32)
        work = [
            pltpu.VMEM(stencil.shape, jnp.int32),
            pltpu.VMEM((1, count), jnp.int32),
            tiled,
            tiled,
            pltpu.SMEM((count,), F32),
            pltpu.SMEM((2, count), jnp.int32),
            pltpu.SemaphoreType.DMA((7 + 2 * blocks,)),
        ] + work
    else:
        operands = [vector, placed[0], rounded, *table, placed[1]]
        in_specs = [anywhere()] * 2 + [whole_vmem()] * 4
        work = [
            pltpu.SMEM((count,), F32),
            pltpu.SMEM((2, count), jnp.int32),
            pltpu.SemaphoreType.DMA((2,)),
        ] + work
    return pl.pallas_call(
        functools.partial(
            start_kernel if placed is None else spread_kernel, reach_x, reach_y, flips
        ),
        in_specs=in_specs,
        out_specs=[whole_vmem()] * len(out_shapes),
        out_shape=out_shapes,
        scratch_shapes=work,
        compiler_params=pltpu.CompilerParams(
            vmem_limit_bytes=START_LIMIT if placed is None else VMEM_LIMIT
        ),
        cost_estimate=cost(2 * half * 256 * 512, 4 * 16 * count * REGION),
        name="start" if placed is None else "spread",
    )(*operands)


def spread_rest_kernel(flips, rounded_ref, wide_high, wide_low, high_ref, low_ref, *refs):
    outs, head = refs[:-1], refs[-1]
    both = (wide_high[...], wide_low[...])
    send_pieces(outs, flips, head, rounded_ref[...], both, high_ref, low_ref)


def spread_rest(rounded, both, table, flips):
    blocks = rounded.shape[0]
    top = up_to(2 + 2 * blocks, 16)
    shape = (top + both[0].shape[0], 2 * HALF)
    return pl.pallas_call(
        functools.partial(spread_rest_kernel, flips),
        in_specs=[whole_vmem()] * 5,
        out_specs=[whole_vmem()] * len(flips),
        out_shape=[jax.ShapeDtypeStruct(shape, jnp.int16)] * len(flips),
        scratch_shapes=[pltpu.VMEM((top, 2 * HALF), F32)],
        compiler_params=params(),
        cost_estimate=cost(2 * shape[0] * 256 * 256 * 3, 4 * shape[0] * 512),
        name="spread_rest",
    )(rounded, *both, *table)


def lines_kernel(place_ref, coeff_ref, *refs):
    out_ref = refs[-1]
    lanes = lax.broadcasted_iota(jnp.int32, (8, REGION), 1)

    def body(group, carry):
        at = pl.multiple_of(group * 16, 16)
        coeff = [coeff_ref[pl.ds(at + 8 * q, 8), :] for q in range(2)]
        for local in range(GROUP):
            panel = group * GROUP + local
            depth = place_ref[1, panel]
            shift = (depth - 4 * local) & (REGION - 1)
            inside = in_window(lanes, depth)
            for q in range(2):
                first = pl.multiple_of(panel * 16 + 8 * q, 8)
                out_ref[pl.ds(first, 8), :] = jnp.where(inside, pltpu.roll(coeff[q], shift, 1), 0.0)
        return carry

    lax.fori_loop(0, place_ref.shape[1] // GROUP, body, 0)


def sample_lines_kernel(tiles, place_ref, *refs):
    out_ref, coeff, held = refs[-3:]
    for tile, ref in enumerate(refs[:tiles]):
        held[tile, :64, :] = ref[...]
    weave([by_depth(held.at[tile]) for tile in range(tiles)], mixing_matrix(), coeff)
    lines_kernel(place_ref, coeff, out_ref)


def place_sample_lines(places, sample):
    count = places.shape[1]
    blocks = count // BLOCK
    tile = lambda t: pl.BlockSpec((64, BLOCK), lambda i: (0, t))
    shape = (count * 16, REGION)
    return pl.pallas_call(
        functools.partial(sample_lines_kernel, blocks),
        grid=(1,),
        in_specs=[in_smem()] + [tile(t) for t in range(blocks)],
        out_specs=pl.BlockSpec(shape, lambda i: (0, 0)),
        out_shape=jax.ShapeDtypeStruct(shape, F32),
        scratch_shapes=[
            pltpu.VMEM((count // GROUP * 16 + SPARE, BLOCK), F32),
            pltpu.VMEM((blocks, 64 + SPARE, BLOCK), F32),
        ],
        compiler_params=params(),
        cost_estimate=cost(16 * count * REGION, 4 * 16 * count * REGION),
        name="place_sample_lines",
    )(places, *[sample] * blocks)


def place_lines(places, coeff, awaited):
    count = places.shape[1]
    shape = (count * 16, REGION)
    return pl.pallas_call(
        lines_kernel,
        in_specs=[in_smem(), whole_vmem()] + [anywhere()] * len(awaited),
        out_specs=whole_vmem(),
        out_shape=jax.ShapeDtypeStruct(shape, F32),
        compiler_params=params(),
        cost_estimate=cost(16 * count * REGION, 4 * 16 * count * REGION),
        name="place_lines",
    )(places, coeff, *awaited)


def put_edges(opened, reach_x, reach_y, edges, first):
    half = reach_x // 2
    low = low_lanes(reach_y)
    layer = lambda i: opened[i * reach_y : (i + 1) * reach_y, :]
    for two in range(2):
        place = slice(first + two * reach_y, first + (two + 1) * reach_y)
        edges[0, place, :] = jnp.where(low, layer(2 * two), swap(layer(2 * two + 1)))
        last = half - 4 + 2 * two
        edges[1, place, :] = jnp.where(low, swap(layer(last)), layer(last + 1))


def stack_layers(layers, at, reach_y, stacked):
    tall = stacked.shape[0] // len(layers)
    place = at * up_to(reach_y, 8)
    for i, layer in enumerate(layers):
        stacked[pl.ds(pl.multiple_of(i * tall + place, 8), reach_y), :] = layer


def stack_pieces(parts, reach_x, reach_y, top, opened, stacked, edges, places):
    chip = lax.axis_index("narrow")
    for flip, (part, place) in enumerate(zip(parts, places)):
        first = from_short(part[:top, :])
        opened[...] = from_short(part[top:, :]) * unit(first[0:1], first[1:2])
        layers = [opened[i * reach_y : (i + 1) * reach_y, :] for i in range(reach_x // 2)]
        stack_layers(layers, chip ^ flip, reach_y, stacked)
        put_edges(opened, reach_x, reach_y, edges, place * 2 * reach_y)


def transform_pieces(table, stacked, before, spectrum):
    half = spectrum.shape[0]
    tall = stacked.shape[0] // half

    def tripled(values):
        high, low = split(values)
        return jnp.concatenate([high, low, high], axis=0)

    for i in range(0, half, 2):
        places = range(i, min(i + 2, half))
        held = jnp.concatenate([stacked[j * tall : (j + 1) * tall, :] for j in places], axis=1)
        result = dot(table, tripled(held))
        for j in places:
            made = result[:, (j - i) * 2 * HALF : (j - i + 1) * 2 * HALF]
            spectrum[j] = made if before is None else before[j] + made


def forward_early_kernel(reach_x, reach_y, chips, *refs):
    parts = refs[:chips]
    table_ref, spectrum, edges, opened, stacked = refs[chips:]
    top = parts[0].shape[0] - opened.shape[0]
    stacked[...] = jnp.zeros_like(stacked)
    stack_pieces(parts, reach_x, reach_y, top, opened, stacked, edges, range(chips))
    transform_pieces(table_ref[lax.axis_index("pair")], stacked, None, spectrum)


def stacking_scratch(chips, reach_x, reach_y):
    half = reach_x // 2
    return [
        pltpu.VMEM((up_to(half * reach_y, 16), 2 * HALF), F32),
        pltpu.VMEM((half * chips * up_to(reach_y, 8), 2 * HALF), F32),
    ]


def forward_early(parts, table, reach_x, reach_y):
    half = reach_x // 2
    chips = len(parts)
    return pl.pallas_call(
        functools.partial(forward_early_kernel, reach_x, reach_y, chips),
        in_specs=[whole_vmem()] * (chips + 1),
        out_specs=[whole_vmem()] * 2,
        out_shape=[
            jax.ShapeDtypeStruct((half, GRID, 2 * HALF), F32),
            jax.ShapeDtypeStruct((2, chips * 2 * reach_y + SPARE, 2 * HALF), F32),
        ],
        scratch_shapes=stacking_scratch(chips, reach_x, reach_y),
        compiler_params=params(),
        cost_estimate=cost(EARLY_FLOPS, 4 * half * GRID * 2 * HALF * 2),
        name="forward_early",
    )(*parts, table)


def forward_kernel(reach_x, reach_y, blocks, pieces, awaited, *refs):
    parts = refs[:pieces]
    early_ref, early_edges, table_ref, modes_ref = refs[pieces : pieces + 4]
    refs = refs[pieces + 4 + awaited :]
    spectrum, even_out, layers_out, odd_out, own_out, peers_out, inner_out, *refs = refs
    opened, stacked, edges, slabs, head = refs
    half = reach_x // 2
    pair = lax.axis_size("pair")
    top = parts[0].shape[0] - opened.shape[0]
    stacked[...] = jnp.zeros_like(stacked)
    head[...] = jnp.zeros_like(head)
    for piece in range(pieces):
        first = from_short(parts[piece][:top, :])
        mantissa, exponent = first[2 : 2 + blocks], first[2 + blocks : 2 + 2 * blocks]
        peers_out[piece * blocks : (piece + 1) * blocks, :] = decode_rounded(mantissa, exponent)
        at = 6 + 2 * piece * blocks
        head[at : at + blocks, :] = mantissa
        head[at + blocks : at + 2 * blocks, :] = exponent
    rows = 2 * reach_y
    for chip in range(pieces // pair):
        place = chip * pair * rows
        edges[:, place : place + rows, :] = early_edges[:, chip * rows : (chip + 1) * rows, :]
    before = early_ref
    for core in range(1, pair):
        places = range(core, pieces, pair)
        stack_pieces(parts[core::pair], reach_x, reach_y, top, opened, stacked, edges, places)
        transform_pieces(table_ref[lax.axis_index("pair") ^ core], stacked, before, spectrum)
        before = spectrum

    chunk = 256

    def body(index, largest):
        rows = pl.ds(pl.multiple_of(index * chunk, chunk), chunk)
        low = low_lanes(chunk)
        decay = modes_ref[0, rows, :]
        log_decay = modes_ref[1, rows, :]
        across_half = jnp.exp(half * log_decay)
        across_cut = jnp.exp((half - 4) * log_decay)
        layers = [spectrum[i, rows, :] for i in range(half)]
        run = layers[0]
        cut_right = run
        for i in range(1, half):
            run = decay * run + layers[i]
            if i == half - 5:
                cut_right = run
        right = run
        run = layers[half - 1]
        cut_left = run
        for i in range(half - 2, -1, -1):
            run = decay * run + layers[i]
            if i == 4:
                cut_left = run
        left = run
        inner_out[rows, :] = jnp.where(low, right, left)
        swapped_right, swapped_left = swap(right), swap(left)
        own = jnp.where(low, left + across_half * swapped_left, right + across_half * swapped_right)
        own_out[rows, :] = own
        made = [
            jnp.where(low, own, cut_right + across_cut * swapped_right),
            jnp.where(low, cut_left + across_cut * swapped_left, own),
        ]
        for slab, values in enumerate(made):
            slabs[slab, rows, :] = values
        return tuple(
            jnp.maximum(old, jnp.max(jnp.abs(values).reshape(chunk // 8, 8, 2 * HALF), axis=0))
            for old, values in zip(largest, made)
        )

    zero = jnp.zeros((8, 2 * HALF), F32)
    largest = lax.fori_loop(0, GRID // chunk, body, (zero,) * 2)
    top = head.shape[0]
    low = low_lanes(GRID // 2)
    upper, lower = own_out[: GRID // 2, :], own_out[GRID // 2 :, :]
    packed = [jnp.where(low, swap(upper), lower), jnp.where(low, upper, swap(lower))]

    def send(out, first, parts):
        place = first
        for index, (values, most) in enumerate(parts):
            exponent, fraction = fit_scale(jnp.max(most, axis=0, keepdims=True))
            head[2 * index : 2 * index + 1, :] = exponent
            head[2 * index + 1 : 2 * index + 2, :] = fraction
            out[place : place + values.shape[0], :] = quantize(values, exponent, fraction)
            place += values.shape[0]
        out[:first, :] = to_short(head[:first, :])

    with_most = lambda values: (values, jnp.abs(values))
    border = pieces * 2 * reach_y
    on_left = lax.axis_index("wide") & 1
    for side, (even, odd) in enumerate(((0, 1), (1, 0))):

        @pl.when(on_left == side)
        def _():
            send(even_out, 16, [(slabs[even], largest[even]), with_most(packed[even])])
            send(layers_out, top, [with_most(edges[1 - even, :border, :])])
            send(odd_out, top, [(slabs[odd], largest[odd]), with_most(edges[1 - odd, :border, :])])


def forward(parts, early, early_edges, table, modes, reach_x, reach_y, blocks, awaited):
    pieces = len(parts)
    half = reach_x // 2
    lanes = 2 * HALF
    head = up_to(6 + 2 * pieces * blocks, 16)
    border = pieces * 2 * reach_y
    short = lambda rows: jax.ShapeDtypeStruct((rows, lanes), jnp.int16)
    return pl.pallas_call(
        functools.partial(
            forward_kernel, reach_x, reach_y, blocks, pieces, len(awaited)
        ),
        in_specs=[whole_vmem()] * (pieces + 4) + [anywhere()] * len(awaited),
        out_specs=[whole_vmem()] * 7,
        out_shape=[
            jax.ShapeDtypeStruct((half, GRID, lanes), F32),
            short(16 + GRID + GRID // 2),
            short(head + border),
            short(head + GRID + border),
            jax.ShapeDtypeStruct((GRID, lanes), F32),
            jax.ShapeDtypeStruct((pieces * blocks, BLOCK), F32),
            jax.ShapeDtypeStruct((GRID, lanes), F32),
        ],
        scratch_shapes=stacking_scratch(pieces // table.shape[0], reach_x, reach_y)
        + [
            pltpu.VMEM((2, border + SPARE, lanes), F32),
            pltpu.VMEM((2, GRID, lanes), F32),
            pltpu.VMEM((head, lanes), F32),
        ],
        compiler_params=params(),
        cost_estimate=cost(2 * half * 256 * 256 * 128, 4 * half * GRID * lanes * 2),
        name="forward",
    )(*parts, early, early_edges, table, modes, *awaited)


def opened_part(ref, index, first, rows):
    head = from_short(ref[:16, :])
    scale = unit(head[2 * index : 2 * index + 1], head[2 * index + 1 : 2 * index + 2])
    return from_short(ref[first : first + rows, :]) * scale


def pair_kernel(reach_x, flips, own_ref, even_ref, modes_ref, *refs):
    outs, head = refs[:-1], refs[-1]
    span = reach_x - 4
    here = lax.axis_index("wide")
    low = low_lanes(GRID)
    log_decay = modes_ref[1]
    own = own_ref[...]
    top = even_ref.shape[0] - GRID - GRID // 2
    cut = opened_part(even_ref, 0, top, GRID)
    packed = opened_part(even_ref, 1, top + GRID, GRID // 2)
    from_left = jnp.where(low, cut, jnp.concatenate([swap(packed), packed], axis=0))
    from_right = jnp.where(low, jnp.concatenate([packed, swap(packed)], axis=0), cut)
    partner = jnp.where((here & 1) == 1, from_left, from_right)

    def weight(distances):
        powers = []
        for distance in distances:
            ahead = span * distance - reach_x
            powers.append(jnp.where(distance >= 2, ahead, ahead + GRID).astype(F32))
        return jnp.exp(jnp.where(low, *powers) * log_decay)

    head[...] = jnp.zeros_like(head)
    for flip, out in zip(flips, outs):
        behind = (here ^ flip) - here
        message = own * weight((-behind, behind))
        behind = (here ^ flip) - (here ^ 1)
        beside = jnp.where(jnp.abs(behind) == 1, 0.0, 1.0)
        send_piece(out, head, message + partner * (weight((-behind, behind)) * beside))


def pair_messages(own, from_even, modes, reach_x, flips):
    return pl.pallas_call(
        functools.partial(pair_kernel, reach_x, flips),
        in_specs=[whole_vmem()] * 3,
        out_specs=[whole_vmem()] * len(flips),
        out_shape=[jax.ShapeDtypeStruct((16 + GRID, 2 * HALF), jnp.int16)] * len(flips),
        scratch_shapes=[pltpu.VMEM((16, 2 * HALF), F32)],
        compiler_params=params(),
        cost_estimate=cost(16 * GRID * 2 * HALF, 4 * GRID * 2 * HALF * (6 + len(flips))),
        name="pair_messages",
    )(own, from_even, modes)


def borders_kernel(reach_y, pieces, layers_ref, odd_ref, table_ref, out_ref, stacked, partial):
    on_left = (lax.axis_index("wide") & 1) == 1
    pair = lax.axis_size("pair")
    rows = pieces * 2 * reach_y
    even = opened_part(layers_ref, 0, layers_ref.shape[0] - rows, rows)
    odd = opened_part(odd_ref, 1, odd_ref.shape[0] - rows, rows)
    left, right = jnp.where(on_left, even, odd), jnp.where(on_left, odd, even)
    low = low_lanes(rows)
    both = [jnp.where(low, left, swap(right)), jnp.where(low, swap(left), right)]
    core = lax.axis_index("pair")
    chip = lax.axis_index("narrow")
    stacked[...] = jnp.zeros_like(stacked)
    before = None
    for other in range(pair):
        for flip in range(pieces // pair):
            first = (flip * pair + other) * 2 * reach_y
            layers = [
                values[first + two * reach_y : first + (two + 1) * reach_y]
                for two in range(2)
                for values in both
            ]
            stack_layers(layers, chip ^ flip, reach_y, stacked)
        target = out_ref if other == pair - 1 else partial
        transform_pieces(table_ref[core ^ other], stacked, before, target)
        before = target


def borders(layers, from_odd, table, reach_y, pieces):
    chips = pieces // table.shape[0]
    shape = (4, GRID, 2 * HALF)
    return pl.pallas_call(
        functools.partial(borders_kernel, reach_y, pieces),
        in_specs=[whole_vmem()] * 3,
        out_specs=whole_vmem(),
        out_shape=jax.ShapeDtypeStruct(shape, F32),
        scratch_shapes=[
            pltpu.VMEM((4 * chips * up_to(reach_y, 8), 2 * HALF), F32),
            pltpu.VMEM(shape, F32),
        ],
        compiler_params=params(),
        cost_estimate=cost(2 * 4 * 256 * 256 * 128, 4 * 6 * GRID * 2 * HALF),
        name="borders",
    )(layers, from_odd, table)


def send_fields(outs, flips, reach_y, field_high, field_low, high_ref, low_ref, ready, head):
    half = field_high.shape[0]
    mine = y_position()
    pitch = up_to(reach_y, 16)
    pick = lambda ref: jnp.concatenate([ref[mine ^ flip] for flip in flips], axis=0)
    table = (pick(high_ref), pick(low_ref))
    for i in range(0, half, 2):
        many = min(2, half - i)
        join = lambda ref: jnp.concatenate([ref[i + j] for j in range(many)], axis=1)
        result = dot_three(table, (join(field_high), join(field_low)))
        for j in range(many):
            for piece in range(len(flips)):
                ready[piece, (i + j) * reach_y : (i + j + 1) * reach_y, :] = result[
                    piece * pitch : piece * pitch + reach_y, j * 2 * HALF : (j + 1) * 2 * HALF
                ]
    head[...] = jnp.zeros_like(head)
    for piece, out in enumerate(outs):
        if ready.shape[1] > half * reach_y:
            ready[piece, half * reach_y :, :] = jnp.zeros_like(ready[piece, half * reach_y :, :])
        send_piece(out, head, ready[piece])


def inverse_kernel(reach_x, reach_y, flips, fars, *refs):
    spectrum, border_ref, from_even, from_odd, own_ref, inner_ref, *far_refs = refs[: 6 + fars]
    refs = refs[6 + fars :]
    high_ref, low_ref, modes_ref = refs[:3]
    outs = refs[3 : 3 + len(flips)]
    field_high, field_low, ready, head = refs[3 + len(flips) :]
    half = reach_x // 2
    span = reach_x - 4
    chunk = 256
    border_rows = lax.axis_size("narrow") * lax.axis_size("pair") * 2 * reach_y
    tops = from_even.shape[0] - GRID - GRID // 2, from_odd.shape[0] - GRID - border_rows
    on_left = (lax.axis_index("wide") & 1) == 1
    moment_units = []
    for ref in (from_even, from_odd):
        first = from_short(ref[:16, :])
        moment_units.append(unit(first[0:1], first[1:2]))

    far_units = []
    for ref in far_refs:
        first = from_short(ref[:16, :])
        far_units.append(unit(first[0:1], first[1:2]))

    def body(index, carry):
        first = pl.multiple_of(index * chunk, chunk)
        rows = pl.ds(first, chunk)
        low = low_lanes(chunk)
        decay = modes_ref[0, rows, :]
        log_decay = modes_ref[1, rows, :]
        ring = modes_ref[2, rows, :]
        gain = modes_ref[3, rows, :]
        across_half = jnp.exp(half * log_decay)
        across_cut = jnp.exp((half - 4) * log_decay)
        around = jnp.exp((GRID - 4) * log_decay)
        beside = jnp.exp((GRID - reach_x - span) * log_decay)
        layers = [spectrum[i, rows, :] for i in range(half)]

        even, odd = (
            from_short(ref[pl.ds(pl.multiple_of(top + index * chunk, 16), chunk), :]) * scale
            for ref, top, scale in zip((from_even, from_odd), tops, moment_units)
        )
        left_moments, right_moments = jnp.where(on_left, even, odd), jnp.where(on_left, odd, even)
        border = [border_ref[i, rows, :] for i in range(4)]
        zero = jnp.zeros_like(decay)
        head_sum = border[0]
        for i in range(1, 4):
            head_sum = decay * head_sum + border[i]
        tail_sum = border[3]
        for i in range(2, -1, -1):
            tail_sum = decay * tail_sum + border[i]
        for i in range(4):
            layers[i] = layers[i] + jnp.where(low, border[i], zero)
        for i in range(4):
            place = half - 4 + i
            layers[place] = layers[place] + jnp.where(low, zero, border[i])
        total = own_ref[rows, :] * jnp.exp((GRID - reach_x) * log_decay)
        at = pl.ds(pl.multiple_of(16 + index * chunk, 16), chunk)
        for ref, scale in zip(far_refs, far_units):
            total = total + from_short(ref[at, :]) * scale
        one = jnp.ones_like(decay)
        total = total + left_moments * jnp.where(low, beside, one)
        total = total + right_moments * jnp.where(low, one, beside)
        shared = jnp.where(low, head_sum, tail_sum)
        entering = (swap(total) + around * shared) * ring
        leaving = swap(across_half * entering + across_cut * shared + inner_ref[rows, :])
        run = jnp.where(low, entering, leaving)
        forward_runs = []
        for i in range(half):
            run = decay * run + layers[i]
            forward_runs.append(run)
        run = jnp.where(low, leaving, entering)
        for i in range(half - 1, -1, -1):
            ahead = decay * run
            high, rest = split(gain * (forward_runs[i] + ahead))
            field_high[i, rows, :] = high
            field_low[i, rows, :] = rest
            run = ahead + layers[i]
        return carry

    lax.fori_loop(0, GRID // chunk, body, 0)
    send_fields(outs, flips, reach_y, field_high, field_low, high_ref, low_ref, ready, head)


def inverse(
    spectrum, border, from_even, from_odd, own, inner, fars, table, modes, reach_x, reach_y, flips
):
    half = reach_x // 2
    lanes = 2 * HALF
    body = up_to(half * reach_y, 16)
    shapes = [jax.ShapeDtypeStruct((16 + body, lanes), jnp.int16)] * len(flips)
    shapes += [jax.ShapeDtypeStruct((half, GRID, lanes), BF16)] * 2
    return pl.pallas_call(
        functools.partial(inverse_kernel, reach_x, reach_y, flips, len(fars)),
        in_specs=[whole_vmem()] * (9 + len(fars)),
        out_specs=[whole_vmem()] * len(shapes),
        out_shape=shapes,
        scratch_shapes=[
            pltpu.VMEM((len(flips), body, lanes), F32),
            pltpu.VMEM((16, lanes), F32),
        ],
        compiler_params=params(),
        cost_estimate=cost(2 * half * 256 * 256 * 128, 4 * half * GRID * lanes * 2),
        name="inverse",
    )(spectrum, border, from_even, from_odd, own, inner, *fars, *table, modes)


def inverse_rest_kernel(reach_y, flips, field_high, field_low, high_ref, low_ref, *refs):
    outs, (ready, head) = refs[: len(flips)], refs[len(flips) :]
    send_fields(outs, flips, reach_y, field_high, field_low, high_ref, low_ref, ready, head)


def inverse_rest(field, table, reach_y, flips):
    half = field[0].shape[0]
    lanes = 2 * HALF
    body = up_to(half * reach_y, 16)
    return pl.pallas_call(
        functools.partial(inverse_rest_kernel, reach_y, flips),
        in_specs=[whole_vmem()] * 4,
        out_specs=[whole_vmem()] * len(flips),
        out_shape=[jax.ShapeDtypeStruct((16 + body, lanes), jnp.int16)] * len(flips),
        scratch_shapes=[
            pltpu.VMEM((len(flips), body, lanes), F32),
            pltpu.VMEM((16, lanes), F32),
        ],
        compiler_params=params(),
        cost_estimate=cost(2 * half * 256 * 256 * 128, 4 * half * GRID * lanes * 2),
        name="inverse_rest",
    )(*field, *table)


def sum_rows(values):
    row = lax.broadcasted_iota(jnp.int32, values[0].shape, 0)
    for step in (4, 2, 1):
        low = (row & step) == 0
        paired = []
        for one, other in zip(values[: len(values) // 2], values[len(values) // 2 :]):
            kept = jnp.where(low, one, other)
            moved = jnp.where(low, other, one)
            if step == 4:
                moved = pltpu.roll(moved, 4, 0)
            else:
                moved = jnp.where(low, pltpu.roll(moved, 8 - step, 0), pltpu.roll(moved, step, 0))
            paired.append(kept + moved)
        values = paired
    return values[0]


def z_lines(parts, flips, high_ref, low_ref):
    mine = y_position()
    opened = []
    for part in parts:
        first = from_short(part[:16, :])
        opened.append(from_short(part[16:, :]) * unit(first[0:1], first[1:2]))
    values = split(jnp.concatenate(opened, axis=1))
    pick = lambda ref: jnp.concatenate([ref[mine ^ flip] for flip in flips], axis=0)
    return dot_three(values, (pick(high_ref), pick(low_ref)))


def sample_early_kernel(flips, *refs):
    *parts, high_ref, low_ref, out_ref = refs
    out_ref[...] = z_lines(parts, flips, high_ref, low_ref)


def sample_early(parts, flips, table):
    rows = parts[0].shape[0] - 16
    return pl.pallas_call(
        functools.partial(sample_early_kernel, flips),
        in_specs=[whole_vmem()] * (len(parts) + 2),
        out_specs=whole_vmem(),
        out_shape=jax.ShapeDtypeStruct((rows, 2 * REGION), F32),
        compiler_params=params(),
        cost_estimate=cost(EARLY_FLOPS, 4 * rows * 512),
        name="sample_early",
    )(*parts, *table)


def sample_kernel(last, reach_x, reach_y, flips, place_in, *refs):
    parts = refs[: len(flips)]
    early_ref, high_ref, low_ref, line_ref, own_ref, vector_ref, near_ref, out_ref = refs[
        len(flips) : len(flips) + 8
    ]
    flat, field, sums, place_ref, sem = refs[len(flips) + 8 :]
    copy = pltpu.make_async_copy(place_in, place_ref, sem)
    copy.start()
    half_rows = reach_x * reach_y // 2
    both = early_ref[...] + z_lines(parts, flips, high_ref, low_ref)
    flat[:half_rows, :] = both[:half_rows, :REGION]
    flat[half_rows : 2 * half_rows, :] = both[:half_rows, REGION:]
    for x in range(reach_x):
        layer = flat[x * reach_y : (x + 1) * reach_y, :]
        for row in pair_rows(x, reach_x, reach_y):
            field[pl.ds(row, reach_y, stride=2), :] = layer
    count = place_ref.shape[1]

    def body(group, carry):
        for eight in range(0, GROUP, 8):
            totals = []
            for local in range(eight, eight + 8):
                panel = group * GROUP + local
                row = place_ref[0, panel]
                first = pl.multiple_of(panel * 16, 16)
                totals.append(
                    field[pl.ds(row, 8), :] * line_ref[pl.ds(first, 8), :]
                    + field[pl.ds(row + 2 * reach_y, 8), :] * line_ref[pl.ds(first + 8, 8), :]
                )
            sums[pl.ds(pl.multiple_of(group * GROUP + eight, 8), 8), :] = sum_rows(totals)
        return carry

    copy.wait()
    lax.fori_loop(0, count // GROUP, body, 0)
    first, rest = split(sums[...])
    second, third = split(sums[...] - first.astype(F32))
    across = lambda values: lax.dot_general(
        jnp.ones((16, REGION), BF16),
        values,
        (((1,), (1,)), ((), ())),
        preferred_element_type=F32,
    )
    sampled = across(first) + (across(second) + across(third))
    for block in range(count // BLOCK):
        lane = slice(block * BLOCK, (block + 1) * BLOCK)
        row = slice(block, block + 1)
        vector = vector_ref[row, :]
        image = jnp.where(own_ref[row, :] == 1, 0.0, 0.5 * vector) + sampled[:1, lane]
        image = image + near_ref[row, :]
        if last:
            out_ref[0:1, lane] = vector
            out_ref[1:2, lane] = image
        else:
            out_ref[row, :] = image


def sample(last, places, parts, flips, early, table, lines, flag, vector, near, reach_x, reach_y):
    count = places.shape[1]
    blocks = count // BLOCK
    shape = (2, count) if last else (blocks, BLOCK)
    return pl.pallas_call(
        functools.partial(sample_kernel, last, reach_x, reach_y, flips),
        in_specs=[anywhere()] + [whole_vmem()] * (len(parts) + 7),
        out_specs=whole_vmem(),
        out_shape=jax.ShapeDtypeStruct(shape, F32),
        scratch_shapes=[
            pltpu.VMEM((reach_x * reach_y + SPARE, REGION), F32),
            pltpu.VMEM((pair_count(reach_x, reach_y), REGION), F32),
            pltpu.VMEM((count, REGION), F32),
            pltpu.SMEM((2, count), jnp.int32),
            pltpu.SemaphoreType.DMA,
        ],
        compiler_params=params(),
        cost_estimate=cost(reach_x * reach_y * 256 * 512, 4 * 16 * count * REGION),
        name="sample",
    )(
        places,
        *parts,
        early,
        *table,
        lines,
        flag.reshape(blocks, BLOCK),
        vector.reshape(blocks, BLOCK),
        near,
    )


def near_kernel(slots, blocks, place_ref, target_ref, *refs):
    even_ref, odd_ref, peers_ref, tile_ref = refs[:4]
    out_ref, held = refs[-2:]
    count = peers_ref.shape[0]
    held[count : 2 * count, :] = peers_ref[...]
    on_left = lax.axis_index("wide") & 1
    for side, ref in ((1 - on_left, even_ref), (on_left, odd_ref)):
        top = from_short(ref[...])
        for piece in range(count // blocks):
            at = 6 + 2 * piece * blocks
            held[pl.ds(side * (2 * count) + piece * blocks, blocks), :] = decode_rounded(
                top[at : at + blocks], top[at + blocks : at + 2 * blocks]
            )
    out_ref[...] = jnp.zeros_like(out_ref)
    for slot in range(slots):
        picked = held[pl.ds(place_ref[slot], 1), :]
        picked = jnp.broadcast_to(picked, (16, BLOCK)).astype(BF16)
        product = lax.dot_general(
            picked,
            tile_ref[slot],
            (((1,), (1,)), ((), ())),
            preferred_element_type=F32,
        )
        target = pl.ds(target_ref[slot], 1)
        out_ref[target, :] = out_ref[target, :] + product[:1]


def near_field(places, targets, from_even, from_odd, peers, tiles, blocks, out_rows, awaited):
    slots = tiles.shape[0]
    head = up_to(6 + 2 * peers.shape[0], 16)
    constant = lambda shape: pl.BlockSpec(shape, lambda i: (0,) * len(shape))
    return pl.pallas_call(
        functools.partial(near_kernel, slots, blocks),
        grid=(1,),
        in_specs=[
            in_smem(),
            in_smem(),
            constant((head, BLOCK)),
            constant((head, BLOCK)),
            constant(peers.shape),
            constant(tiles.shape),
        ]
        + [anywhere()] * len(awaited),
        out_specs=constant((out_rows, BLOCK)),
        out_shape=jax.ShapeDtypeStruct((out_rows, BLOCK), F32),
        scratch_shapes=[pltpu.VMEM((3 * peers.shape[0] + SPARE, BLOCK), F32)],
        compiler_params=params(),
        cost_estimate=cost(2 * slots * 16 * BLOCK * BLOCK, 2 * slots * BLOCK * BLOCK),
        name="near_field",
    )(places, targets, from_even, from_odd, peers, tiles, *awaited)


def shards(
    density,
    surface_flag,
    stencil_base,
    sample_weights,
    dipole_weights,
    near_target,
    near_source,
    near_tiles,
):
    x_count = lax.axis_size("wide")
    y_count = lax.axis_size(Y_AXES)
    y_index = lax.axis_index(Y_AXES)
    pair = lax.axis_size("pair")
    span_x = REGION // x_count
    span_y = REGION // y_count
    reach_x = span_x + 4
    reach_y = span_y + 4
    count = density.shape[0]
    blocks = count // BLOCK

    z_forward, z_inverse, y_forward, y_inverse, modes = tables(y_count, pair, span_y)
    modes = lax.dynamic_index_in_dim(jnp.asarray(modes), y_index, 0, keepdims=False)

    neighbour = near_source // blocks
    flip = (y_index + neighbour % 3 - 1) ^ y_index
    sources = ((neighbour // 3) * y_count + flip) * blocks + near_source % blocks
    out_rows = up_to(blocks + 1, 8)
    live = near_target >= 0
    sources = jnp.where(live, sources, 0)
    targets = jnp.where(live, near_target, out_rows - 1)

    swaps = lambda pairs: [(i, j) for i, j in pairs] + [(j, i) for i, j in pairs]
    even_swap = swaps([(i, i + 1) for i in range(0, x_count - 1, 2)])
    odd_swap = swaps([(i, i + 1) for i in range(1, x_count - 1, 2)])
    far_flips = list(range(2, x_count, 2))

    first, inside, local = list(range(pair, y_count)), list(range(1, pair)), [0]
    same_core = list(range(0, y_count, pair))
    other_core = [flip for flip in range(y_count) if flip not in same_core]

    def turned(sent, then):
        arrived = [None] * y_count
        for flip, part in zip(first + inside + local, list(sent) + list(then)):
            swap_pairs = [(i, i ^ flip) for i in range(y_count)]
            arrived[flip] = part if flip == 0 else lax.ppermute(part, Y_AXES, swap_pairs)
        return arrived

    def chosen(parts, flips):
        return [parts[flip] for flip in flips]

    def convolve_and_sample(last, vector, sent, both, table, places, sample_lines, awaited):
        then = [part for flips in (inside, local) for part in spread_rest(vector, both, table, flips)]
        arrived = turned(sent, then)
        early, edges = forward_early(chosen(arrived, same_core), y_forward, reach_x, reach_y)
        spectrum, even_message, layers, odd_message, own, peers, inner = forward(
            arrived, early, edges, y_forward, modes, reach_x, reach_y, blocks, awaited
        )
        from_even = lax.ppermute(even_message, "wide", even_swap)
        from_odd = lax.ppermute(odd_message, "wide", odd_swap)
        even_layers = lax.ppermute(layers, "wide", even_swap)
        fars = [
            lax.ppermute(message, "wide", [(i, i ^ flip) for i in range(x_count)])
            for flip, message in zip(
                far_flips, pair_messages(own, from_even, modes, reach_x, far_flips)
            )
        ]
        *sent, high, low = inverse(
            spectrum,
            borders(even_layers, from_odd, y_forward, reach_y, y_count),
            from_even,
            from_odd,
            own,
            inner,
            fars,
            y_inverse,
            modes,
            reach_x,
            reach_y,
            first,
        )
        then = [
            part
            for flips in (inside, local)
            for part in inverse_rest((high, low), y_inverse, reach_y, flips)
        ]
        near_part = near_field(
            sources, targets, even_layers, from_odd, peers, near_tiles, blocks, out_rows, then[:1]
        )
        arrived = turned(sent, then)
        image = sample(
            last,
            places,
            chosen(arrived, other_core),
            other_core,
            sample_early(chosen(arrived, same_core), same_core, z_inverse),
            z_inverse,
            sample_lines,
            surface_flag,
            vector,
            near_part,
            reach_x,
            reach_y,
        )
        return image, near_part

    raw = (stencil_base, surface_flag, sample_weights, dipole_weights)
    *sent, wide_high, wide_low, source_coeff, places, vector, high, low = spread(
        density, z_forward, None, raw, reach_x, reach_y, first
    )
    z_forward = (high, low)
    sample_lines = place_sample_lines(places, sample_weights)
    vector, near_part = convolve_and_sample(
        False,
        vector,
        sent,
        (wide_high, wide_low),
        z_forward,
        places,
        sample_lines,
        [sample_lines],
    )
    source_lines = place_lines(places, source_coeff, [near_part])
    *sent, wide_high, wide_low = spread(
        vector.reshape(-1), z_forward, (places, source_lines), None, reach_x, reach_y, first
    )
    both_images, _ = convolve_and_sample(
        True, vector, sent, (wide_high, wide_low), z_forward, places, sample_lines, []
    )
    return both_images


def solution(mesh):
    panels = P(("groups",) + ALL_AXES)
    columns = P(None, ("groups",) + ALL_AXES)
    in_specs = (
        panels,
        panels,
        columns,
        columns,
        columns,
        panels,
        panels,
        P(("groups",) + ALL_AXES, None, None),
    )
    return jax.shard_map(
        shards, mesh=mesh, in_specs=in_specs, out_specs=columns, check_vma=False
    )
```

```python
import functools
import math

import jax
import jax.numpy as jnp
import numpy as np
from jax import lax
from jax.experimental import pallas as pl
from jax.experimental.pallas import tpu as pltpu
from jax.sharding import PartitionSpec as P

GRID = 256
REGION = 128
BLOCK = 128
HALF = 64
KERNEL_GAIN = 4.0
SCREEN = 1.0 / 1024.0
LN2 = math.log(2.0)
SPARE = 16
Y_AXES = ("narrow", "pair")
ALL_AXES = ("wide", "narrow", "pair")
F32 = jnp.float32
BF16 = jnp.bfloat16
VMEM_LIMIT = 24 * 1024 * 1024
START_LIMIT = VMEM_LIMIT
EARLY_FLOPS = 5 * 10**9
GROUP = 32
CHAINS = 1


def cas(angles):
    return np.cos(angles) + np.sin(angles)


def up_to(count, multiple):
    return -(-count // multiple) * multiple


def low_lanes(rows):
    return lax.broadcasted_iota(jnp.int32, (rows, 2 * HALF), 1) < HALF


def swap(values):
    return pltpu.roll(values, HALF, 1)


def split(values):
    high = values.astype(BF16)
    return high, (values - high.astype(F32)).astype(BF16)


def dot(left, right):
    return jnp.dot(left, right, preferred_element_type=F32)


def dot_three(left, right):
    return dot(left[0], right[0]) + (dot(left[0], right[1]) + dot(left[1], right[0]))


def params():
    return pltpu.CompilerParams(vmem_limit_bytes=VMEM_LIMIT)


def whole_vmem():
    return pl.BlockSpec(memory_space=pltpu.VMEM)


def anywhere():
    return pl.BlockSpec(memory_space=pl.ANY)


def in_smem():
    return pl.BlockSpec(memory_space=pltpu.SMEM)


def cost(flops, moved):
    return pl.CostEstimate(flops=flops, bytes_accessed=moved, transcendentals=0)


def full_scale(exponent, fraction):
    return fraction * jnp.exp(exponent * LN2) * (1.0 / 1024.0)


def fit_scale(largest):
    largest = jnp.maximum(largest, 1e-30)
    exponent = jnp.floor(jnp.log(largest) * (1.0 / LN2))
    fraction = jnp.ceil(largest * jnp.exp(-exponent * LN2) * 1024.0) + 1.0
    return exponent, fraction


def to_short(values):
    return values.astype(jnp.int32).astype(jnp.int16)


def from_short(values):
    return values.astype(jnp.int32).astype(F32)


def quantize(values, exponent, fraction):
    return to_short(jnp.round(values * (32767.0 / full_scale(exponent, fraction))))


def unit(exponent, fraction):
    return full_scale(exponent, fraction) * (1.0 / 32767.0)


def encode_rounded(values):
    rounded = values.astype(BF16).astype(F32)
    size = jnp.maximum(jnp.abs(rounded), 1e-30)
    exponent = jnp.floor(jnp.log(size) * (1.0 / LN2))
    return jnp.round(rounded * jnp.exp((10.0 - exponent) * LN2)), exponent


def decode_rounded(mantissa, exponent):
    return (mantissa * jnp.exp((exponent - 10.0) * LN2)).astype(BF16).astype(F32)


def send_piece(out, head, values):
    exponent, fraction = fit_scale(jnp.max(jnp.abs(values), axis=0, keepdims=True))
    head[0:1, :] = exponent
    head[1:2, :] = fraction
    top = head.shape[0]
    out[:top, :] = to_short(head[...])
    out[top:, :] = quantize(values, exponent, fraction)


def y_position():
    return lax.axis_index("narrow") * lax.axis_size("pair") + lax.axis_index("pair")


def halves(table):
    high = table.astype(jnp.bfloat16)
    return high, (table - high.astype(np.float64)).astype(jnp.bfloat16)


def tables(y_count, pair, span_y):
    depth = GRID // y_count
    reach = span_y + 4
    waves = np.arange(GRID)
    step = 2.0 * np.pi / GRID
    z_table = cas(step * np.outer(np.arange(REGION), waves))
    z_forward = np.zeros((y_count, 2 * REGION, 2 * HALF))
    z_inverse = np.zeros((y_count, 2 * HALF, 2 * REGION))
    symbols = 4.0 * np.sin(np.pi * waves / GRID) ** 2
    shift = np.full((y_count, GRID, 2 * HALF), 1.0)
    y_forward = np.zeros((GRID, y_count, up_to(reach, 8)))
    y_inverse = np.zeros((y_count, up_to(reach, 16), GRID))
    for block in range(y_count):
        mine = z_table[:, block * depth : (block + 1) * depth]
        for half in range(2):
            rows = slice(half * REGION, (half + 1) * REGION)
            lanes = slice(half * HALF, half * HALF + depth)
            z_forward[block, rows, lanes] = mine
            z_inverse[block, lanes, rows] = mine.T / GRID
            shift[block, :, lanes] = (
                SCREEN + symbols[:, None] + symbols[None, block * depth : (block + 1) * depth]
            )
        cells = block * span_y - 2 + np.arange(reach)
        y_table = cas(step * np.outer(waves, cells))
        y_forward[:, block, :reach] = y_table
        y_inverse[block, :reach] = y_table.T / GRID
    y_forward = y_forward.reshape(GRID, y_count // pair, pair, -1).transpose(2, 0, 1, 3)
    y_forward = halves(y_forward.reshape(pair, GRID, -1))
    y_forward = np.concatenate([y_forward[0], y_forward[0], y_forward[1]], axis=2)
    root = np.sqrt(shift * (shift + 4.0))
    decay = 2.0 / (2.0 + shift + root)
    log_decay = np.log(decay)
    ring = 1.0 / (1.0 - np.exp(GRID * log_decay))
    gain = KERNEL_GAIN / root
    modes = np.stack([decay, log_decay, ring, gain], axis=1).astype(np.float32)
    return (
        halves(z_forward),
        halves(z_inverse),
        y_forward,
        halves(y_inverse),
        modes,
    )


def mixing_matrix():
    place = lax.broadcasted_iota(jnp.int32, (4 * BLOCK, 4 * BLOCK), 0)
    lane = lax.broadcasted_iota(jnp.int32, (4 * BLOCK, 4 * BLOCK), 1)
    return jnp.where(lane == 4 * (place % BLOCK) + place // BLOCK, 1.0, 0.0).astype(BF16)


def weave(tiles, mixing, out):
    weights = jnp.concatenate([jnp.concatenate(tile, axis=1) for tile in tiles], axis=0)
    first, rest = split(weights)
    second, third = split(weights - first.astype(F32))
    woven = dot(first, mixing) + (dot(second, mixing) + dot(third, mixing))
    for tile in range(len(tiles)):
        for part in range(BLOCK // GROUP):
            at = (tile * (BLOCK // GROUP) + part) * 16
            lanes = slice(part * BLOCK, (part + 1) * BLOCK)
            for a in range(4):
                row = tile * 16 + 4 * a
                out[pl.ds(at + 8 * (a // 2) + a % 2, 4, stride=2), :] = woven[row : row + 4, lanes]


def by_depth(ref):
    return [ref[pl.ds(depth, 16, stride=4), :] for depth in range(4)]


def pair_rows(x, reach_x, reach_y):
    even = (x // 2) * 2 * reach_y + x % 2
    if x == 0 or x == reach_x - 1:
        return [even]
    return [even, reach_x * reach_y + ((x - 1) // 2) * 2 * reach_y + (x - 1) % 2]


def pair_count(reach_x, reach_y):
    return (2 * reach_x - 2) * reach_y + SPARE


def in_window(lanes, depth):
    return ((lanes - depth) & -4) == 0


def add_panels(reach, woven, vector_ref, place_ref, weight_ref, grids):
    lanes = lax.broadcasted_iota(jnp.int32, (8, REGION), 1)

    def body(group, carry):
        at = pl.multiple_of(group * 16, 16)
        coeff = [weight_ref[pl.ds(at + 8 * q, 8), :] for q in range(2)] if woven else None
        for local in range(GROUP):
            panel = group * GROUP + local
            grid = grids[local % len(grids)]
            row = place_ref[0, panel]
            value = vector_ref[panel]
            if woven:
                depth = place_ref[1, panel]
                shift = (depth - 4 * local) & (REGION - 1)
                value = jnp.where(in_window(lanes, depth), value, 0.0)
                lines = [pltpu.roll(coeff[q], shift, 1) for q in range(2)]
            else:
                first = pl.multiple_of(panel * 16, 16)
                lines = [weight_ref[pl.ds(first + 8 * q, 8), :] for q in range(2)]
            places = [pl.ds(row, 8), pl.ds(row + 2 * reach, 8)]
            held = [grid[place, :] for place in places]
            for q in range(2):
                grid[places[q], :] = held[q] + lines[q] * value
        return carry

    lax.fori_loop(0, vector_ref.shape[0] // GROUP, body, 0)


def send_pieces(outs, flips, head, rounded, both, high_ref, low_ref):
    blocks = rounded.shape[0]
    mantissa, exponent = encode_rounded(rounded)
    head[...] = jnp.zeros_like(head)
    head[2 : 2 + blocks, :] = mantissa
    head[2 + blocks : 2 + 2 * blocks, :] = exponent
    mine = y_position()
    for at in range(0, len(flips), 2):
        pick = lambda ref: jnp.concatenate([ref[mine ^ flip] for flip in flips[at : at + 2]], axis=1)
        result = dot_three(both, (pick(high_ref), pick(low_ref)))
        for i, out in enumerate(outs[at : at + 2]):
            send_piece(out, head, result[:, i * 2 * HALF : (i + 1) * 2 * HALF])


def spread_grid(reach_x, reach_y, rounded, tables, outs, flips, wides, head, total, grids):
    for x in range(reach_x):
        parts = [
            grid[pl.ds(row, reach_y, stride=2), :]
            for row in pair_rows(x, reach_x, reach_y)
            for grid in grids
        ]
        total[x * reach_y : (x + 1) * reach_y, :] = sum(parts[1:], parts[0])
    half = reach_x * reach_y // 2
    both = jnp.concatenate([total[:half, :], total[half : 2 * half, :]], axis=1)
    extra = wides[0].shape[0] - half
    if extra:
        both = jnp.concatenate([both, jnp.zeros((extra, 2 * REGION), F32)], axis=0)
    both = split(both)
    for wide, values in zip(wides, both):
        wide[...] = values
    send_pieces(outs, flips, head, rounded, both, *tables)


def start_kernel(reach_x, reach_y, flips, *refs):
    vector_in, *remote = refs[:8]
    refs = refs[8:]
    outs, refs = refs[: len(flips)], refs[len(flips) :]
    wides, (weight_ref, places_out), refs = refs[:2], refs[2:4], refs[4:]
    rounded, high, low, stencil, flag, samples, dipoles, vector_ref = refs[:8]
    place_ref, sems, head, total = refs[8:12]
    grids = refs[12:]
    tiles = samples.shape[0]
    copies = []
    fetch = lambda source, target: copies.append(
        pltpu.make_async_copy(source, target, sems.at[len(copies)])
    )
    rounded_in, high_in, low_in, stencil_in, flag_in, sample_in, dipole_in = remote
    fetch(stencil_in, stencil)
    fetch(flag_in, flag)
    fetch(vector_in, vector_ref)
    for tile in range(tiles):
        lanes = pl.ds(tile * BLOCK, BLOCK)
        fetch(sample_in.at[:, lanes], samples.at[tile, pl.ds(0, 64)])
        fetch(dipole_in.at[:, lanes], dipoles.at[tile, pl.ds(0, 64)])
    needed_first = len(copies)
    fetch(rounded_in, rounded)
    fetch(high_in, high)
    fetch(low_in, low)
    for copy in copies:
        copy.start()
    for grid in grids:
        grid[...] = jnp.zeros_like(grid)
    mixing = mixing_matrix()
    copies[0].wait()
    span_x, span_y = reach_x - 4, reach_y - 4
    local_x = stencil[0:1, :] - (lax.axis_index("wide") * span_x - 2)
    local_y = stencil[1:2, :] - (y_position() * span_y - 2)
    odd = local_x & 1
    places_out[0:1, :] = odd * (reach_x * reach_y) + (local_x >> 1) * (2 * reach_y) + 2 * local_y
    places_out[1:2, :] = stencil[2:3, :]
    to_scalar = pltpu.make_async_copy(places_out, place_ref, sems.at[len(copies)])
    to_scalar.start()
    for copy in copies[1:needed_first]:
        copy.wait()
    sources = []
    for tile in range(tiles):
        charged = flag[:, tile * BLOCK : (tile + 1) * BLOCK] == 1
        pairs = zip(by_depth(samples.at[tile]), by_depth(dipoles.at[tile]))
        sources.append([jnp.where(charged, -sample, dipole) for sample, dipole in pairs])
    weave(sources, mixing, weight_ref)
    to_scalar.wait()
    add_panels(reach_y, True, vector_ref, place_ref, weight_ref, grids)
    for copy in copies[needed_first:]:
        copy.wait()
    spread_grid(
        reach_x, reach_y, rounded[...], (high, low), outs, flips, wides, head, total, grids
    )


def spread_kernel(reach_x, reach_y, flips, *refs):
    vector_in, place_in, rounded_ref, high_ref, low_ref, line_ref = refs[:6]
    refs = refs[6:]
    outs, wides, (vector_ref, place_ref, sems, head, total), grids = (
        refs[: len(flips)],
        refs[len(flips) : len(flips) + 2],
        refs[len(flips) + 2 : len(flips) + 7],
        refs[len(flips) + 7 :],
    )
    copies = [
        pltpu.make_async_copy(vector_in, vector_ref, sems.at[0]),
        pltpu.make_async_copy(place_in, place_ref, sems.at[1]),
    ]
    for copy in copies:
        copy.start()
    for grid in grids:
        grid[...] = jnp.zeros_like(grid)
    for copy in copies:
        copy.wait()
    add_panels(reach_y, False, vector_ref, place_ref, line_ref, grids)
    spread_grid(
        reach_x,
        reach_y,
        rounded_ref[...],
        (high_ref, low_ref),
        outs,
        flips,
        wides,
        head,
        total,
        grids,
    )


def spread(vector, table, placed, raw, reach_x, reach_y, flips):
    count = vector.shape[0]
    half = reach_x * reach_y // 2
    blocks = count // BLOCK
    top = up_to(2 + 2 * blocks, 16)
    lanes = 2 * HALF
    body = up_to(half, 16)
    woven = (count // GROUP * 16 + SPARE, BLOCK)
    out_shapes = [jax.ShapeDtypeStruct((top + body, lanes), jnp.int16)] * len(flips)
    out_shapes += [jax.ShapeDtypeStruct((body, 2 * REGION), BF16)] * 2
    rounded = vector.reshape(blocks, BLOCK)
    work = [
        pltpu.VMEM((top, lanes), F32),
        pltpu.VMEM((reach_x * reach_y + SPARE, REGION), F32),
    ] + [pltpu.VMEM((pair_count(reach_x, reach_y), REGION), F32)] * CHAINS
    if placed is None:
        stencil, flag, sample, dipole = raw
        operands = [vector, rounded, *table, stencil, flag.reshape(1, -1), sample, dipole]
        operands = [pltpu.with_memory_space_constraint(value, pltpu.HBM) for value in operands]
        in_specs = [pl.BlockSpec(memory_space=pltpu.HBM)] * 8
        out_shapes += [jax.ShapeDtypeStruct(woven, F32)]
        out_shapes += [jax.ShapeDtypeStruct((2, count), jnp.int32)]
        out_shapes += [jax.ShapeDtypeStruct(rounded.shape, F32)]
        out_shapes += [jax.ShapeDtypeStruct(values.shape, BF16) for values in table]
        tiled = pltpu.VMEM((blocks, 64 + SPARE, BLOCK), F32)
        work = [
            pltpu.VMEM(stencil.shape, jnp.int32),
            pltpu.VMEM((1, count), jnp.int32),
            tiled,
            tiled,
            pltpu.SMEM((count,), F32),
            pltpu.SMEM((2, count), jnp.int32),
            pltpu.SemaphoreType.DMA((7 + 2 * blocks,)),
        ] + work
    else:
        operands = [vector, placed[0], rounded, *table, placed[1]]
        in_specs = [anywhere()] * 2 + [whole_vmem()] * 4
        work = [
            pltpu.SMEM((count,), F32),
            pltpu.SMEM((2, count), jnp.int32),
            pltpu.SemaphoreType.DMA((2,)),
        ] + work
    return pl.pallas_call(
        functools.partial(
            start_kernel if placed is None else spread_kernel, reach_x, reach_y, flips
        ),
        in_specs=in_specs,
        out_specs=[whole_vmem()] * len(out_shapes),
        out_shape=out_shapes,
        scratch_shapes=work,
        compiler_params=pltpu.CompilerParams(
            vmem_limit_bytes=START_LIMIT if placed is None else VMEM_LIMIT
        ),
        cost_estimate=cost(2 * half * 256 * 512, 4 * 16 * count * REGION),
        name="start" if placed is None else "spread",
    )(*operands)


def spread_rest_kernel(flips, rounded_ref, wide_high, wide_low, high_ref, low_ref, *refs):
    outs, head = refs[:-1], refs[-1]
    both = (wide_high[...], wide_low[...])
    send_pieces(outs, flips, head, rounded_ref[...], both, high_ref, low_ref)


def spread_rest(rounded, both, table, flips):
    blocks = rounded.shape[0]
    top = up_to(2 + 2 * blocks, 16)
    shape = (top + both[0].shape[0], 2 * HALF)
    return pl.pallas_call(
        functools.partial(spread_rest_kernel, flips),
        in_specs=[whole_vmem()] * 5,
        out_specs=[whole_vmem()] * len(flips),
        out_shape=[jax.ShapeDtypeStruct(shape, jnp.int16)] * len(flips),
        scratch_shapes=[pltpu.VMEM((top, 2 * HALF), F32)],
        compiler_params=params(),
        cost_estimate=cost(2 * shape[0] * 256 * 256 * 3, 4 * shape[0] * 512),
        name="spread_rest",
    )(rounded, *both, *table)


def lines_kernel(place_ref, coeff_ref, *refs):
    out_ref = refs[-1]
    lanes = lax.broadcasted_iota(jnp.int32, (8, REGION), 1)

    def body(group, carry):
        at = pl.multiple_of(group * 16, 16)
        coeff = [coeff_ref[pl.ds(at + 8 * q, 8), :] for q in range(2)]
        for local in range(GROUP):
            panel = group * GROUP + local
            depth = place_ref[1, panel]
            shift = (depth - 4 * local) & (REGION - 1)
            inside = in_window(lanes, depth)
            for q in range(2):
                first = pl.multiple_of(panel * 16 + 8 * q, 8)
                out_ref[pl.ds(first, 8), :] = jnp.where(inside, pltpu.roll(coeff[q], shift, 1), 0.0)
        return carry

    lax.fori_loop(0, place_ref.shape[1] // GROUP, body, 0)


def sample_lines_kernel(tiles, place_ref, *refs):
    out_ref, coeff, held = refs[-3:]
    for tile, ref in enumerate(refs[:tiles]):
        held[tile, :64, :] = ref[...]
    weave([by_depth(held.at[tile]) for tile in range(tiles)], mixing_matrix(), coeff)
    lines_kernel(place_ref, coeff, out_ref)


def place_sample_lines(places, sample):
    count = places.shape[1]
    blocks = count // BLOCK
    tile = lambda t: pl.BlockSpec((64, BLOCK), lambda i: (0, t))
    shape = (count * 16, REGION)
    return pl.pallas_call(
        functools.partial(sample_lines_kernel, blocks),
        grid=(1,),
        in_specs=[in_smem()] + [tile(t) for t in range(blocks)],
        out_specs=pl.BlockSpec(shape, lambda i: (0, 0)),
        out_shape=jax.ShapeDtypeStruct(shape, F32),
        scratch_shapes=[
            pltpu.VMEM((count // GROUP * 16 + SPARE, BLOCK), F32),
            pltpu.VMEM((blocks, 64 + SPARE, BLOCK), F32),
        ],
        compiler_params=params(),
        cost_estimate=cost(16 * count * REGION, 4 * 16 * count * REGION),
        name="place_sample_lines",
    )(places, *[sample] * blocks)


def place_lines(places, coeff, awaited):
    count = places.shape[1]
    shape = (count * 16, REGION)
    return pl.pallas_call(
        lines_kernel,
        in_specs=[in_smem(), whole_vmem()] + [anywhere()] * len(awaited),
        out_specs=whole_vmem(),
        out_shape=jax.ShapeDtypeStruct(shape, F32),
        compiler_params=params(),
        cost_estimate=cost(16 * count * REGION, 4 * 16 * count * REGION),
        name="place_lines",
    )(places, coeff, *awaited)


def put_edges(opened, reach_x, reach_y, edges, first):
    half = reach_x // 2
    low = low_lanes(reach_y)
    layer = lambda i: opened[i * reach_y : (i + 1) * reach_y, :]
    for two in range(2):
        place = slice(first + two * reach_y, first + (two + 1) * reach_y)
        edges[0, place, :] = jnp.where(low, layer(2 * two), swap(layer(2 * two + 1)))
        last = half - 4 + 2 * two
        edges[1, place, :] = jnp.where(low, swap(layer(last)), layer(last + 1))


def stack_layers(layers, at, reach_y, stacked):
    tall = stacked.shape[0] // len(layers)
    place = at * up_to(reach_y, 8)
    for i, layer in enumerate(layers):
        stacked[pl.ds(pl.multiple_of(i * tall + place, 8), reach_y), :] = layer


def stack_pieces(parts, reach_x, reach_y, top, opened, stacked, edges, places):
    chip = lax.axis_index("narrow")
    for flip, (part, place) in enumerate(zip(parts, places)):
        first = from_short(part[:top, :])
        opened[...] = from_short(part[top:, :]) * unit(first[0:1], first[1:2])
        layers = [opened[i * reach_y : (i + 1) * reach_y, :] for i in range(reach_x // 2)]
        stack_layers(layers, chip ^ flip, reach_y, stacked)
        put_edges(opened, reach_x, reach_y, edges, place * 2 * reach_y)


def transform_pieces(table, stacked, before, spectrum):
    half = spectrum.shape[0]
    tall = stacked.shape[0] // half

    def tripled(values):
        high, low = split(values)
        return jnp.concatenate([high, low, high], axis=0)

    for i in range(0, half, 2):
        places = range(i, min(i + 2, half))
        held = jnp.concatenate([stacked[j * tall : (j + 1) * tall, :] for j in places], axis=1)
        result = dot(table, tripled(held))
        for j in places:
            made = result[:, (j - i) * 2 * HALF : (j - i + 1) * 2 * HALF]
            spectrum[j] = made if before is None else before[j] + made


def forward_early_kernel(reach_x, reach_y, chips, *refs):
    parts = refs[:chips]
    table_ref, spectrum, edges, opened, stacked = refs[chips:]
    top = parts[0].shape[0] - opened.shape[0]
    stacked[...] = jnp.zeros_like(stacked)
    stack_pieces(parts, reach_x, reach_y, top, opened, stacked, edges, range(chips))
    transform_pieces(table_ref[lax.axis_index("pair")], stacked, None, spectrum)


def stacking_scratch(chips, reach_x, reach_y):
    half = reach_x // 2
    return [
        pltpu.VMEM((up_to(half * reach_y, 16), 2 * HALF), F32),
        pltpu.VMEM((half * chips * up_to(reach_y, 8), 2 * HALF), F32),
    ]


def forward_early(parts, table, reach_x, reach_y):
    half = reach_x // 2
    chips = len(parts)
    return pl.pallas_call(
        functools.partial(forward_early_kernel, reach_x, reach_y, chips),
        in_specs=[whole_vmem()] * (chips + 1),
        out_specs=[whole_vmem()] * 2,
        out_shape=[
            jax.ShapeDtypeStruct((half, GRID, 2 * HALF), F32),
            jax.ShapeDtypeStruct((2, chips * 2 * reach_y + SPARE, 2 * HALF), F32),
        ],
        scratch_shapes=stacking_scratch(chips, reach_x, reach_y),
        compiler_params=params(),
        cost_estimate=cost(EARLY_FLOPS, 4 * half * GRID * 2 * HALF * 2),
        name="forward_early",
    )(*parts, table)


def forward_kernel(reach_x, reach_y, blocks, pieces, awaited, *refs):
    parts = refs[:pieces]
    early_ref, early_edges, table_ref, modes_ref = refs[pieces : pieces + 4]
    refs = refs[pieces + 4 + awaited :]
    spectrum, even_out, layers_out, odd_out, own_out, peers_out, inner_out, *refs = refs
    opened, stacked, edges, slabs, head = refs
    half = reach_x // 2
    pair = lax.axis_size("pair")
    top = parts[0].shape[0] - opened.shape[0]
    stacked[...] = jnp.zeros_like(stacked)
    head[...] = jnp.zeros_like(head)
    for piece in range(pieces):
        first = from_short(parts[piece][:top, :])
        mantissa, exponent = first[2 : 2 + blocks], first[2 + blocks : 2 + 2 * blocks]
        peers_out[piece * blocks : (piece + 1) * blocks, :] = decode_rounded(mantissa, exponent)
        at = 6 + 2 * piece * blocks
        head[at : at + blocks, :] = mantissa
        head[at + blocks : at + 2 * blocks, :] = exponent
    rows = 2 * reach_y
    for chip in range(pieces // pair):
        place = chip * pair * rows
        edges[:, place : place + rows, :] = early_edges[:, chip * rows : (chip + 1) * rows, :]
    before = early_ref
    for core in range(1, pair):
        places = range(core, pieces, pair)
        stack_pieces(parts[core::pair], reach_x, reach_y, top, opened, stacked, edges, places)
        transform_pieces(table_ref[lax.axis_index("pair") ^ core], stacked, before, spectrum)
        before = spectrum

    chunk = 256

    def body(index, largest):
        rows = pl.ds(pl.multiple_of(index * chunk, chunk), chunk)
        low = low_lanes(chunk)
        decay = modes_ref[0, rows, :]
        log_decay = modes_ref[1, rows, :]
        across_half = jnp.exp(half * log_decay)
        across_cut = jnp.exp((half - 4) * log_decay)
        layers = [spectrum[i, rows, :] for i in range(half)]
        run = layers[0]
        cut_right = run
        for i in range(1, half):
            run = decay * run + layers[i]
            if i == half - 5:
                cut_right = run
        right = run
        run = layers[half - 1]
        cut_left = run
        for i in range(half - 2, -1, -1):
            run = decay * run + layers[i]
            if i == 4:
                cut_left = run
        left = run
        inner_out[rows, :] = jnp.where(low, right, left)
        swapped_right, swapped_left = swap(right), swap(left)
        own = jnp.where(low, left + across_half * swapped_left, right + across_half * swapped_right)
        own_out[rows, :] = own
        made = [
            jnp.where(low, own, cut_right + across_cut * swapped_right),
            jnp.where(low, cut_left + across_cut * swapped_left, own),
        ]
        for slab, values in enumerate(made):
            slabs[slab, rows, :] = values
        return tuple(
            jnp.maximum(old, jnp.max(jnp.abs(values).reshape(chunk // 8, 8, 2 * HALF), axis=0))
            for old, values in zip(largest, made)
        )

    zero = jnp.zeros((8, 2 * HALF), F32)
    largest = lax.fori_loop(0, GRID // chunk, body, (zero,) * 2)
    top = head.shape[0]
    low = low_lanes(GRID // 2)
    upper, lower = own_out[: GRID // 2, :], own_out[GRID // 2 :, :]
    packed = [jnp.where(low, swap(upper), lower), jnp.where(low, upper, swap(lower))]

    def send(out, first, parts):
        place = first
        for index, (values, most) in enumerate(parts):
            exponent, fraction = fit_scale(jnp.max(most, axis=0, keepdims=True))
            head[2 * index : 2 * index + 1, :] = exponent
            head[2 * index + 1 : 2 * index + 2, :] = fraction
            out[place : place + values.shape[0], :] = quantize(values, exponent, fraction)
            place += values.shape[0]
        out[:first, :] = to_short(head[:first, :])

    with_most = lambda values: (values, jnp.abs(values))
    border = pieces * 2 * reach_y
    on_left = lax.axis_index("wide") & 1
    for side, (even, odd) in enumerate(((0, 1), (1, 0))):

        @pl.when(on_left == side)
        def _():
            send(even_out, 16, [(slabs[even], largest[even]), with_most(packed[even])])
            send(layers_out, top, [with_most(edges[1 - even, :border, :])])
            send(odd_out, top, [(slabs[odd], largest[odd]), with_most(edges[1 - odd, :border, :])])


def forward(parts, early, early_edges, table, modes, reach_x, reach_y, blocks, awaited):
    pieces = len(parts)
    half = reach_x // 2
    lanes = 2 * HALF
    head = up_to(6 + 2 * pieces * blocks, 16)
    border = pieces * 2 * reach_y
    short = lambda rows: jax.ShapeDtypeStruct((rows, lanes), jnp.int16)
    return pl.pallas_call(
        functools.partial(
            forward_kernel, reach_x, reach_y, blocks, pieces, len(awaited)
        ),
        in_specs=[whole_vmem()] * (pieces + 4) + [anywhere()] * len(awaited),
        out_specs=[whole_vmem()] * 7,
        out_shape=[
            jax.ShapeDtypeStruct((half, GRID, lanes), F32),
            short(16 + GRID + GRID // 2),
            short(head + border),
            short(head + GRID + border),
            jax.ShapeDtypeStruct((GRID, lanes), F32),
            jax.ShapeDtypeStruct((pieces * blocks, BLOCK), F32),
            jax.ShapeDtypeStruct((GRID, lanes), F32),
        ],
        scratch_shapes=stacking_scratch(pieces // table.shape[0], reach_x, reach_y)
        + [
            pltpu.VMEM((2, border + SPARE, lanes), F32),
            pltpu.VMEM((2, GRID, lanes), F32),
            pltpu.VMEM((head, lanes), F32),
        ],
        compiler_params=params(),
        cost_estimate=cost(2 * half * 256 * 256 * 128, 4 * half * GRID * lanes * 2),
        name="forward",
    )(*parts, early, early_edges, table, modes, *awaited)


def opened_part(ref, index, first, rows):
    head = from_short(ref[:16, :])
    scale = unit(head[2 * index : 2 * index + 1], head[2 * index + 1 : 2 * index + 2])
    return from_short(ref[first : first + rows, :]) * scale


def pair_kernel(reach_x, flips, own_ref, even_ref, modes_ref, *refs):
    outs, head = refs[:-1], refs[-1]
    span = reach_x - 4
    here = lax.axis_index("wide")
    low = low_lanes(GRID)
    log_decay = modes_ref[1]
    own = own_ref[...]
    top = even_ref.shape[0] - GRID - GRID // 2
    cut = opened_part(even_ref, 0, top, GRID)
    packed = opened_part(even_ref, 1, top + GRID, GRID // 2)
    from_left = jnp.where(low, cut, jnp.concatenate([swap(packed), packed], axis=0))
    from_right = jnp.where(low, jnp.concatenate([packed, swap(packed)], axis=0), cut)
    partner = jnp.where((here & 1) == 1, from_left, from_right)

    def weight(distances):
        powers = []
        for distance in distances:
            ahead = span * distance - reach_x
            powers.append(jnp.where(distance >= 2, ahead, ahead + GRID).astype(F32))
        return jnp.exp(jnp.where(low, *powers) * log_decay)

    head[...] = jnp.zeros_like(head)
    for flip, out in zip(flips, outs):
        behind = (here ^ flip) - here
        message = own * weight((-behind, behind))
        behind = (here ^ flip) - (here ^ 1)
        beside = jnp.where(jnp.abs(behind) == 1, 0.0, 1.0)
        send_piece(out, head, message + partner * (weight((-behind, behind)) * beside))


def pair_messages(own, from_even, modes, reach_x, flips):
    return pl.pallas_call(
        functools.partial(pair_kernel, reach_x, flips),
        in_specs=[whole_vmem()] * 3,
        out_specs=[whole_vmem()] * len(flips),
        out_shape=[jax.ShapeDtypeStruct((16 + GRID, 2 * HALF), jnp.int16)] * len(flips),
        scratch_shapes=[pltpu.VMEM((16, 2 * HALF), F32)],
        compiler_params=params(),
        cost_estimate=cost(16 * GRID * 2 * HALF, 4 * GRID * 2 * HALF * (6 + len(flips))),
        name="pair_messages",
    )(own, from_even, modes)


def borders_kernel(reach_y, pieces, layers_ref, odd_ref, table_ref, out_ref, stacked, partial):
    on_left = (lax.axis_index("wide") & 1) == 1
    pair = lax.axis_size("pair")
    rows = pieces * 2 * reach_y
    even = opened_part(layers_ref, 0, layers_ref.shape[0] - rows, rows)
    odd = opened_part(odd_ref, 1, odd_ref.shape[0] - rows, rows)
    left, right = jnp.where(on_left, even, odd), jnp.where(on_left, odd, even)
    low = low_lanes(rows)
    both = [jnp.where(low, left, swap(right)), jnp.where(low, swap(left), right)]
    core = lax.axis_index("pair")
    chip = lax.axis_index("narrow")
    stacked[...] = jnp.zeros_like(stacked)
    before = None
    for other in range(pair):
        for flip in range(pieces // pair):
            first = (flip * pair + other) * 2 * reach_y
            layers = [
                values[first + two * reach_y : first + (two + 1) * reach_y]
                for two in range(2)
                for values in both
            ]
            stack_layers(layers, chip ^ flip, reach_y, stacked)
        target = out_ref if other == pair - 1 else partial
        transform_pieces(table_ref[core ^ other], stacked, before, target)
        before = target


def borders(layers, from_odd, table, reach_y, pieces):
    chips = pieces // table.shape[0]
    shape = (4, GRID, 2 * HALF)
    return pl.pallas_call(
        functools.partial(borders_kernel, reach_y, pieces),
        in_specs=[whole_vmem()] * 3,
        out_specs=whole_vmem(),
        out_shape=jax.ShapeDtypeStruct(shape, F32),
        scratch_shapes=[
            pltpu.VMEM((4 * chips * up_to(reach_y, 8), 2 * HALF), F32),
            pltpu.VMEM(shape, F32),
        ],
        compiler_params=params(),
        cost_estimate=cost(2 * 4 * 256 * 256 * 128, 4 * 6 * GRID * 2 * HALF),
        name="borders",
    )(layers, from_odd, table)


def send_fields(outs, flips, reach_y, field_high, field_low, high_ref, low_ref, ready, head):
    half = field_high.shape[0]
    mine = y_position()
    pitch = up_to(reach_y, 16)
    pick = lambda ref: jnp.concatenate([ref[mine ^ flip] for flip in flips], axis=0)
    table = (pick(high_ref), pick(low_ref))
    for i in range(0, half, 2):
        many = min(2, half - i)
        join = lambda ref: jnp.concatenate([ref[i + j] for j in range(many)], axis=1)
        result = dot_three(table, (join(field_high), join(field_low)))
        for j in range(many):
            for piece in range(len(flips)):
                ready[piece, (i + j) * reach_y : (i + j + 1) * reach_y, :] = result[
                    piece * pitch : piece * pitch + reach_y, j * 2 * HALF : (j + 1) * 2 * HALF
                ]
    head[...] = jnp.zeros_like(head)
    for piece, out in enumerate(outs):
        if ready.shape[1] > half * reach_y:
            ready[piece, half * reach_y :, :] = jnp.zeros_like(ready[piece, half * reach_y :, :])
        send_piece(out, head, ready[piece])


def inverse_kernel(reach_x, reach_y, flips, fars, *refs):
    spectrum, border_ref, from_even, from_odd, own_ref, inner_ref, *far_refs = refs[: 6 + fars]
    refs = refs[6 + fars :]
    high_ref, low_ref, modes_ref = refs[:3]
    outs = refs[3 : 3 + len(flips)]
    field_high, field_low, ready, head = refs[3 + len(flips) :]
    half = reach_x // 2
    span = reach_x - 4
    chunk = 256
    border_rows = lax.axis_size("narrow") * lax.axis_size("pair") * 2 * reach_y
    tops = from_even.shape[0] - GRID - GRID // 2, from_odd.shape[0] - GRID - border_rows
    on_left = (lax.axis_index("wide") & 1) == 1
    moment_units = []
    for ref in (from_even, from_odd):
        first = from_short(ref[:16, :])
        moment_units.append(unit(first[0:1], first[1:2]))

    far_units = []
    for ref in far_refs:
        first = from_short(ref[:16, :])
        far_units.append(unit(first[0:1], first[1:2]))

    def body(index, carry):
        first = pl.multiple_of(index * chunk, chunk)
        rows = pl.ds(first, chunk)
        low = low_lanes(chunk)
        decay = modes_ref[0, rows, :]
        log_decay = modes_ref[1, rows, :]
        ring = modes_ref[2, rows, :]
        gain = modes_ref[3, rows, :]
        across_half = jnp.exp(half * log_decay)
        across_cut = jnp.exp((half - 4) * log_decay)
        around = jnp.exp((GRID - 4) * log_decay)
        beside = jnp.exp((GRID - reach_x - span) * log_decay)
        layers = [spectrum[i, rows, :] for i in range(half)]

        even, odd = (
            from_short(ref[pl.ds(pl.multiple_of(top + index * chunk, 16), chunk), :]) * scale
            for ref, top, scale in zip((from_even, from_odd), tops, moment_units)
        )
        left_moments, right_moments = jnp.where(on_left, even, odd), jnp.where(on_left, odd, even)
        border = [border_ref[i, rows, :] for i in range(4)]
        zero = jnp.zeros_like(decay)
        head_sum = border[0]
        for i in range(1, 4):
            head_sum = decay * head_sum + border[i]
        tail_sum = border[3]
        for i in range(2, -1, -1):
            tail_sum = decay * tail_sum + border[i]
        for i in range(4):
            layers[i] = layers[i] + jnp.where(low, border[i], zero)
        for i in range(4):
            place = half - 4 + i
            layers[place] = layers[place] + jnp.where(low, zero, border[i])
        total = own_ref[rows, :] * jnp.exp((GRID - reach_x) * log_decay)
        at = pl.ds(pl.multiple_of(16 + index * chunk, 16), chunk)
        for ref, scale in zip(far_refs, far_units):
            total = total + from_short(ref[at, :]) * scale
        one = jnp.ones_like(decay)
        total = total + left_moments * jnp.where(low, beside, one)
        total = total + right_moments * jnp.where(low, one, beside)
        shared = jnp.where(low, head_sum, tail_sum)
        entering = (swap(total) + around * shared) * ring
        leaving = swap(across_half * entering + across_cut * shared + inner_ref[rows, :])
        run = jnp.where(low, entering, leaving)
        forward_runs = []
        for i in range(half):
            run = decay * run + layers[i]
            forward_runs.append(run)
        run = jnp.where(low, leaving, entering)
        for i in range(half - 1, -1, -1):
            ahead = decay * run
            high, rest = split(gain * (forward_runs[i] + ahead))
            field_high[i, rows, :] = high
            field_low[i, rows, :] = rest
            run = ahead + layers[i]
        return carry

    lax.fori_loop(0, GRID // chunk, body, 0)
    send_fields(outs, flips, reach_y, field_high, field_low, high_ref, low_ref, ready, head)


def inverse(
    spectrum, border, from_even, from_odd, own, inner, fars, table, modes, reach_x, reach_y, flips
):
    half = reach_x // 2
    lanes = 2 * HALF
    body = up_to(half * reach_y, 16)
    shapes = [jax.ShapeDtypeStruct((16 + body, lanes), jnp.int16)] * len(flips)
    shapes += [jax.ShapeDtypeStruct((half, GRID, lanes), BF16)] * 2
    return pl.pallas_call(
        functools.partial(inverse_kernel, reach_x, reach_y, flips, len(fars)),
        in_specs=[whole_vmem()] * (9 + len(fars)),
        out_specs=[whole_vmem()] * len(shapes),
        out_shape=shapes,
        scratch_shapes=[
            pltpu.VMEM((len(flips), body, lanes), F32),
            pltpu.VMEM((16, lanes), F32),
        ],
        compiler_params=params(),
        cost_estimate=cost(2 * half * 256 * 256 * 128, 4 * half * GRID * lanes * 2),
        name="inverse",
    )(spectrum, border, from_even, from_odd, own, inner, *fars, *table, modes)


def inverse_rest_kernel(reach_y, flips, field_high, field_low, high_ref, low_ref, *refs):
    outs, (ready, head) = refs[: len(flips)], refs[len(flips) :]
    send_fields(outs, flips, reach_y, field_high, field_low, high_ref, low_ref, ready, head)


def inverse_rest(field, table, reach_y, flips):
    half = field[0].shape[0]
    lanes = 2 * HALF
    body = up_to(half * reach_y, 16)
    return pl.pallas_call(
        functools.partial(inverse_rest_kernel, reach_y, flips),
        in_specs=[whole_vmem()] * 4,
        out_specs=[whole_vmem()] * len(flips),
        out_shape=[jax.ShapeDtypeStruct((16 + body, lanes), jnp.int16)] * len(flips),
        scratch_shapes=[
            pltpu.VMEM((len(flips), body, lanes), F32),
            pltpu.VMEM((16, lanes), F32),
        ],
        compiler_params=params(),
        cost_estimate=cost(2 * half * 256 * 256 * 128, 4 * half * GRID * lanes * 2),
        name="inverse_rest",
    )(*field, *table)


def sum_rows(values):
    row = lax.broadcasted_iota(jnp.int32, values[0].shape, 0)
    for step in (4, 2, 1):
        low = (row & step) == 0
        paired = []
        for one, other in zip(values[: len(values) // 2], values[len(values) // 2 :]):
            kept = jnp.where(low, one, other)
            moved = jnp.where(low, other, one)
            if step == 4:
                moved = pltpu.roll(moved, 4, 0)
            else:
                moved = jnp.where(low, pltpu.roll(moved, 8 - step, 0), pltpu.roll(moved, step, 0))
            paired.append(kept + moved)
        values = paired
    return values[0]


def z_lines(parts, flips, high_ref, low_ref):
    mine = y_position()
    opened = []
    for part in parts:
        first = from_short(part[:16, :])
        opened.append(from_short(part[16:, :]) * unit(first[0:1], first[1:2]))
    values = split(jnp.concatenate(opened, axis=1))
    pick = lambda ref: jnp.concatenate([ref[mine ^ flip] for flip in flips], axis=0)
    return dot_three(values, (pick(high_ref), pick(low_ref)))


def sample_early_kernel(flips, *refs):
    *parts, high_ref, low_ref, out_ref = refs
    out_ref[...] = z_lines(parts, flips, high_ref, low_ref)


def sample_early(parts, flips, table):
    rows = parts[0].shape[0] - 16
    return pl.pallas_call(
        functools.partial(sample_early_kernel, flips),
        in_specs=[whole_vmem()] * (len(parts) + 2),
        out_specs=whole_vmem(),
        out_shape=jax.ShapeDtypeStruct((rows, 2 * REGION), F32),
        compiler_params=params(),
        cost_estimate=cost(EARLY_FLOPS, 4 * rows * 512),
        name="sample_early",
    )(*parts, *table)


def sample_kernel(last, reach_x, reach_y, flips, place_in, *refs):
    parts = refs[: len(flips)]
    early_ref, high_ref, low_ref, line_ref, own_ref, vector_ref, near_ref, out_ref = refs[
        len(flips) : len(flips) + 8
    ]
    flat, field, sums, place_ref, sem = refs[len(flips) + 8 :]
    copy = pltpu.make_async_copy(place_in, place_ref, sem)
    copy.start()
    half_rows = reach_x * reach_y // 2
    both = early_ref[...] + z_lines(parts, flips, high_ref, low_ref)
    flat[:half_rows, :] = both[:half_rows, :REGION]
    flat[half_rows : 2 * half_rows, :] = both[:half_rows, REGION:]
    for x in range(reach_x):
        layer = flat[x * reach_y : (x + 1) * reach_y, :]
        for row in pair_rows(x, reach_x, reach_y):
            field[pl.ds(row, reach_y, stride=2), :] = layer
    count = place_ref.shape[1]

    def body(group, carry):
        for eight in range(0, GROUP, 8):
            totals = []
            for local in range(eight, eight + 8):
                panel = group * GROUP + local
                row = place_ref[0, panel]
                first = pl.multiple_of(panel * 16, 16)
                totals.append(
                    field[pl.ds(row, 8), :] * line_ref[pl.ds(first, 8), :]
                    + field[pl.ds(row + 2 * reach_y, 8), :] * line_ref[pl.ds(first + 8, 8), :]
                )
            sums[pl.ds(pl.multiple_of(group * GROUP + eight, 8), 8), :] = sum_rows(totals)
        return carry

    copy.wait()
    lax.fori_loop(0, count // GROUP, body, 0)
    first, rest = split(sums[...])
    second, third = split(sums[...] - first.astype(F32))
    across = lambda values: lax.dot_general(
        jnp.ones((16, REGION), BF16),
        values,
        (((1,), (1,)), ((), ())),
        preferred_element_type=F32,
    )
    sampled = across(first) + (across(second) + across(third))
    for block in range(count // BLOCK):
        lane = slice(block * BLOCK, (block + 1) * BLOCK)
        row = slice(block, block + 1)
        vector = vector_ref[row, :]
        image = jnp.where(own_ref[row, :] == 1, 0.0, 0.5 * vector) + sampled[:1, lane]
        image = image + near_ref[row, :]
        if last:
            out_ref[0:1, lane] = vector
            out_ref[1:2, lane] = image
        else:
            out_ref[row, :] = image


def sample(last, places, parts, flips, early, table, lines, flag, vector, near, reach_x, reach_y):
    count = places.shape[1]
    blocks = count // BLOCK
    shape = (2, count) if last else (blocks, BLOCK)
    return pl.pallas_call(
        functools.partial(sample_kernel, last, reach_x, reach_y, flips),
        in_specs=[anywhere()] + [whole_vmem()] * (len(parts) + 7),
        out_specs=whole_vmem(),
        out_shape=jax.ShapeDtypeStruct(shape, F32),
        scratch_shapes=[
            pltpu.VMEM((reach_x * reach_y + SPARE, REGION), F32),
            pltpu.VMEM((pair_count(reach_x, reach_y), REGION), F32),
            pltpu.VMEM((count, REGION), F32),
            pltpu.SMEM((2, count), jnp.int32),
            pltpu.SemaphoreType.DMA,
        ],
        compiler_params=params(),
        cost_estimate=cost(reach_x * reach_y * 256 * 512, 4 * 16 * count * REGION),
        name="sample",
    )(
        places,
        *parts,
        early,
        *table,
        lines,
        flag.reshape(blocks, BLOCK),
        vector.reshape(blocks, BLOCK),
        near,
    )


def near_kernel(slots, blocks, place_ref, target_ref, *refs):
    even_ref, odd_ref, peers_ref, tile_ref = refs[:4]
    out_ref, held = refs[-2:]
    count = peers_ref.shape[0]
    held[count : 2 * count, :] = peers_ref[...]
    on_left = lax.axis_index("wide") & 1
    for side, ref in ((1 - on_left, even_ref), (on_left, odd_ref)):
        top = from_short(ref[...])
        for piece in range(count // blocks):
            at = 6 + 2 * piece * blocks
            held[pl.ds(side * (2 * count) + piece * blocks, blocks), :] = decode_rounded(
                top[at : at + blocks], top[at + blocks : at + 2 * blocks]
            )
    out_ref[...] = jnp.zeros_like(out_ref)
    for slot in range(slots):
        picked = held[pl.ds(place_ref[slot], 1), :]
        picked = jnp.broadcast_to(picked, (16, BLOCK)).astype(BF16)
        product = lax.dot_general(
            picked,
            tile_ref[slot],
            (((1,), (1,)), ((), ())),
            preferred_element_type=F32,
        )
        target = pl.ds(target_ref[slot], 1)
        out_ref[target, :] = out_ref[target, :] + product[:1]


def near_field(places, targets, from_even, from_odd, peers, tiles, blocks, out_rows, awaited):
    slots = tiles.shape[0]
    head = up_to(6 + 2 * peers.shape[0], 16)
    constant = lambda shape: pl.BlockSpec(shape, lambda i: (0,) * len(shape))
    return pl.pallas_call(
        functools.partial(near_kernel, slots, blocks),
        grid=(1,),
        in_specs=[
            in_smem(),
            in_smem(),
            constant((head, BLOCK)),
            constant((head, BLOCK)),
            constant(peers.shape),
            constant(tiles.shape),
        ]
        + [anywhere()] * len(awaited),
        out_specs=constant((out_rows, BLOCK)),
        out_shape=jax.ShapeDtypeStruct((out_rows, BLOCK), F32),
        scratch_shapes=[pltpu.VMEM((3 * peers.shape[0] + SPARE, BLOCK), F32)],
        compiler_params=params(),
        cost_estimate=cost(2 * slots * 16 * BLOCK * BLOCK, 2 * slots * BLOCK * BLOCK),
        name="near_field",
    )(places, targets, from_even, from_odd, peers, tiles, *awaited)


def shards(
    density,
    surface_flag,
    stencil_base,
    sample_weights,
    dipole_weights,
    near_target,
    near_source,
    near_tiles,
):
    x_count = lax.axis_size("wide")
    y_count = lax.axis_size(Y_AXES)
    y_index = lax.axis_index(Y_AXES)
    pair = lax.axis_size("pair")
    span_x = REGION // x_count
    span_y = REGION // y_count
    reach_x = span_x + 4
    reach_y = span_y + 4
    count = density.shape[0]
    blocks = count // BLOCK

    z_forward, z_inverse, y_forward, y_inverse, modes = tables(y_count, pair, span_y)
    modes = lax.dynamic_index_in_dim(jnp.asarray(modes), y_index, 0, keepdims=False)

    neighbour = near_source // blocks
    flip = (y_index + neighbour % 3 - 1) ^ y_index
    sources = ((neighbour // 3) * y_count + flip) * blocks + near_source % blocks
    out_rows = up_to(blocks + 1, 8)
    live = near_target >= 0
    sources = jnp.where(live, sources, 0)
    targets = jnp.where(live, near_target, out_rows - 1)

    swaps = lambda pairs: [(i, j) for i, j in pairs] + [(j, i) for i, j in pairs]
    even_swap = swaps([(i, i + 1) for i in range(0, x_count - 1, 2)])
    odd_swap = swaps([(i, i + 1) for i in range(1, x_count - 1, 2)])
    far_flips = list(range(2, x_count, 2))

    first, inside, local = list(range(pair, y_count)), list(range(1, pair)), [0]
    same_core = list(range(0, y_count, pair))
    other_core = [flip for flip in range(y_count) if flip not in same_core]

    def turned(sent, then):
        arrived = [None] * y_count
        for flip, part in zip(first + inside + local, list(sent) + list(then)):
            swap_pairs = [(i, i ^ flip) for i in range(y_count)]
            arrived[flip] = part if flip == 0 else lax.ppermute(part, Y_AXES, swap_pairs)
        return arrived

    def chosen(parts, flips):
        return [parts[flip] for flip in flips]

    def convolve_and_sample(last, vector, sent, both, table, places, sample_lines, awaited):
        then = [part for flips in (inside, local) for part in spread_rest(vector, both, table, flips)]
        arrived = turned(sent, then)
        early, edges = forward_early(chosen(arrived, same_core), y_forward, reach_x, reach_y)
        spectrum, even_message, layers, odd_message, own, peers, inner = forward(
            arrived, early, edges, y_forward, modes, reach_x, reach_y, blocks, awaited
        )
        from_even = lax.ppermute(even_message, "wide", even_swap)
        from_odd = lax.ppermute(odd_message, "wide", odd_swap)
        even_layers = lax.ppermute(layers, "wide", even_swap)
        fars = [
            lax.ppermute(message, "wide", [(i, i ^ flip) for i in range(x_count)])
            for flip, message in zip(
                far_flips, pair_messages(own, from_even, modes, reach_x, far_flips)
            )
        ]
        *sent, high, low = inverse(
            spectrum,
            borders(even_layers, from_odd, y_forward, reach_y, y_count),
            from_even,
            from_odd,
            own,
            inner,
            fars,
            y_inverse,
            modes,
            reach_x,
            reach_y,
            first,
        )
        then = [
            part
            for flips in (inside, local)
            for part in inverse_rest((high, low), y_inverse, reach_y, flips)
        ]
        near_part = near_field(
            sources, targets, even_layers, from_odd, peers, near_tiles, blocks, out_rows, then[:1]
        )
        arrived = turned(sent, then)
        image = sample(
            last,
            places,
            chosen(arrived, other_core),
            other_core,
            sample_early(chosen(arrived, same_core), same_core, z_inverse),
            z_inverse,
            sample_lines,
            surface_flag,
            vector,
            near_part,
            reach_x,
            reach_y,
        )
        return image, near_part

    raw = (stencil_base, surface_flag, sample_weights, dipole_weights)
    *sent, wide_high, wide_low, source_coeff, places, vector, high, low = spread(
        density, z_forward, None, raw, reach_x, reach_y, first
    )
    z_forward = (high, low)
    sample_lines = place_sample_lines(places, sample_weights)
    vector, near_part = convolve_and_sample(
        False,
        vector,
        sent,
        (wide_high, wide_low),
        z_forward,
        places,
        sample_lines,
        [sample_lines],
    )
    source_lines = place_lines(places, source_coeff, [near_part])
    *sent, wide_high, wide_low = spread(
        vector.reshape(-1), z_forward, (places, source_lines), None, reach_x, reach_y, first
    )
    both_images, _ = convolve_and_sample(
        True, vector, sent, (wide_high, wide_low), z_forward, places, sample_lines, []
    )
    return both_images


def solution(mesh):
    panels = P(("groups",) + ALL_AXES)
    columns = P(None, ("groups",) + ALL_AXES)
    in_specs = (
        panels,
        panels,
        columns,
        columns,
        columns,
        panels,
        panels,
        P(("groups",) + ALL_AXES, None, None),
    )
    return jax.shard_map(
        shards, mesh=mesh, in_specs=in_specs, out_specs=columns, check_vma=False
    )
```

```python
import functools
import math

import jax
import jax.numpy as jnp
import numpy as np
from jax import lax
from jax.experimental import pallas as pl
from jax.experimental.pallas import tpu as pltpu
from jax.sharding import PartitionSpec as P

GRID = 256
REGION = 128
BLOCK = 128
HALF = 64
KERNEL_GAIN = 4.0
SCREEN = 1.0 / 1024.0
LN2 = math.log(2.0)
SPARE = 16
Y_AXES = ("narrow", "pair")
ALL_AXES = ("wide", "narrow", "pair")
F32 = jnp.float32
BF16 = jnp.bfloat16
VMEM_LIMIT = 20 * 1024 * 1024
START_LIMIT = VMEM_LIMIT
EARLY_FLOPS = 5 * 10**9
GROUP = 32
CHAINS = 2


def cas(angles):
    return np.cos(angles) + np.sin(angles)


def up_to(count, multiple):
    return -(-count // multiple) * multiple


def low_lanes(rows):
    return lax.broadcasted_iota(jnp.int32, (rows, 2 * HALF), 1) < HALF


def swap(values):
    return pltpu.roll(values, HALF, 1)


def split(values):
    high = values.astype(BF16)
    return high, (values - high.astype(F32)).astype(BF16)


def dot(left, right):
    return jnp.dot(left, right, preferred_element_type=F32)


def dot_three(left, right):
    return dot(left[0], right[0]) + (dot(left[0], right[1]) + dot(left[1], right[0]))


def params():
    return pltpu.CompilerParams(vmem_limit_bytes=VMEM_LIMIT)


def whole_vmem():
    return pl.BlockSpec(memory_space=pltpu.VMEM)


def anywhere():
    return pl.BlockSpec(memory_space=pl.ANY)


def in_smem():
    return pl.BlockSpec(memory_space=pltpu.SMEM)


def cost(flops, moved):
    return pl.CostEstimate(flops=flops, bytes_accessed=moved, transcendentals=0)


def full_scale(exponent, fraction):
    return fraction * jnp.exp(exponent * LN2) * (1.0 / 1024.0)


def fit_scale(largest):
    largest = jnp.maximum(largest, 1e-30)
    exponent = jnp.floor(jnp.log(largest) * (1.0 / LN2))
    fraction = jnp.ceil(largest * jnp.exp(-exponent * LN2) * 1024.0) + 1.0
    return exponent, fraction


def to_short(values):
    return values.astype(jnp.int32).astype(jnp.int16)


def from_short(values):
    return values.astype(jnp.int32).astype(F32)


def quantize(values, exponent, fraction):
    return to_short(jnp.round(values * (32767.0 / full_scale(exponent, fraction))))


def unit(exponent, fraction):
    return full_scale(exponent, fraction) * (1.0 / 32767.0)


def encode_rounded(values):
    rounded = values.astype(BF16).astype(F32)
    size = jnp.maximum(jnp.abs(rounded), 1e-30)
    exponent = jnp.floor(jnp.log(size) * (1.0 / LN2))
    return jnp.round(rounded * jnp.exp((10.0 - exponent) * LN2)), exponent


def decode_rounded(mantissa, exponent):
    return (mantissa * jnp.exp((exponent - 10.0) * LN2)).astype(BF16).astype(F32)


def send_piece(out, head, values):
    exponent, fraction = fit_scale(jnp.max(jnp.abs(values), axis=0, keepdims=True))
    head[0:1, :] = exponent
    head[1:2, :] = fraction
    top = head.shape[0]
    out[:top, :] = to_short(head[...])
    out[top:, :] = quantize(values, exponent, fraction)


def y_position():
    return lax.axis_index("narrow") * lax.axis_size("pair") + lax.axis_index("pair")


def halves(table):
    high = table.astype(jnp.bfloat16)
    return high, (table - high.astype(np.float64)).astype(jnp.bfloat16)


def tables(y_count, pair, span_y):
    depth = GRID // y_count
    reach = span_y + 4
    waves = np.arange(GRID)
    step = 2.0 * np.pi / GRID
    z_table = cas(step * np.outer(np.arange(REGION), waves))
    z_forward = np.zeros((y_count, 2 * REGION, 2 * HALF))
    z_inverse = np.zeros((y_count, 2 * HALF, 2 * REGION))
    symbols = 4.0 * np.sin(np.pi * waves / GRID) ** 2
    shift = np.full((y_count, GRID, 2 * HALF), 1.0)
    y_forward = np.zeros((GRID, y_count, up_to(reach, 8)))
    y_inverse = np.zeros((y_count, up_to(reach, 16), GRID))
    for block in range(y_count):
        mine = z_table[:, block * depth : (block + 1) * depth]
        for half in range(2):
            rows = slice(half * REGION, (half + 1) * REGION)
            lanes = slice(half * HALF, half * HALF + depth)
            z_forward[block, rows, lanes] = mine
            z_inverse[block, lanes, rows] = mine.T / GRID
            shift[block, :, lanes] = (
                SCREEN + symbols[:, None] + symbols[None, block * depth : (block + 1) * depth]
            )
        cells = block * span_y - 2 + np.arange(reach)
        y_table = cas(step * np.outer(waves, cells))
        y_forward[:, block, :reach] = y_table
        y_inverse[block, :reach] = y_table.T / GRID
    y_forward = y_forward.reshape(GRID, y_count // pair, pair, -1).transpose(2, 0, 1, 3)
    y_forward = halves(y_forward.reshape(pair, GRID, -1))
    y_forward = np.concatenate([y_forward[0], y_forward[0], y_forward[1]], axis=2)
    root = np.sqrt(shift * (shift + 4.0))
    decay = 2.0 / (2.0 + shift + root)
    log_decay = np.log(decay)
    ring = 1.0 / (1.0 - np.exp(GRID * log_decay))
    gain = KERNEL_GAIN / root
    modes = np.stack([decay, log_decay, ring, gain], axis=1).astype(np.float32)
    return (
        halves(z_forward),
        halves(z_inverse),
        y_forward,
        halves(y_inverse),
        modes,
    )


def mixing_matrix():
    place = lax.broadcasted_iota(jnp.int32, (4 * BLOCK, 4 * BLOCK), 0)
    lane = lax.broadcasted_iota(jnp.int32, (4 * BLOCK, 4 * BLOCK), 1)
    return jnp.where(lane == 4 * (place % BLOCK) + place // BLOCK, 1.0, 0.0).astype(BF16)


def weave(tiles, mixing, out):
    weights = jnp.concatenate([jnp.concatenate(tile, axis=1) for tile in tiles], axis=0)
    first, rest = split(weights)
    second, third = split(weights - first.astype(F32))
    woven = dot(first, mixing) + (dot(second, mixing) + dot(third, mixing))
    for tile in range(len(tiles)):
        for part in range(BLOCK // GROUP):
            at = (tile * (BLOCK // GROUP) + part) * 16
            lanes = slice(part * BLOCK, (part + 1) * BLOCK)
            for a in range(4):
                row = tile * 16 + 4 * a
                out[pl.ds(at + 8 * (a // 2) + a % 2, 4, stride=2), :] = woven[row : row + 4, lanes]


def by_depth(ref):
    return [ref[pl.ds(depth, 16, stride=4), :] for depth in range(4)]


def pair_rows(x, reach_x, reach_y):
    even = (x // 2) * 2 * reach_y + x % 2
    if x == 0 or x == reach_x - 1:
        return [even]
    return [even, reach_x * reach_y + ((x - 1) // 2) * 2 * reach_y + (x - 1) % 2]


def pair_count(reach_x, reach_y):
    return (2 * reach_x - 2) * reach_y + SPARE


def in_window(lanes, depth):
    return ((lanes - depth) & -4) == 0


def add_panels(reach, woven, vector_ref, place_ref, weight_ref, grids):
    lanes = lax.broadcasted_iota(jnp.int32, (8, REGION), 1)

    def body(group, carry):
        at = pl.multiple_of(group * 16, 16)
        coeff = [weight_ref[pl.ds(at + 8 * q, 8), :] for q in range(2)] if woven else None
        for local in range(GROUP):
            panel = group * GROUP + local
            grid = grids[local % len(grids)]
            row = place_ref[0, panel]
            value = vector_ref[panel]
            if woven:
                depth = place_ref[1, panel]
                shift = (depth - 4 * local) & (REGION - 1)
                value = jnp.where(in_window(lanes, depth), value, 0.0)
                lines = [pltpu.roll(coeff[q], shift, 1) for q in range(2)]
            else:
                first = pl.multiple_of(panel * 16, 16)
                lines = [weight_ref[pl.ds(first + 8 * q, 8), :] for q in range(2)]
            places = [pl.ds(row, 8), pl.ds(row + 2 * reach, 8)]
            held = [grid[place, :] for place in places]
            for q in range(2):
                grid[places[q], :] = held[q] + lines[q] * value
        return carry

    lax.fori_loop(0, vector_ref.shape[0] // GROUP, body, 0)


def send_pieces(outs, flips, head, rounded, both, high_ref, low_ref):
    blocks = rounded.shape[0]
    mantissa, exponent = encode_rounded(rounded)
    head[...] = jnp.zeros_like(head)
    head[2 : 2 + blocks, :] = mantissa
    head[2 + blocks : 2 + 2 * blocks, :] = exponent
    mine = y_position()
    for at in range(0, len(flips), 2):
        pick = lambda ref: jnp.concatenate([ref[mine ^ flip] for flip in flips[at : at + 2]], axis=1)
        result = dot_three(both, (pick(high_ref), pick(low_ref)))
        for i, out in enumerate(outs[at : at + 2]):
            send_piece(out, head, result[:, i * 2 * HALF : (i + 1) * 2 * HALF])


def spread_grid(reach_x, reach_y, rounded, tables, outs, flips, wides, head, total, grids):
    for x in range(reach_x):
        parts = [
            grid[pl.ds(row, reach_y, stride=2), :]
            for row in pair_rows(x, reach_x, reach_y)
            for grid in grids
        ]
        total[x * reach_y : (x + 1) * reach_y, :] = sum(parts[1:], parts[0])
    half = reach_x * reach_y // 2
    both = jnp.concatenate([total[:half, :], total[half : 2 * half, :]], axis=1)
    extra = wides[0].shape[0] - half
    if extra:
        both = jnp.concatenate([both, jnp.zeros((extra, 2 * REGION), F32)], axis=0)
    both = split(both)
    for wide, values in zip(wides, both):
        wide[...] = values
    send_pieces(outs, flips, head, rounded, both, *tables)


def start_kernel(reach_x, reach_y, flips, *refs):
    vector_in, *remote = refs[:8]
    refs = refs[8:]
    outs, refs = refs[: len(flips)], refs[len(flips) :]
    wides, (weight_ref, places_out), refs = refs[:2], refs[2:4], refs[4:]
    rounded, high, low, stencil, flag, samples, dipoles, vector_ref = refs[:8]
    place_ref, sems, head, total = refs[8:12]
    grids = refs[12:]
    tiles = samples.shape[0]
    copies = []
    fetch = lambda source, target: copies.append(
        pltpu.make_async_copy(source, target, sems.at[len(copies)])
    )
    rounded_in, high_in, low_in, stencil_in, flag_in, sample_in, dipole_in = remote
    fetch(stencil_in, stencil)
    fetch(flag_in, flag)
    fetch(vector_in, vector_ref)
    for tile in range(tiles):
        lanes = pl.ds(tile * BLOCK, BLOCK)
        fetch(sample_in.at[:, lanes], samples.at[tile, pl.ds(0, 64)])
        fetch(dipole_in.at[:, lanes], dipoles.at[tile, pl.ds(0, 64)])
    needed_first = len(copies)
    fetch(rounded_in, rounded)
    fetch(high_in, high)
    fetch(low_in, low)
    for copy in copies:
        copy.start()
    for grid in grids:
        grid[...] = jnp.zeros_like(grid)
    mixing = mixing_matrix()
    copies[0].wait()
    span_x, span_y = reach_x - 4, reach_y - 4
    local_x = stencil[0:1, :] - (lax.axis_index("wide") * span_x - 2)
    local_y = stencil[1:2, :] - (y_position() * span_y - 2)
    odd = local_x & 1
    places_out[0:1, :] = odd * (reach_x * reach_y) + (local_x >> 1) * (2 * reach_y) + 2 * local_y
    places_out[1:2, :] = stencil[2:3, :]
    to_scalar = pltpu.make_async_copy(places_out, place_ref, sems.at[len(copies)])
    to_scalar.start()
    for copy in copies[1:needed_first]:
        copy.wait()
    sources = []
    for tile in range(tiles):
        charged = flag[:, tile * BLOCK : (tile + 1) * BLOCK] == 1
        pairs = zip(by_depth(samples.at[tile]), by_depth(dipoles.at[tile]))
        sources.append([jnp.where(charged, -sample, dipole) for sample, dipole in pairs])
    weave(sources, mixing, weight_ref)
    to_scalar.wait()
    add_panels(reach_y, True, vector_ref, place_ref, weight_ref, grids)
    for copy in copies[needed_first:]:
        copy.wait()
    spread_grid(
        reach_x, reach_y, rounded[...], (high, low), outs, flips, wides, head, total, grids
    )


def spread_kernel(reach_x, reach_y, flips, *refs):
    vector_in, place_in, rounded_ref, high_ref, low_ref, line_ref = refs[:6]
    refs = refs[6:]
    outs, wides, (vector_ref, place_ref, sems, head, total), grids = (
        refs[: len(flips)],
        refs[len(flips) : len(flips) + 2],
        refs[len(flips) + 2 : len(flips) + 7],
        refs[len(flips) + 7 :],
    )
    copies = [
        pltpu.make_async_copy(vector_in, vector_ref, sems.at[0]),
        pltpu.make_async_copy(place_in, place_ref, sems.at[1]),
    ]
    for copy in copies:
        copy.start()
    for grid in grids:
        grid[...] = jnp.zeros_like(grid)
    for copy in copies:
        copy.wait()
    add_panels(reach_y, False, vector_ref, place_ref, line_ref, grids)
    spread_grid(
        reach_x,
        reach_y,
        rounded_ref[...],
        (high_ref, low_ref),
        outs,
        flips,
        wides,
        head,
        total,
        grids,
    )


def spread(vector, table, placed, raw, reach_x, reach_y, flips):
    count = vector.shape[0]
    half = reach_x * reach_y // 2
    blocks = count // BLOCK
    top = up_to(2 + 2 * blocks, 16)
    lanes = 2 * HALF
    body = up_to(half, 16)
    woven = (count // GROUP * 16 + SPARE, BLOCK)
    out_shapes = [jax.ShapeDtypeStruct((top + body, lanes), jnp.int16)] * len(flips)
    out_shapes += [jax.ShapeDtypeStruct((body, 2 * REGION), BF16)] * 2
    rounded = vector.reshape(blocks, BLOCK)
    work = [
        pltpu.VMEM((top, lanes), F32),
        pltpu.VMEM((reach_x * reach_y + SPARE, REGION), F32),
    ] + [pltpu.VMEM((pair_count(reach_x, reach_y), REGION), F32)] * CHAINS
    if placed is None:
        stencil, flag, sample, dipole = raw
        operands = [vector, rounded, *table, stencil, flag.reshape(1, -1), sample, dipole]
        operands = [pltpu.with_memory_space_constraint(value, pltpu.HBM) for value in operands]
        in_specs = [pl.BlockSpec(memory_space=pltpu.HBM)] * 8
        out_shapes += [jax.ShapeDtypeStruct(woven, F32)]
        out_shapes += [jax.ShapeDtypeStruct((2, count), jnp.int32)]
        out_shapes += [jax.ShapeDtypeStruct(rounded.shape, F32)]
        out_shapes += [jax.ShapeDtypeStruct(values.shape, BF16) for values in table]
        tiled = pltpu.VMEM((blocks, 64 + SPARE, BLOCK), F32)
        work = [
            pltpu.VMEM(stencil.shape, jnp.int32),
            pltpu.VMEM((1, count), jnp.int32),
            tiled,
            tiled,
            pltpu.SMEM((count,), F32),
            pltpu.SMEM((2, count), jnp.int32),
            pltpu.SemaphoreType.DMA((7 + 2 * blocks,)),
        ] + work
    else:
        operands = [vector, placed[0], rounded, *table, placed[1]]
        in_specs = [anywhere()] * 2 + [whole_vmem()] * 4
        work = [
            pltpu.SMEM((count,), F32),
            pltpu.SMEM((2, count), jnp.int32),
            pltpu.SemaphoreType.DMA((2,)),
        ] + work
    return pl.pallas_call(
        functools.partial(
            start_kernel if placed is None else spread_kernel, reach_x, reach_y, flips
        ),
        in_specs=in_specs,
        out_specs=[whole_vmem()] * len(out_shapes),
        out_shape=out_shapes,
        scratch_shapes=work,
        compiler_params=pltpu.CompilerParams(
            vmem_limit_bytes=START_LIMIT if placed is None else VMEM_LIMIT
        ),
        cost_estimate=cost(2 * half * 256 * 512, 4 * 16 * count * REGION),
        name="start" if placed is None else "spread",
    )(*operands)


def spread_rest_kernel(flips, rounded_ref, wide_high, wide_low, high_ref, low_ref, *refs):
    outs, head = refs[:-1], refs[-1]
    both = (wide_high[...], wide_low[...])
    send_pieces(outs, flips, head, rounded_ref[...], both, high_ref, low_ref)


def spread_rest(rounded, both, table, flips):
    blocks = rounded.shape[0]
    top = up_to(2 + 2 * blocks, 16)
    shape = (top + both[0].shape[0], 2 * HALF)
    return pl.pallas_call(
        functools.partial(spread_rest_kernel, flips),
        in_specs=[whole_vmem()] * 5,
        out_specs=[whole_vmem()] * len(flips),
        out_shape=[jax.ShapeDtypeStruct(shape, jnp.int16)] * len(flips),
        scratch_shapes=[pltpu.VMEM((top, 2 * HALF), F32)],
        compiler_params=params(),
        cost_estimate=cost(2 * shape[0] * 256 * 256 * 3, 4 * shape[0] * 512),
        name="spread_rest",
    )(rounded, *both, *table)


def lines_kernel(place_ref, coeff_ref, *refs):
    out_ref = refs[-1]
    lanes = lax.broadcasted_iota(jnp.int32, (8, REGION), 1)

    def body(group, carry):
        at = pl.multiple_of(group * 16, 16)
        coeff = [coeff_ref[pl.ds(at + 8 * q, 8), :] for q in range(2)]
        for local in range(GROUP):
            panel = group * GROUP + local
            depth = place_ref[1, panel]
            shift = (depth - 4 * local) & (REGION - 1)
            inside = in_window(lanes, depth)
            for q in range(2):
                first = pl.multiple_of(panel * 16 + 8 * q, 8)
                out_ref[pl.ds(first, 8), :] = jnp.where(inside, pltpu.roll(coeff[q], shift, 1), 0.0)
        return carry

    lax.fori_loop(0, place_ref.shape[1] // GROUP, body, 0)


def sample_lines_kernel(tiles, place_ref, *refs):
    out_ref, coeff, held = refs[-3:]
    for tile, ref in enumerate(refs[:tiles]):
        held[tile, :64, :] = ref[...]
    weave([by_depth(held.at[tile]) for tile in range(tiles)], mixing_matrix(), coeff)
    lines_kernel(place_ref, coeff, out_ref)


def place_sample_lines(places, sample):
    count = places.shape[1]
    blocks = count // BLOCK
    tile = lambda t: pl.BlockSpec((64, BLOCK), lambda i: (0, t))
    shape = (count * 16, REGION)
    return pl.pallas_call(
        functools.partial(sample_lines_kernel, blocks),
        grid=(1,),
        in_specs=[in_smem()] + [tile(t) for t in range(blocks)],
        out_specs=pl.BlockSpec(shape, lambda i: (0, 0)),
        out_shape=jax.ShapeDtypeStruct(shape, F32),
        scratch_shapes=[
            pltpu.VMEM((count // GROUP * 16 + SPARE, BLOCK), F32),
            pltpu.VMEM((blocks, 64 + SPARE, BLOCK), F32),
        ],
        compiler_params=params(),
        cost_estimate=cost(16 * count * REGION, 4 * 16 * count * REGION),
        name="place_sample_lines",
    )(places, *[sample] * blocks)


def place_lines(places, coeff, awaited):
    count = places.shape[1]
    shape = (count * 16, REGION)
    return pl.pallas_call(
        lines_kernel,
        in_specs=[in_smem(), whole_vmem()] + [anywhere()] * len(awaited),
        out_specs=whole_vmem(),
        out_shape=jax.ShapeDtypeStruct(shape, F32),
        compiler_params=params(),
        cost_estimate=cost(16 * count * REGION, 4 * 16 * count * REGION),
        name="place_lines",
    )(places, coeff, *awaited)


def put_edges(opened, reach_x, reach_y, edges, first):
    half = reach_x // 2
    low = low_lanes(reach_y)
    layer = lambda i: opened[i * reach_y : (i + 1) * reach_y, :]
    for two in range(2):
        place = slice(first + two * reach_y, first + (two + 1) * reach_y)
        edges[0, place, :] = jnp.where(low, layer(2 * two), swap(layer(2 * two + 1)))
        last = half - 4 + 2 * two
        edges[1, place, :] = jnp.where(low, swap(layer(last)), layer(last + 1))


def stack_layers(layers, at, reach_y, stacked):
    tall = stacked.shape[0] // len(layers)
    place = at * up_to(reach_y, 8)
    for i, layer in enumerate(layers):
        stacked[pl.ds(pl.multiple_of(i * tall + place, 8), reach_y), :] = layer


def stack_pieces(parts, reach_x, reach_y, top, opened, stacked, edges, places):
    chip = lax.axis_index("narrow")
    for flip, (part, place) in enumerate(zip(parts, places)):
        first = from_short(part[:top, :])
        opened[...] = from_short(part[top:, :]) * unit(first[0:1], first[1:2])
        layers = [opened[i * reach_y : (i + 1) * reach_y, :] for i in range(reach_x // 2)]
        stack_layers(layers, chip ^ flip, reach_y, stacked)
        put_edges(opened, reach_x, reach_y, edges, place * 2 * reach_y)


def transform_pieces(table, stacked, before, spectrum):
    half = spectrum.shape[0]
    tall = stacked.shape[0] // half

    def tripled(values):
        high, low = split(values)
        return jnp.concatenate([high, low, high], axis=0)

    for i in range(0, half, 2):
        places = range(i, min(i + 2, half))
        held = jnp.concatenate([stacked[j * tall : (j + 1) * tall, :] for j in places], axis=1)
        result = dot(table, tripled(held))
        for j in places:
            made = result[:, (j - i) * 2 * HALF : (j - i + 1) * 2 * HALF]
            spectrum[j] = made if before is None else before[j] + made


def forward_early_kernel(reach_x, reach_y, chips, *refs):
    parts = refs[:chips]
    table_ref, spectrum, edges, opened, stacked = refs[chips:]
    top = parts[0].shape[0] - opened.shape[0]
    stacked[...] = jnp.zeros_like(stacked)
    stack_pieces(parts, reach_x, reach_y, top, opened, stacked, edges, range(chips))
    transform_pieces(table_ref[lax.axis_index("pair")], stacked, None, spectrum)


def stacking_scratch(chips, reach_x, reach_y):
    half = reach_x // 2
    return [
        pltpu.VMEM((up_to(half * reach_y, 16), 2 * HALF), F32),
        pltpu.VMEM((half * chips * up_to(reach_y, 8), 2 * HALF), F32),
    ]


def forward_early(parts, table, reach_x, reach_y):
    half = reach_x // 2
    chips = len(parts)
    return pl.pallas_call(
        functools.partial(forward_early_kernel, reach_x, reach_y, chips),
        in_specs=[whole_vmem()] * (chips + 1),
        out_specs=[whole_vmem()] * 2,
        out_shape=[
            jax.ShapeDtypeStruct((half, GRID, 2 * HALF), F32),
            jax.ShapeDtypeStruct((2, chips * 2 * reach_y + SPARE, 2 * HALF), F32),
        ],
        scratch_shapes=stacking_scratch(chips, reach_x, reach_y),
        compiler_params=params(),
        cost_estimate=cost(EARLY_FLOPS, 4 * half * GRID * 2 * HALF * 2),
        name="forward_early",
    )(*parts, table)


def forward_kernel(reach_x, reach_y, blocks, pieces, awaited, *refs):
    parts = refs[:pieces]
    early_ref, early_edges, table_ref, modes_ref = refs[pieces : pieces + 4]
    refs = refs[pieces + 4 + awaited :]
    spectrum, even_out, layers_out, odd_out, own_out, peers_out, inner_out, *refs = refs
    opened, stacked, edges, slabs, head = refs
    half = reach_x // 2
    pair = lax.axis_size("pair")
    top = parts[0].shape[0] - opened.shape[0]
    stacked[...] = jnp.zeros_like(stacked)
    head[...] = jnp.zeros_like(head)
    for piece in range(pieces):
        first = from_short(parts[piece][:top, :])
        mantissa, exponent = first[2 : 2 + blocks], first[2 + blocks : 2 + 2 * blocks]
        peers_out[piece * blocks : (piece + 1) * blocks, :] = decode_rounded(mantissa, exponent)
        at = 6 + 2 * piece * blocks
        head[at : at + blocks, :] = mantissa
        head[at + blocks : at + 2 * blocks, :] = exponent
    rows = 2 * reach_y
    for chip in range(pieces // pair):
        place = chip * pair * rows
        edges[:, place : place + rows, :] = early_edges[:, chip * rows : (chip + 1) * rows, :]
    before = early_ref
    for core in range(1, pair):
        places = range(core, pieces, pair)
        stack_pieces(parts[core::pair], reach_x, reach_y, top, opened, stacked, edges, places)
        transform_pieces(table_ref[lax.axis_index("pair") ^ core], stacked, before, spectrum)
        before = spectrum

    chunk = 256

    def body(index, largest):
        rows = pl.ds(pl.multiple_of(index * chunk, chunk), chunk)
        low = low_lanes(chunk)
        decay = modes_ref[0, rows, :]
        log_decay = modes_ref[1, rows, :]
        across_half = jnp.exp(half * log_decay)
        across_cut = jnp.exp((half - 4) * log_decay)
        layers = [spectrum[i, rows, :] for i in range(half)]
        run = layers[0]
        cut_right = run
        for i in range(1, half):
            run = decay * run + layers[i]
            if i == half - 5:
                cut_right = run
        right = run
        run = layers[half - 1]
        cut_left = run
        for i in range(half - 2, -1, -1):
            run = decay * run + layers[i]
            if i == 4:
                cut_left = run
        left = run
        inner_out[rows, :] = jnp.where(low, right, left)
        swapped_right, swapped_left = swap(right), swap(left)
        own = jnp.where(low, left + across_half * swapped_left, right + across_half * swapped_right)
        own_out[rows, :] = own
        made = [
            jnp.where(low, own, cut_right + across_cut * swapped_right),
            jnp.where(low, cut_left + across_cut * swapped_left, own),
        ]
        for slab, values in enumerate(made):
            slabs[slab, rows, :] = values
        return tuple(
            jnp.maximum(old, jnp.max(jnp.abs(values).reshape(chunk // 8, 8, 2 * HALF), axis=0))
            for old, values in zip(largest, made)
        )

    zero = jnp.zeros((8, 2 * HALF), F32)
    largest = lax.fori_loop(0, GRID // chunk, body, (zero,) * 2)
    top = head.shape[0]
    low = low_lanes(GRID // 2)
    upper, lower = own_out[: GRID // 2, :], own_out[GRID // 2 :, :]
    packed = [jnp.where(low, swap(upper), lower), jnp.where(low, upper, swap(lower))]

    def send(out, first, parts):
        place = first
        for index, (values, most) in enumerate(parts):
            exponent, fraction = fit_scale(jnp.max(most, axis=0, keepdims=True))
            head[2 * index : 2 * index + 1, :] = exponent
            head[2 * index + 1 : 2 * index + 2, :] = fraction
            out[place : place + values.shape[0], :] = quantize(values, exponent, fraction)
            place += values.shape[0]
        out[:first, :] = to_short(head[:first, :])

    with_most = lambda values: (values, jnp.abs(values))
    border = pieces * 2 * reach_y
    on_left = lax.axis_index("wide") & 1
    for side, (even, odd) in enumerate(((0, 1), (1, 0))):

        @pl.when(on_left == side)
        def _():
            send(even_out, 16, [(slabs[even], largest[even]), with_most(packed[even])])
            send(layers_out, top, [with_most(edges[1 - even, :border, :])])
            send(odd_out, top, [(slabs[odd], largest[odd]), with_most(edges[1 - odd, :border, :])])


def forward(parts, early, early_edges, table, modes, reach_x, reach_y, blocks, awaited):
    pieces = len(parts)
    half = reach_x // 2
    lanes = 2 * HALF
    head = up_to(6 + 2 * pieces * blocks, 16)
    border = pieces * 2 * reach_y
    short = lambda rows: jax.ShapeDtypeStruct((rows, lanes), jnp.int16)
    return pl.pallas_call(
        functools.partial(
            forward_kernel, reach_x, reach_y, blocks, pieces, len(awaited)
        ),
        in_specs=[whole_vmem()] * (pieces + 4) + [anywhere()] * len(awaited),
        out_specs=[whole_vmem()] * 7,
        out_shape=[
            jax.ShapeDtypeStruct((half, GRID, lanes), F32),
            short(16 + GRID + GRID // 2),
            short(head + border),
            short(head + GRID + border),
            jax.ShapeDtypeStruct((GRID, lanes), F32),
            jax.ShapeDtypeStruct((pieces * blocks, BLOCK), F32),
            jax.ShapeDtypeStruct((GRID, lanes), F32),
        ],
        scratch_shapes=stacking_scratch(pieces // table.shape[0], reach_x, reach_y)
        + [
            pltpu.VMEM((2, border + SPARE, lanes), F32),
            pltpu.VMEM((2, GRID, lanes), F32),
            pltpu.VMEM((head, lanes), F32),
        ],
        compiler_params=params(),
        cost_estimate=cost(2 * half * 256 * 256 * 128, 4 * half * GRID * lanes * 2),
        name="forward",
    )(*parts, early, early_edges, table, modes, *awaited)


def opened_part(ref, index, first, rows):
    head = from_short(ref[:16, :])
    scale = unit(head[2 * index : 2 * index + 1], head[2 * index + 1 : 2 * index + 2])
    return from_short(ref[first : first + rows, :]) * scale


def pair_kernel(reach_x, flips, own_ref, even_ref, modes_ref, *refs):
    outs, head = refs[:-1], refs[-1]
    span = reach_x - 4
    here = lax.axis_index("wide")
    low = low_lanes(GRID)
    log_decay = modes_ref[1]
    own = own_ref[...]
    top = even_ref.shape[0] - GRID - GRID // 2
    cut = opened_part(even_ref, 0, top, GRID)
    packed = opened_part(even_ref, 1, top + GRID, GRID // 2)
    from_left = jnp.where(low, cut, jnp.concatenate([swap(packed), packed], axis=0))
    from_right = jnp.where(low, jnp.concatenate([packed, swap(packed)], axis=0), cut)
    partner = jnp.where((here & 1) == 1, from_left, from_right)

    def weight(distances):
        powers = []
        for distance in distances:
            ahead = span * distance - reach_x
            powers.append(jnp.where(distance >= 2, ahead, ahead + GRID).astype(F32))
        return jnp.exp(jnp.where(low, *powers) * log_decay)

    head[...] = jnp.zeros_like(head)
    for flip, out in zip(flips, outs):
        behind = (here ^ flip) - here
        message = own * weight((-behind, behind))
        behind = (here ^ flip) - (here ^ 1)
        beside = jnp.where(jnp.abs(behind) == 1, 0.0, 1.0)
        send_piece(out, head, message + partner * (weight((-behind, behind)) * beside))


def pair_messages(own, from_even, modes, reach_x, flips):
    return pl.pallas_call(
        functools.partial(pair_kernel, reach_x, flips),
        in_specs=[whole_vmem()] * 3,
        out_specs=[whole_vmem()] * len(flips),
        out_shape=[jax.ShapeDtypeStruct((16 + GRID, 2 * HALF), jnp.int16)] * len(flips),
        scratch_shapes=[pltpu.VMEM((16, 2 * HALF), F32)],
        compiler_params=params(),
        cost_estimate=cost(16 * GRID * 2 * HALF, 4 * GRID * 2 * HALF * (6 + len(flips))),
        name="pair_messages",
    )(own, from_even, modes)


def borders_kernel(reach_y, pieces, layers_ref, odd_ref, table_ref, out_ref, stacked, partial):
    on_left = (lax.axis_index("wide") & 1) == 1
    pair = lax.axis_size("pair")
    rows = pieces * 2 * reach_y
    even = opened_part(layers_ref, 0, layers_ref.shape[0] - rows, rows)
    odd = opened_part(odd_ref, 1, odd_ref.shape[0] - rows, rows)
    left, right = jnp.where(on_left, even, odd), jnp.where(on_left, odd, even)
    low = low_lanes(rows)
    both = [jnp.where(low, left, swap(right)), jnp.where(low, swap(left), right)]
    core = lax.axis_index("pair")
    chip = lax.axis_index("narrow")
    stacked[...] = jnp.zeros_like(stacked)
    before = None
    for other in range(pair):
        for flip in range(pieces // pair):
            first = (flip * pair + other) * 2 * reach_y
            layers = [
                values[first + two * reach_y : first + (two + 1) * reach_y]
                for two in range(2)
                for values in both
            ]
            stack_layers(layers, chip ^ flip, reach_y, stacked)
        target = out_ref if other == pair - 1 else partial
        transform_pieces(table_ref[core ^ other], stacked, before, target)
        before = target


def borders(layers, from_odd, table, reach_y, pieces):
    chips = pieces // table.shape[0]
    shape = (4, GRID, 2 * HALF)
    return pl.pallas_call(
        functools.partial(borders_kernel, reach_y, pieces),
        in_specs=[whole_vmem()] * 3,
        out_specs=whole_vmem(),
        out_shape=jax.ShapeDtypeStruct(shape, F32),
        scratch_shapes=[
            pltpu.VMEM((4 * chips * up_to(reach_y, 8), 2 * HALF), F32),
            pltpu.VMEM(shape, F32),
        ],
        compiler_params=params(),
        cost_estimate=cost(2 * 4 * 256 * 256 * 128, 4 * 6 * GRID * 2 * HALF),
        name="borders",
    )(layers, from_odd, table)


def send_fields(outs, flips, reach_y, field_high, field_low, high_ref, low_ref, ready, head):
    half = field_high.shape[0]
    mine = y_position()
    pitch = up_to(reach_y, 16)
    pick = lambda ref: jnp.concatenate([ref[mine ^ flip] for flip in flips], axis=0)
    table = (pick(high_ref), pick(low_ref))
    for i in range(0, half, 2):
        many = min(2, half - i)
        join = lambda ref: jnp.concatenate([ref[i + j] for j in range(many)], axis=1)
        result = dot_three(table, (join(field_high), join(field_low)))
        for j in range(many):
            for piece in range(len(flips)):
                ready[piece, (i + j) * reach_y : (i + j + 1) * reach_y, :] = result[
                    piece * pitch : piece * pitch + reach_y, j * 2 * HALF : (j + 1) * 2 * HALF
                ]
    head[...] = jnp.zeros_like(head)
    for piece, out in enumerate(outs):
        if ready.shape[1] > half * reach_y:
            ready[piece, half * reach_y :, :] = jnp.zeros_like(ready[piece, half * reach_y :, :])
        send_piece(out, head, ready[piece])


def inverse_kernel(reach_x, reach_y, flips, fars, *refs):
    spectrum, border_ref, from_even, from_odd, own_ref, inner_ref, *far_refs = refs[: 6 + fars]
    refs = refs[6 + fars :]
    high_ref, low_ref, modes_ref = refs[:3]
    outs = refs[3 : 3 + len(flips)]
    field_high, field_low, ready, head = refs[3 + len(flips) :]
    half = reach_x // 2
    span = reach_x - 4
    chunk = 256
    border_rows = lax.axis_size("narrow") * lax.axis_size("pair") * 2 * reach_y
    tops = from_even.shape[0] - GRID - GRID // 2, from_odd.shape[0] - GRID - border_rows
    on_left = (lax.axis_index("wide") & 1) == 1
    moment_units = []
    for ref in (from_even, from_odd):
        first = from_short(ref[:16, :])
        moment_units.append(unit(first[0:1], first[1:2]))

    far_units = []
    for ref in far_refs:
        first = from_short(ref[:16, :])
        far_units.append(unit(first[0:1], first[1:2]))

    def body(index, carry):
        first = pl.multiple_of(index * chunk, chunk)
        rows = pl.ds(first, chunk)
        low = low_lanes(chunk)
        decay = modes_ref[0, rows, :]
        log_decay = modes_ref[1, rows, :]
        ring = modes_ref[2, rows, :]
        gain = modes_ref[3, rows, :]
        across_half = jnp.exp(half * log_decay)
        across_cut = jnp.exp((half - 4) * log_decay)
        around = jnp.exp((GRID - 4) * log_decay)
        beside = jnp.exp((GRID - reach_x - span) * log_decay)
        layers = [spectrum[i, rows, :] for i in range(half)]

        even, odd = (
            from_short(ref[pl.ds(pl.multiple_of(top + index * chunk, 16), chunk), :]) * scale
            for ref, top, scale in zip((from_even, from_odd), tops, moment_units)
        )
        left_moments, right_moments = jnp.where(on_left, even, odd), jnp.where(on_left, odd, even)
        border = [border_ref[i, rows, :] for i in range(4)]
        zero = jnp.zeros_like(decay)
        head_sum = border[0]
        for i in range(1, 4):
            head_sum = decay * head_sum + border[i]
        tail_sum = border[3]
        for i in range(2, -1, -1):
            tail_sum = decay * tail_sum + border[i]
        for i in range(4):
            layers[i] = layers[i] + jnp.where(low, border[i], zero)
        for i in range(4):
            place = half - 4 + i
            layers[place] = layers[place] + jnp.where(low, zero, border[i])
        total = own_ref[rows, :] * jnp.exp((GRID - reach_x) * log_decay)
        at = pl.ds(pl.multiple_of(16 + index * chunk, 16), chunk)
        for ref, scale in zip(far_refs, far_units):
            total = total + from_short(ref[at, :]) * scale
        one = jnp.ones_like(decay)
        total = total + left_moments * jnp.where(low, beside, one)
        total = total + right_moments * jnp.where(low, one, beside)
        shared = jnp.where(low, head_sum, tail_sum)
        entering = (swap(total) + around * shared) * ring
        leaving = swap(across_half * entering + across_cut * shared + inner_ref[rows, :])
        run = jnp.where(low, entering, leaving)
        forward_runs = []
        for i in range(half):
            run = decay * run + layers[i]
            forward_runs.append(run)
        run = jnp.where(low, leaving, entering)
        for i in range(half - 1, -1, -1):
            ahead = decay * run
            high, rest = split(gain * (forward_runs[i] + ahead))
            field_high[i, rows, :] = high
            field_low[i, rows, :] = rest
            run = ahead + layers[i]
        return carry

    lax.fori_loop(0, GRID // chunk, body, 0)
    send_fields(outs, flips, reach_y, field_high, field_low, high_ref, low_ref, ready, head)


def inverse(
    spectrum, border, from_even, from_odd, own, inner, fars, table, modes, reach_x, reach_y, flips
):
    half = reach_x // 2
    lanes = 2 * HALF
    body = up_to(half * reach_y, 16)
    shapes = [jax.ShapeDtypeStruct((16 + body, lanes), jnp.int16)] * len(flips)
    shapes += [jax.ShapeDtypeStruct((half, GRID, lanes), BF16)] * 2
    return pl.pallas_call(
        functools.partial(inverse_kernel, reach_x, reach_y, flips, len(fars)),
        in_specs=[whole_vmem()] * (9 + len(fars)),
        out_specs=[whole_vmem()] * len(shapes),
        out_shape=shapes,
        scratch_shapes=[
            pltpu.VMEM((len(flips), body, lanes), F32),
            pltpu.VMEM((16, lanes), F32),
        ],
        compiler_params=params(),
        cost_estimate=cost(2 * half * 256 * 256 * 128, 4 * half * GRID * lanes * 2),
        name="inverse",
    )(spectrum, border, from_even, from_odd, own, inner, *fars, *table, modes)


def inverse_rest_kernel(reach_y, flips, field_high, field_low, high_ref, low_ref, *refs):
    outs, (ready, head) = refs[: len(flips)], refs[len(flips) :]
    send_fields(outs, flips, reach_y, field_high, field_low, high_ref, low_ref, ready, head)


def inverse_rest(field, table, reach_y, flips):
    half = field[0].shape[0]
    lanes = 2 * HALF
    body = up_to(half * reach_y, 16)
    return pl.pallas_call(
        functools.partial(inverse_rest_kernel, reach_y, flips),
        in_specs=[whole_vmem()] * 4,
        out_specs=[whole_vmem()] * len(flips),
        out_shape=[jax.ShapeDtypeStruct((16 + body, lanes), jnp.int16)] * len(flips),
        scratch_shapes=[
            pltpu.VMEM((len(flips), body, lanes), F32),
            pltpu.VMEM((16, lanes), F32),
        ],
        compiler_params=params(),
        cost_estimate=cost(2 * half * 256 * 256 * 128, 4 * half * GRID * lanes * 2),
        name="inverse_rest",
    )(*field, *table)


def sum_rows(values):
    row = lax.broadcasted_iota(jnp.int32, values[0].shape, 0)
    for step in (4, 2, 1):
        low = (row & step) == 0
        paired = []
        for one, other in zip(values[: len(values) // 2], values[len(values) // 2 :]):
            kept = jnp.where(low, one, other)
            moved = jnp.where(low, other, one)
            if step == 4:
                moved = pltpu.roll(moved, 4, 0)
            else:
                moved = jnp.where(low, pltpu.roll(moved, 8 - step, 0), pltpu.roll(moved, step, 0))
            paired.append(kept + moved)
        values = paired
    return values[0]


def z_lines(parts, flips, high_ref, low_ref):
    mine = y_position()
    opened = []
    for part in parts:
        first = from_short(part[:16, :])
        opened.append(from_short(part[16:, :]) * unit(first[0:1], first[1:2]))
    values = split(jnp.concatenate(opened, axis=1))
    pick = lambda ref: jnp.concatenate([ref[mine ^ flip] for flip in flips], axis=0)
    return dot_three(values, (pick(high_ref), pick(low_ref)))


def sample_early_kernel(flips, *refs):
    *parts, high_ref, low_ref, out_ref = refs
    out_ref[...] = z_lines(parts, flips, high_ref, low_ref)


def sample_early(parts, flips, table):
    rows = parts[0].shape[0] - 16
    return pl.pallas_call(
        functools.partial(sample_early_kernel, flips),
        in_specs=[whole_vmem()] * (len(parts) + 2),
        out_specs=whole_vmem(),
        out_shape=jax.ShapeDtypeStruct((rows, 2 * REGION), F32),
        compiler_params=params(),
        cost_estimate=cost(EARLY_FLOPS, 4 * rows * 512),
        name="sample_early",
    )(*parts, *table)


def sample_kernel(last, reach_x, reach_y, flips, place_in, *refs):
    parts = refs[: len(flips)]
    early_ref, high_ref, low_ref, line_ref, own_ref, vector_ref, near_ref, out_ref = refs[
        len(flips) : len(flips) + 8
    ]
    flat, field, sums, place_ref, sem = refs[len(flips) + 8 :]
    copy = pltpu.make_async_copy(place_in, place_ref, sem)
    copy.start()
    half_rows = reach_x * reach_y // 2
    both = early_ref[...] + z_lines(parts, flips, high_ref, low_ref)
    flat[:half_rows, :] = both[:half_rows, :REGION]
    flat[half_rows : 2 * half_rows, :] = both[:half_rows, REGION:]
    for x in range(reach_x):
        layer = flat[x * reach_y : (x + 1) * reach_y, :]
        for row in pair_rows(x, reach_x, reach_y):
            field[pl.ds(row, reach_y, stride=2), :] = layer
    count = place_ref.shape[1]

    def body(group, carry):
        for eight in range(0, GROUP, 8):
            totals = []
            for local in range(eight, eight + 8):
                panel = group * GROUP + local
                row = place_ref[0, panel]
                first = pl.multiple_of(panel * 16, 16)
                totals.append(
                    field[pl.ds(row, 8), :] * line_ref[pl.ds(first, 8), :]
                    + field[pl.ds(row + 2 * reach_y, 8), :] * line_ref[pl.ds(first + 8, 8), :]
                )
            sums[pl.ds(pl.multiple_of(group * GROUP + eight, 8), 8), :] = sum_rows(totals)
        return carry

    copy.wait()
    lax.fori_loop(0, count // GROUP, body, 0)
    first, rest = split(sums[...])
    second, third = split(sums[...] - first.astype(F32))
    across = lambda values: lax.dot_general(
        jnp.ones((16, REGION), BF16),
        values,
        (((1,), (1,)), ((), ())),
        preferred_element_type=F32,
    )
    sampled = across(first) + (across(second) + across(third))
    for block in range(count // BLOCK):
        lane = slice(block * BLOCK, (block + 1) * BLOCK)
        row = slice(block, block + 1)
        vector = vector_ref[row, :]
        image = jnp.where(own_ref[row, :] == 1, 0.0, 0.5 * vector) + sampled[:1, lane]
        image = image + near_ref[row, :]
        if last:
            out_ref[0:1, lane] = vector
            out_ref[1:2, lane] = image
        else:
            out_ref[row, :] = image


def sample(last, places, parts, flips, early, table, lines, flag, vector, near, reach_x, reach_y):
    count = places.shape[1]
    blocks = count // BLOCK
    shape = (2, count) if last else (blocks, BLOCK)
    return pl.pallas_call(
        functools.partial(sample_kernel, last, reach_x, reach_y, flips),
        in_specs=[anywhere()] + [whole_vmem()] * (len(parts) + 7),
        out_specs=whole_vmem(),
        out_shape=jax.ShapeDtypeStruct(shape, F32),
        scratch_shapes=[
            pltpu.VMEM((reach_x * reach_y + SPARE, REGION), F32),
            pltpu.VMEM((pair_count(reach_x, reach_y), REGION), F32),
            pltpu.VMEM((count, REGION), F32),
            pltpu.SMEM((2, count), jnp.int32),
            pltpu.SemaphoreType.DMA,
        ],
        compiler_params=params(),
        cost_estimate=cost(reach_x * reach_y * 256 * 512, 4 * 16 * count * REGION),
        name="sample",
    )(
        places,
        *parts,
        early,
        *table,
        lines,
        flag.reshape(blocks, BLOCK),
        vector.reshape(blocks, BLOCK),
        near,
    )


def near_kernel(slots, blocks, place_ref, target_ref, *refs):
    even_ref, odd_ref, peers_ref, tile_ref = refs[:4]
    out_ref, held = refs[-2:]
    count = peers_ref.shape[0]
    held[count : 2 * count, :] = peers_ref[...]
    on_left = lax.axis_index("wide") & 1
    for side, ref in ((1 - on_left, even_ref), (on_left, odd_ref)):
        top = from_short(ref[...])
        for piece in range(count // blocks):
            at = 6 + 2 * piece * blocks
            held[pl.ds(side * (2 * count) + piece * blocks, blocks), :] = decode_rounded(
                top[at : at + blocks], top[at + blocks : at + 2 * blocks]
            )
    out_ref[...] = jnp.zeros_like(out_ref)
    for slot in range(slots):
        picked = held[pl.ds(place_ref[slot], 1), :]
        picked = jnp.broadcast_to(picked, (16, BLOCK)).astype(BF16)
        product = lax.dot_general(
            picked,
            tile_ref[slot],
            (((1,), (1,)), ((), ())),
            preferred_element_type=F32,
        )
        target = pl.ds(target_ref[slot], 1)
        out_ref[target, :] = out_ref[target, :] + product[:1]


def near_field(places, targets, from_even, from_odd, peers, tiles, blocks, out_rows, awaited):
    slots = tiles.shape[0]
    head = up_to(6 + 2 * peers.shape[0], 16)
    constant = lambda shape: pl.BlockSpec(shape, lambda i: (0,) * len(shape))
    return pl.pallas_call(
        functools.partial(near_kernel, slots, blocks),
        grid=(1,),
        in_specs=[
            in_smem(),
            in_smem(),
            constant((head, BLOCK)),
            constant((head, BLOCK)),
            constant(peers.shape),
            constant(tiles.shape),
        ]
        + [anywhere()] * len(awaited),
        out_specs=constant((out_rows, BLOCK)),
        out_shape=jax.ShapeDtypeStruct((out_rows, BLOCK), F32),
        scratch_shapes=[pltpu.VMEM((3 * peers.shape[0] + SPARE, BLOCK), F32)],
        compiler_params=params(),
        cost_estimate=cost(2 * slots * 16 * BLOCK * BLOCK, 2 * slots * BLOCK * BLOCK),
        name="near_field",
    )(places, targets, from_even, from_odd, peers, tiles, *awaited)


def shards(
    density,
    surface_flag,
    stencil_base,
    sample_weights,
    dipole_weights,
    near_target,
    near_source,
    near_tiles,
):
    x_count = lax.axis_size("wide")
    y_count = lax.axis_size(Y_AXES)
    y_index = lax.axis_index(Y_AXES)
    pair = lax.axis_size("pair")
    span_x = REGION // x_count
    span_y = REGION // y_count
    reach_x = span_x + 4
    reach_y = span_y + 4
    count = density.shape[0]
    blocks = count // BLOCK

    z_forward, z_inverse, y_forward, y_inverse, modes = tables(y_count, pair, span_y)
    modes = lax.dynamic_index_in_dim(jnp.asarray(modes), y_index, 0, keepdims=False)

    neighbour = near_source // blocks
    flip = (y_index + neighbour % 3 - 1) ^ y_index
    sources = ((neighbour // 3) * y_count + flip) * blocks + near_source % blocks
    out_rows = up_to(blocks + 1, 8)
    live = near_target >= 0
    sources = jnp.where(live, sources, 0)
    targets = jnp.where(live, near_target, out_rows - 1)

    swaps = lambda pairs: [(i, j) for i, j in pairs] + [(j, i) for i, j in pairs]
    even_swap = swaps([(i, i + 1) for i in range(0, x_count - 1, 2)])
    odd_swap = swaps([(i, i + 1) for i in range(1, x_count - 1, 2)])
    far_flips = list(range(2, x_count, 2))

    first, inside, local = list(range(pair, y_count)), list(range(1, pair)), [0]
    same_core = list(range(0, y_count, pair))
    other_core = [flip for flip in range(y_count) if flip not in same_core]

    def turned(sent, then):
        arrived = [None] * y_count
        for flip, part in zip(first + inside + local, list(sent) + list(then)):
            swap_pairs = [(i, i ^ flip) for i in range(y_count)]
            arrived[flip] = part if flip == 0 else lax.ppermute(part, Y_AXES, swap_pairs)
        return arrived

    def chosen(parts, flips):
        return [parts[flip] for flip in flips]

    def convolve_and_sample(last, vector, sent, both, table, places, sample_lines, awaited):
        then = [part for flips in (inside, local) for part in spread_rest(vector, both, table, flips)]
        arrived = turned(sent, then)
        early, edges = forward_early(chosen(arrived, same_core), y_forward, reach_x, reach_y)
        spectrum, even_message, layers, odd_message, own, peers, inner = forward(
            arrived, early, edges, y_forward, modes, reach_x, reach_y, blocks, awaited
        )
        from_even = lax.ppermute(even_message, "wide", even_swap)
        from_odd = lax.ppermute(odd_message, "wide", odd_swap)
        even_layers = lax.ppermute(layers, "wide", even_swap)
        fars = [
            lax.ppermute(message, "wide", [(i, i ^ flip) for i in range(x_count)])
            for flip, message in zip(
                far_flips, pair_messages(own, from_even, modes, reach_x, far_flips)
            )
        ]
        *sent, high, low = inverse(
            spectrum,
            borders(even_layers, from_odd, y_forward, reach_y, y_count),
            from_even,
            from_odd,
            own,
            inner,
            fars,
            y_inverse,
            modes,
            reach_x,
            reach_y,
            first,
        )
        then = [
            part
            for flips in (inside, local)
            for part in inverse_rest((high, low), y_inverse, reach_y, flips)
        ]
        near_part = near_field(
            sources, targets, even_layers, from_odd, peers, near_tiles, blocks, out_rows, then[:1]
        )
        arrived = turned(sent, then)
        image = sample(
            last,
            places,
            chosen(arrived, other_core),
            other_core,
            sample_early(chosen(arrived, same_core), same_core, z_inverse),
            z_inverse,
            sample_lines,
            surface_flag,
            vector,
            near_part,
            reach_x,
            reach_y,
        )
        return image, near_part

    raw = (stencil_base, surface_flag, sample_weights, dipole_weights)
    *sent, wide_high, wide_low, source_coeff, places, vector, high, low = spread(
        density, z_forward, None, raw, reach_x, reach_y, first
    )
    z_forward = (high, low)
    sample_lines = place_sample_lines(places, sample_weights)
    vector, near_part = convolve_and_sample(
        False,
        vector,
        sent,
        (wide_high, wide_low),
        z_forward,
        places,
        sample_lines,
        [sample_lines],
    )
    source_lines = place_lines(places, source_coeff, [near_part])
    *sent, wide_high, wide_low = spread(
        vector.reshape(-1), z_forward, (places, source_lines), None, reach_x, reach_y, first
    )
    both_images, _ = convolve_and_sample(
        True, vector, sent, (wide_high, wide_low), z_forward, places, sample_lines, []
    )
    return both_images


def solution(mesh):
    panels = P(("groups",) + ALL_AXES)
    columns = P(None, ("groups",) + ALL_AXES)
    in_specs = (
        panels,
        panels,
        columns,
        columns,
        columns,
        panels,
        panels,
        P(("groups",) + ALL_AXES, None, None),
    )
    return jax.shard_map(
        shards, mesh=mesh, in_specs=in_specs, out_specs=columns, check_vma=False
    )
```
